32 devices in a mesh: seg: 8 (over z, y), rep: 4 (over x, core).
Axes of the slice: x: 2, y: 2, z: 4, core: 2. Of those that a mesh axis runs over, the one named last changes fastest.
Arguments:
- frames: bfloat16 [2, 4, 1024, 512], P(None, 'rep', 'seg'), may hold values from -6 to 6
- utt_segments: int32 [2, 4, 4], P(None, 'rep'), may hold values from 1 to 60, as said below
- out_grad: bfloat16 [2, 4, 1024, 512], P(None, 'rep', 'seg'), may hold values from -6 to 6
- qkv_weight: bfloat16 [2, 512, 1536], P(None, 'rep', 'seg'), may hold values from -0.25 to 0.25
- out_weight: bfloat16 [2, 512, 512], P(None, 'rep', 'seg'), may hold values from -0.75 to 0.75
- ffn_in_weight: bfloat16 [2, 512, 2048], P(None, 'rep', 'seg'), may hold values from -0.25 to 0.25
- ffn_out_weight: bfloat16 [2, 2048, 512], P(None, 'rep', 'seg'), may hold values from -0.125 to 0.125
- norm_gains: float32 [2, 2, 512], replicated, may hold values from 0.5 to 1.5
- biases: float32 [2, 6, 512], replicated, may hold values from -1 to 1
- ffn_bias: float32 [2, 2048], replicated, may hold values from -1 to 1
Outputs:
- encoded: float32 [2, 4, 1024, 512], P(None, 'rep', 'seg')
- frames_grad: float32 [2, 4, 1024, 512], P(None, 'rep', 'seg')
- grad_qkv: float32 [2, 512, 1536], P(None, 'rep', 'seg')
- grad_out_weight: float32 [2, 512, 512], P(None, 'rep', 'seg')
- grad_ffn_in: float32 [2, 512, 2048], P(None, 'rep', 'seg')
- grad_ffn_out: float32 [2, 2048, 512], P(None, 'rep', 'seg')
- grad_norm_gains: float32 [2, 2, 512], replicated
- grad_biases: float32 [2, 6, 512], replicated
- grad_ffn_bias: float32 [2, 2048], replicated
The draws below stay inside these ranges and needn't reach their ends.
Inputs may be any that keep to these rules, and one draw needn't show every extreme that they name: `utt_segments`: A group's 4 entries are the segment counts of its utterances in time order and sum to 64; in every group one utterance holds the most.
All inputs are finite; a program needn't handle non-finite values.
Results may differ from the reference program's by a relative error of at most 0.019.
Values may be sent and summed in bfloat16 or wider, within the bound.
No kernel may reach another device: no remote copies, remote signals or barrier semaphores. Data moves between devices by JAX's collectives and lax.ppermute only.
A program may use at most 192 MiB of HBM per device.

```python
import math
import jax
import jax.numpy as jnp
from jax import lax

D = 512
HEADS = 8
FF = 2048
SEG_LEN = 16
LEFT_LEN = 30
RIGHT_LEN = 4
MEM_LEN = 4
LAYERS = 2
MICRO = 2
UTTS = 4
GROUPS = 4
SEG_DEV = 8
SEGS = 64
FRAMES = 1024


def draw_utt_segments(key, part):
    key = jax.random.fold_in(key, 7)
    short_key, spot_key = jax.random.split(key)
    short_most = max(1, (SEG_DEV - 1) // (UTTS - 1))
    pair_count = (UTTS - 1) // 2
    pieces = []
    if pair_count > 0:
        firsts = jax.random.randint(short_key, (MICRO, GROUPS, pair_count), 1, short_most + 1, dtype=jnp.int32)
        pieces.append(firsts)
        pieces.append((short_most + 1 - firsts).astype(jnp.int32))
    if (UTTS - 1) % 2 == 1:
        pieces.append(jnp.full((MICRO, GROUPS, 1), (short_most + 1) // 2, jnp.int32))
    shorts = jnp.concatenate(pieces, axis=2).astype(jnp.int32)
    longest = (SEGS - jnp.sum(shorts, axis=2, keepdims=True)).astype(jnp.int32)
    position = jax.random.randint(spot_key, (MICRO, GROUPS, 1), 0, UTTS, dtype=jnp.int32)
    column = jnp.arange(UTTS, dtype=jnp.int32)[None, None, :]
    source = jnp.clip(jnp.where(column < position, column, column - 1), 0, UTTS - 2).astype(jnp.int32)
    source = jnp.broadcast_to(source, (MICRO, GROUPS, UTTS))
    picked = jnp.take_along_axis(shorts, source, axis=2)
    return jnp.where(column == position, longest, picked).astype(jnp.int32)


def block_levels(key, dims, shards, low, high):
    level, own = 1.0, jax.random.fold_in(key, 6)
    for axis_at, shards_of in shards:
        draws = jnp.exp(jax.random.uniform(jax.random.fold_in(own, axis_at), (shards_of,), jnp.float32, low / len(shards), high / len(shards)))
        level = level * jnp.repeat(draws, dims[axis_at] // shards_of).reshape([-1 if axis == axis_at else 1 for axis in range(len(dims))])
    return level


def noise(stream_key, extent, spread, limit, shards=(), kind=jnp.bfloat16):
    loudness = block_levels(stream_key, extent, shards, -0.22, 0.18) if shards else 1.0
    drawn = jax.random.normal(stream_key, extent, jnp.float32) * spread * loudness
    return jnp.minimum(jnp.maximum(drawn, -limit), limit).astype(kind)


def setup_inputs(seed: int = 0) -> dict:
    seeds = jax.random.split(jax.random.key(seed), 11)
    return {
        "frames": noise(seeds[0], (MICRO, GROUPS, FRAMES, D), 1.0, 6.0, ((1, 4), (2, 8))),
        "utt_segments": draw_utt_segments(jax.random.fold_in(seeds[10], 71), 0),
        "out_grad": noise(seeds[2], (MICRO, GROUPS, FRAMES, D), 1.0, 6.0, ((1, 4), (2, 8))),
        "qkv_weight": noise(seeds[3], (LAYERS, D, 3 * D), D ** -0.5, 0.25, ((1, 4), (2, 8))),
        "out_weight": noise(seeds[4], (LAYERS, D, D), (D // 8) ** -0.5, 0.75, ((1, 4), (2, 8))),
        "ffn_in_weight": noise(seeds[5], (LAYERS, D, FF), D ** -0.5, 0.25, ((1, 4), (2, 8))),
        "ffn_out_weight": noise(seeds[6], (LAYERS, FF, D), FF ** -0.5, 0.125, ((1, 4), (2, 8))),
        "norm_gains": jnp.clip(1.0 + 0.1 * jax.random.normal(seeds[7], (LAYERS, 2, D), jnp.float32), 0.5, 1.5),
        "biases": noise(seeds[8], (LAYERS, 6, D), 0.2, 1.0, (), jnp.float32),
        "ffn_bias": noise(seeds[9], (LAYERS, FF), 0.2, 1.0, (), jnp.float32),
    }


HIGH = lax.Precision.HIGHEST
EPS = 1e-05
ROOT_HALF = 0.7071067811865476

@jax.custom_vjp
def low(v):
    return lax.optimization_barrier(v.astype(jnp.bfloat16)).astype(jnp.float32)

@jax.custom_vjp
def low_back(v):
    return v

def low_keep(v):
    return (low(v), None)

def low_pass(kept, grad):
    return (grad,)

def back_keep(v):
    return (v, None)

def back_low(kept, grad):
    return (low(grad),)
low.defvjp(low_keep, low_pass)
low_back.defvjp(back_keep, back_low)

def product(left_side, right_side):
    return jnp.dot(left_side, right_side, precision=HIGH)

def norm_rows(inputs, gain, bias):
    center = inputs - lax.optimization_barrier(jnp.mean(inputs, axis=1, keepdims=True))
    inverse = lax.rsqrt(lax.optimization_barrier(jnp.mean(center * center, axis=1, keepdims=True)) + EPS)
    return center * inverse * gain + bias

def gelu_value(upward):
    return 0.5 * upward * (1.0 + lax.erf(upward * ROOT_HALF))

def segment_owner(segment, starts):
    return (lax.optimization_barrier(jnp.sum((segment[:, None] >= starts[None, :]).astype(jnp.int32), axis=1)) - 1).astype(jnp.int32)

def build_mask(query_seg, query_frame, frame_pos, mem_seg, starts, total_segs):
    frame_seg = jnp.floor_divide(frame_pos, SEG_LEN)
    query_owner = segment_owner(query_seg, starts)
    frame_owner = segment_owner(frame_seg, starts)
    mem_owner = segment_owner(mem_seg, starts)
    frame_in = (frame_seg >= 0) & (frame_seg < total_segs)
    mem_in = (mem_seg >= 0) & (mem_seg < total_segs)
    query_col = query_seg[:, None]
    frame_at = frame_pos[None, :]
    frame_of = frame_seg[None, :]
    nearby = (frame_of == query_col) | (frame_at >= query_col * SEG_LEN - LEFT_LEN) & (frame_at < query_col * SEG_LEN) | (frame_of == query_col + 1) & (frame_at < query_col * SEG_LEN + SEG_LEN + RIGHT_LEN)
    frame_ok = nearby & frame_in[None, :] & (frame_owner[None, :] == query_owner[:, None])
    memory_of = mem_seg[None, :]
    mem_ok = (memory_of >= query_col - MEM_LEN) & (memory_of < query_col) & mem_in[None, :] & (mem_owner[None, :] == query_owner[:, None]) & query_frame[:, None]
    return jnp.concatenate([mem_ok, frame_ok], axis=1)

def attend_block(query_rows, keys_all, values_all, allowed, scale_factor):
    scores = low_back(jnp.einsum('rhe,khe->hrk', query_rows, keys_all, precision=HIGH)) * scale_factor
    scores = jnp.where(allowed[None], scores, -1e+30)
    row_max = lax.optimization_barrier(jnp.max(scores, axis=2, keepdims=True))
    probs = jnp.exp(scores - row_max)
    probs = probs / lax.optimization_barrier(jnp.sum(probs, axis=2, keepdims=True))
    return jnp.einsum('hrk,khe->rhe', low(probs), values_all, precision=HIGH)

def encoder_layer(inputs, memory, layer_params, starts, with_summary):
    qkv_w, out_w, ffn_w1, ffn_w2, gain_rows, biases, ffn_b1 = layer_params
    frame_count, model_width = inputs.shape
    seg_count = frame_count // SEG_LEN
    head_size = model_width // HEADS
    scale_factor = head_size ** (-0.5)
    hidden = norm_rows(inputs, gain_rows[0], biases[0])
    projected = product(low(hidden), qkv_w)
    query = low_back(low(projected[:, :model_width] + biases[1]))
    keys_now = low_back(low(projected[:, model_width:2 * model_width]))
    values_now = low_back(low(projected[:, 2 * model_width:] + biases[2]))
    mem_proj = product(low(memory), qkv_w[:, model_width:])
    mem_keys = low_back(low(mem_proj[:, :model_width]))
    mem_values = low_back(low(mem_proj[:, model_width:] + biases[2]))
    block_rows = math.gcd(frame_count, 512)
    block_segs = block_rows // SEG_LEN
    span_rows = block_rows + LEFT_LEN + RIGHT_LEN
    keys_pad = jnp.pad(keys_now, ((LEFT_LEN, RIGHT_LEN), (0, 0)))
    values_pad = jnp.pad(values_now, ((LEFT_LEN, RIGHT_LEN), (0, 0)))
    mem_keys_pad = jnp.pad(mem_keys, ((MEM_LEN, 0), (0, 0)))
    mem_values_pad = jnp.pad(mem_values, ((MEM_LEN, 0), (0, 0)))
    summary_query = None
    if with_summary:
        summary = lax.optimization_barrier(jnp.mean(hidden.reshape(seg_count, SEG_LEN, model_width), axis=1))
        summary_query = low_back(low(product(low(summary), qkv_w[:, :model_width]) + biases[1]))

    def one_block(number):
        first_row = number * block_rows
        first_seg = number * block_segs
        query_rows = lax.dynamic_slice_in_dim(query, first_row, block_rows, 0)
        query_seg = first_seg + jnp.arange(block_rows, dtype=jnp.int32) // SEG_LEN
        query_frame = jnp.ones((block_rows,), jnp.bool_)
        if with_summary:
            query_rows = jnp.concatenate([query_rows, lax.dynamic_slice_in_dim(summary_query, first_seg, block_segs, 0)], axis=0)
            query_seg = jnp.concatenate([query_seg, first_seg + jnp.arange(block_segs, dtype=jnp.int32)])
            query_frame = jnp.concatenate([query_frame, jnp.zeros((block_segs,), jnp.bool_)])
        keys_all = jnp.concatenate([lax.dynamic_slice_in_dim(mem_keys_pad, first_seg, block_segs + MEM_LEN, 0), lax.dynamic_slice_in_dim(keys_pad, first_row, span_rows, 0)], axis=0)
        values_all = jnp.concatenate([lax.dynamic_slice_in_dim(mem_values_pad, first_seg, block_segs + MEM_LEN, 0), lax.dynamic_slice_in_dim(values_pad, first_row, span_rows, 0)], axis=0)
        frame_pos = first_row - LEFT_LEN + jnp.arange(span_rows, dtype=jnp.int32)
        mem_seg = first_seg - MEM_LEN + jnp.arange(block_segs + MEM_LEN, dtype=jnp.int32)
        allowed = build_mask(query_seg, query_frame, frame_pos, mem_seg, starts, seg_count)
        result = attend_block(query_rows.reshape(-1, HEADS, head_size), keys_all.reshape(-1, HEADS, head_size), values_all.reshape(-1, HEADS, head_size), allowed, scale_factor)
        return result.reshape(-1, model_width)
    attended = lax.map(jax.checkpoint(one_block), jnp.arange(frame_count // block_rows, dtype=jnp.int32))
    frame_out = low_back(low(attended[:, :block_rows].reshape(frame_count, model_width)))
    mixed = inputs + (low_back(product(frame_out, out_w)) + biases[3])
    if with_summary:
        summary_out = low_back(low(attended[:, block_rows:].reshape(seg_count, model_width)))
        memory = low_back(product(summary_out, out_w)) + biases[3]
    hidden2 = norm_rows(mixed, gain_rows[1], biases[4])
    upward = low_back(product(low(hidden2), ffn_w1) + ffn_b1)
    output = mixed + (low_back(product(low(gelu_value(upward)), ffn_w2)) + biases[5])
    return (output, memory)

def sequence_forward(all_params, inputs, starts):
    memory = lax.optimization_barrier(jnp.mean(inputs.reshape(inputs.shape[0] // SEG_LEN, SEG_LEN, inputs.shape[1]), axis=1))
    hidden = inputs
    for layer_number in range(LAYERS):
        layer_params = tuple((member[layer_number] for member in all_params))
        hidden, memory = encoder_layer(hidden, memory, layer_params, starts, layer_number < LAYERS - 1)
    return hidden

def reference(frames, utt_segments, out_grad, qkv_weight, out_weight, ffn_in_weight, ffn_out_weight, norm_gains, biases, ffn_bias):
    params = tuple((member.astype(jnp.float32) for member in (qkv_weight, out_weight, ffn_in_weight, ffn_out_weight, norm_gains, biases, ffn_bias)))
    flat_frames = frames.astype(jnp.float32).reshape(MICRO * GROUPS, FRAMES, D)
    flat_grads = out_grad.astype(jnp.float32).reshape(MICRO * GROUPS, FRAMES, D)
    flat_lengths = utt_segments.reshape(MICRO * GROUPS, UTTS)

    def scan_step(totals, element):
        inputs, cotangent, lengths = element
        starts = (jnp.cumsum(lengths) - lengths).astype(jnp.int32)

        def forward_only(weights_all, inputs_now):
            return sequence_forward(weights_all, inputs_now, starts)
        result, pullback = jax.vjp(forward_only, params, inputs)
        param_grads, input_grad = pullback(cotangent)
        return (jax.tree.map(jnp.add, totals, param_grads), (result, input_grad))
    zero_grads = tuple((jnp.zeros_like(member) for member in params))
    totals, stacked = lax.scan(scan_step, zero_grads, (flat_frames, flat_grads, flat_lengths))
    encoded = stacked[0].reshape(MICRO, GROUPS, FRAMES, D)
    frames_grad = stacked[1].reshape(MICRO, GROUPS, FRAMES, D)
    return (encoded, frames_grad, totals[0], totals[1], totals[2], totals[3], totals[4], totals[5], totals[6])
```

```python
import jax
import jax.numpy as jnp
from jax import lax
from jax.experimental import pallas as pl
from jax.experimental.pallas import tpu as pltpu
from jax.sharding import PartitionSpec as P

HEADS = 8
SEG_LEN = 16
LEFT_LEN = 30
RIGHT_LEN = 4
MEM_LEN = 4
LAYERS = 2

EPS = 1e-05
ROOT_HALF = 0.7071067811865476
INV_ROOT_TWO_PI = 0.3989422804014327

LANES = 128
TILE = 16
RIGHT_ROWS = 16
LEFT_ROWS = 32
MEM_ROWS = 16
BACK_ROWS = LEFT_ROWS + MEM_ROWS
BLOCKS = 8
VMEM_BYTES = 56 * 1024 * 1024

BF16 = jnp.bfloat16
F32 = jnp.float32


def nn(a, b):
    return lax.dot_general(a, b, (((1,), (0,)), ((), ())), preferred_element_type=F32)


def nt(a, b):
    return lax.dot_general(a, b, (((1,), (1,)), ((), ())), preferred_element_type=F32)


def tn(a, b):
    return lax.dot_general(a, b, (((0,), (0,)), ((), ())), preferred_element_type=F32)


def col_sum(value):
    return jnp.sum(value, axis=0, keepdims=True)


def norm_forward(inputs, gain, bias):
    center = inputs - jnp.mean(inputs, axis=1, keepdims=True)
    inverse = lax.rsqrt(jnp.mean(center * center, axis=1, keepdims=True) + EPS)
    scaled = center * inverse
    return scaled * gain + bias, scaled, inverse


def norm_backward(grad_in, scaled, inverse, gain):
    grad_scaled = grad_in * gain
    return inverse * (
        grad_scaled
        - jnp.mean(grad_scaled, axis=1, keepdims=True)
        - scaled * jnp.mean(grad_scaled * scaled, axis=1, keepdims=True)
    )


def segment_mean(inputs):
    rows, width = inputs.shape
    return jnp.mean(inputs.reshape(rows // SEG_LEN, SEG_LEN, width), axis=1)


def segment_spread(rows, width, per_segment):
    segs = rows // SEG_LEN
    return jnp.broadcast_to(per_segment[:, None, :], (segs, SEG_LEN, width)).reshape(rows, width)


def identity(size):
    row = lax.broadcasted_iota(jnp.int32, (size, size), 0)
    col = lax.broadcasted_iota(jnp.int32, (size, size), 1)
    return (row == col).astype(F32).astype(BF16)


class Sizes:
    def __init__(self, rows, width, ff, with_summary):
        self.rows = rows
        self.width = width
        self.ff = ff
        self.segs = rows // SEG_LEN
        self.top = TILE if with_summary else 0
        self.keys = rows + RIGHT_ROWS + LEFT_ROWS + MEM_ROWS
        self.ext = self.top + self.keys
        self.queries = self.top + rows
        self.right_at = self.top + rows
        self.left_at = self.right_at + RIGHT_ROWS
        self.mem_at = self.left_at + LEFT_ROWS
        self.pairs = width // LANES


class Matrices:
    def __init__(self, width, ff):
        self.qkv = (BLOCKS, 3 * width // BLOCKS, width)
        self.out = (BLOCKS, width // BLOCKS, width)
        self.up = (BLOCKS, ff // BLOCKS, width)
        self.down = (BLOCKS, width // BLOCKS, ff)
        self.down_parts = ff // width
        self.attn_rows = self.qkv[1] + self.out[1]
        self.ffn_rows = self.up[1] + self.down_parts * self.down[1]


def attn_pairs(mats, by_blocks, hbm, first, qkv_ref, out_ref, place_ref):
    if not by_blocks:
        return [(hbm[0], qkv_ref), (hbm[1], out_ref)]
    pairs = []
    high = mats.qkv[1]
    for k, block in enumerate(hbm):
        lane = pl.multiple_of(place_ref[2 + k], LANES)
        pairs.append((block.at[:, pl.ds(first, high), :], qkv_ref.at[:, :, pl.ds(lane, LANES)]))
        pairs.append(
            (
                block.at[:, pl.ds(first + high, mats.out[1]), :],
                out_ref.at[:, :, pl.ds(lane, LANES)],
            )
        )
    return pairs


def ffn_pairs(mats, by_blocks, hbm, first, up_ref, down_ref, place_ref):
    if not by_blocks:
        return [(hbm[0], up_ref), (hbm[1], down_ref)]
    pairs = []
    high = mats.up[1]
    low = mats.down[1]
    for k, block in enumerate(hbm):
        lane = pl.multiple_of(place_ref[2 + k], LANES)
        pairs.append((block.at[:, pl.ds(first, high), :], up_ref.at[:, :, pl.ds(lane, LANES)]))
        for part in range(mats.down_parts):
            there = pl.multiple_of(place_ref[2 + k] * mats.down_parts + part * LANES, LANES)
            pairs.append(
                (
                    block.at[:, pl.ds(first + high + part * low, low), :],
                    down_ref.at[:, :, pl.ds(there, LANES)],
                )
            )
    return pairs


def start_in(pairs, sems, at):
    copies = [pltpu.make_async_copy(s, d, sems.at[at + i]) for i, (s, d) in enumerate(pairs)]
    for copy in copies:
        copy.start()
    return copies


def start_out(pairs, sems, at):
    copies = [pltpu.make_async_copy(d, s, sems.at[at + i]) for i, (s, d) in enumerate(pairs)]
    for copy in copies:
        copy.start()
    return copies


def wait_all(copies):
    for copy in copies:
        copy.wait()


def fill_mask(sizes, seqs, starts_ref, place_ref, mask_ref):
    shape = (sizes.queries, sizes.keys)
    row = lax.broadcasted_iota(jnp.int32, shape, 0)
    col = lax.broadcasted_iota(jnp.int32, shape, 1)
    base = place_ref[0]
    total = place_ref[1]
    query = jnp.where(row < sizes.top, row, lax.shift_right_arithmetic(row - sizes.top, 4))
    left_at = sizes.rows + RIGHT_ROWS
    mem_at = left_at + LEFT_ROWS
    spot = jnp.where(col < left_at, col, col - mem_at)
    mem_seg = jnp.where(col < mem_at + sizes.segs, col - mem_at, col - mem_at - 2 * sizes.segs)
    key_seg = jnp.where(col < mem_at, lax.shift_right_arithmetic(spot, 4), mem_seg)
    near = (
        (key_seg == query)
        | ((spot >= query * SEG_LEN - LEFT_LEN) & (spot < query * SEG_LEN))
        | ((key_seg == query + 1) & (spot < query * SEG_LEN + SEG_LEN + RIGHT_LEN))
    )
    recent = (key_seg >= query - MEM_LEN) & (key_seg < query) & (row >= sizes.top)
    allowed = ((col < mem_at) & near) | ((col >= mem_at) & recent)
    key_abs = key_seg + base
    query_abs = query + base
    allowed = allowed & (key_abs >= 0) & (key_abs < total)
    if sizes.top:
        allowed = allowed & ((row < sizes.segs) | (row >= sizes.top))
    for n in range(seqs):
        key_owner = jnp.zeros(shape, jnp.int32)
        query_owner = jnp.zeros(shape, jnp.int32)
        for u in range(starts_ref.shape[1]):
            first = starts_ref[n, u]
            key_owner = key_owner + (key_abs >= first).astype(jnp.int32)
            query_owner = query_owner + (query_abs >= first).astype(jnp.int32)
        mask_ref[n] = jnp.where(allowed & (key_owner == query_owner), 0.0, -1e30)


def half_masks():
    lane = lax.broadcasted_iota(jnp.int32, (1, LANES), 1)
    even = (lane < LANES // 2).astype(F32)
    return even.astype(BF16), (1.0 - even).astype(BF16), lane < LANES // 2


def project(sizes, z_ref, qkv_ref, row_bias_ref, proj_ref):
    step = BLOCKS // 2
    for c in range(2):
        block = qkv_ref[pl.ds(c * step, step)].reshape(-1, sizes.width)
        wide = block.shape[0]
        made = nt(z_ref[...], block) + row_bias_ref[:, pl.ds(c * wide, wide)]
        proj_ref[:, pl.ds(c * wide, wide)] = made.astype(BF16)


def split_heads(sizes, ref, first, rows, lane):
    return ref[pl.ds(first, rows), pl.ds(lane, LANES)]


def attend(sizes, seqs, proj_ref, mask_ref, probs_ref, att_ref):
    even, odd, is_even = half_masks()
    scale = (sizes.width // HEADS) ** (-0.5)
    count = sizes.queries

    def body(p, carry):
        for n in range(seqs):
            lane = pl.multiple_of(p * LANES, LANES)
            query = proj_ref[pl.ds(n * sizes.ext, count), pl.ds(lane, LANES)]
            first = n * sizes.ext + sizes.top
            key = proj_ref[pl.ds(first, sizes.keys), pl.ds(sizes.width + lane, LANES)]
            value = proj_ref[pl.ds(first, sizes.keys), pl.ds(2 * sizes.width + lane, LANES)]
            scores = nt(jnp.concatenate([query * even, query * odd], axis=0), key) * scale
            outs = []
            for half in range(2):
                part = scores[half * count : (half + 1) * count] + mask_ref[n]
                part = jnp.exp(part - jnp.max(part, axis=1, keepdims=True))
                part = part * (1.0 / jnp.sum(part, axis=1, keepdims=True))
                probs_ref[n * sizes.pairs + p, pl.ds(half * count, count), :] = part
                outs.append(nn(part.astype(BF16), value))
            att_ref[pl.ds(n * count, count), pl.ds(lane, LANES)] = jnp.where(
                is_even, outs[0], outs[1]
            ).astype(BF16)
        return carry

    lax.fori_loop(0, sizes.pairs, body, 0)


def attend_back(sizes, seqs, proj_ref, probs_ref, go_ref, gproj_ref):
    even, odd, is_even = half_masks()
    scale = (sizes.width // HEADS) ** (-0.5)
    count = sizes.queries
    wide = sizes.width
    for n in range(seqs):
        base = n * sizes.ext
        rest = sizes.ext - count
        gproj_ref[pl.ds(base + count, rest), pl.ds(0, wide)] = jnp.zeros((rest, wide), BF16)
        if sizes.top:
            gproj_ref[pl.ds(base, sizes.top), pl.ds(wide, 2 * wide)] = jnp.zeros(
                (sizes.top, 2 * wide), BF16
            )

    def body(p, carry):
        for n in range(seqs):
            lane = pl.multiple_of(p * LANES, LANES)
            base = n * sizes.ext
            first = base + sizes.top
            query = proj_ref[pl.ds(base, count), pl.ds(lane, LANES)]
            key = proj_ref[pl.ds(first, sizes.keys), pl.ds(wide + lane, LANES)]
            value = proj_ref[pl.ds(first, sizes.keys), pl.ds(2 * wide + lane, LANES)]
            grad = go_ref[pl.ds(n * count, count), pl.ds(lane, LANES)]
            queries = jnp.concatenate([query * even, query * odd], axis=0)
            grads = jnp.concatenate([grad * even, grad * odd], axis=0)
            probs = probs_ref[n * sizes.pairs + p]
            grad_values = tn(probs.astype(BF16), grads)
            grad_probs = nt(grads, value)
            weighted = grad_probs * probs
            grad_scores = (
                (weighted - probs * jnp.sum(weighted, axis=1, keepdims=True)) * scale
            ).astype(BF16)
            grad_keys = tn(grad_scores, queries)
            grad_query = jnp.where(
                is_even, nn(grad_scores[:count], key), nn(grad_scores[count:], key)
            )
            gproj_ref[pl.ds(base, count), pl.ds(lane, LANES)] = grad_query.astype(BF16)
            gproj_ref[pl.ds(first, sizes.keys), pl.ds(wide + lane, LANES)] = grad_keys.astype(BF16)
            gproj_ref[pl.ds(first, sizes.keys), pl.ds(2 * wide + lane, LANES)] = (
                grad_values.astype(BF16)
            )
        return carry

    lax.fori_loop(0, sizes.pairs, body, 0)


def gelu_both(upward):
    half = 0.5 * (1.0 + lax.erf(upward * ROOT_HALF))
    slope = half + upward * jnp.exp(-0.5 * upward * upward) * INV_ROOT_TWO_PI
    return upward * half, slope


def up_block(up_ref, c, step):
    return up_ref[pl.ds(c * step, step)].reshape(-1, up_ref.shape[2])


def down_block(down_ref, c, wide):
    at = pl.multiple_of(c * wide, wide)
    return down_ref[:, :, pl.ds(at, wide)].reshape(-1, wide)


def ffn_back_step(
    sizes, c, wide, grad_low, hidden_low, active, slope, up_ref, down_ref, gup_ref, gdown_ref, vec
):
    at = pl.multiple_of(c * wide, wide)
    up = up_block(up_ref, c, wide // up_ref.shape[1])
    down = down_block(down_ref, c, wide)
    grad_active = nn(grad_low, down)
    grad_up_f = grad_active * slope
    grad_up = grad_up_f.astype(BF16)
    gdown_ref[:, :, pl.ds(at, wide)] = (
        tn(grad_low, active).astype(BF16).reshape(gdown_ref.shape[0], gdown_ref.shape[1], wide)
    )
    step = wide // gup_ref.shape[1]
    gup_ref[pl.ds(c * step, step)] = (
        tn(grad_up, hidden_low).astype(BF16).reshape(step, gup_ref.shape[1], gup_ref.shape[2])
    )
    vec[pl.ds(8 + c, 1), :] = col_sum(grad_up.astype(F32))
    return nn(grad_up, up)


def attn_back_stage(
    sizes, seqs, gz, grad_mem_ref, att_ref, proj_ref, probs_ref, z_ref, qkv_ref, out_ref,
    gqkv_ref, gout_ref, go_ref, gproj_ref, branch_ref, vec, gh_ref, gmem_ref, back_left_ref,
    back_right_ref,
):
    wide = sizes.width
    count = sizes.queries
    bias_out = col_sum(gz)
    for n in range(seqs):
        if sizes.top:
            mem_grad = grad_mem_ref[pl.ds(n * sizes.segs, sizes.segs), :]
            bias_out = bias_out + col_sum(mem_grad)
            branch_ref[pl.ds(n * count, sizes.top), :] = jnp.concatenate(
                [mem_grad, jnp.zeros((sizes.top - sizes.segs, wide), F32)], axis=0
            ).astype(BF16)
        branch_ref[pl.ds(n * count + sizes.top, sizes.rows), :] = gz[
            n * sizes.rows : (n + 1) * sizes.rows
        ].astype(BF16)
    vec[pl.ds(5, 1), :] = bias_out
    branch = branch_ref[...]
    gout_ref[...] = tn(branch, att_ref[...]).astype(BF16).reshape(gout_ref.shape)
    go_ref[...] = nn(branch, out_ref[...].reshape(-1, wide)).astype(BF16)
    attend_back(sizes, seqs, proj_ref, probs_ref, go_ref, gproj_ref)
    vec[pl.ds(3, 1), :] = col_sum(gproj_ref[:, pl.ds(0, wide)].astype(F32))
    vec[pl.ds(4, 1), :] = col_sum(gproj_ref[:, pl.ds(2 * wide, wide)].astype(F32))
    grad_ext = nn(gproj_ref[...], qkv_ref[...].reshape(-1, wide))
    for n in range(seqs):
        base = n * sizes.ext
        own = grad_ext[base + sizes.top : base + sizes.top + sizes.rows]
        if sizes.top:
            spread = grad_ext[base : base + sizes.segs] * (1.0 / SEG_LEN)
            own = own + segment_spread(sizes.rows, wide, spread)
        gh_ref[pl.ds(n * sizes.rows, sizes.rows), :] = own
        mem = base + sizes.mem_at
        gmem_ref[pl.ds(n * sizes.segs, sizes.segs), :] = grad_ext[mem : mem + sizes.segs]
        left = base + sizes.left_at
        back_left_ref[n] = grad_ext[left : left + BACK_ROWS].astype(BF16)
        right = base + sizes.right_at
        back_right_ref[n] = grad_ext[right : right + RIGHT_ROWS].astype(BF16)
    step = BLOCKS // 2
    part = gqkv_ref.shape[1] * step
    for c in range(2):
        gqkv_ref[pl.ds(c * step, step)] = (
            tn(gproj_ref[:, pl.ds(c * part, part)], z_ref[...])
            .astype(BF16)
            .reshape(step, gqkv_ref.shape[1], wide)
        )


def merge_halo(sizes, n, gh_ref, gmem_ref, from_right_ref, from_left_ref):
    first = n * sizes.rows
    back = from_right_ref[n].astype(F32)
    head = gh_ref[pl.ds(first, RIGHT_ROWS), :] + from_left_ref[n].astype(F32)
    middle = gh_ref[pl.ds(first + RIGHT_ROWS, sizes.rows - RIGHT_ROWS - LEFT_ROWS), :]
    tail = gh_ref[pl.ds(first + sizes.rows - LEFT_ROWS, LEFT_ROWS), :] + back[:LEFT_ROWS]
    mem = gmem_ref[pl.ds(n * sizes.segs, sizes.segs), :] + back[LEFT_ROWS + sizes.segs :]
    return jnp.concatenate([head, middle, tail], axis=0), mem


def pack_kernel(counts, qkv_ref, out_ref, up_ref, down_ref, *packed):
    eye = identity(LANES)
    for layer, (attn_ref, attn_at, ffn_ref, ffn_at) in enumerate(
        [(packed[a], b, packed[c], d) for a, b, c, d in counts]
    ):
        high = qkv_ref.shape[2]
        wide = out_ref.shape[2]
        attn_ref[pl.ds(attn_at, high), :] = tn(qkv_ref[layer], eye).astype(BF16)
        attn_ref[pl.ds(attn_at + high, wide), :] = tn(out_ref[layer], eye).astype(BF16)
        up = up_ref.shape[2]
        ffn_ref[pl.ds(ffn_at, up), :] = tn(up_ref[layer], eye).astype(BF16)
        low = down_ref.shape[2]
        for part in range(down_ref.shape[1] // LANES):
            ffn_ref[pl.ds(ffn_at + up + part * low, low), :] = tn(
                down_ref[layer, pl.ds(part * LANES, LANES), :], eye
            ).astype(BF16)


def unpack_kernel(counts, count_in, *refs):
    sources = refs[:count_in]
    qkv_ref, out_ref, up_ref, down_ref = refs[count_in:]
    eye = identity(LANES)
    for layer, (attn_i, attn_at, ffn_i, ffn_at) in enumerate(counts):
        attn_ref, ffn_ref = sources[attn_i], sources[ffn_i]
        high = qkv_ref.shape[2]
        wide = out_ref.shape[2]
        qkv_ref[layer] = nt(eye, attn_ref[pl.ds(attn_at, high), :])
        out_ref[layer] = nt(eye, attn_ref[pl.ds(attn_at + high, wide), :])
        up = up_ref.shape[2]
        up_ref[layer] = nt(eye, ffn_ref[pl.ds(ffn_at, up), :])
        low = down_ref.shape[2]
        for part in range(down_ref.shape[1] // LANES):
            down_ref[layer, pl.ds(part * LANES, LANES), :] = nt(
                eye, ffn_ref[pl.ds(ffn_at + up + part * low, low), :]
            )


def first_attn_kernel(
    sizes, seqs, mats, by_blocks, count_in, at, place_ref, starts_ref, frames_ref, left_ref,
    right_ref, gains_ref, biases_ref, row_bias_ref, *refs
):
    hbm = refs[:count_in]
    z_ref, proj_ref, probs_ref, att_ref, mixed_ref, mem_ref, qkv_ref, out_ref, mask_ref, sems = (
        refs[count_in:]
    )
    wide = sizes.width
    copies = start_in(
        attn_pairs(mats, by_blocks, hbm, at, qkv_ref, out_ref, place_ref), sems, 0
    )
    gain = gains_ref[0, pl.ds(0, 1), :]
    bias = biases_ref[0, pl.ds(0, 1), :]
    pad = jnp.zeros((TILE - sizes.segs, wide), F32)
    for n in range(seqs):
        own = frames_ref[n].astype(F32)
        before = left_ref[n].astype(F32)
        hidden = norm_forward(own, gain, bias)[0]
        halo = norm_forward(before[before.shape[0] - LEFT_ROWS :], gain, bias)[0]
        after = norm_forward(right_ref[n].astype(F32), gain, bias)[0]
        memory = jnp.concatenate(
            [
                segment_mean(own),
                jnp.zeros((sizes.segs - before.shape[0] // SEG_LEN, wide), F32),
                segment_mean(before),
            ],
            axis=0,
        )
        base = n * sizes.ext
        z_ref[pl.ds(base, sizes.top), :] = jnp.concatenate(
            [segment_mean(hidden), pad], axis=0
        ).astype(BF16)
        z_ref[pl.ds(base + sizes.top, sizes.rows), :] = hidden.astype(BF16)
        z_ref[pl.ds(base + sizes.right_at, RIGHT_ROWS), :] = after.astype(BF16)
        z_ref[pl.ds(base + sizes.left_at, LEFT_ROWS), :] = halo.astype(BF16)
        z_ref[pl.ds(base + sizes.mem_at, MEM_ROWS), :] = memory.astype(BF16)
    fill_mask(sizes, seqs, starts_ref, place_ref, mask_ref)
    wait_all(copies)
    project(sizes, z_ref, qkv_ref, row_bias_ref, proj_ref)
    attend(sizes, seqs, proj_ref, mask_ref, probs_ref, att_ref)
    mixed = nt(att_ref[...], out_ref[...].reshape(-1, wide)) + biases_ref[0, pl.ds(3, 1), :]
    for n in range(seqs):
        base = n * sizes.queries
        mem_ref[pl.ds(n * sizes.segs, sizes.segs), :] = mixed[base : base + sizes.segs]
        mixed_ref[pl.ds(n * sizes.rows, sizes.rows), :] = (
            frames_ref[n].astype(F32) + mixed[base + sizes.top : base + sizes.top + sizes.rows]
        )


def first_ffn_kernel(
    sizes, seqs, mats, by_blocks, count_in, at, place_ref, mixed_ref, mem_ref, gains_ref,
    biases_ref, ffn_bias_ref, *refs
):
    hbm = refs[:count_in]
    (
        next_ref, active_ref, slope_ref, low_ref, send_right_ref, send_left_ref, up_ref, down_ref,
        hidden_ref, sems,
    ) = refs[count_in:]
    copies = start_in(ffn_pairs(mats, by_blocks, hbm, at, up_ref, down_ref, place_ref), sems, 0)
    mixed = mixed_ref[...]
    hidden, _, _ = norm_forward(mixed, gains_ref[0, pl.ds(1, 1), :], biases_ref[0, pl.ds(4, 1), :])
    hidden_ref[...] = hidden.astype(BF16)
    next_ref[...] = mixed + biases_ref[0, pl.ds(5, 1), :]
    wait_all(copies)
    wide = sizes.width

    def body(c, carry):
        at_lane = pl.multiple_of(c * wide, wide)
        upward = nt(hidden_ref[...], up_block(up_ref, c, wide // up_ref.shape[1]))
        upward = upward + ffn_bias_ref[pl.ds(0, 1), pl.ds(at_lane, wide)]
        active, slope = gelu_both(upward)
        active = active.astype(BF16)
        active_ref[:, pl.ds(at_lane, wide)] = active
        slope_ref[:, pl.ds(at_lane, wide)] = slope.astype(BF16)
        next_ref[...] += nt(active, down_block(down_ref, c, wide))
        return carry

    lax.fori_loop(0, sizes.ff // wide, body, 0)
    low, _, _ = norm_forward(
        next_ref[...], gains_ref[1, pl.ds(0, 1), :], biases_ref[1, pl.ds(0, 1), :]
    )
    low = low.astype(BF16)
    low_ref[...] = low
    for n in range(seqs):
        base = n * sizes.rows
        send_right_ref[n, pl.ds(0, LEFT_ROWS), :] = low[
            base + sizes.rows - LEFT_ROWS : base + sizes.rows
        ]
        send_right_ref[n, pl.ds(LEFT_ROWS, MEM_ROWS), :] = jnp.concatenate(
            [
                mem_ref[pl.ds(n * sizes.segs, sizes.segs), :],
                jnp.zeros((MEM_ROWS - sizes.segs, wide), F32),
            ],
            axis=0,
        ).astype(BF16)
        send_left_ref[n] = low[base : base + RIGHT_ROWS]


def last_layer_kernel(
    sizes, seqs, mats, by_blocks, count_in, attn_at, ffn_at, place_ref, starts_ref, low_ref,
    left_ref, right_ref, mem_ref, inputs_ref, out_grad_ref, gains_ref, biases_ref, ffn_bias_ref,
    row_bias_ref, *refs
):
    hbm = refs[:count_in]
    count_out = count_in
    (encoded_ref, gz_ref, gh_ref, gmem_ref, back_left_ref, back_right_ref, vec) = refs[
        count_in : count_in + 7
    ]
    hbm_out = refs[count_in + 7 : count_in + 7 + count_out]
    (
        qkv_ref, out_ref, up_ref, down_ref, gqkv_ref, gout_ref, gup_ref, gdown_ref, mask_ref,
        z_ref, proj_ref, probs_ref, att_ref, hidden_ref, go_ref, gproj_ref, branch_ref,
        grad_low_ref, grad_hidden_ref, sems,
    ) = refs[count_in + 7 + count_out :]
    half = count_in if by_blocks else 2
    attn_hbm, ffn_hbm = (hbm, hbm) if by_blocks else (hbm[:half], hbm[half:])
    attn_out, ffn_out = (hbm_out, hbm_out) if by_blocks else (hbm_out[:half], hbm_out[half:])
    wide = sizes.width
    attn_copies = start_in(
        attn_pairs(mats, by_blocks, attn_hbm, attn_at, qkv_ref, out_ref, place_ref), sems, 0
    )
    ffn_copies = start_in(
        ffn_pairs(mats, by_blocks, ffn_hbm, ffn_at, up_ref, down_ref, place_ref),
        sems,
        len(attn_copies),
    )
    vec[...] = jnp.zeros_like(vec)
    for n in range(seqs):
        base = n * sizes.ext
        z_ref[pl.ds(base, sizes.rows), :] = low_ref[pl.ds(n * sizes.rows, sizes.rows), :]
        z_ref[pl.ds(base + sizes.right_at, RIGHT_ROWS), :] = right_ref[n]
        z_ref[pl.ds(base + sizes.left_at, LEFT_ROWS), :] = left_ref[n, pl.ds(0, LEFT_ROWS), :]
        memory = jnp.concatenate(
            [
                mem_ref[pl.ds(n * sizes.segs, sizes.segs), :],
                left_ref[n, pl.ds(LEFT_ROWS, MEM_ROWS), :].astype(F32)[: sizes.segs],
            ],
            axis=0,
        )
        z_ref[pl.ds(base + sizes.mem_at, MEM_ROWS), :] = memory.astype(BF16)
        grad_low_ref[pl.ds(n * sizes.rows, sizes.rows), :] = out_grad_ref[n]
    fill_mask(sizes, seqs, starts_ref, place_ref, mask_ref)
    wait_all(attn_copies)
    project(sizes, z_ref, qkv_ref, row_bias_ref, proj_ref)
    attend(sizes, seqs, proj_ref, mask_ref, probs_ref, att_ref)
    mixed = (
        inputs_ref[...]
        + nt(att_ref[...], out_ref[...].reshape(-1, wide))
        + biases_ref[1, pl.ds(3, 1), :]
    )
    gain = gains_ref[1, pl.ds(1, 1), :]
    hidden, scaled, inverse = norm_forward(mixed, gain, biases_ref[1, pl.ds(4, 1), :])
    hidden_ref[...] = hidden.astype(BF16)
    for n in range(seqs):
        encoded_ref[n] = mixed[n * sizes.rows : (n + 1) * sizes.rows] + biases_ref[
            1, pl.ds(5, 1), :
        ]
    grad_hidden_ref[...] = jnp.zeros_like(grad_hidden_ref)
    wait_all(ffn_copies)

    def body(c, carry):
        at_lane = pl.multiple_of(c * wide, wide)
        upward = nt(hidden_ref[...], up_block(up_ref, c, wide // up_ref.shape[1]))
        upward = upward + ffn_bias_ref[pl.ds(1, 1), pl.ds(at_lane, wide)]
        active, slope = gelu_both(upward)
        active = active.astype(BF16)
        made = nt(active, down_block(down_ref, c, wide))
        for n in range(seqs):
            encoded_ref[n] += made[n * sizes.rows : (n + 1) * sizes.rows]
        grad_hidden_ref[...] += ffn_back_step(
            sizes, c, wide, grad_low_ref[...], hidden_ref[...], active, slope, up_ref, down_ref,
            gup_ref, gdown_ref, vec,
        )
        return carry

    lax.fori_loop(0, sizes.ff // wide, body, 0)
    out_at = len(attn_copies) + len(ffn_copies)
    outs = start_out(
        ffn_pairs(mats, by_blocks, ffn_out, ffn_at, gup_ref, gdown_ref, place_ref), sems, out_at
    )
    grad = grad_low_ref[...].astype(F32)
    grad_hidden = grad_hidden_ref[...]
    vec[pl.ds(1, 1), :] = col_sum(grad_hidden * scaled)
    vec[pl.ds(6, 1), :] = col_sum(grad_hidden)
    vec[pl.ds(7, 1), :] = col_sum(grad)
    gz = grad + norm_backward(grad_hidden, scaled, inverse, gain)
    gz_ref[...] = gz
    attn_back_stage(
        sizes, seqs, gz, None, att_ref, proj_ref, probs_ref, z_ref, qkv_ref, out_ref, gqkv_ref,
        gout_ref, go_ref, gproj_ref, branch_ref, vec, gh_ref, gmem_ref, back_left_ref,
        back_right_ref,
    )
    outs = outs + start_out(
        attn_pairs(mats, by_blocks, attn_out, attn_at, gqkv_ref, gout_ref, place_ref),
        sems,
        out_at + len(outs),
    )
    wait_all(outs)


def first_back_kernel(
    last, sizes, seqs, mats, by_blocks, counts, offsets, place_ref, inputs_ref, gz_in_ref,
    gh_in_ref, gmem_in_ref, from_right_ref, from_left_ref, mixed_ref, active_ref, slope_ref,
    att_ref, probs_ref, proj_ref, z_ref, gains_ref, biases_ref, *refs
):
    attn_count, ffn_count, count_out = counts
    attn_in_at, ffn_in_at, attn_at, ffn_at = offsets
    attn_hbm = refs[:attn_count]
    ffn_hbm = refs[attn_count : attn_count + ffn_count]
    refs = refs[attn_count + ffn_count :]
    (gz_ref, gh_ref, gmem_ref, back_left_ref, back_right_ref, upper_vec, vec) = refs[:7]
    hbm_out = refs[7 : 7 + count_out]
    (
        qkv_ref, out_ref, up_ref, down_ref, gqkv_ref, gout_ref, gup_ref, gdown_ref, hidden_ref,
        go_ref, gproj_ref, branch_ref, grad_low_ref, grad_ref, grad_hidden_ref, grad_mem_ref, sems,
    ) = refs[7 + count_out :]
    attn_out, ffn_out = (hbm_out, hbm_out) if by_blocks else (hbm_out[:2], hbm_out[2:])
    wide = sizes.width
    ffn_copies = start_in(
        ffn_pairs(mats, by_blocks, ffn_hbm, ffn_in_at, up_ref, down_ref, place_ref), sems, 0
    )
    attn_copies = start_in(
        attn_pairs(mats, by_blocks, attn_hbm, attn_in_at, qkv_ref, out_ref, place_ref),
        sems,
        len(ffn_copies),
    )
    vec[...] = jnp.zeros_like(vec)
    upper_vec[...] = jnp.zeros_like(upper_vec)
    gain = gains_ref[1, pl.ds(0, 1), :]
    gain_sum = jnp.zeros((1, wide), F32)
    bias_sum = jnp.zeros((1, wide), F32)
    for n in range(seqs):
        rows = pl.ds(n * sizes.rows, sizes.rows)
        _, scaled, inverse = norm_forward(
            inputs_ref[rows, :], gain, biases_ref[1, pl.ds(0, 1), :]
        )
        total, mem = merge_halo(last, n, gh_in_ref, gmem_in_ref, from_right_ref, from_left_ref)
        gain_sum = gain_sum + col_sum(total * scaled)
        bias_sum = bias_sum + col_sum(total)
        grad = gz_in_ref[rows, :] + norm_backward(total, scaled, inverse, gain)
        grad_ref[rows, :] = grad
        grad_low_ref[rows, :] = grad.astype(BF16)
        grad_mem_ref[pl.ds(n * sizes.segs, sizes.segs), :] = mem
    upper_vec[pl.ds(0, 1), :] = gain_sum
    upper_vec[pl.ds(2, 1), :] = bias_sum
    gain = gains_ref[0, pl.ds(1, 1), :]
    hidden, scaled, inverse = norm_forward(
        mixed_ref[...], gain, biases_ref[0, pl.ds(4, 1), :]
    )
    hidden_ref[...] = hidden.astype(BF16)
    grad_hidden_ref[...] = jnp.zeros_like(grad_hidden_ref)
    wait_all(ffn_copies)

    def body(c, carry):
        at_lane = pl.multiple_of(c * wide, wide)
        grad_hidden_ref[...] += ffn_back_step(
            sizes, c, wide, grad_low_ref[...], hidden_ref[...],
            active_ref[:, pl.ds(at_lane, wide)], slope_ref[:, pl.ds(at_lane, wide)].astype(F32),
            up_ref, down_ref, gup_ref, gdown_ref, vec,
        )
        return carry

    lax.fori_loop(0, sizes.ff // wide, body, 0)
    out_at = len(attn_copies) + len(ffn_copies)
    outs = start_out(
        ffn_pairs(mats, by_blocks, ffn_out, ffn_at, gup_ref, gdown_ref, place_ref), sems, out_at
    )
    grad_hidden = grad_hidden_ref[...]
    grad = grad_ref[...]
    vec[pl.ds(1, 1), :] = col_sum(grad_hidden * scaled)
    vec[pl.ds(6, 1), :] = col_sum(grad_hidden)
    vec[pl.ds(7, 1), :] = col_sum(grad)
    gz = grad + norm_backward(grad_hidden, scaled, inverse, gain)
    gz_ref[...] = gz
    wait_all(attn_copies)
    attn_back_stage(
        sizes, seqs, gz, grad_mem_ref, att_ref, proj_ref, probs_ref, z_ref, qkv_ref, out_ref,
        gqkv_ref, gout_ref, go_ref, gproj_ref, branch_ref, vec, gh_ref, gmem_ref, back_left_ref,
        back_right_ref,
    )
    outs = outs + start_out(
        attn_pairs(mats, by_blocks, attn_out, attn_at, gqkv_ref, gout_ref, place_ref),
        sems,
        out_at + len(outs),
    )
    wait_all(outs)


def frames_grad_kernel(
    sizes, seqs, frames_ref, gz_ref, gh_ref, gmem_ref, from_right_ref, from_left_ref, gains_ref,
    biases_ref, lower_vec, grad_ref, vec
):
    gain = gains_ref[0, pl.ds(0, 1), :]
    wide = sizes.width
    gain_sum = jnp.zeros((1, wide), F32)
    bias_sum = jnp.zeros((1, wide), F32)
    for n in range(seqs):
        _, scaled, inverse = norm_forward(
            frames_ref[n].astype(F32), gain, biases_ref[0, pl.ds(0, 1), :]
        )
        total, mem = merge_halo(sizes, n, gh_ref, gmem_ref, from_right_ref, from_left_ref)
        gain_sum = gain_sum + col_sum(total * scaled)
        bias_sum = bias_sum + col_sum(total)
        grad_ref[n] = (
            gz_ref[pl.ds(n * sizes.rows, sizes.rows), :]
            + norm_backward(total, scaled, inverse, gain)
            + segment_spread(sizes.rows, wide, mem * (1.0 / SEG_LEN))
        )
    vec[...] = lower_vec[...]
    vec[pl.ds(0, 1), :] = gain_sum
    vec[pl.ds(2, 1), :] = bias_sum


def shifted(value, axis, by):
    size = lax.axis_size(axis)
    pairs = [(i, i + by) for i in range(size) if 0 <= i + by < size]
    return lax.ppermute(value, axis, pairs)


def from_x(value, reps, by):
    chips = reps // 2
    pairs = [
        (2 * ((x + by) % chips) + core, 2 * x + core) for x in range(chips) for core in range(2)
    ]
    return lax.ppermute(value, "rep", pairs)


def to_x(value, reps, by):
    chips = reps // 2
    pairs = [
        (2 * x + core, 2 * ((x + by) % chips) + core) for x in range(chips) for core in range(2)
    ]
    return lax.ppermute(value, "rep", pairs)


def other_core(value, reps):
    return lax.ppermute(value, "rep", [(i, i ^ 1) for i in range(reps)])


def gather_blocks(shard, reps):
    here = lax.all_gather(shard, "seg", axis=0, tiled=False)
    chips = [here] + [from_x(here, reps, by) for by in range(1, reps // 2)]
    return chips + [other_core(block, reps) for block in chips]


def scatter_blocks(blocks, reps):
    chips = reps // 2
    received = [other_core(block, reps) for block in blocks[chips:]]
    sums = [
        (mine.astype(F32) + theirs.astype(F32)).astype(BF16)
        for mine, theirs in zip(blocks[:chips], received)
    ]
    total = sums[0].astype(F32)
    for by in range(1, chips):
        total = total + to_x(sums[by], reps, by).astype(F32)
    return lax.psum_scatter(total.astype(BF16), "seg", scatter_dimension=0, tiled=False)


def vmem_spec():
    return pl.BlockSpec(memory_space=pltpu.VMEM)


def smem_spec():
    return pl.BlockSpec(memory_space=pltpu.SMEM)


def hbm_spec():
    return pl.BlockSpec(memory_space=pl.ANY)


def call(body, in_specs, out_shapes, out_specs, scratch, args, flops=0, moved=0):
    return pl.pallas_call(
        body,
        in_specs=in_specs,
        out_shape=tuple(jax.ShapeDtypeStruct(shape, kind) for shape, kind in out_shapes),
        out_specs=tuple(out_specs),
        scratch_shapes=scratch,
        compiler_params=pltpu.CompilerParams(vmem_limit_bytes=VMEM_BYTES),
        cost_estimate=pl.CostEstimate(flops=flops, bytes_accessed=moved, transcendentals=0),
    )(*args)


def on_device(
    frames,
    utt_segments,
    out_grad,
    qkv_weight,
    out_weight,
    ffn_in_weight,
    ffn_out_weight,
    norm_gains,
    biases,
    ffn_bias,
):
    micros, groups, rows, width = frames.shape
    seqs = micros * groups
    ff = ffn_bias.shape[1]
    reps = lax.axis_size("rep")
    seg_count = lax.axis_size("seg")
    mats = Matrices(width, ff)
    by_blocks = width // reps == LANES and seg_count == BLOCKS
    first = Sizes(rows, width, ff, True)
    last = Sizes(rows, width, ff, False)
    own = seqs * rows
    mem_own = seqs * first.segs
    blocks_each = reps if by_blocks else 2

    seg_base = lax.axis_index("seg") * first.segs
    rep_at = lax.axis_index("rep")
    chips = reps // 2
    place = [seg_base, jnp.int32(first.segs * seg_count)]
    for core in range(2):
        for by in range(chips):
            there = lax.rem(rep_at // 2 + by, chips) * 2 + lax.bitwise_xor(rep_at % 2, core)
            place.append(there * LANES)
    place = jnp.stack([jnp.asarray(entry, jnp.int32) for entry in place])
    lengths = utt_segments.reshape(seqs, utt_segments.shape[2])
    starts = (jnp.cumsum(lengths, axis=1) - lengths).astype(jnp.int32)
    zero_bias = jnp.zeros((width,), F32)
    row_bias = jnp.stack(
        [jnp.concatenate([biases[l, 1], zero_bias, biases[l, 2]]) for l in range(LAYERS)]
    ).reshape(LAYERS, 1, 3 * width)

    frames_own = frames.reshape(seqs, rows, width)
    grads_own = out_grad.reshape(seqs, rows, width)
    far = MEM_LEN * SEG_LEN
    frames_left = shifted(frames_own[:, rows - far :], "seg", 1)
    frames_right = shifted(frames_own[:, :RIGHT_ROWS], "seg", -1)

    attn_rows, ffn_rows = mats.attn_rows, mats.ffn_rows
    if by_blocks:
        counts = [(0, 0, 1, 0), (2, 0, 2, attn_rows)]
        packed = call(
            lambda *refs: pack_kernel(counts, *refs),
            [vmem_spec()] * 4,
            [((attn_rows, LANES), BF16), ((ffn_rows, LANES), BF16),
             ((attn_rows + ffn_rows, LANES), BF16)],
            [vmem_spec()] * 3,
            [],
            (qkv_weight, out_weight, ffn_in_weight, ffn_out_weight),
        )
        gathered = [gather_blocks(shard, reps) for shard in packed]
        first_attn, first_ffn, last_all = gathered
        last_attn_at, last_ffn_at = 0, attn_rows
        grad_outs = [((BLOCKS, attn_rows + ffn_rows, LANES), BF16)] * reps
        copies_in = reps * (3 + mats.down_parts)
    else:
        whole = []
        for member, shape in zip(
            (qkv_weight, out_weight, ffn_in_weight, ffn_out_weight),
            (mats.qkv, mats.out, mats.up, mats.down),
        ):
            member = lax.all_gather(member, "rep", axis=1, tiled=True)
            member = lax.all_gather(member, "seg", axis=2, tiled=True)
            whole.append(jnp.swapaxes(member, 1, 2).reshape((LAYERS,) + shape))
        first_attn = [whole[0][0], whole[1][0]]
        first_ffn = [whole[2][0], whole[3][0]]
        last_all = [member[1] for member in whole]
        last_attn_at, last_ffn_at = 0, 0
        grad_outs = [(shape, BF16) for shape in (mats.qkv, mats.out, mats.up, mats.down)]
        copies_in = 4
    dma = pltpu.SemaphoreType.DMA

    z0, proj0, probs0, att0, mixed0, mem1 = call(
        lambda *refs: first_attn_kernel(
            first, seqs, mats, by_blocks, len(first_attn), 0, *refs
        ),
        [smem_spec()] * 2 + [vmem_spec()] * 6 + [hbm_spec()] * len(first_attn),
        [
            ((seqs * first.ext, width), BF16),
            ((seqs * first.ext, 3 * width), BF16),
            ((seqs * first.pairs, 2 * first.queries, first.keys), F32),
            ((seqs * first.queries, width), BF16),
            ((own, width), F32),
            ((mem_own, width), F32),
        ],
        [vmem_spec()] * 6,
        [
            pltpu.VMEM(mats.qkv, BF16),
            pltpu.VMEM(mats.out, BF16),
            pltpu.VMEM((seqs, first.queries, first.keys), F32),
            dma((copies_in,)),
        ],
        (place, starts, frames_own, frames_left, frames_right, norm_gains, biases, row_bias[0])
        + tuple(first_attn),
        flops=2 * own * 4 * width * width,
        moved=8 * width * width,
    )
    x1, active0, slope0, low1, send_right, send_left = call(
        lambda *refs: first_ffn_kernel(first, seqs, mats, by_blocks, len(first_ffn), 0, *refs),
        [smem_spec()] + [vmem_spec()] * 5 + [hbm_spec()] * len(first_ffn),
        [
            ((own, width), F32),
            ((own, ff), BF16),
            ((own, ff), BF16),
            ((own, width), BF16),
            ((seqs, BACK_ROWS, width), BF16),
            ((seqs, RIGHT_ROWS, width), BF16),
        ],
        [vmem_spec()] * 6,
        [
            pltpu.VMEM(mats.up, BF16),
            pltpu.VMEM(mats.down, BF16),
            pltpu.VMEM((own, width), BF16),
            dma((copies_in,)),
        ],
        (place, mixed0, mem1, norm_gains, biases, ffn_bias) + tuple(first_ffn),
        flops=2 * own * 2 * width * ff,
        moved=4 * width * ff,
    )
    left1 = shifted(send_right, "seg", 1)
    right1 = shifted(send_left, "seg", -1)

    vec_shape = (TILE, width)
    outs = call(
        lambda *refs: last_layer_kernel(
            last, seqs, mats, by_blocks, len(last_all), last_attn_at, last_ffn_at, *refs
        ),
        [smem_spec()] * 2 + [vmem_spec()] * 10 + [hbm_spec()] * len(last_all),
        [
            ((seqs, rows, width), F32),
            ((own, width), F32),
            ((own, width), F32),
            ((mem_own, width), F32),
            ((seqs, BACK_ROWS, width), BF16),
            ((seqs, RIGHT_ROWS, width), BF16),
            (vec_shape, F32),
        ]
        + grad_outs,
        [vmem_spec()] * 7 + [hbm_spec()] * len(grad_outs),
        [
            pltpu.VMEM(mats.qkv, BF16),
            pltpu.VMEM(mats.out, BF16),
            pltpu.VMEM(mats.up, BF16),
            pltpu.VMEM(mats.down, BF16),
            pltpu.VMEM(mats.qkv, BF16),
            pltpu.VMEM(mats.out, BF16),
            pltpu.VMEM(mats.up, BF16),
            pltpu.VMEM(mats.down, BF16),
            pltpu.VMEM((seqs, last.queries, last.keys), F32),
            pltpu.VMEM((seqs * last.ext, width), BF16),
            pltpu.VMEM((seqs * last.ext, 3 * width), BF16),
            pltpu.VMEM((seqs * last.pairs, 2 * last.queries, last.keys), F32),
            pltpu.VMEM((seqs * last.queries, width), BF16),
            pltpu.VMEM((own, width), BF16),
            pltpu.VMEM((seqs * last.queries, width), BF16),
            pltpu.VMEM((seqs * last.ext, 3 * width), BF16),
            pltpu.VMEM((seqs * last.queries, width), BF16),
            pltpu.VMEM((own, width), BF16),
            pltpu.VMEM((own, width), F32),
            dma((2 * copies_in,)),
        ],
        (place, starts, low1, left1, right1, mem1, x1, grads_own, norm_gains, biases, ffn_bias,
         row_bias[1]) + tuple(last_all),
        flops=6 * own * (4 * width * width + 2 * width * ff),
        moved=4 * (4 * width * width + 2 * width * ff),
    )
    encoded, gz1, gh1, gmem1, back_left1, back_right1, vec1 = outs[:7]
    grad_blocks1 = outs[7:]
    from_right1 = shifted(back_left1, "seg", -1)
    from_left1 = shifted(back_right1, "seg", 1)

    outs = call(
        lambda *refs: first_back_kernel(
            last, first, seqs, mats, by_blocks, (len(first_attn), len(first_ffn), len(grad_outs)),
            (0, 0, last_attn_at, last_ffn_at), *refs
        ),
        [smem_spec()] + [vmem_spec()] * 15 + [hbm_spec()] * (len(first_attn) + len(first_ffn)),
        [
            ((own, width), F32),
            ((own, width), F32),
            ((mem_own, width), F32),
            ((seqs, BACK_ROWS, width), BF16),
            ((seqs, RIGHT_ROWS, width), BF16),
            (vec_shape, F32),
            (vec_shape, F32),
        ]
        + grad_outs,
        [vmem_spec()] * 7 + [hbm_spec()] * len(grad_outs),
        [
            pltpu.VMEM(mats.qkv, BF16),
            pltpu.VMEM(mats.out, BF16),
            pltpu.VMEM(mats.up, BF16),
            pltpu.VMEM(mats.down, BF16),
            pltpu.VMEM(mats.qkv, BF16),
            pltpu.VMEM(mats.out, BF16),
            pltpu.VMEM(mats.up, BF16),
            pltpu.VMEM(mats.down, BF16),
            pltpu.VMEM((own, width), BF16),
            pltpu.VMEM((seqs * first.queries, width), BF16),
            pltpu.VMEM((seqs * first.ext, 3 * width), BF16),
            pltpu.VMEM((seqs * first.queries, width), BF16),
            pltpu.VMEM((own, width), BF16),
            pltpu.VMEM((own, width), F32),
            pltpu.VMEM((own, width), F32),
            pltpu.VMEM((mem_own, width), F32),
            dma((2 * copies_in,)),
        ],
        (place, x1, gz1, gh1, gmem1, from_right1, from_left1, mixed0, active0, slope0, att0, probs0,
         proj0, z0, norm_gains, biases) + tuple(first_attn) + tuple(first_ffn),
        flops=4 * own * (4 * width * width + 2 * width * ff),
        moved=4 * (4 * width * width + 2 * width * ff),
    )
    gz0, gh0, gmem0, back_left0, back_right0, upper_vec, vec0 = outs[:7]
    grad_blocks0 = outs[7:]
    from_right0 = shifted(back_left0, "seg", -1)
    from_left0 = shifted(back_right0, "seg", 1)
    frames_grad, vec0 = call(
        lambda *refs: frames_grad_kernel(first, seqs, *refs),
        [vmem_spec()] * 9,
        [((seqs, rows, width), F32), (vec_shape, F32)],
        [vmem_spec()] * 2,
        [],
        (frames_own, gz0, gh0, gmem0, from_right0, from_left0, norm_gains, biases, vec0),
    )

    shapes = [
        member.shape for member in (qkv_weight, out_weight, ffn_in_weight, ffn_out_weight)
    ]
    if by_blocks:
        reduced1 = scatter_blocks(grad_blocks1, reps)
        reduced0 = scatter_blocks(grad_blocks0, reps)
        places = [(0, 0, 0, attn_rows), (1, 0, 1, attn_rows)]
        reduced = call(
            lambda *refs: unpack_kernel(places, 2, *refs),
            [vmem_spec()] * 2,
            [(shape, F32) for shape in shapes],
            [vmem_spec()] * 4,
            [],
            (reduced0, reduced1),
        )
    else:
        reduced = []
        for member0, member1 in zip(grad_blocks0, grad_blocks1):
            both = jnp.stack([member0, member1]).reshape(LAYERS, -1, member0.shape[2])
            both = jnp.swapaxes(both, 1, 2)
            both = lax.psum_scatter(both, "seg", scatter_dimension=2, tiled=True)
            both = lax.psum_scatter(both, "rep", scatter_dimension=1, tiled=True)
            reduced.append(both.astype(F32))

    small = lax.psum(jnp.stack([vec0, vec1 + upper_vec]), ("seg", "rep"))
    return (
        encoded.reshape(frames.shape),
        frames_grad.reshape(frames.shape),
        reduced[0],
        reduced[1],
        reduced[2],
        reduced[3],
        small[:, 0:2],
        small[:, 2:8],
        small[:, 8:12].reshape(ffn_bias.shape),
    )


def solution(mesh):
    in_specs = (
        P(None, "rep", "seg", None),
        P(None, "rep", None),
        P(None, "rep", "seg", None),
        P(None, "rep", "seg"),
        P(None, "rep", "seg"),
        P(None, "rep", "seg"),
        P(None, "rep", "seg"),
        P(),
        P(),
        P(),
    )
    out_specs = (
        P(None, "rep", "seg", None),
        P(None, "rep", "seg", None),
        P(None, "rep", "seg"),
        P(None, "rep", "seg"),
        P(None, "rep", "seg"),
        P(None, "rep", "seg"),
        P(),
        P(),
        P(),
    )
    return jax.shard_map(
        on_device, mesh=mesh, in_specs=in_specs, out_specs=out_specs, check_vma=False
    )
```

```python
import jax
import jax.numpy as jnp
from jax import lax
from jax.experimental import pallas as pl
from jax.experimental.pallas import tpu as pltpu
from jax.sharding import PartitionSpec as P

HEADS = 8
SEG_LEN = 16
LEFT_LEN = 30
RIGHT_LEN = 4
MEM_LEN = 4
LAYERS = 2

EPS = 1e-05
ROOT_HALF = 0.7071067811865476
INV_ROOT_TWO_PI = 0.3989422804014327

LANES = 128
TILE = 16
RIGHT_ROWS = 16
LEFT_ROWS = 32
MEM_ROWS = 16
BACK_ROWS = LEFT_ROWS + MEM_ROWS
CHIPS_Z = 4
CHIPS_Y = 2
BLOCKS = CHIPS_Z * CHIPS_Y
VMEM_BYTES = 56 * 1024 * 1024

BF16 = jnp.bfloat16
F32 = jnp.float32


def nn(a, b):
    return lax.dot_general(a, b, (((1,), (0,)), ((), ())), preferred_element_type=F32)


def nt(a, b):
    return lax.dot_general(a, b, (((1,), (1,)), ((), ())), preferred_element_type=F32)


def tn(a, b):
    return lax.dot_general(a, b, (((0,), (0,)), ((), ())), preferred_element_type=F32)


def col_sum(value):
    return jnp.sum(value, axis=0, keepdims=True)


def norm_forward(inputs, gain, bias):
    center = inputs - jnp.mean(inputs, axis=1, keepdims=True)
    inverse = lax.rsqrt(jnp.mean(center * center, axis=1, keepdims=True) + EPS)
    scaled = center * inverse
    return scaled * gain + bias, scaled, inverse


def norm_backward(grad_in, scaled, inverse, gain):
    grad_scaled = grad_in * gain
    return inverse * (
        grad_scaled
        - jnp.mean(grad_scaled, axis=1, keepdims=True)
        - scaled * jnp.mean(grad_scaled * scaled, axis=1, keepdims=True)
    )


def segment_mean(inputs):
    rows, width = inputs.shape
    return jnp.mean(inputs.reshape(rows // SEG_LEN, SEG_LEN, width), axis=1)


def segment_spread(rows, width, per_segment):
    segs = rows // SEG_LEN
    return jnp.broadcast_to(per_segment[:, None, :], (segs, SEG_LEN, width)).reshape(rows, width)


def identity(size):
    row = lax.broadcasted_iota(jnp.int32, (size, size), 0)
    col = lax.broadcasted_iota(jnp.int32, (size, size), 1)
    return (row == col).astype(F32).astype(BF16)


class Sizes:
    def __init__(self, rows, width, ff, with_summary):
        self.rows = rows
        self.width = width
        self.ff = ff
        self.segs = rows // SEG_LEN
        self.top = TILE if with_summary else 0
        self.keys = rows + RIGHT_ROWS + LEFT_ROWS + MEM_ROWS
        self.ext = self.top + self.keys
        self.queries = self.top + rows
        self.right_at = self.top + rows
        self.left_at = self.right_at + RIGHT_ROWS
        self.mem_at = self.left_at + LEFT_ROWS
        self.pairs = width // LANES


class Matrices:
    def __init__(self, width, ff):
        self.qkv = (CHIPS_Z, CHIPS_Y, 3 * width // BLOCKS, width)
        self.out = (CHIPS_Z, CHIPS_Y, width // BLOCKS, width)
        self.up = (CHIPS_Z, CHIPS_Y, ff // BLOCKS, width)
        self.down = (CHIPS_Z, CHIPS_Y, width // BLOCKS, ff)
        self.down_parts = ff // width
        self.attn_rows = self.qkv[2] + self.out[2]
        self.ffn_rows = self.up[2] + self.down_parts * self.down[2]


def attn_pairs(mats, by_blocks, hbm, first, qkv_ref, out_ref, place_ref):
    if not by_blocks:
        return [(hbm[0], qkv_ref), (hbm[1], out_ref)]
    pairs = []
    high = mats.qkv[2]
    for k, block in enumerate(hbm):
        row = place_ref[2 + 2 * k]
        lane = pl.multiple_of(place_ref[3 + 2 * k], LANES)
        pairs.append(
            (block.at[:, pl.ds(first, high), :], qkv_ref.at[:, row, :, pl.ds(lane, LANES)])
        )
        pairs.append(
            (
                block.at[:, pl.ds(first + high, mats.out[2]), :],
                out_ref.at[:, row, :, pl.ds(lane, LANES)],
            )
        )
    return pairs


def ffn_pairs(mats, by_blocks, hbm, first, up_ref, down_ref, place_ref):
    if not by_blocks:
        return [(hbm[0], up_ref), (hbm[1], down_ref)]
    pairs = []
    high = mats.up[2]
    low = mats.down[2]
    for k, block in enumerate(hbm):
        row = place_ref[2 + 2 * k]
        lane = pl.multiple_of(place_ref[3 + 2 * k], LANES)
        pairs.append(
            (block.at[:, pl.ds(first, high), :], up_ref.at[:, row, :, pl.ds(lane, LANES)])
        )
        for part in range(mats.down_parts):
            there = pl.multiple_of(
                place_ref[3 + 2 * k] * mats.down_parts + part * LANES, LANES
            )
            pairs.append(
                (
                    block.at[:, pl.ds(first + high + part * low, low), :],
                    down_ref.at[:, row, :, pl.ds(there, LANES)],
                )
            )
    return pairs


def start_in(pairs, sems, at):
    copies = [pltpu.make_async_copy(s, d, sems.at[at + i]) for i, (s, d) in enumerate(pairs)]
    for copy in copies:
        copy.start()
    return copies


def start_out(pairs, sems, at):
    copies = [pltpu.make_async_copy(d, s, sems.at[at + i]) for i, (s, d) in enumerate(pairs)]
    for copy in copies:
        copy.start()
    return copies


def wait_all(copies):
    for copy in copies:
        copy.wait()


def fill_mask(sizes, seqs, starts_ref, place_ref, mask_ref):
    shape = (sizes.queries, sizes.keys)
    row = lax.broadcasted_iota(jnp.int32, shape, 0)
    col = lax.broadcasted_iota(jnp.int32, shape, 1)
    base = place_ref[0]
    total = place_ref[1]
    query = jnp.where(row < sizes.top, row, lax.shift_right_arithmetic(row - sizes.top, 4))
    left_at = sizes.rows + RIGHT_ROWS
    mem_at = left_at + LEFT_ROWS
    spot = jnp.where(col < left_at, col, col - mem_at)
    mem_seg = jnp.where(col < mem_at + sizes.segs, col - mem_at, col - mem_at - 2 * sizes.segs)
    key_seg = jnp.where(col < mem_at, lax.shift_right_arithmetic(spot, 4), mem_seg)
    near = (
        (key_seg == query)
        | ((spot >= query * SEG_LEN - LEFT_LEN) & (spot < query * SEG_LEN))
        | ((key_seg == query + 1) & (spot < query * SEG_LEN + SEG_LEN + RIGHT_LEN))
    )
    recent = (key_seg >= query - MEM_LEN) & (key_seg < query) & (row >= sizes.top)
    allowed = ((col < mem_at) & near) | ((col >= mem_at) & recent)
    key_abs = key_seg + base
    query_abs = query + base
    allowed = allowed & (key_abs >= 0) & (key_abs < total)
    if sizes.top:
        allowed = allowed & ((row < sizes.segs) | (row >= sizes.top))
    for n in range(seqs):
        key_owner = jnp.zeros(shape, jnp.int32)
        query_owner = jnp.zeros(shape, jnp.int32)
        for u in range(starts_ref.shape[1]):
            first = starts_ref[n, u]
            key_owner = key_owner + (key_abs >= first).astype(jnp.int32)
            query_owner = query_owner + (query_abs >= first).astype(jnp.int32)
        mask_ref[n] = jnp.where(allowed & (key_owner == query_owner), 0.0, -1e30)


def half_masks():
    lane = lax.broadcasted_iota(jnp.int32, (1, LANES), 1)
    even = (lane < LANES // 2).astype(F32)
    return even.astype(BF16), (1.0 - even).astype(BF16), lane < LANES // 2


def project(sizes, z_ref, qkv_ref, row_bias_ref, proj_ref):
    step = CHIPS_Z // 2
    for c in range(2):
        block = qkv_ref[pl.ds(c * step, step)].reshape(-1, sizes.width)
        wide = block.shape[0]
        made = nt(z_ref[...], block) + row_bias_ref[:, pl.ds(c * wide, wide)]
        proj_ref[:, pl.ds(c * wide, wide)] = made.astype(BF16)


def split_heads(sizes, ref, first, rows, lane):
    return ref[pl.ds(first, rows), pl.ds(lane, LANES)]


def attend(sizes, seqs, proj_ref, mask_ref, probs_ref, att_ref):
    even, odd, is_even = half_masks()
    scale = (sizes.width // HEADS) ** (-0.5)
    count = sizes.queries

    def body(p, carry):
        for n in range(seqs):
            lane = pl.multiple_of(p * LANES, LANES)
            query = proj_ref[pl.ds(n * sizes.ext, count), pl.ds(lane, LANES)]
            first = n * sizes.ext + sizes.top
            key = proj_ref[pl.ds(first, sizes.keys), pl.ds(sizes.width + lane, LANES)]
            value = proj_ref[pl.ds(first, sizes.keys), pl.ds(2 * sizes.width + lane, LANES)]
            scores = nt(jnp.concatenate([query * even, query * odd], axis=0), key) * scale
            outs = []
            for half in range(2):
                part = scores[half * count : (half + 1) * count] + mask_ref[n]
                part = jnp.exp(part - jnp.max(part, axis=1, keepdims=True))
                part = part * (1.0 / jnp.sum(part, axis=1, keepdims=True))
                probs_ref[n * sizes.pairs + p, pl.ds(half * count, count), :] = part
                outs.append(nn(part.astype(BF16), value))
            att_ref[pl.ds(n * count, count), pl.ds(lane, LANES)] = jnp.where(
                is_even, outs[0], outs[1]
            ).astype(BF16)
        return carry

    lax.fori_loop(0, sizes.pairs, body, 0)


def attend_back(sizes, seqs, proj_ref, probs_ref, go_ref, gproj_ref):
    even, odd, is_even = half_masks()
    scale = (sizes.width // HEADS) ** (-0.5)
    count = sizes.queries
    wide = sizes.width
    for n in range(seqs):
        base = n * sizes.ext
        rest = sizes.ext - count
        gproj_ref[pl.ds(base + count, rest), pl.ds(0, wide)] = jnp.zeros((rest, wide), BF16)
        if sizes.top:
            gproj_ref[pl.ds(base, sizes.top), pl.ds(wide, 2 * wide)] = jnp.zeros(
                (sizes.top, 2 * wide), BF16
            )

    def body(p, carry):
        for n in range(seqs):
            lane = pl.multiple_of(p * LANES, LANES)
            base = n * sizes.ext
            first = base + sizes.top
            query = proj_ref[pl.ds(base, count), pl.ds(lane, LANES)]
            key = proj_ref[pl.ds(first, sizes.keys), pl.ds(wide + lane, LANES)]
            value = proj_ref[pl.ds(first, sizes.keys), pl.ds(2 * wide + lane, LANES)]
            grad = go_ref[pl.ds(n * count, count), pl.ds(lane, LANES)]
            queries = jnp.concatenate([query * even, query * odd], axis=0)
            grads = jnp.concatenate([grad * even, grad * odd], axis=0)
            probs = probs_ref[n * sizes.pairs + p]
            grad_values = tn(probs.astype(BF16), grads)
            grad_probs = nt(grads, value)
            weighted = grad_probs * probs
            grad_scores = (
                (weighted - probs * jnp.sum(weighted, axis=1, keepdims=True)) * scale
            ).astype(BF16)
            grad_keys = tn(grad_scores, queries)
            grad_query = jnp.where(
                is_even, nn(grad_scores[:count], key), nn(grad_scores[count:], key)
            )
            gproj_ref[pl.ds(base, count), pl.ds(lane, LANES)] = grad_query.astype(BF16)
            gproj_ref[pl.ds(first, sizes.keys), pl.ds(wide + lane, LANES)] = grad_keys.astype(BF16)
            gproj_ref[pl.ds(first, sizes.keys), pl.ds(2 * wide + lane, LANES)] = (
                grad_values.astype(BF16)
            )
        return carry

    lax.fori_loop(0, sizes.pairs, body, 0)


def gelu_both(upward):
    half = 0.5 * (1.0 + lax.erf(upward * ROOT_HALF))
    slope = half + upward * jnp.exp(-0.5 * upward * upward) * INV_ROOT_TWO_PI
    return upward * half, slope


def up_block(up_ref, c, wide):
    step = wide // (up_ref.shape[1] * up_ref.shape[2])
    return up_ref[pl.ds(c * step, step)].reshape(-1, up_ref.shape[3])


def down_block(down_ref, c, wide):
    at = pl.multiple_of(c * wide, wide)
    return down_ref[:, :, :, pl.ds(at, wide)].reshape(-1, wide)


def ffn_back_step(
    sizes, c, wide, grad_low, hidden_low, active, slope, up_ref, down_ref, gup_ref, gdown_ref, vec
):
    at = pl.multiple_of(c * wide, wide)
    up = up_block(up_ref, c, wide)
    down = down_block(down_ref, c, wide)
    grad_active = nn(grad_low, down)
    grad_up_f = grad_active * slope
    grad_up = grad_up_f.astype(BF16)
    gdown_ref[:, :, :, pl.ds(at, wide)] = (
        tn(grad_low, active).astype(BF16).reshape(gdown_ref.shape[:3] + (wide,))
    )
    step = wide // (gup_ref.shape[1] * gup_ref.shape[2])
    gup_ref[pl.ds(c * step, step)] = (
        tn(grad_up, hidden_low).astype(BF16).reshape((step,) + gup_ref.shape[1:])
    )
    vec[pl.ds(8 + c, 1), :] = col_sum(grad_up.astype(F32))
    return nn(grad_up, up)


def attn_back_stage(
    sizes, seqs, gz, grad_mem_ref, att_ref, proj_ref, probs_ref, z_ref, qkv_ref, out_ref,
    gqkv_ref, gout_ref, go_ref, gproj_ref, branch_ref, vec, gh_ref, gmem_ref, back_left_ref,
    back_right_ref,
):
    wide = sizes.width
    count = sizes.queries
    bias_out = col_sum(gz)
    for n in range(seqs):
        if sizes.top:
            mem_grad = grad_mem_ref[pl.ds(n * sizes.segs, sizes.segs), :]
            bias_out = bias_out + col_sum(mem_grad)
            branch_ref[pl.ds(n * count, sizes.top), :] = jnp.concatenate(
                [mem_grad, jnp.zeros((sizes.top - sizes.segs, wide), F32)], axis=0
            ).astype(BF16)
        branch_ref[pl.ds(n * count + sizes.top, sizes.rows), :] = gz[
            n * sizes.rows : (n + 1) * sizes.rows
        ].astype(BF16)
    vec[pl.ds(5, 1), :] = bias_out
    branch = branch_ref[...]
    gout_ref[...] = tn(branch, att_ref[...]).astype(BF16).reshape(gout_ref.shape)
    go_ref[...] = nn(branch, out_ref[...].reshape(-1, wide)).astype(BF16)
    attend_back(sizes, seqs, proj_ref, probs_ref, go_ref, gproj_ref)
    vec[pl.ds(3, 1), :] = col_sum(gproj_ref[:, pl.ds(0, wide)].astype(F32))
    vec[pl.ds(4, 1), :] = col_sum(gproj_ref[:, pl.ds(2 * wide, wide)].astype(F32))
    grad_ext = nn(gproj_ref[...], qkv_ref[...].reshape(-1, wide))
    for n in range(seqs):
        base = n * sizes.ext
        own = grad_ext[base + sizes.top : base + sizes.top + sizes.rows]
        if sizes.top:
            spread = grad_ext[base : base + sizes.segs] * (1.0 / SEG_LEN)
            own = own + segment_spread(sizes.rows, wide, spread)
        gh_ref[pl.ds(n * sizes.rows, sizes.rows), :] = own
        mem = base + sizes.mem_at
        gmem_ref[pl.ds(n * sizes.segs, sizes.segs), :] = grad_ext[mem : mem + sizes.segs]
        left = base + sizes.left_at
        back_left_ref[n] = grad_ext[left : left + BACK_ROWS].astype(BF16)
        right = base + sizes.right_at
        back_right_ref[n] = grad_ext[right : right + RIGHT_ROWS].astype(BF16)
    step = CHIPS_Z // 2
    part = gqkv_ref.shape[1] * gqkv_ref.shape[2] * step
    for c in range(2):
        gqkv_ref[pl.ds(c * step, step)] = (
            tn(gproj_ref[:, pl.ds(c * part, part)], z_ref[...])
            .astype(BF16)
            .reshape((step,) + gqkv_ref.shape[1:])
        )


def merge_halo(sizes, n, gh_ref, gmem_ref, from_right_ref, from_left_ref):
    first = n * sizes.rows
    back = from_right_ref[n].astype(F32)
    head = gh_ref[pl.ds(first, RIGHT_ROWS), :] + from_left_ref[n].astype(F32)
    middle = gh_ref[pl.ds(first + RIGHT_ROWS, sizes.rows - RIGHT_ROWS - LEFT_ROWS), :]
    tail = gh_ref[pl.ds(first + sizes.rows - LEFT_ROWS, LEFT_ROWS), :] + back[:LEFT_ROWS]
    mem = gmem_ref[pl.ds(n * sizes.segs, sizes.segs), :] + back[LEFT_ROWS + sizes.segs :]
    return jnp.concatenate([head, middle, tail], axis=0), mem


def pack_kernel(qkv_ref, out_ref, up_ref, down_ref, *packed):
    eye = identity(LANES)
    high, wide, low = qkv_ref.shape[1], out_ref.shape[1], down_ref.shape[1]
    up = up_ref.shape[2]
    for layer, ref in enumerate(packed):
        ref[pl.ds(0, high), :] = qkv_ref[layer]
        ref[pl.ds(high, wide), :] = out_ref[layer]
        ref[pl.ds(high + wide, up), :] = tn(up_ref[layer], eye).astype(BF16)
        for part in range(down_ref.shape[2] // LANES):
            ref[pl.ds(high + wide + up + part * low, low), :] = down_ref[
                layer, :, pl.ds(part * LANES, LANES)
            ]


def unpack_kernel(each, *refs):
    sources, (qkv_ref, out_ref, up_ref, down_ref) = refs[:-4], refs[-4:]
    eye = identity(LANES)
    high, wide, low = qkv_ref.shape[1], out_ref.shape[1], down_ref.shape[1]
    up = up_ref.shape[2]
    for layer in range(qkv_ref.shape[0]):
        parts = sources[layer * each : (layer + 1) * each]

        def total(first, rows):
            value = parts[0][pl.ds(first, rows), :].astype(F32)
            for part in parts[1:]:
                value = value + part[pl.ds(first, rows), :].astype(F32)
            return value

        qkv_ref[layer] = total(0, high)
        out_ref[layer] = total(high, wide)
        up_ref[layer] = nt(eye, total(high + wide, up).astype(BF16))
        for part in range(down_ref.shape[2] // LANES):
            down_ref[layer, :, pl.ds(part * LANES, LANES)] = total(
                high + wide + up + part * low, low
            )


def stack_kernel(count, place_ref, *refs):
    sources, out_ref, sems = refs[:count], refs[count], refs[count + 1]
    copies = []
    for k, source in enumerate(sources):
        spot = lax.rem(place_ref[0] + count - k, count)
        copies.append(pltpu.make_async_copy(source, out_ref.at[spot], sems.at[k]))
    for copy in copies:
        copy.start()
    wait_all(copies)


def split_kernel(count, place_ref, mine_ref, theirs_ref, *outs):
    for k, out in enumerate(outs):
        spot = lax.rem(place_ref[0] + k, count)
        out[...] = (mine_ref[spot].astype(F32) + theirs_ref[spot].astype(F32)).astype(BF16)


def first_attn_kernel(
    sizes, seqs, mats, by_blocks, count_in, at, place_ref, starts_ref, frames_ref, left_ref,
    right_ref, gains_ref, biases_ref, row_bias_ref, *refs
):
    hbm = refs[:count_in]
    z_ref, proj_ref, probs_ref, att_ref, mixed_ref, mem_ref, qkv_ref, out_ref, mask_ref, sems = (
        refs[count_in:]
    )
    wide = sizes.width
    copies = start_in(
        attn_pairs(mats, by_blocks, hbm, at, qkv_ref, out_ref, place_ref), sems, 0
    )
    gain = gains_ref[0, pl.ds(0, 1), :]
    bias = biases_ref[0, pl.ds(0, 1), :]
    pad = jnp.zeros((TILE - sizes.segs, wide), F32)
    for n in range(seqs):
        own = frames_ref[n].astype(F32)
        before = left_ref[n].astype(F32)
        hidden = norm_forward(own, gain, bias)[0]
        halo = norm_forward(before[before.shape[0] - LEFT_ROWS :], gain, bias)[0]
        after = norm_forward(right_ref[n].astype(F32), gain, bias)[0]
        memory = jnp.concatenate(
            [
                segment_mean(own),
                jnp.zeros((sizes.segs - before.shape[0] // SEG_LEN, wide), F32),
                segment_mean(before),
            ],
            axis=0,
        )
        base = n * sizes.ext
        z_ref[pl.ds(base, sizes.top), :] = jnp.concatenate(
            [segment_mean(hidden), pad], axis=0
        ).astype(BF16)
        z_ref[pl.ds(base + sizes.top, sizes.rows), :] = hidden.astype(BF16)
        z_ref[pl.ds(base + sizes.right_at, RIGHT_ROWS), :] = after.astype(BF16)
        z_ref[pl.ds(base + sizes.left_at, LEFT_ROWS), :] = halo.astype(BF16)
        z_ref[pl.ds(base + sizes.mem_at, MEM_ROWS), :] = memory.astype(BF16)
    fill_mask(sizes, seqs, starts_ref, place_ref, mask_ref)
    wait_all(copies)
    project(sizes, z_ref, qkv_ref, row_bias_ref, proj_ref)
    attend(sizes, seqs, proj_ref, mask_ref, probs_ref, att_ref)
    mixed = nt(att_ref[...], out_ref[...].reshape(-1, wide)) + biases_ref[0, pl.ds(3, 1), :]
    for n in range(seqs):
        base = n * sizes.queries
        mem_ref[pl.ds(n * sizes.segs, sizes.segs), :] = mixed[base : base + sizes.segs]
        mixed_ref[pl.ds(n * sizes.rows, sizes.rows), :] = (
            frames_ref[n].astype(F32) + mixed[base + sizes.top : base + sizes.top + sizes.rows]
        )


def first_ffn_kernel(
    sizes, seqs, mats, by_blocks, count_in, at, place_ref, mixed_ref, mem_ref, gains_ref,
    biases_ref, ffn_bias_ref, *refs
):
    hbm = refs[:count_in]
    (
        next_ref, active_ref, slope_ref, low_ref, send_right_ref, send_left_ref, up_ref, down_ref,
        hidden_ref, sems,
    ) = refs[count_in:]
    copies = start_in(ffn_pairs(mats, by_blocks, hbm, at, up_ref, down_ref, place_ref), sems, 0)
    mixed = mixed_ref[...]
    hidden, _, _ = norm_forward(mixed, gains_ref[0, pl.ds(1, 1), :], biases_ref[0, pl.ds(4, 1), :])
    hidden_ref[...] = hidden.astype(BF16)
    next_ref[...] = mixed + biases_ref[0, pl.ds(5, 1), :]
    wait_all(copies)
    wide = sizes.width

    def body(c, carry):
        at_lane = pl.multiple_of(c * wide, wide)
        upward = nt(hidden_ref[...], up_block(up_ref, c, wide))
        upward = upward + ffn_bias_ref[pl.ds(0, 1), pl.ds(at_lane, wide)]
        active, slope = gelu_both(upward)
        active = active.astype(BF16)
        active_ref[:, pl.ds(at_lane, wide)] = active
        slope_ref[:, pl.ds(at_lane, wide)] = slope.astype(BF16)
        next_ref[...] += nt(active, down_block(down_ref, c, wide))
        return carry

    lax.fori_loop(0, sizes.ff // wide, body, 0)
    low, _, _ = norm_forward(
        next_ref[...], gains_ref[1, pl.ds(0, 1), :], biases_ref[1, pl.ds(0, 1), :]
    )
    low = low.astype(BF16)
    low_ref[...] = low
    for n in range(seqs):
        base = n * sizes.rows
        send_right_ref[n, pl.ds(0, LEFT_ROWS), :] = low[
            base + sizes.rows - LEFT_ROWS : base + sizes.rows
        ]
        send_right_ref[n, pl.ds(LEFT_ROWS, MEM_ROWS), :] = jnp.concatenate(
            [
                mem_ref[pl.ds(n * sizes.segs, sizes.segs), :],
                jnp.zeros((MEM_ROWS - sizes.segs, wide), F32),
            ],
            axis=0,
        ).astype(BF16)
        send_left_ref[n] = low[base : base + RIGHT_ROWS]


def last_layer_kernel(
    sizes, seqs, mats, by_blocks, count_in, attn_at, ffn_at, place_ref, starts_ref, low_ref,
    left_ref, right_ref, mem_ref, inputs_ref, out_grad_ref, gains_ref, biases_ref, ffn_bias_ref,
    row_bias_ref, *refs
):
    hbm = refs[:count_in]
    count_out = count_in
    (encoded_ref, gz_ref, gh_ref, gmem_ref, back_left_ref, back_right_ref, vec) = refs[
        count_in : count_in + 7
    ]
    hbm_out = refs[count_in + 7 : count_in + 7 + count_out]
    (
        qkv_ref, out_ref, up_ref, down_ref, gqkv_ref, gout_ref, gup_ref, gdown_ref, mask_ref,
        z_ref, proj_ref, probs_ref, att_ref, hidden_ref, go_ref, gproj_ref, branch_ref,
        grad_low_ref, grad_hidden_ref, sems,
    ) = refs[count_in + 7 + count_out :]
    half = count_in if by_blocks else 2
    attn_hbm, ffn_hbm = (hbm, hbm) if by_blocks else (hbm[:half], hbm[half:])
    attn_out, ffn_out = (hbm_out, hbm_out) if by_blocks else (hbm_out[:half], hbm_out[half:])
    wide = sizes.width
    attn_copies = start_in(
        attn_pairs(mats, by_blocks, attn_hbm, attn_at, qkv_ref, out_ref, place_ref), sems, 0
    )
    ffn_copies = start_in(
        ffn_pairs(mats, by_blocks, ffn_hbm, ffn_at, up_ref, down_ref, place_ref),
        sems,
        len(attn_copies),
    )
    vec[...] = jnp.zeros_like(vec)
    for n in range(seqs):
        base = n * sizes.ext
        z_ref[pl.ds(base, sizes.rows), :] = low_ref[pl.ds(n * sizes.rows, sizes.rows), :]
        z_ref[pl.ds(base + sizes.right_at, RIGHT_ROWS), :] = right_ref[n]
        z_ref[pl.ds(base + sizes.left_at, LEFT_ROWS), :] = left_ref[n, pl.ds(0, LEFT_ROWS), :]
        memory = jnp.concatenate(
            [
                mem_ref[pl.ds(n * sizes.segs, sizes.segs), :],
                left_ref[n, pl.ds(LEFT_ROWS, MEM_ROWS), :].astype(F32)[: sizes.segs],
            ],
            axis=0,
        )
        z_ref[pl.ds(base + sizes.mem_at, MEM_ROWS), :] = memory.astype(BF16)
        grad_low_ref[pl.ds(n * sizes.rows, sizes.rows), :] = out_grad_ref[n]
    fill_mask(sizes, seqs, starts_ref, place_ref, mask_ref)
    wait_all(attn_copies)
    project(sizes, z_ref, qkv_ref, row_bias_ref, proj_ref)
    attend(sizes, seqs, proj_ref, mask_ref, probs_ref, att_ref)
    mixed = (
        inputs_ref[...]
        + nt(att_ref[...], out_ref[...].reshape(-1, wide))
        + biases_ref[1, pl.ds(3, 1), :]
    )
    gain = gains_ref[1, pl.ds(1, 1), :]
    hidden, scaled, inverse = norm_forward(mixed, gain, biases_ref[1, pl.ds(4, 1), :])
    hidden_ref[...] = hidden.astype(BF16)
    for n in range(seqs):
        encoded_ref[n] = mixed[n * sizes.rows : (n + 1) * sizes.rows] + biases_ref[
            1, pl.ds(5, 1), :
        ]
    grad_hidden_ref[...] = jnp.zeros_like(grad_hidden_ref)
    wait_all(ffn_copies)

    def body(c, carry):
        at_lane = pl.multiple_of(c * wide, wide)
        upward = nt(hidden_ref[...], up_block(up_ref, c, wide))
        upward = upward + ffn_bias_ref[pl.ds(1, 1), pl.ds(at_lane, wide)]
        active, slope = gelu_both(upward)
        active = active.astype(BF16)
        made = nt(active, down_block(down_ref, c, wide))
        for n in range(seqs):
            encoded_ref[n] += made[n * sizes.rows : (n + 1) * sizes.rows]
        grad_hidden_ref[...] += ffn_back_step(
            sizes, c, wide, grad_low_ref[...], hidden_ref[...], active, slope, up_ref, down_ref,
            gup_ref, gdown_ref, vec,
        )
        return carry

    lax.fori_loop(0, sizes.ff // wide, body, 0)
    out_at = len(attn_copies) + len(ffn_copies)
    outs = start_out(
        ffn_pairs(mats, by_blocks, ffn_out, ffn_at, gup_ref, gdown_ref, place_ref), sems, out_at
    )
    grad = grad_low_ref[...].astype(F32)
    grad_hidden = grad_hidden_ref[...]
    vec[pl.ds(1, 1), :] = col_sum(grad_hidden * scaled)
    vec[pl.ds(6, 1), :] = col_sum(grad_hidden)
    vec[pl.ds(7, 1), :] = col_sum(grad)
    gz = grad + norm_backward(grad_hidden, scaled, inverse, gain)
    gz_ref[...] = gz
    attn_back_stage(
        sizes, seqs, gz, None, att_ref, proj_ref, probs_ref, z_ref, qkv_ref, out_ref, gqkv_ref,
        gout_ref, go_ref, gproj_ref, branch_ref, vec, gh_ref, gmem_ref, back_left_ref,
        back_right_ref,
    )
    outs = outs + start_out(
        attn_pairs(mats, by_blocks, attn_out, attn_at, gqkv_ref, gout_ref, place_ref),
        sems,
        out_at + len(outs),
    )
    wait_all(outs)


def first_back_kernel(
    last, sizes, seqs, mats, by_blocks, counts, offsets, place_ref, inputs_ref, gz_in_ref,
    gh_in_ref, gmem_in_ref, from_right_ref, from_left_ref, mixed_ref, active_ref, slope_ref,
    att_ref, probs_ref, proj_ref, z_ref, gains_ref, biases_ref, *refs
):
    attn_count, ffn_count, count_out = counts
    attn_in_at, ffn_in_at, attn_at, ffn_at = offsets
    attn_hbm = refs[:attn_count]
    ffn_hbm = refs[attn_count : attn_count + ffn_count]
    refs = refs[attn_count + ffn_count :]
    (gz_ref, gh_ref, gmem_ref, back_left_ref, back_right_ref, upper_vec, vec) = refs[:7]
    hbm_out = refs[7 : 7 + count_out]
    (
        qkv_ref, out_ref, up_ref, down_ref, gqkv_ref, gout_ref, gup_ref, gdown_ref, hidden_ref,
        go_ref, gproj_ref, branch_ref, grad_low_ref, grad_ref, grad_hidden_ref, grad_mem_ref, sems,
    ) = refs[7 + count_out :]
    attn_out, ffn_out = (hbm_out, hbm_out) if by_blocks else (hbm_out[:2], hbm_out[2:])
    wide = sizes.width
    ffn_copies = start_in(
        ffn_pairs(mats, by_blocks, ffn_hbm, ffn_in_at, up_ref, down_ref, place_ref), sems, 0
    )
    attn_copies = start_in(
        attn_pairs(mats, by_blocks, attn_hbm, attn_in_at, qkv_ref, out_ref, place_ref),
        sems,
        len(ffn_copies),
    )
    vec[...] = jnp.zeros_like(vec)
    upper_vec[...] = jnp.zeros_like(upper_vec)
    gain = gains_ref[1, pl.ds(0, 1), :]
    gain_sum = jnp.zeros((1, wide), F32)
    bias_sum = jnp.zeros((1, wide), F32)
    for n in range(seqs):
        rows = pl.ds(n * sizes.rows, sizes.rows)
        _, scaled, inverse = norm_forward(
            inputs_ref[rows, :], gain, biases_ref[1, pl.ds(0, 1), :]
        )
        total, mem = merge_halo(last, n, gh_in_ref, gmem_in_ref, from_right_ref, from_left_ref)
        gain_sum = gain_sum + col_sum(total * scaled)
        bias_sum = bias_sum + col_sum(total)
        grad = gz_in_ref[rows, :] + norm_backward(total, scaled, inverse, gain)
        grad_ref[rows, :] = grad
        grad_low_ref[rows, :] = grad.astype(BF16)
        grad_mem_ref[pl.ds(n * sizes.segs, sizes.segs), :] = mem
    upper_vec[pl.ds(0, 1), :] = gain_sum
    upper_vec[pl.ds(2, 1), :] = bias_sum
    gain = gains_ref[0, pl.ds(1, 1), :]
    hidden, scaled, inverse = norm_forward(
        mixed_ref[...], gain, biases_ref[0, pl.ds(4, 1), :]
    )
    hidden_ref[...] = hidden.astype(BF16)
    grad_hidden_ref[...] = jnp.zeros_like(grad_hidden_ref)
    wait_all(ffn_copies)

    def body(c, carry):
        at_lane = pl.multiple_of(c * wide, wide)
        grad_hidden_ref[...] += ffn_back_step(
            sizes, c, wide, grad_low_ref[...], hidden_ref[...],
            active_ref[:, pl.ds(at_lane, wide)], slope_ref[:, pl.ds(at_lane, wide)].astype(F32),
            up_ref, down_ref, gup_ref, gdown_ref, vec,
        )
        return carry

    lax.fori_loop(0, sizes.ff // wide, body, 0)
    out_at = len(attn_copies) + len(ffn_copies)
    outs = start_out(
        ffn_pairs(mats, by_blocks, ffn_out, ffn_at, gup_ref, gdown_ref, place_ref), sems, out_at
    )
    grad_hidden = grad_hidden_ref[...]
    grad = grad_ref[...]
    vec[pl.ds(1, 1), :] = col_sum(grad_hidden * scaled)
    vec[pl.ds(6, 1), :] = col_sum(grad_hidden)
    vec[pl.ds(7, 1), :] = col_sum(grad)
    gz = grad + norm_backward(grad_hidden, scaled, inverse, gain)
    gz_ref[...] = gz
    wait_all(attn_copies)
    attn_back_stage(
        sizes, seqs, gz, grad_mem_ref, att_ref, proj_ref, probs_ref, z_ref, qkv_ref, out_ref,
        gqkv_ref, gout_ref, go_ref, gproj_ref, branch_ref, vec, gh_ref, gmem_ref, back_left_ref,
        back_right_ref,
    )
    outs = outs + start_out(
        attn_pairs(mats, by_blocks, attn_out, attn_at, gqkv_ref, gout_ref, place_ref),
        sems,
        out_at + len(outs),
    )
    wait_all(outs)


def frames_grad_kernel(
    sizes, seqs, frames_ref, gz_ref, gh_ref, gmem_ref, from_right_ref, from_left_ref, gains_ref,
    biases_ref, lower_vec, grad_ref, vec
):
    gain = gains_ref[0, pl.ds(0, 1), :]
    wide = sizes.width
    gain_sum = jnp.zeros((1, wide), F32)
    bias_sum = jnp.zeros((1, wide), F32)
    for n in range(seqs):
        _, scaled, inverse = norm_forward(
            frames_ref[n].astype(F32), gain, biases_ref[0, pl.ds(0, 1), :]
        )
        total, mem = merge_halo(sizes, n, gh_ref, gmem_ref, from_right_ref, from_left_ref)
        gain_sum = gain_sum + col_sum(total * scaled)
        bias_sum = bias_sum + col_sum(total)
        grad_ref[n] = (
            gz_ref[pl.ds(n * sizes.rows, sizes.rows), :]
            + norm_backward(total, scaled, inverse, gain)
            + segment_spread(sizes.rows, wide, mem * (1.0 / SEG_LEN))
        )
    vec[...] = lower_vec[...]
    vec[pl.ds(0, 1), :] = gain_sum
    vec[pl.ds(2, 1), :] = bias_sum


def shifted(value, axis, by):
    size = lax.axis_size(axis)
    pairs = [(i, i + by) for i in range(size) if 0 <= i + by < size]
    return lax.ppermute(value, axis, pairs)


def permuted(value, move):
    reps = lax.axis_size("rep")
    pairs = []
    for flat in range(lax.axis_size("seg") * reps):
        seg, rep = divmod(flat, reps)
        z, y, x, core = move(seg // CHIPS_Y, seg % CHIPS_Y, rep // 2, rep % 2)
        pairs.append((flat, (z * CHIPS_Y + y) * reps + 2 * x + core))
    return lax.ppermute(value, ("seg", "rep"), pairs)


def along_z(value, by):
    return permuted(value, lambda z, y, x, core: ((z + by) % CHIPS_Z, y, x, core))


def across_first(value):
    return permuted(value, lambda z, y, x, c: (z, y, x ^ 1, c) if c == 0 else (z, y ^ 1, x, c))


def across_second(value):
    return permuted(value, lambda z, y, x, c: (z, y ^ 1, x, c) if c == 0 else (z, y, x ^ 1, c))


def other_core(value):
    return permuted(value, lambda z, y, x, c: (z, y, x, c ^ 1))


def gather_blocks(shard, z_place):
    parts = [shard] + [along_z(shard, by) for by in range(1, CHIPS_Z)]
    here = call(
        lambda *refs: stack_kernel(CHIPS_Z, *refs),
        [smem_spec()] + [hbm_spec()] * CHIPS_Z,
        [((CHIPS_Z,) + shard.shape, BF16)],
        [hbm_spec()],
        [pltpu.SemaphoreType.DMA((CHIPS_Z,))],
        [z_place] + parts,
    )[0]
    first = across_first(here)
    blocks = [here, first, across_second(here), across_second(first)]
    return blocks + [other_core(block) for block in blocks]


def added(mine, theirs):
    return (mine.astype(F32) + theirs.astype(F32)).astype(BF16)


def scatter_blocks(blocks, z_place):
    sums = [added(mine, other_core(theirs)) for mine, theirs in zip(blocks[:4], blocks[4:])]
    far = added(sums[1], across_second(sums[3]))
    near = added(sums[0], across_second(sums[2]))
    shape = near.shape[1:]
    parts = call(
        lambda *refs: split_kernel(CHIPS_Z, *refs),
        [smem_spec()] + [vmem_spec()] * 2,
        [(shape, BF16)] * CHIPS_Z,
        [vmem_spec()] * CHIPS_Z,
        [],
        [z_place, near, across_first(far)],
    )
    return [parts[0]] + [along_z(parts[by], by) for by in range(1, CHIPS_Z)]


def sum_everywhere(value):
    count = lax.axis_size("seg") * lax.axis_size("rep")
    bit = 1
    while bit < count:
        value = value + lax.ppermute(value, ("seg", "rep"), [(i, i ^ bit) for i in range(count)])
        bit *= 2
    return value


def vmem_spec():
    return pl.BlockSpec(memory_space=pltpu.VMEM)


def smem_spec():
    return pl.BlockSpec(memory_space=pltpu.SMEM)


def hbm_spec():
    return pl.BlockSpec(memory_space=pl.ANY)


def call(body, in_specs, out_shapes, out_specs, scratch, args, flops=0, moved=0):
    return pl.pallas_call(
        body,
        in_specs=in_specs,
        out_shape=tuple(jax.ShapeDtypeStruct(shape, kind) for shape, kind in out_shapes),
        out_specs=tuple(out_specs),
        scratch_shapes=scratch,
        compiler_params=pltpu.CompilerParams(vmem_limit_bytes=VMEM_BYTES),
        cost_estimate=pl.CostEstimate(flops=flops, bytes_accessed=moved, transcendentals=0),
    )(*args)


def on_device(
    frames,
    utt_segments,
    out_grad,
    qkv_weight,
    out_weight,
    ffn_in_weight,
    ffn_out_weight,
    norm_gains,
    biases,
    ffn_bias,
):
    micros, groups, rows, width = frames.shape
    seqs = micros * groups
    ff = ffn_bias.shape[1]
    reps = lax.axis_size("rep")
    seg_count = lax.axis_size("seg")
    mats = Matrices(width, ff)
    by_blocks = width // reps == LANES and reps == 4 and seg_count == BLOCKS
    first = Sizes(rows, width, ff, True)
    last = Sizes(rows, width, ff, False)
    own = seqs * rows
    mem_own = seqs * first.segs

    seg_at = lax.axis_index("seg")
    seg_base = seg_at * first.segs
    rep_at = lax.axis_index("rep")
    place = [seg_base, jnp.int32(first.segs * seg_count)]
    y_at, x_at, core_at = seg_at % CHIPS_Y, rep_at // 2, rep_at % 2
    z_place = jnp.reshape(seg_at // CHIPS_Y, (1,)).astype(jnp.int32)
    for other in range(2):
        core = lax.bitwise_xor(core_at, other)
        for hop2 in range(2):
            for hop1 in range(2):
                x_hop = jnp.where(core == 0, hop1, hop2)
                y_hop = jnp.where(core == 0, hop2, hop1)
                place.append(lax.bitwise_xor(y_at, y_hop))
                place.append((lax.bitwise_xor(x_at, x_hop) * 2 + core) * LANES)
    place = jnp.stack([jnp.asarray(entry, jnp.int32) for entry in place])
    lengths = utt_segments.reshape(seqs, utt_segments.shape[2])
    starts = (jnp.cumsum(lengths, axis=1) - lengths).astype(jnp.int32)
    zero_bias = jnp.zeros((width,), F32)
    row_bias = jnp.stack(
        [jnp.concatenate([biases[l, 1], zero_bias, biases[l, 2]]) for l in range(LAYERS)]
    ).reshape(LAYERS, 1, 3 * width)

    frames_own = frames.reshape(seqs, rows, width)
    grads_own = out_grad.reshape(seqs, rows, width)
    far = MEM_LEN * SEG_LEN
    frames_left = shifted(frames_own[:, rows - far :], "seg", 1)
    frames_right = shifted(frames_own[:, :RIGHT_ROWS], "seg", -1)

    attn_rows, ffn_rows = mats.attn_rows, mats.ffn_rows
    if by_blocks:
        qkv_t, out_t, down_t = (
            jnp.swapaxes(member, 1, 2) for member in (qkv_weight, out_weight, ffn_out_weight)
        )
        shard0, shard1 = call(
            pack_kernel,
            [vmem_spec()] * 4,
            [((attn_rows + ffn_rows, LANES), BF16)] * LAYERS,
            [vmem_spec()] * LAYERS,
            [],
            (qkv_t, out_t, ffn_in_weight, down_t),
        )
        first_attn = first_ffn = gather_blocks(shard0, z_place)
        shard1, _ = lax.optimization_barrier((shard1, first_attn[0]))
        last_all = gather_blocks(shard1, z_place)
        attn_at, ffn_at = 0, attn_rows
        grad_outs = [((CHIPS_Z, attn_rows + ffn_rows, LANES), BF16)] * len(last_all)
        copies_in = len(last_all) * (3 + mats.down_parts)
    else:
        whole = []
        for member, shape in zip(
            (qkv_weight, out_weight, ffn_in_weight, ffn_out_weight),
            (mats.qkv, mats.out, mats.up, mats.down),
        ):
            member = lax.all_gather(member, "rep", axis=1, tiled=True)
            member = lax.all_gather(member, "seg", axis=2, tiled=True)
            whole.append(jnp.swapaxes(member, 1, 2).reshape((LAYERS,) + shape))
        first_attn = [whole[0][0], whole[1][0]]
        first_ffn = [whole[2][0], whole[3][0]]
        last_all = [member[1] for member in whole]
        attn_at, ffn_at = 0, 0
        grad_outs = [(shape, BF16) for shape in (mats.qkv, mats.out, mats.up, mats.down)]
        copies_in = 4
    dma = pltpu.SemaphoreType.DMA

    z0, proj0, probs0, att0, mixed0, mem1 = call(
        lambda *refs: first_attn_kernel(
            first, seqs, mats, by_blocks, len(first_attn), attn_at, *refs
        ),
        [smem_spec()] * 2 + [vmem_spec()] * 6 + [hbm_spec()] * len(first_attn),
        [
            ((seqs * first.ext, width), BF16),
            ((seqs * first.ext, 3 * width), BF16),
            ((seqs * first.pairs, 2 * first.queries, first.keys), F32),
            ((seqs * first.queries, width), BF16),
            ((own, width), F32),
            ((mem_own, width), F32),
        ],
        [vmem_spec()] * 6,
        [
            pltpu.VMEM(mats.qkv, BF16),
            pltpu.VMEM(mats.out, BF16),
            pltpu.VMEM((seqs, first.queries, first.keys), F32),
            dma((copies_in,)),
        ],
        (place, starts, frames_own, frames_left, frames_right, norm_gains, biases, row_bias[0])
        + tuple(first_attn),
        flops=40 * own * 4 * width * width,
        moved=8 * width * width,
    )
    x1, active0, slope0, low1, send_right, send_left = call(
        lambda *refs: first_ffn_kernel(first, seqs, mats, by_blocks, len(first_ffn), ffn_at, *refs),
        [smem_spec()] + [vmem_spec()] * 5 + [hbm_spec()] * len(first_ffn),
        [
            ((own, width), F32),
            ((own, ff), BF16),
            ((own, ff), BF16),
            ((own, width), BF16),
            ((seqs, BACK_ROWS, width), BF16),
            ((seqs, RIGHT_ROWS, width), BF16),
        ],
        [vmem_spec()] * 6,
        [
            pltpu.VMEM(mats.up, BF16),
            pltpu.VMEM(mats.down, BF16),
            pltpu.VMEM((own, width), BF16),
            dma((copies_in,)),
        ],
        (place, mixed0, mem1, norm_gains, biases, ffn_bias) + tuple(first_ffn),
        flops=16 * own * 2 * width * ff,
        moved=4 * width * ff,
    )
    left1 = shifted(send_right, "seg", 1)
    right1 = shifted(send_left, "seg", -1)

    vec_shape = (TILE, width)
    outs = call(
        lambda *refs: last_layer_kernel(
            last, seqs, mats, by_blocks, len(last_all), attn_at, ffn_at, *refs
        ),
        [smem_spec()] * 2 + [vmem_spec()] * 10 + [hbm_spec()] * len(last_all),
        [
            ((seqs, rows, width), F32),
            ((own, width), F32),
            ((own, width), F32),
            ((mem_own, width), F32),
            ((seqs, BACK_ROWS, width), BF16),
            ((seqs, RIGHT_ROWS, width), BF16),
            (vec_shape, F32),
        ]
        + grad_outs,
        [vmem_spec()] * 7 + [hbm_spec()] * len(grad_outs),
        [
            pltpu.VMEM(mats.qkv, BF16),
            pltpu.VMEM(mats.out, BF16),
            pltpu.VMEM(mats.up, BF16),
            pltpu.VMEM(mats.down, BF16),
            pltpu.VMEM(mats.qkv, BF16),
            pltpu.VMEM(mats.out, BF16),
            pltpu.VMEM(mats.up, BF16),
            pltpu.VMEM(mats.down, BF16),
            pltpu.VMEM((seqs, last.queries, last.keys), F32),
            pltpu.VMEM((seqs * last.ext, width), BF16),
            pltpu.VMEM((seqs * last.ext, 3 * width), BF16),
            pltpu.VMEM((seqs * last.pairs, 2 * last.queries, last.keys), F32),
            pltpu.VMEM((seqs * last.queries, width), BF16),
            pltpu.VMEM((own, width), BF16),
            pltpu.VMEM((seqs * last.queries, width), BF16),
            pltpu.VMEM((seqs * last.ext, 3 * width), BF16),
            pltpu.VMEM((seqs * last.queries, width), BF16),
            pltpu.VMEM((own, width), BF16),
            pltpu.VMEM((own, width), F32),
            dma((2 * copies_in,)),
        ],
        (place, starts, low1, left1, right1, mem1, x1, grads_own, norm_gains, biases, ffn_bias,
         row_bias[1]) + tuple(last_all),
        flops=30 * own * (4 * width * width + 2 * width * ff),
        moved=4 * (4 * width * width + 2 * width * ff),
    )
    encoded, gz1, gh1, gmem1, back_left1, back_right1, vec1 = outs[:7]
    grad_blocks1 = outs[7:]
    from_right1 = shifted(back_left1, "seg", -1)
    from_left1 = shifted(back_right1, "seg", 1)

    outs = call(
        lambda *refs: first_back_kernel(
            last, first, seqs, mats, by_blocks, (len(first_attn), len(first_ffn), len(grad_outs)),
            (attn_at, ffn_at, attn_at, ffn_at), *refs
        ),
        [smem_spec()] + [vmem_spec()] * 15 + [hbm_spec()] * (len(first_attn) + len(first_ffn)),
        [
            ((own, width), F32),
            ((own, width), F32),
            ((mem_own, width), F32),
            ((seqs, BACK_ROWS, width), BF16),
            ((seqs, RIGHT_ROWS, width), BF16),
            (vec_shape, F32),
            (vec_shape, F32),
        ]
        + grad_outs,
        [vmem_spec()] * 7 + [hbm_spec()] * len(grad_outs),
        [
            pltpu.VMEM(mats.qkv, BF16),
            pltpu.VMEM(mats.out, BF16),
            pltpu.VMEM(mats.up, BF16),
            pltpu.VMEM(mats.down, BF16),
            pltpu.VMEM(mats.qkv, BF16),
            pltpu.VMEM(mats.out, BF16),
            pltpu.VMEM(mats.up, BF16),
            pltpu.VMEM(mats.down, BF16),
            pltpu.VMEM((own, width), BF16),
            pltpu.VMEM((seqs * first.queries, width), BF16),
            pltpu.VMEM((seqs * first.ext, 3 * width), BF16),
            pltpu.VMEM((seqs * first.queries, width), BF16),
            pltpu.VMEM((own, width), BF16),
            pltpu.VMEM((own, width), F32),
            pltpu.VMEM((own, width), F32),
            pltpu.VMEM((mem_own, width), F32),
            dma((2 * copies_in,)),
        ],
        (place, x1, gz1, gh1, gmem1, from_right1, from_left1, mixed0, active0, slope0, att0, probs0,
         proj0, z0, norm_gains, biases) + tuple(first_attn) + tuple(first_ffn),
        flops=28 * own * (4 * width * width + 2 * width * ff),
        moved=4 * (4 * width * width + 2 * width * ff),
    )
    gz0, gh0, gmem0, back_left0, back_right0, upper_vec, vec0 = outs[:7]
    grad_blocks0 = outs[7:]
    from_right0 = shifted(back_left0, "seg", -1)
    from_left0 = shifted(back_right0, "seg", 1)
    frames_grad, vec0 = call(
        lambda *refs: frames_grad_kernel(first, seqs, *refs),
        [vmem_spec()] * 9,
        [((seqs, rows, width), F32), (vec_shape, F32)],
        [vmem_spec()] * 2,
        [],
        (frames_own, gz0, gh0, gmem0, from_right0, from_left0, norm_gains, biases, vec0),
    )

    if by_blocks:
        parts = scatter_blocks(grad_blocks0, z_place), scatter_blocks(grad_blocks1, z_place)
        shapes = [member.shape for member in (qkv_t, out_t, ffn_in_weight, down_t)]
        reduced = call(
            lambda *refs: unpack_kernel(CHIPS_Z, *refs),
            [vmem_spec()] * (LAYERS * CHIPS_Z),
            [(shape, F32) for shape in shapes],
            [vmem_spec()] * 4,
            [],
            parts[0] + parts[1],
        )
        reduced = [
            jnp.swapaxes(reduced[0], 1, 2),
            jnp.swapaxes(reduced[1], 1, 2),
            reduced[2],
            jnp.swapaxes(reduced[3], 1, 2),
        ]
    else:
        reduced = []
        for member0, member1 in zip(grad_blocks0, grad_blocks1):
            both = jnp.stack([member0, member1]).reshape(LAYERS, -1, member0.shape[3])
            both = jnp.swapaxes(both, 1, 2)
            both = lax.psum_scatter(both, "seg", scatter_dimension=2, tiled=True)
            both = lax.psum_scatter(both, "rep", scatter_dimension=1, tiled=True)
            reduced.append(both.astype(F32))

    small = sum_everywhere(jnp.stack([vec0, vec1 + upper_vec]))
    return (
        encoded.reshape(frames.shape),
        frames_grad.reshape(frames.shape),
        reduced[0],
        reduced[1],
        reduced[2],
        reduced[3],
        small[:, 0:2],
        small[:, 2:8],
        small[:, 8:12].reshape(ffn_bias.shape),
    )


def solution(mesh):
    in_specs = (
        P(None, "rep", "seg", None),
        P(None, "rep", None),
        P(None, "rep", "seg", None),
        P(None, "rep", "seg"),
        P(None, "rep", "seg"),
        P(None, "rep", "seg"),
        P(None, "rep", "seg"),
        P(),
        P(),
        P(),
    )
    out_specs = (
        P(None, "rep", "seg", None),
        P(None, "rep", "seg", None),
        P(None, "rep", "seg"),
        P(None, "rep", "seg"),
        P(None, "rep", "seg"),
        P(None, "rep", "seg"),
        P(),
        P(),
        P(),
    )
    return jax.shard_map(
        on_device, mesh=mesh, in_specs=in_specs, out_specs=out_specs, check_vma=False
    )
```

```python
import jax
import jax.numpy as jnp
from jax import lax
from jax.experimental import pallas as pl
from jax.experimental.pallas import tpu as pltpu
from jax.sharding import PartitionSpec as P

HEADS = 8
SEG_LEN = 16
LEFT_LEN = 30
RIGHT_LEN = 4
MEM_LEN = 4
LAYERS = 2

EPS = 1e-05
ROOT_HALF = 0.7071067811865476
INV_ROOT_TWO_PI = 0.3989422804014327

LANES = 128
TILE = 16
RIGHT_ROWS = 16
LEFT_ROWS = 32
MEM_ROWS = 16
BACK_ROWS = LEFT_ROWS + MEM_ROWS
CHIPS_Z = 4
CHIPS_Y = 2
BLOCKS = CHIPS_Z * CHIPS_Y
VMEM_BYTES = 56 * 1024 * 1024

BF16 = jnp.bfloat16
F32 = jnp.float32


def nn(a, b):
    return lax.dot_general(a, b, (((1,), (0,)), ((), ())), preferred_element_type=F32)


def nt(a, b):
    return lax.dot_general(a, b, (((1,), (1,)), ((), ())), preferred_element_type=F32)


def tn(a, b):
    return lax.dot_general(a, b, (((0,), (0,)), ((), ())), preferred_element_type=F32)


def col_sum(value):
    return jnp.sum(value, axis=0, keepdims=True)


def norm_forward(inputs, gain, bias):
    center = inputs - jnp.mean(inputs, axis=1, keepdims=True)
    inverse = lax.rsqrt(jnp.mean(center * center, axis=1, keepdims=True) + EPS)
    scaled = center * inverse
    return scaled * gain + bias, scaled, inverse


def norm_backward(grad_in, scaled, inverse, gain):
    grad_scaled = grad_in * gain
    return inverse * (
        grad_scaled
        - jnp.mean(grad_scaled, axis=1, keepdims=True)
        - scaled * jnp.mean(grad_scaled * scaled, axis=1, keepdims=True)
    )


def segment_mean(inputs):
    rows, width = inputs.shape
    return jnp.mean(inputs.reshape(rows // SEG_LEN, SEG_LEN, width), axis=1)


def segment_spread(rows, width, per_segment):
    segs = rows // SEG_LEN
    return jnp.broadcast_to(per_segment[:, None, :], (segs, SEG_LEN, width)).reshape(rows, width)


def identity(size):
    row = lax.broadcasted_iota(jnp.int32, (size, size), 0)
    col = lax.broadcasted_iota(jnp.int32, (size, size), 1)
    return (row == col).astype(F32).astype(BF16)


class Sizes:
    def __init__(self, rows, width, ff, with_summary):
        self.rows = rows
        self.width = width
        self.ff = ff
        self.segs = rows // SEG_LEN
        self.top = TILE if with_summary else 0
        self.keys = rows + RIGHT_ROWS + LEFT_ROWS + MEM_ROWS
        self.ext = self.top + self.keys
        self.queries = self.top + rows
        self.right_at = self.top + rows
        self.left_at = self.right_at + RIGHT_ROWS
        self.mem_at = self.left_at + LEFT_ROWS
        self.pairs = width // LANES


class Matrices:
    def __init__(self, width, ff):
        self.qkv = (CHIPS_Z, CHIPS_Y, 3 * width // BLOCKS, width)
        self.out = (CHIPS_Z, CHIPS_Y, width // BLOCKS, width)
        self.up = (CHIPS_Z, CHIPS_Y, ff // BLOCKS, width)
        self.down = (CHIPS_Z, CHIPS_Y, width // BLOCKS, ff)
        self.down_parts = ff // width
        self.attn_rows = self.qkv[2] + self.out[2]
        self.ffn_rows = self.up[2] + self.down_parts * self.down[2]


def attn_pairs(mats, by_blocks, hbm, first, qkv_ref, out_ref, place_ref):
    if not by_blocks:
        return [(hbm[0], qkv_ref), (hbm[1], out_ref)]
    pairs = []
    high = mats.qkv[2]
    for k, block in enumerate(hbm):
        row = place_ref[2 + 2 * k]
        lane = pl.multiple_of(place_ref[3 + 2 * k], LANES)
        pairs.append(
            (block.at[:, pl.ds(first, high), :], qkv_ref.at[:, row, :, pl.ds(lane, LANES)])
        )
        pairs.append(
            (
                block.at[:, pl.ds(first + high, mats.out[2]), :],
                out_ref.at[:, row, :, pl.ds(lane, LANES)],
            )
        )
    return pairs


def ffn_pairs(mats, by_blocks, hbm, first, up_ref, down_ref, place_ref):
    if not by_blocks:
        return [(hbm[0], up_ref), (hbm[1], down_ref)]
    pairs = []
    high = mats.up[2]
    low = mats.down[2]
    for k, block in enumerate(hbm):
        row = place_ref[2 + 2 * k]
        lane = pl.multiple_of(place_ref[3 + 2 * k], LANES)
        pairs.append(
            (block.at[:, pl.ds(first, high), :], up_ref.at[:, row, :, pl.ds(lane, LANES)])
        )
        for part in range(mats.down_parts):
            there = pl.multiple_of(
                place_ref[3 + 2 * k] * mats.down_parts + part * LANES, LANES
            )
            pairs.append(
                (
                    block.at[:, pl.ds(first + high + part * low, low), :],
                    down_ref.at[:, row, :, pl.ds(there, LANES)],
                )
            )
    return pairs


def start_in(pairs, sems, at):
    copies = [pltpu.make_async_copy(s, d, sems.at[at + i]) for i, (s, d) in enumerate(pairs)]
    for copy in copies:
        copy.start()
    return copies


def start_out(pairs, sems, at):
    copies = [pltpu.make_async_copy(d, s, sems.at[at + i]) for i, (s, d) in enumerate(pairs)]
    for copy in copies:
        copy.start()
    return copies


def out_views(by_blocks, hbm):
    if not by_blocks:
        return hbm[:2], hbm[2:]
    views = [ref.at[k] for ref in hbm for k in range(ref.shape[0])]
    return views, views


def wait_all(copies):
    for copy in copies:
        copy.wait()


def fill_mask(sizes, seqs, starts_ref, place_ref, mask_ref):
    shape = (sizes.queries, sizes.keys)
    row = lax.broadcasted_iota(jnp.int32, shape, 0)
    col = lax.broadcasted_iota(jnp.int32, shape, 1)
    base = place_ref[0]
    total = place_ref[1]
    query = jnp.where(row < sizes.top, row, lax.shift_right_arithmetic(row - sizes.top, 4))
    left_at = sizes.rows + RIGHT_ROWS
    mem_at = left_at + LEFT_ROWS
    spot = jnp.where(col < left_at, col, col - mem_at)
    mem_seg = jnp.where(col < mem_at + sizes.segs, col - mem_at, col - mem_at - 2 * sizes.segs)
    key_seg = jnp.where(col < mem_at, lax.shift_right_arithmetic(spot, 4), mem_seg)
    near = (
        (key_seg == query)
        | ((spot >= query * SEG_LEN - LEFT_LEN) & (spot < query * SEG_LEN))
        | ((key_seg == query + 1) & (spot < query * SEG_LEN + SEG_LEN + RIGHT_LEN))
    )
    recent = (key_seg >= query - MEM_LEN) & (key_seg < query) & (row >= sizes.top)
    allowed = ((col < mem_at) & near) | ((col >= mem_at) & recent)
    key_abs = key_seg + base
    query_abs = query + base
    allowed = allowed & (key_abs >= 0) & (key_abs < total)
    if sizes.top:
        allowed = allowed & ((row < sizes.segs) | (row >= sizes.top))
    for n in range(seqs):
        key_owner = jnp.zeros(shape, jnp.int32)
        query_owner = jnp.zeros(shape, jnp.int32)
        for u in range(starts_ref.shape[1]):
            first = starts_ref[n, u]
            key_owner = key_owner + (key_abs >= first).astype(jnp.int32)
            query_owner = query_owner + (query_abs >= first).astype(jnp.int32)
        mask_ref[n] = jnp.where(allowed & (key_owner == query_owner), 0.0, -1e30)


def half_masks():
    lane = lax.broadcasted_iota(jnp.int32, (1, LANES), 1)
    even = (lane < LANES // 2).astype(F32)
    return even.astype(BF16), (1.0 - even).astype(BF16), lane < LANES // 2


def project(sizes, z_ref, qkv_ref, row_bias_ref, proj_ref):
    step = CHIPS_Z // 2
    for c in range(2):
        block = qkv_ref[pl.ds(c * step, step)].reshape(-1, sizes.width)
        wide = block.shape[0]
        made = nt(z_ref[...], block) + row_bias_ref[:, pl.ds(c * wide, wide)]
        proj_ref[:, pl.ds(c * wide, wide)] = made.astype(BF16)


def split_heads(sizes, ref, first, rows, lane):
    return ref[pl.ds(first, rows), pl.ds(lane, LANES)]


def attend(sizes, seqs, proj_ref, mask_ref, probs_ref, att_ref):
    even, odd, is_even = half_masks()
    scale = (sizes.width // HEADS) ** (-0.5)
    count = sizes.queries

    def body(p, carry):
        for n in range(seqs):
            lane = pl.multiple_of(p * LANES, LANES)
            query = proj_ref[pl.ds(n * sizes.ext, count), pl.ds(lane, LANES)]
            first = n * sizes.ext + sizes.top
            key = proj_ref[pl.ds(first, sizes.keys), pl.ds(sizes.width + lane, LANES)]
            value = proj_ref[pl.ds(first, sizes.keys), pl.ds(2 * sizes.width + lane, LANES)]
            scores = nt(jnp.concatenate([query * even, query * odd], axis=0), key) * scale
            outs = []
            for half in range(2):
                part = scores[half * count : (half + 1) * count] + mask_ref[n]
                part = jnp.exp(part - jnp.max(part, axis=1, keepdims=True))
                part = part * (1.0 / jnp.sum(part, axis=1, keepdims=True))
                probs_ref[n * sizes.pairs + p, pl.ds(half * count, count), :] = part
                outs.append(nn(part.astype(BF16), value))
            att_ref[pl.ds(n * count, count), pl.ds(lane, LANES)] = jnp.where(
                is_even, outs[0], outs[1]
            ).astype(BF16)
        return carry

    lax.fori_loop(0, sizes.pairs, body, 0)


def attend_back(sizes, seqs, proj_ref, probs_ref, go_ref, gproj_ref):
    even, odd, is_even = half_masks()
    scale = (sizes.width // HEADS) ** (-0.5)
    count = sizes.queries
    wide = sizes.width
    for n in range(seqs):
        base = n * sizes.ext
        rest = sizes.ext - count
        gproj_ref[pl.ds(base + count, rest), pl.ds(0, wide)] = jnp.zeros((rest, wide), BF16)
        if sizes.top:
            gproj_ref[pl.ds(base, sizes.top), pl.ds(wide, 2 * wide)] = jnp.zeros(
                (sizes.top, 2 * wide), BF16
            )

    def body(p, carry):
        for n in range(seqs):
            lane = pl.multiple_of(p * LANES, LANES)
            base = n * sizes.ext
            first = base + sizes.top
            query = proj_ref[pl.ds(base, count), pl.ds(lane, LANES)]
            key = proj_ref[pl.ds(first, sizes.keys), pl.ds(wide + lane, LANES)]
            value = proj_ref[pl.ds(first, sizes.keys), pl.ds(2 * wide + lane, LANES)]
            grad = go_ref[pl.ds(n * count, count), pl.ds(lane, LANES)]
            queries = jnp.concatenate([query * even, query * odd], axis=0)
            grads = jnp.concatenate([grad * even, grad * odd], axis=0)
            probs = probs_ref[n * sizes.pairs + p]
            grad_values = tn(probs.astype(BF16), grads)
            grad_probs = nt(grads, value)
            weighted = grad_probs * probs
            grad_scores = (
                (weighted - probs * jnp.sum(weighted, axis=1, keepdims=True)) * scale
            ).astype(BF16)
            grad_keys = tn(grad_scores, queries)
            grad_query = jnp.where(
                is_even, nn(grad_scores[:count], key), nn(grad_scores[count:], key)
            )
            gproj_ref[pl.ds(base, count), pl.ds(lane, LANES)] = grad_query.astype(BF16)
            gproj_ref[pl.ds(first, sizes.keys), pl.ds(wide + lane, LANES)] = grad_keys.astype(BF16)
            gproj_ref[pl.ds(first, sizes.keys), pl.ds(2 * wide + lane, LANES)] = (
                grad_values.astype(BF16)
            )
        return carry

    lax.fori_loop(0, sizes.pairs, body, 0)


def gelu_both(upward):
    half = 0.5 * (1.0 + lax.erf(upward * ROOT_HALF))
    slope = half + upward * jnp.exp(-0.5 * upward * upward) * INV_ROOT_TWO_PI
    return upward * half, slope


def up_block(up_ref, c, wide):
    step = wide // (up_ref.shape[1] * up_ref.shape[2])
    return up_ref[pl.ds(c * step, step)].reshape(-1, up_ref.shape[3])


def down_block(down_ref, c, wide):
    at = pl.multiple_of(c * wide, wide)
    return down_ref[:, :, :, pl.ds(at, wide)].reshape(-1, wide)


def ffn_back_step(
    sizes, c, wide, grad_low, hidden_low, active, slope, up_ref, down_ref, gup_ref, gdown_ref, vec
):
    at = pl.multiple_of(c * wide, wide)
    up = up_block(up_ref, c, wide)
    down = down_block(down_ref, c, wide)
    grad_active = nn(grad_low, down)
    grad_up_f = grad_active * slope
    grad_up = grad_up_f.astype(BF16)
    gdown_ref[:, :, :, pl.ds(at, wide)] = (
        tn(grad_low, active).astype(BF16).reshape(gdown_ref.shape[:3] + (wide,))
    )
    step = wide // (gup_ref.shape[1] * gup_ref.shape[2])
    gup_ref[pl.ds(c * step, step)] = (
        tn(grad_up, hidden_low).astype(BF16).reshape((step,) + gup_ref.shape[1:])
    )
    vec[pl.ds(8 + c, 1), :] = col_sum(grad_up.astype(F32))
    return nn(grad_up, up)


def attn_back_stage(
    sizes, seqs, gz, grad_mem_ref, att_ref, proj_ref, probs_ref, z_ref, qkv_ref, out_ref,
    gqkv_ref, gout_ref, go_ref, gproj_ref, branch_ref, vec, gh_ref, gmem_ref, back_left_ref,
    back_right_ref,
):
    wide = sizes.width
    count = sizes.queries
    bias_out = col_sum(gz)
    for n in range(seqs):
        if sizes.top:
            mem_grad = grad_mem_ref[pl.ds(n * sizes.segs, sizes.segs), :]
            bias_out = bias_out + col_sum(mem_grad)
            branch_ref[pl.ds(n * count, sizes.top), :] = jnp.concatenate(
                [mem_grad, jnp.zeros((sizes.top - sizes.segs, wide), F32)], axis=0
            ).astype(BF16)
        branch_ref[pl.ds(n * count + sizes.top, sizes.rows), :] = gz[
            n * sizes.rows : (n + 1) * sizes.rows
        ].astype(BF16)
    vec[pl.ds(5, 1), :] = bias_out
    branch = branch_ref[...]
    gout_ref[...] = tn(branch, att_ref[...]).astype(BF16).reshape(gout_ref.shape)
    go_ref[...] = nn(branch, out_ref[...].reshape(-1, wide)).astype(BF16)
    attend_back(sizes, seqs, proj_ref, probs_ref, go_ref, gproj_ref)
    vec[pl.ds(3, 1), :] = col_sum(gproj_ref[:, pl.ds(0, wide)].astype(F32))
    vec[pl.ds(4, 1), :] = col_sum(gproj_ref[:, pl.ds(2 * wide, wide)].astype(F32))
    grad_ext = nn(gproj_ref[...], qkv_ref[...].reshape(-1, wide))
    for n in range(seqs):
        base = n * sizes.ext
        own = grad_ext[base + sizes.top : base + sizes.top + sizes.rows]
        if sizes.top:
            spread = grad_ext[base : base + sizes.segs] * (1.0 / SEG_LEN)
            own = own + segment_spread(sizes.rows, wide, spread)
        gh_ref[pl.ds(n * sizes.rows, sizes.rows), :] = own
        mem = base + sizes.mem_at
        gmem_ref[pl.ds(n * sizes.segs, sizes.segs), :] = grad_ext[mem : mem + sizes.segs]
        left = base + sizes.left_at
        back_left_ref[n] = grad_ext[left : left + BACK_ROWS].astype(BF16)
        right = base + sizes.right_at
        back_right_ref[n] = grad_ext[right : right + RIGHT_ROWS].astype(BF16)
    step = CHIPS_Z // 2
    part = gqkv_ref.shape[1] * gqkv_ref.shape[2] * step
    for c in range(2):
        gqkv_ref[pl.ds(c * step, step)] = (
            tn(gproj_ref[:, pl.ds(c * part, part)], z_ref[...])
            .astype(BF16)
            .reshape((step,) + gqkv_ref.shape[1:])
        )


def merge_halo(sizes, n, gh_ref, gmem_ref, from_right_ref, from_left_ref):
    first = n * sizes.rows
    back = from_right_ref[n].astype(F32)
    head = gh_ref[pl.ds(first, RIGHT_ROWS), :] + from_left_ref[n].astype(F32)
    middle = gh_ref[pl.ds(first + RIGHT_ROWS, sizes.rows - RIGHT_ROWS - LEFT_ROWS), :]
    tail = gh_ref[pl.ds(first + sizes.rows - LEFT_ROWS, LEFT_ROWS), :] + back[:LEFT_ROWS]
    mem = gmem_ref[pl.ds(n * sizes.segs, sizes.segs), :] + back[LEFT_ROWS + sizes.segs :]
    return jnp.concatenate([head, middle, tail], axis=0), mem


def pack_kernel(qkv_ref, out_ref, up_ref, down_ref, *packed):
    eye = identity(LANES)
    high, wide, low = qkv_ref.shape[1], out_ref.shape[1], down_ref.shape[1]
    up = up_ref.shape[2]
    for layer, ref in enumerate(packed):
        ref[pl.ds(0, high), :] = qkv_ref[layer]
        ref[pl.ds(high, wide), :] = out_ref[layer]
        ref[pl.ds(high + wide, up), :] = tn(up_ref[layer], eye).astype(BF16)
        for part in range(down_ref.shape[2] // LANES):
            ref[pl.ds(high + wide + up + part * low, low), :] = down_ref[
                layer, :, pl.ds(part * LANES, LANES)
            ]


def unpack_kernel(each, *refs):
    sources, (qkv_ref, out_ref, up_ref, down_ref) = refs[:-4], refs[-4:]
    eye = identity(LANES)
    high, wide, low = qkv_ref.shape[1], out_ref.shape[1], down_ref.shape[1]
    up = up_ref.shape[2]
    for layer in range(qkv_ref.shape[0]):
        parts = sources[layer * each : (layer + 1) * each]

        def total(first, rows):
            value = parts[0][pl.ds(first, rows), :].astype(F32)
            for part in parts[1:]:
                value = value + part[pl.ds(first, rows), :].astype(F32)
            return value

        qkv_ref[layer] = total(0, high)
        out_ref[layer] = total(high, wide)
        up_ref[layer] = nt(eye, total(high + wide, up).astype(BF16))
        for part in range(down_ref.shape[2] // LANES):
            down_ref[layer, :, pl.ds(part * LANES, LANES)] = total(
                high + wide + up + part * low, low
            )


def stack_kernel(count, place_ref, *refs):
    sources, out_ref, sems = refs[:count], refs[count], refs[count + 1]
    copies = []
    for k, source in enumerate(sources):
        spot = lax.rem(place_ref[0] + count - k, count)
        copies.append(pltpu.make_async_copy(source, out_ref.at[spot], sems.at[k]))
    for copy in copies:
        copy.start()
    wait_all(copies)


def split_kernel(count, place_ref, mine_ref, theirs_ref, *outs):
    for k, out in enumerate(outs):
        spot = lax.rem(place_ref[0] + k, count)
        out[...] = (mine_ref[spot].astype(F32) + theirs_ref[spot].astype(F32)).astype(BF16)


def first_attn_kernel(
    sizes, seqs, mats, by_blocks, count_in, at, place_ref, starts_ref, frames_ref, left_ref,
    right_ref, gains_ref, biases_ref, row_bias_ref, *refs
):
    hbm = refs[:count_in]
    z_ref, proj_ref, probs_ref, att_ref, mixed_ref, mem_ref, qkv_ref, out_ref, mask_ref, sems = (
        refs[count_in:]
    )
    wide = sizes.width
    copies = start_in(
        attn_pairs(mats, by_blocks, hbm, at, qkv_ref, out_ref, place_ref), sems, 0
    )
    gain = gains_ref[0, pl.ds(0, 1), :]
    bias = biases_ref[0, pl.ds(0, 1), :]
    pad = jnp.zeros((TILE - sizes.segs, wide), F32)
    for n in range(seqs):
        own = frames_ref[n].astype(F32)
        before = left_ref[n].astype(F32)
        hidden = norm_forward(own, gain, bias)[0]
        halo = norm_forward(before[before.shape[0] - LEFT_ROWS :], gain, bias)[0]
        after = norm_forward(right_ref[n].astype(F32), gain, bias)[0]
        memory = jnp.concatenate(
            [
                segment_mean(own),
                jnp.zeros((sizes.segs - before.shape[0] // SEG_LEN, wide), F32),
                segment_mean(before),
            ],
            axis=0,
        )
        base = n * sizes.ext
        z_ref[pl.ds(base, sizes.top), :] = jnp.concatenate(
            [segment_mean(hidden), pad], axis=0
        ).astype(BF16)
        z_ref[pl.ds(base + sizes.top, sizes.rows), :] = hidden.astype(BF16)
        z_ref[pl.ds(base + sizes.right_at, RIGHT_ROWS), :] = after.astype(BF16)
        z_ref[pl.ds(base + sizes.left_at, LEFT_ROWS), :] = halo.astype(BF16)
        z_ref[pl.ds(base + sizes.mem_at, MEM_ROWS), :] = memory.astype(BF16)
    fill_mask(sizes, seqs, starts_ref, place_ref, mask_ref)
    wait_all(copies)
    project(sizes, z_ref, qkv_ref, row_bias_ref, proj_ref)
    attend(sizes, seqs, proj_ref, mask_ref, probs_ref, att_ref)
    mixed = nt(att_ref[...], out_ref[...].reshape(-1, wide)) + biases_ref[0, pl.ds(3, 1), :]
    for n in range(seqs):
        base = n * sizes.queries
        mem_ref[pl.ds(n * sizes.segs, sizes.segs), :] = mixed[base : base + sizes.segs]
        mixed_ref[pl.ds(n * sizes.rows, sizes.rows), :] = (
            frames_ref[n].astype(F32) + mixed[base + sizes.top : base + sizes.top + sizes.rows]
        )


def first_ffn_kernel(
    sizes, seqs, mats, by_blocks, count_in, at, place_ref, mixed_ref, mem_ref, gains_ref,
    biases_ref, ffn_bias_ref, *refs
):
    hbm = refs[:count_in]
    (
        next_ref, active_ref, slope_ref, low_ref, send_right_ref, send_left_ref, up_ref, down_ref,
        hidden_ref, sems,
    ) = refs[count_in:]
    copies = start_in(ffn_pairs(mats, by_blocks, hbm, at, up_ref, down_ref, place_ref), sems, 0)
    mixed = mixed_ref[...]
    hidden, _, _ = norm_forward(mixed, gains_ref[0, pl.ds(1, 1), :], biases_ref[0, pl.ds(4, 1), :])
    hidden_ref[...] = hidden.astype(BF16)
    next_ref[...] = mixed + biases_ref[0, pl.ds(5, 1), :]
    wait_all(copies)
    wide = sizes.width

    def body(c, carry):
        at_lane = pl.multiple_of(c * wide, wide)
        upward = nt(hidden_ref[...], up_block(up_ref, c, wide))
        upward = upward + ffn_bias_ref[pl.ds(0, 1), pl.ds(at_lane, wide)]
        active, slope = gelu_both(upward)
        active = active.astype(BF16)
        active_ref[:, pl.ds(at_lane, wide)] = active
        slope_ref[:, pl.ds(at_lane, wide)] = slope.astype(BF16)
        next_ref[...] += nt(active, down_block(down_ref, c, wide))
        return carry

    lax.fori_loop(0, sizes.ff // wide, body, 0)
    low, _, _ = norm_forward(
        next_ref[...], gains_ref[1, pl.ds(0, 1), :], biases_ref[1, pl.ds(0, 1), :]
    )
    low = low.astype(BF16)
    low_ref[...] = low
    for n in range(seqs):
        base = n * sizes.rows
        send_right_ref[n, pl.ds(0, LEFT_ROWS), :] = low[
            base + sizes.rows - LEFT_ROWS : base + sizes.rows
        ]
        send_right_ref[n, pl.ds(LEFT_ROWS, MEM_ROWS), :] = jnp.concatenate(
            [
                mem_ref[pl.ds(n * sizes.segs, sizes.segs), :],
                jnp.zeros((MEM_ROWS - sizes.segs, wide), F32),
            ],
            axis=0,
        ).astype(BF16)
        send_left_ref[n] = low[base : base + RIGHT_ROWS]


def last_layer_kernel(
    sizes, seqs, mats, by_blocks, count_in, attn_at, ffn_at, place_ref, starts_ref, low_ref,
    left_ref, right_ref, mem_ref, inputs_ref, out_grad_ref, gains_ref, biases_ref, ffn_bias_ref,
    row_bias_ref, *refs
):
    hbm = refs[:count_in]
    count_out = 2 if by_blocks else 4
    (encoded_ref, gz_ref, gh_ref, gmem_ref, back_left_ref, back_right_ref, vec) = refs[
        count_in : count_in + 7
    ]
    hbm_out = refs[count_in + 7 : count_in + 7 + count_out]
    (
        qkv_ref, out_ref, up_ref, down_ref, gqkv_ref, gout_ref, gup_ref, gdown_ref, mask_ref,
        z_ref, proj_ref, probs_ref, att_ref, hidden_ref, go_ref, gproj_ref, branch_ref,
        grad_low_ref, grad_hidden_ref, sems,
    ) = refs[count_in + 7 + count_out :]
    attn_hbm, ffn_hbm = (hbm, hbm) if by_blocks else (hbm[:2], hbm[2:])
    attn_out, ffn_out = out_views(by_blocks, hbm_out)
    wide = sizes.width
    attn_copies = start_in(
        attn_pairs(mats, by_blocks, attn_hbm, attn_at, qkv_ref, out_ref, place_ref), sems, 0
    )
    ffn_copies = start_in(
        ffn_pairs(mats, by_blocks, ffn_hbm, ffn_at, up_ref, down_ref, place_ref),
        sems,
        len(attn_copies),
    )
    vec[...] = jnp.zeros_like(vec)
    for n in range(seqs):
        base = n * sizes.ext
        z_ref[pl.ds(base, sizes.rows), :] = low_ref[pl.ds(n * sizes.rows, sizes.rows), :]
        z_ref[pl.ds(base + sizes.right_at, RIGHT_ROWS), :] = right_ref[n]
        z_ref[pl.ds(base + sizes.left_at, LEFT_ROWS), :] = left_ref[n, pl.ds(0, LEFT_ROWS), :]
        memory = jnp.concatenate(
            [
                mem_ref[pl.ds(n * sizes.segs, sizes.segs), :],
                left_ref[n, pl.ds(LEFT_ROWS, MEM_ROWS), :].astype(F32)[: sizes.segs],
            ],
            axis=0,
        )
        z_ref[pl.ds(base + sizes.mem_at, MEM_ROWS), :] = memory.astype(BF16)
        grad_low_ref[pl.ds(n * sizes.rows, sizes.rows), :] = out_grad_ref[n]
    fill_mask(sizes, seqs, starts_ref, place_ref, mask_ref)
    wait_all(attn_copies)
    project(sizes, z_ref, qkv_ref, row_bias_ref, proj_ref)
    attend(sizes, seqs, proj_ref, mask_ref, probs_ref, att_ref)
    mixed = (
        inputs_ref[...]
        + nt(att_ref[...], out_ref[...].reshape(-1, wide))
        + biases_ref[1, pl.ds(3, 1), :]
    )
    gain = gains_ref[1, pl.ds(1, 1), :]
    hidden, scaled, inverse = norm_forward(mixed, gain, biases_ref[1, pl.ds(4, 1), :])
    hidden_ref[...] = hidden.astype(BF16)
    for n in range(seqs):
        encoded_ref[n] = mixed[n * sizes.rows : (n + 1) * sizes.rows] + biases_ref[
            1, pl.ds(5, 1), :
        ]
    grad_hidden_ref[...] = jnp.zeros_like(grad_hidden_ref)
    wait_all(ffn_copies)

    def body(c, carry):
        at_lane = pl.multiple_of(c * wide, wide)
        upward = nt(hidden_ref[...], up_block(up_ref, c, wide))
        upward = upward + ffn_bias_ref[pl.ds(1, 1), pl.ds(at_lane, wide)]
        active, slope = gelu_both(upward)
        active = active.astype(BF16)
        made = nt(active, down_block(down_ref, c, wide))
        for n in range(seqs):
            encoded_ref[n] += made[n * sizes.rows : (n + 1) * sizes.rows]
        grad_hidden_ref[...] += ffn_back_step(
            sizes, c, wide, grad_low_ref[...], hidden_ref[...], active, slope, up_ref, down_ref,
            gup_ref, gdown_ref, vec,
        )
        return carry

    lax.fori_loop(0, sizes.ff // wide, body, 0)
    out_at = len(attn_copies) + len(ffn_copies)
    outs = start_out(
        ffn_pairs(mats, by_blocks, ffn_out, ffn_at, gup_ref, gdown_ref, place_ref), sems, out_at
    )
    grad = grad_low_ref[...].astype(F32)
    grad_hidden = grad_hidden_ref[...]
    vec[pl.ds(1, 1), :] = col_sum(grad_hidden * scaled)
    vec[pl.ds(6, 1), :] = col_sum(grad_hidden)
    vec[pl.ds(7, 1), :] = col_sum(grad)
    gz = grad + norm_backward(grad_hidden, scaled, inverse, gain)
    gz_ref[...] = gz
    attn_back_stage(
        sizes, seqs, gz, None, att_ref, proj_ref, probs_ref, z_ref, qkv_ref, out_ref, gqkv_ref,
        gout_ref, go_ref, gproj_ref, branch_ref, vec, gh_ref, gmem_ref, back_left_ref,
        back_right_ref,
    )
    outs = outs + start_out(
        attn_pairs(mats, by_blocks, attn_out, attn_at, gqkv_ref, gout_ref, place_ref),
        sems,
        out_at + len(outs),
    )
    wait_all(outs)


def first_back_kernel(
    last, sizes, seqs, mats, by_blocks, counts, offsets, place_ref, inputs_ref, gz_in_ref,
    gh_in_ref, gmem_in_ref, from_right_ref, from_left_ref, mixed_ref, active_ref, slope_ref,
    att_ref, probs_ref, proj_ref, z_ref, gains_ref, biases_ref, *refs
):
    attn_count, ffn_count, count_out = counts
    attn_in_at, ffn_in_at, attn_at, ffn_at = offsets
    attn_hbm = refs[:attn_count]
    ffn_hbm = refs[attn_count : attn_count + ffn_count]
    refs = refs[attn_count + ffn_count :]
    (gz_ref, gh_ref, gmem_ref, back_left_ref, back_right_ref, upper_vec, vec) = refs[:7]
    hbm_out = refs[7 : 7 + count_out]
    (
        qkv_ref, out_ref, up_ref, down_ref, gqkv_ref, gout_ref, gup_ref, gdown_ref, hidden_ref,
        go_ref, gproj_ref, branch_ref, grad_low_ref, grad_ref, grad_hidden_ref, grad_mem_ref, sems,
    ) = refs[7 + count_out :]
    attn_out, ffn_out = out_views(by_blocks, hbm_out)
    wide = sizes.width
    ffn_copies = start_in(
        ffn_pairs(mats, by_blocks, ffn_hbm, ffn_in_at, up_ref, down_ref, place_ref), sems, 0
    )
    attn_copies = start_in(
        attn_pairs(mats, by_blocks, attn_hbm, attn_in_at, qkv_ref, out_ref, place_ref),
        sems,
        len(ffn_copies),
    )
    vec[...] = jnp.zeros_like(vec)
    upper_vec[...] = jnp.zeros_like(upper_vec)
    gain = gains_ref[1, pl.ds(0, 1), :]
    gain_sum = jnp.zeros((1, wide), F32)
    bias_sum = jnp.zeros((1, wide), F32)
    for n in range(seqs):
        rows = pl.ds(n * sizes.rows, sizes.rows)
        _, scaled, inverse = norm_forward(
            inputs_ref[rows, :], gain, biases_ref[1, pl.ds(0, 1), :]
        )
        total, mem = merge_halo(last, n, gh_in_ref, gmem_in_ref, from_right_ref, from_left_ref)
        gain_sum = gain_sum + col_sum(total * scaled)
        bias_sum = bias_sum + col_sum(total)
        grad = gz_in_ref[rows, :] + norm_backward(total, scaled, inverse, gain)
        grad_ref[rows, :] = grad
        grad_low_ref[rows, :] = grad.astype(BF16)
        grad_mem_ref[pl.ds(n * sizes.segs, sizes.segs), :] = mem
    upper_vec[pl.ds(0, 1), :] = gain_sum
    upper_vec[pl.ds(2, 1), :] = bias_sum
    gain = gains_ref[0, pl.ds(1, 1), :]
    hidden, scaled, inverse = norm_forward(
        mixed_ref[...], gain, biases_ref[0, pl.ds(4, 1), :]
    )
    hidden_ref[...] = hidden.astype(BF16)
    grad_hidden_ref[...] = jnp.zeros_like(grad_hidden_ref)
    wait_all(ffn_copies)

    def body(c, carry):
        at_lane = pl.multiple_of(c * wide, wide)
        grad_hidden_ref[...] += ffn_back_step(
            sizes, c, wide, grad_low_ref[...], hidden_ref[...],
            active_ref[:, pl.ds(at_lane, wide)], slope_ref[:, pl.ds(at_lane, wide)].astype(F32),
            up_ref, down_ref, gup_ref, gdown_ref, vec,
        )
        return carry

    lax.fori_loop(0, sizes.ff // wide, body, 0)
    out_at = len(attn_copies) + len(ffn_copies)
    outs = start_out(
        ffn_pairs(mats, by_blocks, ffn_out, ffn_at, gup_ref, gdown_ref, place_ref), sems, out_at
    )
    grad_hidden = grad_hidden_ref[...]
    grad = grad_ref[...]
    vec[pl.ds(1, 1), :] = col_sum(grad_hidden * scaled)
    vec[pl.ds(6, 1), :] = col_sum(grad_hidden)
    vec[pl.ds(7, 1), :] = col_sum(grad)
    gz = grad + norm_backward(grad_hidden, scaled, inverse, gain)
    gz_ref[...] = gz
    wait_all(attn_copies)
    attn_back_stage(
        sizes, seqs, gz, grad_mem_ref, att_ref, proj_ref, probs_ref, z_ref, qkv_ref, out_ref,
        gqkv_ref, gout_ref, go_ref, gproj_ref, branch_ref, vec, gh_ref, gmem_ref, back_left_ref,
        back_right_ref,
    )
    outs = outs + start_out(
        attn_pairs(mats, by_blocks, attn_out, attn_at, gqkv_ref, gout_ref, place_ref),
        sems,
        out_at + len(outs),
    )
    wait_all(outs)


def frames_grad_kernel(
    sizes, seqs, frames_ref, gz_ref, gh_ref, gmem_ref, from_right_ref, from_left_ref, gains_ref,
    biases_ref, lower_vec, grad_ref, vec
):
    gain = gains_ref[0, pl.ds(0, 1), :]
    wide = sizes.width
    gain_sum = jnp.zeros((1, wide), F32)
    bias_sum = jnp.zeros((1, wide), F32)
    for n in range(seqs):
        _, scaled, inverse = norm_forward(
            frames_ref[n].astype(F32), gain, biases_ref[0, pl.ds(0, 1), :]
        )
        total, mem = merge_halo(sizes, n, gh_ref, gmem_ref, from_right_ref, from_left_ref)
        gain_sum = gain_sum + col_sum(total * scaled)
        bias_sum = bias_sum + col_sum(total)
        grad_ref[n] = (
            gz_ref[pl.ds(n * sizes.rows, sizes.rows), :]
            + norm_backward(total, scaled, inverse, gain)
            + segment_spread(sizes.rows, wide, mem * (1.0 / SEG_LEN))
        )
    vec[...] = lower_vec[...]
    vec[pl.ds(0, 1), :] = gain_sum
    vec[pl.ds(2, 1), :] = bias_sum


def shifted(value, axis, by):
    size = lax.axis_size(axis)
    pairs = [(i, i + by) for i in range(size) if 0 <= i + by < size]
    return lax.ppermute(value, axis, pairs)


def permuted(value, move):
    reps = lax.axis_size("rep")
    pairs = []
    for flat in range(lax.axis_size("seg") * reps):
        seg, rep = divmod(flat, reps)
        z, y, x, core = move(seg // CHIPS_Y, seg % CHIPS_Y, rep // 2, rep % 2)
        pairs.append((flat, (z * CHIPS_Y + y) * reps + 2 * x + core))
    return lax.ppermute(value, ("seg", "rep"), pairs)


def along_z(value, by):
    return permuted(value, lambda z, y, x, core: ((z + by) % CHIPS_Z, y, x, core))


def across_first(value):
    return permuted(value, lambda z, y, x, c: (z, y, x ^ 1, c) if c == 0 else (z, y ^ 1, x, c))


def across_second(value):
    return permuted(value, lambda z, y, x, c: (z, y ^ 1, x, c) if c == 0 else (z, y, x ^ 1, c))


def other_core(value):
    return permuted(value, lambda z, y, x, c: (z, y, x, c ^ 1))


def gather_blocks(shard, z_place):
    parts = [shard] + [along_z(shard, by) for by in range(1, CHIPS_Z)]
    here = call(
        lambda *refs: stack_kernel(CHIPS_Z, *refs),
        [smem_spec()] + [vmem_spec()] * CHIPS_Z,
        [((CHIPS_Z,) + shard.shape, BF16)],
        [hbm_spec()],
        [pltpu.SemaphoreType.DMA((CHIPS_Z,))],
        [z_place] + parts,
    )[0]
    first = across_first(here)
    blocks = [here, first, across_second(here), across_second(first)]
    return blocks + [other_core(block) for block in blocks]


def scatter_plane(blocks, z_place):
    mine, theirs = blocks[0], other_core(blocks[1])

    def pair(at):
        return mine[at].astype(F32) + theirs[at].astype(F32)

    second = across_second(pair(slice(2, 4)).astype(BF16))
    far = (pair(1) + second[1].astype(F32)).astype(BF16)
    near = (pair(0) + second[0].astype(F32)).astype(BF16)
    shape = near.shape[1:]
    return call(
        lambda *refs: split_kernel(CHIPS_Z, *refs),
        [smem_spec()] + [vmem_spec()] * 2,
        [(shape, BF16)] * CHIPS_Z,
        [vmem_spec()] * CHIPS_Z,
        [],
        [z_place, near, across_first(far)],
    )


def scatter_z(parts):
    return [parts[0]] + [along_z(parts[by], by) for by in range(1, CHIPS_Z)]


def sum_everywhere(value):
    count = lax.axis_size("seg") * lax.axis_size("rep")
    bit = 1
    while bit < count:
        value = value + lax.ppermute(value, ("seg", "rep"), [(i, i ^ bit) for i in range(count)])
        bit *= 2
    return value


def vmem_spec():
    return pl.BlockSpec(memory_space=pltpu.VMEM)


def smem_spec():
    return pl.BlockSpec(memory_space=pltpu.SMEM)


def hbm_spec():
    return pl.BlockSpec(memory_space=pl.ANY)


def call(body, in_specs, out_shapes, out_specs, scratch, args, flops=0, moved=0):
    return pl.pallas_call(
        body,
        in_specs=in_specs,
        out_shape=tuple(jax.ShapeDtypeStruct(shape, kind) for shape, kind in out_shapes),
        out_specs=tuple(out_specs),
        scratch_shapes=scratch,
        compiler_params=pltpu.CompilerParams(vmem_limit_bytes=VMEM_BYTES),
        cost_estimate=pl.CostEstimate(flops=flops, bytes_accessed=moved, transcendentals=0),
    )(*args)


def on_device(
    frames,
    utt_segments,
    out_grad,
    qkv_weight,
    out_weight,
    ffn_in_weight,
    ffn_out_weight,
    norm_gains,
    biases,
    ffn_bias,
):
    micros, groups, rows, width = frames.shape
    seqs = micros * groups
    ff = ffn_bias.shape[1]
    reps = lax.axis_size("rep")
    seg_count = lax.axis_size("seg")
    mats = Matrices(width, ff)
    by_blocks = width // reps == LANES and reps == 4 and seg_count == BLOCKS
    first = Sizes(rows, width, ff, True)
    last = Sizes(rows, width, ff, False)
    own = seqs * rows
    mem_own = seqs * first.segs

    seg_at = lax.axis_index("seg")
    seg_base = seg_at * first.segs
    rep_at = lax.axis_index("rep")
    place = [seg_base, jnp.int32(first.segs * seg_count)]
    y_at, x_at, core_at = seg_at % CHIPS_Y, rep_at // 2, rep_at % 2
    z_place = jnp.reshape(seg_at // CHIPS_Y, (1,)).astype(jnp.int32)
    for other in range(2):
        core = lax.bitwise_xor(core_at, other)
        for hop2 in range(2):
            for hop1 in range(2):
                x_hop = jnp.where(core == 0, hop1, hop2)
                y_hop = jnp.where(core == 0, hop2, hop1)
                place.append(lax.bitwise_xor(y_at, y_hop))
                place.append((lax.bitwise_xor(x_at, x_hop) * 2 + core) * LANES)
    place = jnp.stack([jnp.asarray(entry, jnp.int32) for entry in place])
    lengths = utt_segments.reshape(seqs, utt_segments.shape[2])
    starts = (jnp.cumsum(lengths, axis=1) - lengths).astype(jnp.int32)
    zero_bias = jnp.zeros((width,), F32)
    row_bias = jnp.stack(
        [jnp.concatenate([biases[l, 1], zero_bias, biases[l, 2]]) for l in range(LAYERS)]
    ).reshape(LAYERS, 1, 3 * width)

    frames_own = frames.reshape(seqs, rows, width)
    grads_own = out_grad.reshape(seqs, rows, width)
    far = MEM_LEN * SEG_LEN
    frames_left = shifted(frames_own[:, rows - far :], "seg", 1)
    frames_right = shifted(frames_own[:, :RIGHT_ROWS], "seg", -1)

    attn_rows, ffn_rows = mats.attn_rows, mats.ffn_rows
    if by_blocks:
        qkv_t, out_t, down_t = (
            jnp.swapaxes(member, 1, 2) for member in (qkv_weight, out_weight, ffn_out_weight)
        )
        shard0, shard1 = call(
            pack_kernel,
            [vmem_spec()] * 4,
            [((attn_rows + ffn_rows, LANES), BF16)] * LAYERS,
            [vmem_spec()] * LAYERS,
            [],
            (qkv_t, out_t, ffn_in_weight, down_t),
        )
        first_attn = first_ffn = gather_blocks(shard0, z_place)
        shard1, _ = lax.optimization_barrier((shard1, first_attn[0]))
        last_all = gather_blocks(shard1, z_place)
        attn_at, ffn_at = 0, attn_rows
        half = len(last_all) // 2
        grad_outs = [((half, CHIPS_Z, attn_rows + ffn_rows, LANES), BF16)] * 2
        copies_in = len(last_all) * (3 + mats.down_parts)
    else:
        whole = []
        for member, shape in zip(
            (qkv_weight, out_weight, ffn_in_weight, ffn_out_weight),
            (mats.qkv, mats.out, mats.up, mats.down),
        ):
            member = lax.all_gather(member, "rep", axis=1, tiled=True)
            member = lax.all_gather(member, "seg", axis=2, tiled=True)
            whole.append(jnp.swapaxes(member, 1, 2).reshape((LAYERS,) + shape))
        first_attn = [whole[0][0], whole[1][0]]
        first_ffn = [whole[2][0], whole[3][0]]
        last_all = [member[1] for member in whole]
        attn_at, ffn_at = 0, 0
        grad_outs = [(shape, BF16) for shape in (mats.qkv, mats.out, mats.up, mats.down)]
        copies_in = 4
    dma = pltpu.SemaphoreType.DMA

    z0, proj0, probs0, att0, mixed0, mem1 = call(
        lambda *refs: first_attn_kernel(
            first, seqs, mats, by_blocks, len(first_attn), attn_at, *refs
        ),
        [smem_spec()] * 2 + [vmem_spec()] * 6 + [hbm_spec()] * len(first_attn),
        [
            ((seqs * first.ext, width), BF16),
            ((seqs * first.ext, 3 * width), BF16),
            ((seqs * first.pairs, 2 * first.queries, first.keys), F32),
            ((seqs * first.queries, width), BF16),
            ((own, width), F32),
            ((mem_own, width), F32),
        ],
        [vmem_spec()] * 6,
        [
            pltpu.VMEM(mats.qkv, BF16),
            pltpu.VMEM(mats.out, BF16),
            pltpu.VMEM((seqs, first.queries, first.keys), F32),
            dma((copies_in,)),
        ],
        (place, starts, frames_own, frames_left, frames_right, norm_gains, biases, row_bias[0])
        + tuple(first_attn),
        flops=40 * own * 4 * width * width,
        moved=8 * width * width,
    )
    x1, active0, slope0, low1, send_right, send_left = call(
        lambda *refs: first_ffn_kernel(first, seqs, mats, by_blocks, len(first_ffn), ffn_at, *refs),
        [smem_spec()] + [vmem_spec()] * 5 + [hbm_spec()] * len(first_ffn),
        [
            ((own, width), F32),
            ((own, ff), BF16),
            ((own, ff), BF16),
            ((own, width), BF16),
            ((seqs, BACK_ROWS, width), BF16),
            ((seqs, RIGHT_ROWS, width), BF16),
        ],
        [vmem_spec()] * 6,
        [
            pltpu.VMEM(mats.up, BF16),
            pltpu.VMEM(mats.down, BF16),
            pltpu.VMEM((own, width), BF16),
            dma((copies_in,)),
        ],
        (place, mixed0, mem1, norm_gains, biases, ffn_bias) + tuple(first_ffn),
        flops=16 * own * 2 * width * ff,
        moved=4 * width * ff,
    )
    left1 = shifted(send_right, "seg", 1)
    right1 = shifted(send_left, "seg", -1)

    vec_shape = (TILE, width)
    outs = call(
        lambda *refs: last_layer_kernel(
            last, seqs, mats, by_blocks, len(last_all), attn_at, ffn_at, *refs
        ),
        [smem_spec()] * 2 + [vmem_spec()] * 10 + [hbm_spec()] * len(last_all),
        [
            ((seqs, rows, width), F32),
            ((own, width), F32),
            ((own, width), F32),
            ((mem_own, width), F32),
            ((seqs, BACK_ROWS, width), BF16),
            ((seqs, RIGHT_ROWS, width), BF16),
            (vec_shape, F32),
        ]
        + grad_outs,
        [vmem_spec()] * 7 + [hbm_spec()] * len(grad_outs),
        [
            pltpu.VMEM(mats.qkv, BF16),
            pltpu.VMEM(mats.out, BF16),
            pltpu.VMEM(mats.up, BF16),
            pltpu.VMEM(mats.down, BF16),
            pltpu.VMEM(mats.qkv, BF16),
            pltpu.VMEM(mats.out, BF16),
            pltpu.VMEM(mats.up, BF16),
            pltpu.VMEM(mats.down, BF16),
            pltpu.VMEM((seqs, last.queries, last.keys), F32),
            pltpu.VMEM((seqs * last.ext, width), BF16),
            pltpu.VMEM((seqs * last.ext, 3 * width), BF16),
            pltpu.VMEM((seqs * last.pairs, 2 * last.queries, last.keys), F32),
            pltpu.VMEM((seqs * last.queries, width), BF16),
            pltpu.VMEM((own, width), BF16),
            pltpu.VMEM((seqs * last.queries, width), BF16),
            pltpu.VMEM((seqs * last.ext, 3 * width), BF16),
            pltpu.VMEM((seqs * last.queries, width), BF16),
            pltpu.VMEM((own, width), BF16),
            pltpu.VMEM((own, width), F32),
            dma((2 * copies_in,)),
        ],
        (place, starts, low1, left1, right1, mem1, x1, grads_own, norm_gains, biases, ffn_bias,
         row_bias[1]) + tuple(last_all),
        flops=30 * own * (4 * width * width + 2 * width * ff),
        moved=4 * (4 * width * width + 2 * width * ff),
    )
    encoded, gz1, gh1, gmem1, back_left1, back_right1, vec1 = outs[:7]
    grad_blocks1 = outs[7:]
    from_right1 = shifted(back_left1, "seg", -1)
    from_left1 = shifted(back_right1, "seg", 1)

    outs = call(
        lambda *refs: first_back_kernel(
            last, first, seqs, mats, by_blocks, (len(first_attn), len(first_ffn), len(grad_outs)),
            (attn_at, ffn_at, attn_at, ffn_at), *refs
        ),
        [smem_spec()] + [vmem_spec()] * 15 + [hbm_spec()] * (len(first_attn) + len(first_ffn)),
        [
            ((own, width), F32),
            ((own, width), F32),
            ((mem_own, width), F32),
            ((seqs, BACK_ROWS, width), BF16),
            ((seqs, RIGHT_ROWS, width), BF16),
            (vec_shape, F32),
            (vec_shape, F32),
        ]
        + grad_outs,
        [vmem_spec()] * 7 + [hbm_spec()] * len(grad_outs),
        [
            pltpu.VMEM(mats.qkv, BF16),
            pltpu.VMEM(mats.out, BF16),
            pltpu.VMEM(mats.up, BF16),
            pltpu.VMEM(mats.down, BF16),
            pltpu.VMEM(mats.qkv, BF16),
            pltpu.VMEM(mats.out, BF16),
            pltpu.VMEM(mats.up, BF16),
            pltpu.VMEM(mats.down, BF16),
            pltpu.VMEM((own, width), BF16),
            pltpu.VMEM((seqs * first.queries, width), BF16),
            pltpu.VMEM((seqs * first.ext, 3 * width), BF16),
            pltpu.VMEM((seqs * first.queries, width), BF16),
            pltpu.VMEM((own, width), BF16),
            pltpu.VMEM((own, width), F32),
            pltpu.VMEM((own, width), F32),
            pltpu.VMEM((mem_own, width), F32),
            dma((2 * copies_in,)),
        ],
        (place, x1, gz1, gh1, gmem1, from_right1, from_left1, mixed0, active0, slope0, att0, probs0,
         proj0, z0, norm_gains, biases) + tuple(first_attn) + tuple(first_ffn),
        flops=28 * own * (4 * width * width + 2 * width * ff),
        moved=4 * (4 * width * width + 2 * width * ff),
    )
    gz0, gh0, gmem0, back_left0, back_right0, upper_vec, vec0 = outs[:7]
    grad_blocks0 = outs[7:]
    from_right0 = shifted(back_left0, "seg", -1)
    from_left0 = shifted(back_right0, "seg", 1)
    if by_blocks:
        split1 = scatter_plane(grad_blocks1, z_place)
        gz0, split1 = lax.optimization_barrier((gz0, split1))
    frames_grad, vec0 = call(
        lambda *refs: frames_grad_kernel(first, seqs, *refs),
        [vmem_spec()] * 9,
        [((seqs, rows, width), F32), (vec_shape, F32)],
        [vmem_spec()] * 2,
        [],
        (frames_own, gz0, gh0, gmem0, from_right0, from_left0, norm_gains, biases, vec0),
    )

    if by_blocks:
        parts = scatter_z(scatter_plane(grad_blocks0, z_place)), scatter_z(split1)
        shapes = [member.shape for member in (qkv_t, out_t, ffn_in_weight, down_t)]
        reduced = call(
            lambda *refs: unpack_kernel(CHIPS_Z, *refs),
            [vmem_spec()] * (LAYERS * CHIPS_Z),
            [(shape, F32) for shape in shapes],
            [vmem_spec()] * 4,
            [],
            parts[0] + parts[1],
        )
        reduced = [
            jnp.swapaxes(reduced[0], 1, 2),
            jnp.swapaxes(reduced[1], 1, 2),
            reduced[2],
            jnp.swapaxes(reduced[3], 1, 2),
        ]
    else:
        reduced = []
        for member0, member1 in zip(grad_blocks0, grad_blocks1):
            both = jnp.stack([member0, member1]).reshape(LAYERS, -1, member0.shape[3])
            both = jnp.swapaxes(both, 1, 2)
            both = lax.psum_scatter(both, "seg", scatter_dimension=2, tiled=True)
            both = lax.psum_scatter(both, "rep", scatter_dimension=1, tiled=True)
            reduced.append(both.astype(F32))

    small = sum_everywhere(jnp.stack([vec0, vec1 + upper_vec]))
    return (
        encoded.reshape(frames.shape),
        frames_grad.reshape(frames.shape),
        reduced[0],
        reduced[1],
        reduced[2],
        reduced[3],
        small[:, 0:2],
        small[:, 2:8],
        small[:, 8:12].reshape(ffn_bias.shape),
    )


def solution(mesh):
    in_specs = (
        P(None, "rep", "seg", None),
        P(None, "rep", None),
        P(None, "rep", "seg", None),
        P(None, "rep", "seg"),
        P(None, "rep", "seg"),
        P(None, "rep", "seg"),
        P(None, "rep", "seg"),
        P(),
        P(),
        P(),
    )
    out_specs = (
        P(None, "rep", "seg", None),
        P(None, "rep", "seg", None),
        P(None, "rep", "seg"),
        P(None, "rep", "seg"),
        P(None, "rep", "seg"),
        P(None, "rep", "seg"),
        P(),
        P(),
        P(),
    )
    return jax.shard_map(
        on_device, mesh=mesh, in_specs=in_specs, out_specs=out_specs, check_vma=False
    )
```

```python
import jax
import jax.numpy as jnp
from jax import lax
from jax.experimental import pallas as pl
from jax.experimental.pallas import tpu as pltpu
from jax.sharding import PartitionSpec as P

HEADS = 8
SEG_LEN = 16
LEFT_LEN = 30
RIGHT_LEN = 4
MEM_LEN = 4
LAYERS = 2

EPS = 1e-05
ROOT_HALF = 0.7071067811865476
INV_ROOT_TWO_PI = 0.3989422804014327

LANES = 128
TILE = 16
RIGHT_ROWS = 16
LEFT_ROWS = 32
MEM_ROWS = 16
BACK_ROWS = LEFT_ROWS + MEM_ROWS
CHIPS_Z = 4
CHIPS_Y = 2
BLOCKS = CHIPS_Z * CHIPS_Y
VMEM_BYTES = 56 * 1024 * 1024

BF16 = jnp.bfloat16
F32 = jnp.float32


def nn(a, b):
    return lax.dot_general(a, b, (((1,), (0,)), ((), ())), preferred_element_type=F32)


def nt(a, b):
    return lax.dot_general(a, b, (((1,), (1,)), ((), ())), preferred_element_type=F32)


def tn(a, b):
    return lax.dot_general(a, b, (((0,), (0,)), ((), ())), preferred_element_type=F32)


def col_sum(value):
    return jnp.sum(value, axis=0, keepdims=True)


def norm_forward(inputs, gain, bias):
    center = inputs - jnp.mean(inputs, axis=1, keepdims=True)
    inverse = lax.rsqrt(jnp.mean(center * center, axis=1, keepdims=True) + EPS)
    scaled = center * inverse
    return scaled * gain + bias, scaled, inverse


def norm_backward(grad_in, scaled, inverse, gain):
    grad_scaled = grad_in * gain
    return inverse * (
        grad_scaled
        - jnp.mean(grad_scaled, axis=1, keepdims=True)
        - scaled * jnp.mean(grad_scaled * scaled, axis=1, keepdims=True)
    )


def segment_mean(inputs):
    rows, width = inputs.shape
    return jnp.mean(inputs.reshape(rows // SEG_LEN, SEG_LEN, width), axis=1)


def segment_spread(rows, width, per_segment):
    segs = rows // SEG_LEN
    return jnp.broadcast_to(per_segment[:, None, :], (segs, SEG_LEN, width)).reshape(rows, width)


def identity(size):
    row = lax.broadcasted_iota(jnp.int32, (size, size), 0)
    col = lax.broadcasted_iota(jnp.int32, (size, size), 1)
    return (row == col).astype(F32).astype(BF16)


class Sizes:
    def __init__(self, rows, width, ff, with_summary):
        self.rows = rows
        self.width = width
        self.ff = ff
        self.segs = rows // SEG_LEN
        self.top = TILE if with_summary else 0
        self.keys = rows + RIGHT_ROWS + LEFT_ROWS + MEM_ROWS
        self.ext = self.top + self.keys
        self.queries = self.top + rows
        self.right_at = self.top + rows
        self.left_at = self.right_at + RIGHT_ROWS
        self.mem_at = self.left_at + LEFT_ROWS
        self.pairs = width // LANES


class Matrices:
    def __init__(self, width, ff):
        self.qkv = (CHIPS_Z, CHIPS_Y, 3 * width // BLOCKS, width)
        self.out = (CHIPS_Z, CHIPS_Y, width // BLOCKS, width)
        self.up = (CHIPS_Z, CHIPS_Y, ff // BLOCKS, width)
        self.down = (CHIPS_Z, CHIPS_Y, width // BLOCKS, ff)
        self.down_parts = ff // width
        self.attn_rows = self.qkv[2] + self.out[2]
        self.ffn_rows = self.up[2] + self.down_parts * self.down[2]


def attn_pairs(mats, by_blocks, hbm, first, qkv_ref, out_ref, place_ref):
    if not by_blocks:
        return [(hbm[0], qkv_ref), (hbm[1], out_ref)]
    pairs = []
    high = mats.qkv[2]
    for k, block in enumerate(hbm):
        row = place_ref[2 + 2 * k]
        lane = pl.multiple_of(place_ref[3 + 2 * k], LANES)
        pairs.append(
            (block.at[:, pl.ds(first, high), :], qkv_ref.at[:, row, :, pl.ds(lane, LANES)])
        )
        pairs.append(
            (
                block.at[:, pl.ds(first + high, mats.out[2]), :],
                out_ref.at[:, row, :, pl.ds(lane, LANES)],
            )
        )
    return pairs


def ffn_pairs(mats, by_blocks, hbm, first, up_ref, down_ref, place_ref):
    if not by_blocks:
        return [(hbm[0], up_ref), (hbm[1], down_ref)]
    pairs = []
    high = mats.up[2]
    low = mats.down[2]
    for k, block in enumerate(hbm):
        row = place_ref[2 + 2 * k]
        lane = pl.multiple_of(place_ref[3 + 2 * k], LANES)
        pairs.append(
            (block.at[:, pl.ds(first, high), :], up_ref.at[:, row, :, pl.ds(lane, LANES)])
        )
        for part in range(mats.down_parts):
            there = pl.multiple_of(
                place_ref[3 + 2 * k] * mats.down_parts + part * LANES, LANES
            )
            pairs.append(
                (
                    block.at[:, pl.ds(first + high + part * low, low), :],
                    down_ref.at[:, row, :, pl.ds(there, LANES)],
                )
            )
    return pairs


def start_in(pairs, sems, at):
    copies = [pltpu.make_async_copy(s, d, sems.at[at + i]) for i, (s, d) in enumerate(pairs)]
    for copy in copies:
        copy.start()
    return copies


def start_out(pairs, sems, at):
    copies = [pltpu.make_async_copy(d, s, sems.at[at + i]) for i, (s, d) in enumerate(pairs)]
    for copy in copies:
        copy.start()
    return copies


def out_views(by_blocks, hbm):
    if not by_blocks:
        return hbm[:2], hbm[2:]
    views = [ref.at[k] for ref in hbm for k in range(ref.shape[0])]
    return views, views


def wait_all(copies):
    for copy in copies:
        copy.wait()


def fill_mask(sizes, seqs, starts_ref, place_ref, mask_ref):
    shape = (sizes.queries, sizes.keys)
    row = lax.broadcasted_iota(jnp.int32, shape, 0)
    col = lax.broadcasted_iota(jnp.int32, shape, 1)
    base = place_ref[0]
    total = place_ref[1]
    query = jnp.where(row < sizes.top, row, lax.shift_right_arithmetic(row - sizes.top, 4))
    left_at = sizes.rows + RIGHT_ROWS
    mem_at = left_at + LEFT_ROWS
    spot = jnp.where(col < left_at, col, col - mem_at)
    mem_seg = jnp.where(col < mem_at + sizes.segs, col - mem_at, col - mem_at - 2 * sizes.segs)
    key_seg = jnp.where(col < mem_at, lax.shift_right_arithmetic(spot, 4), mem_seg)
    near = (
        (key_seg == query)
        | ((spot >= query * SEG_LEN - LEFT_LEN) & (spot < query * SEG_LEN))
        | ((key_seg == query + 1) & (spot < query * SEG_LEN + SEG_LEN + RIGHT_LEN))
    )
    recent = (key_seg >= query - MEM_LEN) & (key_seg < query) & (row >= sizes.top)
    allowed = ((col < mem_at) & near) | ((col >= mem_at) & recent)
    key_abs = key_seg + base
    query_abs = query + base
    allowed = allowed & (key_abs >= 0) & (key_abs < total)
    if sizes.top:
        allowed = allowed & ((row < sizes.segs) | (row >= sizes.top))
    for n in range(seqs):
        key_owner = jnp.zeros(shape, jnp.int32)
        query_owner = jnp.zeros(shape, jnp.int32)
        for u in range(starts_ref.shape[1]):
            first = starts_ref[n, u]
            key_owner = key_owner + (key_abs >= first).astype(jnp.int32)
            query_owner = query_owner + (query_abs >= first).astype(jnp.int32)
        mask_ref[n] = jnp.where(allowed & (key_owner == query_owner), 0.0, -1e30)


def half_masks():
    lane = lax.broadcasted_iota(jnp.int32, (1, LANES), 1)
    even = (lane < LANES // 2).astype(F32)
    return even.astype(BF16), (1.0 - even).astype(BF16), lane < LANES // 2


def project(sizes, z_ref, qkv_ref, row_bias_ref, proj_ref):
    step = CHIPS_Z // 2
    for c in range(2):
        block = qkv_ref[pl.ds(c * step, step)].reshape(-1, sizes.width)
        wide = block.shape[0]
        made = nt(z_ref[...], block) + row_bias_ref[:, pl.ds(c * wide, wide)]
        proj_ref[:, pl.ds(c * wide, wide)] = made.astype(BF16)


def split_heads(sizes, ref, first, rows, lane):
    return ref[pl.ds(first, rows), pl.ds(lane, LANES)]


def attend(sizes, seqs, proj_ref, mask_ref, probs_ref, att_ref):
    even, odd, is_even = half_masks()
    scale = (sizes.width // HEADS) ** (-0.5)
    count = sizes.queries

    def body(p, carry):
        for n in range(seqs):
            lane = pl.multiple_of(p * LANES, LANES)
            query = proj_ref[pl.ds(n * sizes.ext, count), pl.ds(lane, LANES)]
            first = n * sizes.ext + sizes.top
            key = proj_ref[pl.ds(first, sizes.keys), pl.ds(sizes.width + lane, LANES)]
            value = proj_ref[pl.ds(first, sizes.keys), pl.ds(2 * sizes.width + lane, LANES)]
            scores = nt(jnp.concatenate([query * even, query * odd], axis=0), key) * scale
            outs = []
            for half in range(2):
                part = scores[half * count : (half + 1) * count] + mask_ref[n]
                part = jnp.exp(part - jnp.max(part, axis=1, keepdims=True))
                part = part * (1.0 / jnp.sum(part, axis=1, keepdims=True))
                probs_ref[n * sizes.pairs + p, pl.ds(half * count, count), :] = part
                outs.append(nn(part.astype(BF16), value))
            att_ref[pl.ds(n * count, count), pl.ds(lane, LANES)] = jnp.where(
                is_even, outs[0], outs[1]
            ).astype(BF16)
        return carry

    lax.fori_loop(0, sizes.pairs, body, 0)


def attend_back(sizes, seqs, proj_ref, probs_ref, go_ref, gproj_ref):
    even, odd, is_even = half_masks()
    scale = (sizes.width // HEADS) ** (-0.5)
    count = sizes.queries
    wide = sizes.width
    for n in range(seqs):
        base = n * sizes.ext
        rest = sizes.ext - count
        gproj_ref[pl.ds(base + count, rest), pl.ds(0, wide)] = jnp.zeros((rest, wide), BF16)
        if sizes.top:
            gproj_ref[pl.ds(base, sizes.top), pl.ds(wide, 2 * wide)] = jnp.zeros(
                (sizes.top, 2 * wide), BF16
            )

    def body(p, carry):
        for n in range(seqs):
            lane = pl.multiple_of(p * LANES, LANES)
            base = n * sizes.ext
            first = base + sizes.top
            query = proj_ref[pl.ds(base, count), pl.ds(lane, LANES)]
            key = proj_ref[pl.ds(first, sizes.keys), pl.ds(wide + lane, LANES)]
            value = proj_ref[pl.ds(first, sizes.keys), pl.ds(2 * wide + lane, LANES)]
            grad = go_ref[pl.ds(n * count, count), pl.ds(lane, LANES)]
            queries = jnp.concatenate([query * even, query * odd], axis=0)
            grads = jnp.concatenate([grad * even, grad * odd], axis=0)
            probs = probs_ref[n * sizes.pairs + p]
            grad_values = tn(probs.astype(BF16), grads)
            grad_probs = nt(grads, value)
            weighted = grad_probs * probs
            grad_scores = (
                (weighted - probs * jnp.sum(weighted, axis=1, keepdims=True)) * scale
            ).astype(BF16)
            grad_keys = tn(grad_scores, queries)
            grad_query = jnp.where(
                is_even, nn(grad_scores[:count], key), nn(grad_scores[count:], key)
            )
            gproj_ref[pl.ds(base, count), pl.ds(lane, LANES)] = grad_query.astype(BF16)
            gproj_ref[pl.ds(first, sizes.keys), pl.ds(wide + lane, LANES)] = grad_keys.astype(BF16)
            gproj_ref[pl.ds(first, sizes.keys), pl.ds(2 * wide + lane, LANES)] = (
                grad_values.astype(BF16)
            )
        return carry

    lax.fori_loop(0, sizes.pairs, body, 0)


def gelu_both(upward):
    half = 0.5 * (1.0 + lax.erf(upward * ROOT_HALF))
    slope = half + upward * jnp.exp(-0.5 * upward * upward) * INV_ROOT_TWO_PI
    return upward * half, slope


def up_block(up_ref, c, wide):
    step = wide // (up_ref.shape[1] * up_ref.shape[2])
    return up_ref[pl.ds(c * step, step)].reshape(-1, up_ref.shape[3])


def down_block(down_ref, c, wide):
    at = pl.multiple_of(c * wide, wide)
    return down_ref[:, :, :, pl.ds(at, wide)].reshape(-1, wide)


def ffn_back_step(
    sizes, c, wide, grad_low, hidden_low, active, slope, up_ref, down_ref, gup_ref, gdown_ref, vec
):
    at = pl.multiple_of(c * wide, wide)
    up = up_block(up_ref, c, wide)
    down = down_block(down_ref, c, wide)
    grad_active = nn(grad_low, down)
    grad_up_f = grad_active * slope
    grad_up = grad_up_f.astype(BF16)
    gdown_ref[:, :, :, pl.ds(at, wide)] = (
        tn(grad_low, active).astype(BF16).reshape(gdown_ref.shape[:3] + (wide,))
    )
    step = wide // (gup_ref.shape[1] * gup_ref.shape[2])
    gup_ref[pl.ds(c * step, step)] = (
        tn(grad_up, hidden_low).astype(BF16).reshape((step,) + gup_ref.shape[1:])
    )
    vec[pl.ds(8 + c, 1), :] = col_sum(grad_up.astype(F32))
    return nn(grad_up, up)


def attn_back_stage(
    sizes, seqs, gz, grad_mem_ref, att_ref, proj_ref, probs_ref, z_ref, qkv_ref, out_ref,
    gqkv_ref, gout_ref, go_ref, gproj_ref, branch_ref, vec, gh_ref, gmem_ref, back_left_ref,
    back_right_ref, scaled_rows=None,
):
    wide = sizes.width
    count = sizes.queries
    bias_out = col_sum(gz)
    for n in range(seqs):
        if sizes.top:
            mem_grad = grad_mem_ref[pl.ds(n * sizes.segs, sizes.segs), :]
            bias_out = bias_out + col_sum(mem_grad)
            branch_ref[pl.ds(n * count, sizes.top), :] = jnp.concatenate(
                [mem_grad, jnp.zeros((sizes.top - sizes.segs, wide), F32)], axis=0
            ).astype(BF16)
        branch_ref[pl.ds(n * count + sizes.top, sizes.rows), :] = gz[
            n * sizes.rows : (n + 1) * sizes.rows
        ].astype(BF16)
    vec[pl.ds(5, 1), :] = bias_out
    branch = branch_ref[...]
    gout_ref[...] = tn(branch, att_ref[...]).astype(BF16).reshape(gout_ref.shape)
    go_ref[...] = nn(branch, out_ref[...].reshape(-1, wide)).astype(BF16)
    attend_back(sizes, seqs, proj_ref, probs_ref, go_ref, gproj_ref)
    vec[pl.ds(3, 1), :] = col_sum(gproj_ref[:, pl.ds(0, wide)].astype(F32))
    vec[pl.ds(4, 1), :] = col_sum(gproj_ref[:, pl.ds(2 * wide, wide)].astype(F32))
    grad_ext = nn(gproj_ref[...], qkv_ref[...].reshape(-1, wide))
    gain_sum = jnp.zeros((1, wide), F32)
    bias_sum = jnp.zeros((1, wide), F32)
    for n in range(seqs):
        base = n * sizes.ext
        own = grad_ext[base + sizes.top : base + sizes.top + sizes.rows]
        if sizes.top:
            spread = grad_ext[base : base + sizes.segs] * (1.0 / SEG_LEN)
            own = own + segment_spread(sizes.rows, wide, spread)
        gh_ref[pl.ds(n * sizes.rows, sizes.rows), :] = own
        mem = base + sizes.mem_at
        gmem_ref[pl.ds(n * sizes.segs, sizes.segs), :] = grad_ext[mem : mem + sizes.segs]
        left = base + sizes.left_at
        back_left_ref[n] = grad_ext[left : left + BACK_ROWS].astype(BF16)
        right = base + sizes.right_at
        back_right_ref[n] = grad_ext[right : right + RIGHT_ROWS].astype(BF16)
        if scaled_rows is not None:
            grads = (
                own,
                grad_ext[right : right + RIGHT_ROWS],
                grad_ext[left : left + LEFT_ROWS],
            )
            for rows, scaled in zip(grads, scaled_rows(n)):
                gain_sum = gain_sum + col_sum(rows * scaled)
                bias_sum = bias_sum + col_sum(rows)
    if scaled_rows is not None:
        vec[pl.ds(0, 1), :] = gain_sum
        vec[pl.ds(2, 1), :] = bias_sum
    step = CHIPS_Z // 2
    part = gqkv_ref.shape[1] * gqkv_ref.shape[2] * step
    for c in range(2):
        gqkv_ref[pl.ds(c * step, step)] = (
            tn(gproj_ref[:, pl.ds(c * part, part)], z_ref[...])
            .astype(BF16)
            .reshape((step,) + gqkv_ref.shape[1:])
        )


def merge_halo(sizes, n, gh_ref, gmem_ref, from_right_ref, from_left_ref):
    first = n * sizes.rows
    back = from_right_ref[n].astype(F32)
    head = gh_ref[pl.ds(first, RIGHT_ROWS), :] + from_left_ref[n].astype(F32)
    middle = gh_ref[pl.ds(first + RIGHT_ROWS, sizes.rows - RIGHT_ROWS - LEFT_ROWS), :]
    tail = gh_ref[pl.ds(first + sizes.rows - LEFT_ROWS, LEFT_ROWS), :] + back[:LEFT_ROWS]
    mem = gmem_ref[pl.ds(n * sizes.segs, sizes.segs), :] + back[LEFT_ROWS + sizes.segs :]
    return jnp.concatenate([head, middle, tail], axis=0), mem


def pack_kernel(places, qkv_ref, out_ref, up_ref, down_ref, *packed):
    eye = identity(LANES)
    high, wide, low = qkv_ref.shape[1], out_ref.shape[1], down_ref.shape[1]
    up = up_ref.shape[2]
    for layer, (attn, attn_at, ffn, ffn_at) in enumerate(places):
        ref = packed[attn]
        ref[pl.ds(attn_at, high), :] = qkv_ref[layer]
        ref[pl.ds(attn_at + high, wide), :] = out_ref[layer]
        ref = packed[ffn]
        ref[pl.ds(ffn_at, up), :] = tn(up_ref[layer], eye).astype(BF16)
        for part in range(down_ref.shape[2] // LANES):
            ref[pl.ds(ffn_at + up + part * low, low), :] = down_ref[
                layer, :, pl.ds(part * LANES, LANES)
            ]


def unpack_kernel(each, places, *refs):
    sources, (qkv_ref, out_ref, up_ref, down_ref) = refs[:-4], refs[-4:]
    eye = identity(LANES)
    high, wide, low = qkv_ref.shape[1], out_ref.shape[1], down_ref.shape[1]
    up = up_ref.shape[2]

    def total(source, first, rows):
        value = sources[source * each][pl.ds(first, rows), :].astype(F32)
        for part in sources[source * each + 1 : (source + 1) * each]:
            value = value + part[pl.ds(first, rows), :].astype(F32)
        return value

    for layer, (attn, attn_at, ffn, ffn_at) in enumerate(places):
        qkv_ref[layer] = total(attn, attn_at, high)
        out_ref[layer] = total(attn, attn_at + high, wide)
        up_ref[layer] = nt(eye, total(ffn, ffn_at, up).astype(BF16))
        for part in range(down_ref.shape[2] // LANES):
            down_ref[layer, :, pl.ds(part * LANES, LANES)] = total(
                ffn, ffn_at + up + part * low, low
            )


def stack_kernel(count, place_ref, *refs):
    sources, out_ref, sems = refs[:count], refs[count], refs[count + 1]
    copies = []
    for k, source in enumerate(sources):
        spot = lax.rem(place_ref[0] + count - k, count)
        copies.append(pltpu.make_async_copy(source, out_ref.at[spot], sems.at[k]))
    for copy in copies:
        copy.start()
    wait_all(copies)


def split_kernel(count, place_ref, mine_ref, theirs_ref, *outs):
    for k, out in enumerate(outs):
        spot = lax.rem(place_ref[0] + k, count)
        out[...] = (mine_ref[spot].astype(F32) + theirs_ref[spot].astype(F32)).astype(BF16)


def first_attn_kernel(
    sizes, seqs, mats, by_blocks, count_in, at, place_ref, starts_ref, frames_ref, left_ref,
    right_ref, gains_ref, biases_ref, row_bias_ref, *refs
):
    hbm = refs[:count_in]
    z_ref, proj_ref, probs_ref, att_ref, mixed_ref, mem_ref, qkv_ref, out_ref, mask_ref, sems = (
        refs[count_in:]
    )
    wide = sizes.width
    copies = start_in(
        attn_pairs(mats, by_blocks, hbm, at, qkv_ref, out_ref, place_ref), sems, 0
    )
    gain = gains_ref[0, pl.ds(0, 1), :]
    bias = biases_ref[0, pl.ds(0, 1), :]
    pad = jnp.zeros((TILE - sizes.segs, wide), F32)
    for n in range(seqs):
        own = frames_ref[n].astype(F32)
        before = left_ref[n].astype(F32)
        hidden = norm_forward(own, gain, bias)[0]
        halo = norm_forward(before[before.shape[0] - LEFT_ROWS :], gain, bias)[0]
        after = norm_forward(right_ref[n].astype(F32), gain, bias)[0]
        memory = jnp.concatenate(
            [
                segment_mean(own),
                jnp.zeros((sizes.segs - before.shape[0] // SEG_LEN, wide), F32),
                segment_mean(before),
            ],
            axis=0,
        )
        base = n * sizes.ext
        z_ref[pl.ds(base, sizes.top), :] = jnp.concatenate(
            [segment_mean(hidden), pad], axis=0
        ).astype(BF16)
        z_ref[pl.ds(base + sizes.top, sizes.rows), :] = hidden.astype(BF16)
        z_ref[pl.ds(base + sizes.right_at, RIGHT_ROWS), :] = after.astype(BF16)
        z_ref[pl.ds(base + sizes.left_at, LEFT_ROWS), :] = halo.astype(BF16)
        z_ref[pl.ds(base + sizes.mem_at, MEM_ROWS), :] = memory.astype(BF16)
    fill_mask(sizes, seqs, starts_ref, place_ref, mask_ref)
    wait_all(copies)
    project(sizes, z_ref, qkv_ref, row_bias_ref, proj_ref)
    attend(sizes, seqs, proj_ref, mask_ref, probs_ref, att_ref)
    mixed = nt(att_ref[...], out_ref[...].reshape(-1, wide)) + biases_ref[0, pl.ds(3, 1), :]
    for n in range(seqs):
        base = n * sizes.queries
        mem_ref[pl.ds(n * sizes.segs, sizes.segs), :] = mixed[base : base + sizes.segs]
        mixed_ref[pl.ds(n * sizes.rows, sizes.rows), :] = (
            frames_ref[n].astype(F32) + mixed[base + sizes.top : base + sizes.top + sizes.rows]
        )


def first_ffn_kernel(
    sizes, seqs, mats, by_blocks, count_in, at, place_ref, mixed_ref, mem_ref, gains_ref,
    biases_ref, ffn_bias_ref, *refs
):
    hbm = refs[:count_in]
    (
        next_ref, active_ref, slope_ref, low_ref, send_right_ref, send_left_ref, up_ref, down_ref,
        hidden_ref, sems,
    ) = refs[count_in:]
    copies = start_in(ffn_pairs(mats, by_blocks, hbm, at, up_ref, down_ref, place_ref), sems, 0)
    mixed = mixed_ref[...]
    hidden, _, _ = norm_forward(mixed, gains_ref[0, pl.ds(1, 1), :], biases_ref[0, pl.ds(4, 1), :])
    hidden_ref[...] = hidden.astype(BF16)
    next_ref[...] = mixed + biases_ref[0, pl.ds(5, 1), :]
    wait_all(copies)
    wide = sizes.width

    def body(c, carry):
        at_lane = pl.multiple_of(c * wide, wide)
        upward = nt(hidden_ref[...], up_block(up_ref, c, wide))
        upward = upward + ffn_bias_ref[pl.ds(0, 1), pl.ds(at_lane, wide)]
        active, slope = gelu_both(upward)
        active = active.astype(BF16)
        active_ref[:, pl.ds(at_lane, wide)] = active
        slope_ref[:, pl.ds(at_lane, wide)] = slope.astype(BF16)
        next_ref[...] += nt(active, down_block(down_ref, c, wide))
        return carry

    lax.fori_loop(0, sizes.ff // wide, body, 0)
    low, _, _ = norm_forward(
        next_ref[...], gains_ref[1, pl.ds(0, 1), :], biases_ref[1, pl.ds(0, 1), :]
    )
    low = low.astype(BF16)
    low_ref[...] = low
    for n in range(seqs):
        base = n * sizes.rows
        send_right_ref[n, pl.ds(0, LEFT_ROWS), :] = low[
            base + sizes.rows - LEFT_ROWS : base + sizes.rows
        ]
        send_right_ref[n, pl.ds(LEFT_ROWS, MEM_ROWS), :] = jnp.concatenate(
            [
                mem_ref[pl.ds(n * sizes.segs, sizes.segs), :],
                jnp.zeros((MEM_ROWS - sizes.segs, wide), F32),
            ],
            axis=0,
        ).astype(BF16)
        send_left_ref[n] = low[base : base + RIGHT_ROWS]


def last_layer_kernel(
    sizes, seqs, mats, by_blocks, count_in, attn_at, ffn_at, place_ref, starts_ref, low_ref,
    left_ref, right_ref, mem_ref, inputs_ref, out_grad_ref, gains_ref, biases_ref, ffn_bias_ref,
    row_bias_ref, *refs
):
    hbm = refs[:count_in]
    count_out = 2 if by_blocks else 4
    (encoded_ref, gz_ref, gh_ref, gmem_ref, back_left_ref, back_right_ref, vec) = refs[
        count_in : count_in + 7
    ]
    hbm_out = refs[count_in + 7 : count_in + 7 + count_out]
    (
        qkv_ref, out_ref, up_ref, down_ref, gqkv_ref, gout_ref, gup_ref, gdown_ref, mask_ref,
        z_ref, proj_ref, probs_ref, att_ref, hidden_ref, go_ref, gproj_ref, branch_ref,
        grad_low_ref, grad_hidden_ref, sems,
    ) = refs[count_in + 7 + count_out :]
    attn_hbm, ffn_hbm = (hbm, hbm) if by_blocks else (hbm[:2], hbm[2:])
    attn_out, ffn_out = out_views(by_blocks, hbm_out)
    wide = sizes.width
    attn_copies = start_in(
        attn_pairs(mats, by_blocks, attn_hbm, attn_at, qkv_ref, out_ref, place_ref), sems, 0
    )
    ffn_copies = start_in(
        ffn_pairs(mats, by_blocks, ffn_hbm, ffn_at, up_ref, down_ref, place_ref),
        sems,
        len(attn_copies),
    )
    vec[...] = jnp.zeros_like(vec)
    for n in range(seqs):
        base = n * sizes.ext
        z_ref[pl.ds(base, sizes.rows), :] = low_ref[pl.ds(n * sizes.rows, sizes.rows), :]
        z_ref[pl.ds(base + sizes.right_at, RIGHT_ROWS), :] = right_ref[n]
        z_ref[pl.ds(base + sizes.left_at, LEFT_ROWS), :] = left_ref[n, pl.ds(0, LEFT_ROWS), :]
        memory = jnp.concatenate(
            [
                mem_ref[pl.ds(n * sizes.segs, sizes.segs), :],
                left_ref[n, pl.ds(LEFT_ROWS, MEM_ROWS), :].astype(F32)[: sizes.segs],
            ],
            axis=0,
        )
        z_ref[pl.ds(base + sizes.mem_at, MEM_ROWS), :] = memory.astype(BF16)
        grad_low_ref[pl.ds(n * sizes.rows, sizes.rows), :] = out_grad_ref[n]
    fill_mask(sizes, seqs, starts_ref, place_ref, mask_ref)
    wait_all(attn_copies)
    project(sizes, z_ref, qkv_ref, row_bias_ref, proj_ref)
    attend(sizes, seqs, proj_ref, mask_ref, probs_ref, att_ref)
    mixed = (
        inputs_ref[...]
        + nt(att_ref[...], out_ref[...].reshape(-1, wide))
        + biases_ref[1, pl.ds(3, 1), :]
    )
    gain = gains_ref[1, pl.ds(1, 1), :]
    hidden, scaled, inverse = norm_forward(mixed, gain, biases_ref[1, pl.ds(4, 1), :])
    hidden_ref[...] = hidden.astype(BF16)
    for n in range(seqs):
        encoded_ref[n] = mixed[n * sizes.rows : (n + 1) * sizes.rows] + biases_ref[
            1, pl.ds(5, 1), :
        ]
    grad_hidden_ref[...] = jnp.zeros_like(grad_hidden_ref)
    wait_all(ffn_copies)

    def body(c, carry):
        at_lane = pl.multiple_of(c * wide, wide)
        upward = nt(hidden_ref[...], up_block(up_ref, c, wide))
        upward = upward + ffn_bias_ref[pl.ds(1, 1), pl.ds(at_lane, wide)]
        active, slope = gelu_both(upward)
        active = active.astype(BF16)
        made = nt(active, down_block(down_ref, c, wide))
        for n in range(seqs):
            encoded_ref[n] += made[n * sizes.rows : (n + 1) * sizes.rows]
        grad_hidden_ref[...] += ffn_back_step(
            sizes, c, wide, grad_low_ref[...], hidden_ref[...], active, slope, up_ref, down_ref,
            gup_ref, gdown_ref, vec,
        )
        return carry

    lax.fori_loop(0, sizes.ff // wide, body, 0)
    out_at = len(attn_copies) + len(ffn_copies)
    outs = start_out(
        ffn_pairs(mats, by_blocks, ffn_out, ffn_at, gup_ref, gdown_ref, place_ref), sems, out_at
    )
    grad = grad_low_ref[...].astype(F32)
    grad_hidden = grad_hidden_ref[...]
    vec[pl.ds(1, 1), :] = col_sum(grad_hidden * scaled)
    vec[pl.ds(6, 1), :] = col_sum(grad_hidden)
    vec[pl.ds(7, 1), :] = col_sum(grad)
    gz = grad + norm_backward(grad_hidden, scaled, inverse, gain)
    gz_ref[...] = gz
    attn_back_stage(
        sizes, seqs, gz, None, att_ref, proj_ref, probs_ref, z_ref, qkv_ref, out_ref, gqkv_ref,
        gout_ref, go_ref, gproj_ref, branch_ref, vec, gh_ref, gmem_ref, back_left_ref,
        back_right_ref,
    )
    outs = outs + start_out(
        attn_pairs(mats, by_blocks, attn_out, attn_at, gqkv_ref, gout_ref, place_ref),
        sems,
        out_at + len(outs),
    )
    wait_all(outs)


def first_ffn_back_kernel(
    last, sizes, seqs, mats, by_blocks, count_in, count_out, at_in, place_ref, inputs_ref,
    gz_in_ref, gh_in_ref, gmem_in_ref, from_right_ref, from_left_ref, mixed_ref, active_ref,
    slope_ref, gains_ref, biases_ref, *refs
):
    hbm = refs[:count_in]
    gz_ref, grad_mem_ref, upper_vec, vec = refs[count_in : count_in + 4]
    refs = refs[count_in + 4 :]
    hbm_out = refs[:count_out]
    if by_blocks:
        hbm_out = out_views(by_blocks, hbm_out)[0]
    (
        up_ref, down_ref, gup_ref, gdown_ref, hidden_ref, grad_low_ref, grad_ref, grad_hidden_ref,
        sems,
    ) = refs[count_out:]
    wide = sizes.width
    copies = start_in(
        ffn_pairs(mats, by_blocks, hbm, at_in, up_ref, down_ref, place_ref), sems, 0
    )
    vec[...] = jnp.zeros_like(vec)
    upper_vec[...] = jnp.zeros_like(upper_vec)
    gain = gains_ref[1, pl.ds(0, 1), :]
    gain_sum = jnp.zeros((1, wide), F32)
    bias_sum = jnp.zeros((1, wide), F32)
    for n in range(seqs):
        rows = pl.ds(n * sizes.rows, sizes.rows)
        _, scaled, inverse = norm_forward(
            inputs_ref[rows, :], gain, biases_ref[1, pl.ds(0, 1), :]
        )
        total, mem = merge_halo(last, n, gh_in_ref, gmem_in_ref, from_right_ref, from_left_ref)
        gain_sum = gain_sum + col_sum(total * scaled)
        bias_sum = bias_sum + col_sum(total)
        grad = gz_in_ref[rows, :] + norm_backward(total, scaled, inverse, gain)
        grad_ref[rows, :] = grad
        grad_low_ref[rows, :] = grad.astype(BF16)
        grad_mem_ref[pl.ds(n * sizes.segs, sizes.segs), :] = mem
    upper_vec[pl.ds(0, 1), :] = gain_sum
    upper_vec[pl.ds(2, 1), :] = bias_sum
    gain = gains_ref[0, pl.ds(1, 1), :]
    hidden, scaled, inverse = norm_forward(
        mixed_ref[...], gain, biases_ref[0, pl.ds(4, 1), :]
    )
    hidden_ref[...] = hidden.astype(BF16)
    grad_hidden_ref[...] = jnp.zeros_like(grad_hidden_ref)
    wait_all(copies)

    def body(c, carry):
        at_lane = pl.multiple_of(c * wide, wide)
        grad_hidden_ref[...] += ffn_back_step(
            sizes, c, wide, grad_low_ref[...], hidden_ref[...],
            active_ref[:, pl.ds(at_lane, wide)], slope_ref[:, pl.ds(at_lane, wide)].astype(F32),
            up_ref, down_ref, gup_ref, gdown_ref, vec,
        )
        return carry

    lax.fori_loop(0, sizes.ff // wide, body, 0)
    outs = start_out(
        ffn_pairs(mats, by_blocks, hbm_out, 0, gup_ref, gdown_ref, place_ref), sems, len(copies)
    )
    grad_hidden = grad_hidden_ref[...]
    grad = grad_ref[...]
    vec[pl.ds(1, 1), :] = col_sum(grad_hidden * scaled)
    vec[pl.ds(6, 1), :] = col_sum(grad_hidden)
    vec[pl.ds(7, 1), :] = col_sum(grad)
    gz_ref[...] = grad + norm_backward(grad_hidden, scaled, inverse, gain)
    wait_all(outs)


def first_attn_back_kernel(
    sizes, seqs, mats, by_blocks, count_in, count_out, at_in, place_ref, gz_ref, grad_mem_ref,
    att_ref, probs_ref, proj_ref, z_ref, frames_ref, left_ref, right_ref, gains_ref, biases_ref,
    *refs
):
    hbm = refs[:count_in]
    gh_ref, gmem_ref, back_left_ref, back_right_ref, vec = refs[count_in : count_in + 5]
    refs = refs[count_in + 5 :]
    hbm_out = refs[:count_out]
    if by_blocks:
        hbm_out = out_views(by_blocks, hbm_out)[0]
    qkv_ref, out_ref, gqkv_ref, gout_ref, go_ref, gproj_ref, branch_ref, sems = refs[count_out:]
    copies = start_in(
        attn_pairs(mats, by_blocks, hbm, at_in, qkv_ref, out_ref, place_ref), sems, 0
    )
    vec[...] = jnp.zeros_like(vec)
    gain = gains_ref[0, pl.ds(0, 1), :]
    bias = biases_ref[0, pl.ds(0, 1), :]

    def scaled_rows(n):
        before = left_ref[n, pl.ds(left_ref.shape[1] - LEFT_ROWS, LEFT_ROWS), :]
        parts = (frames_ref[n], right_ref[n], before)
        return [norm_forward(part.astype(F32), gain, bias)[1] for part in parts]

    wait_all(copies)
    attn_back_stage(
        sizes, seqs, gz_ref[...], grad_mem_ref, att_ref, proj_ref, probs_ref, z_ref, qkv_ref,
        out_ref, gqkv_ref, gout_ref, go_ref, gproj_ref, branch_ref, vec, gh_ref, gmem_ref,
        back_left_ref, back_right_ref, scaled_rows,
    )
    wait_all(
        start_out(
            attn_pairs(mats, by_blocks, hbm_out, 0, gqkv_ref, gout_ref, place_ref),
            sems,
            len(copies),
        )
    )


def frames_grad_kernel(
    sizes, seqs, frames_ref, gz_ref, gh_ref, gmem_ref, from_right_ref, from_left_ref, gains_ref,
    biases_ref, grad_ref
):
    gain = gains_ref[0, pl.ds(0, 1), :]
    for n in range(seqs):
        _, scaled, inverse = norm_forward(
            frames_ref[n].astype(F32), gain, biases_ref[0, pl.ds(0, 1), :]
        )
        total, mem = merge_halo(sizes, n, gh_ref, gmem_ref, from_right_ref, from_left_ref)
        grad_ref[n] = (
            gz_ref[pl.ds(n * sizes.rows, sizes.rows), :]
            + norm_backward(total, scaled, inverse, gain)
            + segment_spread(sizes.rows, sizes.width, mem * (1.0 / SEG_LEN))
        )


def shifted(value, axis, by):
    size = lax.axis_size(axis)
    pairs = [(i, i + by) for i in range(size) if 0 <= i + by < size]
    return lax.ppermute(value, axis, pairs)


def permuted(value, move):
    reps = lax.axis_size("rep")
    pairs = []
    for flat in range(lax.axis_size("seg") * reps):
        seg, rep = divmod(flat, reps)
        z, y, x, core = move(seg // CHIPS_Y, seg % CHIPS_Y, rep // 2, rep % 2)
        pairs.append((flat, (z * CHIPS_Y + y) * reps + 2 * x + core))
    return lax.ppermute(value, ("seg", "rep"), pairs)


def along_z(value, by):
    return permuted(value, lambda z, y, x, core: ((z + by) % CHIPS_Z, y, x, core))


def across_first(value):
    return permuted(value, lambda z, y, x, c: (z, y, x ^ 1, c) if c == 0 else (z, y ^ 1, x, c))


def across_second(value):
    return permuted(value, lambda z, y, x, c: (z, y ^ 1, x, c) if c == 0 else (z, y, x ^ 1, c))


def other_core(value):
    return permuted(value, lambda z, y, x, c: (z, y, x, c ^ 1))


def after(value, *others):
    return lax.optimization_barrier((value,) + others)[0]


def gather_z(shard, z_place):
    parts = [shard] + [along_z(shard, by) for by in range(1, CHIPS_Z)]
    return call(
        lambda *refs: stack_kernel(CHIPS_Z, *refs),
        [smem_spec()] + [vmem_spec()] * CHIPS_Z,
        [((CHIPS_Z,) + shard.shape, BF16)],
        [hbm_spec()],
        [pltpu.SemaphoreType.DMA((CHIPS_Z,))],
        [z_place] + parts,
    )[0]


def gather_plane(here):
    first = across_first(here)
    return [here, first, across_second(here), across_second(first)]


def both_cores(blocks):
    return blocks + [other_core(block) for block in blocks]


def scatter_core(blocks, others):
    mine, theirs = blocks[0], other_core(blocks[1])
    far = (mine[2:4].astype(F32) + theirs[2:4].astype(F32)).astype(BF16)
    return mine, theirs, after(far, *others)


def scatter_second(hop):
    mine, theirs, far = hop
    came = across_second(far)

    def total(at):
        return (
            mine[at].astype(F32) + theirs[at].astype(F32) + came[at].astype(F32)
        ).astype(BF16)

    return total(0), total(1)


def scatter_first(hop, z_place):
    near, far = hop
    return call(
        lambda *refs: split_kernel(CHIPS_Z, *refs),
        [smem_spec()] + [vmem_spec()] * 2,
        [(near.shape[1:], BF16)] * CHIPS_Z,
        [vmem_spec()] * CHIPS_Z,
        [],
        [z_place, near, across_first(far)],
    )


def scatter_z(parts):
    return [parts[0]] + [along_z(parts[by], by) for by in range(1, CHIPS_Z)]


def sum_everywhere(value):
    count = lax.axis_size("seg") * lax.axis_size("rep")
    bit = 1
    while bit < count:
        value = value + lax.ppermute(value, ("seg", "rep"), [(i, i ^ bit) for i in range(count)])
        bit *= 2
    return value


def vmem_spec():
    return pl.BlockSpec(memory_space=pltpu.VMEM)


def smem_spec():
    return pl.BlockSpec(memory_space=pltpu.SMEM)


def hbm_spec():
    return pl.BlockSpec(memory_space=pl.ANY)


def call(body, in_specs, out_shapes, out_specs, scratch, args, flops=0, moved=0):
    return pl.pallas_call(
        body,
        in_specs=in_specs,
        out_shape=tuple(jax.ShapeDtypeStruct(shape, kind) for shape, kind in out_shapes),
        out_specs=tuple(out_specs),
        scratch_shapes=scratch,
        compiler_params=pltpu.CompilerParams(vmem_limit_bytes=VMEM_BYTES),
        cost_estimate=pl.CostEstimate(flops=flops, bytes_accessed=moved, transcendentals=0),
    )(*args)


def on_device(
    frames,
    utt_segments,
    out_grad,
    qkv_weight,
    out_weight,
    ffn_in_weight,
    ffn_out_weight,
    norm_gains,
    biases,
    ffn_bias,
):
    micros, groups, rows, width = frames.shape
    seqs = micros * groups
    ff = ffn_bias.shape[1]
    reps = lax.axis_size("rep")
    seg_count = lax.axis_size("seg")
    mats = Matrices(width, ff)
    by_blocks = width // reps == LANES and reps == 4 and seg_count == BLOCKS
    first = Sizes(rows, width, ff, True)
    last = Sizes(rows, width, ff, False)
    own = seqs * rows
    mem_own = seqs * first.segs

    seg_at = lax.axis_index("seg")
    seg_base = seg_at * first.segs
    rep_at = lax.axis_index("rep")
    place = [seg_base, jnp.int32(first.segs * seg_count)]
    y_at, x_at, core_at = seg_at % CHIPS_Y, rep_at // 2, rep_at % 2
    z_place = jnp.reshape(seg_at // CHIPS_Y, (1,)).astype(jnp.int32)
    for other in range(2):
        core = lax.bitwise_xor(core_at, other)
        for hop2 in range(2):
            for hop1 in range(2):
                x_hop = jnp.where(core == 0, hop1, hop2)
                y_hop = jnp.where(core == 0, hop2, hop1)
                place.append(lax.bitwise_xor(y_at, y_hop))
                place.append((lax.bitwise_xor(x_at, x_hop) * 2 + core) * LANES)
    place = jnp.stack([jnp.asarray(entry, jnp.int32) for entry in place])
    lengths = utt_segments.reshape(seqs, utt_segments.shape[2])
    starts = (jnp.cumsum(lengths, axis=1) - lengths).astype(jnp.int32)
    zero_bias = jnp.zeros((width,), F32)
    row_bias = jnp.stack(
        [jnp.concatenate([biases[l, 1], zero_bias, biases[l, 2]]) for l in range(LAYERS)]
    ).reshape(LAYERS, 1, 3 * width)

    frames_own = frames.reshape(seqs, rows, width)
    grads_own = out_grad.reshape(seqs, rows, width)
    far = MEM_LEN * SEG_LEN
    frames_left = shifted(frames_own[:, rows - far :], "seg", 1)
    frames_right = shifted(frames_own[:, :RIGHT_ROWS], "seg", -1)

    attn_rows, ffn_rows = mats.attn_rows, mats.ffn_rows
    if by_blocks:
        qkv_t, out_t, down_t = (
            jnp.swapaxes(member, 1, 2) for member in (qkv_weight, out_weight, ffn_out_weight)
        )
        places = [(0, 0, 1, 0), (2, 0, 2, attn_rows)]
        chunk_rows = [attn_rows, ffn_rows, attn_rows + ffn_rows]
        shards = call(
            lambda *refs: pack_kernel(places, *refs),
            [vmem_spec()] * 4,
            [((high, LANES), BF16) for high in chunk_rows],
            [vmem_spec()] * len(chunk_rows),
            [],
            (qkv_t, out_t, ffn_in_weight, down_t),
        )
        planes = []
        before = (frames_left, frames_right)
        for shard in shards:
            if planes:
                shard = after(shard, planes[-1][0])
            here = after(gather_z(shard, z_place), *before)
            planes.append(gather_plane(here))
            before = planes[-1][1:2]
        first_attn, first_ffn, last_all = (both_cores(plane) for plane in planes)
        first_at = 0, 0
        last_at = 0, attn_rows
        half = len(last_all) // 2
        grad_outs = [
            [((half, CHIPS_Z, high, LANES), BF16)] * 2 for high in chunk_rows
        ]
        copies_in = len(last_all) * (3 + mats.down_parts)
    else:
        whole = []
        for member, shape in zip(
            (qkv_weight, out_weight, ffn_in_weight, ffn_out_weight),
            (mats.qkv, mats.out, mats.up, mats.down),
        ):
            member = lax.all_gather(member, "rep", axis=1, tiled=True)
            member = lax.all_gather(member, "seg", axis=2, tiled=True)
            whole.append(jnp.swapaxes(member, 1, 2).reshape((LAYERS,) + shape))
        first_attn = [whole[0][0], whole[1][0]]
        first_ffn = [whole[2][0], whole[3][0]]
        last_all = [member[1] for member in whole]
        first_at = last_at = 0, 0
        shapes = [(shape, BF16) for shape in (mats.qkv, mats.out, mats.up, mats.down)]
        grad_outs = [shapes[:2], shapes[2:], shapes]
        copies_in = 4
    dma = pltpu.SemaphoreType.DMA

    z0, proj0, probs0, att0, mixed0, mem1 = call(
        lambda *refs: first_attn_kernel(
            first, seqs, mats, by_blocks, len(first_attn), first_at[0], *refs
        ),
        [smem_spec()] * 2 + [vmem_spec()] * 6 + [hbm_spec()] * len(first_attn),
        [
            ((seqs * first.ext, width), BF16),
            ((seqs * first.ext, 3 * width), BF16),
            ((seqs * first.pairs, 2 * first.queries, first.keys), F32),
            ((seqs * first.queries, width), BF16),
            ((own, width), F32),
            ((mem_own, width), F32),
        ],
        [vmem_spec()] * 6,
        [
            pltpu.VMEM(mats.qkv, BF16),
            pltpu.VMEM(mats.out, BF16),
            pltpu.VMEM((seqs, first.queries, first.keys), F32),
            dma((copies_in,)),
        ],
        (place, starts, frames_own, frames_left, frames_right, norm_gains, biases, row_bias[0])
        + tuple(first_attn),
        flops=40 * own * 4 * width * width,
        moved=8 * width * width,
    )
    x1, active0, slope0, low1, send_right, send_left = call(
        lambda *refs: first_ffn_kernel(first, seqs, mats, by_blocks, len(first_ffn), first_at[1], *refs),
        [smem_spec()] + [vmem_spec()] * 5 + [hbm_spec()] * len(first_ffn),
        [
            ((own, width), F32),
            ((own, ff), BF16),
            ((own, ff), BF16),
            ((own, width), BF16),
            ((seqs, BACK_ROWS, width), BF16),
            ((seqs, RIGHT_ROWS, width), BF16),
        ],
        [vmem_spec()] * 6,
        [
            pltpu.VMEM(mats.up, BF16),
            pltpu.VMEM(mats.down, BF16),
            pltpu.VMEM((own, width), BF16),
            dma((copies_in,)),
        ],
        (place, mixed0, mem1, norm_gains, biases, ffn_bias) + tuple(first_ffn),
        flops=16 * own * 2 * width * ff,
        moved=4 * width * ff,
    )
    left1 = shifted(send_right, "seg", 1)
    right1 = shifted(send_left, "seg", -1)

    vec_shape = (TILE, width)
    outs = call(
        lambda *refs: last_layer_kernel(
            last, seqs, mats, by_blocks, len(last_all), *last_at, *refs
        ),
        [smem_spec()] * 2 + [vmem_spec()] * 10 + [hbm_spec()] * len(last_all),
        [
            ((seqs, rows, width), F32),
            ((own, width), F32),
            ((own, width), F32),
            ((mem_own, width), F32),
            ((seqs, BACK_ROWS, width), BF16),
            ((seqs, RIGHT_ROWS, width), BF16),
            (vec_shape, F32),
        ]
        + grad_outs[2],
        [vmem_spec()] * 7 + [hbm_spec()] * len(grad_outs[2]),
        [
            pltpu.VMEM(mats.qkv, BF16),
            pltpu.VMEM(mats.out, BF16),
            pltpu.VMEM(mats.up, BF16),
            pltpu.VMEM(mats.down, BF16),
            pltpu.VMEM(mats.qkv, BF16),
            pltpu.VMEM(mats.out, BF16),
            pltpu.VMEM(mats.up, BF16),
            pltpu.VMEM(mats.down, BF16),
            pltpu.VMEM((seqs, last.queries, last.keys), F32),
            pltpu.VMEM((seqs * last.ext, width), BF16),
            pltpu.VMEM((seqs * last.ext, 3 * width), BF16),
            pltpu.VMEM((seqs * last.pairs, 2 * last.queries, last.keys), F32),
            pltpu.VMEM((seqs * last.queries, width), BF16),
            pltpu.VMEM((own, width), BF16),
            pltpu.VMEM((seqs * last.queries, width), BF16),
            pltpu.VMEM((seqs * last.ext, 3 * width), BF16),
            pltpu.VMEM((seqs * last.queries, width), BF16),
            pltpu.VMEM((own, width), BF16),
            pltpu.VMEM((own, width), F32),
            dma((2 * copies_in,)),
        ],
        (place, starts, low1, left1, right1, mem1, x1, grads_own, norm_gains, biases, ffn_bias,
         row_bias[1]) + tuple(last_all),
        flops=30 * own * (4 * width * width + 2 * width * ff),
        moved=4 * (4 * width * width + 2 * width * ff),
    )
    encoded, gz1, gh1, gmem1, back_left1, back_right1, vec1 = outs[:7]
    grad_blocks1 = outs[7:]
    from_right1 = shifted(back_left1, "seg", -1)
    from_left1 = shifted(back_right1, "seg", 1)

    if by_blocks:
        hop1 = scatter_core(grad_blocks1, (from_right1, from_left1))
    gz0, grad_mem, upper_vec, vec0_ffn, *grad_ffn0 = call(
        lambda *refs: first_ffn_back_kernel(
            last, first, seqs, mats, by_blocks, len(first_ffn), len(grad_outs[1]), first_at[1],
            *refs
        ),
        [smem_spec()] + [vmem_spec()] * 11 + [hbm_spec()] * len(first_ffn),
        [
            ((own, width), F32),
            ((mem_own, width), F32),
            (vec_shape, F32),
            (vec_shape, F32),
        ]
        + grad_outs[1],
        [vmem_spec()] * 4 + [hbm_spec()] * len(grad_outs[1]),
        [
            pltpu.VMEM(mats.up, BF16),
            pltpu.VMEM(mats.down, BF16),
            pltpu.VMEM(mats.up, BF16),
            pltpu.VMEM(mats.down, BF16),
            pltpu.VMEM((own, width), BF16),
            pltpu.VMEM((own, width), BF16),
            pltpu.VMEM((own, width), F32),
            pltpu.VMEM((own, width), F32),
            dma((2 * copies_in,)),
        ],
        (place, x1, gz1, gh1, gmem1, from_right1, from_left1, mixed0, active0, slope0, norm_gains,
         biases) + tuple(first_ffn),
        flops=28 * own * 2 * width * ff,
        moved=8 * width * ff,
    )
    if by_blocks:
        hop1 = scatter_second(hop1)
        gz0_tied = after(gz0, *hop1)
        hop_ffn = scatter_core(grad_ffn0, hop1)
    else:
        gz0_tied = gz0
    gh0, gmem0, back_left0, back_right0, vec0_attn, *grad_attn0 = call(
        lambda *refs: first_attn_back_kernel(
            first, seqs, mats, by_blocks, len(first_attn), len(grad_outs[0]), first_at[0], *refs
        ),
        [smem_spec()] + [vmem_spec()] * 11 + [hbm_spec()] * len(first_attn),
        [
            ((own, width), F32),
            ((mem_own, width), F32),
            ((seqs, BACK_ROWS, width), BF16),
            ((seqs, RIGHT_ROWS, width), BF16),
            (vec_shape, F32),
        ]
        + grad_outs[0],
        [vmem_spec()] * 5 + [hbm_spec()] * len(grad_outs[0]),
        [
            pltpu.VMEM(mats.qkv, BF16),
            pltpu.VMEM(mats.out, BF16),
            pltpu.VMEM(mats.qkv, BF16),
            pltpu.VMEM(mats.out, BF16),
            pltpu.VMEM((seqs * first.queries, width), BF16),
            pltpu.VMEM((seqs * first.ext, 3 * width), BF16),
            pltpu.VMEM((seqs * first.queries, width), BF16),
            dma((2 * copies_in,)),
        ],
        (place, gz0_tied, grad_mem, att0, probs0, proj0, z0, frames_own, frames_left, frames_right,
         norm_gains, biases) + tuple(first_attn),
        flops=56 * own * 4 * width * width,
        moved=16 * width * width,
    )
    from_right0 = shifted(back_left0, "seg", -1)
    from_left0 = shifted(back_right0, "seg", 1)
    gz0_last = gz0
    if by_blocks:
        split1 = scatter_first(hop1, z_place)
        gz0_last = after(gz0, *split1)
    frames_grad = call(
        lambda *refs: frames_grad_kernel(first, seqs, *refs),
        [vmem_spec()] * 8,
        [((seqs, rows, width), F32)],
        [vmem_spec()],
        [],
        (frames_own, gz0_last, gh0, gmem0, from_right0, from_left0, norm_gains, biases),
    )[0]

    if by_blocks:
        hop_ffn = scatter_second(hop_ffn)
        hop_attn = scatter_second(scatter_core(grad_attn0, ()))
        parts = [
            scatter_z(scatter_first(hop_attn, z_place)),
            scatter_z(scatter_first(hop_ffn, z_place)),
            scatter_z(split1),
        ]
        shapes = [member.shape for member in (qkv_t, out_t, ffn_in_weight, down_t)]
        reduced = call(
            lambda *refs: unpack_kernel(CHIPS_Z, places, *refs),
            [vmem_spec()] * (3 * CHIPS_Z),
            [(shape, F32) for shape in shapes],
            [vmem_spec()] * 4,
            [],
            parts[0] + parts[1] + parts[2],
        )
        reduced = [
            jnp.swapaxes(reduced[0], 1, 2),
            jnp.swapaxes(reduced[1], 1, 2),
            reduced[2],
            jnp.swapaxes(reduced[3], 1, 2),
        ]
    else:
        reduced = []
        for member0, member1 in zip(grad_attn0 + grad_ffn0, grad_blocks1):
            both = jnp.stack([member0, member1]).reshape(LAYERS, -1, member0.shape[3])
            both = jnp.swapaxes(both, 1, 2)
            both = lax.psum_scatter(both, "seg", scatter_dimension=2, tiled=True)
            both = lax.psum_scatter(both, "rep", scatter_dimension=1, tiled=True)
            reduced.append(both.astype(F32))

    small = sum_everywhere(jnp.stack([vec0_ffn + vec0_attn, vec1 + upper_vec]))
    return (
        encoded.reshape(frames.shape),
        frames_grad.reshape(frames.shape),
        reduced[0],
        reduced[1],
        reduced[2],
        reduced[3],
        small[:, 0:2],
        small[:, 2:8],
        small[:, 8:12].reshape(ffn_bias.shape),
    )


def solution(mesh):
    in_specs = (
        P(None, "rep", "seg", None),
        P(None, "rep", None),
        P(None, "rep", "seg", None),
        P(None, "rep", "seg"),
        P(None, "rep", "seg"),
        P(None, "rep", "seg"),
        P(None, "rep", "seg"),
        P(),
        P(),
        P(),
    )
    out_specs = (
        P(None, "rep", "seg", None),
        P(None, "rep", "seg", None),
        P(None, "rep", "seg"),
        P(None, "rep", "seg"),
        P(None, "rep", "seg"),
        P(None, "rep", "seg"),
        P(),
        P(),
        P(),
    )
    return jax.shard_map(
        on_device, mesh=mesh, in_specs=in_specs, out_specs=out_specs, check_vma=False
    )
```

```python
import jax
import jax.numpy as jnp
from jax import lax
from jax.experimental import pallas as pl
from jax.experimental.pallas import tpu as pltpu
from jax.sharding import PartitionSpec as P

HEADS = 8
SEG_LEN = 16
LEFT_LEN = 30
RIGHT_LEN = 4
MEM_LEN = 4
LAYERS = 2

EPS = 1e-05
ROOT_HALF = 0.7071067811865476
INV_ROOT_TWO_PI = 0.3989422804014327

LANES = 128
TILE = 16
RIGHT_ROWS = 16
LEFT_ROWS = 32
MEM_ROWS = 16
BACK_ROWS = LEFT_ROWS + MEM_ROWS
CHIPS_Z = 4
CHIPS_Y = 2
BLOCKS = CHIPS_Z * CHIPS_Y
SMALL_ROWS = 128
VMEM_BYTES = 56 * 1024 * 1024

BF16 = jnp.bfloat16
F32 = jnp.float32


def nn(a, b):
    return lax.dot_general(a, b, (((1,), (0,)), ((), ())), preferred_element_type=F32)


def nt(a, b):
    return lax.dot_general(a, b, (((1,), (1,)), ((), ())), preferred_element_type=F32)


def tn(a, b):
    return lax.dot_general(a, b, (((0,), (0,)), ((), ())), preferred_element_type=F32)


def col_sum(value):
    return jnp.sum(value, axis=0, keepdims=True)


def norm_forward(inputs, gain, bias):
    center = inputs - jnp.mean(inputs, axis=1, keepdims=True)
    inverse = lax.rsqrt(jnp.mean(center * center, axis=1, keepdims=True) + EPS)
    scaled = center * inverse
    return scaled * gain + bias, scaled, inverse


def norm_backward(grad_in, scaled, inverse, gain):
    grad_scaled = grad_in * gain
    return inverse * (
        grad_scaled
        - jnp.mean(grad_scaled, axis=1, keepdims=True)
        - scaled * jnp.mean(grad_scaled * scaled, axis=1, keepdims=True)
    )


def segment_mean(inputs):
    rows, width = inputs.shape
    return jnp.mean(inputs.reshape(rows // SEG_LEN, SEG_LEN, width), axis=1)


def segment_spread(rows, width, per_segment):
    segs = rows // SEG_LEN
    return jnp.broadcast_to(per_segment[:, None, :], (segs, SEG_LEN, width)).reshape(rows, width)


def identity(size):
    row = lax.broadcasted_iota(jnp.int32, (size, size), 0)
    col = lax.broadcasted_iota(jnp.int32, (size, size), 1)
    return (row == col).astype(F32).astype(BF16)


class Sizes:
    def __init__(self, rows, width, ff, with_summary):
        self.rows = rows
        self.width = width
        self.ff = ff
        self.segs = rows // SEG_LEN
        self.top = TILE if with_summary else 0
        self.keys = rows + RIGHT_ROWS + LEFT_ROWS + MEM_ROWS
        self.ext = self.top + self.keys
        self.queries = self.top + rows
        self.right_at = self.top + rows
        self.left_at = self.right_at + RIGHT_ROWS
        self.mem_at = self.left_at + LEFT_ROWS
        self.pairs = width // LANES


class Matrices:
    def __init__(self, width, ff):
        self.qkv = (CHIPS_Z, CHIPS_Y, 3 * width // BLOCKS, width)
        self.out = (CHIPS_Z, CHIPS_Y, width // BLOCKS, width)
        self.up = (CHIPS_Z, CHIPS_Y, ff // BLOCKS, width)
        self.down = (CHIPS_Z, CHIPS_Y, width // BLOCKS, ff)
        self.down_parts = ff // width
        self.attn_rows = self.qkv[2] + self.out[2]
        self.ffn_rows = self.up[2] + self.down_parts * self.down[2]


def attn_pairs(mats, by_blocks, hbm, first, qkv_ref, out_ref, place_ref):
    if not by_blocks:
        return [(hbm[0], qkv_ref), (hbm[1], out_ref)]
    pairs = []
    high = mats.qkv[2]
    for k, block in enumerate(hbm):
        row = place_ref[2 + 2 * k]
        lane = pl.multiple_of(place_ref[3 + 2 * k], LANES)
        pairs.append(
            (block.at[:, pl.ds(first, high), :], qkv_ref.at[:, row, :, pl.ds(lane, LANES)])
        )
        pairs.append(
            (
                block.at[:, pl.ds(first + high, mats.out[2]), :],
                out_ref.at[:, row, :, pl.ds(lane, LANES)],
            )
        )
    return pairs


def ffn_pairs(mats, by_blocks, hbm, first, up_ref, down_ref, place_ref):
    if not by_blocks:
        return [(hbm[0], up_ref), (hbm[1], down_ref)]
    pairs = []
    high = mats.up[2]
    low = mats.down[2]
    for k, block in enumerate(hbm):
        row = place_ref[2 + 2 * k]
        lane = pl.multiple_of(place_ref[3 + 2 * k], LANES)
        pairs.append(
            (block.at[:, pl.ds(first, high), :], up_ref.at[:, row, :, pl.ds(lane, LANES)])
        )
        for part in range(mats.down_parts):
            there = pl.multiple_of(
                place_ref[3 + 2 * k] * mats.down_parts + part * LANES, LANES
            )
            pairs.append(
                (
                    block.at[:, pl.ds(first + high + part * low, low), :],
                    down_ref.at[:, row, :, pl.ds(there, LANES)],
                )
            )
    return pairs


def start_in(pairs, sems, at):
    copies = [pltpu.make_async_copy(s, d, sems.at[at + i]) for i, (s, d) in enumerate(pairs)]
    for copy in copies:
        copy.start()
    return copies


def start_out(pairs, sems, at):
    copies = [pltpu.make_async_copy(d, s, sems.at[at + i]) for i, (s, d) in enumerate(pairs)]
    for copy in copies:
        copy.start()
    return copies


def out_views(by_blocks, hbm):
    if not by_blocks:
        return hbm[:2], hbm[2:]
    views = [ref.at[k] for ref in hbm for k in range(ref.shape[0])]
    return views, views


def wait_all(copies):
    for copy in copies:
        copy.wait()


def fill_mask(sizes, seqs, starts_ref, place_ref, mask_ref):
    shape = (sizes.queries, sizes.keys)
    row = lax.broadcasted_iota(jnp.int32, shape, 0)
    col = lax.broadcasted_iota(jnp.int32, shape, 1)
    base = place_ref[0]
    total = place_ref[1]
    query = jnp.where(row < sizes.top, row, lax.shift_right_arithmetic(row - sizes.top, 4))
    left_at = sizes.rows + RIGHT_ROWS
    mem_at = left_at + LEFT_ROWS
    spot = jnp.where(col < left_at, col, col - mem_at)
    mem_seg = jnp.where(col < mem_at + sizes.segs, col - mem_at, col - mem_at - 2 * sizes.segs)
    key_seg = jnp.where(col < mem_at, lax.shift_right_arithmetic(spot, 4), mem_seg)
    near = (
        (key_seg == query)
        | ((spot >= query * SEG_LEN - LEFT_LEN) & (spot < query * SEG_LEN))
        | ((key_seg == query + 1) & (spot < query * SEG_LEN + SEG_LEN + RIGHT_LEN))
    )
    recent = (key_seg >= query - MEM_LEN) & (key_seg < query) & (row >= sizes.top)
    allowed = ((col < mem_at) & near) | ((col >= mem_at) & recent)
    key_abs = key_seg + base
    query_abs = query + base
    allowed = allowed & (key_abs >= 0) & (key_abs < total)
    if sizes.top:
        allowed = allowed & ((row < sizes.segs) | (row >= sizes.top))
    for n in range(seqs):
        key_owner = jnp.zeros(shape, jnp.int32)
        query_owner = jnp.zeros(shape, jnp.int32)
        for u in range(starts_ref.shape[1]):
            first = starts_ref[n, u]
            key_owner = key_owner + (key_abs >= first).astype(jnp.int32)
            query_owner = query_owner + (query_abs >= first).astype(jnp.int32)
        mask_ref[n] = jnp.where(allowed & (key_owner == query_owner), 0.0, -1e30)


def half_masks():
    lane = lax.broadcasted_iota(jnp.int32, (1, LANES), 1)
    even = (lane < LANES // 2).astype(F32)
    return even.astype(BF16), (1.0 - even).astype(BF16), lane < LANES // 2


def project(sizes, z_ref, qkv_ref, row_bias_ref, proj_ref):
    step = CHIPS_Z // 2
    for c in range(2):
        block = qkv_ref[pl.ds(c * step, step)].reshape(-1, sizes.width)
        wide = block.shape[0]
        made = nt(z_ref[...], block) + row_bias_ref[:, pl.ds(c * wide, wide)]
        proj_ref[:, pl.ds(c * wide, wide)] = made.astype(BF16)


def split_heads(sizes, ref, first, rows, lane):
    return ref[pl.ds(first, rows), pl.ds(lane, LANES)]


def attend(sizes, seqs, proj_ref, mask_ref, probs_ref, att_ref):
    even, odd, is_even = half_masks()
    scale = (sizes.width // HEADS) ** (-0.5)
    count = sizes.queries

    def body(p, carry):
        for n in range(seqs):
            lane = pl.multiple_of(p * LANES, LANES)
            query = proj_ref[pl.ds(n * sizes.ext, count), pl.ds(lane, LANES)]
            first = n * sizes.ext + sizes.top
            key = proj_ref[pl.ds(first, sizes.keys), pl.ds(sizes.width + lane, LANES)]
            value = proj_ref[pl.ds(first, sizes.keys), pl.ds(2 * sizes.width + lane, LANES)]
            scores = nt(jnp.concatenate([query * even, query * odd], axis=0), key) * scale
            outs = []
            for half in range(2):
                part = scores[half * count : (half + 1) * count] + mask_ref[n]
                part = jnp.exp(part - jnp.max(part, axis=1, keepdims=True))
                part = part * (1.0 / jnp.sum(part, axis=1, keepdims=True))
                probs_ref[n * sizes.pairs + p, pl.ds(half * count, count), :] = part
                outs.append(nn(part.astype(BF16), value))
            att_ref[pl.ds(n * count, count), pl.ds(lane, LANES)] = jnp.where(
                is_even, outs[0], outs[1]
            ).astype(BF16)
        return carry

    lax.fori_loop(0, sizes.pairs, body, 0)


def attend_back(sizes, seqs, proj_ref, probs_ref, go_ref, gproj_ref):
    even, odd, is_even = half_masks()
    scale = (sizes.width // HEADS) ** (-0.5)
    count = sizes.queries
    wide = sizes.width
    for n in range(seqs):
        base = n * sizes.ext
        rest = sizes.ext - count
        gproj_ref[pl.ds(base + count, rest), pl.ds(0, wide)] = jnp.zeros((rest, wide), BF16)
        if sizes.top:
            gproj_ref[pl.ds(base, sizes.top), pl.ds(wide, 2 * wide)] = jnp.zeros(
                (sizes.top, 2 * wide), BF16
            )

    def body(p, carry):
        for n in range(seqs):
            lane = pl.multiple_of(p * LANES, LANES)
            base = n * sizes.ext
            first = base + sizes.top
            query = proj_ref[pl.ds(base, count), pl.ds(lane, LANES)]
            key = proj_ref[pl.ds(first, sizes.keys), pl.ds(wide + lane, LANES)]
            value = proj_ref[pl.ds(first, sizes.keys), pl.ds(2 * wide + lane, LANES)]
            grad = go_ref[pl.ds(n * count, count), pl.ds(lane, LANES)]
            queries = jnp.concatenate([query * even, query * odd], axis=0)
            grads = jnp.concatenate([grad * even, grad * odd], axis=0)
            probs = probs_ref[n * sizes.pairs + p]
            grad_values = tn(probs.astype(BF16), grads)
            grad_probs = nt(grads, value)
            weighted = grad_probs * probs
            grad_scores = (
                (weighted - probs * jnp.sum(weighted, axis=1, keepdims=True)) * scale
            ).astype(BF16)
            grad_keys = tn(grad_scores, queries)
            grad_query = jnp.where(
                is_even, nn(grad_scores[:count], key), nn(grad_scores[count:], key)
            )
            gproj_ref[pl.ds(base, count), pl.ds(lane, LANES)] = grad_query.astype(BF16)
            gproj_ref[pl.ds(first, sizes.keys), pl.ds(wide + lane, LANES)] = grad_keys.astype(BF16)
            gproj_ref[pl.ds(first, sizes.keys), pl.ds(2 * wide + lane, LANES)] = (
                grad_values.astype(BF16)
            )
        return carry

    lax.fori_loop(0, sizes.pairs, body, 0)


def gelu_both(upward):
    half = 0.5 * (1.0 + lax.erf(upward * ROOT_HALF))
    slope = half + upward * jnp.exp(-0.5 * upward * upward) * INV_ROOT_TWO_PI
    return upward * half, slope


def up_block(up_ref, c, wide):
    step = wide // (up_ref.shape[1] * up_ref.shape[2])
    return up_ref[pl.ds(c * step, step)].reshape(-1, up_ref.shape[3])


def down_block(down_ref, c, wide):
    at = pl.multiple_of(c * wide, wide)
    return down_ref[:, :, :, pl.ds(at, wide)].reshape(-1, wide)


def ffn_back_step(
    sizes, c, wide, grad_low, hidden_low, active, slope, up_ref, down_ref, gup_ref, gdown_ref, vec
):
    at = pl.multiple_of(c * wide, wide)
    up = up_block(up_ref, c, wide)
    down = down_block(down_ref, c, wide)
    grad_active = nn(grad_low, down)
    grad_up_f = grad_active * slope
    grad_up = grad_up_f.astype(BF16)
    gdown_ref[:, :, :, pl.ds(at, wide)] = (
        tn(grad_low, active).astype(BF16).reshape(gdown_ref.shape[:3] + (wide,))
    )
    step = wide // (gup_ref.shape[1] * gup_ref.shape[2])
    gup_ref[pl.ds(c * step, step)] = (
        tn(grad_up, hidden_low).astype(BF16).reshape((step,) + gup_ref.shape[1:])
    )
    vec[pl.ds(8 + c, 1), :] = col_sum(grad_up.astype(F32))
    return nn(grad_up, up)


def attn_back_stage(
    sizes, seqs, gz, grad_mem_ref, att_ref, proj_ref, probs_ref, z_ref, qkv_ref, out_ref,
    gqkv_ref, gout_ref, go_ref, gproj_ref, branch_ref, vec, gh_ref, gmem_ref, back_left_ref,
    back_right_ref, scaled_rows=None,
):
    wide = sizes.width
    count = sizes.queries
    bias_out = col_sum(gz)
    for n in range(seqs):
        if sizes.top:
            mem_grad = grad_mem_ref[pl.ds(n * sizes.segs, sizes.segs), :]
            bias_out = bias_out + col_sum(mem_grad)
            branch_ref[pl.ds(n * count, sizes.top), :] = jnp.concatenate(
                [mem_grad, jnp.zeros((sizes.top - sizes.segs, wide), F32)], axis=0
            ).astype(BF16)
        branch_ref[pl.ds(n * count + sizes.top, sizes.rows), :] = gz[
            n * sizes.rows : (n + 1) * sizes.rows
        ].astype(BF16)
    vec[pl.ds(5, 1), :] = bias_out
    branch = branch_ref[...]
    gout_ref[...] = tn(branch, att_ref[...]).astype(BF16).reshape(gout_ref.shape)
    go_ref[...] = nn(branch, out_ref[...].reshape(-1, wide)).astype(BF16)
    attend_back(sizes, seqs, proj_ref, probs_ref, go_ref, gproj_ref)
    vec[pl.ds(3, 1), :] = col_sum(gproj_ref[:, pl.ds(0, wide)].astype(F32))
    vec[pl.ds(4, 1), :] = col_sum(gproj_ref[:, pl.ds(2 * wide, wide)].astype(F32))
    grad_ext = nn(gproj_ref[...], qkv_ref[...].reshape(-1, wide))
    gain_sum = jnp.zeros((1, wide), F32)
    bias_sum = jnp.zeros((1, wide), F32)
    for n in range(seqs):
        base = n * sizes.ext
        own = grad_ext[base + sizes.top : base + sizes.top + sizes.rows]
        if sizes.top:
            spread = grad_ext[base : base + sizes.segs] * (1.0 / SEG_LEN)
            own = own + segment_spread(sizes.rows, wide, spread)
        gh_ref[pl.ds(n * sizes.rows, sizes.rows), :] = own
        mem = base + sizes.mem_at
        gmem_ref[pl.ds(n * sizes.segs, sizes.segs), :] = grad_ext[mem : mem + sizes.segs]
        left = base + sizes.left_at
        back_left_ref[n] = grad_ext[left : left + BACK_ROWS].astype(BF16)
        right = base + sizes.right_at
        back_right_ref[n] = grad_ext[right : right + RIGHT_ROWS].astype(BF16)
        if scaled_rows is not None:
            grads = (
                own,
                grad_ext[right : right + RIGHT_ROWS],
                grad_ext[left : left + LEFT_ROWS],
            )
            for rows, scaled in zip(grads, scaled_rows(n)):
                gain_sum = gain_sum + col_sum(rows * scaled)
                bias_sum = bias_sum + col_sum(rows)
    if scaled_rows is not None:
        vec[pl.ds(0, 1), :] = gain_sum
        vec[pl.ds(2, 1), :] = bias_sum
    step = CHIPS_Z // 2
    part = gqkv_ref.shape[1] * gqkv_ref.shape[2] * step
    for c in range(2):
        gqkv_ref[pl.ds(c * step, step)] = (
            tn(gproj_ref[:, pl.ds(c * part, part)], z_ref[...])
            .astype(BF16)
            .reshape((step,) + gqkv_ref.shape[1:])
        )


def merge_halo(sizes, n, gh_ref, gmem_ref, from_right_ref, from_left_ref):
    first = n * sizes.rows
    back = from_right_ref[n].astype(F32)
    head = gh_ref[pl.ds(first, RIGHT_ROWS), :] + from_left_ref[n].astype(F32)
    middle = gh_ref[pl.ds(first + RIGHT_ROWS, sizes.rows - RIGHT_ROWS - LEFT_ROWS), :]
    tail = gh_ref[pl.ds(first + sizes.rows - LEFT_ROWS, LEFT_ROWS), :] + back[:LEFT_ROWS]
    mem = gmem_ref[pl.ds(n * sizes.segs, sizes.segs), :] + back[LEFT_ROWS + sizes.segs :]
    return jnp.concatenate([head, middle, tail], axis=0), mem


def pack_kernel(places, qkv_ref, out_ref, up_ref, down_ref, *packed):
    eye = identity(LANES)
    high, wide, low = qkv_ref.shape[1], out_ref.shape[1], down_ref.shape[1]
    up = up_ref.shape[2]
    for layer, (attn, attn_at, ffn, ffn_at) in enumerate(places):
        ref = packed[attn]
        ref[pl.ds(attn_at, high), :] = qkv_ref[layer]
        ref[pl.ds(attn_at + high, wide), :] = out_ref[layer]
        ref = packed[ffn]
        ref[pl.ds(ffn_at, up), :] = tn(up_ref[layer], eye).astype(BF16)
        for part in range(down_ref.shape[2] // LANES):
            ref[pl.ds(ffn_at + up + part * low, low), :] = down_ref[
                layer, :, pl.ds(part * LANES, LANES)
            ]


def unpack_kernel(each, places, place_ref, *refs):
    sources, outs = refs[:-8], refs[-8:]
    qkv_ref, out_ref, up_ref, down_ref, gains_ref, biases_ref, ffn_bias_ref, small_ref = outs
    eye = identity(LANES)
    high, wide, low = qkv_ref.shape[1], out_ref.shape[1], down_ref.shape[1]
    up = up_ref.shape[2]

    def total(source, first, rows):
        value = sources[source * each][pl.ds(first, rows), :].astype(F32)
        for part in sources[source * each + 1 : (source + 1) * each]:
            value = value + part[pl.ds(first, rows), :].astype(F32)
        return value

    for layer, (attn, attn_at, ffn, ffn_at) in enumerate(places):
        qkv_ref[layer] = total(attn, attn_at, high)
        out_ref[layer] = total(attn, attn_at + high, wide)
        up_ref[layer] = nt(eye, total(ffn, ffn_at, up).astype(BF16))
        for part in range(down_ref.shape[2] // LANES):
            down_ref[layer, :, pl.ds(part * LANES, LANES)] = total(
                ffn, ffn_at + up + part * low, low
            )
    for k in range(each):
        spot = lax.rem(place_ref[0] + each - k, each)
        small_ref[spot] = sources[k][pl.ds(high + wide, SMALL_ROWS), :].astype(F32)
    sums = small_ref[0]
    for k in range(1, each):
        sums = sums + small_ref[k]
    parts = gains_ref.shape[2] // LANES
    for layer in range(gains_ref.shape[0]):
        for part in range(parts):
            lanes = pl.ds(part * LANES, LANES)
            block = sums[(layer * parts + part) * TILE : (layer * parts + part + 1) * TILE]
            gains_ref[layer, :, lanes] = block[0:2]
            biases_ref[layer, :, lanes] = block[2:8]
            for row in range(ffn_bias_ref.shape[1] // gains_ref.shape[2]):
                at = row * gains_ref.shape[2] + part * LANES
                ffn_bias_ref[pl.ds(layer, 1), pl.ds(at, LANES)] = block[8 + row : 9 + row]


def stack_kernel(count, place_ref, *refs):
    sources, out_ref, sems = refs[:count], refs[count], refs[count + 1]
    copies = []
    for k, source in enumerate(sources):
        spot = lax.rem(place_ref[0] + count - k, count)
        copies.append(pltpu.make_async_copy(source, out_ref.at[spot], sems.at[k]))
    for copy in copies:
        copy.start()
    wait_all(copies)


def split_kernel(count, place_ref, mine_ref, theirs_ref, second_ref, first_ref, *outs):
    for k, out in enumerate(outs):
        spot = lax.rem(place_ref[0] + k, count)
        total = mine_ref[0, spot].astype(F32) + theirs_ref[0, spot].astype(F32)
        total = total + second_ref[0, spot].astype(F32) + first_ref[spot].astype(F32)
        out[...] = total.astype(BF16)


def far_kernel(rows, mine_ref, theirs_ref, sent_ref, came_ref, out_ref):
    group = pl.ds(rows, rows)
    total = mine_ref[group, :].astype(F32) + theirs_ref[group, :].astype(F32)
    out_ref[pl.ds(0, rows), :] = (total + came_ref[group, :].astype(F32)).astype(BF16)
    small = pl.ds(2 * rows, SMALL_ROWS)
    out_ref[pl.ds(rows, SMALL_ROWS), :] = (
        sent_ref[small, :].astype(F32) + came_ref[small, :].astype(F32)
    ).astype(BF16)


def split_small_kernel(
    count, rows, place_ref, mine_ref, theirs_ref, second_ref, sent_ref, first_ref, *outs
):
    small = pl.ds(count * rows, SMALL_ROWS)
    sums = (sent_ref[small, :].astype(F32) + first_ref[small, :].astype(F32)).astype(BF16)
    for k, out in enumerate(outs):
        spot = lax.rem(place_ref[0] + k, count)
        group = pl.ds(pl.multiple_of(spot * rows, rows), rows)
        total = mine_ref[group, :].astype(F32) + theirs_ref[group, :].astype(F32)
        total = total + second_ref[group, :].astype(F32) + first_ref[group, :].astype(F32)
        out[pl.ds(0, rows), :] = total.astype(BF16)
        out[pl.ds(rows, SMALL_ROWS), :] = sums


def first_attn_kernel(
    sizes, seqs, mats, by_blocks, count_in, at, place_ref, starts_ref, frames_ref, left_ref,
    right_ref, gains_ref, biases_ref, row_bias_ref, *refs
):
    hbm = refs[:count_in]
    z_ref, proj_ref, probs_ref, att_ref, mixed_ref, mem_ref, qkv_ref, out_ref, mask_ref, sems = (
        refs[count_in:]
    )
    wide = sizes.width
    copies = start_in(
        attn_pairs(mats, by_blocks, hbm, at, qkv_ref, out_ref, place_ref), sems, 0
    )
    gain = gains_ref[0, pl.ds(0, 1), :]
    bias = biases_ref[0, pl.ds(0, 1), :]
    pad = jnp.zeros((TILE - sizes.segs, wide), F32)
    for n in range(seqs):
        own = frames_ref[n].astype(F32)
        before = left_ref[n].astype(F32)
        hidden = norm_forward(own, gain, bias)[0]
        halo = norm_forward(before[before.shape[0] - LEFT_ROWS :], gain, bias)[0]
        after = norm_forward(right_ref[n].astype(F32), gain, bias)[0]
        memory = jnp.concatenate(
            [
                segment_mean(own),
                jnp.zeros((sizes.segs - before.shape[0] // SEG_LEN, wide), F32),
                segment_mean(before),
            ],
            axis=0,
        )
        base = n * sizes.ext
        z_ref[pl.ds(base, sizes.top), :] = jnp.concatenate(
            [segment_mean(hidden), pad], axis=0
        ).astype(BF16)
        z_ref[pl.ds(base + sizes.top, sizes.rows), :] = hidden.astype(BF16)
        z_ref[pl.ds(base + sizes.right_at, RIGHT_ROWS), :] = after.astype(BF16)
        z_ref[pl.ds(base + sizes.left_at, LEFT_ROWS), :] = halo.astype(BF16)
        z_ref[pl.ds(base + sizes.mem_at, MEM_ROWS), :] = memory.astype(BF16)
    fill_mask(sizes, seqs, starts_ref, place_ref, mask_ref)
    wait_all(copies)
    project(sizes, z_ref, qkv_ref, row_bias_ref, proj_ref)
    attend(sizes, seqs, proj_ref, mask_ref, probs_ref, att_ref)
    mixed = nt(att_ref[...], out_ref[...].reshape(-1, wide)) + biases_ref[0, pl.ds(3, 1), :]
    for n in range(seqs):
        base = n * sizes.queries
        mem_ref[pl.ds(n * sizes.segs, sizes.segs), :] = mixed[base : base + sizes.segs]
        mixed_ref[pl.ds(n * sizes.rows, sizes.rows), :] = (
            frames_ref[n].astype(F32) + mixed[base + sizes.top : base + sizes.top + sizes.rows]
        )


def first_ffn_kernel(
    sizes, seqs, mats, by_blocks, count_in, at, place_ref, mixed_ref, mem_ref, gains_ref,
    biases_ref, ffn_bias_ref, *refs
):
    hbm = refs[:count_in]
    (
        next_ref, active_ref, slope_ref, low_ref, send_right_ref, send_left_ref, up_ref, down_ref,
        hidden_ref, sems,
    ) = refs[count_in:]
    copies = start_in(ffn_pairs(mats, by_blocks, hbm, at, up_ref, down_ref, place_ref), sems, 0)
    mixed = mixed_ref[...]
    hidden, _, _ = norm_forward(mixed, gains_ref[0, pl.ds(1, 1), :], biases_ref[0, pl.ds(4, 1), :])
    hidden_ref[...] = hidden.astype(BF16)
    next_ref[...] = mixed + biases_ref[0, pl.ds(5, 1), :]
    wait_all(copies)
    wide = sizes.width

    def body(c, carry):
        at_lane = pl.multiple_of(c * wide, wide)
        upward = nt(hidden_ref[...], up_block(up_ref, c, wide))
        upward = upward + ffn_bias_ref[pl.ds(0, 1), pl.ds(at_lane, wide)]
        active, slope = gelu_both(upward)
        active = active.astype(BF16)
        active_ref[:, pl.ds(at_lane, wide)] = active
        slope_ref[:, pl.ds(at_lane, wide)] = slope.astype(BF16)
        next_ref[...] += nt(active, down_block(down_ref, c, wide))
        return carry

    lax.fori_loop(0, sizes.ff // wide, body, 0)
    low, _, _ = norm_forward(
        next_ref[...], gains_ref[1, pl.ds(0, 1), :], biases_ref[1, pl.ds(0, 1), :]
    )
    low = low.astype(BF16)
    low_ref[...] = low
    for n in range(seqs):
        base = n * sizes.rows
        send_right_ref[n, pl.ds(0, LEFT_ROWS), :] = low[
            base + sizes.rows - LEFT_ROWS : base + sizes.rows
        ]
        send_right_ref[n, pl.ds(LEFT_ROWS, MEM_ROWS), :] = jnp.concatenate(
            [
                mem_ref[pl.ds(n * sizes.segs, sizes.segs), :],
                jnp.zeros((MEM_ROWS - sizes.segs, wide), F32),
            ],
            axis=0,
        ).astype(BF16)
        send_left_ref[n] = low[base : base + RIGHT_ROWS]


def last_layer_kernel(
    sizes, seqs, mats, by_blocks, count_in, attn_at, ffn_at, place_ref, starts_ref, low_ref,
    left_ref, right_ref, mem_ref, inputs_ref, out_grad_ref, gains_ref, biases_ref, ffn_bias_ref,
    row_bias_ref, *refs
):
    hbm = refs[:count_in]
    count_out = 2 if by_blocks else 4
    (encoded_ref, gz_ref, gh_ref, gmem_ref, back_left_ref, back_right_ref, vec) = refs[
        count_in : count_in + 7
    ]
    hbm_out = refs[count_in + 7 : count_in + 7 + count_out]
    (
        qkv_ref, out_ref, up_ref, down_ref, gqkv_ref, gout_ref, gup_ref, gdown_ref, mask_ref,
        z_ref, proj_ref, probs_ref, att_ref, hidden_ref, go_ref, gproj_ref, branch_ref,
        grad_low_ref, grad_hidden_ref, sems,
    ) = refs[count_in + 7 + count_out :]
    attn_hbm, ffn_hbm = (hbm, hbm) if by_blocks else (hbm[:2], hbm[2:])
    attn_out, ffn_out = out_views(by_blocks, hbm_out)
    wide = sizes.width
    attn_copies = start_in(
        attn_pairs(mats, by_blocks, attn_hbm, attn_at, qkv_ref, out_ref, place_ref), sems, 0
    )
    ffn_copies = start_in(
        ffn_pairs(mats, by_blocks, ffn_hbm, ffn_at, up_ref, down_ref, place_ref),
        sems,
        len(attn_copies),
    )
    vec[...] = jnp.zeros_like(vec)
    for n in range(seqs):
        base = n * sizes.ext
        z_ref[pl.ds(base, sizes.rows), :] = low_ref[pl.ds(n * sizes.rows, sizes.rows), :]
        z_ref[pl.ds(base + sizes.right_at, RIGHT_ROWS), :] = right_ref[n]
        z_ref[pl.ds(base + sizes.left_at, LEFT_ROWS), :] = left_ref[n, pl.ds(0, LEFT_ROWS), :]
        memory = jnp.concatenate(
            [
                mem_ref[pl.ds(n * sizes.segs, sizes.segs), :],
                left_ref[n, pl.ds(LEFT_ROWS, MEM_ROWS), :].astype(F32)[: sizes.segs],
            ],
            axis=0,
        )
        z_ref[pl.ds(base + sizes.mem_at, MEM_ROWS), :] = memory.astype(BF16)
        grad_low_ref[pl.ds(n * sizes.rows, sizes.rows), :] = out_grad_ref[n]
    fill_mask(sizes, seqs, starts_ref, place_ref, mask_ref)
    wait_all(attn_copies)
    project(sizes, z_ref, qkv_ref, row_bias_ref, proj_ref)
    attend(sizes, seqs, proj_ref, mask_ref, probs_ref, att_ref)
    mixed = (
        inputs_ref[...]
        + nt(att_ref[...], out_ref[...].reshape(-1, wide))
        + biases_ref[1, pl.ds(3, 1), :]
    )
    gain = gains_ref[1, pl.ds(1, 1), :]
    hidden, scaled, inverse = norm_forward(mixed, gain, biases_ref[1, pl.ds(4, 1), :])
    hidden_ref[...] = hidden.astype(BF16)
    for n in range(seqs):
        encoded_ref[n] = mixed[n * sizes.rows : (n + 1) * sizes.rows] + biases_ref[
            1, pl.ds(5, 1), :
        ]
    grad_hidden_ref[...] = jnp.zeros_like(grad_hidden_ref)
    wait_all(ffn_copies)

    def body(c, carry):
        at_lane = pl.multiple_of(c * wide, wide)
        upward = nt(hidden_ref[...], up_block(up_ref, c, wide))
        upward = upward + ffn_bias_ref[pl.ds(1, 1), pl.ds(at_lane, wide)]
        active, slope = gelu_both(upward)
        active = active.astype(BF16)
        made = nt(active, down_block(down_ref, c, wide))
        for n in range(seqs):
            encoded_ref[n] += made[n * sizes.rows : (n + 1) * sizes.rows]
        grad_hidden_ref[...] += ffn_back_step(
            sizes, c, wide, grad_low_ref[...], hidden_ref[...], active, slope, up_ref, down_ref,
            gup_ref, gdown_ref, vec,
        )
        return carry

    lax.fori_loop(0, sizes.ff // wide, body, 0)
    out_at = len(attn_copies) + len(ffn_copies)
    outs = start_out(
        ffn_pairs(mats, by_blocks, ffn_out, ffn_at, gup_ref, gdown_ref, place_ref), sems, out_at
    )
    grad = grad_low_ref[...].astype(F32)
    grad_hidden = grad_hidden_ref[...]
    vec[pl.ds(1, 1), :] = col_sum(grad_hidden * scaled)
    vec[pl.ds(6, 1), :] = col_sum(grad_hidden)
    vec[pl.ds(7, 1), :] = col_sum(grad)
    gz = grad + norm_backward(grad_hidden, scaled, inverse, gain)
    gz_ref[...] = gz
    attn_back_stage(
        sizes, seqs, gz, None, att_ref, proj_ref, probs_ref, z_ref, qkv_ref, out_ref, gqkv_ref,
        gout_ref, go_ref, gproj_ref, branch_ref, vec, gh_ref, gmem_ref, back_left_ref,
        back_right_ref,
    )
    outs = outs + start_out(
        attn_pairs(mats, by_blocks, attn_out, attn_at, gqkv_ref, gout_ref, place_ref),
        sems,
        out_at + len(outs),
    )
    wait_all(outs)


def first_ffn_back_kernel(
    last, sizes, seqs, mats, by_blocks, count_in, count_out, at_in, place_ref, inputs_ref,
    gz_in_ref, gh_in_ref, gmem_in_ref, from_right_ref, from_left_ref, mixed_ref, active_ref,
    slope_ref, gains_ref, biases_ref, *refs
):
    hbm = refs[:count_in]
    gz_ref, grad_mem_ref, upper_vec, vec = refs[count_in : count_in + 4]
    refs = refs[count_in + 4 :]
    hbm_out = refs[:count_out]
    if by_blocks:
        hbm_out = out_views(by_blocks, hbm_out)[0]
    (
        up_ref, down_ref, gup_ref, gdown_ref, hidden_ref, grad_low_ref, grad_ref, grad_hidden_ref,
        sems,
    ) = refs[count_out:]
    wide = sizes.width
    copies = start_in(
        ffn_pairs(mats, by_blocks, hbm, at_in, up_ref, down_ref, place_ref), sems, 0
    )
    vec[...] = jnp.zeros_like(vec)
    upper_vec[...] = jnp.zeros_like(upper_vec)
    gain = gains_ref[1, pl.ds(0, 1), :]
    gain_sum = jnp.zeros((1, wide), F32)
    bias_sum = jnp.zeros((1, wide), F32)
    for n in range(seqs):
        rows = pl.ds(n * sizes.rows, sizes.rows)
        _, scaled, inverse = norm_forward(
            inputs_ref[rows, :], gain, biases_ref[1, pl.ds(0, 1), :]
        )
        total, mem = merge_halo(last, n, gh_in_ref, gmem_in_ref, from_right_ref, from_left_ref)
        gain_sum = gain_sum + col_sum(total * scaled)
        bias_sum = bias_sum + col_sum(total)
        grad = gz_in_ref[rows, :] + norm_backward(total, scaled, inverse, gain)
        grad_ref[rows, :] = grad
        grad_low_ref[rows, :] = grad.astype(BF16)
        grad_mem_ref[pl.ds(n * sizes.segs, sizes.segs), :] = mem
    upper_vec[pl.ds(0, 1), :] = gain_sum
    upper_vec[pl.ds(2, 1), :] = bias_sum
    gain = gains_ref[0, pl.ds(1, 1), :]
    hidden, scaled, inverse = norm_forward(
        mixed_ref[...], gain, biases_ref[0, pl.ds(4, 1), :]
    )
    hidden_ref[...] = hidden.astype(BF16)
    grad_hidden_ref[...] = jnp.zeros_like(grad_hidden_ref)
    wait_all(copies)

    def body(c, carry):
        at_lane = pl.multiple_of(c * wide, wide)
        grad_hidden_ref[...] += ffn_back_step(
            sizes, c, wide, grad_low_ref[...], hidden_ref[...],
            active_ref[:, pl.ds(at_lane, wide)], slope_ref[:, pl.ds(at_lane, wide)].astype(F32),
            up_ref, down_ref, gup_ref, gdown_ref, vec,
        )
        return carry

    lax.fori_loop(0, sizes.ff // wide, body, 0)
    outs = start_out(
        ffn_pairs(mats, by_blocks, hbm_out, 0, gup_ref, gdown_ref, place_ref), sems, len(copies)
    )
    grad_hidden = grad_hidden_ref[...]
    grad = grad_ref[...]
    vec[pl.ds(1, 1), :] = col_sum(grad_hidden * scaled)
    vec[pl.ds(6, 1), :] = col_sum(grad_hidden)
    vec[pl.ds(7, 1), :] = col_sum(grad)
    gz_ref[...] = grad + norm_backward(grad_hidden, scaled, inverse, gain)
    wait_all(outs)


def first_attn_back_kernel(
    sizes, seqs, mats, by_blocks, count_in, count_out, at_in, place_ref, gz_ref, grad_mem_ref,
    att_ref, probs_ref, proj_ref, z_ref, frames_ref, left_ref, right_ref, gains_ref, biases_ref,
    ffn_vec, last_vec, upper_vec, *refs
):
    hbm = refs[:count_in]
    gh_ref, gmem_ref, back_left_ref, back_right_ref, vec = refs[count_in : count_in + 5]
    refs = refs[count_in + 5 :]
    hbm_out = refs[:count_out]
    small = []
    if by_blocks:
        rows = mats.attn_rows
        blocks = count_in // 2 * CHIPS_Z * rows
        small = [ref.at[pl.ds(blocks, SMALL_ROWS), :] for ref in hbm_out]
        hbm_out = [
            ref.at[pl.ds(0, blocks), :].reshape(count_in // 2, CHIPS_Z, rows, LANES).at[k]
            for ref in hbm_out
            for k in range(count_in // 2)
        ]
    (
        qkv_ref, out_ref, gqkv_ref, gout_ref, go_ref, gproj_ref, branch_ref, small_ref, sems,
    ) = refs[count_out:]
    copies = start_in(
        attn_pairs(mats, by_blocks, hbm, at_in, qkv_ref, out_ref, place_ref), sems, 0
    )
    vec[...] = jnp.zeros_like(vec)
    gain = gains_ref[0, pl.ds(0, 1), :]
    bias = biases_ref[0, pl.ds(0, 1), :]

    def scaled_rows(n):
        before = left_ref[n, pl.ds(left_ref.shape[1] - LEFT_ROWS, LEFT_ROWS), :]
        parts = (frames_ref[n], right_ref[n], before)
        return [norm_forward(part.astype(F32), gain, bias)[1] for part in parts]

    wait_all(copies)
    attn_back_stage(
        sizes, seqs, gz_ref[...], grad_mem_ref, att_ref, proj_ref, probs_ref, z_ref, qkv_ref,
        out_ref, gqkv_ref, gout_ref, go_ref, gproj_ref, branch_ref, vec, gh_ref, gmem_ref,
        back_left_ref, back_right_ref, scaled_rows,
    )
    outs = start_out(
        attn_pairs(mats, by_blocks, hbm_out, 0, gqkv_ref, gout_ref, place_ref), sems, len(copies)
    )
    parts = sizes.width // LANES
    for layer, total in enumerate((vec[...] + ffn_vec[...], last_vec[...] + upper_vec[...])):
        for part in range(parts):
            small_ref[pl.ds((layer * parts + part) * TILE, TILE), :] = total[
                :, part * LANES : (part + 1) * LANES
            ].astype(BF16)
    outs = outs + start_out([(ref, small_ref) for ref in small], sems, len(copies) + len(outs))
    wait_all(outs)


def frames_grad_kernel(
    sizes, seqs, frames_ref, gz_ref, gh_ref, gmem_ref, from_right_ref, from_left_ref, gains_ref,
    biases_ref, grad_ref
):
    gain = gains_ref[0, pl.ds(0, 1), :]
    for n in range(seqs):
        _, scaled, inverse = norm_forward(
            frames_ref[n].astype(F32), gain, biases_ref[0, pl.ds(0, 1), :]
        )
        total, mem = merge_halo(sizes, n, gh_ref, gmem_ref, from_right_ref, from_left_ref)
        grad_ref[n] = (
            gz_ref[pl.ds(n * sizes.rows, sizes.rows), :]
            + norm_backward(total, scaled, inverse, gain)
            + segment_spread(sizes.rows, sizes.width, mem * (1.0 / SEG_LEN))
        )


def shifted(value, axis, by):
    size = lax.axis_size(axis)
    pairs = [(i, i + by) for i in range(size) if 0 <= i + by < size]
    return lax.ppermute(value, axis, pairs)


def permuted(value, move):
    reps = lax.axis_size("rep")
    pairs = []
    for flat in range(lax.axis_size("seg") * reps):
        seg, rep = divmod(flat, reps)
        z, y, x, core = move(seg // CHIPS_Y, seg % CHIPS_Y, rep // 2, rep % 2)
        pairs.append((flat, (z * CHIPS_Y + y) * reps + 2 * x + core))
    return lax.ppermute(value, ("seg", "rep"), pairs)


def along_z(value, by):
    return permuted(value, lambda z, y, x, core: ((z + by) % CHIPS_Z, y, x, core))


def across_first(value):
    return permuted(value, lambda z, y, x, c: (z, y, x ^ 1, c) if c == 0 else (z, y ^ 1, x, c))


def across_second(value):
    return permuted(value, lambda z, y, x, c: (z, y ^ 1, x, c) if c == 0 else (z, y, x ^ 1, c))


def other_core(value):
    return permuted(value, lambda z, y, x, c: (z, y, x, c ^ 1))


def after(value, *others):
    return lax.optimization_barrier((value,) + others)[0]


def gather_z(shard, z_place, others):
    parts = [after(shard, *others)] + [along_z(shard, by) for by in range(1, CHIPS_Z)]
    return call(
        lambda *refs: stack_kernel(CHIPS_Z, *refs),
        [smem_spec()] + [vmem_spec()] * CHIPS_Z,
        [((CHIPS_Z,) + shard.shape, BF16)],
        [hbm_spec()],
        [pltpu.SemaphoreType.DMA((CHIPS_Z,))],
        [z_place] + parts,
    )[0]


def gather_sides(here):
    return [here, across_first(here), across_second(here)]


def both_cores(blocks):
    return blocks + [other_core(block) for block in blocks]


def summed(*parts):
    total = parts[0].astype(F32)
    for part in parts[1:]:
        total = total + part.astype(F32)
    return total.astype(BF16)


def one_block(shape):
    return pl.BlockSpec((1,) + tuple(shape[1:]), lambda i: (0,) * len(shape))


def split_z(mine, theirs, second, first, z_place):
    return call(
        lambda *refs: split_kernel(CHIPS_Z, *refs),
        [smem_spec()]
        + [one_block(member.shape) for member in (mine, theirs, second)]
        + [vmem_spec()],
        [(first.shape[1:], BF16)] * CHIPS_Z,
        [vmem_spec()] * CHIPS_Z,
        [],
        [z_place, mine, theirs, second, first],
        grid=(1,),
    )


def scatter_z(parts):
    return [parts[0]] + [along_z(parts[by], by) for by in range(1, CHIPS_Z)]


def sum_everywhere(value):
    count = lax.axis_size("seg") * lax.axis_size("rep")
    bit = 1
    while bit < count:
        value = value + lax.ppermute(value, ("seg", "rep"), [(i, i ^ bit) for i in range(count)])
        bit *= 2
    return value


def vmem_spec():
    return pl.BlockSpec(memory_space=pltpu.VMEM)


def smem_spec():
    return pl.BlockSpec(memory_space=pltpu.SMEM)


def hbm_spec():
    return pl.BlockSpec(memory_space=pl.ANY)


def call(body, in_specs, out_shapes, out_specs, scratch, args, flops=0, moved=0, grid=()):
    return pl.pallas_call(
        body,
        grid=grid,
        in_specs=in_specs,
        out_shape=tuple(jax.ShapeDtypeStruct(shape, kind) for shape, kind in out_shapes),
        out_specs=tuple(out_specs),
        scratch_shapes=scratch,
        compiler_params=pltpu.CompilerParams(vmem_limit_bytes=VMEM_BYTES),
        cost_estimate=pl.CostEstimate(flops=flops, bytes_accessed=moved, transcendentals=0),
    )(*args)


def on_device(
    frames,
    utt_segments,
    out_grad,
    qkv_weight,
    out_weight,
    ffn_in_weight,
    ffn_out_weight,
    norm_gains,
    biases,
    ffn_bias,
):
    micros, groups, rows, width = frames.shape
    seqs = micros * groups
    ff = ffn_bias.shape[1]
    reps = lax.axis_size("rep")
    seg_count = lax.axis_size("seg")
    mats = Matrices(width, ff)
    by_blocks = width // reps == LANES and reps == 4 and seg_count == BLOCKS
    first = Sizes(rows, width, ff, True)
    last = Sizes(rows, width, ff, False)
    own = seqs * rows
    mem_own = seqs * first.segs

    seg_at = lax.axis_index("seg")
    seg_base = seg_at * first.segs
    rep_at = lax.axis_index("rep")
    place = [seg_base, jnp.int32(first.segs * seg_count)]
    y_at, x_at, core_at = seg_at % CHIPS_Y, rep_at // 2, rep_at % 2
    z_place = jnp.reshape(seg_at // CHIPS_Y, (1,)).astype(jnp.int32)
    for other in range(2):
        core = lax.bitwise_xor(core_at, other)
        for hop2 in range(2):
            for hop1 in range(2):
                x_hop = jnp.where(core == 0, hop1, hop2)
                y_hop = jnp.where(core == 0, hop2, hop1)
                place.append(lax.bitwise_xor(y_at, y_hop))
                place.append((lax.bitwise_xor(x_at, x_hop) * 2 + core) * LANES)
    place = jnp.stack([jnp.asarray(entry, jnp.int32) for entry in place])
    lengths = utt_segments.reshape(seqs, utt_segments.shape[2])
    starts = (jnp.cumsum(lengths, axis=1) - lengths).astype(jnp.int32)
    zero_bias = jnp.zeros((width,), F32)
    row_bias = jnp.stack(
        [jnp.concatenate([biases[l, 1], zero_bias, biases[l, 2]]) for l in range(LAYERS)]
    ).reshape(LAYERS, 1, 3 * width)

    frames_own = frames.reshape(seqs, rows, width)
    grads_own = out_grad.reshape(seqs, rows, width)
    far = MEM_LEN * SEG_LEN
    frames_left = shifted(frames_own[:, rows - far :], "seg", 1)
    frames_right = shifted(frames_own[:, :RIGHT_ROWS], "seg", -1)

    attn_rows, ffn_rows = mats.attn_rows, mats.ffn_rows
    if by_blocks:
        qkv_t, out_t, down_t = (
            jnp.swapaxes(member, 1, 2) for member in (qkv_weight, out_weight, ffn_out_weight)
        )
        places = [(0, 0, 1, 0), (2, 0, 2, attn_rows)]
        chunk_rows = [attn_rows, ffn_rows, attn_rows + ffn_rows]
        shards = call(
            lambda *refs: pack_kernel(places, *refs),
            [vmem_spec()] * 4,
            [((high, LANES), BF16) for high in chunk_rows],
            [vmem_spec()] * len(chunk_rows),
            [],
            (qkv_t, out_t, ffn_in_weight, down_t),
        )
        halos = (frames_left, frames_right)
        sides0 = gather_sides(gather_z(shards[0], z_place, halos))
        shard = after(shards[1], sides0[0])
        sides1 = gather_sides(gather_z(shard, z_place, tuple(sides0[1:])))
        first_attn = both_cores(sides0 + [across_second(sides0[1])])
        first_ffn = both_cores(sides1 + [across_second(sides1[1])])
        first_at = 0, 0
        last_at = 0, attn_rows
        half = len(first_attn) // 2
        grad_outs = [
            [((half, CHIPS_Z, high, LANES), BF16)] * 2 for high in chunk_rows
        ]
        flat_rows = half * CHIPS_Z * attn_rows
        grad_outs[0] = [((flat_rows + SMALL_ROWS, LANES), BF16)] * 2
        copies_in = len(first_attn) * (3 + mats.down_parts)
    else:
        whole = []
        for member, shape in zip(
            (qkv_weight, out_weight, ffn_in_weight, ffn_out_weight),
            (mats.qkv, mats.out, mats.up, mats.down),
        ):
            member = lax.all_gather(member, "rep", axis=1, tiled=True)
            member = lax.all_gather(member, "seg", axis=2, tiled=True)
            whole.append(jnp.swapaxes(member, 1, 2).reshape((LAYERS,) + shape))
        first_attn = [whole[0][0], whole[1][0]]
        first_ffn = [whole[2][0], whole[3][0]]
        last_all = [member[1] for member in whole]
        first_at = last_at = 0, 0
        shapes = [(shape, BF16) for shape in (mats.qkv, mats.out, mats.up, mats.down)]
        grad_outs = [shapes[:2], shapes[2:], shapes]
        copies_in = 4
    dma = pltpu.SemaphoreType.DMA

    z0, proj0, probs0, att0, mixed0, mem1 = call(
        lambda *refs: first_attn_kernel(
            first, seqs, mats, by_blocks, len(first_attn), first_at[0], *refs
        ),
        [smem_spec()] * 2 + [vmem_spec()] * 6 + [hbm_spec()] * len(first_attn),
        [
            ((seqs * first.ext, width), BF16),
            ((seqs * first.ext, 3 * width), BF16),
            ((seqs * first.pairs, 2 * first.queries, first.keys), F32),
            ((seqs * first.queries, width), BF16),
            ((own, width), F32),
            ((mem_own, width), F32),
        ],
        [vmem_spec()] * 6,
        [
            pltpu.VMEM(mats.qkv, BF16),
            pltpu.VMEM(mats.out, BF16),
            pltpu.VMEM((seqs, first.queries, first.keys), F32),
            dma((copies_in,)),
        ],
        (place, starts, frames_own, frames_left, frames_right, norm_gains, biases, row_bias[0])
        + tuple(first_attn),
        flops=40 * own * 4 * width * width,
        moved=8 * width * width,
    )
    if by_blocks:
        shard = after(shards[2], sides1[0])
        sides2 = gather_sides(gather_z(shard, z_place, (mixed0,) + tuple(sides1[1:])))
    x1, active0, slope0, low1, send_right, send_left = call(
        lambda *refs: first_ffn_kernel(first, seqs, mats, by_blocks, len(first_ffn), first_at[1], *refs),
        [smem_spec()] + [vmem_spec()] * 5 + [hbm_spec()] * len(first_ffn),
        [
            ((own, width), F32),
            ((own, ff), BF16),
            ((own, ff), BF16),
            ((own, width), BF16),
            ((seqs, BACK_ROWS, width), BF16),
            ((seqs, RIGHT_ROWS, width), BF16),
        ],
        [vmem_spec()] * 6,
        [
            pltpu.VMEM(mats.up, BF16),
            pltpu.VMEM(mats.down, BF16),
            pltpu.VMEM((own, width), BF16),
            dma((copies_in,)),
        ],
        (place, mixed0, mem1, norm_gains, biases, ffn_bias) + tuple(first_ffn),
        flops=16 * own * 2 * width * ff,
        moved=4 * width * ff,
    )
    if by_blocks:
        last_all = both_cores(sides2 + [across_second(after(sides2[1], low1))])
    left1 = shifted(send_right, "seg", 1)
    right1 = shifted(send_left, "seg", -1)

    vec_shape = (TILE, width)
    outs = call(
        lambda *refs: last_layer_kernel(
            last, seqs, mats, by_blocks, len(last_all), *last_at, *refs
        ),
        [smem_spec()] * 2 + [vmem_spec()] * 10 + [hbm_spec()] * len(last_all),
        [
            ((seqs, rows, width), F32),
            ((own, width), F32),
            ((own, width), F32),
            ((mem_own, width), F32),
            ((seqs, BACK_ROWS, width), BF16),
            ((seqs, RIGHT_ROWS, width), BF16),
            (vec_shape, F32),
        ]
        + grad_outs[2],
        [vmem_spec()] * 7 + [hbm_spec()] * len(grad_outs[2]),
        [
            pltpu.VMEM(mats.qkv, BF16),
            pltpu.VMEM(mats.out, BF16),
            pltpu.VMEM(mats.up, BF16),
            pltpu.VMEM(mats.down, BF16),
            pltpu.VMEM(mats.qkv, BF16),
            pltpu.VMEM(mats.out, BF16),
            pltpu.VMEM(mats.up, BF16),
            pltpu.VMEM(mats.down, BF16),
            pltpu.VMEM((seqs, last.queries, last.keys), F32),
            pltpu.VMEM((seqs * last.ext, width), BF16),
            pltpu.VMEM((seqs * last.ext, 3 * width), BF16),
            pltpu.VMEM((seqs * last.pairs, 2 * last.queries, last.keys), F32),
            pltpu.VMEM((seqs * last.queries, width), BF16),
            pltpu.VMEM((own, width), BF16),
            pltpu.VMEM((seqs * last.queries, width), BF16),
            pltpu.VMEM((seqs * last.ext, 3 * width), BF16),
            pltpu.VMEM((seqs * last.queries, width), BF16),
            pltpu.VMEM((own, width), BF16),
            pltpu.VMEM((own, width), F32),
            dma((2 * copies_in,)),
        ],
        (place, starts, low1, left1, right1, mem1, x1, grads_own, norm_gains, biases, ffn_bias,
         row_bias[1]) + tuple(last_all),
        flops=30 * own * (4 * width * width + 2 * width * ff),
        moved=4 * (4 * width * width + 2 * width * ff),
    )
    encoded, gz1, gh1, gmem1, back_left1, back_right1, vec1 = outs[:7]
    grad_blocks1 = outs[7:]
    from_right1 = shifted(back_left1, "seg", -1)
    from_left1 = shifted(back_right1, "seg", 1)

    gh1_tied = gh1
    if by_blocks:
        mine1, theirs1 = grad_blocks1[0], other_core(grad_blocks1[1])
        far1 = after(summed(mine1[2:], theirs1[2:]), from_right1, from_left1)
        gh1_tied = after(gh1, far1)
    gz0, grad_mem, upper_vec, vec0_ffn, *grad_ffn0 = call(
        lambda *refs: first_ffn_back_kernel(
            last, first, seqs, mats, by_blocks, len(first_ffn), len(grad_outs[1]), first_at[1],
            *refs
        ),
        [smem_spec()] + [vmem_spec()] * 11 + [hbm_spec()] * len(first_ffn),
        [
            ((own, width), F32),
            ((mem_own, width), F32),
            (vec_shape, F32),
            (vec_shape, F32),
        ]
        + grad_outs[1],
        [vmem_spec()] * 4 + [hbm_spec()] * len(grad_outs[1]),
        [
            pltpu.VMEM(mats.up, BF16),
            pltpu.VMEM(mats.down, BF16),
            pltpu.VMEM(mats.up, BF16),
            pltpu.VMEM(mats.down, BF16),
            pltpu.VMEM((own, width), BF16),
            pltpu.VMEM((own, width), BF16),
            pltpu.VMEM((own, width), F32),
            pltpu.VMEM((own, width), F32),
            dma((2 * copies_in,)),
        ],
        (place, x1, gz1, gh1_tied, gmem1, from_right1, from_left1, mixed0, active0, slope0, norm_gains,
         biases) + tuple(first_ffn),
        flops=28 * own * 2 * width * ff,
        moved=8 * width * ff,
    )
    gz0_tied = gz0
    if by_blocks:
        second1 = across_second(far1)
        near1 = summed(mine1[1], theirs1[1], second1[1])
        mine_ffn, theirs_ffn = grad_ffn0[0], other_core(after(grad_ffn0[1], second1))
        far_ffn = summed(mine_ffn[2:], theirs_ffn[2:])
        gz0_tied = after(gz0, near1, far_ffn)
    gh0, gmem0, back_left0, back_right0, vec0_attn, *grad_attn0 = call(
        lambda *refs: first_attn_back_kernel(
            first, seqs, mats, by_blocks, len(first_attn), len(grad_outs[0]), first_at[0], *refs
        ),
        [smem_spec()] + [vmem_spec()] * 14 + [hbm_spec()] * len(first_attn),
        [
            ((own, width), F32),
            ((mem_own, width), F32),
            ((seqs, BACK_ROWS, width), BF16),
            ((seqs, RIGHT_ROWS, width), BF16),
            (vec_shape, F32),
        ]
        + grad_outs[0],
        [vmem_spec()] * 5 + [hbm_spec()] * len(grad_outs[0]),
        [
            pltpu.VMEM(mats.qkv, BF16),
            pltpu.VMEM(mats.out, BF16),
            pltpu.VMEM(mats.qkv, BF16),
            pltpu.VMEM(mats.out, BF16),
            pltpu.VMEM((seqs * first.queries, width), BF16),
            pltpu.VMEM((seqs * first.ext, 3 * width), BF16),
            pltpu.VMEM((seqs * first.queries, width), BF16),
            pltpu.VMEM((SMALL_ROWS, LANES), BF16),
            dma((2 * copies_in,)),
        ],
        (place, gz0_tied, grad_mem, att0, probs0, proj0, z0, frames_own, frames_left, frames_right,
         norm_gains, biases, vec0_ffn, vec1, upper_vec) + tuple(first_attn),
        flops=56 * own * 4 * width * width,
        moved=16 * width * width,
    )
    from_right0 = shifted(back_left0, "seg", -1)
    from_left0 = shifted(back_right0, "seg", 1)
    frames_grad = call(
        lambda *refs: frames_grad_kernel(first, seqs, *refs),
        [vmem_spec()] * 8,
        [((seqs, rows, width), F32)],
        [vmem_spec()],
        [],
        (frames_own, gz0, gh0, gmem0, from_right0, from_left0, norm_gains, biases),
    )[0]

    if by_blocks:
        first1 = across_first(near1)
        last_parts = split_z(mine1, theirs1, second1, after(first1, gh0), z_place)
        second_ffn = across_second(far_ffn)
        mine_attn = grad_attn0[0]
        theirs_attn = other_core(after(grad_attn0[1], *last_parts, second_ffn))
        near_ffn = summed(mine_ffn[1], theirs_ffn[1], second_ffn[1])
        last_parts = scatter_z(last_parts)
        ffn_parts = scatter_z(
            split_z(mine_ffn, theirs_ffn, second_ffn, across_first(near_ffn), z_place)
        )
        rows2, rows1 = flat_rows // 2, flat_rows // 4
        far_attn = after(summed(mine_attn[rows2:], theirs_attn[rows2:]), second_ffn)
        second_attn = across_second(far_attn)
        near_attn = call(
            lambda *refs: far_kernel(rows1, *refs),
            [vmem_spec()] * 4,
            [((rows1 + SMALL_ROWS, LANES), BF16)],
            [vmem_spec()],
            [],
            [mine_attn, theirs_attn, far_attn, second_attn],
        )[0]
        first_attn_sum = across_first(after(near_attn, *last_parts))
        attn_parts = scatter_z(
            call(
                lambda *refs: split_small_kernel(CHIPS_Z, attn_rows, *refs),
                [smem_spec()] + [vmem_spec()] * 5,
                [((attn_rows + SMALL_ROWS, LANES), BF16)] * CHIPS_Z,
                [vmem_spec()] * CHIPS_Z,
                [],
                [z_place, mine_attn, theirs_attn, second_attn, near_attn,
                 after(first_attn_sum, frames_grad)],
            )
        )
        shapes = [member.shape for member in (qkv_t, out_t, ffn_in_weight, down_t)]
        shapes += [member.shape for member in (norm_gains, biases, ffn_bias)]
        reduced = call(
            lambda *refs: unpack_kernel(CHIPS_Z, places, *refs),
            [smem_spec()] + [vmem_spec()] * (3 * CHIPS_Z),
            [(shape, F32) for shape in shapes],
            [vmem_spec()] * len(shapes),
            [pltpu.VMEM((CHIPS_Z, SMALL_ROWS, LANES), F32)],
            [z_place] + attn_parts + ffn_parts + last_parts,
        )
        small = reduced[4:]
        reduced = [
            jnp.swapaxes(reduced[0], 1, 2),
            jnp.swapaxes(reduced[1], 1, 2),
            reduced[2],
            jnp.swapaxes(reduced[3], 1, 2),
        ]
    else:
        reduced = []
        for member0, member1 in zip(grad_attn0 + grad_ffn0, grad_blocks1):
            both = jnp.stack([member0, member1]).reshape(LAYERS, -1, member0.shape[3])
            both = jnp.swapaxes(both, 1, 2)
            both = lax.psum_scatter(both, "seg", scatter_dimension=2, tiled=True)
            both = lax.psum_scatter(both, "rep", scatter_dimension=1, tiled=True)
            reduced.append(both.astype(F32))
        small = sum_everywhere(jnp.stack([vec0_ffn + vec0_attn, vec1 + upper_vec]))
        small = small[:, 0:2], small[:, 2:8], small[:, 8:12].reshape(ffn_bias.shape)

    return (
        encoded.reshape(frames.shape),
        frames_grad.reshape(frames.shape),
        reduced[0],
        reduced[1],
        reduced[2],
        reduced[3],
        small[0],
        small[1],
        small[2],
    )


def solution(mesh):
    in_specs = (
        P(None, "rep", "seg", None),
        P(None, "rep", None),
        P(None, "rep", "seg", None),
        P(None, "rep", "seg"),
        P(None, "rep", "seg"),
        P(None, "rep", "seg"),
        P(None, "rep", "seg"),
        P(),
        P(),
        P(),
    )
    out_specs = (
        P(None, "rep", "seg", None),
        P(None, "rep", "seg", None),
        P(None, "rep", "seg"),
        P(None, "rep", "seg"),
        P(None, "rep", "seg"),
        P(None, "rep", "seg"),
        P(),
        P(),
        P(),
    )
    return jax.shard_map(
        on_device, mesh=mesh, in_specs=in_specs, out_specs=out_specs, check_vma=False
    )
```

```python
import jax
import jax.numpy as jnp
from jax import lax
from jax.experimental import pallas as pl
from jax.experimental.pallas import tpu as pltpu
from jax.sharding import PartitionSpec as P

HEADS = 8
SEG_LEN = 16
LEFT_LEN = 30
RIGHT_LEN = 4
MEM_LEN = 4
LAYERS = 2

EPS = 1e-05
ROOT_HALF = 0.7071067811865476
INV_ROOT_TWO_PI = 0.3989422804014327

LANES = 128
TILE = 16
RIGHT_ROWS = 16
LEFT_ROWS = 32
MEM_ROWS = 16
BACK_ROWS = LEFT_ROWS + MEM_ROWS
CHIPS_Z = 4
CHIPS_Y = 2
BLOCKS = CHIPS_Z * CHIPS_Y
SMALL_ROWS = 128
VMEM_BYTES = 56 * 1024 * 1024

BF16 = jnp.bfloat16
F32 = jnp.float32


def nn(a, b):
    return lax.dot_general(a, b, (((1,), (0,)), ((), ())), preferred_element_type=F32)


def nt(a, b):
    return lax.dot_general(a, b, (((1,), (1,)), ((), ())), preferred_element_type=F32)


def tn(a, b):
    return lax.dot_general(a, b, (((0,), (0,)), ((), ())), preferred_element_type=F32)


def col_sum(value):
    return jnp.sum(value, axis=0, keepdims=True)


def norm_forward(inputs, gain, bias):
    center = inputs - jnp.mean(inputs, axis=1, keepdims=True)
    inverse = lax.rsqrt(jnp.mean(center * center, axis=1, keepdims=True) + EPS)
    scaled = center * inverse
    return scaled * gain + bias, scaled, inverse


def norm_backward(grad_in, scaled, inverse, gain):
    grad_scaled = grad_in * gain
    return inverse * (
        grad_scaled
        - jnp.mean(grad_scaled, axis=1, keepdims=True)
        - scaled * jnp.mean(grad_scaled * scaled, axis=1, keepdims=True)
    )


def segment_mean(inputs):
    rows, width = inputs.shape
    return jnp.mean(inputs.reshape(rows // SEG_LEN, SEG_LEN, width), axis=1)


def segment_spread(rows, width, per_segment):
    segs = rows // SEG_LEN
    return jnp.broadcast_to(per_segment[:, None, :], (segs, SEG_LEN, width)).reshape(rows, width)


def identity(size):
    row = lax.broadcasted_iota(jnp.int32, (size, size), 0)
    col = lax.broadcasted_iota(jnp.int32, (size, size), 1)
    return (row == col).astype(F32).astype(BF16)


class Sizes:
    def __init__(self, rows, width, ff, with_summary):
        self.rows = rows
        self.width = width
        self.ff = ff
        self.segs = rows // SEG_LEN
        self.top = TILE if with_summary else 0
        self.keys = rows + RIGHT_ROWS + LEFT_ROWS + MEM_ROWS
        self.ext = self.top + self.keys
        self.queries = self.top + rows
        self.right_at = self.top + rows
        self.left_at = self.right_at + RIGHT_ROWS
        self.mem_at = self.left_at + LEFT_ROWS
        self.pairs = width // LANES


class Matrices:
    def __init__(self, width, ff):
        self.qkv = (CHIPS_Z, CHIPS_Y, 3 * width // BLOCKS, width)
        self.out = (CHIPS_Z, CHIPS_Y, width // BLOCKS, width)
        self.up = (CHIPS_Z, CHIPS_Y, ff // BLOCKS, width)
        self.down = (CHIPS_Z, CHIPS_Y, width // BLOCKS, ff)
        self.down_parts = ff // width
        self.attn_rows = self.qkv[2] + self.out[2]
        self.ffn_rows = self.up[2] + self.down_parts * self.down[2]


def attn_pairs(mats, by_blocks, hbm, first, qkv_ref, out_ref, place_ref):
    if not by_blocks:
        return [(hbm[0], qkv_ref), (hbm[1], out_ref)]
    pairs = []
    high = mats.qkv[2]
    for k, block in enumerate(hbm):
        row = place_ref[2 + 2 * k]
        lane = pl.multiple_of(place_ref[3 + 2 * k], LANES)
        pairs.append(
            (block.at[:, pl.ds(first, high), :], qkv_ref.at[:, row, :, pl.ds(lane, LANES)])
        )
        pairs.append(
            (
                block.at[:, pl.ds(first + high, mats.out[2]), :],
                out_ref.at[:, row, :, pl.ds(lane, LANES)],
            )
        )
    return pairs


def ffn_pairs(mats, by_blocks, hbm, first, up_ref, down_ref, place_ref):
    if not by_blocks:
        return [(hbm[0], up_ref), (hbm[1], down_ref)]
    pairs = []
    high = mats.up[2]
    low = mats.down[2]
    for k, block in enumerate(hbm):
        row = place_ref[2 + 2 * k]
        lane = pl.multiple_of(place_ref[3 + 2 * k], LANES)
        pairs.append(
            (block.at[:, pl.ds(first, high), :], up_ref.at[:, row, :, pl.ds(lane, LANES)])
        )
        for part in range(mats.down_parts):
            there = pl.multiple_of(
                place_ref[3 + 2 * k] * mats.down_parts + part * LANES, LANES
            )
            pairs.append(
                (
                    block.at[:, pl.ds(first + high + part * low, low), :],
                    down_ref.at[:, row, :, pl.ds(there, LANES)],
                )
            )
    return pairs


def start_in(pairs, sems, at):
    copies = [pltpu.make_async_copy(s, d, sems.at[at + i]) for i, (s, d) in enumerate(pairs)]
    for copy in copies:
        copy.start()
    return copies


def start_out(pairs, sems, at):
    copies = [pltpu.make_async_copy(d, s, sems.at[at + i]) for i, (s, d) in enumerate(pairs)]
    for copy in copies:
        copy.start()
    return copies


def out_views(by_blocks, hbm):
    if not by_blocks:
        return hbm[:2], hbm[2:]
    views = [ref.at[k] for ref in hbm for k in range(ref.shape[0])]
    return views, views


def wait_all(copies):
    for copy in copies:
        copy.wait()


def fill_mask(sizes, seqs, starts_ref, place_ref, mask_ref):
    shape = (sizes.queries, sizes.keys)
    row = lax.broadcasted_iota(jnp.int32, shape, 0)
    col = lax.broadcasted_iota(jnp.int32, shape, 1)
    base = place_ref[0]
    total = place_ref[1]
    query = jnp.where(row < sizes.top, row, lax.shift_right_arithmetic(row - sizes.top, 4))
    left_at = sizes.rows + RIGHT_ROWS
    mem_at = left_at + LEFT_ROWS
    spot = jnp.where(col < left_at, col, col - mem_at)
    mem_seg = jnp.where(col < mem_at + sizes.segs, col - mem_at, col - mem_at - 2 * sizes.segs)
    key_seg = jnp.where(col < mem_at, lax.shift_right_arithmetic(spot, 4), mem_seg)
    near = (
        (key_seg == query)
        | ((spot >= query * SEG_LEN - LEFT_LEN) & (spot < query * SEG_LEN))
        | ((key_seg == query + 1) & (spot < query * SEG_LEN + SEG_LEN + RIGHT_LEN))
    )
    recent = (key_seg >= query - MEM_LEN) & (key_seg < query) & (row >= sizes.top)
    allowed = ((col < mem_at) & near) | ((col >= mem_at) & recent)
    key_abs = key_seg + base
    query_abs = query + base
    allowed = allowed & (key_abs >= 0) & (key_abs < total)
    if sizes.top:
        allowed = allowed & ((row < sizes.segs) | (row >= sizes.top))
    for n in range(seqs):
        key_owner = jnp.zeros(shape, jnp.int32)
        query_owner = jnp.zeros(shape, jnp.int32)
        for u in range(starts_ref.shape[1]):
            first = starts_ref[n, u]
            key_owner = key_owner + (key_abs >= first).astype(jnp.int32)
            query_owner = query_owner + (query_abs >= first).astype(jnp.int32)
        mask_ref[n] = jnp.where(allowed & (key_owner == query_owner), 0.0, -1e30)


def half_masks():
    lane = lax.broadcasted_iota(jnp.int32, (1, LANES), 1)
    even = (lane < LANES // 2).astype(F32)
    return even.astype(BF16), (1.0 - even).astype(BF16), lane < LANES // 2


def project(sizes, z_ref, qkv_ref, row_bias_ref, proj_ref):
    step = CHIPS_Z // 2
    for c in range(2):
        block = qkv_ref[pl.ds(c * step, step)].reshape(-1, sizes.width)
        wide = block.shape[0]
        made = nt(z_ref[...], block) + row_bias_ref[:, pl.ds(c * wide, wide)]
        proj_ref[:, pl.ds(c * wide, wide)] = made.astype(BF16)


def split_heads(sizes, ref, first, rows, lane):
    return ref[pl.ds(first, rows), pl.ds(lane, LANES)]


def attend(sizes, seqs, proj_ref, mask_ref, probs_ref, att_ref):
    even, odd, is_even = half_masks()
    scale = (sizes.width // HEADS) ** (-0.5)
    count = sizes.queries

    def body(p, carry):
        for n in range(seqs):
            lane = pl.multiple_of(p * LANES, LANES)
            query = proj_ref[pl.ds(n * sizes.ext, count), pl.ds(lane, LANES)]
            first = n * sizes.ext + sizes.top
            key = proj_ref[pl.ds(first, sizes.keys), pl.ds(sizes.width + lane, LANES)]
            value = proj_ref[pl.ds(first, sizes.keys), pl.ds(2 * sizes.width + lane, LANES)]
            scores = nt(jnp.concatenate([query * even, query * odd], axis=0), key) * scale
            outs = []
            for half in range(2):
                part = scores[half * count : (half + 1) * count] + mask_ref[n]
                part = jnp.exp(part - jnp.max(part, axis=1, keepdims=True))
                part = part * (1.0 / jnp.sum(part, axis=1, keepdims=True))
                probs_ref[n * sizes.pairs + p, pl.ds(half * count, count), :] = part
                outs.append(nn(part.astype(BF16), value))
            att_ref[pl.ds(n * count, count), pl.ds(lane, LANES)] = jnp.where(
                is_even, outs[0], outs[1]
            ).astype(BF16)
        return carry

    lax.fori_loop(0, sizes.pairs, body, 0)


def attend_back(sizes, seqs, proj_ref, probs_ref, go_ref, gproj_ref):
    even, odd, is_even = half_masks()
    scale = (sizes.width // HEADS) ** (-0.5)
    count = sizes.queries
    wide = sizes.width
    for n in range(seqs):
        base = n * sizes.ext
        rest = sizes.ext - count
        gproj_ref[pl.ds(base + count, rest), pl.ds(0, wide)] = jnp.zeros((rest, wide), BF16)
        if sizes.top:
            gproj_ref[pl.ds(base, sizes.top), pl.ds(wide, 2 * wide)] = jnp.zeros(
                (sizes.top, 2 * wide), BF16
            )

    def body(p, carry):
        for n in range(seqs):
            lane = pl.multiple_of(p * LANES, LANES)
            base = n * sizes.ext
            first = base + sizes.top
            query = proj_ref[pl.ds(base, count), pl.ds(lane, LANES)]
            key = proj_ref[pl.ds(first, sizes.keys), pl.ds(wide + lane, LANES)]
            value = proj_ref[pl.ds(first, sizes.keys), pl.ds(2 * wide + lane, LANES)]
            grad = go_ref[pl.ds(n * count, count), pl.ds(lane, LANES)]
            queries = jnp.concatenate([query * even, query * odd], axis=0)
            grads = jnp.concatenate([grad * even, grad * odd], axis=0)
            probs = probs_ref[n * sizes.pairs + p]
            grad_values = tn(probs.astype(BF16), grads)
            grad_probs = nt(grads, value)
            weighted = grad_probs * probs
            grad_scores = (
                (weighted - probs * jnp.sum(weighted, axis=1, keepdims=True)) * scale
            ).astype(BF16)
            grad_keys = tn(grad_scores, queries)
            grad_query = jnp.where(
                is_even, nn(grad_scores[:count], key), nn(grad_scores[count:], key)
            )
            gproj_ref[pl.ds(base, count), pl.ds(lane, LANES)] = grad_query.astype(BF16)
            gproj_ref[pl.ds(first, sizes.keys), pl.ds(wide + lane, LANES)] = grad_keys.astype(BF16)
            gproj_ref[pl.ds(first, sizes.keys), pl.ds(2 * wide + lane, LANES)] = (
                grad_values.astype(BF16)
            )
        return carry

    lax.fori_loop(0, sizes.pairs, body, 0)


def gelu_both(upward):
    half = 0.5 * (1.0 + lax.erf(upward * ROOT_HALF))
    slope = half + upward * jnp.exp(-0.5 * upward * upward) * INV_ROOT_TWO_PI
    return upward * half, slope


def up_block(up_ref, c, wide):
    step = wide // (up_ref.shape[1] * up_ref.shape[2])
    return up_ref[pl.ds(c * step, step)].reshape(-1, up_ref.shape[3])


def down_block(down_ref, c, wide):
    at = pl.multiple_of(c * wide, wide)
    return down_ref[:, :, :, pl.ds(at, wide)].reshape(-1, wide)


def ffn_back_step(
    sizes, c, wide, grad_low, hidden_low, active, slope, up_ref, down_ref, gup_ref, gdown_ref, vec
):
    at = pl.multiple_of(c * wide, wide)
    up = up_block(up_ref, c, wide)
    down = down_block(down_ref, c, wide)
    grad_active = nn(grad_low, down)
    grad_up_f = grad_active * slope
    grad_up = grad_up_f.astype(BF16)
    gdown_ref[:, :, :, pl.ds(at, wide)] = (
        tn(grad_low, active).astype(BF16).reshape(gdown_ref.shape[:3] + (wide,))
    )
    step = wide // (gup_ref.shape[1] * gup_ref.shape[2])
    gup_ref[pl.ds(c * step, step)] = (
        tn(grad_up, hidden_low).astype(BF16).reshape((step,) + gup_ref.shape[1:])
    )
    vec[pl.ds(8 + c, 1), :] = col_sum(grad_up.astype(F32))
    return nn(grad_up, up)


def attn_back_stage(
    sizes, seqs, gz, grad_mem_ref, att_ref, proj_ref, probs_ref, z_ref, qkv_ref, out_ref,
    gqkv_ref, gout_ref, go_ref, gproj_ref, branch_ref, vec, gh_ref, gmem_ref, back_left_ref,
    back_right_ref, scaled_rows=None,
):
    wide = sizes.width
    count = sizes.queries
    bias_out = col_sum(gz)
    for n in range(seqs):
        if sizes.top:
            mem_grad = grad_mem_ref[pl.ds(n * sizes.segs, sizes.segs), :]
            bias_out = bias_out + col_sum(mem_grad)
            branch_ref[pl.ds(n * count, sizes.top), :] = jnp.concatenate(
                [mem_grad, jnp.zeros((sizes.top - sizes.segs, wide), F32)], axis=0
            ).astype(BF16)
        branch_ref[pl.ds(n * count + sizes.top, sizes.rows), :] = gz[
            n * sizes.rows : (n + 1) * sizes.rows
        ].astype(BF16)
    vec[pl.ds(5, 1), :] = bias_out
    branch = branch_ref[...]
    gout_ref[...] = tn(branch, att_ref[...]).astype(BF16).reshape(gout_ref.shape)
    go_ref[...] = nn(branch, out_ref[...].reshape(-1, wide)).astype(BF16)
    attend_back(sizes, seqs, proj_ref, probs_ref, go_ref, gproj_ref)
    vec[pl.ds(3, 1), :] = col_sum(gproj_ref[:, pl.ds(0, wide)].astype(F32))
    vec[pl.ds(4, 1), :] = col_sum(gproj_ref[:, pl.ds(2 * wide, wide)].astype(F32))
    grad_ext = nn(gproj_ref[...], qkv_ref[...].reshape(-1, wide))
    gain_sum = jnp.zeros((1, wide), F32)
    bias_sum = jnp.zeros((1, wide), F32)
    for n in range(seqs):
        base = n * sizes.ext
        own = grad_ext[base + sizes.top : base + sizes.top + sizes.rows]
        if sizes.top:
            spread = grad_ext[base : base + sizes.segs] * (1.0 / SEG_LEN)
            own = own + segment_spread(sizes.rows, wide, spread)
        gh_ref[pl.ds(n * sizes.rows, sizes.rows), :] = own
        mem = base + sizes.mem_at
        gmem_ref[pl.ds(n * sizes.segs, sizes.segs), :] = grad_ext[mem : mem + sizes.segs]
        left = base + sizes.left_at
        back_left_ref[n] = grad_ext[left : left + BACK_ROWS].astype(BF16)
        right = base + sizes.right_at
        back_right_ref[n] = grad_ext[right : right + RIGHT_ROWS].astype(BF16)
        if scaled_rows is not None:
            grads = (
                own,
                grad_ext[right : right + RIGHT_ROWS],
                grad_ext[left : left + LEFT_ROWS],
            )
            for rows, scaled in zip(grads, scaled_rows(n)):
                gain_sum = gain_sum + col_sum(rows * scaled)
                bias_sum = bias_sum + col_sum(rows)
    if scaled_rows is not None:
        vec[pl.ds(0, 1), :] = gain_sum
        vec[pl.ds(2, 1), :] = bias_sum
    step = CHIPS_Z // 2
    part = gqkv_ref.shape[1] * gqkv_ref.shape[2] * step
    for c in range(2):
        gqkv_ref[pl.ds(c * step, step)] = (
            tn(gproj_ref[:, pl.ds(c * part, part)], z_ref[...])
            .astype(BF16)
            .reshape((step,) + gqkv_ref.shape[1:])
        )


def merge_halo(sizes, n, gh_ref, gmem_ref, from_right_ref, from_left_ref):
    first = n * sizes.rows
    back = from_right_ref[n].astype(F32)
    head = gh_ref[pl.ds(first, RIGHT_ROWS), :] + from_left_ref[n].astype(F32)
    middle = gh_ref[pl.ds(first + RIGHT_ROWS, sizes.rows - RIGHT_ROWS - LEFT_ROWS), :]
    tail = gh_ref[pl.ds(first + sizes.rows - LEFT_ROWS, LEFT_ROWS), :] + back[:LEFT_ROWS]
    mem = gmem_ref[pl.ds(n * sizes.segs, sizes.segs), :] + back[LEFT_ROWS + sizes.segs :]
    return jnp.concatenate([head, middle, tail], axis=0), mem


def pack_kernel(places, qkv_ref, out_ref, up_ref, down_ref, *packed):
    eye = identity(LANES)
    high, wide, low = qkv_ref.shape[1], out_ref.shape[1], down_ref.shape[1]
    up = up_ref.shape[2]
    for layer, (attn, attn_at, ffn, ffn_at) in enumerate(places):
        ref = packed[attn]
        ref[pl.ds(attn_at, high), :] = qkv_ref[layer]
        ref[pl.ds(attn_at + high, wide), :] = out_ref[layer]
        ref = packed[ffn]
        ref[pl.ds(ffn_at, up), :] = tn(up_ref[layer], eye).astype(BF16)
        for part in range(down_ref.shape[2] // LANES):
            ref[pl.ds(ffn_at + up + part * low, low), :] = down_ref[
                layer, :, pl.ds(part * LANES, LANES)
            ]


def unpack_kernel(each, places, place_ref, *refs):
    sources, outs = refs[:-8], refs[-8:]
    qkv_ref, out_ref, up_ref, down_ref, gains_ref, biases_ref, ffn_bias_ref, small_ref = outs
    eye = identity(LANES)
    high, wide, low = qkv_ref.shape[1], out_ref.shape[1], down_ref.shape[1]
    up = up_ref.shape[2]

    def total(source, first, rows):
        value = sources[source * each][pl.ds(first, rows), :].astype(F32)
        for part in sources[source * each + 1 : (source + 1) * each]:
            value = value + part[pl.ds(first, rows), :].astype(F32)
        return value

    for layer, (attn, attn_at, ffn, ffn_at) in enumerate(places):
        qkv_ref[layer] = total(attn, attn_at, high)
        out_ref[layer] = total(attn, attn_at + high, wide)
        up_ref[layer] = nt(eye, total(ffn, ffn_at, up).astype(BF16))
        for part in range(down_ref.shape[2] // LANES):
            down_ref[layer, :, pl.ds(part * LANES, LANES)] = total(
                ffn, ffn_at + up + part * low, low
            )
    for k in range(each):
        spot = lax.rem(place_ref[0] + each - k, each)
        small_ref[spot] = sources[k][pl.ds(high + wide, SMALL_ROWS), :].astype(F32)
    sums = small_ref[0]
    for k in range(1, each):
        sums = sums + small_ref[k]
    parts = gains_ref.shape[2] // LANES
    for layer in range(gains_ref.shape[0]):
        for part in range(parts):
            lanes = pl.ds(part * LANES, LANES)
            block = sums[(layer * parts + part) * TILE : (layer * parts + part + 1) * TILE]
            gains_ref[layer, :, lanes] = block[0:2]
            biases_ref[layer, :, lanes] = block[2:8]
            for row in range(ffn_bias_ref.shape[1] // gains_ref.shape[2]):
                at = row * gains_ref.shape[2] + part * LANES
                ffn_bias_ref[pl.ds(layer, 1), pl.ds(at, LANES)] = block[8 + row : 9 + row]


def stack_kernel(count, place_ref, *refs):
    sources, out_ref, sems = refs[:count], refs[count], refs[count + 1]
    copies = []
    for k, source in enumerate(sources):
        spot = lax.rem(place_ref[0] + count - k, count)
        copies.append(pltpu.make_async_copy(source, out_ref.at[spot], sems.at[k]))
    for copy in copies:
        copy.start()
    wait_all(copies)


def split_kernel(count, place_ref, mine_ref, theirs_ref, second_ref, first_ref, *outs):
    for k, out in enumerate(outs):
        spot = lax.rem(place_ref[0] + k, count)
        total = mine_ref[0, spot].astype(F32) + theirs_ref[0, spot].astype(F32)
        total = total + second_ref[0, spot].astype(F32) + first_ref[spot].astype(F32)
        out[...] = total.astype(BF16)


def far_kernel(rows, mine_ref, theirs_ref, came_ref, sent_small, came_small, out_ref):
    total = mine_ref[...].astype(F32) + theirs_ref[...].astype(F32)
    out_ref[pl.ds(0, rows), :] = (total + came_ref[...].astype(F32)).astype(BF16)
    out_ref[pl.ds(rows, SMALL_ROWS), :] = (
        sent_small[...].astype(F32) + came_small[...].astype(F32)
    ).astype(BF16)


def split_small_kernel(
    count, rows, place_ref, mine_ref, theirs_ref, second_ref, first_ref, sent_small, came_small,
    *outs
):
    sums = (sent_small[...].astype(F32) + came_small[...].astype(F32)).astype(BF16)
    for k, out in enumerate(outs):
        spot = lax.rem(place_ref[0] + k, count)
        group = pl.ds(pl.multiple_of(spot * rows, rows), rows)
        total = mine_ref[group, :].astype(F32) + theirs_ref[group, :].astype(F32)
        total = total + second_ref[group, :].astype(F32) + first_ref[group, :].astype(F32)
        out[pl.ds(0, rows), :] = total.astype(BF16)
        out[pl.ds(rows, SMALL_ROWS), :] = sums


def first_attn_kernel(
    sizes, seqs, mats, by_blocks, count_in, at, place_ref, starts_ref, frames_ref, left_ref,
    right_ref, gains_ref, biases_ref, row_bias_ref, *refs
):
    hbm = refs[:count_in]
    z_ref, proj_ref, probs_ref, att_ref, mixed_ref, mem_ref, qkv_ref, out_ref, mask_ref, sems = (
        refs[count_in:]
    )
    wide = sizes.width
    copies = start_in(
        attn_pairs(mats, by_blocks, hbm, at, qkv_ref, out_ref, place_ref), sems, 0
    )
    gain = gains_ref[0, pl.ds(0, 1), :]
    bias = biases_ref[0, pl.ds(0, 1), :]
    pad = jnp.zeros((TILE - sizes.segs, wide), F32)
    for n in range(seqs):
        own = frames_ref[n].astype(F32)
        before = left_ref[n].astype(F32)
        hidden = norm_forward(own, gain, bias)[0]
        halo = norm_forward(before[before.shape[0] - LEFT_ROWS :], gain, bias)[0]
        after = norm_forward(right_ref[n].astype(F32), gain, bias)[0]
        memory = jnp.concatenate(
            [
                segment_mean(own),
                jnp.zeros((sizes.segs - before.shape[0] // SEG_LEN, wide), F32),
                segment_mean(before),
            ],
            axis=0,
        )
        base = n * sizes.ext
        z_ref[pl.ds(base, sizes.top), :] = jnp.concatenate(
            [segment_mean(hidden), pad], axis=0
        ).astype(BF16)
        z_ref[pl.ds(base + sizes.top, sizes.rows), :] = hidden.astype(BF16)
        z_ref[pl.ds(base + sizes.right_at, RIGHT_ROWS), :] = after.astype(BF16)
        z_ref[pl.ds(base + sizes.left_at, LEFT_ROWS), :] = halo.astype(BF16)
        z_ref[pl.ds(base + sizes.mem_at, MEM_ROWS), :] = memory.astype(BF16)
    fill_mask(sizes, seqs, starts_ref, place_ref, mask_ref)
    wait_all(copies)
    project(sizes, z_ref, qkv_ref, row_bias_ref, proj_ref)
    attend(sizes, seqs, proj_ref, mask_ref, probs_ref, att_ref)
    mixed = nt(att_ref[...], out_ref[...].reshape(-1, wide)) + biases_ref[0, pl.ds(3, 1), :]
    for n in range(seqs):
        base = n * sizes.queries
        mem_ref[pl.ds(n * sizes.segs, sizes.segs), :] = mixed[base : base + sizes.segs]
        mixed_ref[pl.ds(n * sizes.rows, sizes.rows), :] = (
            frames_ref[n].astype(F32) + mixed[base + sizes.top : base + sizes.top + sizes.rows]
        )


def first_ffn_kernel(
    sizes, seqs, mats, by_blocks, count_in, at, place_ref, mixed_ref, mem_ref, gains_ref,
    biases_ref, ffn_bias_ref, *refs
):
    hbm = refs[:count_in]
    (
        next_ref, active_ref, slope_ref, low_ref, send_right_ref, send_left_ref, up_ref, down_ref,
        hidden_ref, sems,
    ) = refs[count_in:]
    copies = start_in(ffn_pairs(mats, by_blocks, hbm, at, up_ref, down_ref, place_ref), sems, 0)
    mixed = mixed_ref[...]
    hidden, _, _ = norm_forward(mixed, gains_ref[0, pl.ds(1, 1), :], biases_ref[0, pl.ds(4, 1), :])
    hidden_ref[...] = hidden.astype(BF16)
    next_ref[...] = mixed + biases_ref[0, pl.ds(5, 1), :]
    wait_all(copies)
    wide = sizes.width

    def body(c, carry):
        at_lane = pl.multiple_of(c * wide, wide)
        upward = nt(hidden_ref[...], up_block(up_ref, c, wide))
        upward = upward + ffn_bias_ref[pl.ds(0, 1), pl.ds(at_lane, wide)]
        active, slope = gelu_both(upward)
        active = active.astype(BF16)
        active_ref[:, pl.ds(at_lane, wide)] = active
        slope_ref[:, pl.ds(at_lane, wide)] = slope.astype(BF16)
        next_ref[...] += nt(active, down_block(down_ref, c, wide))
        return carry

    lax.fori_loop(0, sizes.ff // wide, body, 0)
    low, _, _ = norm_forward(
        next_ref[...], gains_ref[1, pl.ds(0, 1), :], biases_ref[1, pl.ds(0, 1), :]
    )
    low = low.astype(BF16)
    low_ref[...] = low
    for n in range(seqs):
        base = n * sizes.rows
        send_right_ref[n, pl.ds(0, LEFT_ROWS), :] = low[
            base + sizes.rows - LEFT_ROWS : base + sizes.rows
        ]
        send_right_ref[n, pl.ds(LEFT_ROWS, MEM_ROWS), :] = jnp.concatenate(
            [
                mem_ref[pl.ds(n * sizes.segs, sizes.segs), :],
                jnp.zeros((MEM_ROWS - sizes.segs, wide), F32),
            ],
            axis=0,
        ).astype(BF16)
        send_left_ref[n] = low[base : base + RIGHT_ROWS]


def last_layer_kernel(
    sizes, seqs, mats, by_blocks, count_in, attn_at, ffn_at, place_ref, starts_ref, low_ref,
    left_ref, right_ref, mem_ref, inputs_ref, out_grad_ref, gains_ref, biases_ref, ffn_bias_ref,
    row_bias_ref, *refs
):
    hbm = refs[:count_in]
    count_out = 2 if by_blocks else 4
    (encoded_ref, gz_ref, gh_ref, gmem_ref, back_left_ref, back_right_ref, vec) = refs[
        count_in : count_in + 7
    ]
    hbm_out = refs[count_in + 7 : count_in + 7 + count_out]
    (
        qkv_ref, out_ref, up_ref, down_ref, gqkv_ref, gout_ref, gup_ref, gdown_ref, mask_ref,
        z_ref, proj_ref, probs_ref, att_ref, hidden_ref, go_ref, gproj_ref, branch_ref,
        grad_low_ref, grad_hidden_ref, sems,
    ) = refs[count_in + 7 + count_out :]
    attn_hbm, ffn_hbm = (hbm, hbm) if by_blocks else (hbm[:2], hbm[2:])
    attn_out, ffn_out = out_views(by_blocks, hbm_out)
    wide = sizes.width
    attn_copies = start_in(
        attn_pairs(mats, by_blocks, attn_hbm, attn_at, qkv_ref, out_ref, place_ref), sems, 0
    )
    ffn_copies = start_in(
        ffn_pairs(mats, by_blocks, ffn_hbm, ffn_at, up_ref, down_ref, place_ref),
        sems,
        len(attn_copies),
    )
    vec[...] = jnp.zeros_like(vec)
    for n in range(seqs):
        base = n * sizes.ext
        z_ref[pl.ds(base, sizes.rows), :] = low_ref[pl.ds(n * sizes.rows, sizes.rows), :]
        z_ref[pl.ds(base + sizes.right_at, RIGHT_ROWS), :] = right_ref[n]
        z_ref[pl.ds(base + sizes.left_at, LEFT_ROWS), :] = left_ref[n, pl.ds(0, LEFT_ROWS), :]
        memory = jnp.concatenate(
            [
                mem_ref[pl.ds(n * sizes.segs, sizes.segs), :],
                left_ref[n, pl.ds(LEFT_ROWS, MEM_ROWS), :].astype(F32)[: sizes.segs],
            ],
            axis=0,
        )
        z_ref[pl.ds(base + sizes.mem_at, MEM_ROWS), :] = memory.astype(BF16)
        grad_low_ref[pl.ds(n * sizes.rows, sizes.rows), :] = out_grad_ref[n]
    fill_mask(sizes, seqs, starts_ref, place_ref, mask_ref)
    wait_all(attn_copies)
    project(sizes, z_ref, qkv_ref, row_bias_ref, proj_ref)
    attend(sizes, seqs, proj_ref, mask_ref, probs_ref, att_ref)
    mixed = (
        inputs_ref[...]
        + nt(att_ref[...], out_ref[...].reshape(-1, wide))
        + biases_ref[1, pl.ds(3, 1), :]
    )
    gain = gains_ref[1, pl.ds(1, 1), :]
    hidden, scaled, inverse = norm_forward(mixed, gain, biases_ref[1, pl.ds(4, 1), :])
    hidden_ref[...] = hidden.astype(BF16)
    for n in range(seqs):
        encoded_ref[n] = mixed[n * sizes.rows : (n + 1) * sizes.rows] + biases_ref[
            1, pl.ds(5, 1), :
        ]
    grad_hidden_ref[...] = jnp.zeros_like(grad_hidden_ref)
    wait_all(ffn_copies)

    def body(c, carry):
        at_lane = pl.multiple_of(c * wide, wide)
        upward = nt(hidden_ref[...], up_block(up_ref, c, wide))
        upward = upward + ffn_bias_ref[pl.ds(1, 1), pl.ds(at_lane, wide)]
        active, slope = gelu_both(upward)
        active = active.astype(BF16)
        made = nt(active, down_block(down_ref, c, wide))
        for n in range(seqs):
            encoded_ref[n] += made[n * sizes.rows : (n + 1) * sizes.rows]
        grad_hidden_ref[...] += ffn_back_step(
            sizes, c, wide, grad_low_ref[...], hidden_ref[...], active, slope, up_ref, down_ref,
            gup_ref, gdown_ref, vec,
        )
        return carry

    lax.fori_loop(0, sizes.ff // wide, body, 0)
    out_at = len(attn_copies) + len(ffn_copies)
    outs = start_out(
        ffn_pairs(mats, by_blocks, ffn_out, ffn_at, gup_ref, gdown_ref, place_ref), sems, out_at
    )
    grad = grad_low_ref[...].astype(F32)
    grad_hidden = grad_hidden_ref[...]
    vec[pl.ds(1, 1), :] = col_sum(grad_hidden * scaled)
    vec[pl.ds(6, 1), :] = col_sum(grad_hidden)
    vec[pl.ds(7, 1), :] = col_sum(grad)
    gz = grad + norm_backward(grad_hidden, scaled, inverse, gain)
    gz_ref[...] = gz
    attn_back_stage(
        sizes, seqs, gz, None, att_ref, proj_ref, probs_ref, z_ref, qkv_ref, out_ref, gqkv_ref,
        gout_ref, go_ref, gproj_ref, branch_ref, vec, gh_ref, gmem_ref, back_left_ref,
        back_right_ref,
    )
    outs = outs + start_out(
        attn_pairs(mats, by_blocks, attn_out, attn_at, gqkv_ref, gout_ref, place_ref),
        sems,
        out_at + len(outs),
    )
    wait_all(outs)


def first_ffn_back_kernel(
    last, sizes, seqs, mats, by_blocks, count_in, count_out, at_in, place_ref, inputs_ref,
    gz_in_ref, gh_in_ref, gmem_in_ref, from_right_ref, from_left_ref, mixed_ref, active_ref,
    slope_ref, gains_ref, biases_ref, *refs
):
    hbm = refs[:count_in]
    gz_ref, grad_mem_ref, upper_vec, vec = refs[count_in : count_in + 4]
    refs = refs[count_in + 4 :]
    hbm_out = refs[:count_out]
    if by_blocks:
        hbm_out = out_views(by_blocks, hbm_out)[0]
    (
        up_ref, down_ref, gup_ref, gdown_ref, hidden_ref, grad_low_ref, grad_ref, grad_hidden_ref,
        sems,
    ) = refs[count_out:]
    wide = sizes.width
    copies = start_in(
        ffn_pairs(mats, by_blocks, hbm, at_in, up_ref, down_ref, place_ref), sems, 0
    )
    vec[...] = jnp.zeros_like(vec)
    upper_vec[...] = jnp.zeros_like(upper_vec)
    gain = gains_ref[1, pl.ds(0, 1), :]
    gain_sum = jnp.zeros((1, wide), F32)
    bias_sum = jnp.zeros((1, wide), F32)
    for n in range(seqs):
        rows = pl.ds(n * sizes.rows, sizes.rows)
        _, scaled, inverse = norm_forward(
            inputs_ref[rows, :], gain, biases_ref[1, pl.ds(0, 1), :]
        )
        total, mem = merge_halo(last, n, gh_in_ref, gmem_in_ref, from_right_ref, from_left_ref)
        gain_sum = gain_sum + col_sum(total * scaled)
        bias_sum = bias_sum + col_sum(total)
        grad = gz_in_ref[rows, :] + norm_backward(total, scaled, inverse, gain)
        grad_ref[rows, :] = grad
        grad_low_ref[rows, :] = grad.astype(BF16)
        grad_mem_ref[pl.ds(n * sizes.segs, sizes.segs), :] = mem
    upper_vec[pl.ds(0, 1), :] = gain_sum
    upper_vec[pl.ds(2, 1), :] = bias_sum
    gain = gains_ref[0, pl.ds(1, 1), :]
    hidden, scaled, inverse = norm_forward(
        mixed_ref[...], gain, biases_ref[0, pl.ds(4, 1), :]
    )
    hidden_ref[...] = hidden.astype(BF16)
    grad_hidden_ref[...] = jnp.zeros_like(grad_hidden_ref)
    wait_all(copies)

    def body(c, carry):
        at_lane = pl.multiple_of(c * wide, wide)
        grad_hidden_ref[...] += ffn_back_step(
            sizes, c, wide, grad_low_ref[...], hidden_ref[...],
            active_ref[:, pl.ds(at_lane, wide)], slope_ref[:, pl.ds(at_lane, wide)].astype(F32),
            up_ref, down_ref, gup_ref, gdown_ref, vec,
        )
        return carry

    lax.fori_loop(0, sizes.ff // wide, body, 0)
    outs = start_out(
        ffn_pairs(mats, by_blocks, hbm_out, 0, gup_ref, gdown_ref, place_ref), sems, len(copies)
    )
    grad_hidden = grad_hidden_ref[...]
    grad = grad_ref[...]
    vec[pl.ds(1, 1), :] = col_sum(grad_hidden * scaled)
    vec[pl.ds(6, 1), :] = col_sum(grad_hidden)
    vec[pl.ds(7, 1), :] = col_sum(grad)
    gz_ref[...] = grad + norm_backward(grad_hidden, scaled, inverse, gain)
    wait_all(outs)


def first_attn_back_kernel(
    sizes, seqs, mats, by_blocks, count_in, count_out, at_in, place_ref, gz_ref, grad_mem_ref,
    att_ref, probs_ref, proj_ref, z_ref, frames_ref, left_ref, right_ref, gains_ref, biases_ref,
    ffn_vec, last_vec, upper_vec, *refs
):
    hbm = refs[:count_in]
    gh_ref, gmem_ref, back_left_ref, back_right_ref, vec = refs[count_in : count_in + 5]
    refs = refs[count_in + 5 :]
    hbm_out = refs[:count_out]
    small = []
    if by_blocks:
        rows = mats.attn_rows
        blocks = count_in // 2 * CHIPS_Z * rows
        small = [ref.at[pl.ds(blocks, SMALL_ROWS), :] for ref in hbm_out]
        hbm_out = [
            ref.at[pl.ds(0, blocks), :].reshape(count_in // 2, CHIPS_Z, rows, LANES).at[k]
            for ref in hbm_out
            for k in range(count_in // 2)
        ]
    (
        qkv_ref, out_ref, gqkv_ref, gout_ref, go_ref, gproj_ref, branch_ref, small_ref, sems,
    ) = refs[count_out:]
    copies = start_in(
        attn_pairs(mats, by_blocks, hbm, at_in, qkv_ref, out_ref, place_ref), sems, 0
    )
    vec[...] = jnp.zeros_like(vec)
    gain = gains_ref[0, pl.ds(0, 1), :]
    bias = biases_ref[0, pl.ds(0, 1), :]

    def scaled_rows(n):
        before = left_ref[n, pl.ds(left_ref.shape[1] - LEFT_ROWS, LEFT_ROWS), :]
        parts = (frames_ref[n], right_ref[n], before)
        return [norm_forward(part.astype(F32), gain, bias)[1] for part in parts]

    wait_all(copies)
    attn_back_stage(
        sizes, seqs, gz_ref[...], grad_mem_ref, att_ref, proj_ref, probs_ref, z_ref, qkv_ref,
        out_ref, gqkv_ref, gout_ref, go_ref, gproj_ref, branch_ref, vec, gh_ref, gmem_ref,
        back_left_ref, back_right_ref, scaled_rows,
    )
    outs = start_out(
        attn_pairs(mats, by_blocks, hbm_out, 0, gqkv_ref, gout_ref, place_ref), sems, len(copies)
    )
    parts = sizes.width // LANES
    for layer, total in enumerate((vec[...] + ffn_vec[...], last_vec[...] + upper_vec[...])):
        for part in range(parts):
            small_ref[pl.ds((layer * parts + part) * TILE, TILE), :] = total[
                :, part * LANES : (part + 1) * LANES
            ].astype(BF16)
    outs = outs + start_out([(ref, small_ref) for ref in small], sems, len(copies) + len(outs))
    wait_all(outs)


def frames_grad_kernel(
    sizes, seqs, frames_ref, gz_ref, gh_ref, gmem_ref, from_right_ref, from_left_ref, gains_ref,
    biases_ref, grad_ref
):
    gain = gains_ref[0, pl.ds(0, 1), :]
    for n in range(seqs):
        _, scaled, inverse = norm_forward(
            frames_ref[n].astype(F32), gain, biases_ref[0, pl.ds(0, 1), :]
        )
        total, mem = merge_halo(sizes, n, gh_ref, gmem_ref, from_right_ref, from_left_ref)
        grad_ref[n] = (
            gz_ref[pl.ds(n * sizes.rows, sizes.rows), :]
            + norm_backward(total, scaled, inverse, gain)
            + segment_spread(sizes.rows, sizes.width, mem * (1.0 / SEG_LEN))
        )


def shifted(value, axis, by):
    size = lax.axis_size(axis)
    pairs = [(i, i + by) for i in range(size) if 0 <= i + by < size]
    return lax.ppermute(value, axis, pairs)


def permuted(value, move):
    reps = lax.axis_size("rep")
    pairs = []
    for flat in range(lax.axis_size("seg") * reps):
        seg, rep = divmod(flat, reps)
        z, y, x, core = move(seg // CHIPS_Y, seg % CHIPS_Y, rep // 2, rep % 2)
        pairs.append((flat, (z * CHIPS_Y + y) * reps + 2 * x + core))
    return lax.ppermute(value, ("seg", "rep"), pairs)


def along_z(value, by):
    return permuted(value, lambda z, y, x, core: ((z + by) % CHIPS_Z, y, x, core))


def across_first(value):
    return permuted(value, lambda z, y, x, c: (z, y, x ^ 1, c) if c == 0 else (z, y ^ 1, x, c))


def across_second(value):
    return permuted(value, lambda z, y, x, c: (z, y ^ 1, x, c) if c == 0 else (z, y, x ^ 1, c))


def other_core(value):
    return permuted(value, lambda z, y, x, c: (z, y, x, c ^ 1))


def after(value, *others):
    return lax.optimization_barrier((value,) + others)[0]


def parts_along_z(shard):
    return [shard] + [along_z(shard, by) for by in range(1, CHIPS_Z)]


def stack_z(parts, z_place, others):
    return call(
        lambda *refs: stack_kernel(CHIPS_Z, *refs),
        [smem_spec()] + [vmem_spec()] * CHIPS_Z,
        [((CHIPS_Z,) + parts[0].shape, BF16)],
        [hbm_spec()],
        [pltpu.SemaphoreType.DMA((CHIPS_Z,))],
        [z_place, after(parts[0], *others)] + parts[1:],
    )[0]


def gather_sides(here):
    return [here, across_first(here), across_second(here)]


def both_cores(blocks):
    return blocks + [other_core(block) for block in blocks]


def summed(*parts):
    total = parts[0].astype(F32)
    for part in parts[1:]:
        total = total + part.astype(F32)
    return total.astype(BF16)


def one_block(shape):
    return pl.BlockSpec((1,) + tuple(shape[1:]), lambda i: (0,) * len(shape))


def row_block(rows, at):
    return pl.BlockSpec((rows, LANES), lambda i: (at, 0))


def split_z(mine, theirs, second, first, z_place):
    return call(
        lambda *refs: split_kernel(CHIPS_Z, *refs),
        [smem_spec()]
        + [one_block(member.shape) for member in (mine, theirs, second)]
        + [vmem_spec()],
        [(first.shape[1:], BF16)] * CHIPS_Z,
        [vmem_spec()] * CHIPS_Z,
        [],
        [z_place, mine, theirs, second, first],
        grid=(1,),
    )


def scatter_z(parts):
    return [parts[0]] + [along_z(parts[by], by) for by in range(1, CHIPS_Z)]


def sum_everywhere(value):
    count = lax.axis_size("seg") * lax.axis_size("rep")
    bit = 1
    while bit < count:
        value = value + lax.ppermute(value, ("seg", "rep"), [(i, i ^ bit) for i in range(count)])
        bit *= 2
    return value


def vmem_spec():
    return pl.BlockSpec(memory_space=pltpu.VMEM)


def smem_spec():
    return pl.BlockSpec(memory_space=pltpu.SMEM)


def hbm_spec():
    return pl.BlockSpec(memory_space=pl.ANY)


def call(body, in_specs, out_shapes, out_specs, scratch, args, flops=0, moved=0, grid=()):
    return pl.pallas_call(
        body,
        grid=grid,
        in_specs=in_specs,
        out_shape=tuple(jax.ShapeDtypeStruct(shape, kind) for shape, kind in out_shapes),
        out_specs=tuple(out_specs),
        scratch_shapes=scratch,
        compiler_params=pltpu.CompilerParams(vmem_limit_bytes=VMEM_BYTES),
        cost_estimate=pl.CostEstimate(flops=flops, bytes_accessed=moved, transcendentals=0),
    )(*args)


def on_device(
    frames,
    utt_segments,
    out_grad,
    qkv_weight,
    out_weight,
    ffn_in_weight,
    ffn_out_weight,
    norm_gains,
    biases,
    ffn_bias,
):
    micros, groups, rows, width = frames.shape
    seqs = micros * groups
    ff = ffn_bias.shape[1]
    reps = lax.axis_size("rep")
    seg_count = lax.axis_size("seg")
    mats = Matrices(width, ff)
    by_blocks = width // reps == LANES and reps == 4 and seg_count == BLOCKS
    first = Sizes(rows, width, ff, True)
    last = Sizes(rows, width, ff, False)
    own = seqs * rows
    mem_own = seqs * first.segs

    seg_at = lax.axis_index("seg")
    seg_base = seg_at * first.segs
    rep_at = lax.axis_index("rep")
    place = [seg_base, jnp.int32(first.segs * seg_count)]
    y_at, x_at, core_at = seg_at % CHIPS_Y, rep_at // 2, rep_at % 2
    z_place = jnp.reshape(seg_at // CHIPS_Y, (1,)).astype(jnp.int32)
    for other in range(2):
        core = lax.bitwise_xor(core_at, other)
        for hop2 in range(2):
            for hop1 in range(2):
                x_hop = jnp.where(core == 0, hop1, hop2)
                y_hop = jnp.where(core == 0, hop2, hop1)
                place.append(lax.bitwise_xor(y_at, y_hop))
                place.append((lax.bitwise_xor(x_at, x_hop) * 2 + core) * LANES)
    place = jnp.stack([jnp.asarray(entry, jnp.int32) for entry in place])
    lengths = utt_segments.reshape(seqs, utt_segments.shape[2])
    starts = (jnp.cumsum(lengths, axis=1) - lengths).astype(jnp.int32)
    zero_bias = jnp.zeros((width,), F32)
    row_bias = jnp.stack(
        [jnp.concatenate([biases[l, 1], zero_bias, biases[l, 2]]) for l in range(LAYERS)]
    ).reshape(LAYERS, 1, 3 * width)

    frames_own = frames.reshape(seqs, rows, width)
    grads_own = out_grad.reshape(seqs, rows, width)
    far = MEM_LEN * SEG_LEN
    frames_left = shifted(frames_own[:, rows - far :], "seg", 1)
    frames_right = shifted(frames_own[:, :RIGHT_ROWS], "seg", -1)

    attn_rows, ffn_rows = mats.attn_rows, mats.ffn_rows
    if by_blocks:
        qkv_t, out_t, down_t = (
            jnp.swapaxes(member, 1, 2) for member in (qkv_weight, out_weight, ffn_out_weight)
        )
        places = [(0, 0, 1, 0), (2, 0, 2, attn_rows)]
        chunk_rows = [attn_rows, ffn_rows, attn_rows + ffn_rows]
        shards = call(
            lambda *refs: pack_kernel(places, *refs),
            [vmem_spec()] * 4,
            [((high, LANES), BF16) for high in chunk_rows],
            [vmem_spec()] * len(chunk_rows),
            [],
            (qkv_t, out_t, ffn_in_weight, down_t),
        )
        sides0 = gather_sides(stack_z(parts_along_z(shards[0]), z_place, ()))
        parts = parts_along_z(after(shards[1], sides0[0]))
        halos = (frames_left, frames_right)
        sides1 = gather_sides(stack_z(parts, z_place, tuple(sides0[1:]) + halos))
        first_attn = both_cores(sides0 + [across_second(sides0[1])])
        first_at = 0, 0
        last_at = 0, attn_rows
        half = len(first_attn) // 2
        grad_outs = [
            [((half, CHIPS_Z, high, LANES), BF16)] * 2 for high in chunk_rows
        ]
        flat_rows = half * CHIPS_Z * attn_rows
        grad_outs[0] = [((flat_rows + SMALL_ROWS, LANES), BF16)] * 2
        copies_in = len(first_attn) * (3 + mats.down_parts)
    else:
        whole = []
        for member, shape in zip(
            (qkv_weight, out_weight, ffn_in_weight, ffn_out_weight),
            (mats.qkv, mats.out, mats.up, mats.down),
        ):
            member = lax.all_gather(member, "rep", axis=1, tiled=True)
            member = lax.all_gather(member, "seg", axis=2, tiled=True)
            whole.append(jnp.swapaxes(member, 1, 2).reshape((LAYERS,) + shape))
        first_attn = [whole[0][0], whole[1][0]]
        first_ffn = [whole[2][0], whole[3][0]]
        last_all = [member[1] for member in whole]
        first_at = last_at = 0, 0
        shapes = [(shape, BF16) for shape in (mats.qkv, mats.out, mats.up, mats.down)]
        grad_outs = [shapes[:2], shapes[2:], shapes]
        copies_in = 4
    dma = pltpu.SemaphoreType.DMA

    z0, proj0, probs0, att0, mixed0, mem1 = call(
        lambda *refs: first_attn_kernel(
            first, seqs, mats, by_blocks, len(first_attn), first_at[0], *refs
        ),
        [smem_spec()] * 2 + [vmem_spec()] * 6 + [hbm_spec()] * len(first_attn),
        [
            ((seqs * first.ext, width), BF16),
            ((seqs * first.ext, 3 * width), BF16),
            ((seqs * first.pairs, 2 * first.queries, first.keys), F32),
            ((seqs * first.queries, width), BF16),
            ((own, width), F32),
            ((mem_own, width), F32),
        ],
        [vmem_spec()] * 6,
        [
            pltpu.VMEM(mats.qkv, BF16),
            pltpu.VMEM(mats.out, BF16),
            pltpu.VMEM((seqs, first.queries, first.keys), F32),
            dma((copies_in,)),
        ],
        (place, starts, frames_own, frames_left, frames_right, norm_gains, biases, row_bias[0])
        + tuple(first_attn),
        flops=40 * own * 4 * width * width,
        moved=8 * width * width,
    )
    if by_blocks:
        parts = parts_along_z(after(shards[2], sides1[0]))
        first_ffn = both_cores(sides1 + [across_second(after(sides1[1], mixed0, *parts))])
        sides2 = gather_sides(stack_z(parts, z_place, tuple(first_ffn[4:7])))
    x1, active0, slope0, low1, send_right, send_left = call(
        lambda *refs: first_ffn_kernel(first, seqs, mats, by_blocks, len(first_ffn), first_at[1], *refs),
        [smem_spec()] + [vmem_spec()] * 5 + [hbm_spec()] * len(first_ffn),
        [
            ((own, width), F32),
            ((own, ff), BF16),
            ((own, ff), BF16),
            ((own, width), BF16),
            ((seqs, BACK_ROWS, width), BF16),
            ((seqs, RIGHT_ROWS, width), BF16),
        ],
        [vmem_spec()] * 6,
        [
            pltpu.VMEM(mats.up, BF16),
            pltpu.VMEM(mats.down, BF16),
            pltpu.VMEM((own, width), BF16),
            dma((copies_in,)),
        ],
        (place, mixed0, mem1, norm_gains, biases, ffn_bias) + tuple(first_ffn),
        flops=16 * own * 2 * width * ff,
        moved=4 * width * ff,
    )
    left1 = shifted(send_right, "seg", 1)
    right1 = shifted(send_left, "seg", -1)
    if by_blocks:
        last_all = both_cores(sides2 + [across_second(after(sides2[1], sides2[2], left1, right1))])

    vec_shape = (TILE, width)
    outs = call(
        lambda *refs: last_layer_kernel(
            last, seqs, mats, by_blocks, len(last_all), *last_at, *refs
        ),
        [smem_spec()] * 2 + [vmem_spec()] * 10 + [hbm_spec()] * len(last_all),
        [
            ((seqs, rows, width), F32),
            ((own, width), F32),
            ((own, width), F32),
            ((mem_own, width), F32),
            ((seqs, BACK_ROWS, width), BF16),
            ((seqs, RIGHT_ROWS, width), BF16),
            (vec_shape, F32),
        ]
        + grad_outs[2],
        [vmem_spec()] * 7 + [hbm_spec()] * len(grad_outs[2]),
        [
            pltpu.VMEM(mats.qkv, BF16),
            pltpu.VMEM(mats.out, BF16),
            pltpu.VMEM(mats.up, BF16),
            pltpu.VMEM(mats.down, BF16),
            pltpu.VMEM(mats.qkv, BF16),
            pltpu.VMEM(mats.out, BF16),
            pltpu.VMEM(mats.up, BF16),
            pltpu.VMEM(mats.down, BF16),
            pltpu.VMEM((seqs, last.queries, last.keys), F32),
            pltpu.VMEM((seqs * last.ext, width), BF16),
            pltpu.VMEM((seqs * last.ext, 3 * width), BF16),
            pltpu.VMEM((seqs * last.pairs, 2 * last.queries, last.keys), F32),
            pltpu.VMEM((seqs * last.queries, width), BF16),
            pltpu.VMEM((own, width), BF16),
            pltpu.VMEM((seqs * last.queries, width), BF16),
            pltpu.VMEM((seqs * last.ext, 3 * width), BF16),
            pltpu.VMEM((seqs * last.queries, width), BF16),
            pltpu.VMEM((own, width), BF16),
            pltpu.VMEM((own, width), F32),
            dma((2 * copies_in,)),
        ],
        (place, starts, low1, left1, right1, mem1, x1, grads_own, norm_gains, biases, ffn_bias,
         row_bias[1]) + tuple(last_all),
        flops=30 * own * (4 * width * width + 2 * width * ff),
        moved=4 * (4 * width * width + 2 * width * ff),
    )
    encoded, gz1, gh1, gmem1, back_left1, back_right1, vec1 = outs[:7]
    grad_blocks1 = outs[7:]
    from_right1 = shifted(back_left1, "seg", -1)
    from_left1 = shifted(back_right1, "seg", 1)

    gh1_tied = gh1
    if by_blocks:
        mine1, theirs1 = grad_blocks1[0], other_core(grad_blocks1[1])
        far1 = after(summed(mine1[2:], theirs1[2:]), from_right1, from_left1)
        gh1_tied = after(gh1, far1)
    gz0, grad_mem, upper_vec, vec0_ffn, *grad_ffn0 = call(
        lambda *refs: first_ffn_back_kernel(
            last, first, seqs, mats, by_blocks, len(first_ffn), len(grad_outs[1]), first_at[1],
            *refs
        ),
        [smem_spec()] + [vmem_spec()] * 11 + [hbm_spec()] * len(first_ffn),
        [
            ((own, width), F32),
            ((mem_own, width), F32),
            (vec_shape, F32),
            (vec_shape, F32),
        ]
        + grad_outs[1],
        [vmem_spec()] * 4 + [hbm_spec()] * len(grad_outs[1]),
        [
            pltpu.VMEM(mats.up, BF16),
            pltpu.VMEM(mats.down, BF16),
            pltpu.VMEM(mats.up, BF16),
            pltpu.VMEM(mats.down, BF16),
            pltpu.VMEM((own, width), BF16),
            pltpu.VMEM((own, width), BF16),
            pltpu.VMEM((own, width), F32),
            pltpu.VMEM((own, width), F32),
            dma((2 * copies_in,)),
        ],
        (place, x1, gz1, gh1_tied, gmem1, from_right1, from_left1, mixed0, active0, slope0, norm_gains,
         biases) + tuple(first_ffn),
        flops=28 * own * 2 * width * ff,
        moved=8 * width * ff,
    )
    gz0_tied = gz0
    if by_blocks:
        second1 = across_second(far1)
        near1 = summed(mine1[1], theirs1[1], second1[1])
        mine_ffn, theirs_ffn = grad_ffn0[0], other_core(after(grad_ffn0[1], second1))
        far_ffn = summed(mine_ffn[2:], theirs_ffn[2:])
        gz0_tied = after(gz0, near1, far_ffn)
    gh0, gmem0, back_left0, back_right0, vec0_attn, *grad_attn0 = call(
        lambda *refs: first_attn_back_kernel(
            first, seqs, mats, by_blocks, len(first_attn), len(grad_outs[0]), first_at[0], *refs
        ),
        [smem_spec()] + [vmem_spec()] * 14 + [hbm_spec()] * len(first_attn),
        [
            ((own, width), F32),
            ((mem_own, width), F32),
            ((seqs, BACK_ROWS, width), BF16),
            ((seqs, RIGHT_ROWS, width), BF16),
            (vec_shape, F32),
        ]
        + grad_outs[0],
        [vmem_spec()] * 5 + [hbm_spec()] * len(grad_outs[0]),
        [
            pltpu.VMEM(mats.qkv, BF16),
            pltpu.VMEM(mats.out, BF16),
            pltpu.VMEM(mats.qkv, BF16),
            pltpu.VMEM(mats.out, BF16),
            pltpu.VMEM((seqs * first.queries, width), BF16),
            pltpu.VMEM((seqs * first.ext, 3 * width), BF16),
            pltpu.VMEM((seqs * first.queries, width), BF16),
            pltpu.VMEM((SMALL_ROWS, LANES), BF16),
            dma((2 * copies_in,)),
        ],
        (place, gz0_tied, grad_mem, att0, probs0, proj0, z0, frames_own, frames_left, frames_right,
         norm_gains, biases, vec0_ffn, vec1, upper_vec) + tuple(first_attn),
        flops=56 * own * 4 * width * width,
        moved=16 * width * width,
    )
    from_right0 = shifted(back_left0, "seg", -1)
    from_left0 = shifted(back_right0, "seg", 1)
    gz0_last = gz0
    if by_blocks:
        first1 = across_first(near1)
        split1 = split_z(mine1, theirs1, second1, after(first1, gh0), z_place)
        last_parts = scatter_z(split1)
        gz0_last = after(gz0, *last_parts)
    frames_grad = call(
        lambda *refs: frames_grad_kernel(first, seqs, *refs),
        [vmem_spec()] * 8,
        [((seqs, rows, width), F32)],
        [vmem_spec()],
        [],
        (frames_own, gz0_last, gh0, gmem0, from_right0, from_left0, norm_gains, biases),
    )[0]

    if by_blocks:
        second_ffn = across_second(far_ffn)
        mine_attn = grad_attn0[0]
        theirs_attn = other_core(after(grad_attn0[1], *split1, second_ffn))
        near_ffn = summed(mine_ffn[1], theirs_ffn[1], second_ffn[1])
        ffn_parts = scatter_z(
            split_z(mine_ffn, theirs_ffn, second_ffn, across_first(near_ffn), z_place)
        )
        rows2, rows1 = flat_rows // 2, flat_rows // 4
        far_attn = after(summed(mine_attn[rows2:], theirs_attn[rows2:]), second_ffn)
        second_attn = across_second(far_attn)
        second_tied = after(second_attn, frames_grad)
        near_attn = call(
            lambda *refs: far_kernel(rows1, *refs),
            [row_block(rows1, 1)] * 3 + [row_block(SMALL_ROWS, rows2 // SMALL_ROWS)] * 2,
            [((rows1 + SMALL_ROWS, LANES), BF16)],
            [vmem_spec()],
            [],
            [mine_attn, theirs_attn, second_tied, far_attn, second_tied],
            grid=(1,),
        )[0]
        first_attn_sum = across_first(near_attn)
        attn_parts = scatter_z(
            call(
                lambda *refs: split_small_kernel(CHIPS_Z, attn_rows, *refs),
                [smem_spec()]
                + [row_block(rows1, 0)] * 4
                + [row_block(SMALL_ROWS, rows1 // SMALL_ROWS)] * 2,
                [((attn_rows + SMALL_ROWS, LANES), BF16)] * CHIPS_Z,
                [vmem_spec()] * CHIPS_Z,
                [],
                [z_place, mine_attn, theirs_attn, second_attn, first_attn_sum, near_attn,
                 first_attn_sum],
                grid=(1,),
            )
        )
        shapes = [member.shape for member in (qkv_t, out_t, ffn_in_weight, down_t)]
        shapes += [member.shape for member in (norm_gains, biases, ffn_bias)]
        reduced = call(
            lambda *refs: unpack_kernel(CHIPS_Z, places, *refs),
            [smem_spec()] + [vmem_spec()] * (3 * CHIPS_Z),
            [(shape, F32) for shape in shapes],
            [vmem_spec()] * len(shapes),
            [pltpu.VMEM((CHIPS_Z, SMALL_ROWS, LANES), F32)],
            [z_place] + attn_parts + ffn_parts + last_parts,
        )
        small = reduced[4:]
        reduced = [
            jnp.swapaxes(reduced[0], 1, 2),
            jnp.swapaxes(reduced[1], 1, 2),
            reduced[2],
            jnp.swapaxes(reduced[3], 1, 2),
        ]
    else:
        reduced = []
        for member0, member1 in zip(grad_attn0 + grad_ffn0, grad_blocks1):
            both = jnp.stack([member0, member1]).reshape(LAYERS, -1, member0.shape[3])
            both = jnp.swapaxes(both, 1, 2)
            both = lax.psum_scatter(both, "seg", scatter_dimension=2, tiled=True)
            both = lax.psum_scatter(both, "rep", scatter_dimension=1, tiled=True)
            reduced.append(both.astype(F32))
        small = sum_everywhere(jnp.stack([vec0_ffn + vec0_attn, vec1 + upper_vec]))
        small = small[:, 0:2], small[:, 2:8], small[:, 8:12].reshape(ffn_bias.shape)

    return (
        encoded.reshape(frames.shape),
        frames_grad.reshape(frames.shape),
        reduced[0],
        reduced[1],
        reduced[2],
        reduced[3],
        small[0],
        small[1],
        small[2],
    )


def solution(mesh):
    in_specs = (
        P(None, "rep", "seg", None),
        P(None, "rep", None),
        P(None, "rep", "seg", None),
        P(None, "rep", "seg"),
        P(None, "rep", "seg"),
        P(None, "rep", "seg"),
        P(None, "rep", "seg"),
        P(),
        P(),
        P(),
    )
    out_specs = (
        P(None, "rep", "seg", None),
        P(None, "rep", "seg", None),
        P(None, "rep", "seg"),
        P(None, "rep", "seg"),
        P(None, "rep", "seg"),
        P(None, "rep", "seg"),
        P(),
        P(),
        P(),
    )
    return jax.shard_map(
        on_device, mesh=mesh, in_specs=in_specs, out_specs=out_specs, check_vma=False
    )
```

```python
import jax
import jax.numpy as jnp
from jax import lax
from jax.experimental import pallas as pl
from jax.experimental.pallas import tpu as pltpu
from jax.sharding import PartitionSpec as P

HEADS = 8
SEG_LEN = 16
LEFT_LEN = 30
RIGHT_LEN = 4
MEM_LEN = 4
LAYERS = 2

EPS = 1e-05
ROOT_HALF = 0.7071067811865476
INV_ROOT_TWO_PI = 0.3989422804014327

LANES = 128
TILE = 16
RIGHT_ROWS = 16
LEFT_ROWS = 32
MEM_ROWS = 16
BACK_ROWS = LEFT_ROWS + MEM_ROWS
CHIPS_Z = 4
CHIPS_Y = 2
BLOCKS = CHIPS_Z * CHIPS_Y
SMALL_ROWS = 128
VMEM_BYTES = 56 * 1024 * 1024

BF16 = jnp.bfloat16
F32 = jnp.float32


def nn(a, b):
    return lax.dot_general(a, b, (((1,), (0,)), ((), ())), preferred_element_type=F32)


def nt(a, b):
    return lax.dot_general(a, b, (((1,), (1,)), ((), ())), preferred_element_type=F32)


def tn(a, b):
    return lax.dot_general(a, b, (((0,), (0,)), ((), ())), preferred_element_type=F32)


def col_sum(value):
    return jnp.sum(value, axis=0, keepdims=True)


def norm_forward(inputs, gain, bias):
    center = inputs - jnp.mean(inputs, axis=1, keepdims=True)
    inverse = lax.rsqrt(jnp.mean(center * center, axis=1, keepdims=True) + EPS)
    scaled = center * inverse
    return scaled * gain + bias, scaled, inverse


def norm_backward(grad_in, scaled, inverse, gain):
    grad_scaled = grad_in * gain
    return inverse * (
        grad_scaled
        - jnp.mean(grad_scaled, axis=1, keepdims=True)
        - scaled * jnp.mean(grad_scaled * scaled, axis=1, keepdims=True)
    )


def segment_mean(inputs):
    rows, width = inputs.shape
    return jnp.mean(inputs.reshape(rows // SEG_LEN, SEG_LEN, width), axis=1)


def segment_spread(rows, width, per_segment):
    segs = rows // SEG_LEN
    return jnp.broadcast_to(per_segment[:, None, :], (segs, SEG_LEN, width)).reshape(rows, width)


def identity(size):
    row = lax.broadcasted_iota(jnp.int32, (size, size), 0)
    col = lax.broadcasted_iota(jnp.int32, (size, size), 1)
    return (row == col).astype(F32).astype(BF16)


class Sizes:
    def __init__(self, rows, width, ff, with_summary):
        self.rows = rows
        self.width = width
        self.ff = ff
        self.segs = rows // SEG_LEN
        self.top = TILE if with_summary else 0
        self.keys = rows + RIGHT_ROWS + LEFT_ROWS + MEM_ROWS
        self.ext = self.top + self.keys
        self.queries = self.top + rows
        self.right_at = self.top + rows
        self.left_at = self.right_at + RIGHT_ROWS
        self.mem_at = self.left_at + LEFT_ROWS
        self.pairs = width // LANES


class Matrices:
    def __init__(self, width, ff):
        self.qkv = (CHIPS_Z, CHIPS_Y, 3 * width // BLOCKS, width)
        self.out = (CHIPS_Z, CHIPS_Y, width // BLOCKS, width)
        self.up = (CHIPS_Z, CHIPS_Y, ff // BLOCKS, width)
        self.down = (CHIPS_Z, CHIPS_Y, width // BLOCKS, ff)
        self.down_parts = ff // width
        self.attn_rows = self.qkv[2] + self.out[2]
        self.ffn_rows = self.up[2] + self.down_parts * self.down[2]


def attn_pairs(mats, by_blocks, hbm, first, qkv_ref, out_ref, place_ref):
    if not by_blocks:
        return [(hbm[0], qkv_ref), (hbm[1], out_ref)]
    pairs = []
    high = mats.qkv[2]
    for k, block in enumerate(hbm):
        row = place_ref[2 + 2 * k]
        lane = pl.multiple_of(place_ref[3 + 2 * k], LANES)
        pairs.append(
            (block.at[:, pl.ds(first, high), :], qkv_ref.at[:, row, :, pl.ds(lane, LANES)])
        )
        pairs.append(
            (
                block.at[:, pl.ds(first + high, mats.out[2]), :],
                out_ref.at[:, row, :, pl.ds(lane, LANES)],
            )
        )
    return pairs


def ffn_pairs(mats, by_blocks, hbm, first, up_ref, down_ref, place_ref):
    if not by_blocks:
        return [(hbm[0], up_ref), (hbm[1], down_ref)]
    pairs = []
    high = mats.up[2]
    low = mats.down[2]
    for k, block in enumerate(hbm):
        row = place_ref[2 + 2 * k]
        lane = pl.multiple_of(place_ref[3 + 2 * k], LANES)
        pairs.append(
            (block.at[:, pl.ds(first, high), :], up_ref.at[:, row, :, pl.ds(lane, LANES)])
        )
        for part in range(mats.down_parts):
            there = pl.multiple_of(
                place_ref[3 + 2 * k] * mats.down_parts + part * LANES, LANES
            )
            pairs.append(
                (
                    block.at[:, pl.ds(first + high + part * low, low), :],
                    down_ref.at[:, row, :, pl.ds(there, LANES)],
                )
            )
    return pairs


def start_in(pairs, sems, at):
    copies = [pltpu.make_async_copy(s, d, sems.at[at + i]) for i, (s, d) in enumerate(pairs)]
    for copy in copies:
        copy.start()
    return copies


def start_out(pairs, sems, at):
    copies = [pltpu.make_async_copy(d, s, sems.at[at + i]) for i, (s, d) in enumerate(pairs)]
    for copy in copies:
        copy.start()
    return copies


def out_views(by_blocks, hbm):
    if not by_blocks:
        return hbm[:2], hbm[2:]
    views = [ref.at[k] for ref in hbm for k in range(ref.shape[0])]
    return views, views


def wait_all(copies):
    for copy in copies:
        copy.wait()


def fill_mask(sizes, seqs, starts_ref, place_ref, mask_ref):
    shape = (sizes.queries, sizes.keys)
    row = lax.broadcasted_iota(jnp.int32, shape, 0)
    col = lax.broadcasted_iota(jnp.int32, shape, 1)
    base = place_ref[0]
    total = place_ref[1]
    query = jnp.where(row < sizes.top, row, lax.shift_right_arithmetic(row - sizes.top, 4))
    left_at = sizes.rows + RIGHT_ROWS
    mem_at = left_at + LEFT_ROWS
    spot = jnp.where(col < left_at, col, col - mem_at)
    mem_seg = jnp.where(col < mem_at + sizes.segs, col - mem_at, col - mem_at - 2 * sizes.segs)
    key_seg = jnp.where(col < mem_at, lax.shift_right_arithmetic(spot, 4), mem_seg)
    near = (
        (key_seg == query)
        | ((spot >= query * SEG_LEN - LEFT_LEN) & (spot < query * SEG_LEN))
        | ((key_seg == query + 1) & (spot < query * SEG_LEN + SEG_LEN + RIGHT_LEN))
    )
    recent = (key_seg >= query - MEM_LEN) & (key_seg < query) & (row >= sizes.top)
    allowed = ((col < mem_at) & near) | ((col >= mem_at) & recent)
    key_abs = key_seg + base
    query_abs = query + base
    allowed = allowed & (key_abs >= 0) & (key_abs < total)
    if sizes.top:
        allowed = allowed & ((row < sizes.segs) | (row >= sizes.top))
    for n in range(seqs):
        key_owner = jnp.zeros(shape, jnp.int32)
        query_owner = jnp.zeros(shape, jnp.int32)
        for u in range(starts_ref.shape[1]):
            first = starts_ref[n, u]
            key_owner = key_owner + (key_abs >= first).astype(jnp.int32)
            query_owner = query_owner + (query_abs >= first).astype(jnp.int32)
        mask_ref[n] = jnp.where(allowed & (key_owner == query_owner), 0.0, -1e30)


def half_masks():
    lane = lax.broadcasted_iota(jnp.int32, (1, LANES), 1)
    even = (lane < LANES // 2).astype(F32)
    return even.astype(BF16), (1.0 - even).astype(BF16), lane < LANES // 2


def project(sizes, z_ref, qkv_ref, row_bias_ref, proj_ref):
    step = CHIPS_Z // 2
    for c in range(2):
        block = qkv_ref[pl.ds(c * step, step)].reshape(-1, sizes.width)
        wide = block.shape[0]
        made = nt(z_ref[...], block) + row_bias_ref[:, pl.ds(c * wide, wide)]
        proj_ref[:, pl.ds(c * wide, wide)] = made.astype(BF16)


def split_heads(sizes, ref, first, rows, lane):
    return ref[pl.ds(first, rows), pl.ds(lane, LANES)]


def attend(sizes, seqs, proj_ref, mask_ref, probs_ref, att_ref):
    even, odd, is_even = half_masks()
    scale = (sizes.width // HEADS) ** (-0.5)
    count = sizes.queries

    def body(p, carry):
        for n in range(seqs):
            lane = pl.multiple_of(p * LANES, LANES)
            query = proj_ref[pl.ds(n * sizes.ext, count), pl.ds(lane, LANES)]
            first = n * sizes.ext + sizes.top
            key = proj_ref[pl.ds(first, sizes.keys), pl.ds(sizes.width + lane, LANES)]
            value = proj_ref[pl.ds(first, sizes.keys), pl.ds(2 * sizes.width + lane, LANES)]
            scores = nt(jnp.concatenate([query * even, query * odd], axis=0), key) * scale
            outs = []
            for half in range(2):
                part = scores[half * count : (half + 1) * count] + mask_ref[n]
                part = jnp.exp(part - jnp.max(part, axis=1, keepdims=True))
                part = part * (1.0 / jnp.sum(part, axis=1, keepdims=True))
                probs_ref[n * sizes.pairs + p, pl.ds(half * count, count), :] = part
                outs.append(nn(part.astype(BF16), value))
            att_ref[pl.ds(n * count, count), pl.ds(lane, LANES)] = jnp.where(
                is_even, outs[0], outs[1]
            ).astype(BF16)
        return carry

    lax.fori_loop(0, sizes.pairs, body, 0)


def attend_back(sizes, seqs, proj_ref, probs_ref, go_ref, gproj_ref):
    even, odd, is_even = half_masks()
    scale = (sizes.width // HEADS) ** (-0.5)
    count = sizes.queries
    wide = sizes.width
    for n in range(seqs):
        base = n * sizes.ext
        rest = sizes.ext - count
        gproj_ref[pl.ds(base + count, rest), pl.ds(0, wide)] = jnp.zeros((rest, wide), BF16)
        if sizes.top:
            gproj_ref[pl.ds(base, sizes.top), pl.ds(wide, 2 * wide)] = jnp.zeros(
                (sizes.top, 2 * wide), BF16
            )

    def body(p, carry):
        for n in range(seqs):
            lane = pl.multiple_of(p * LANES, LANES)
            base = n * sizes.ext
            first = base + sizes.top
            query = proj_ref[pl.ds(base, count), pl.ds(lane, LANES)]
            key = proj_ref[pl.ds(first, sizes.keys), pl.ds(wide + lane, LANES)]
            value = proj_ref[pl.ds(first, sizes.keys), pl.ds(2 * wide + lane, LANES)]
            grad = go_ref[pl.ds(n * count, count), pl.ds(lane, LANES)]
            queries = jnp.concatenate([query * even, query * odd], axis=0)
            grads = jnp.concatenate([grad * even, grad * odd], axis=0)
            probs = probs_ref[n * sizes.pairs + p]
            grad_values = tn(probs.astype(BF16), grads)
            grad_probs = nt(grads, value)
            weighted = grad_probs * probs
            grad_scores = (
                (weighted - probs * jnp.sum(weighted, axis=1, keepdims=True)) * scale
            ).astype(BF16)
            grad_keys = tn(grad_scores, queries)
            grad_query = jnp.where(
                is_even, nn(grad_scores[:count], key), nn(grad_scores[count:], key)
            )
            gproj_ref[pl.ds(base, count), pl.ds(lane, LANES)] = grad_query.astype(BF16)
            gproj_ref[pl.ds(first, sizes.keys), pl.ds(wide + lane, LANES)] = grad_keys.astype(BF16)
            gproj_ref[pl.ds(first, sizes.keys), pl.ds(2 * wide + lane, LANES)] = (
                grad_values.astype(BF16)
            )
        return carry

    lax.fori_loop(0, sizes.pairs, body, 0)


def gelu_both(upward):
    half = 0.5 * (1.0 + lax.erf(upward * ROOT_HALF))
    slope = half + upward * jnp.exp(-0.5 * upward * upward) * INV_ROOT_TWO_PI
    return upward * half, slope


def up_block(up_ref, c, wide):
    step = wide // (up_ref.shape[1] * up_ref.shape[2])
    return up_ref[pl.ds(c * step, step)].reshape(-1, up_ref.shape[3])


def down_block(down_ref, c, wide):
    at = pl.multiple_of(c * wide, wide)
    return down_ref[:, :, :, pl.ds(at, wide)].reshape(-1, wide)


def ffn_back_step(
    sizes, c, wide, grad_low, hidden_low, active, slope, up_ref, down_ref, gup_ref, gdown_ref, vec
):
    at = pl.multiple_of(c * wide, wide)
    up = up_block(up_ref, c, wide)
    down = down_block(down_ref, c, wide)
    grad_active = nn(grad_low, down)
    grad_up_f = grad_active * slope
    grad_up = grad_up_f.astype(BF16)
    gdown_ref[:, :, :, pl.ds(at, wide)] = (
        tn(grad_low, active).astype(BF16).reshape(gdown_ref.shape[:3] + (wide,))
    )
    step = wide // (gup_ref.shape[1] * gup_ref.shape[2])
    gup_ref[pl.ds(c * step, step)] = (
        tn(grad_up, hidden_low).astype(BF16).reshape((step,) + gup_ref.shape[1:])
    )
    vec[pl.ds(8 + c, 1), :] = col_sum(grad_up.astype(F32))
    return nn(grad_up, up)


def attn_back_stage(
    sizes, seqs, gz, grad_mem_ref, att_ref, proj_ref, probs_ref, z_ref, qkv_ref, out_ref,
    gqkv_ref, gout_ref, go_ref, gproj_ref, branch_ref, vec, gh_ref, gmem_ref, back_left_ref,
    back_right_ref, scaled_rows=None,
):
    wide = sizes.width
    count = sizes.queries
    bias_out = col_sum(gz)
    for n in range(seqs):
        if sizes.top:
            mem_grad = grad_mem_ref[pl.ds(n * sizes.segs, sizes.segs), :]
            bias_out = bias_out + col_sum(mem_grad)
            branch_ref[pl.ds(n * count, sizes.top), :] = jnp.concatenate(
                [mem_grad, jnp.zeros((sizes.top - sizes.segs, wide), F32)], axis=0
            ).astype(BF16)
        branch_ref[pl.ds(n * count + sizes.top, sizes.rows), :] = gz[
            n * sizes.rows : (n + 1) * sizes.rows
        ].astype(BF16)
    vec[pl.ds(5, 1), :] = bias_out
    branch = branch_ref[...]
    gout_ref[...] = tn(branch, att_ref[...]).astype(BF16).reshape(gout_ref.shape)
    go_ref[...] = nn(branch, out_ref[...].reshape(-1, wide)).astype(BF16)
    attend_back(sizes, seqs, proj_ref, probs_ref, go_ref, gproj_ref)
    vec[pl.ds(3, 1), :] = col_sum(gproj_ref[:, pl.ds(0, wide)].astype(F32))
    vec[pl.ds(4, 1), :] = col_sum(gproj_ref[:, pl.ds(2 * wide, wide)].astype(F32))
    grad_ext = nn(gproj_ref[...], qkv_ref[...].reshape(-1, wide))
    gain_sum = jnp.zeros((1, wide), F32)
    bias_sum = jnp.zeros((1, wide), F32)
    for n in range(seqs):
        base = n * sizes.ext
        own = grad_ext[base + sizes.top : base + sizes.top + sizes.rows]
        if sizes.top:
            spread = grad_ext[base : base + sizes.segs] * (1.0 / SEG_LEN)
            own = own + segment_spread(sizes.rows, wide, spread)
        gh_ref[pl.ds(n * sizes.rows, sizes.rows), :] = own
        mem = base + sizes.mem_at
        gmem_ref[pl.ds(n * sizes.segs, sizes.segs), :] = grad_ext[mem : mem + sizes.segs]
        left = base + sizes.left_at
        back_left_ref[n] = grad_ext[left : left + BACK_ROWS].astype(BF16)
        right = base + sizes.right_at
        back_right_ref[n] = grad_ext[right : right + RIGHT_ROWS].astype(BF16)
        if scaled_rows is not None:
            grads = (
                own,
                grad_ext[right : right + RIGHT_ROWS],
                grad_ext[left : left + LEFT_ROWS],
            )
            for rows, scaled in zip(grads, scaled_rows(n)):
                gain_sum = gain_sum + col_sum(rows * scaled)
                bias_sum = bias_sum + col_sum(rows)
    if scaled_rows is not None:
        vec[pl.ds(0, 1), :] = gain_sum
        vec[pl.ds(2, 1), :] = bias_sum
    step = CHIPS_Z // 2
    part = gqkv_ref.shape[1] * gqkv_ref.shape[2] * step
    for c in range(2):
        gqkv_ref[pl.ds(c * step, step)] = (
            tn(gproj_ref[:, pl.ds(c * part, part)], z_ref[...])
            .astype(BF16)
            .reshape((step,) + gqkv_ref.shape[1:])
        )


def merge_halo(sizes, n, gh_ref, gmem_ref, from_right_ref, from_left_ref):
    first = n * sizes.rows
    back = from_right_ref[n].astype(F32)
    head = gh_ref[pl.ds(first, RIGHT_ROWS), :] + from_left_ref[n].astype(F32)
    middle = gh_ref[pl.ds(first + RIGHT_ROWS, sizes.rows - RIGHT_ROWS - LEFT_ROWS), :]
    tail = gh_ref[pl.ds(first + sizes.rows - LEFT_ROWS, LEFT_ROWS), :] + back[:LEFT_ROWS]
    mem = gmem_ref[pl.ds(n * sizes.segs, sizes.segs), :] + back[LEFT_ROWS + sizes.segs :]
    return jnp.concatenate([head, middle, tail], axis=0), mem


def pack_kernel(places, qkv_ref, out_ref, up_ref, down_ref, *packed):
    eye = identity(LANES)
    high, wide, low = qkv_ref.shape[1], out_ref.shape[1], down_ref.shape[1]
    up = up_ref.shape[2]
    for layer, (attn, attn_at, ffn, ffn_at) in enumerate(places):
        ref = packed[attn]
        ref[pl.ds(attn_at, high), :] = qkv_ref[layer]
        ref[pl.ds(attn_at + high, wide), :] = out_ref[layer]
        ref = packed[ffn]
        ref[pl.ds(ffn_at, up), :] = tn(up_ref[layer], eye).astype(BF16)
        for part in range(down_ref.shape[2] // LANES):
            ref[pl.ds(ffn_at + up + part * low, low), :] = down_ref[
                layer, :, pl.ds(part * LANES, LANES)
            ]


def unpack_kernel(places, *refs):
    sources, outs = refs[:-7], refs[-7:]
    qkv_ref, out_ref, up_ref, down_ref, gains_ref, biases_ref, ffn_bias_ref = outs
    eye = identity(LANES)
    high, wide, low = qkv_ref.shape[1], out_ref.shape[1], down_ref.shape[1]
    up = up_ref.shape[2]

    def total(source, first, rows):
        ref = sources[source]
        value = ref[0, pl.ds(first, rows), :].astype(F32)
        for z in range(1, ref.shape[0]):
            value = value + ref[z, pl.ds(first, rows), :].astype(F32)
        return value

    for layer, (attn, attn_at, ffn, ffn_at) in enumerate(places):
        qkv_ref[layer] = total(attn, attn_at, high)
        out_ref[layer] = total(attn, attn_at + high, wide)
        up_ref[layer] = nt(eye, total(ffn, ffn_at, up).astype(BF16))
        for part in range(down_ref.shape[2] // LANES):
            down_ref[layer, :, pl.ds(part * LANES, LANES)] = total(
                ffn, ffn_at + up + part * low, low
            )
    sums = total(places[0][0], high + wide, SMALL_ROWS)
    parts = gains_ref.shape[2] // LANES
    for layer in range(gains_ref.shape[0]):
        for part in range(parts):
            lanes = pl.ds(part * LANES, LANES)
            block = sums[(layer * parts + part) * TILE : (layer * parts + part + 1) * TILE]
            gains_ref[layer, :, lanes] = block[0:2]
            biases_ref[layer, :, lanes] = block[2:8]
            for row in range(ffn_bias_ref.shape[1] // gains_ref.shape[2]):
                at = row * gains_ref.shape[2] + part * LANES
                ffn_bias_ref[pl.ds(layer, 1), pl.ds(at, LANES)] = block[8 + row : 9 + row]


def far_kernel(rows, mine_ref, theirs_ref, came_ref, sent_small, came_small, out_ref):
    total = mine_ref[...].astype(F32) + theirs_ref[...].astype(F32)
    out_ref[pl.ds(0, rows), :] = (total + came_ref[...].astype(F32)).astype(BF16)
    out_ref[pl.ds(rows, SMALL_ROWS), :] = (
        sent_small[...].astype(F32) + came_small[...].astype(F32)
    ).astype(BF16)


def near_small_kernel(
    count, rows, mine_ref, theirs_ref, second_ref, first_ref, sent_small, came_small, out_ref
):
    sums = (sent_small[...].astype(F32) + came_small[...].astype(F32)).astype(BF16)
    for z in range(count):
        group = pl.ds(z * rows, rows)
        total = mine_ref[group, :].astype(F32) + theirs_ref[group, :].astype(F32)
        total = total + second_ref[group, :].astype(F32) + first_ref[group, :].astype(F32)
        out_ref[z, pl.ds(0, rows), :] = total.astype(BF16)
        out_ref[z, pl.ds(rows, SMALL_ROWS), :] = sums


def first_attn_kernel(
    sizes, seqs, mats, by_blocks, count_in, at, place_ref, starts_ref, frames_ref, left_ref,
    right_ref, gains_ref, biases_ref, row_bias_ref, *refs
):
    hbm = refs[:count_in]
    z_ref, proj_ref, probs_ref, att_ref, mixed_ref, mem_ref, qkv_ref, out_ref, mask_ref, sems = (
        refs[count_in:]
    )
    wide = sizes.width
    copies = start_in(
        attn_pairs(mats, by_blocks, hbm, at, qkv_ref, out_ref, place_ref), sems, 0
    )
    gain = gains_ref[0, pl.ds(0, 1), :]
    bias = biases_ref[0, pl.ds(0, 1), :]
    pad = jnp.zeros((TILE - sizes.segs, wide), F32)
    for n in range(seqs):
        own = frames_ref[n].astype(F32)
        before = left_ref[n].astype(F32)
        hidden = norm_forward(own, gain, bias)[0]
        halo = norm_forward(before[before.shape[0] - LEFT_ROWS :], gain, bias)[0]
        after = norm_forward(right_ref[n].astype(F32), gain, bias)[0]
        memory = jnp.concatenate(
            [
                segment_mean(own),
                jnp.zeros((sizes.segs - before.shape[0] // SEG_LEN, wide), F32),
                segment_mean(before),
            ],
            axis=0,
        )
        base = n * sizes.ext
        z_ref[pl.ds(base, sizes.top), :] = jnp.concatenate(
            [segment_mean(hidden), pad], axis=0
        ).astype(BF16)
        z_ref[pl.ds(base + sizes.top, sizes.rows), :] = hidden.astype(BF16)
        z_ref[pl.ds(base + sizes.right_at, RIGHT_ROWS), :] = after.astype(BF16)
        z_ref[pl.ds(base + sizes.left_at, LEFT_ROWS), :] = halo.astype(BF16)
        z_ref[pl.ds(base + sizes.mem_at, MEM_ROWS), :] = memory.astype(BF16)
    fill_mask(sizes, seqs, starts_ref, place_ref, mask_ref)
    wait_all(copies)
    project(sizes, z_ref, qkv_ref, row_bias_ref, proj_ref)
    attend(sizes, seqs, proj_ref, mask_ref, probs_ref, att_ref)
    mixed = nt(att_ref[...], out_ref[...].reshape(-1, wide)) + biases_ref[0, pl.ds(3, 1), :]
    for n in range(seqs):
        base = n * sizes.queries
        mem_ref[pl.ds(n * sizes.segs, sizes.segs), :] = mixed[base : base + sizes.segs]
        mixed_ref[pl.ds(n * sizes.rows, sizes.rows), :] = (
            frames_ref[n].astype(F32) + mixed[base + sizes.top : base + sizes.top + sizes.rows]
        )


def first_ffn_kernel(
    sizes, seqs, mats, by_blocks, count_in, at, place_ref, mixed_ref, mem_ref, gains_ref,
    biases_ref, ffn_bias_ref, *refs
):
    hbm = refs[:count_in]
    (
        next_ref, active_ref, slope_ref, low_ref, send_right_ref, send_left_ref, up_ref, down_ref,
        hidden_ref, sems,
    ) = refs[count_in:]
    copies = start_in(ffn_pairs(mats, by_blocks, hbm, at, up_ref, down_ref, place_ref), sems, 0)
    mixed = mixed_ref[...]
    hidden, _, _ = norm_forward(mixed, gains_ref[0, pl.ds(1, 1), :], biases_ref[0, pl.ds(4, 1), :])
    hidden_ref[...] = hidden.astype(BF16)
    next_ref[...] = mixed + biases_ref[0, pl.ds(5, 1), :]
    wait_all(copies)
    wide = sizes.width

    def body(c, carry):
        at_lane = pl.multiple_of(c * wide, wide)
        upward = nt(hidden_ref[...], up_block(up_ref, c, wide))
        upward = upward + ffn_bias_ref[pl.ds(0, 1), pl.ds(at_lane, wide)]
        active, slope = gelu_both(upward)
        active = active.astype(BF16)
        active_ref[:, pl.ds(at_lane, wide)] = active
        slope_ref[:, pl.ds(at_lane, wide)] = slope.astype(BF16)
        next_ref[...] += nt(active, down_block(down_ref, c, wide))
        return carry

    lax.fori_loop(0, sizes.ff // wide, body, 0)
    low, _, _ = norm_forward(
        next_ref[...], gains_ref[1, pl.ds(0, 1), :], biases_ref[1, pl.ds(0, 1), :]
    )
    low = low.astype(BF16)
    low_ref[...] = low
    for n in range(seqs):
        base = n * sizes.rows
        send_right_ref[n, pl.ds(0, LEFT_ROWS), :] = low[
            base + sizes.rows - LEFT_ROWS : base + sizes.rows
        ]
        send_right_ref[n, pl.ds(LEFT_ROWS, MEM_ROWS), :] = jnp.concatenate(
            [
                mem_ref[pl.ds(n * sizes.segs, sizes.segs), :],
                jnp.zeros((MEM_ROWS - sizes.segs, wide), F32),
            ],
            axis=0,
        ).astype(BF16)
        send_left_ref[n] = low[base : base + RIGHT_ROWS]


def last_layer_kernel(
    sizes, seqs, mats, by_blocks, count_in, attn_at, ffn_at, place_ref, starts_ref, low_ref,
    left_ref, right_ref, mem_ref, inputs_ref, out_grad_ref, gains_ref, biases_ref, ffn_bias_ref,
    row_bias_ref, *refs
):
    hbm = refs[:count_in]
    count_out = 2 if by_blocks else 4
    (encoded_ref, gz_ref, gh_ref, gmem_ref, back_left_ref, back_right_ref, vec) = refs[
        count_in : count_in + 7
    ]
    hbm_out = refs[count_in + 7 : count_in + 7 + count_out]
    (
        qkv_ref, out_ref, up_ref, down_ref, gqkv_ref, gout_ref, gup_ref, gdown_ref, mask_ref,
        z_ref, proj_ref, probs_ref, att_ref, hidden_ref, go_ref, gproj_ref, branch_ref,
        grad_low_ref, grad_hidden_ref, sems,
    ) = refs[count_in + 7 + count_out :]
    attn_hbm, ffn_hbm = (hbm, hbm) if by_blocks else (hbm[:2], hbm[2:])
    attn_out, ffn_out = out_views(by_blocks, hbm_out)
    wide = sizes.width
    attn_copies = start_in(
        attn_pairs(mats, by_blocks, attn_hbm, attn_at, qkv_ref, out_ref, place_ref), sems, 0
    )
    ffn_copies = start_in(
        ffn_pairs(mats, by_blocks, ffn_hbm, ffn_at, up_ref, down_ref, place_ref),
        sems,
        len(attn_copies),
    )
    vec[...] = jnp.zeros_like(vec)
    for n in range(seqs):
        base = n * sizes.ext
        z_ref[pl.ds(base, sizes.rows), :] = low_ref[pl.ds(n * sizes.rows, sizes.rows), :]
        z_ref[pl.ds(base + sizes.right_at, RIGHT_ROWS), :] = right_ref[n]
        z_ref[pl.ds(base + sizes.left_at, LEFT_ROWS), :] = left_ref[n, pl.ds(0, LEFT_ROWS), :]
        memory = jnp.concatenate(
            [
                mem_ref[pl.ds(n * sizes.segs, sizes.segs), :],
                left_ref[n, pl.ds(LEFT_ROWS, MEM_ROWS), :].astype(F32)[: sizes.segs],
            ],
            axis=0,
        )
        z_ref[pl.ds(base + sizes.mem_at, MEM_ROWS), :] = memory.astype(BF16)
        grad_low_ref[pl.ds(n * sizes.rows, sizes.rows), :] = out_grad_ref[n]
    fill_mask(sizes, seqs, starts_ref, place_ref, mask_ref)
    wait_all(attn_copies)
    project(sizes, z_ref, qkv_ref, row_bias_ref, proj_ref)
    attend(sizes, seqs, proj_ref, mask_ref, probs_ref, att_ref)
    mixed = (
        inputs_ref[...]
        + nt(att_ref[...], out_ref[...].reshape(-1, wide))
        + biases_ref[1, pl.ds(3, 1), :]
    )
    gain = gains_ref[1, pl.ds(1, 1), :]
    hidden, scaled, inverse = norm_forward(mixed, gain, biases_ref[1, pl.ds(4, 1), :])
    hidden_ref[...] = hidden.astype(BF16)
    for n in range(seqs):
        encoded_ref[n] = mixed[n * sizes.rows : (n + 1) * sizes.rows] + biases_ref[
            1, pl.ds(5, 1), :
        ]
    grad_hidden_ref[...] = jnp.zeros_like(grad_hidden_ref)
    wait_all(ffn_copies)

    def body(c, carry):
        at_lane = pl.multiple_of(c * wide, wide)
        upward = nt(hidden_ref[...], up_block(up_ref, c, wide))
        upward = upward + ffn_bias_ref[pl.ds(1, 1), pl.ds(at_lane, wide)]
        active, slope = gelu_both(upward)
        active = active.astype(BF16)
        made = nt(active, down_block(down_ref, c, wide))
        for n in range(seqs):
            encoded_ref[n] += made[n * sizes.rows : (n + 1) * sizes.rows]
        grad_hidden_ref[...] += ffn_back_step(
            sizes, c, wide, grad_low_ref[...], hidden_ref[...], active, slope, up_ref, down_ref,
            gup_ref, gdown_ref, vec,
        )
        return carry

    lax.fori_loop(0, sizes.ff // wide, body, 0)
    out_at = len(attn_copies) + len(ffn_copies)
    outs = start_out(
        ffn_pairs(mats, by_blocks, ffn_out, ffn_at, gup_ref, gdown_ref, place_ref), sems, out_at
    )
    grad = grad_low_ref[...].astype(F32)
    grad_hidden = grad_hidden_ref[...]
    vec[pl.ds(1, 1), :] = col_sum(grad_hidden * scaled)
    vec[pl.ds(6, 1), :] = col_sum(grad_hidden)
    vec[pl.ds(7, 1), :] = col_sum(grad)
    gz = grad + norm_backward(grad_hidden, scaled, inverse, gain)
    gz_ref[...] = gz
    attn_back_stage(
        sizes, seqs, gz, None, att_ref, proj_ref, probs_ref, z_ref, qkv_ref, out_ref, gqkv_ref,
        gout_ref, go_ref, gproj_ref, branch_ref, vec, gh_ref, gmem_ref, back_left_ref,
        back_right_ref,
    )
    outs = outs + start_out(
        attn_pairs(mats, by_blocks, attn_out, attn_at, gqkv_ref, gout_ref, place_ref),
        sems,
        out_at + len(outs),
    )
    wait_all(outs)


def first_ffn_back_kernel(
    last, sizes, seqs, mats, by_blocks, count_in, count_out, at_in, place_ref, inputs_ref,
    gz_in_ref, gh_in_ref, gmem_in_ref, from_right_ref, from_left_ref, mixed_ref, active_ref,
    slope_ref, gains_ref, biases_ref, *refs
):
    hbm = refs[:count_in]
    gz_ref, grad_mem_ref, upper_vec, vec = refs[count_in : count_in + 4]
    refs = refs[count_in + 4 :]
    hbm_out = refs[:count_out]
    if by_blocks:
        hbm_out = out_views(by_blocks, hbm_out)[0]
    (
        up_ref, down_ref, gup_ref, gdown_ref, hidden_ref, grad_low_ref, grad_ref, grad_hidden_ref,
        sems,
    ) = refs[count_out:]
    wide = sizes.width
    copies = start_in(
        ffn_pairs(mats, by_blocks, hbm, at_in, up_ref, down_ref, place_ref), sems, 0
    )
    vec[...] = jnp.zeros_like(vec)
    upper_vec[...] = jnp.zeros_like(upper_vec)
    gain = gains_ref[1, pl.ds(0, 1), :]
    gain_sum = jnp.zeros((1, wide), F32)
    bias_sum = jnp.zeros((1, wide), F32)
    for n in range(seqs):
        rows = pl.ds(n * sizes.rows, sizes.rows)
        _, scaled, inverse = norm_forward(
            inputs_ref[rows, :], gain, biases_ref[1, pl.ds(0, 1), :]
        )
        total, mem = merge_halo(last, n, gh_in_ref, gmem_in_ref, from_right_ref, from_left_ref)
        gain_sum = gain_sum + col_sum(total * scaled)
        bias_sum = bias_sum + col_sum(total)
        grad = gz_in_ref[rows, :] + norm_backward(total, scaled, inverse, gain)
        grad_ref[rows, :] = grad
        grad_low_ref[rows, :] = grad.astype(BF16)
        grad_mem_ref[pl.ds(n * sizes.segs, sizes.segs), :] = mem
    upper_vec[pl.ds(0, 1), :] = gain_sum
    upper_vec[pl.ds(2, 1), :] = bias_sum
    gain = gains_ref[0, pl.ds(1, 1), :]
    hidden, scaled, inverse = norm_forward(
        mixed_ref[...], gain, biases_ref[0, pl.ds(4, 1), :]
    )
    hidden_ref[...] = hidden.astype(BF16)
    grad_hidden_ref[...] = jnp.zeros_like(grad_hidden_ref)
    wait_all(copies)

    def body(c, carry):
        at_lane = pl.multiple_of(c * wide, wide)
        grad_hidden_ref[...] += ffn_back_step(
            sizes, c, wide, grad_low_ref[...], hidden_ref[...],
            active_ref[:, pl.ds(at_lane, wide)], slope_ref[:, pl.ds(at_lane, wide)].astype(F32),
            up_ref, down_ref, gup_ref, gdown_ref, vec,
        )
        return carry

    lax.fori_loop(0, sizes.ff // wide, body, 0)
    outs = start_out(
        ffn_pairs(mats, by_blocks, hbm_out, 0, gup_ref, gdown_ref, place_ref), sems, len(copies)
    )
    grad_hidden = grad_hidden_ref[...]
    grad = grad_ref[...]
    vec[pl.ds(1, 1), :] = col_sum(grad_hidden * scaled)
    vec[pl.ds(6, 1), :] = col_sum(grad_hidden)
    vec[pl.ds(7, 1), :] = col_sum(grad)
    gz_ref[...] = grad + norm_backward(grad_hidden, scaled, inverse, gain)
    wait_all(outs)


def first_attn_back_kernel(
    sizes, seqs, mats, by_blocks, count_in, count_out, at_in, place_ref, gz_ref, grad_mem_ref,
    att_ref, probs_ref, proj_ref, z_ref, frames_ref, left_ref, right_ref, gains_ref, biases_ref,
    ffn_vec, last_vec, upper_vec, *refs
):
    hbm = refs[:count_in]
    gh_ref, gmem_ref, back_left_ref, back_right_ref, vec = refs[count_in : count_in + 5]
    refs = refs[count_in + 5 :]
    hbm_out = refs[:count_out]
    small = []
    if by_blocks:
        rows = mats.attn_rows
        blocks = count_in // 2 * CHIPS_Z * rows
        small = [ref.at[pl.ds(blocks, SMALL_ROWS), :] for ref in hbm_out]
        hbm_out = [
            ref.at[pl.ds(0, blocks), :].reshape(count_in // 2, CHIPS_Z, rows, LANES).at[k]
            for ref in hbm_out
            for k in range(count_in // 2)
        ]
    (
        qkv_ref, out_ref, gqkv_ref, gout_ref, go_ref, gproj_ref, branch_ref, small_ref, sems,
    ) = refs[count_out:]
    copies = start_in(
        attn_pairs(mats, by_blocks, hbm, at_in, qkv_ref, out_ref, place_ref), sems, 0
    )
    vec[...] = jnp.zeros_like(vec)
    gain = gains_ref[0, pl.ds(0, 1), :]
    bias = biases_ref[0, pl.ds(0, 1), :]

    def scaled_rows(n):
        before = left_ref[n, pl.ds(left_ref.shape[1] - LEFT_ROWS, LEFT_ROWS), :]
        parts = (frames_ref[n], right_ref[n], before)
        return [norm_forward(part.astype(F32), gain, bias)[1] for part in parts]

    wait_all(copies)
    attn_back_stage(
        sizes, seqs, gz_ref[...], grad_mem_ref, att_ref, proj_ref, probs_ref, z_ref, qkv_ref,
        out_ref, gqkv_ref, gout_ref, go_ref, gproj_ref, branch_ref, vec, gh_ref, gmem_ref,
        back_left_ref, back_right_ref, scaled_rows,
    )
    outs = start_out(
        attn_pairs(mats, by_blocks, hbm_out, 0, gqkv_ref, gout_ref, place_ref), sems, len(copies)
    )
    parts = sizes.width // LANES
    for layer, total in enumerate((vec[...] + ffn_vec[...], last_vec[...] + upper_vec[...])):
        for part in range(parts):
            small_ref[pl.ds((layer * parts + part) * TILE, TILE), :] = total[
                :, part * LANES : (part + 1) * LANES
            ].astype(BF16)
    outs = outs + start_out([(ref, small_ref) for ref in small], sems, len(copies) + len(outs))
    wait_all(outs)


def frames_grad_kernel(
    sizes, seqs, frames_ref, gz_ref, gh_ref, gmem_ref, from_right_ref, from_left_ref, gains_ref,
    biases_ref, grad_ref
):
    gain = gains_ref[0, pl.ds(0, 1), :]
    for n in range(seqs):
        _, scaled, inverse = norm_forward(
            frames_ref[n].astype(F32), gain, biases_ref[0, pl.ds(0, 1), :]
        )
        total, mem = merge_halo(sizes, n, gh_ref, gmem_ref, from_right_ref, from_left_ref)
        grad_ref[n] = (
            gz_ref[pl.ds(n * sizes.rows, sizes.rows), :]
            + norm_backward(total, scaled, inverse, gain)
            + segment_spread(sizes.rows, sizes.width, mem * (1.0 / SEG_LEN))
        )


def shifted(value, axis, by):
    size = lax.axis_size(axis)
    pairs = [(i, i + by) for i in range(size) if 0 <= i + by < size]
    return lax.ppermute(value, axis, pairs)


def permuted(value, move):
    reps = lax.axis_size("rep")
    pairs = []
    for flat in range(lax.axis_size("seg") * reps):
        seg, rep = divmod(flat, reps)
        z, y, x, core = move(seg // CHIPS_Y, seg % CHIPS_Y, rep // 2, rep % 2)
        pairs.append((flat, (z * CHIPS_Y + y) * reps + 2 * x + core))
    return lax.ppermute(value, ("seg", "rep"), pairs)


def across_first(value):
    return permuted(value, lambda z, y, x, c: (z, y, x ^ 1, c) if c == 0 else (z, y ^ 1, x, c))


def across_second(value):
    return permuted(value, lambda z, y, x, c: (z, y ^ 1, x, c) if c == 0 else (z, y, x ^ 1, c))


def other_core(value):
    return permuted(value, lambda z, y, x, c: (z, y, x, c ^ 1))


def after(value, *others):
    return lax.optimization_barrier((value,) + others)[0]


def swap_z(blocks):
    groups = [
        [z * CHIPS_Y + y for z in range(CHIPS_Z)] for y in range(CHIPS_Y)
    ]
    return lax.all_to_all(blocks, "seg", 0, 0, axis_index_groups=groups, tiled=True)


def gather_z(shard):
    return swap_z(jnp.broadcast_to(shard[None], (CHIPS_Z,) + shard.shape))


def gather_sides(here):
    return [here, across_first(here), across_second(here)]


def both_cores(blocks):
    return blocks + [other_core(block) for block in blocks]


def summed(*parts):
    total = parts[0].astype(F32)
    for part in parts[1:]:
        total = total + part.astype(F32)
    return total.astype(BF16)


def row_block(rows, at):
    return pl.BlockSpec((rows, LANES), lambda i: (at, 0))


def sum_everywhere(value):
    count = lax.axis_size("seg") * lax.axis_size("rep")
    bit = 1
    while bit < count:
        value = value + lax.ppermute(value, ("seg", "rep"), [(i, i ^ bit) for i in range(count)])
        bit *= 2
    return value


def vmem_spec():
    return pl.BlockSpec(memory_space=pltpu.VMEM)


def smem_spec():
    return pl.BlockSpec(memory_space=pltpu.SMEM)


def hbm_spec():
    return pl.BlockSpec(memory_space=pl.ANY)


def call(body, in_specs, out_shapes, out_specs, scratch, args, flops=0, moved=0, grid=()):
    return pl.pallas_call(
        body,
        grid=grid,
        in_specs=in_specs,
        out_shape=tuple(jax.ShapeDtypeStruct(shape, kind) for shape, kind in out_shapes),
        out_specs=tuple(out_specs),
        scratch_shapes=scratch,
        compiler_params=pltpu.CompilerParams(vmem_limit_bytes=VMEM_BYTES),
        cost_estimate=pl.CostEstimate(flops=flops, bytes_accessed=moved, transcendentals=0),
    )(*args)


def on_device(
    frames,
    utt_segments,
    out_grad,
    qkv_weight,
    out_weight,
    ffn_in_weight,
    ffn_out_weight,
    norm_gains,
    biases,
    ffn_bias,
):
    micros, groups, rows, width = frames.shape
    seqs = micros * groups
    ff = ffn_bias.shape[1]
    reps = lax.axis_size("rep")
    seg_count = lax.axis_size("seg")
    mats = Matrices(width, ff)
    by_blocks = width // reps == LANES and reps == 4 and seg_count == BLOCKS
    first = Sizes(rows, width, ff, True)
    last = Sizes(rows, width, ff, False)
    own = seqs * rows
    mem_own = seqs * first.segs

    seg_at = lax.axis_index("seg")
    seg_base = seg_at * first.segs
    rep_at = lax.axis_index("rep")
    place = [seg_base, jnp.int32(first.segs * seg_count)]
    y_at, x_at, core_at = seg_at % CHIPS_Y, rep_at // 2, rep_at % 2
    for other in range(2):
        core = lax.bitwise_xor(core_at, other)
        for hop2 in range(2):
            for hop1 in range(2):
                x_hop = jnp.where(core == 0, hop1, hop2)
                y_hop = jnp.where(core == 0, hop2, hop1)
                place.append(lax.bitwise_xor(y_at, y_hop))
                place.append((lax.bitwise_xor(x_at, x_hop) * 2 + core) * LANES)
    place = jnp.stack([jnp.asarray(entry, jnp.int32) for entry in place])
    lengths = utt_segments.reshape(seqs, utt_segments.shape[2])
    starts = (jnp.cumsum(lengths, axis=1) - lengths).astype(jnp.int32)
    zero_bias = jnp.zeros((width,), F32)
    row_bias = jnp.stack(
        [jnp.concatenate([biases[l, 1], zero_bias, biases[l, 2]]) for l in range(LAYERS)]
    ).reshape(LAYERS, 1, 3 * width)

    frames_own = frames.reshape(seqs, rows, width)
    grads_own = out_grad.reshape(seqs, rows, width)
    far = MEM_LEN * SEG_LEN
    frames_left = shifted(frames_own[:, rows - far :], "seg", 1)
    frames_right = shifted(frames_own[:, :RIGHT_ROWS], "seg", -1)

    attn_rows, ffn_rows = mats.attn_rows, mats.ffn_rows
    if by_blocks:
        qkv_t, out_t, down_t = (
            jnp.swapaxes(member, 1, 2) for member in (qkv_weight, out_weight, ffn_out_weight)
        )
        places = [(0, 0, 1, 0), (2, 0, 2, attn_rows)]
        chunk_rows = [attn_rows, ffn_rows, attn_rows + ffn_rows]
        shards = call(
            lambda *refs: pack_kernel(places, *refs),
            [vmem_spec()] * 4,
            [((high, LANES), BF16) for high in chunk_rows],
            [vmem_spec()] * len(chunk_rows),
            [],
            (qkv_t, out_t, ffn_in_weight, down_t),
        )
        sides0 = gather_sides(gather_z(shards[0]))
        sides1 = gather_sides(gather_z(after(shards[1], sides0[0])))
        first_attn = both_cores(sides0 + [across_second(sides0[1])])
        first_at = 0, 0
        last_at = 0, attn_rows
        half = len(first_attn) // 2
        grad_outs = [
            [((half, CHIPS_Z, high, LANES), BF16)] * 2 for high in chunk_rows
        ]
        flat_rows = half * CHIPS_Z * attn_rows
        grad_outs[0] = [((flat_rows + SMALL_ROWS, LANES), BF16)] * 2
        copies_in = len(first_attn) * (3 + mats.down_parts)
    else:
        whole = []
        for member, shape in zip(
            (qkv_weight, out_weight, ffn_in_weight, ffn_out_weight),
            (mats.qkv, mats.out, mats.up, mats.down),
        ):
            member = lax.all_gather(member, "rep", axis=1, tiled=True)
            member = lax.all_gather(member, "seg", axis=2, tiled=True)
            whole.append(jnp.swapaxes(member, 1, 2).reshape((LAYERS,) + shape))
        first_attn = [whole[0][0], whole[1][0]]
        first_ffn = [whole[2][0], whole[3][0]]
        last_all = [member[1] for member in whole]
        first_at = last_at = 0, 0
        shapes = [(shape, BF16) for shape in (mats.qkv, mats.out, mats.up, mats.down)]
        grad_outs = [shapes[:2], shapes[2:], shapes]
        copies_in = 4
    dma = pltpu.SemaphoreType.DMA

    z0, proj0, probs0, att0, mixed0, mem1 = call(
        lambda *refs: first_attn_kernel(
            first, seqs, mats, by_blocks, len(first_attn), first_at[0], *refs
        ),
        [smem_spec()] * 2 + [vmem_spec()] * 6 + [hbm_spec()] * len(first_attn),
        [
            ((seqs * first.ext, width), BF16),
            ((seqs * first.ext, 3 * width), BF16),
            ((seqs * first.pairs, 2 * first.queries, first.keys), F32),
            ((seqs * first.queries, width), BF16),
            ((own, width), F32),
            ((mem_own, width), F32),
        ],
        [vmem_spec()] * 6,
        [
            pltpu.VMEM(mats.qkv, BF16),
            pltpu.VMEM(mats.out, BF16),
            pltpu.VMEM((seqs, first.queries, first.keys), F32),
            dma((copies_in,)),
        ],
        (place, starts, frames_own, frames_left, frames_right, norm_gains, biases, row_bias[0])
        + tuple(first_attn),
        flops=40 * own * 4 * width * width,
        moved=8 * width * width,
    )
    if by_blocks:
        sides2 = gather_sides(gather_z(after(shards[2], sides1[0])))
        first_ffn = both_cores(sides1 + [across_second(after(sides1[1], mixed0))])
    x1, active0, slope0, low1, send_right, send_left = call(
        lambda *refs: first_ffn_kernel(first, seqs, mats, by_blocks, len(first_ffn), first_at[1], *refs),
        [smem_spec()] + [vmem_spec()] * 5 + [hbm_spec()] * len(first_ffn),
        [
            ((own, width), F32),
            ((own, ff), BF16),
            ((own, ff), BF16),
            ((own, width), BF16),
            ((seqs, BACK_ROWS, width), BF16),
            ((seqs, RIGHT_ROWS, width), BF16),
        ],
        [vmem_spec()] * 6,
        [
            pltpu.VMEM(mats.up, BF16),
            pltpu.VMEM(mats.down, BF16),
            pltpu.VMEM((own, width), BF16),
            dma((copies_in,)),
        ],
        (place, mixed0, mem1, norm_gains, biases, ffn_bias) + tuple(first_ffn),
        flops=16 * own * 2 * width * ff,
        moved=4 * width * ff,
    )
    left1 = shifted(send_right, "seg", 1)
    right1 = shifted(send_left, "seg", -1)
    if by_blocks:
        last_all = both_cores(sides2 + [across_second(after(sides2[1], sides2[2], left1, right1))])

    vec_shape = (TILE, width)
    outs = call(
        lambda *refs: last_layer_kernel(
            last, seqs, mats, by_blocks, len(last_all), *last_at, *refs
        ),
        [smem_spec()] * 2 + [vmem_spec()] * 10 + [hbm_spec()] * len(last_all),
        [
            ((seqs, rows, width), F32),
            ((own, width), F32),
            ((own, width), F32),
            ((mem_own, width), F32),
            ((seqs, BACK_ROWS, width), BF16),
            ((seqs, RIGHT_ROWS, width), BF16),
            (vec_shape, F32),
        ]
        + grad_outs[2],
        [vmem_spec()] * 7 + [hbm_spec()] * len(grad_outs[2]),
        [
            pltpu.VMEM(mats.qkv, BF16),
            pltpu.VMEM(mats.out, BF16),
            pltpu.VMEM(mats.up, BF16),
            pltpu.VMEM(mats.down, BF16),
            pltpu.VMEM(mats.qkv, BF16),
            pltpu.VMEM(mats.out, BF16),
            pltpu.VMEM(mats.up, BF16),
            pltpu.VMEM(mats.down, BF16),
            pltpu.VMEM((seqs, last.queries, last.keys), F32),
            pltpu.VMEM((seqs * last.ext, width), BF16),
            pltpu.VMEM((seqs * last.ext, 3 * width), BF16),
            pltpu.VMEM((seqs * last.pairs, 2 * last.queries, last.keys), F32),
            pltpu.VMEM((seqs * last.queries, width), BF16),
            pltpu.VMEM((own, width), BF16),
            pltpu.VMEM((seqs * last.queries, width), BF16),
            pltpu.VMEM((seqs * last.ext, 3 * width), BF16),
            pltpu.VMEM((seqs * last.queries, width), BF16),
            pltpu.VMEM((own, width), BF16),
            pltpu.VMEM((own, width), F32),
            dma((2 * copies_in,)),
        ],
        (place, starts, low1, left1, right1, mem1, x1, grads_own, norm_gains, biases, ffn_bias,
         row_bias[1]) + tuple(last_all),
        flops=30 * own * (4 * width * width + 2 * width * ff),
        moved=4 * (4 * width * width + 2 * width * ff),
    )
    encoded, gz1, gh1, gmem1, back_left1, back_right1, vec1 = outs[:7]
    grad_blocks1 = outs[7:]
    from_right1 = shifted(back_left1, "seg", -1)
    from_left1 = shifted(back_right1, "seg", 1)

    gh1_tied = gh1
    if by_blocks:
        mine1, theirs1 = grad_blocks1[0], other_core(grad_blocks1[1])
        far1 = after(summed(mine1[2:], theirs1[2:]), from_right1, from_left1)
        gh1_tied = after(gh1, far1)
    gz0, grad_mem, upper_vec, vec0_ffn, *grad_ffn0 = call(
        lambda *refs: first_ffn_back_kernel(
            last, first, seqs, mats, by_blocks, len(first_ffn), len(grad_outs[1]), first_at[1],
            *refs
        ),
        [smem_spec()] + [vmem_spec()] * 11 + [hbm_spec()] * len(first_ffn),
        [
            ((own, width), F32),
            ((mem_own, width), F32),
            (vec_shape, F32),
            (vec_shape, F32),
        ]
        + grad_outs[1],
        [vmem_spec()] * 4 + [hbm_spec()] * len(grad_outs[1]),
        [
            pltpu.VMEM(mats.up, BF16),
            pltpu.VMEM(mats.down, BF16),
            pltpu.VMEM(mats.up, BF16),
            pltpu.VMEM(mats.down, BF16),
            pltpu.VMEM((own, width), BF16),
            pltpu.VMEM((own, width), BF16),
            pltpu.VMEM((own, width), F32),
            pltpu.VMEM((own, width), F32),
            dma((2 * copies_in,)),
        ],
        (place, x1, gz1, gh1_tied, gmem1, from_right1, from_left1, mixed0, active0, slope0, norm_gains,
         biases) + tuple(first_ffn),
        flops=28 * own * 2 * width * ff,
        moved=8 * width * ff,
    )
    gz0_tied = gz0
    if by_blocks:
        second1 = across_second(far1)
        near1 = summed(mine1[1], theirs1[1], second1[1])
        mine_ffn, theirs_ffn = grad_ffn0[0], other_core(after(grad_ffn0[1], second1))
        far_ffn = summed(mine_ffn[2:], theirs_ffn[2:])
        gz0_tied = after(gz0, near1, far_ffn)
    gh0, gmem0, back_left0, back_right0, vec0_attn, *grad_attn0 = call(
        lambda *refs: first_attn_back_kernel(
            first, seqs, mats, by_blocks, len(first_attn), len(grad_outs[0]), first_at[0], *refs
        ),
        [smem_spec()] + [vmem_spec()] * 14 + [hbm_spec()] * len(first_attn),
        [
            ((own, width), F32),
            ((mem_own, width), F32),
            ((seqs, BACK_ROWS, width), BF16),
            ((seqs, RIGHT_ROWS, width), BF16),
            (vec_shape, F32),
        ]
        + grad_outs[0],
        [vmem_spec()] * 5 + [hbm_spec()] * len(grad_outs[0]),
        [
            pltpu.VMEM(mats.qkv, BF16),
            pltpu.VMEM(mats.out, BF16),
            pltpu.VMEM(mats.qkv, BF16),
            pltpu.VMEM(mats.out, BF16),
            pltpu.VMEM((seqs * first.queries, width), BF16),
            pltpu.VMEM((seqs * first.ext, 3 * width), BF16),
            pltpu.VMEM((seqs * first.queries, width), BF16),
            pltpu.VMEM((SMALL_ROWS, LANES), BF16),
            dma((2 * copies_in,)),
        ],
        (place, gz0_tied, grad_mem, att0, probs0, proj0, z0, frames_own, frames_left, frames_right,
         norm_gains, biases, vec0_ffn, vec1, upper_vec) + tuple(first_attn),
        flops=56 * own * 4 * width * width,
        moved=16 * width * width,
    )
    from_right0 = shifted(back_left0, "seg", -1)
    from_left0 = shifted(back_right0, "seg", 1)
    gz0_last = gz0
    if by_blocks:
        first1 = across_first(near1)
        total1 = summed(mine1[0], theirs1[0], second1[0], after(first1, gh0))
        last_parts = swap_z(total1)
        gz0_last = after(gz0, last_parts)
    frames_grad = call(
        lambda *refs: frames_grad_kernel(first, seqs, *refs),
        [vmem_spec()] * 8,
        [((seqs, rows, width), F32)],
        [vmem_spec()],
        [],
        (frames_own, gz0_last, gh0, gmem0, from_right0, from_left0, norm_gains, biases),
    )[0]

    if by_blocks:
        second_ffn = across_second(far_ffn)
        mine_attn = grad_attn0[0]
        theirs_attn = other_core(after(grad_attn0[1], total1, second_ffn))
        near_ffn = summed(mine_ffn[1], theirs_ffn[1], second_ffn[1])
        first_ffn_sum = across_first(near_ffn)
        ffn_parts = swap_z(summed(mine_ffn[0], theirs_ffn[0], second_ffn[0], first_ffn_sum))
        rows2, rows1 = flat_rows // 2, flat_rows // 4
        far_attn = after(summed(mine_attn[rows2:], theirs_attn[rows2:]), second_ffn)
        second_attn = across_second(far_attn)
        second_tied = after(second_attn, frames_grad)
        near_attn = call(
            lambda *refs: far_kernel(rows1, *refs),
            [row_block(rows1, 1)] * 3 + [row_block(SMALL_ROWS, rows2 // SMALL_ROWS)] * 2,
            [((rows1 + SMALL_ROWS, LANES), BF16)],
            [vmem_spec()],
            [],
            [mine_attn, theirs_attn, second_tied, far_attn, second_tied],
            grid=(1,),
        )[0]
        first_attn_sum = across_first(near_attn)
        attn_parts = swap_z(
            call(
                lambda *refs: near_small_kernel(CHIPS_Z, attn_rows, *refs),
                [row_block(rows1, 0)] * 4 + [row_block(SMALL_ROWS, rows1 // SMALL_ROWS)] * 2,
                [((CHIPS_Z, attn_rows + SMALL_ROWS, LANES), BF16)],
                [vmem_spec()],
                [],
                [mine_attn, theirs_attn, second_attn, first_attn_sum, near_attn, first_attn_sum],
                grid=(1,),
            )[0]
        )
        shapes = [member.shape for member in (qkv_t, out_t, ffn_in_weight, down_t)]
        shapes += [member.shape for member in (norm_gains, biases, ffn_bias)]
        reduced = call(
            lambda *refs: unpack_kernel(places, *refs),
            [vmem_spec()] * 3,
            [(shape, F32) for shape in shapes],
            [vmem_spec()] * len(shapes),
            [],
            [attn_parts, ffn_parts, last_parts],
        )
        small = reduced[4:]
        reduced = [
            jnp.swapaxes(reduced[0], 1, 2),
            jnp.swapaxes(reduced[1], 1, 2),
            reduced[2],
            jnp.swapaxes(reduced[3], 1, 2),
        ]
    else:
        reduced = []
        for member0, member1 in zip(grad_attn0 + grad_ffn0, grad_blocks1):
            both = jnp.stack([member0, member1]).reshape(LAYERS, -1, member0.shape[3])
            both = jnp.swapaxes(both, 1, 2)
            both = lax.psum_scatter(both, "seg", scatter_dimension=2, tiled=True)
            both = lax.psum_scatter(both, "rep", scatter_dimension=1, tiled=True)
            reduced.append(both.astype(F32))
        small = sum_everywhere(jnp.stack([vec0_ffn + vec0_attn, vec1 + upper_vec]))
        small = small[:, 0:2], small[:, 2:8], small[:, 8:12].reshape(ffn_bias.shape)

    return (
        encoded.reshape(frames.shape),
        frames_grad.reshape(frames.shape),
        reduced[0],
        reduced[1],
        reduced[2],
        reduced[3],
        small[0],
        small[1],
        small[2],
    )


def solution(mesh):
    in_specs = (
        P(None, "rep", "seg", None),
        P(None, "rep", None),
        P(None, "rep", "seg", None),
        P(None, "rep", "seg"),
        P(None, "rep", "seg"),
        P(None, "rep", "seg"),
        P(None, "rep", "seg"),
        P(),
        P(),
        P(),
    )
    out_specs = (
        P(None, "rep", "seg", None),
        P(None, "rep", "seg", None),
        P(None, "rep", "seg"),
        P(None, "rep", "seg"),
        P(None, "rep", "seg"),
        P(None, "rep", "seg"),
        P(),
        P(),
        P(),
    )
    return jax.shard_map(
        on_device, mesh=mesh, in_specs=in_specs, out_specs=out_specs, check_vma=False
    )
```

```python
import jax
import jax.numpy as jnp
from jax import lax
from jax.experimental import pallas as pl
from jax.experimental.pallas import tpu as pltpu
from jax.sharding import PartitionSpec as P

HEADS = 8
SEG_LEN = 16
LEFT_LEN = 30
RIGHT_LEN = 4
MEM_LEN = 4
LAYERS = 2

EPS = 1e-05
ROOT_HALF = 0.7071067811865476
INV_ROOT_TWO_PI = 0.3989422804014327

LANES = 128
TILE = 16
RIGHT_ROWS = 16
LEFT_ROWS = 32
MEM_ROWS = 16
BACK_ROWS = LEFT_ROWS + MEM_ROWS
CHIPS_Z = 4
CHIPS_Y = 2
BLOCKS = CHIPS_Z * CHIPS_Y
SMALL_ROWS = 128
VMEM_BYTES = 56 * 1024 * 1024

BF16 = jnp.bfloat16
F32 = jnp.float32


def nn(a, b):
    return lax.dot_general(a, b, (((1,), (0,)), ((), ())), preferred_element_type=F32)


def nt(a, b):
    return lax.dot_general(a, b, (((1,), (1,)), ((), ())), preferred_element_type=F32)


def tn(a, b):
    return lax.dot_general(a, b, (((0,), (0,)), ((), ())), preferred_element_type=F32)


def col_sum(value):
    return jnp.sum(value, axis=0, keepdims=True)


def norm_forward(inputs, gain, bias):
    center = inputs - jnp.mean(inputs, axis=1, keepdims=True)
    inverse = lax.rsqrt(jnp.mean(center * center, axis=1, keepdims=True) + EPS)
    scaled = center * inverse
    return scaled * gain + bias, scaled, inverse


def norm_backward(grad_in, scaled, inverse, gain):
    grad_scaled = grad_in * gain
    return inverse * (
        grad_scaled
        - jnp.mean(grad_scaled, axis=1, keepdims=True)
        - scaled * jnp.mean(grad_scaled * scaled, axis=1, keepdims=True)
    )


def segment_mean(inputs):
    rows, width = inputs.shape
    return jnp.mean(inputs.reshape(rows // SEG_LEN, SEG_LEN, width), axis=1)


def segment_spread(rows, width, per_segment):
    segs = rows // SEG_LEN
    return jnp.broadcast_to(per_segment[:, None, :], (segs, SEG_LEN, width)).reshape(rows, width)


def identity(size):
    row = lax.broadcasted_iota(jnp.int32, (size, size), 0)
    col = lax.broadcasted_iota(jnp.int32, (size, size), 1)
    return (row == col).astype(F32).astype(BF16)


class Sizes:
    def __init__(self, rows, width, ff, with_summary):
        self.rows = rows
        self.width = width
        self.ff = ff
        self.segs = rows // SEG_LEN
        self.top = TILE if with_summary else 0
        self.keys = rows + RIGHT_ROWS + LEFT_ROWS + MEM_ROWS
        self.ext = self.top + self.keys
        self.queries = self.top + rows
        self.right_at = self.top + rows
        self.left_at = self.right_at + RIGHT_ROWS
        self.mem_at = self.left_at + LEFT_ROWS
        self.pairs = width // LANES


class Matrices:
    def __init__(self, width, ff):
        self.qkv = (CHIPS_Z, CHIPS_Y, 3 * width // BLOCKS, width)
        self.out = (CHIPS_Z, CHIPS_Y, width // BLOCKS, width)
        self.up = (CHIPS_Z, CHIPS_Y, ff // BLOCKS, width)
        self.down = (CHIPS_Z, CHIPS_Y, width // BLOCKS, ff)
        self.down_parts = ff // width
        self.attn_rows = self.qkv[2] + self.out[2]
        self.ffn_rows = self.up[2] + self.down_parts * self.down[2]


def attn_pairs(mats, by_blocks, hbm, first, qkv_ref, out_ref, place_ref):
    if not by_blocks:
        return [(hbm[0], qkv_ref), (hbm[1], out_ref)]
    pairs = []
    high = mats.qkv[2]
    for k, block in enumerate(hbm):
        row = place_ref[2 + 2 * k]
        lane = pl.multiple_of(place_ref[3 + 2 * k], LANES)
        pairs.append(
            (block.at[:, pl.ds(first, high), :], qkv_ref.at[:, row, :, pl.ds(lane, LANES)])
        )
        pairs.append(
            (
                block.at[:, pl.ds(first + high, mats.out[2]), :],
                out_ref.at[:, row, :, pl.ds(lane, LANES)],
            )
        )
    return pairs


def ffn_pairs(mats, by_blocks, hbm, first, up_ref, down_ref, place_ref):
    if not by_blocks:
        return [(hbm[0], up_ref), (hbm[1], down_ref)]
    pairs = []
    high = mats.up[2]
    low = mats.down[2]
    for k, block in enumerate(hbm):
        row = place_ref[2 + 2 * k]
        lane = pl.multiple_of(place_ref[3 + 2 * k], LANES)
        pairs.append(
            (block.at[:, pl.ds(first, high), :], up_ref.at[:, row, :, pl.ds(lane, LANES)])
        )
        for part in range(mats.down_parts):
            there = pl.multiple_of(
                place_ref[3 + 2 * k] * mats.down_parts + part * LANES, LANES
            )
            pairs.append(
                (
                    block.at[:, pl.ds(first + high + part * low, low), :],
                    down_ref.at[:, row, :, pl.ds(there, LANES)],
                )
            )
    return pairs


def start_in(pairs, sems, at):
    copies = [pltpu.make_async_copy(s, d, sems.at[at + i]) for i, (s, d) in enumerate(pairs)]
    for copy in copies:
        copy.start()
    return copies


def start_out(pairs, sems, at):
    copies = [pltpu.make_async_copy(d, s, sems.at[at + i]) for i, (s, d) in enumerate(pairs)]
    for copy in copies:
        copy.start()
    return copies


def out_views(by_blocks, hbm):
    if not by_blocks:
        return hbm[:2], hbm[2:]
    views = [ref.at[k] for ref in hbm for k in range(ref.shape[0])]
    return views, views


def wait_all(copies):
    for copy in copies:
        copy.wait()


def fill_mask(sizes, seqs, starts_ref, place_ref, mask_ref):
    shape = (sizes.queries, sizes.keys)
    row = lax.broadcasted_iota(jnp.int32, shape, 0)
    col = lax.broadcasted_iota(jnp.int32, shape, 1)
    base = place_ref[0]
    total = place_ref[1]
    query = jnp.where(row < sizes.top, row, lax.shift_right_arithmetic(row - sizes.top, 4))
    left_at = sizes.rows + RIGHT_ROWS
    mem_at = left_at + LEFT_ROWS
    spot = jnp.where(col < left_at, col, col - mem_at)
    mem_seg = jnp.where(col < mem_at + sizes.segs, col - mem_at, col - mem_at - 2 * sizes.segs)
    key_seg = jnp.where(col < mem_at, lax.shift_right_arithmetic(spot, 4), mem_seg)
    near = (
        (key_seg == query)
        | ((spot >= query * SEG_LEN - LEFT_LEN) & (spot < query * SEG_LEN))
        | ((key_seg == query + 1) & (spot < query * SEG_LEN + SEG_LEN + RIGHT_LEN))
    )
    recent = (key_seg >= query - MEM_LEN) & (key_seg < query) & (row >= sizes.top)
    allowed = ((col < mem_at) & near) | ((col >= mem_at) & recent)
    key_abs = key_seg + base
    query_abs = query + base
    allowed = allowed & (key_abs >= 0) & (key_abs < total)
    if sizes.top:
        allowed = allowed & ((row < sizes.segs) | (row >= sizes.top))
    for n in range(seqs):
        key_owner = jnp.zeros(shape, jnp.int32)
        query_owner = jnp.zeros(shape, jnp.int32)
        for u in range(starts_ref.shape[1]):
            first = starts_ref[n, u]
            key_owner = key_owner + (key_abs >= first).astype(jnp.int32)
            query_owner = query_owner + (query_abs >= first).astype(jnp.int32)
        mask_ref[n] = jnp.where(allowed & (key_owner == query_owner), 0.0, -1e30)


def half_masks():
    lane = lax.broadcasted_iota(jnp.int32, (1, LANES), 1)
    even = (lane < LANES // 2).astype(F32)
    return even.astype(BF16), (1.0 - even).astype(BF16), lane < LANES // 2


def project(sizes, z_ref, qkv_ref, row_bias_ref, proj_ref):
    step = CHIPS_Z // 2
    for c in range(2):
        block = qkv_ref[pl.ds(c * step, step)].reshape(-1, sizes.width)
        wide = block.shape[0]
        made = nt(z_ref[...], block) + row_bias_ref[:, pl.ds(c * wide, wide)]
        proj_ref[:, pl.ds(c * wide, wide)] = made.astype(BF16)


def attend(sizes, seqs, proj_ref, mask_ref, probs_ref, att_ref):
    even, odd, is_even = half_masks()
    scale = (sizes.width // HEADS) ** (-0.5)
    count = sizes.queries

    def body(p, carry):
        for n in range(seqs):
            lane = pl.multiple_of(p * LANES, LANES)
            query = proj_ref[pl.ds(n * sizes.ext, count), pl.ds(lane, LANES)]
            first = n * sizes.ext + sizes.top
            key = proj_ref[pl.ds(first, sizes.keys), pl.ds(sizes.width + lane, LANES)]
            value = proj_ref[pl.ds(first, sizes.keys), pl.ds(2 * sizes.width + lane, LANES)]
            scores = nt(jnp.concatenate([query * even, query * odd], axis=0), key) * scale
            outs = []
            for half in range(2):
                part = scores[half * count : (half + 1) * count] + mask_ref[n]
                part = jnp.exp(part - jnp.max(part, axis=1, keepdims=True))
                part = (part * (1.0 / jnp.sum(part, axis=1, keepdims=True))).astype(BF16)
                probs_ref[n * sizes.pairs + p, pl.ds(half * count, count), :] = part
                outs.append(nn(part, value))
            att_ref[pl.ds(n * count, count), pl.ds(lane, LANES)] = jnp.where(
                is_even, outs[0], outs[1]
            ).astype(BF16)
        return carry

    lax.fori_loop(0, sizes.pairs, body, 0)


def attend_back(sizes, seqs, proj_ref, probs_ref, go_ref, gproj_ref):
    even, odd, is_even = half_masks()
    scale = (sizes.width // HEADS) ** (-0.5)
    count = sizes.queries
    wide = sizes.width
    for n in range(seqs):
        base = n * sizes.ext
        rest = sizes.ext - count
        gproj_ref[pl.ds(base + count, rest), pl.ds(0, wide)] = jnp.zeros((rest, wide), BF16)
        if sizes.top:
            gproj_ref[pl.ds(base, sizes.top), pl.ds(wide, 2 * wide)] = jnp.zeros(
                (sizes.top, 2 * wide), BF16
            )

    def body(p, carry):
        for n in range(seqs):
            lane = pl.multiple_of(p * LANES, LANES)
            base = n * sizes.ext
            first = base + sizes.top
            query = proj_ref[pl.ds(base, count), pl.ds(lane, LANES)]
            key = proj_ref[pl.ds(first, sizes.keys), pl.ds(wide + lane, LANES)]
            value = proj_ref[pl.ds(first, sizes.keys), pl.ds(2 * wide + lane, LANES)]
            grad = go_ref[pl.ds(n * count, count), pl.ds(lane, LANES)]
            queries = jnp.concatenate([query * even, query * odd], axis=0)
            grads = jnp.concatenate([grad * even, grad * odd], axis=0)
            probs_low = probs_ref[n * sizes.pairs + p]
            grad_values = tn(probs_low, grads)
            probs = probs_low.astype(F32)
            grad_probs = nt(grads, value)
            weighted = grad_probs * probs
            grad_scores = (
                (weighted - probs * jnp.sum(weighted, axis=1, keepdims=True)) * scale
            ).astype(BF16)
            grad_keys = tn(grad_scores, queries)
            grad_query = jnp.where(
                is_even, nn(grad_scores[:count], key), nn(grad_scores[count:], key)
            )
            gproj_ref[pl.ds(base, count), pl.ds(lane, LANES)] = grad_query.astype(BF16)
            gproj_ref[pl.ds(first, sizes.keys), pl.ds(wide + lane, LANES)] = grad_keys.astype(BF16)
            gproj_ref[pl.ds(first, sizes.keys), pl.ds(2 * wide + lane, LANES)] = (
                grad_values.astype(BF16)
            )
        return carry

    lax.fori_loop(0, sizes.pairs, body, 0)


def gelu_both(upward):
    half = 0.5 * (1.0 + lax.erf(upward * ROOT_HALF))
    slope = half + upward * jnp.exp(-0.5 * upward * upward) * INV_ROOT_TWO_PI
    return upward * half, slope


def up_block(up_ref, c, wide):
    step = wide // (up_ref.shape[1] * up_ref.shape[2])
    return up_ref[pl.ds(c * step, step)].reshape(-1, up_ref.shape[3])


def down_block(down_ref, c, wide):
    at = pl.multiple_of(c * wide, wide)
    return down_ref[:, :, :, pl.ds(at, wide)].reshape(-1, wide)


def ffn_back_step(
    sizes, c, wide, grad_low, hidden_low, active, slope, up_ref, down_ref, gup_ref, gdown_ref, vec
):
    at = pl.multiple_of(c * wide, wide)
    up = up_block(up_ref, c, wide)
    down = down_block(down_ref, c, wide)
    grad_active = nn(grad_low, down)
    grad_up_f = grad_active * slope
    grad_up = grad_up_f.astype(BF16)
    gdown_ref[:, :, :, pl.ds(at, wide)] = (
        tn(grad_low, active).astype(BF16).reshape(gdown_ref.shape[:3] + (wide,))
    )
    step = wide // (gup_ref.shape[1] * gup_ref.shape[2])
    gup_ref[pl.ds(c * step, step)] = (
        tn(grad_up, hidden_low).astype(BF16).reshape((step,) + gup_ref.shape[1:])
    )
    vec[pl.ds(8 + c, 1), :] = col_sum(grad_up.astype(F32))
    return nn(grad_up, up)


def attn_back_stage(
    sizes, seqs, gz, grad_mem_ref, att_ref, proj_ref, probs_ref, z_ref, qkv_ref, out_ref,
    gqkv_ref, gout_ref, go_ref, gproj_ref, branch_ref, vec, gh_ref, gmem_ref, back_left_ref,
    back_right_ref, scaled_rows=None,
):
    wide = sizes.width
    count = sizes.queries
    bias_out = col_sum(gz)
    for n in range(seqs):
        if sizes.top:
            mem_grad = grad_mem_ref[pl.ds(n * sizes.segs, sizes.segs), :]
            bias_out = bias_out + col_sum(mem_grad)
            branch_ref[pl.ds(n * count, sizes.top), :] = jnp.concatenate(
                [mem_grad, jnp.zeros((sizes.top - sizes.segs, wide), F32)], axis=0
            ).astype(BF16)
        branch_ref[pl.ds(n * count + sizes.top, sizes.rows), :] = gz[
            n * sizes.rows : (n + 1) * sizes.rows
        ].astype(BF16)
    vec[pl.ds(5, 1), :] = bias_out
    branch = branch_ref[...]
    gout_ref[...] = tn(branch, att_ref[...]).astype(BF16).reshape(gout_ref.shape)
    go_ref[...] = nn(branch, out_ref[...].reshape(-1, wide)).astype(BF16)
    attend_back(sizes, seqs, proj_ref, probs_ref, go_ref, gproj_ref)
    vec[pl.ds(3, 1), :] = col_sum(gproj_ref[:, pl.ds(0, wide)].astype(F32))
    vec[pl.ds(4, 1), :] = col_sum(gproj_ref[:, pl.ds(2 * wide, wide)].astype(F32))
    grad_ext = nn(gproj_ref[...], qkv_ref[...].reshape(-1, wide))
    gain_sum = jnp.zeros((1, wide), F32)
    bias_sum = jnp.zeros((1, wide), F32)
    for n in range(seqs):
        base = n * sizes.ext
        own = grad_ext[base + sizes.top : base + sizes.top + sizes.rows]
        if sizes.top:
            spread = grad_ext[base : base + sizes.segs] * (1.0 / SEG_LEN)
            own = own + segment_spread(sizes.rows, wide, spread)
        gh_ref[pl.ds(n * sizes.rows, sizes.rows), :] = own
        mem = base + sizes.mem_at
        gmem_ref[pl.ds(n * sizes.segs, sizes.segs), :] = grad_ext[mem : mem + sizes.segs]
        left = base + sizes.left_at
        back_left_ref[n] = grad_ext[left : left + BACK_ROWS].astype(BF16)
        right = base + sizes.right_at
        back_right_ref[n] = grad_ext[right : right + RIGHT_ROWS].astype(BF16)
        if scaled_rows is not None:
            grads = (
                own,
                grad_ext[right : right + RIGHT_ROWS],
                grad_ext[left : left + LEFT_ROWS],
            )
            for rows, scaled in zip(grads, scaled_rows(n)):
                gain_sum = gain_sum + col_sum(rows * scaled)
                bias_sum = bias_sum + col_sum(rows)
    if scaled_rows is not None:
        vec[pl.ds(0, 1), :] = gain_sum
        vec[pl.ds(2, 1), :] = bias_sum
    step = CHIPS_Z // 2
    part = gqkv_ref.shape[1] * gqkv_ref.shape[2] * step
    for c in range(2):
        gqkv_ref[pl.ds(c * step, step)] = (
            tn(gproj_ref[:, pl.ds(c * part, part)], z_ref[...])
            .astype(BF16)
            .reshape((step,) + gqkv_ref.shape[1:])
        )


def merge_halo(sizes, n, gh_ref, gmem_ref, from_right_ref, from_left_ref):
    first = n * sizes.rows
    back = from_right_ref[n].astype(F32)
    head = gh_ref[pl.ds(first, RIGHT_ROWS), :] + from_left_ref[n].astype(F32)
    middle = gh_ref[pl.ds(first + RIGHT_ROWS, sizes.rows - RIGHT_ROWS - LEFT_ROWS), :]
    tail = gh_ref[pl.ds(first + sizes.rows - LEFT_ROWS, LEFT_ROWS), :] + back[:LEFT_ROWS]
    mem = gmem_ref[pl.ds(n * sizes.segs, sizes.segs), :] + back[LEFT_ROWS + sizes.segs :]
    return jnp.concatenate([head, middle, tail], axis=0), mem


def pack_kernel(places, qkv_ref, out_ref, up_ref, down_ref, *packed):
    eye = identity(LANES)
    high, wide, low = qkv_ref.shape[1], out_ref.shape[1], down_ref.shape[1]
    up = up_ref.shape[2]
    for layer, (attn, attn_at, ffn, ffn_at) in enumerate(places):
        ref = packed[attn]
        ref[pl.ds(attn_at, high), :] = qkv_ref[layer]
        ref[pl.ds(attn_at + high, wide), :] = out_ref[layer]
        ref = packed[ffn]
        ref[pl.ds(ffn_at, up), :] = tn(up_ref[layer], eye).astype(BF16)
        for part in range(down_ref.shape[2] // LANES):
            ref[pl.ds(ffn_at + up + part * low, low), :] = down_ref[
                layer, :, pl.ds(part * LANES, LANES)
            ]


def unpack_kernel(places, *refs):
    sources, outs = refs[:-7], refs[-7:]
    qkv_ref, out_ref, up_ref, down_ref, gains_ref, biases_ref, ffn_bias_ref = outs
    eye = identity(LANES)
    high, wide, low = qkv_ref.shape[1], out_ref.shape[1], down_ref.shape[1]
    up = up_ref.shape[2]

    def total(source, first, rows):
        ref = sources[source]
        value = ref[0, pl.ds(first, rows), :].astype(F32)
        for z in range(1, ref.shape[0]):
            value = value + ref[z, pl.ds(first, rows), :].astype(F32)
        return value

    for layer, (attn, attn_at, ffn, ffn_at) in enumerate(places):
        qkv_ref[layer] = total(attn, attn_at, high)
        out_ref[layer] = total(attn, attn_at + high, wide)
        up_ref[layer] = nt(eye, total(ffn, ffn_at, up).astype(BF16))
        for part in range(down_ref.shape[2] // LANES):
            down_ref[layer, :, pl.ds(part * LANES, LANES)] = total(
                ffn, ffn_at + up + part * low, low
            )
    sums = total(0, sources[0].shape[1] - SMALL_ROWS, SMALL_ROWS)
    parts = gains_ref.shape[2] // LANES
    for layer in range(gains_ref.shape[0]):
        for part in range(parts):
            lanes = pl.ds(part * LANES, LANES)
            block = sums[(layer * parts + part) * TILE : (layer * parts + part + 1) * TILE]
            gains_ref[layer, :, lanes] = block[0:2]
            biases_ref[layer, :, lanes] = block[2:8]
            for row in range(ffn_bias_ref.shape[1] // gains_ref.shape[2]):
                at = row * gains_ref.shape[2] + part * LANES
                ffn_bias_ref[pl.ds(layer, 1), pl.ds(at, LANES)] = block[8 + row : 9 + row]


def far_kernel(rows, mine_ref, theirs_ref, came_ref, sent_small, came_small, out_ref):
    total = mine_ref[...].astype(F32) + theirs_ref[...].astype(F32)
    out_ref[pl.ds(0, rows), :] = (total + came_ref[...].astype(F32)).astype(BF16)
    out_ref[pl.ds(rows, SMALL_ROWS), :] = (
        sent_small[...].astype(F32) + came_small[...].astype(F32)
    ).astype(BF16)


def near_small_kernel(
    count, rows, mine_ref, theirs_ref, second_ref, first_ref, sent_small, came_small, out_ref
):
    sums = (sent_small[...].astype(F32) + came_small[...].astype(F32)).astype(BF16)
    for z in range(count):
        group = pl.ds(z * rows, rows)
        total = mine_ref[group, :].astype(F32) + theirs_ref[group, :].astype(F32)
        total = total + second_ref[group, :].astype(F32) + first_ref[group, :].astype(F32)
        out_ref[z, pl.ds(0, rows), :] = total.astype(BF16)
        out_ref[z, pl.ds(rows, SMALL_ROWS), :] = sums


def first_layer_kernel(
    sizes, seqs, mats, by_blocks, count_in, at, place_ref, starts_ref, frames_ref, left_ref,
    right_ref, gains_ref, biases_ref, ffn_bias_ref, row_bias_ref, *refs
):
    hbm = refs[:count_in]
    (
        z_ref, proj_ref, probs_ref, att_ref, mixed_ref, mem_ref, next_ref, active_ref, slope_ref,
        low_ref, send_right_ref, send_left_ref, qkv_ref, out_ref, up_ref, down_ref, mask_ref,
        hidden_ref, sems,
    ) = refs[count_in:]
    attn_hbm, ffn_hbm = (hbm, hbm) if by_blocks else (hbm[:2], hbm[2:])
    wide = sizes.width
    copies = start_in(
        attn_pairs(mats, by_blocks, attn_hbm, at[0], qkv_ref, out_ref, place_ref), sems, 0
    )
    ffn_copies = start_in(
        ffn_pairs(mats, by_blocks, ffn_hbm, at[1], up_ref, down_ref, place_ref), sems, len(copies)
    )
    gain = gains_ref[0, pl.ds(0, 1), :]
    bias = biases_ref[0, pl.ds(0, 1), :]
    pad = jnp.zeros((TILE - sizes.segs, wide), F32)
    for n in range(seqs):
        own = frames_ref[n].astype(F32)
        before = left_ref[n].astype(F32)
        hidden = norm_forward(own, gain, bias)[0]
        halo = norm_forward(before[before.shape[0] - LEFT_ROWS :], gain, bias)[0]
        after = norm_forward(right_ref[n].astype(F32), gain, bias)[0]
        memory = jnp.concatenate(
            [
                segment_mean(own),
                jnp.zeros((sizes.segs - before.shape[0] // SEG_LEN, wide), F32),
                segment_mean(before),
            ],
            axis=0,
        )
        base = n * sizes.ext
        z_ref[pl.ds(base, sizes.top), :] = jnp.concatenate(
            [segment_mean(hidden), pad], axis=0
        ).astype(BF16)
        z_ref[pl.ds(base + sizes.top, sizes.rows), :] = hidden.astype(BF16)
        z_ref[pl.ds(base + sizes.right_at, RIGHT_ROWS), :] = after.astype(BF16)
        z_ref[pl.ds(base + sizes.left_at, LEFT_ROWS), :] = halo.astype(BF16)
        z_ref[pl.ds(base + sizes.mem_at, MEM_ROWS), :] = memory.astype(BF16)
    fill_mask(sizes, seqs, starts_ref, place_ref, mask_ref)
    wait_all(copies)
    project(sizes, z_ref, qkv_ref, row_bias_ref, proj_ref)
    attend(sizes, seqs, proj_ref, mask_ref, probs_ref, att_ref)
    mixed = nt(att_ref[...], out_ref[...].reshape(-1, wide)) + biases_ref[0, pl.ds(3, 1), :]
    for n in range(seqs):
        base = n * sizes.queries
        mem_ref[pl.ds(n * sizes.segs, sizes.segs), :] = mixed[base : base + sizes.segs]
        mixed_ref[pl.ds(n * sizes.rows, sizes.rows), :] = (
            frames_ref[n].astype(F32) + mixed[base + sizes.top : base + sizes.top + sizes.rows]
        )
    mixed = mixed_ref[...]
    hidden, _, _ = norm_forward(mixed, gains_ref[0, pl.ds(1, 1), :], biases_ref[0, pl.ds(4, 1), :])
    hidden_ref[...] = hidden.astype(BF16)
    next_ref[...] = mixed + biases_ref[0, pl.ds(5, 1), :]
    wait_all(ffn_copies)

    def body(c, carry):
        at_lane = pl.multiple_of(c * wide, wide)
        upward = nt(hidden_ref[...], up_block(up_ref, c, wide))
        upward = upward + ffn_bias_ref[pl.ds(0, 1), pl.ds(at_lane, wide)]
        active, slope = gelu_both(upward)
        active = active.astype(BF16)
        active_ref[:, pl.ds(at_lane, wide)] = active
        slope_ref[:, pl.ds(at_lane, wide)] = slope.astype(BF16)
        next_ref[...] += nt(active, down_block(down_ref, c, wide))
        return carry

    lax.fori_loop(0, sizes.ff // wide, body, 0)
    low, _, _ = norm_forward(
        next_ref[...], gains_ref[1, pl.ds(0, 1), :], biases_ref[1, pl.ds(0, 1), :]
    )
    low = low.astype(BF16)
    low_ref[...] = low
    for n in range(seqs):
        base = n * sizes.rows
        send_right_ref[n, pl.ds(0, LEFT_ROWS), :] = low[
            base + sizes.rows - LEFT_ROWS : base + sizes.rows
        ]
        send_right_ref[n, pl.ds(LEFT_ROWS, MEM_ROWS), :] = jnp.concatenate(
            [
                mem_ref[pl.ds(n * sizes.segs, sizes.segs), :],
                jnp.zeros((MEM_ROWS - sizes.segs, wide), F32),
            ],
            axis=0,
        ).astype(BF16)
        send_left_ref[n] = low[base : base + RIGHT_ROWS]


def last_layer_kernel(
    sizes, seqs, mats, by_blocks, count_in, attn_at, ffn_at, place_ref, starts_ref, low_ref,
    left_ref, right_ref, mem_ref, inputs_ref, out_grad_ref, gains_ref, biases_ref, ffn_bias_ref,
    row_bias_ref, *refs
):
    hbm = refs[:count_in]
    count_out = 2 if by_blocks else 4
    (encoded_ref, gz_ref, gh_ref, gmem_ref, back_left_ref, back_right_ref, vec) = refs[
        count_in : count_in + 7
    ]
    hbm_out = refs[count_in + 7 : count_in + 7 + count_out]
    (
        qkv_ref, out_ref, up_ref, down_ref, gqkv_ref, gout_ref, gup_ref, gdown_ref, mask_ref,
        z_ref, proj_ref, probs_ref, att_ref, hidden_ref, go_ref, gproj_ref, branch_ref,
        grad_low_ref, grad_hidden_ref, sems,
    ) = refs[count_in + 7 + count_out :]
    attn_hbm, ffn_hbm = (hbm, hbm) if by_blocks else (hbm[:2], hbm[2:])
    attn_out, ffn_out = out_views(by_blocks, hbm_out)
    wide = sizes.width
    attn_copies = start_in(
        attn_pairs(mats, by_blocks, attn_hbm, attn_at, qkv_ref, out_ref, place_ref), sems, 0
    )
    ffn_copies = start_in(
        ffn_pairs(mats, by_blocks, ffn_hbm, ffn_at, up_ref, down_ref, place_ref),
        sems,
        len(attn_copies),
    )
    vec[...] = jnp.zeros_like(vec)
    for n in range(seqs):
        base = n * sizes.ext
        z_ref[pl.ds(base, sizes.rows), :] = low_ref[pl.ds(n * sizes.rows, sizes.rows), :]
        z_ref[pl.ds(base + sizes.right_at, RIGHT_ROWS), :] = right_ref[n]
        z_ref[pl.ds(base + sizes.left_at, LEFT_ROWS), :] = left_ref[n, pl.ds(0, LEFT_ROWS), :]
        memory = jnp.concatenate(
            [
                mem_ref[pl.ds(n * sizes.segs, sizes.segs), :],
                left_ref[n, pl.ds(LEFT_ROWS, MEM_ROWS), :].astype(F32)[: sizes.segs],
            ],
            axis=0,
        )
        z_ref[pl.ds(base + sizes.mem_at, MEM_ROWS), :] = memory.astype(BF16)
        grad_low_ref[pl.ds(n * sizes.rows, sizes.rows), :] = out_grad_ref[n]
    fill_mask(sizes, seqs, starts_ref, place_ref, mask_ref)
    wait_all(attn_copies)
    project(sizes, z_ref, qkv_ref, row_bias_ref, proj_ref)
    attend(sizes, seqs, proj_ref, mask_ref, probs_ref, att_ref)
    mixed = (
        inputs_ref[...]
        + nt(att_ref[...], out_ref[...].reshape(-1, wide))
        + biases_ref[1, pl.ds(3, 1), :]
    )
    gain = gains_ref[1, pl.ds(1, 1), :]
    hidden, scaled, inverse = norm_forward(mixed, gain, biases_ref[1, pl.ds(4, 1), :])
    hidden_ref[...] = hidden.astype(BF16)
    for n in range(seqs):
        encoded_ref[n] = mixed[n * sizes.rows : (n + 1) * sizes.rows] + biases_ref[
            1, pl.ds(5, 1), :
        ]
    grad_hidden_ref[...] = jnp.zeros_like(grad_hidden_ref)
    wait_all(ffn_copies)

    def body(c, carry):
        at_lane = pl.multiple_of(c * wide, wide)
        upward = nt(hidden_ref[...], up_block(up_ref, c, wide))
        upward = upward + ffn_bias_ref[pl.ds(1, 1), pl.ds(at_lane, wide)]
        active, slope = gelu_both(upward)
        active = active.astype(BF16)
        made = nt(active, down_block(down_ref, c, wide))
        for n in range(seqs):
            encoded_ref[n] += made[n * sizes.rows : (n + 1) * sizes.rows]
        grad_hidden_ref[...] += ffn_back_step(
            sizes, c, wide, grad_low_ref[...], hidden_ref[...], active, slope, up_ref, down_ref,
            gup_ref, gdown_ref, vec,
        )
        return carry

    lax.fori_loop(0, sizes.ff // wide, body, 0)
    out_at = len(attn_copies) + len(ffn_copies)
    outs = start_out(
        ffn_pairs(mats, by_blocks, ffn_out, ffn_at, gup_ref, gdown_ref, place_ref), sems, out_at
    )
    grad = grad_low_ref[...].astype(F32)
    grad_hidden = grad_hidden_ref[...]
    vec[pl.ds(1, 1), :] = col_sum(grad_hidden * scaled)
    vec[pl.ds(6, 1), :] = col_sum(grad_hidden)
    vec[pl.ds(7, 1), :] = col_sum(grad)
    gz = grad + norm_backward(grad_hidden, scaled, inverse, gain)
    gz_ref[...] = gz
    attn_back_stage(
        sizes, seqs, gz, None, att_ref, proj_ref, probs_ref, z_ref, qkv_ref, out_ref, gqkv_ref,
        gout_ref, go_ref, gproj_ref, branch_ref, vec, gh_ref, gmem_ref, back_left_ref,
        back_right_ref,
    )
    outs = outs + start_out(
        attn_pairs(mats, by_blocks, attn_out, attn_at, gqkv_ref, gout_ref, place_ref),
        sems,
        out_at + len(outs),
    )
    wait_all(outs)


def first_back_kernel(
    last, sizes, seqs, mats, by_blocks, count_in, count_out, at, place_ref, inputs_ref, gz_in_ref,
    gh_in_ref, gmem_in_ref, from_right_ref, from_left_ref, mixed_ref, active_ref, slope_ref,
    att_ref, probs_ref, proj_ref, z_ref, frames_ref, left_ref, right_ref, gains_ref, biases_ref,
    last_vec, *refs
):
    hbm = refs[:count_in]
    gz_ref, gh_ref, gmem_ref, back_left_ref, back_right_ref, upper_vec, vec = refs[
        count_in : count_in + 7
    ]
    refs = refs[count_in + 7 :]
    hbm_out = refs[:count_out]
    (
        qkv_ref, out_ref, up_ref, down_ref, gqkv_ref, gout_ref, gup_ref, gdown_ref, hidden_ref,
        grad_low_ref, grad_ref, grad_hidden_ref, grad_mem_ref, go_ref, gproj_ref, branch_ref,
        small_ref, sems,
    ) = refs[count_out:]
    wide = sizes.width
    small = []
    if by_blocks:
        rows = mats.attn_rows + mats.ffn_rows
        classes = count_in // 2
        blocks = classes * CHIPS_Z * rows
        small = [ref.at[pl.ds(blocks, SMALL_ROWS), :] for ref in hbm_out]
        attn_out = ffn_out = [
            ref.at[pl.ds(0, blocks), :].reshape(classes, CHIPS_Z, rows, LANES).at[k]
            for ref in hbm_out
            for k in range(classes)
        ]
        attn_hbm = ffn_hbm = hbm
    else:
        attn_out, ffn_out = hbm_out[:2], hbm_out[2:]
        attn_hbm, ffn_hbm = hbm[:2], hbm[2:]
    ffn_copies = start_in(
        ffn_pairs(mats, by_blocks, ffn_hbm, at[1], up_ref, down_ref, place_ref), sems, 0
    )
    attn_copies = start_in(
        attn_pairs(mats, by_blocks, attn_hbm, at[0], qkv_ref, out_ref, place_ref),
        sems,
        len(ffn_copies),
    )
    vec[...] = jnp.zeros_like(vec)
    upper_vec[...] = jnp.zeros_like(upper_vec)
    gain = gains_ref[1, pl.ds(0, 1), :]
    gain_sum = jnp.zeros((1, wide), F32)
    bias_sum = jnp.zeros((1, wide), F32)
    for n in range(seqs):
        rows = pl.ds(n * sizes.rows, sizes.rows)
        _, scaled, inverse = norm_forward(
            inputs_ref[rows, :], gain, biases_ref[1, pl.ds(0, 1), :]
        )
        total, mem = merge_halo(last, n, gh_in_ref, gmem_in_ref, from_right_ref, from_left_ref)
        gain_sum = gain_sum + col_sum(total * scaled)
        bias_sum = bias_sum + col_sum(total)
        grad = gz_in_ref[rows, :] + norm_backward(total, scaled, inverse, gain)
        grad_ref[rows, :] = grad
        grad_low_ref[rows, :] = grad.astype(BF16)
        grad_mem_ref[pl.ds(n * sizes.segs, sizes.segs), :] = mem
    upper_vec[pl.ds(0, 1), :] = gain_sum
    upper_vec[pl.ds(2, 1), :] = bias_sum
    gain = gains_ref[0, pl.ds(1, 1), :]
    hidden, scaled, inverse = norm_forward(
        mixed_ref[...], gain, biases_ref[0, pl.ds(4, 1), :]
    )
    hidden_ref[...] = hidden.astype(BF16)
    grad_hidden_ref[...] = jnp.zeros_like(grad_hidden_ref)
    wait_all(ffn_copies)

    def body(c, carry):
        at_lane = pl.multiple_of(c * wide, wide)
        grad_hidden_ref[...] += ffn_back_step(
            sizes, c, wide, grad_low_ref[...], hidden_ref[...],
            active_ref[:, pl.ds(at_lane, wide)], slope_ref[:, pl.ds(at_lane, wide)].astype(F32),
            up_ref, down_ref, gup_ref, gdown_ref, vec,
        )
        return carry

    lax.fori_loop(0, sizes.ff // wide, body, 0)
    out_at = len(ffn_copies) + len(attn_copies)
    outs = start_out(
        ffn_pairs(mats, by_blocks, ffn_out, at[1], gup_ref, gdown_ref, place_ref), sems, out_at
    )
    grad_hidden = grad_hidden_ref[...]
    grad = grad_ref[...]
    vec[pl.ds(1, 1), :] = col_sum(grad_hidden * scaled)
    vec[pl.ds(6, 1), :] = col_sum(grad_hidden)
    vec[pl.ds(7, 1), :] = col_sum(grad)
    gz = grad + norm_backward(grad_hidden, scaled, inverse, gain)
    gz_ref[...] = gz

    def scaled_rows(n):
        before = left_ref[n, pl.ds(left_ref.shape[1] - LEFT_ROWS, LEFT_ROWS), :]
        parts = (frames_ref[n], right_ref[n], before)
        first_gain = gains_ref[0, pl.ds(0, 1), :]
        first_bias = biases_ref[0, pl.ds(0, 1), :]
        return [norm_forward(part.astype(F32), first_gain, first_bias)[1] for part in parts]

    wait_all(attn_copies)
    attn_back_stage(
        sizes, seqs, gz, grad_mem_ref, att_ref, proj_ref, probs_ref, z_ref, qkv_ref, out_ref,
        gqkv_ref, gout_ref, go_ref, gproj_ref, branch_ref, vec, gh_ref, gmem_ref, back_left_ref,
        back_right_ref, scaled_rows,
    )
    outs = outs + start_out(
        attn_pairs(mats, by_blocks, attn_out, at[0], gqkv_ref, gout_ref, place_ref),
        sems,
        out_at + len(outs),
    )
    parts = sizes.width // LANES
    for layer, total in enumerate((vec[...], last_vec[...] + upper_vec[...])):
        for part in range(parts):
            small_ref[pl.ds((layer * parts + part) * TILE, TILE), :] = total[
                :, part * LANES : (part + 1) * LANES
            ].astype(BF16)
    outs = outs + start_out([(ref, small_ref) for ref in small], sems, out_at + len(outs))
    wait_all(outs)


def frames_grad_kernel(
    sizes, seqs, frames_ref, gz_ref, gh_ref, gmem_ref, from_right_ref, from_left_ref, gains_ref,
    biases_ref, grad_ref
):
    gain = gains_ref[0, pl.ds(0, 1), :]
    for n in range(seqs):
        _, scaled, inverse = norm_forward(
            frames_ref[n].astype(F32), gain, biases_ref[0, pl.ds(0, 1), :]
        )
        total, mem = merge_halo(sizes, n, gh_ref, gmem_ref, from_right_ref, from_left_ref)
        grad_ref[n] = (
            gz_ref[pl.ds(n * sizes.rows, sizes.rows), :]
            + norm_backward(total, scaled, inverse, gain)
            + segment_spread(sizes.rows, sizes.width, mem * (1.0 / SEG_LEN))
        )


def shifted(value, axis, by):
    size = lax.axis_size(axis)
    pairs = [(i, i + by) for i in range(size) if 0 <= i + by < size]
    return lax.ppermute(value, axis, pairs)


def permuted(value, move):
    reps = lax.axis_size("rep")
    pairs = []
    for flat in range(lax.axis_size("seg") * reps):
        seg, rep = divmod(flat, reps)
        z, y, x, core = move(seg // CHIPS_Y, seg % CHIPS_Y, rep // 2, rep % 2)
        pairs.append((flat, (z * CHIPS_Y + y) * reps + 2 * x + core))
    return lax.ppermute(value, ("seg", "rep"), pairs)


def across_first(value):
    return permuted(value, lambda z, y, x, c: (z, y, x ^ 1, c) if c == 0 else (z, y ^ 1, x, c))


def across_second(value):
    return permuted(value, lambda z, y, x, c: (z, y ^ 1, x, c) if c == 0 else (z, y, x ^ 1, c))


def other_core(value):
    return permuted(value, lambda z, y, x, c: (z, y, x, c ^ 1))


def after(value, *others):
    return lax.optimization_barrier((value,) + others)[0]


def swap_z(blocks):
    groups = [
        [z * CHIPS_Y + y for z in range(CHIPS_Z)] for y in range(CHIPS_Y)
    ]
    return lax.all_to_all(blocks, "seg", 0, 0, axis_index_groups=groups, tiled=True)


def gather_z(shard):
    return swap_z(jnp.broadcast_to(shard[None], (CHIPS_Z,) + shard.shape))


def gather_sides(here):
    return [here, across_first(here), across_second(here)]


def both_cores(blocks):
    return blocks + [other_core(block) for block in blocks]


def summed(*parts):
    total = parts[0].astype(F32)
    for part in parts[1:]:
        total = total + part.astype(F32)
    return total.astype(BF16)


def row_block(rows, at):
    return pl.BlockSpec((rows, LANES), lambda i: (at, 0))


def sum_everywhere(value):
    count = lax.axis_size("seg") * lax.axis_size("rep")
    bit = 1
    while bit < count:
        value = value + lax.ppermute(value, ("seg", "rep"), [(i, i ^ bit) for i in range(count)])
        bit *= 2
    return value


def vmem_spec():
    return pl.BlockSpec(memory_space=pltpu.VMEM)


def smem_spec():
    return pl.BlockSpec(memory_space=pltpu.SMEM)


def hbm_spec():
    return pl.BlockSpec(memory_space=pl.ANY)


def call(body, in_specs, out_shapes, out_specs, scratch, args, flops=0, moved=0, grid=()):
    return pl.pallas_call(
        body,
        grid=grid,
        in_specs=in_specs,
        out_shape=tuple(jax.ShapeDtypeStruct(shape, kind) for shape, kind in out_shapes),
        out_specs=tuple(out_specs),
        scratch_shapes=scratch,
        compiler_params=pltpu.CompilerParams(vmem_limit_bytes=VMEM_BYTES),
        cost_estimate=pl.CostEstimate(flops=flops, bytes_accessed=moved, transcendentals=0),
    )(*args)


def on_device(
    frames,
    utt_segments,
    out_grad,
    qkv_weight,
    out_weight,
    ffn_in_weight,
    ffn_out_weight,
    norm_gains,
    biases,
    ffn_bias,
):
    micros, groups, rows, width = frames.shape
    seqs = micros * groups
    ff = ffn_bias.shape[1]
    reps = lax.axis_size("rep")
    seg_count = lax.axis_size("seg")
    mats = Matrices(width, ff)
    by_blocks = width // reps == LANES and reps == 4 and seg_count == BLOCKS
    first = Sizes(rows, width, ff, True)
    last = Sizes(rows, width, ff, False)
    own = seqs * rows
    mem_own = seqs * first.segs

    seg_at = lax.axis_index("seg")
    seg_base = seg_at * first.segs
    rep_at = lax.axis_index("rep")
    place = [seg_base, jnp.int32(first.segs * seg_count)]
    y_at, x_at, core_at = seg_at % CHIPS_Y, rep_at // 2, rep_at % 2
    for other in range(2):
        core = lax.bitwise_xor(core_at, other)
        for hop2 in range(2):
            for hop1 in range(2):
                x_hop = jnp.where(core == 0, hop1, hop2)
                y_hop = jnp.where(core == 0, hop2, hop1)
                place.append(lax.bitwise_xor(y_at, y_hop))
                place.append((lax.bitwise_xor(x_at, x_hop) * 2 + core) * LANES)
    place = jnp.stack([jnp.asarray(entry, jnp.int32) for entry in place])
    lengths = utt_segments.reshape(seqs, utt_segments.shape[2])
    starts = (jnp.cumsum(lengths, axis=1) - lengths).astype(jnp.int32)
    zero_bias = jnp.zeros((width,), F32)
    row_bias = jnp.stack(
        [jnp.concatenate([biases[l, 1], zero_bias, biases[l, 2]]) for l in range(LAYERS)]
    ).reshape(LAYERS, 1, 3 * width)

    frames_own = frames.reshape(seqs, rows, width)
    grads_own = out_grad.reshape(seqs, rows, width)
    far = MEM_LEN * SEG_LEN
    frames_left = shifted(frames_own[:, rows - far :], "seg", 1)
    frames_right = shifted(frames_own[:, :RIGHT_ROWS], "seg", -1)

    attn_rows, ffn_rows = mats.attn_rows, mats.ffn_rows
    if by_blocks:
        qkv_t, out_t, down_t = (
            jnp.swapaxes(member, 1, 2) for member in (qkv_weight, out_weight, ffn_out_weight)
        )
        all_rows = attn_rows + ffn_rows
        places = [(layer, 0, layer, attn_rows) for layer in range(LAYERS)]
        shards = call(
            lambda *refs: pack_kernel(places, *refs),
            [vmem_spec()] * 4,
            [((all_rows, LANES), BF16)] * LAYERS,
            [vmem_spec()] * LAYERS,
            [],
            (qkv_t, out_t, ffn_in_weight, down_t),
        )
        sides0 = gather_sides(gather_z(shards[0]))
        sides1 = gather_sides(gather_z(after(shards[1], sides0[0], frames_left, frames_right)))
        first_all = both_cores(sides0 + [across_second(sides0[1])])
        at = 0, attn_rows
        classes = len(first_all) // 2
        flat_rows = classes * CHIPS_Z * all_rows
        grad_outs0 = [((flat_rows + SMALL_ROWS, LANES), BF16)] * 2
        grad_outs1 = [((classes, CHIPS_Z, all_rows, LANES), BF16)] * 2
        copies_in = len(first_all) * (3 + mats.down_parts)
    else:
        whole = []
        for member, shape in zip(
            (qkv_weight, out_weight, ffn_in_weight, ffn_out_weight),
            (mats.qkv, mats.out, mats.up, mats.down),
        ):
            member = lax.all_gather(member, "rep", axis=1, tiled=True)
            member = lax.all_gather(member, "seg", axis=2, tiled=True)
            whole.append(jnp.swapaxes(member, 1, 2).reshape((LAYERS,) + shape))
        first_all = [member[0] for member in whole]
        last_all = [member[1] for member in whole]
        at = 0, 0
        grad_outs0 = grad_outs1 = [
            (shape, BF16) for shape in (mats.qkv, mats.out, mats.up, mats.down)
        ]
        copies_in = 4
    dma = pltpu.SemaphoreType.DMA

    matrices = [pltpu.VMEM(shape, BF16) for shape in (mats.qkv, mats.out, mats.up, mats.down)]

    (
        z0, proj0, probs0, att0, mixed0, mem1, x1, active0, slope0, low1, send_right, send_left,
    ) = call(
        lambda *refs: first_layer_kernel(
            first, seqs, mats, by_blocks, len(first_all), at, *refs
        ),
        [smem_spec()] * 2 + [vmem_spec()] * 7 + [hbm_spec()] * len(first_all),
        [
            ((seqs * first.ext, width), BF16),
            ((seqs * first.ext, 3 * width), BF16),
            ((seqs * first.pairs, 2 * first.queries, first.keys), BF16),
            ((seqs * first.queries, width), BF16),
            ((own, width), F32),
            ((mem_own, width), F32),
            ((own, width), F32),
            ((own, ff), BF16),
            ((own, ff), BF16),
            ((own, width), BF16),
            ((seqs, BACK_ROWS, width), BF16),
            ((seqs, RIGHT_ROWS, width), BF16),
        ],
        [vmem_spec()] * 12,
        matrices
        + [
            pltpu.VMEM((seqs, first.queries, first.keys), F32),
            pltpu.VMEM((own, width), BF16),
            dma((copies_in,)),
        ],
        (place, starts, frames_own, frames_left, frames_right, norm_gains, biases, ffn_bias,
         row_bias[0]) + tuple(first_all),
        flops=24 * own * (4 * width * width + 2 * width * ff) // 2,
        moved=2 * (4 * width * width + 2 * width * ff),
    )
    left1 = shifted(send_right, "seg", 1)
    right1 = shifted(send_left, "seg", -1)
    if by_blocks:
        last_all = both_cores(
            sides1 + [across_second(after(sides1[1], sides1[2], left1, right1))]
        )

    vec_shape = (TILE, width)
    outs = call(
        lambda *refs: last_layer_kernel(
            last, seqs, mats, by_blocks, len(last_all), *at, *refs
        ),
        [smem_spec()] * 2 + [vmem_spec()] * 10 + [hbm_spec()] * len(last_all),
        [
            ((seqs, rows, width), F32),
            ((own, width), F32),
            ((own, width), F32),
            ((mem_own, width), F32),
            ((seqs, BACK_ROWS, width), BF16),
            ((seqs, RIGHT_ROWS, width), BF16),
            (vec_shape, F32),
        ]
        + grad_outs1,
        [vmem_spec()] * 7 + [hbm_spec()] * len(grad_outs1),
        matrices
        + matrices
        + [
            pltpu.VMEM((seqs, last.queries, last.keys), F32),
            pltpu.VMEM((seqs * last.ext, width), BF16),
            pltpu.VMEM((seqs * last.ext, 3 * width), BF16),
            pltpu.VMEM((seqs * last.pairs, 2 * last.queries, last.keys), BF16),
            pltpu.VMEM((seqs * last.queries, width), BF16),
            pltpu.VMEM((own, width), BF16),
            pltpu.VMEM((seqs * last.queries, width), BF16),
            pltpu.VMEM((seqs * last.ext, 3 * width), BF16),
            pltpu.VMEM((seqs * last.queries, width), BF16),
            pltpu.VMEM((own, width), BF16),
            pltpu.VMEM((own, width), F32),
            dma((2 * copies_in,)),
        ],
        (place, starts, low1, left1, right1, mem1, x1, grads_own, norm_gains, biases, ffn_bias,
         row_bias[1]) + tuple(last_all),
        flops=30 * own * (4 * width * width + 2 * width * ff),
        moved=4 * (4 * width * width + 2 * width * ff),
    )
    encoded, gz1, gh1, gmem1, back_left1, back_right1, vec1 = outs[:7]
    grad_blocks1 = outs[7:]
    from_right1 = shifted(back_left1, "seg", -1)
    from_left1 = shifted(back_right1, "seg", 1)

    gh1_tied = gh1
    if by_blocks:
        mine1, theirs1 = grad_blocks1[0], other_core(grad_blocks1[1])
        far1 = after(summed(mine1[2:], theirs1[2:]), from_right1, from_left1)
        gh1_tied = after(gh1, far1)
    gz0, gh0, gmem0, back_left0, back_right0, upper_vec, vec0, *grad_blocks0 = call(
        lambda *refs: first_back_kernel(
            last, first, seqs, mats, by_blocks, len(first_all), len(grad_outs0), at, *refs
        ),
        [smem_spec()] + [vmem_spec()] * 19 + [hbm_spec()] * len(first_all),
        [
            ((own, width), F32),
            ((own, width), F32),
            ((mem_own, width), F32),
            ((seqs, BACK_ROWS, width), BF16),
            ((seqs, RIGHT_ROWS, width), BF16),
            (vec_shape, F32),
            (vec_shape, F32),
        ]
        + grad_outs0,
        [vmem_spec()] * 7 + [hbm_spec()] * len(grad_outs0),
        matrices
        + matrices
        + [
            pltpu.VMEM((own, width), BF16),
            pltpu.VMEM((own, width), BF16),
            pltpu.VMEM((own, width), F32),
            pltpu.VMEM((own, width), F32),
            pltpu.VMEM((mem_own, width), F32),
            pltpu.VMEM((seqs * first.queries, width), BF16),
            pltpu.VMEM((seqs * first.ext, 3 * width), BF16),
            pltpu.VMEM((seqs * first.queries, width), BF16),
            pltpu.VMEM((SMALL_ROWS, LANES), BF16),
            dma((2 * copies_in + 2,)),
        ],
        (place, x1, gz1, gh1_tied, gmem1, from_right1, from_left1, mixed0, active0, slope0, att0,
         probs0, proj0, z0, frames_own, frames_left, frames_right, norm_gains, biases, vec1)
        + tuple(first_all),
        flops=28 * own * (4 * width * width + 2 * width * ff),
        moved=4 * (4 * width * width + 2 * width * ff),
    )
    from_right0 = shifted(back_left0, "seg", -1)
    from_left0 = shifted(back_right0, "seg", 1)
    gz0_last = gz0
    if by_blocks:
        second1 = across_second(far1)
        near1 = summed(mine1[1], theirs1[1], second1[1])
        first1 = across_first(near1)
        mine0, theirs0 = grad_blocks0[0], other_core(after(grad_blocks0[1], second1))
        rows2, rows1 = flat_rows // 2, flat_rows // 4
        far0 = after(summed(mine0[rows2:], theirs0[rows2:]), near1)
        second0 = across_second(far0)
        total1 = summed(mine1[0], theirs1[0], second1[0], first1)
        last_parts = swap_z(total1)
        gz0_last = after(gz0, total1)
    frames_grad = call(
        lambda *refs: frames_grad_kernel(first, seqs, *refs),
        [vmem_spec()] * 8,
        [((seqs, rows, width), F32)],
        [vmem_spec()],
        [],
        (frames_own, gz0_last, gh0, gmem0, from_right0, from_left0, norm_gains, biases),
    )[0]

    if by_blocks:
        second_tied = after(second0, frames_grad, last_parts)
        near0 = call(
            lambda *refs: far_kernel(rows1, *refs),
            [row_block(rows1, 1)] * 3 + [row_block(SMALL_ROWS, rows2 // SMALL_ROWS)] * 2,
            [((rows1 + SMALL_ROWS, LANES), BF16)],
            [vmem_spec()],
            [],
            [mine0, theirs0, second_tied, far0, second_tied],
            grid=(1,),
        )[0]
        first0 = across_first(near0)
        first_parts = swap_z(
            call(
                lambda *refs: near_small_kernel(CHIPS_Z, all_rows, *refs),
                [row_block(rows1, 0)] * 4 + [row_block(SMALL_ROWS, rows1 // SMALL_ROWS)] * 2,
                [((CHIPS_Z, all_rows + SMALL_ROWS, LANES), BF16)],
                [vmem_spec()],
                [],
                [mine0, theirs0, second0, first0, near0, first0],
                grid=(1,),
            )[0]
        )
        shapes = [member.shape for member in (qkv_t, out_t, ffn_in_weight, down_t)]
        shapes += [member.shape for member in (norm_gains, biases, ffn_bias)]
        reduced = call(
            lambda *refs: unpack_kernel(places, *refs),
            [vmem_spec()] * LAYERS,
            [(shape, F32) for shape in shapes],
            [vmem_spec()] * len(shapes),
            [],
            [first_parts, last_parts],
        )
        small = reduced[4:]
        reduced = [
            jnp.swapaxes(reduced[0], 1, 2),
            jnp.swapaxes(reduced[1], 1, 2),
            reduced[2],
            jnp.swapaxes(reduced[3], 1, 2),
        ]
    else:
        reduced = []
        for member0, member1 in zip(grad_blocks0, grad_blocks1):
            both = jnp.stack([member0, member1]).reshape(LAYERS, -1, member0.shape[3])
            both = jnp.swapaxes(both, 1, 2)
            both = lax.psum_scatter(both, "seg", scatter_dimension=2, tiled=True)
            both = lax.psum_scatter(both, "rep", scatter_dimension=1, tiled=True)
            reduced.append(both.astype(F32))
        small = sum_everywhere(jnp.stack([vec0, vec1 + upper_vec]))
        small = small[:, 0:2], small[:, 2:8], small[:, 8:12].reshape(ffn_bias.shape)

    return (
        encoded.reshape(frames.shape),
        frames_grad.reshape(frames.shape),
        reduced[0],
        reduced[1],
        reduced[2],
        reduced[3],
        small[0],
        small[1],
        small[2],
    )


def solution(mesh):
    in_specs = (
        P(None, "rep", "seg", None),
        P(None, "rep", None),
        P(None, "rep", "seg", None),
        P(None, "rep", "seg"),
        P(None, "rep", "seg"),
        P(None, "rep", "seg"),
        P(None, "rep", "seg"),
        P(),
        P(),
        P(),
    )
    out_specs = (
        P(None, "rep", "seg", None),
        P(None, "rep", "seg", None),
        P(None, "rep", "seg"),
        P(None, "rep", "seg"),
        P(None, "rep", "seg"),
        P(None, "rep", "seg"),
        P(),
        P(),
        P(),
    )
    return jax.shard_map(
        on_device, mesh=mesh, in_specs=in_specs, out_specs=out_specs, check_vma=False
    )
```

```python
import jax
import jax.numpy as jnp
from jax import lax
from jax.experimental import pallas as pl
from jax.experimental.pallas import tpu as pltpu
from jax.sharding import PartitionSpec as P

HEADS = 8
SEG_LEN = 16
LEFT_LEN = 30
RIGHT_LEN = 4
MEM_LEN = 4
LAYERS = 2

EPS = 1e-05
ROOT_HALF = 0.7071067811865476
INV_ROOT_TWO_PI = 0.3989422804014327

LANES = 128
TILE = 16
RIGHT_ROWS = 16
LEFT_ROWS = 32
MEM_ROWS = 16
BACK_ROWS = LEFT_ROWS + MEM_ROWS
CHIPS_Z = 4
CHIPS_Y = 2
BLOCKS = CHIPS_Z * CHIPS_Y
SMALL_ROWS = 128
VMEM_BYTES = 56 * 1024 * 1024

BF16 = jnp.bfloat16
F32 = jnp.float32


def nn(a, b):
    return lax.dot_general(a, b, (((1,), (0,)), ((), ())), preferred_element_type=F32)


def nt(a, b):
    return lax.dot_general(a, b, (((1,), (1,)), ((), ())), preferred_element_type=F32)


def tn(a, b):
    return lax.dot_general(a, b, (((0,), (0,)), ((), ())), preferred_element_type=F32)


def col_sum(value):
    return jnp.sum(value, axis=0, keepdims=True)


def norm_forward(inputs, gain, bias):
    center = inputs - jnp.mean(inputs, axis=1, keepdims=True)
    inverse = lax.rsqrt(jnp.mean(center * center, axis=1, keepdims=True) + EPS)
    scaled = center * inverse
    return scaled * gain + bias, scaled, inverse


def norm_backward(grad_in, scaled, inverse, gain):
    grad_scaled = grad_in * gain
    return inverse * (
        grad_scaled
        - jnp.mean(grad_scaled, axis=1, keepdims=True)
        - scaled * jnp.mean(grad_scaled * scaled, axis=1, keepdims=True)
    )


def segment_mean(inputs):
    rows, width = inputs.shape
    return jnp.mean(inputs.reshape(rows // SEG_LEN, SEG_LEN, width), axis=1)


def segment_spread(rows, width, per_segment):
    segs = rows // SEG_LEN
    return jnp.broadcast_to(per_segment[:, None, :], (segs, SEG_LEN, width)).reshape(rows, width)


def identity(size):
    row = lax.broadcasted_iota(jnp.int32, (size, size), 0)
    col = lax.broadcasted_iota(jnp.int32, (size, size), 1)
    return (row == col).astype(F32).astype(BF16)


class Sizes:
    def __init__(self, rows, width, ff, with_summary):
        self.rows = rows
        self.width = width
        self.ff = ff
        self.segs = rows // SEG_LEN
        self.top = TILE if with_summary else 0
        self.keys = rows + RIGHT_ROWS + LEFT_ROWS + MEM_ROWS
        self.ext = self.top + self.keys
        self.queries = self.top + rows
        self.right_at = self.top + rows
        self.left_at = self.right_at + RIGHT_ROWS
        self.mem_at = self.left_at + LEFT_ROWS
        self.pairs = width // LANES


class Matrices:
    def __init__(self, width, ff):
        self.qkv = (CHIPS_Z, CHIPS_Y, 3 * width // BLOCKS, width)
        self.out = (CHIPS_Z, CHIPS_Y, width // BLOCKS, width)
        self.up = (CHIPS_Z, CHIPS_Y, ff // BLOCKS, width)
        self.down = (CHIPS_Z, CHIPS_Y, width // BLOCKS, ff)
        self.down_parts = ff // width
        self.attn_rows = self.qkv[2] + self.out[2]
        self.ffn_rows = self.up[2] + self.down_parts * self.down[2]


class Spots:
    def __init__(self, mats, halves):
        high, wide, up, low = mats.qkv[2], mats.out[2], mats.up[2], mats.down[2]
        parts = range(mats.down_parts)
        if halves:
            split = mats.down_parts // 2
            self.up = (0, 0)
            self.qkv = (1, 0)
            self.out = (1, high)
            self.down = [
                (0, up + low * j) if j < split else (1, high + wide + low * (j - split))
                for j in parts
            ]
        else:
            self.qkv = (0, 0)
            self.out = (0, high)
            self.up = (0, high + wide)
            self.down = [(0, high + wide + up + low * j) for j in parts]


def attn_pairs(mats, spots, groups, qkv_ref, out_ref, place_ref):
    if spots is None:
        return [(groups[0], qkv_ref), (groups[1], out_ref)]
    pairs = []
    for k in range(len(groups[0])):
        row = place_ref[2 + 2 * k]
        lane = pl.multiple_of(place_ref[3 + 2 * k], LANES)
        for (group, first), ref, shape in (
            (spots.qkv, qkv_ref, mats.qkv),
            (spots.out, out_ref, mats.out),
        ):
            block = groups[group][k]
            pairs.append(
                (
                    block.at[:, pl.ds(first, shape[2]), :],
                    ref.at[:, row, :, pl.ds(lane, LANES)],
                )
            )
    return pairs


def ffn_pairs(mats, spots, groups, up_ref, down_ref, place_ref):
    if spots is None:
        return [(groups[2], up_ref), (groups[3], down_ref)]
    pairs = []
    for k in range(len(groups[0])):
        row = place_ref[2 + 2 * k]
        lane = pl.multiple_of(place_ref[3 + 2 * k], LANES)
        group, first = spots.up
        block = groups[group][k]
        pairs.append(
            (block.at[:, pl.ds(first, mats.up[2]), :], up_ref.at[:, row, :, pl.ds(lane, LANES)])
        )
        for part, (group, first) in enumerate(spots.down):
            there = pl.multiple_of(
                place_ref[3 + 2 * k] * mats.down_parts + part * LANES, LANES
            )
            block = groups[group][k]
            pairs.append(
                (
                    block.at[:, pl.ds(first, mats.down[2]), :],
                    down_ref.at[:, row, :, pl.ds(there, LANES)],
                )
            )
    return pairs


def start_in(pairs, sems, at):
    copies = [pltpu.make_async_copy(s, d, sems.at[at + i]) for i, (s, d) in enumerate(pairs)]
    for copy in copies:
        copy.start()
    return copies


def start_out(pairs, sems, at):
    copies = [pltpu.make_async_copy(d, s, sems.at[at + i]) for i, (s, d) in enumerate(pairs)]
    for copy in copies:
        copy.start()
    return copies


def in_groups(spots, refs):
    return refs if spots is None else [refs]


def wait_all(copies):
    for copy in copies:
        copy.wait()


def fill_mask(sizes, seqs, starts_ref, place_ref, mask_ref):
    shape = (sizes.queries, sizes.keys)
    row = lax.broadcasted_iota(jnp.int32, shape, 0)
    col = lax.broadcasted_iota(jnp.int32, shape, 1)
    base = place_ref[0]
    total = place_ref[1]
    query = jnp.where(row < sizes.top, row, lax.shift_right_arithmetic(row - sizes.top, 4))
    left_at = sizes.rows + RIGHT_ROWS
    mem_at = left_at + LEFT_ROWS
    spot = jnp.where(col < left_at, col, col - mem_at)
    mem_seg = jnp.where(col < mem_at + sizes.segs, col - mem_at, col - mem_at - 2 * sizes.segs)
    key_seg = jnp.where(col < mem_at, lax.shift_right_arithmetic(spot, 4), mem_seg)
    near = (
        (key_seg == query)
        | ((spot >= query * SEG_LEN - LEFT_LEN) & (spot < query * SEG_LEN))
        | ((key_seg == query + 1) & (spot < query * SEG_LEN + SEG_LEN + RIGHT_LEN))
    )
    recent = (key_seg >= query - MEM_LEN) & (key_seg < query) & (row >= sizes.top)
    allowed = ((col < mem_at) & near) | ((col >= mem_at) & recent)
    key_abs = key_seg + base
    query_abs = query + base
    allowed = allowed & (key_abs >= 0) & (key_abs < total)
    if sizes.top:
        allowed = allowed & ((row < sizes.segs) | (row >= sizes.top))
    for n in range(seqs):
        key_owner = jnp.zeros(shape, jnp.int32)
        query_owner = jnp.zeros(shape, jnp.int32)
        for u in range(starts_ref.shape[1]):
            first = starts_ref[n, u]
            key_owner = key_owner + (key_abs >= first).astype(jnp.int32)
            query_owner = query_owner + (query_abs >= first).astype(jnp.int32)
        mask_ref[n] = jnp.where(allowed & (key_owner == query_owner), 0.0, -1e30)


def half_masks():
    lane = lax.broadcasted_iota(jnp.int32, (1, LANES), 1)
    even = (lane < LANES // 2).astype(F32)
    return even.astype(BF16), (1.0 - even).astype(BF16), lane < LANES // 2


def project(sizes, z_ref, qkv_ref, row_bias_ref, proj_ref):
    step = CHIPS_Z // 2
    for c in range(2):
        block = qkv_ref[pl.ds(c * step, step)].reshape(-1, sizes.width)
        wide = block.shape[0]
        made = nt(z_ref[...], block) + row_bias_ref[:, pl.ds(c * wide, wide)]
        proj_ref[:, pl.ds(c * wide, wide)] = made.astype(BF16)


def attend(sizes, seqs, proj_ref, mask_ref, probs_ref, att_ref):
    even, odd, is_even = half_masks()
    scale = (sizes.width // HEADS) ** (-0.5)
    count = sizes.queries

    def body(p, carry):
        for n in range(seqs):
            lane = pl.multiple_of(p * LANES, LANES)
            query = proj_ref[pl.ds(n * sizes.ext, count), pl.ds(lane, LANES)]
            first = n * sizes.ext + sizes.top
            key = proj_ref[pl.ds(first, sizes.keys), pl.ds(sizes.width + lane, LANES)]
            value = proj_ref[pl.ds(first, sizes.keys), pl.ds(2 * sizes.width + lane, LANES)]
            scores = nt(jnp.concatenate([query * even, query * odd], axis=0), key) * scale
            outs = []
            for half in range(2):
                part = scores[half * count : (half + 1) * count] + mask_ref[n]
                part = jnp.exp(part - jnp.max(part, axis=1, keepdims=True))
                part = (part * (1.0 / jnp.sum(part, axis=1, keepdims=True))).astype(BF16)
                probs_ref[n * sizes.pairs + p, pl.ds(half * count, count), :] = part
                outs.append(nn(part, value))
            att_ref[pl.ds(n * count, count), pl.ds(lane, LANES)] = jnp.where(
                is_even, outs[0], outs[1]
            ).astype(BF16)
        return carry

    lax.fori_loop(0, sizes.pairs, body, 0)


def attend_back(sizes, seqs, proj_ref, probs_ref, go_ref, gproj_ref):
    even, odd, is_even = half_masks()
    scale = (sizes.width // HEADS) ** (-0.5)
    count = sizes.queries
    wide = sizes.width
    for n in range(seqs):
        base = n * sizes.ext
        rest = sizes.ext - count
        gproj_ref[pl.ds(base + count, rest), pl.ds(0, wide)] = jnp.zeros((rest, wide), BF16)
        if sizes.top:
            gproj_ref[pl.ds(base, sizes.top), pl.ds(wide, 2 * wide)] = jnp.zeros(
                (sizes.top, 2 * wide), BF16
            )

    def body(p, carry):
        for n in range(seqs):
            lane = pl.multiple_of(p * LANES, LANES)
            base = n * sizes.ext
            first = base + sizes.top
            query = proj_ref[pl.ds(base, count), pl.ds(lane, LANES)]
            key = proj_ref[pl.ds(first, sizes.keys), pl.ds(wide + lane, LANES)]
            value = proj_ref[pl.ds(first, sizes.keys), pl.ds(2 * wide + lane, LANES)]
            grad = go_ref[pl.ds(n * count, count), pl.ds(lane, LANES)]
            queries = jnp.concatenate([query * even, query * odd], axis=0)
            grads = jnp.concatenate([grad * even, grad * odd], axis=0)
            probs_low = probs_ref[n * sizes.pairs + p]
            grad_values = tn(probs_low, grads)
            probs = probs_low.astype(F32)
            grad_probs = nt(grads, value)
            weighted = grad_probs * probs
            grad_scores = (
                (weighted - probs * jnp.sum(weighted, axis=1, keepdims=True)) * scale
            ).astype(BF16)
            grad_keys = tn(grad_scores, queries)
            grad_query = jnp.where(
                is_even, nn(grad_scores[:count], key), nn(grad_scores[count:], key)
            )
            gproj_ref[pl.ds(base, count), pl.ds(lane, LANES)] = grad_query.astype(BF16)
            gproj_ref[pl.ds(first, sizes.keys), pl.ds(wide + lane, LANES)] = grad_keys.astype(BF16)
            gproj_ref[pl.ds(first, sizes.keys), pl.ds(2 * wide + lane, LANES)] = (
                grad_values.astype(BF16)
            )
        return carry

    lax.fori_loop(0, sizes.pairs, body, 0)


def gelu_both(upward):
    half = 0.5 * (1.0 + lax.erf(upward * ROOT_HALF))
    slope = half + upward * jnp.exp(-0.5 * upward * upward) * INV_ROOT_TWO_PI
    return upward * half, slope


def up_block(up_ref, c, wide):
    step = wide // (up_ref.shape[1] * up_ref.shape[2])
    return up_ref[pl.ds(c * step, step)].reshape(-1, up_ref.shape[3])


def down_block(down_ref, c, wide):
    at = pl.multiple_of(c * wide, wide)
    return down_ref[:, :, :, pl.ds(at, wide)].reshape(-1, wide)


def ffn_back_step(
    sizes, c, wide, grad_low, hidden_low, active, slope, up_ref, down_ref, gup_ref, gdown_ref, vec
):
    at = pl.multiple_of(c * wide, wide)
    up = up_block(up_ref, c, wide)
    down = down_block(down_ref, c, wide)
    grad_active = nn(grad_low, down)
    grad_up_f = grad_active * slope
    grad_up = grad_up_f.astype(BF16)
    gdown_ref[:, :, :, pl.ds(at, wide)] = (
        tn(grad_low, active).astype(BF16).reshape(gdown_ref.shape[:3] + (wide,))
    )
    step = wide // (gup_ref.shape[1] * gup_ref.shape[2])
    gup_ref[pl.ds(c * step, step)] = (
        tn(grad_up, hidden_low).astype(BF16).reshape((step,) + gup_ref.shape[1:])
    )
    vec[pl.ds(8 + c, 1), :] = col_sum(grad_up.astype(F32))
    return nn(grad_up, up)


def attn_back_stage(
    sizes, seqs, gz, grad_mem_ref, att_ref, proj_ref, probs_ref, z_ref, qkv_ref, out_ref,
    gqkv_ref, gout_ref, go_ref, gproj_ref, branch_ref, vec, gh_ref, gmem_ref, back_left_ref,
    back_right_ref, scaled_rows=None,
):
    wide = sizes.width
    count = sizes.queries
    bias_out = col_sum(gz)
    for n in range(seqs):
        if sizes.top:
            mem_grad = grad_mem_ref[pl.ds(n * sizes.segs, sizes.segs), :]
            bias_out = bias_out + col_sum(mem_grad)
            branch_ref[pl.ds(n * count, sizes.top), :] = jnp.concatenate(
                [mem_grad, jnp.zeros((sizes.top - sizes.segs, wide), F32)], axis=0
            ).astype(BF16)
        branch_ref[pl.ds(n * count + sizes.top, sizes.rows), :] = gz[
            n * sizes.rows : (n + 1) * sizes.rows
        ].astype(BF16)
    vec[pl.ds(5, 1), :] = bias_out
    branch = branch_ref[...]
    gout_ref[...] = tn(branch, att_ref[...]).astype(BF16).reshape(gout_ref.shape)
    go_ref[...] = nn(branch, out_ref[...].reshape(-1, wide)).astype(BF16)
    attend_back(sizes, seqs, proj_ref, probs_ref, go_ref, gproj_ref)
    vec[pl.ds(3, 1), :] = col_sum(gproj_ref[:, pl.ds(0, wide)].astype(F32))
    vec[pl.ds(4, 1), :] = col_sum(gproj_ref[:, pl.ds(2 * wide, wide)].astype(F32))
    grad_ext = nn(gproj_ref[...], qkv_ref[...].reshape(-1, wide))
    gain_sum = jnp.zeros((1, wide), F32)
    bias_sum = jnp.zeros((1, wide), F32)
    for n in range(seqs):
        base = n * sizes.ext
        own = grad_ext[base + sizes.top : base + sizes.top + sizes.rows]
        if sizes.top:
            spread = grad_ext[base : base + sizes.segs] * (1.0 / SEG_LEN)
            own = own + segment_spread(sizes.rows, wide, spread)
        gh_ref[pl.ds(n * sizes.rows, sizes.rows), :] = own
        mem = base + sizes.mem_at
        gmem_ref[pl.ds(n * sizes.segs, sizes.segs), :] = grad_ext[mem : mem + sizes.segs]
        left = base + sizes.left_at
        back_left_ref[n] = grad_ext[left : left + BACK_ROWS].astype(BF16)
        right = base + sizes.right_at
        back_right_ref[n] = grad_ext[right : right + RIGHT_ROWS].astype(BF16)
        if scaled_rows is not None:
            grads = (
                own,
                grad_ext[right : right + RIGHT_ROWS],
                grad_ext[left : left + LEFT_ROWS],
            )
            for rows, scaled in zip(grads, scaled_rows(n)):
                gain_sum = gain_sum + col_sum(rows * scaled)
                bias_sum = bias_sum + col_sum(rows)
    if scaled_rows is not None:
        vec[pl.ds(0, 1), :] = gain_sum
        vec[pl.ds(2, 1), :] = bias_sum
    step = CHIPS_Z // 2
    part = gqkv_ref.shape[1] * gqkv_ref.shape[2] * step
    for c in range(2):
        gqkv_ref[pl.ds(c * step, step)] = (
            tn(gproj_ref[:, pl.ds(c * part, part)], z_ref[...])
            .astype(BF16)
            .reshape((step,) + gqkv_ref.shape[1:])
        )


def merge_halo(sizes, n, gh_ref, gmem_ref, from_right_ref, from_left_ref):
    first = n * sizes.rows
    back = from_right_ref[n].astype(F32)
    head = gh_ref[pl.ds(first, RIGHT_ROWS), :] + from_left_ref[n].astype(F32)
    middle = gh_ref[pl.ds(first + RIGHT_ROWS, sizes.rows - RIGHT_ROWS - LEFT_ROWS), :]
    tail = gh_ref[pl.ds(first + sizes.rows - LEFT_ROWS, LEFT_ROWS), :] + back[:LEFT_ROWS]
    mem = gmem_ref[pl.ds(n * sizes.segs, sizes.segs), :] + back[LEFT_ROWS + sizes.segs :]
    return jnp.concatenate([head, middle, tail], axis=0), mem


def pack_kernel(spots, qkv_ref, out_ref, up_ref, down_ref, *packed):
    eye = identity(LANES)
    high, wide, low = qkv_ref.shape[1], out_ref.shape[1], down_ref.shape[1]
    for layer, ref in enumerate(packed):
        ref[pl.ds(spots.qkv[1], high), :] = qkv_ref[layer]
        ref[pl.ds(spots.out[1], wide), :] = out_ref[layer]
        ref[pl.ds(spots.up[1], up_ref.shape[2]), :] = tn(up_ref[layer], eye).astype(BF16)
        for part, (_, first) in enumerate(spots.down):
            ref[pl.ds(first, low), :] = down_ref[layer, :, pl.ds(part * LANES, LANES)]


def unpack_kernel(layers, small_at, *refs):
    sources, outs = refs[:-7], refs[-7:]
    qkv_ref, out_ref, up_ref, down_ref, gains_ref, biases_ref, ffn_bias_ref = outs
    eye = identity(LANES)
    high, wide, low = qkv_ref.shape[1], out_ref.shape[1], down_ref.shape[1]

    def total(source, first, rows):
        ref = sources[source]
        value = ref[0, pl.ds(first, rows), :].astype(F32)
        for z in range(1, ref.shape[0]):
            value = value + ref[z, pl.ds(first, rows), :].astype(F32)
        return value

    base = 0
    for layer, spots in enumerate(layers):
        qkv_ref[layer] = total(base + spots.qkv[0], spots.qkv[1], high)
        out_ref[layer] = total(base + spots.out[0], spots.out[1], wide)
        up_ref[layer] = nt(
            eye, total(base + spots.up[0], spots.up[1], up_ref.shape[2]).astype(BF16)
        )
        for part, (group, first) in enumerate(spots.down):
            down_ref[layer, :, pl.ds(part * LANES, LANES)] = total(base + group, first, low)
        base += 1 + max(group for group, _ in spots.down)
    sums = total(small_at[0], small_at[1], SMALL_ROWS)
    parts = gains_ref.shape[2] // LANES
    for layer in range(gains_ref.shape[0]):
        for part in range(parts):
            lanes = pl.ds(part * LANES, LANES)
            block = sums[(layer * parts + part) * TILE : (layer * parts + part + 1) * TILE]
            gains_ref[layer, :, lanes] = block[0:2]
            for row in range(biases_ref.shape[0]):
                biases_ref[row, pl.ds(layer, 1), lanes] = block[2 + row : 3 + row]
            for row in range(ffn_bias_ref.shape[1] // gains_ref.shape[2]):
                at = row * gains_ref.shape[2] + part * LANES
                ffn_bias_ref[pl.ds(layer, 1), pl.ds(at, LANES)] = block[8 + row : 9 + row]


def near_small_kernel(count, mine_ref, theirs_ref, second_ref, first_ref, out_ref):
    rows = out_ref.shape[1] - SMALL_ROWS

    def total(at, size):
        group = pl.ds(at, size)
        value = mine_ref[0, group, :].astype(F32) + theirs_ref[0, group, :].astype(F32)
        return (
            value + second_ref[0, group, :].astype(F32) + first_ref[group, :].astype(F32)
        ).astype(BF16)

    small = total(count * rows, SMALL_ROWS)
    for z in range(count):
        out_ref[z, pl.ds(0, rows), :] = total(z * rows, rows)
        out_ref[z, pl.ds(rows, SMALL_ROWS), :] = small


def first_layer_kernel(
    sizes, seqs, mats, spots, count_in, place_ref, starts_ref, frames_ref, left_ref, right_ref,
    gains_ref, biases_ref, ffn_bias_ref, row_bias_ref, *refs
):
    groups = in_groups(spots, refs[:count_in])
    (
        z_ref, proj_ref, probs_ref, att_ref, mixed_ref, mem_ref, next_ref, active_ref, slope_ref,
        low_ref, send_right_ref, send_left_ref, qkv_ref, out_ref, up_ref, down_ref, mask_ref,
        hidden_ref, sems,
    ) = refs[count_in:]
    wide = sizes.width
    copies = start_in(attn_pairs(mats, spots, groups, qkv_ref, out_ref, place_ref), sems, 0)
    ffn_copies = start_in(
        ffn_pairs(mats, spots, groups, up_ref, down_ref, place_ref), sems, len(copies)
    )
    gain = gains_ref[0, pl.ds(0, 1), :]
    bias = biases_ref[0, pl.ds(0, 1), :]
    pad = jnp.zeros((TILE - sizes.segs, wide), F32)
    for n in range(seqs):
        own = frames_ref[n].astype(F32)
        before = left_ref[n].astype(F32)
        hidden = norm_forward(own, gain, bias)[0]
        halo = norm_forward(before[before.shape[0] - LEFT_ROWS :], gain, bias)[0]
        after = norm_forward(right_ref[n].astype(F32), gain, bias)[0]
        memory = jnp.concatenate(
            [
                segment_mean(own),
                jnp.zeros((sizes.segs - before.shape[0] // SEG_LEN, wide), F32),
                segment_mean(before),
            ],
            axis=0,
        )
        base = n * sizes.ext
        z_ref[pl.ds(base, sizes.top), :] = jnp.concatenate(
            [segment_mean(hidden), pad], axis=0
        ).astype(BF16)
        z_ref[pl.ds(base + sizes.top, sizes.rows), :] = hidden.astype(BF16)
        z_ref[pl.ds(base + sizes.right_at, RIGHT_ROWS), :] = after.astype(BF16)
        z_ref[pl.ds(base + sizes.left_at, LEFT_ROWS), :] = halo.astype(BF16)
        z_ref[pl.ds(base + sizes.mem_at, MEM_ROWS), :] = memory.astype(BF16)
    fill_mask(sizes, seqs, starts_ref, place_ref, mask_ref)
    wait_all(copies)
    project(sizes, z_ref, qkv_ref, row_bias_ref, proj_ref)
    attend(sizes, seqs, proj_ref, mask_ref, probs_ref, att_ref)
    mixed = nt(att_ref[...], out_ref[...].reshape(-1, wide)) + biases_ref[0, pl.ds(3, 1), :]
    for n in range(seqs):
        base = n * sizes.queries
        mem_ref[pl.ds(n * sizes.segs, sizes.segs), :] = mixed[base : base + sizes.segs]
        mixed_ref[pl.ds(n * sizes.rows, sizes.rows), :] = (
            frames_ref[n].astype(F32) + mixed[base + sizes.top : base + sizes.top + sizes.rows]
        )
    mixed = mixed_ref[...]
    hidden, _, _ = norm_forward(mixed, gains_ref[0, pl.ds(1, 1), :], biases_ref[0, pl.ds(4, 1), :])
    hidden_ref[...] = hidden.astype(BF16)
    next_ref[...] = mixed + biases_ref[0, pl.ds(5, 1), :]
    wait_all(ffn_copies)

    def body(c, carry):
        at_lane = pl.multiple_of(c * wide, wide)
        upward = nt(hidden_ref[...], up_block(up_ref, c, wide))
        upward = upward + ffn_bias_ref[pl.ds(0, 1), pl.ds(at_lane, wide)]
        active, slope = gelu_both(upward)
        active = active.astype(BF16)
        active_ref[:, pl.ds(at_lane, wide)] = active
        slope_ref[:, pl.ds(at_lane, wide)] = slope.astype(BF16)
        next_ref[...] += nt(active, down_block(down_ref, c, wide))
        return carry

    lax.fori_loop(0, sizes.ff // wide, body, 0)
    low, _, _ = norm_forward(
        next_ref[...], gains_ref[1, pl.ds(0, 1), :], biases_ref[1, pl.ds(0, 1), :]
    )
    low = low.astype(BF16)
    low_ref[...] = low
    for n in range(seqs):
        base = n * sizes.rows
        send_right_ref[n, pl.ds(0, LEFT_ROWS), :] = low[
            base + sizes.rows - LEFT_ROWS : base + sizes.rows
        ]
        send_right_ref[n, pl.ds(LEFT_ROWS, MEM_ROWS), :] = jnp.concatenate(
            [
                mem_ref[pl.ds(n * sizes.segs, sizes.segs), :],
                jnp.zeros((MEM_ROWS - sizes.segs, wide), F32),
            ],
            axis=0,
        ).astype(BF16)
        send_left_ref[n] = low[base : base + RIGHT_ROWS]


def last_layer_kernel(
    sizes, seqs, mats, spots, count_in, count_out, place_ref, starts_ref, low_ref, left_ref,
    right_ref, mem_ref, inputs_ref, out_grad_ref, gains_ref, biases_ref, ffn_bias_ref,
    row_bias_ref, *refs
):
    groups = in_groups(spots, refs[:count_in])
    (encoded_ref, gz_ref, gh_ref, gmem_ref, back_left_ref, back_right_ref, vec) = refs[
        count_in : count_in + 7
    ]
    hbm_out = refs[count_in + 7 : count_in + 7 + count_out]
    (
        qkv_ref, out_ref, up_ref, down_ref, gqkv_ref, gout_ref, gup_ref, gdown_ref, mask_ref,
        z_ref, proj_ref, probs_ref, att_ref, hidden_ref, go_ref, gproj_ref, branch_ref,
        grad_low_ref, grad_hidden_ref, sems,
    ) = refs[count_in + 7 + count_out :]
    outs_to = hbm_out
    if spots is not None:
        outs_to = [[ref.at[k] for ref in hbm_out for k in range(ref.shape[0])]]
    wide = sizes.width
    attn_copies = start_in(attn_pairs(mats, spots, groups, qkv_ref, out_ref, place_ref), sems, 0)
    ffn_copies = start_in(
        ffn_pairs(mats, spots, groups, up_ref, down_ref, place_ref), sems, len(attn_copies)
    )
    vec[...] = jnp.zeros_like(vec)
    for n in range(seqs):
        base = n * sizes.ext
        z_ref[pl.ds(base, sizes.rows), :] = low_ref[pl.ds(n * sizes.rows, sizes.rows), :]
        z_ref[pl.ds(base + sizes.right_at, RIGHT_ROWS), :] = right_ref[n]
        z_ref[pl.ds(base + sizes.left_at, LEFT_ROWS), :] = left_ref[n, pl.ds(0, LEFT_ROWS), :]
        memory = jnp.concatenate(
            [
                mem_ref[pl.ds(n * sizes.segs, sizes.segs), :],
                left_ref[n, pl.ds(LEFT_ROWS, MEM_ROWS), :].astype(F32)[: sizes.segs],
            ],
            axis=0,
        )
        z_ref[pl.ds(base + sizes.mem_at, MEM_ROWS), :] = memory.astype(BF16)
        grad_low_ref[pl.ds(n * sizes.rows, sizes.rows), :] = out_grad_ref[n]
    fill_mask(sizes, seqs, starts_ref, place_ref, mask_ref)
    wait_all(attn_copies)
    project(sizes, z_ref, qkv_ref, row_bias_ref, proj_ref)
    attend(sizes, seqs, proj_ref, mask_ref, probs_ref, att_ref)
    mixed = (
        inputs_ref[...]
        + nt(att_ref[...], out_ref[...].reshape(-1, wide))
        + biases_ref[1, pl.ds(3, 1), :]
    )
    gain = gains_ref[1, pl.ds(1, 1), :]
    hidden, scaled, inverse = norm_forward(mixed, gain, biases_ref[1, pl.ds(4, 1), :])
    hidden_ref[...] = hidden.astype(BF16)
    for n in range(seqs):
        encoded_ref[n] = mixed[n * sizes.rows : (n + 1) * sizes.rows] + biases_ref[
            1, pl.ds(5, 1), :
        ]
    grad_hidden_ref[...] = jnp.zeros_like(grad_hidden_ref)
    wait_all(ffn_copies)

    def body(c, carry):
        at_lane = pl.multiple_of(c * wide, wide)
        upward = nt(hidden_ref[...], up_block(up_ref, c, wide))
        upward = upward + ffn_bias_ref[pl.ds(1, 1), pl.ds(at_lane, wide)]
        active, slope = gelu_both(upward)
        active = active.astype(BF16)
        made = nt(active, down_block(down_ref, c, wide))
        for n in range(seqs):
            encoded_ref[n] += made[n * sizes.rows : (n + 1) * sizes.rows]
        grad_hidden_ref[...] += ffn_back_step(
            sizes, c, wide, grad_low_ref[...], hidden_ref[...], active, slope, up_ref, down_ref,
            gup_ref, gdown_ref, vec,
        )
        return carry

    lax.fori_loop(0, sizes.ff // wide, body, 0)
    out_at = len(attn_copies) + len(ffn_copies)
    outs = start_out(
        ffn_pairs(mats, spots, outs_to, gup_ref, gdown_ref, place_ref), sems, out_at
    )
    grad = grad_low_ref[...].astype(F32)
    grad_hidden = grad_hidden_ref[...]
    vec[pl.ds(1, 1), :] = col_sum(grad_hidden * scaled)
    vec[pl.ds(6, 1), :] = col_sum(grad_hidden)
    vec[pl.ds(7, 1), :] = col_sum(grad)
    gz = grad + norm_backward(grad_hidden, scaled, inverse, gain)
    gz_ref[...] = gz
    attn_back_stage(
        sizes, seqs, gz, None, att_ref, proj_ref, probs_ref, z_ref, qkv_ref, out_ref, gqkv_ref,
        gout_ref, go_ref, gproj_ref, branch_ref, vec, gh_ref, gmem_ref, back_left_ref,
        back_right_ref,
    )
    outs = outs + start_out(
        attn_pairs(mats, spots, outs_to, gqkv_ref, gout_ref, place_ref),
        sems,
        out_at + len(outs),
    )
    wait_all(outs)


def first_back_kernel(
    last, sizes, seqs, mats, spots, halves, count_in, count_out, place_ref, inputs_ref, gz_in_ref,
    gh_in_ref, gmem_in_ref, from_right_ref, from_left_ref, mixed_ref, active_ref, slope_ref,
    att_ref, probs_ref, proj_ref, z_ref, frames_ref, left_ref, right_ref, gains_ref, biases_ref,
    last_vec, *refs
):
    groups = in_groups(spots, refs[:count_in])
    gz_ref, gh_ref, gmem_ref, back_left_ref, back_right_ref, upper_vec, vec = refs[
        count_in : count_in + 7
    ]
    refs = refs[count_in + 7 :]
    hbm_out = refs[:count_out]
    (
        qkv_ref, out_ref, up_ref, down_ref, gqkv_ref, gout_ref, gup_ref, gdown_ref, hidden_ref,
        grad_low_ref, grad_ref, grad_hidden_ref, grad_mem_ref, go_ref, gproj_ref, branch_ref,
        small_ref, sems,
    ) = refs[count_out:]
    wide = sizes.width
    small = []
    outs_to = hbm_out
    if spots is not None:
        classes = count_in // 2
        rows = (mats.attn_rows + mats.ffn_rows) // 2
        half = CHIPS_Z * rows
        each = [ref.at[k] for ref in hbm_out for k in range(classes)]
        small = [ref.at[pl.ds(2 * half, SMALL_ROWS), :] for ref in each]
        outs_to = [
            [ref.at[pl.ds(g * half, half), :].reshape(CHIPS_Z, rows, LANES) for ref in each]
            for g in range(2)
        ]
    ffn_copies = start_in(ffn_pairs(mats, spots, groups, up_ref, down_ref, place_ref), sems, 0)
    attn_copies = start_in(
        attn_pairs(mats, spots, groups, qkv_ref, out_ref, place_ref), sems, len(ffn_copies)
    )
    vec[...] = jnp.zeros_like(vec)
    upper_vec[...] = jnp.zeros_like(upper_vec)
    gain = gains_ref[1, pl.ds(0, 1), :]
    gain_sum = jnp.zeros((1, wide), F32)
    bias_sum = jnp.zeros((1, wide), F32)
    for n in range(seqs):
        rows = pl.ds(n * sizes.rows, sizes.rows)
        _, scaled, inverse = norm_forward(
            inputs_ref[rows, :], gain, biases_ref[1, pl.ds(0, 1), :]
        )
        total, mem = merge_halo(last, n, gh_in_ref, gmem_in_ref, from_right_ref, from_left_ref)
        gain_sum = gain_sum + col_sum(total * scaled)
        bias_sum = bias_sum + col_sum(total)
        grad = gz_in_ref[rows, :] + norm_backward(total, scaled, inverse, gain)
        grad_ref[rows, :] = grad
        grad_low_ref[rows, :] = grad.astype(BF16)
        grad_mem_ref[pl.ds(n * sizes.segs, sizes.segs), :] = mem
    upper_vec[pl.ds(0, 1), :] = gain_sum
    upper_vec[pl.ds(2, 1), :] = bias_sum
    gain = gains_ref[0, pl.ds(1, 1), :]
    hidden, scaled, inverse = norm_forward(
        mixed_ref[...], gain, biases_ref[0, pl.ds(4, 1), :]
    )
    hidden_ref[...] = hidden.astype(BF16)
    grad_hidden_ref[...] = jnp.zeros_like(grad_hidden_ref)
    wait_all(ffn_copies)

    def body(c, carry):
        at_lane = pl.multiple_of(c * wide, wide)
        grad_hidden_ref[...] += ffn_back_step(
            sizes, c, wide, grad_low_ref[...], hidden_ref[...],
            active_ref[:, pl.ds(at_lane, wide)], slope_ref[:, pl.ds(at_lane, wide)].astype(F32),
            up_ref, down_ref, gup_ref, gdown_ref, vec,
        )
        return carry

    lax.fori_loop(0, sizes.ff // wide, body, 0)
    out_at = len(ffn_copies) + len(attn_copies)
    outs = start_out(
        ffn_pairs(mats, halves, outs_to, gup_ref, gdown_ref, place_ref), sems, out_at
    )
    grad_hidden = grad_hidden_ref[...]
    grad = grad_ref[...]
    vec[pl.ds(1, 1), :] = col_sum(grad_hidden * scaled)
    vec[pl.ds(6, 1), :] = col_sum(grad_hidden)
    vec[pl.ds(7, 1), :] = col_sum(grad)
    gz = grad + norm_backward(grad_hidden, scaled, inverse, gain)
    gz_ref[...] = gz

    def scaled_rows(n):
        before = left_ref[n, pl.ds(left_ref.shape[1] - LEFT_ROWS, LEFT_ROWS), :]
        parts = (frames_ref[n], right_ref[n], before)
        first_gain = gains_ref[0, pl.ds(0, 1), :]
        first_bias = biases_ref[0, pl.ds(0, 1), :]
        return [norm_forward(part.astype(F32), first_gain, first_bias)[1] for part in parts]

    wait_all(attn_copies)
    attn_back_stage(
        sizes, seqs, gz, grad_mem_ref, att_ref, proj_ref, probs_ref, z_ref, qkv_ref, out_ref,
        gqkv_ref, gout_ref, go_ref, gproj_ref, branch_ref, vec, gh_ref, gmem_ref, back_left_ref,
        back_right_ref, scaled_rows,
    )
    outs = outs + start_out(
        attn_pairs(mats, halves, outs_to, gqkv_ref, gout_ref, place_ref),
        sems,
        out_at + len(outs),
    )
    parts = sizes.width // LANES
    for layer, total in enumerate((vec[...], last_vec[...] + upper_vec[...])):
        for part in range(parts):
            small_ref[pl.ds((layer * parts + part) * TILE, TILE), :] = total[
                :, part * LANES : (part + 1) * LANES
            ].astype(BF16)
    outs = outs + start_out([(ref, small_ref) for ref in small], sems, out_at + len(outs))
    wait_all(outs)


def frames_grad_kernel(
    sizes, seqs, frames_ref, gz_ref, gh_ref, gmem_ref, from_right_ref, from_left_ref, gains_ref,
    biases_ref, grad_ref
):
    gain = gains_ref[0, pl.ds(0, 1), :]
    for n in range(seqs):
        _, scaled, inverse = norm_forward(
            frames_ref[n].astype(F32), gain, biases_ref[0, pl.ds(0, 1), :]
        )
        total, mem = merge_halo(sizes, n, gh_ref, gmem_ref, from_right_ref, from_left_ref)
        grad_ref[n] = (
            gz_ref[pl.ds(n * sizes.rows, sizes.rows), :]
            + norm_backward(total, scaled, inverse, gain)
            + segment_spread(sizes.rows, sizes.width, mem * (1.0 / SEG_LEN))
        )


def shifted(value, axis, by):
    size = lax.axis_size(axis)
    pairs = [(i, i + by) for i in range(size) if 0 <= i + by < size]
    return lax.ppermute(value, axis, pairs)


def permuted(value, move):
    reps = lax.axis_size("rep")
    pairs = []
    for flat in range(lax.axis_size("seg") * reps):
        seg, rep = divmod(flat, reps)
        z, y, x, core = move(seg // CHIPS_Y, seg % CHIPS_Y, rep // 2, rep % 2)
        pairs.append((flat, (z * CHIPS_Y + y) * reps + 2 * x + core))
    return lax.ppermute(value, ("seg", "rep"), pairs)


def across_first(value):
    return permuted(value, lambda z, y, x, c: (z, y, x ^ 1, c) if c == 0 else (z, y ^ 1, x, c))


def across_second(value):
    return permuted(value, lambda z, y, x, c: (z, y ^ 1, x, c) if c == 0 else (z, y, x ^ 1, c))


def other_core(value):
    return permuted(value, lambda z, y, x, c: (z, y, x, c ^ 1))


def after(value, *others):
    return lax.optimization_barrier((value,) + others)[0]


def swap_z(blocks):
    groups = [
        [z * CHIPS_Y + y for z in range(CHIPS_Z)] for y in range(CHIPS_Y)
    ]
    return lax.all_to_all(blocks, "seg", 0, 0, axis_index_groups=groups, tiled=True)


def gather_z(shard):
    return swap_z(jnp.broadcast_to(shard[None], (CHIPS_Z,) + shard.shape))


def gather_sides(here):
    return [here, across_first(here), across_second(here)]


def both_cores(blocks):
    return blocks + [other_core(block) for block in blocks]


def summed(*parts):
    total = parts[0].astype(F32)
    for part in parts[1:]:
        total = total + part.astype(F32)
    return total.astype(BF16)


def first_entry(array):
    return pl.BlockSpec((1,) + tuple(array.shape[1:]), lambda i: (0,) * array.ndim)


def sum_everywhere(value):
    count = lax.axis_size("seg") * lax.axis_size("rep")
    bit = 1
    while bit < count:
        value = value + lax.ppermute(value, ("seg", "rep"), [(i, i ^ bit) for i in range(count)])
        bit *= 2
    return value


def vmem_spec():
    return pl.BlockSpec(memory_space=pltpu.VMEM)


def smem_spec():
    return pl.BlockSpec(memory_space=pltpu.SMEM)


def hbm_spec():
    return pl.BlockSpec(memory_space=pl.ANY)


def call(body, in_specs, out_shapes, out_specs, scratch, args, flops=0, moved=0, grid=()):
    return pl.pallas_call(
        body,
        grid=grid,
        in_specs=in_specs,
        out_shape=tuple(jax.ShapeDtypeStruct(shape, kind) for shape, kind in out_shapes),
        out_specs=tuple(out_specs),
        scratch_shapes=scratch,
        compiler_params=pltpu.CompilerParams(vmem_limit_bytes=VMEM_BYTES),
        cost_estimate=pl.CostEstimate(flops=flops, bytes_accessed=moved, transcendentals=0),
    )(*args)


def on_device(
    frames,
    utt_segments,
    out_grad,
    qkv_weight,
    out_weight,
    ffn_in_weight,
    ffn_out_weight,
    norm_gains,
    biases,
    ffn_bias,
):
    micros, groups, rows, width = frames.shape
    seqs = micros * groups
    ff = ffn_bias.shape[1]
    reps = lax.axis_size("rep")
    seg_count = lax.axis_size("seg")
    mats = Matrices(width, ff)
    by_blocks = width // reps == LANES and reps == 4 and seg_count == BLOCKS
    first = Sizes(rows, width, ff, True)
    last = Sizes(rows, width, ff, False)
    own = seqs * rows
    mem_own = seqs * first.segs

    seg_at = lax.axis_index("seg")
    seg_base = seg_at * first.segs
    rep_at = lax.axis_index("rep")
    place = [seg_base, jnp.int32(first.segs * seg_count)]
    y_at, x_at, core_at = seg_at % CHIPS_Y, rep_at // 2, rep_at % 2
    for other in range(2):
        core = lax.bitwise_xor(core_at, other)
        for hop2 in range(2):
            for hop1 in range(2):
                x_hop = jnp.where(core == 0, hop1, hop2)
                y_hop = jnp.where(core == 0, hop2, hop1)
                place.append(lax.bitwise_xor(y_at, y_hop))
                place.append((lax.bitwise_xor(x_at, x_hop) * 2 + core) * LANES)
    place = jnp.stack([jnp.asarray(entry, jnp.int32) for entry in place])
    lengths = utt_segments.reshape(seqs, utt_segments.shape[2])
    starts = (jnp.cumsum(lengths, axis=1) - lengths).astype(jnp.int32)
    zero_bias = jnp.zeros((width,), F32)
    row_bias = jnp.stack(
        [jnp.concatenate([biases[l, 1], zero_bias, biases[l, 2]]) for l in range(LAYERS)]
    ).reshape(LAYERS, 1, 3 * width)

    frames_own = frames.reshape(seqs, rows, width)
    grads_own = out_grad.reshape(seqs, rows, width)
    far = MEM_LEN * SEG_LEN
    frames_left = shifted(frames_own[:, rows - far :], "seg", 1)
    frames_right = shifted(frames_own[:, :RIGHT_ROWS], "seg", -1)

    attn_rows, ffn_rows = mats.attn_rows, mats.ffn_rows
    if by_blocks:
        qkv_t, out_t, down_t = (
            jnp.swapaxes(member, 1, 2) for member in (qkv_weight, out_weight, ffn_out_weight)
        )
        all_rows = attn_rows + ffn_rows
        spots, halves = Spots(mats, False), Spots(mats, True)
        shards = call(
            lambda *refs: pack_kernel(spots, *refs),
            [vmem_spec()] * 4,
            [((all_rows, LANES), BF16)] * LAYERS,
            [vmem_spec()] * LAYERS,
            [],
            (qkv_t, out_t, ffn_in_weight, down_t),
        )
        sides0 = gather_sides(after(gather_z(shards[0]), frames_left, frames_right))
        sides1 = gather_sides(gather_z(after(shards[1], sides0[0])))
        first_all = both_cores(sides0 + [across_second(after(sides0[1], sides1[0]))])
        classes = len(first_all) // 2
        half_rows = CHIPS_Z * all_rows // 2
        grad_outs0 = [((classes, 2 * half_rows + SMALL_ROWS, LANES), BF16)] * 2
        grad_outs1 = [((classes, CHIPS_Z, all_rows, LANES), BF16)] * 2
        copies_in = len(first_all) * (3 + mats.down_parts)
    else:
        whole = []
        for member, shape in zip(
            (qkv_weight, out_weight, ffn_in_weight, ffn_out_weight),
            (mats.qkv, mats.out, mats.up, mats.down),
        ):
            member = lax.all_gather(member, "rep", axis=1, tiled=True)
            member = lax.all_gather(member, "seg", axis=2, tiled=True)
            whole.append(jnp.swapaxes(member, 1, 2).reshape((LAYERS,) + shape))
        first_all = [member[0] for member in whole]
        last_all = [member[1] for member in whole]
        spots = halves = None
        grad_outs0 = grad_outs1 = [
            (shape, BF16) for shape in (mats.qkv, mats.out, mats.up, mats.down)
        ]
        copies_in = 4
    dma = pltpu.SemaphoreType.DMA

    matrices = [pltpu.VMEM(shape, BF16) for shape in (mats.qkv, mats.out, mats.up, mats.down)]

    (
        z0, proj0, probs0, att0, mixed0, mem1, x1, active0, slope0, low1, send_right, send_left,
    ) = call(
        lambda *refs: first_layer_kernel(
            first, seqs, mats, spots, len(first_all), *refs
        ),
        [smem_spec()] * 2 + [vmem_spec()] * 7 + [hbm_spec()] * len(first_all),
        [
            ((seqs * first.ext, width), BF16),
            ((seqs * first.ext, 3 * width), BF16),
            ((seqs * first.pairs, 2 * first.queries, first.keys), BF16),
            ((seqs * first.queries, width), BF16),
            ((own, width), F32),
            ((mem_own, width), F32),
            ((own, width), F32),
            ((own, ff), BF16),
            ((own, ff), BF16),
            ((own, width), BF16),
            ((seqs, BACK_ROWS, width), BF16),
            ((seqs, RIGHT_ROWS, width), BF16),
        ],
        [vmem_spec()] * 12,
        matrices
        + [
            pltpu.VMEM((seqs, first.queries, first.keys), F32),
            pltpu.VMEM((own, width), BF16),
            dma((copies_in,)),
        ],
        (place, starts, frames_own, frames_left, frames_right, norm_gains, biases, ffn_bias,
         row_bias[0]) + tuple(first_all),
        flops=24 * own * (4 * width * width + 2 * width * ff) // 2,
        moved=2 * (4 * width * width + 2 * width * ff),
    )
    left1 = shifted(send_right, "seg", 1)
    right1 = shifted(send_left, "seg", -1)
    if by_blocks:
        last_side = across_second(after(sides1[1], sides1[2], low1))
        last_all = both_cores(sides1 + [last_side])
        last_all[-1] = other_core(after(last_side, left1, right1))

    vec_shape = (TILE, width)
    outs = call(
        lambda *refs: last_layer_kernel(
            last, seqs, mats, spots, len(last_all), len(grad_outs1), *refs
        ),
        [smem_spec()] * 2 + [vmem_spec()] * 10 + [hbm_spec()] * len(last_all),
        [
            ((seqs, rows, width), F32),
            ((own, width), F32),
            ((own, width), F32),
            ((mem_own, width), F32),
            ((seqs, BACK_ROWS, width), BF16),
            ((seqs, RIGHT_ROWS, width), BF16),
            (vec_shape, F32),
        ]
        + grad_outs1,
        [vmem_spec()] * 7 + [hbm_spec()] * len(grad_outs1),
        matrices
        + matrices
        + [
            pltpu.VMEM((seqs, last.queries, last.keys), F32),
            pltpu.VMEM((seqs * last.ext, width), BF16),
            pltpu.VMEM((seqs * last.ext, 3 * width), BF16),
            pltpu.VMEM((seqs * last.pairs, 2 * last.queries, last.keys), BF16),
            pltpu.VMEM((seqs * last.queries, width), BF16),
            pltpu.VMEM((own, width), BF16),
            pltpu.VMEM((seqs * last.queries, width), BF16),
            pltpu.VMEM((seqs * last.ext, 3 * width), BF16),
            pltpu.VMEM((seqs * last.queries, width), BF16),
            pltpu.VMEM((own, width), BF16),
            pltpu.VMEM((own, width), F32),
            dma((2 * copies_in,)),
        ],
        (place, starts, low1, left1, right1, mem1, x1, grads_own, norm_gains, biases, ffn_bias,
         row_bias[1]) + tuple(last_all),
        flops=30 * own * (4 * width * width + 2 * width * ff),
        moved=4 * (4 * width * width + 2 * width * ff),
    )
    encoded, gz1, gh1, gmem1, back_left1, back_right1, vec1 = outs[:7]
    grad_blocks1 = outs[7:]
    from_right1 = shifted(back_left1, "seg", -1)
    from_left1 = shifted(back_right1, "seg", 1)

    gh1_tied = gh1
    if by_blocks:
        mine1, theirs1 = grad_blocks1[0], other_core(grad_blocks1[1])
        far1 = after(summed(mine1[2:], theirs1[2:]), from_right1, from_left1)
        gh1_tied = after(gh1, far1)
    gz0, gh0, gmem0, back_left0, back_right0, upper_vec, vec0, *grad_blocks0 = call(
        lambda *refs: first_back_kernel(
            last, first, seqs, mats, spots, halves, len(first_all), len(grad_outs0), *refs
        ),
        [smem_spec()] + [vmem_spec()] * 19 + [hbm_spec()] * len(first_all),
        [
            ((own, width), F32),
            ((own, width), F32),
            ((mem_own, width), F32),
            ((seqs, BACK_ROWS, width), BF16),
            ((seqs, RIGHT_ROWS, width), BF16),
            (vec_shape, F32),
            (vec_shape, F32),
        ]
        + grad_outs0,
        [vmem_spec()] * 7 + [hbm_spec()] * len(grad_outs0),
        matrices
        + matrices
        + [
            pltpu.VMEM((own, width), BF16),
            pltpu.VMEM((own, width), BF16),
            pltpu.VMEM((own, width), F32),
            pltpu.VMEM((own, width), F32),
            pltpu.VMEM((mem_own, width), F32),
            pltpu.VMEM((seqs * first.queries, width), BF16),
            pltpu.VMEM((seqs * first.ext, 3 * width), BF16),
            pltpu.VMEM((seqs * first.queries, width), BF16),
            pltpu.VMEM((SMALL_ROWS, LANES), BF16),
            dma((2 * copies_in + 8,)),
        ],
        (place, x1, gz1, gh1_tied, gmem1, from_right1, from_left1, mixed0, active0, slope0, att0,
         probs0, proj0, z0, frames_own, frames_left, frames_right, norm_gains, biases, vec1)
        + tuple(first_all),
        flops=28 * own * (4 * width * width + 2 * width * ff),
        moved=4 * (4 * width * width + 2 * width * ff),
    )
    from_right0 = shifted(back_left0, "seg", -1)
    from_left0 = shifted(back_right0, "seg", 1)
    gz0_last = gz0
    if by_blocks:
        second1 = across_second(far1)
        near1 = summed(mine1[1], theirs1[1], second1[1])
        first1 = across_first(near1)
        mine0, theirs0 = grad_blocks0[0], other_core(after(grad_blocks0[1], second1))
        half0, half1 = slice(0, half_rows), slice(half_rows, None)
        far_a = after(summed(mine0[2:, half0], theirs0[2:, half0]), near1)
        second_a = across_second(far_a)
        far_b = after(summed(mine0[2:, half1], theirs0[2:, half1]), near1)
        second_b = across_second(far_b)
        total1 = summed(mine1[0], theirs1[0], second1[0], after(first1, far_a, far_b))
        last_parts = swap_z(total1)
        gz0_last = after(gz0, total1)
    frames_grad = call(
        lambda *refs: frames_grad_kernel(first, seqs, *refs),
        [vmem_spec()] * 8,
        [((seqs, rows, width), F32)],
        [vmem_spec()],
        [],
        (frames_own, gz0_last, gh0, gmem0, from_right0, from_left0, norm_gains, biases),
    )[0]

    if by_blocks:
        mid_a = summed(mine0[1, half0], theirs0[1, half0], second_a[1])
        first_a = across_first(mid_a)
        second_b = after(second_b, frames_grad, last_parts)
        mid_b = summed(mine0[1, half1], theirs0[1, half1], second_b[1])
        first_b = across_first(mid_b)
        near_a = summed(mine0[0, half0], theirs0[0, half0], second_a[0], first_a)
        parts_a = swap_z(near_a.reshape(CHIPS_Z, -1, LANES))
        near_b = [mine0[:1, half1], theirs0[:1, half1], second_b, first_b]
        parts_b = swap_z(
            call(
                lambda *refs: near_small_kernel(CHIPS_Z, *refs),
                [vmem_spec()] * 2 + [first_entry(second_b), vmem_spec()],
                [((CHIPS_Z, half_rows // CHIPS_Z + SMALL_ROWS, LANES), BF16)],
                [vmem_spec()],
                [],
                near_b,
                grid=(1,),
            )[0]
        )
        shapes = [member.shape for member in (qkv_t, out_t, ffn_in_weight, down_t)]
        shapes += [norm_gains.shape, (biases.shape[1], LAYERS, width), ffn_bias.shape]
        reduced = call(
            lambda *refs: unpack_kernel(
                [halves, spots], (1, half_rows // CHIPS_Z), *refs
            ),
            [vmem_spec()] * 3,
            [(shape, F32) for shape in shapes],
            [vmem_spec()] * len(shapes),
            [],
            [parts_a, parts_b, last_parts],
        )
        small = reduced[4], jnp.swapaxes(reduced[5], 0, 1), reduced[6]
        reduced = [
            jnp.swapaxes(reduced[0], 1, 2),
            jnp.swapaxes(reduced[1], 1, 2),
            reduced[2],
            jnp.swapaxes(reduced[3], 1, 2),
        ]
    else:
        reduced = []
        for member0, member1 in zip(grad_blocks0, grad_blocks1):
            both = jnp.stack([member0, member1]).reshape(LAYERS, -1, member0.shape[3])
            both = jnp.swapaxes(both, 1, 2)
            both = lax.psum_scatter(both, "seg", scatter_dimension=2, tiled=True)
            both = lax.psum_scatter(both, "rep", scatter_dimension=1, tiled=True)
            reduced.append(both.astype(F32))
        small = sum_everywhere(jnp.stack([vec0, vec1 + upper_vec]))
        small = small[:, 0:2], small[:, 2:8], small[:, 8:12].reshape(ffn_bias.shape)

    return (
        encoded.reshape(frames.shape),
        frames_grad.reshape(frames.shape),
        reduced[0],
        reduced[1],
        reduced[2],
        reduced[3],
        small[0],
        small[1],
        small[2],
    )


def solution(mesh):
    in_specs = (
        P(None, "rep", "seg", None),
        P(None, "rep", None),
        P(None, "rep", "seg", None),
        P(None, "rep", "seg"),
        P(None, "rep", "seg"),
        P(None, "rep", "seg"),
        P(None, "rep", "seg"),
        P(),
        P(),
        P(),
    )
    out_specs = (
        P(None, "rep", "seg", None),
        P(None, "rep", "seg", None),
        P(None, "rep", "seg"),
        P(None, "rep", "seg"),
        P(None, "rep", "seg"),
        P(None, "rep", "seg"),
        P(),
        P(),
        P(),
    )
    return jax.shard_map(
        on_device, mesh=mesh, in_specs=in_specs, out_specs=out_specs, check_vma=False
    )
```

```python
import jax
import jax.numpy as jnp
from jax import lax
from jax.experimental import pallas as pl
from jax.experimental.pallas import tpu as pltpu
from jax.sharding import PartitionSpec as P

HEADS = 8
SEG_LEN = 16
LEFT_LEN = 30
RIGHT_LEN = 4
MEM_LEN = 4
LAYERS = 2

EPS = 1e-05
ROOT_HALF = 0.7071067811865476
INV_ROOT_TWO_PI = 0.3989422804014327

LANES = 128
TILE = 16
RIGHT_ROWS = 16
LEFT_ROWS = 32
MEM_ROWS = 16
BACK_ROWS = LEFT_ROWS + MEM_ROWS
CHIPS_Z = 4
CHIPS_Y = 2
BLOCKS = CHIPS_Z * CHIPS_Y
SMALL_ROWS = 128
VMEM_BYTES = 56 * 1024 * 1024

BF16 = jnp.bfloat16
F32 = jnp.float32


def nn(a, b):
    return lax.dot_general(a, b, (((1,), (0,)), ((), ())), preferred_element_type=F32)


def nt(a, b):
    return lax.dot_general(a, b, (((1,), (1,)), ((), ())), preferred_element_type=F32)


def tn(a, b):
    return lax.dot_general(a, b, (((0,), (0,)), ((), ())), preferred_element_type=F32)


def col_sum(value):
    return jnp.sum(value, axis=0, keepdims=True)


def norm_forward(inputs, gain, bias):
    center = inputs - jnp.mean(inputs, axis=1, keepdims=True)
    inverse = lax.rsqrt(jnp.mean(center * center, axis=1, keepdims=True) + EPS)
    scaled = center * inverse
    return scaled * gain + bias, scaled, inverse


def norm_backward(grad_in, scaled, inverse, gain):
    grad_scaled = grad_in * gain
    return inverse * (
        grad_scaled
        - jnp.mean(grad_scaled, axis=1, keepdims=True)
        - scaled * jnp.mean(grad_scaled * scaled, axis=1, keepdims=True)
    )


def segment_mean(inputs):
    rows, width = inputs.shape
    return jnp.mean(inputs.reshape(rows // SEG_LEN, SEG_LEN, width), axis=1)


def segment_spread(rows, width, per_segment):
    segs = rows // SEG_LEN
    return jnp.broadcast_to(per_segment[:, None, :], (segs, SEG_LEN, width)).reshape(rows, width)


def identity(size):
    row = lax.broadcasted_iota(jnp.int32, (size, size), 0)
    col = lax.broadcasted_iota(jnp.int32, (size, size), 1)
    return (row == col).astype(F32).astype(BF16)


class Sizes:
    def __init__(self, rows, width, ff, with_summary):
        self.rows = rows
        self.width = width
        self.ff = ff
        self.segs = rows // SEG_LEN
        self.top = TILE if with_summary else 0
        self.keys = rows + RIGHT_ROWS + LEFT_ROWS + MEM_ROWS
        self.ext = self.top + self.keys
        self.queries = self.top + rows
        self.right_at = self.top + rows
        self.left_at = self.right_at + RIGHT_ROWS
        self.mem_at = self.left_at + LEFT_ROWS
        self.pairs = width // LANES


class Matrices:
    def __init__(self, width, ff):
        self.qkv = (CHIPS_Z, CHIPS_Y, 3 * width // BLOCKS, width)
        self.out = (CHIPS_Z, CHIPS_Y, width // BLOCKS, width)
        self.up = (CHIPS_Z, CHIPS_Y, ff // BLOCKS, width)
        self.down = (CHIPS_Z, CHIPS_Y, width // BLOCKS, ff)
        self.down_parts = ff // width
        self.attn_rows = self.qkv[2] + self.out[2]
        self.ffn_rows = self.up[2] + self.down_parts * self.down[2]


class Spots:
    def __init__(self, mats, halves):
        high, wide, up, low = mats.qkv[2], mats.out[2], mats.up[2], mats.down[2]
        parts = range(mats.down_parts)
        if halves:
            split = mats.down_parts // 2
            self.up = (0, 0)
            self.qkv = (1, 0)
            self.out = (1, high)
            self.down = [
                (0, up + low * j) if j < split else (1, high + wide + low * (j - split))
                for j in parts
            ]
        else:
            self.qkv = (0, 0)
            self.out = (0, high)
            self.up = (0, high + wide)
            self.down = [(0, high + wide + up + low * j) for j in parts]


def attn_pairs(mats, spots, groups, qkv_ref, out_ref, place_ref):
    if spots is None:
        return [(groups[0], qkv_ref), (groups[1], out_ref)]
    pairs = []
    for k in range(len(groups[0])):
        row = place_ref[2 + 2 * k]
        lane = pl.multiple_of(place_ref[3 + 2 * k], LANES)
        for (group, first), ref, shape in (
            (spots.qkv, qkv_ref, mats.qkv),
            (spots.out, out_ref, mats.out),
        ):
            block = groups[group][k]
            pairs.append(
                (
                    block.at[:, pl.ds(first, shape[2]), :],
                    ref.at[:, row, :, pl.ds(lane, LANES)],
                )
            )
    return pairs


def ffn_pairs(mats, spots, groups, up_ref, down_ref, place_ref):
    if spots is None:
        return [(groups[2], up_ref), (groups[3], down_ref)]
    pairs = []
    for k in range(len(groups[0])):
        row = place_ref[2 + 2 * k]
        lane = pl.multiple_of(place_ref[3 + 2 * k], LANES)
        group, first = spots.up
        block = groups[group][k]
        pairs.append(
            (block.at[:, pl.ds(first, mats.up[2]), :], up_ref.at[:, row, :, pl.ds(lane, LANES)])
        )
        for part, (group, first) in enumerate(spots.down):
            there = pl.multiple_of(
                place_ref[3 + 2 * k] * mats.down_parts + part * LANES, LANES
            )
            block = groups[group][k]
            pairs.append(
                (
                    block.at[:, pl.ds(first, mats.down[2]), :],
                    down_ref.at[:, row, :, pl.ds(there, LANES)],
                )
            )
    return pairs


def start_in(pairs, sems, at):
    copies = [pltpu.make_async_copy(s, d, sems.at[at + i]) for i, (s, d) in enumerate(pairs)]
    for copy in copies:
        copy.start()
    return copies


def start_out(pairs, sems, at):
    copies = [pltpu.make_async_copy(d, s, sems.at[at + i]) for i, (s, d) in enumerate(pairs)]
    for copy in copies:
        copy.start()
    return copies


def in_groups(spots, refs):
    return refs if spots is None else [refs]


def wait_all(copies):
    for copy in copies:
        copy.wait()


def fill_mask(sizes, seqs, starts_ref, place_ref, mask_ref):
    shape = (sizes.queries, sizes.keys)
    row = lax.broadcasted_iota(jnp.int32, shape, 0)
    col = lax.broadcasted_iota(jnp.int32, shape, 1)
    base = place_ref[0]
    total = place_ref[1]
    query = jnp.where(row < sizes.top, row, lax.shift_right_arithmetic(row - sizes.top, 4))
    left_at = sizes.rows + RIGHT_ROWS
    mem_at = left_at + LEFT_ROWS
    spot = jnp.where(col < left_at, col, col - mem_at)
    mem_seg = jnp.where(col < mem_at + sizes.segs, col - mem_at, col - mem_at - 2 * sizes.segs)
    key_seg = jnp.where(col < mem_at, lax.shift_right_arithmetic(spot, 4), mem_seg)
    near = (
        (key_seg == query)
        | ((spot >= query * SEG_LEN - LEFT_LEN) & (spot < query * SEG_LEN))
        | ((key_seg == query + 1) & (spot < query * SEG_LEN + SEG_LEN + RIGHT_LEN))
    )
    recent = (key_seg >= query - MEM_LEN) & (key_seg < query) & (row >= sizes.top)
    allowed = ((col < mem_at) & near) | ((col >= mem_at) & recent)
    key_abs = key_seg + base
    query_abs = query + base
    allowed = allowed & (key_abs >= 0) & (key_abs < total)
    if sizes.top:
        allowed = allowed & ((row < sizes.segs) | (row >= sizes.top))
    for n in range(seqs):
        key_owner = jnp.zeros(shape, jnp.int32)
        query_owner = jnp.zeros(shape, jnp.int32)
        for u in range(starts_ref.shape[1]):
            first = starts_ref[n, u]
            key_owner = key_owner + (key_abs >= first).astype(jnp.int32)
            query_owner = query_owner + (query_abs >= first).astype(jnp.int32)
        mask_ref[n] = jnp.where(allowed & (key_owner == query_owner), 0.0, -1e30)


def half_masks():
    lane = lax.broadcasted_iota(jnp.int32, (1, LANES), 1)
    even = (lane < LANES // 2).astype(F32)
    return even.astype(BF16), (1.0 - even).astype(BF16), lane < LANES // 2


def project(sizes, z_ref, qkv_ref, row_bias_ref, proj_ref):
    step = CHIPS_Z // 2
    for c in range(2):
        block = qkv_ref[pl.ds(c * step, step)].reshape(-1, sizes.width)
        wide = block.shape[0]
        made = nt(z_ref[...], block) + row_bias_ref[:, pl.ds(c * wide, wide)]
        proj_ref[:, pl.ds(c * wide, wide)] = made.astype(BF16)


def attend(sizes, seqs, proj_ref, mask_ref, probs_ref, att_ref):
    even, odd, is_even = half_masks()
    scale = (sizes.width // HEADS) ** (-0.5)
    count = sizes.queries

    def body(p, carry):
        for n in range(seqs):
            lane = pl.multiple_of(p * LANES, LANES)
            query = proj_ref[pl.ds(n * sizes.ext, count), pl.ds(lane, LANES)]
            first = n * sizes.ext + sizes.top
            key = proj_ref[pl.ds(first, sizes.keys), pl.ds(sizes.width + lane, LANES)]
            value = proj_ref[pl.ds(first, sizes.keys), pl.ds(2 * sizes.width + lane, LANES)]
            scores = nt(jnp.concatenate([query * even, query * odd], axis=0), key) * scale
            outs = []
            for half in range(2):
                part = scores[half * count : (half + 1) * count] + mask_ref[n]
                part = jnp.exp(part - jnp.max(part, axis=1, keepdims=True))
                part = (part * (1.0 / jnp.sum(part, axis=1, keepdims=True))).astype(BF16)
                probs_ref[n * sizes.pairs + p, pl.ds(half * count, count), :] = part
                outs.append(nn(part, value))
            att_ref[pl.ds(n * count, count), pl.ds(lane, LANES)] = jnp.where(
                is_even, outs[0], outs[1]
            ).astype(BF16)
        return carry

    lax.fori_loop(0, sizes.pairs, body, 0)


def attend_back(sizes, seqs, proj_ref, probs_ref, go_ref, gproj_ref):
    even, odd, is_even = half_masks()
    scale = (sizes.width // HEADS) ** (-0.5)
    count = sizes.queries
    wide = sizes.width
    for n in range(seqs):
        base = n * sizes.ext
        rest = sizes.ext - count
        gproj_ref[pl.ds(base + count, rest), pl.ds(0, wide)] = jnp.zeros((rest, wide), BF16)
        if sizes.top:
            gproj_ref[pl.ds(base, sizes.top), pl.ds(wide, 2 * wide)] = jnp.zeros(
                (sizes.top, 2 * wide), BF16
            )

    def body(p, carry):
        for n in range(seqs):
            lane = pl.multiple_of(p * LANES, LANES)
            base = n * sizes.ext
            first = base + sizes.top
            query = proj_ref[pl.ds(base, count), pl.ds(lane, LANES)]
            key = proj_ref[pl.ds(first, sizes.keys), pl.ds(wide + lane, LANES)]
            value = proj_ref[pl.ds(first, sizes.keys), pl.ds(2 * wide + lane, LANES)]
            grad = go_ref[pl.ds(n * count, count), pl.ds(lane, LANES)]
            queries = jnp.concatenate([query * even, query * odd], axis=0)
            grads = jnp.concatenate([grad * even, grad * odd], axis=0)
            probs_low = probs_ref[n * sizes.pairs + p]
            grad_values = tn(probs_low, grads)
            probs = probs_low.astype(F32)
            grad_probs = nt(grads, value)
            weighted = grad_probs * probs
            grad_scores = (
                (weighted - probs * jnp.sum(weighted, axis=1, keepdims=True)) * scale
            ).astype(BF16)
            grad_keys = tn(grad_scores, queries)
            grad_query = jnp.where(
                is_even, nn(grad_scores[:count], key), nn(grad_scores[count:], key)
            )
            gproj_ref[pl.ds(base, count), pl.ds(lane, LANES)] = grad_query.astype(BF16)
            gproj_ref[pl.ds(first, sizes.keys), pl.ds(wide + lane, LANES)] = grad_keys.astype(BF16)
            gproj_ref[pl.ds(first, sizes.keys), pl.ds(2 * wide + lane, LANES)] = (
                grad_values.astype(BF16)
            )
        return carry

    lax.fori_loop(0, sizes.pairs, body, 0)


def gelu_both(upward):
    half = 0.5 * (1.0 + lax.erf(upward * ROOT_HALF))
    slope = half + upward * jnp.exp(-0.5 * upward * upward) * INV_ROOT_TWO_PI
    return upward * half, slope


def up_block(up_ref, c, wide):
    step = wide // (up_ref.shape[1] * up_ref.shape[2])
    return up_ref[pl.ds(c * step, step)].reshape(-1, up_ref.shape[3])


def down_block(down_ref, c, wide):
    at = pl.multiple_of(c * wide, wide)
    return down_ref[:, :, :, pl.ds(at, wide)].reshape(-1, wide)


def ffn_back_step(
    sizes, c, wide, grad_low, hidden_low, active, slope, up_ref, down_ref, gup_ref, gdown_ref, vec
):
    at = pl.multiple_of(c * wide, wide)
    up = up_block(up_ref, c, wide)
    down = down_block(down_ref, c, wide)
    grad_active = nn(grad_low, down)
    grad_up_f = grad_active * slope
    grad_up = grad_up_f.astype(BF16)
    gdown_ref[:, :, :, pl.ds(at, wide)] = (
        tn(grad_low, active).astype(BF16).reshape(gdown_ref.shape[:3] + (wide,))
    )
    step = wide // (gup_ref.shape[1] * gup_ref.shape[2])
    gup_ref[pl.ds(c * step, step)] = (
        tn(grad_up, hidden_low).astype(BF16).reshape((step,) + gup_ref.shape[1:])
    )
    vec[pl.ds(8 + c, 1), :] = col_sum(grad_up.astype(F32))
    return nn(grad_up, up)


def attn_back_stage(
    sizes, seqs, gz, grad_mem_ref, att_ref, proj_ref, probs_ref, z_ref, qkv_ref, out_ref,
    gqkv_ref, gout_ref, go_ref, gproj_ref, branch_ref, vec, gh_ref, gmem_ref, back_left_ref,
    back_right_ref, scaled_rows=None,
):
    wide = sizes.width
    count = sizes.queries
    bias_out = col_sum(gz)
    for n in range(seqs):
        if sizes.top:
            mem_grad = grad_mem_ref[pl.ds(n * sizes.segs, sizes.segs), :]
            bias_out = bias_out + col_sum(mem_grad)
            branch_ref[pl.ds(n * count, sizes.top), :] = jnp.concatenate(
                [mem_grad, jnp.zeros((sizes.top - sizes.segs, wide), F32)], axis=0
            ).astype(BF16)
        branch_ref[pl.ds(n * count + sizes.top, sizes.rows), :] = gz[
            n * sizes.rows : (n + 1) * sizes.rows
        ].astype(BF16)
    vec[pl.ds(5, 1), :] = bias_out
    branch = branch_ref[...]
    gout_ref[...] = tn(branch, att_ref[...]).astype(BF16).reshape(gout_ref.shape)
    go_ref[...] = nn(branch, out_ref[...].reshape(-1, wide)).astype(BF16)
    attend_back(sizes, seqs, proj_ref, probs_ref, go_ref, gproj_ref)
    vec[pl.ds(3, 1), :] = col_sum(gproj_ref[:, pl.ds(0, wide)].astype(F32))
    vec[pl.ds(4, 1), :] = col_sum(gproj_ref[:, pl.ds(2 * wide, wide)].astype(F32))
    grad_ext = nn(gproj_ref[...], qkv_ref[...].reshape(-1, wide))
    gain_sum = jnp.zeros((1, wide), F32)
    bias_sum = jnp.zeros((1, wide), F32)
    for n in range(seqs):
        base = n * sizes.ext
        own = grad_ext[base + sizes.top : base + sizes.top + sizes.rows]
        if sizes.top:
            spread = grad_ext[base : base + sizes.segs] * (1.0 / SEG_LEN)
            own = own + segment_spread(sizes.rows, wide, spread)
        gh_ref[pl.ds(n * sizes.rows, sizes.rows), :] = own
        mem = base + sizes.mem_at
        gmem_ref[pl.ds(n * sizes.segs, sizes.segs), :] = grad_ext[mem : mem + sizes.segs]
        left = base + sizes.left_at
        back_left_ref[n] = grad_ext[left : left + BACK_ROWS].astype(BF16)
        right = base + sizes.right_at
        back_right_ref[n] = grad_ext[right : right + RIGHT_ROWS].astype(BF16)
        if scaled_rows is not None:
            grads = (
                own,
                grad_ext[right : right + RIGHT_ROWS],
                grad_ext[left : left + LEFT_ROWS],
            )
            for rows, scaled in zip(grads, scaled_rows(n)):
                gain_sum = gain_sum + col_sum(rows * scaled)
                bias_sum = bias_sum + col_sum(rows)
    if scaled_rows is not None:
        vec[pl.ds(0, 1), :] = gain_sum
        vec[pl.ds(2, 1), :] = bias_sum
    step = CHIPS_Z // 2
    part = gqkv_ref.shape[1] * gqkv_ref.shape[2] * step
    for c in range(2):
        gqkv_ref[pl.ds(c * step, step)] = (
            tn(gproj_ref[:, pl.ds(c * part, part)], z_ref[...])
            .astype(BF16)
            .reshape((step,) + gqkv_ref.shape[1:])
        )


def merge_halo(sizes, n, gh_ref, gmem_ref, from_right_ref, from_left_ref):
    first = n * sizes.rows
    back = from_right_ref[n].astype(F32)
    head = gh_ref[pl.ds(first, RIGHT_ROWS), :] + from_left_ref[n].astype(F32)
    middle = gh_ref[pl.ds(first + RIGHT_ROWS, sizes.rows - RIGHT_ROWS - LEFT_ROWS), :]
    tail = gh_ref[pl.ds(first + sizes.rows - LEFT_ROWS, LEFT_ROWS), :] + back[:LEFT_ROWS]
    mem = gmem_ref[pl.ds(n * sizes.segs, sizes.segs), :] + back[LEFT_ROWS + sizes.segs :]
    return jnp.concatenate([head, middle, tail], axis=0), mem


def pack_kernel(spots, qkv_ref, out_ref, up_ref, down_ref, *packed):
    eye = identity(LANES)
    high, wide, low = qkv_ref.shape[1], out_ref.shape[1], down_ref.shape[1]
    for layer, ref in enumerate(packed):
        up = tn(up_ref[layer], eye).astype(BF16)
        for z in range(ref.shape[0]):
            ref[z, pl.ds(spots.qkv[1], high), :] = qkv_ref[layer]
            ref[z, pl.ds(spots.out[1], wide), :] = out_ref[layer]
            ref[z, pl.ds(spots.up[1], up_ref.shape[2]), :] = up
            for part, (_, first) in enumerate(spots.down):
                ref[z, pl.ds(first, low), :] = down_ref[layer, :, pl.ds(part * LANES, LANES)]


def unpack_kernel(layers, small_at, *refs):
    sources, outs = refs[:-7], refs[-7:]
    qkv_ref, out_ref, up_ref, down_ref, gains_ref, biases_ref, ffn_bias_ref = outs
    eye = identity(LANES)
    high, wide, low = qkv_ref.shape[1], out_ref.shape[1], down_ref.shape[1]

    def total(source, first, rows):
        ref = sources[source]
        value = ref[0, pl.ds(first, rows), :].astype(F32)
        for z in range(1, ref.shape[0]):
            value = value + ref[z, pl.ds(first, rows), :].astype(F32)
        return value

    base = 0
    for layer, spots in enumerate(layers):
        qkv_ref[layer] = total(base + spots.qkv[0], spots.qkv[1], high)
        out_ref[layer] = total(base + spots.out[0], spots.out[1], wide)
        up_ref[layer] = nt(
            eye, total(base + spots.up[0], spots.up[1], up_ref.shape[2]).astype(BF16)
        )
        for part, (group, first) in enumerate(spots.down):
            down_ref[layer, :, pl.ds(part * LANES, LANES)] = total(base + group, first, low)
        base += 1 + max(group for group, _ in spots.down)
    sums = total(small_at[0], small_at[1], SMALL_ROWS)
    parts = gains_ref.shape[2] // LANES
    for layer in range(gains_ref.shape[0]):
        for part in range(parts):
            lanes = pl.ds(part * LANES, LANES)
            block = sums[(layer * parts + part) * TILE : (layer * parts + part + 1) * TILE]
            gains_ref[layer, :, lanes] = block[0:2]
            for row in range(biases_ref.shape[0]):
                biases_ref[row, pl.ds(layer, 1), lanes] = block[2 + row : 3 + row]
            for row in range(ffn_bias_ref.shape[1] // gains_ref.shape[2]):
                at = row * gains_ref.shape[2] + part * LANES
                ffn_bias_ref[pl.ds(layer, 1), pl.ds(at, LANES)] = block[8 + row : 9 + row]


def near_small_kernel(count, mine_ref, theirs_ref, second_ref, first_ref, out_ref):
    rows = out_ref.shape[1] - SMALL_ROWS

    def total(at, size):
        group = pl.ds(at, size)
        value = mine_ref[0, group, :].astype(F32) + theirs_ref[0, group, :].astype(F32)
        return (
            value + second_ref[0, group, :].astype(F32) + first_ref[group, :].astype(F32)
        ).astype(BF16)

    small = total(count * rows, SMALL_ROWS)
    for z in range(count):
        out_ref[z, pl.ds(0, rows), :] = total(z * rows, rows)
        out_ref[z, pl.ds(rows, SMALL_ROWS), :] = small


def first_layer_kernel(
    sizes, seqs, mats, spots, count_in, place_ref, starts_ref, frames_ref, left_ref, right_ref,
    gains_ref, biases_ref, ffn_bias_ref, row_bias_ref, *refs
):
    groups = in_groups(spots, refs[:count_in])
    (
        z_ref, proj_ref, probs_ref, att_ref, mixed_ref, mem_ref, next_ref, active_ref, slope_ref,
        low_ref, send_right_ref, send_left_ref, qkv_ref, out_ref, up_ref, down_ref, mask_ref,
        hidden_ref, sems,
    ) = refs[count_in:]
    wide = sizes.width
    copies = start_in(attn_pairs(mats, spots, groups, qkv_ref, out_ref, place_ref), sems, 0)
    ffn_copies = start_in(
        ffn_pairs(mats, spots, groups, up_ref, down_ref, place_ref), sems, len(copies)
    )
    gain = gains_ref[0, pl.ds(0, 1), :]
    bias = biases_ref[0, pl.ds(0, 1), :]
    pad = jnp.zeros((TILE - sizes.segs, wide), F32)
    for n in range(seqs):
        own = frames_ref[n].astype(F32)
        before = left_ref[n].astype(F32)
        hidden = norm_forward(own, gain, bias)[0]
        halo = norm_forward(before[before.shape[0] - LEFT_ROWS :], gain, bias)[0]
        after = norm_forward(right_ref[n].astype(F32), gain, bias)[0]
        memory = jnp.concatenate(
            [
                segment_mean(own),
                jnp.zeros((sizes.segs - before.shape[0] // SEG_LEN, wide), F32),
                segment_mean(before),
            ],
            axis=0,
        )
        base = n * sizes.ext
        z_ref[pl.ds(base, sizes.top), :] = jnp.concatenate(
            [segment_mean(hidden), pad], axis=0
        ).astype(BF16)
        z_ref[pl.ds(base + sizes.top, sizes.rows), :] = hidden.astype(BF16)
        z_ref[pl.ds(base + sizes.right_at, RIGHT_ROWS), :] = after.astype(BF16)
        z_ref[pl.ds(base + sizes.left_at, LEFT_ROWS), :] = halo.astype(BF16)
        z_ref[pl.ds(base + sizes.mem_at, MEM_ROWS), :] = memory.astype(BF16)
    fill_mask(sizes, seqs, starts_ref, place_ref, mask_ref)
    wait_all(copies)
    project(sizes, z_ref, qkv_ref, row_bias_ref, proj_ref)
    attend(sizes, seqs, proj_ref, mask_ref, probs_ref, att_ref)
    mixed = nt(att_ref[...], out_ref[...].reshape(-1, wide)) + biases_ref[0, pl.ds(3, 1), :]
    for n in range(seqs):
        base = n * sizes.queries
        mem_ref[pl.ds(n * sizes.segs, sizes.segs), :] = mixed[base : base + sizes.segs]
        mixed_ref[pl.ds(n * sizes.rows, sizes.rows), :] = (
            frames_ref[n].astype(F32) + mixed[base + sizes.top : base + sizes.top + sizes.rows]
        )
    mixed = mixed_ref[...]
    hidden, _, _ = norm_forward(mixed, gains_ref[0, pl.ds(1, 1), :], biases_ref[0, pl.ds(4, 1), :])
    hidden_ref[...] = hidden.astype(BF16)
    next_ref[...] = mixed + biases_ref[0, pl.ds(5, 1), :]
    wait_all(ffn_copies)

    def body(c, carry):
        at_lane = pl.multiple_of(c * wide, wide)
        upward = nt(hidden_ref[...], up_block(up_ref, c, wide))
        upward = upward + ffn_bias_ref[pl.ds(0, 1), pl.ds(at_lane, wide)]
        active, slope = gelu_both(upward)
        active = active.astype(BF16)
        active_ref[:, pl.ds(at_lane, wide)] = active
        slope_ref[:, pl.ds(at_lane, wide)] = slope.astype(BF16)
        next_ref[...] += nt(active, down_block(down_ref, c, wide))
        return carry

    lax.fori_loop(0, sizes.ff // wide, body, 0)
    low, _, _ = norm_forward(
        next_ref[...], gains_ref[1, pl.ds(0, 1), :], biases_ref[1, pl.ds(0, 1), :]
    )
    low = low.astype(BF16)
    low_ref[...] = low
    for n in range(seqs):
        base = n * sizes.rows
        send_right_ref[n, pl.ds(0, LEFT_ROWS), :] = low[
            base + sizes.rows - LEFT_ROWS : base + sizes.rows
        ]
        send_right_ref[n, pl.ds(LEFT_ROWS, MEM_ROWS), :] = jnp.concatenate(
            [
                mem_ref[pl.ds(n * sizes.segs, sizes.segs), :],
                jnp.zeros((MEM_ROWS - sizes.segs, wide), F32),
            ],
            axis=0,
        ).astype(BF16)
        send_left_ref[n] = low[base : base + RIGHT_ROWS]


def last_layer_kernel(
    sizes, seqs, mats, spots, count_in, count_out, place_ref, starts_ref, low_ref, left_ref,
    right_ref, mem_ref, inputs_ref, out_grad_ref, gains_ref, biases_ref, ffn_bias_ref,
    row_bias_ref, *refs
):
    groups = in_groups(spots, refs[:count_in])
    (encoded_ref, gz_ref, gh_ref, gmem_ref, back_left_ref, back_right_ref, vec) = refs[
        count_in : count_in + 7
    ]
    hbm_out = refs[count_in + 7 : count_in + 7 + count_out]
    (
        qkv_ref, out_ref, up_ref, down_ref, gqkv_ref, gout_ref, gup_ref, gdown_ref, mask_ref,
        z_ref, proj_ref, probs_ref, att_ref, hidden_ref, go_ref, gproj_ref, branch_ref,
        grad_low_ref, grad_hidden_ref, sems,
    ) = refs[count_in + 7 + count_out :]
    outs_to = hbm_out
    if spots is not None:
        outs_to = [[ref.at[k] for ref in hbm_out for k in range(ref.shape[0])]]
    wide = sizes.width
    attn_copies = start_in(attn_pairs(mats, spots, groups, qkv_ref, out_ref, place_ref), sems, 0)
    ffn_copies = start_in(
        ffn_pairs(mats, spots, groups, up_ref, down_ref, place_ref), sems, len(attn_copies)
    )
    vec[...] = jnp.zeros_like(vec)
    for n in range(seqs):
        base = n * sizes.ext
        z_ref[pl.ds(base, sizes.rows), :] = low_ref[pl.ds(n * sizes.rows, sizes.rows), :]
        z_ref[pl.ds(base + sizes.right_at, RIGHT_ROWS), :] = right_ref[n]
        z_ref[pl.ds(base + sizes.left_at, LEFT_ROWS), :] = left_ref[n, pl.ds(0, LEFT_ROWS), :]
        memory = jnp.concatenate(
            [
                mem_ref[pl.ds(n * sizes.segs, sizes.segs), :],
                left_ref[n, pl.ds(LEFT_ROWS, MEM_ROWS), :].astype(F32)[: sizes.segs],
            ],
            axis=0,
        )
        z_ref[pl.ds(base + sizes.mem_at, MEM_ROWS), :] = memory.astype(BF16)
        grad_low_ref[pl.ds(n * sizes.rows, sizes.rows), :] = out_grad_ref[n]
    fill_mask(sizes, seqs, starts_ref, place_ref, mask_ref)
    wait_all(attn_copies)
    project(sizes, z_ref, qkv_ref, row_bias_ref, proj_ref)
    attend(sizes, seqs, proj_ref, mask_ref, probs_ref, att_ref)
    mixed = (
        inputs_ref[...]
        + nt(att_ref[...], out_ref[...].reshape(-1, wide))
        + biases_ref[1, pl.ds(3, 1), :]
    )
    gain = gains_ref[1, pl.ds(1, 1), :]
    hidden, scaled, inverse = norm_forward(mixed, gain, biases_ref[1, pl.ds(4, 1), :])
    hidden_ref[...] = hidden.astype(BF16)
    for n in range(seqs):
        encoded_ref[n] = mixed[n * sizes.rows : (n + 1) * sizes.rows] + biases_ref[
            1, pl.ds(5, 1), :
        ]
    grad_hidden_ref[...] = jnp.zeros_like(grad_hidden_ref)
    wait_all(ffn_copies)

    def body(c, carry):
        at_lane = pl.multiple_of(c * wide, wide)
        upward = nt(hidden_ref[...], up_block(up_ref, c, wide))
        upward = upward + ffn_bias_ref[pl.ds(1, 1), pl.ds(at_lane, wide)]
        active, slope = gelu_both(upward)
        active = active.astype(BF16)
        made = nt(active, down_block(down_ref, c, wide))
        for n in range(seqs):
            encoded_ref[n] += made[n * sizes.rows : (n + 1) * sizes.rows]
        grad_hidden_ref[...] += ffn_back_step(
            sizes, c, wide, grad_low_ref[...], hidden_ref[...], active, slope, up_ref, down_ref,
            gup_ref, gdown_ref, vec,
        )
        return carry

    lax.fori_loop(0, sizes.ff // wide, body, 0)
    out_at = len(attn_copies) + len(ffn_copies)
    outs = start_out(
        ffn_pairs(mats, spots, outs_to, gup_ref, gdown_ref, place_ref), sems, out_at
    )
    grad = grad_low_ref[...].astype(F32)
    grad_hidden = grad_hidden_ref[...]
    vec[pl.ds(1, 1), :] = col_sum(grad_hidden * scaled)
    vec[pl.ds(6, 1), :] = col_sum(grad_hidden)
    vec[pl.ds(7, 1), :] = col_sum(grad)
    gz = grad + norm_backward(grad_hidden, scaled, inverse, gain)
    gz_ref[...] = gz
    attn_back_stage(
        sizes, seqs, gz, None, att_ref, proj_ref, probs_ref, z_ref, qkv_ref, out_ref, gqkv_ref,
        gout_ref, go_ref, gproj_ref, branch_ref, vec, gh_ref, gmem_ref, back_left_ref,
        back_right_ref,
    )
    outs = outs + start_out(
        attn_pairs(mats, spots, outs_to, gqkv_ref, gout_ref, place_ref),
        sems,
        out_at + len(outs),
    )
    wait_all(outs)


def first_back_kernel(
    last, sizes, seqs, mats, spots, halves, count_in, count_out, place_ref, inputs_ref, gz_in_ref,
    gh_in_ref, gmem_in_ref, from_right_ref, from_left_ref, mixed_ref, active_ref, slope_ref,
    att_ref, probs_ref, proj_ref, z_ref, frames_ref, left_ref, right_ref, gains_ref, biases_ref,
    last_vec, *refs
):
    groups = in_groups(spots, refs[:count_in])
    gz_ref, gh_ref, gmem_ref, back_left_ref, back_right_ref, upper_vec, vec = refs[
        count_in : count_in + 7
    ]
    refs = refs[count_in + 7 :]
    hbm_out = refs[:count_out]
    (
        qkv_ref, out_ref, up_ref, down_ref, gqkv_ref, gout_ref, gup_ref, gdown_ref, hidden_ref,
        grad_low_ref, grad_ref, grad_hidden_ref, grad_mem_ref, go_ref, gproj_ref, branch_ref,
        small_ref, sems,
    ) = refs[count_out:]
    wide = sizes.width
    small = []
    outs_to = hbm_out
    if spots is not None:
        classes = count_in // 2
        rows = (mats.attn_rows + mats.ffn_rows) // 2
        half = CHIPS_Z * rows
        each = [ref.at[k] for ref in hbm_out for k in range(classes)]
        small = [ref.at[pl.ds(half, SMALL_ROWS), :] for ref in each]
        outs_to = [
            [ref.at[pl.ds(at, half), :].reshape(CHIPS_Z, rows, LANES) for ref in each]
            for at in (half + SMALL_ROWS, 0)
        ]
    ffn_copies = start_in(ffn_pairs(mats, spots, groups, up_ref, down_ref, place_ref), sems, 0)
    attn_copies = start_in(
        attn_pairs(mats, spots, groups, qkv_ref, out_ref, place_ref), sems, len(ffn_copies)
    )
    vec[...] = jnp.zeros_like(vec)
    upper_vec[...] = jnp.zeros_like(upper_vec)
    gain = gains_ref[1, pl.ds(0, 1), :]
    gain_sum = jnp.zeros((1, wide), F32)
    bias_sum = jnp.zeros((1, wide), F32)
    for n in range(seqs):
        rows = pl.ds(n * sizes.rows, sizes.rows)
        _, scaled, inverse = norm_forward(
            inputs_ref[rows, :], gain, biases_ref[1, pl.ds(0, 1), :]
        )
        total, mem = merge_halo(last, n, gh_in_ref, gmem_in_ref, from_right_ref, from_left_ref)
        gain_sum = gain_sum + col_sum(total * scaled)
        bias_sum = bias_sum + col_sum(total)
        grad = gz_in_ref[rows, :] + norm_backward(total, scaled, inverse, gain)
        grad_ref[rows, :] = grad
        grad_low_ref[rows, :] = grad.astype(BF16)
        grad_mem_ref[pl.ds(n * sizes.segs, sizes.segs), :] = mem
    upper_vec[pl.ds(0, 1), :] = gain_sum
    upper_vec[pl.ds(2, 1), :] = bias_sum
    gain = gains_ref[0, pl.ds(1, 1), :]
    hidden, scaled, inverse = norm_forward(
        mixed_ref[...], gain, biases_ref[0, pl.ds(4, 1), :]
    )
    hidden_ref[...] = hidden.astype(BF16)
    grad_hidden_ref[...] = jnp.zeros_like(grad_hidden_ref)
    wait_all(ffn_copies)

    def body(c, carry):
        at_lane = pl.multiple_of(c * wide, wide)
        grad_hidden_ref[...] += ffn_back_step(
            sizes, c, wide, grad_low_ref[...], hidden_ref[...],
            active_ref[:, pl.ds(at_lane, wide)], slope_ref[:, pl.ds(at_lane, wide)].astype(F32),
            up_ref, down_ref, gup_ref, gdown_ref, vec,
        )
        return carry

    lax.fori_loop(0, sizes.ff // wide, body, 0)
    out_at = len(ffn_copies) + len(attn_copies)
    outs = start_out(
        ffn_pairs(mats, halves, outs_to, gup_ref, gdown_ref, place_ref), sems, out_at
    )
    grad_hidden = grad_hidden_ref[...]
    grad = grad_ref[...]
    vec[pl.ds(1, 1), :] = col_sum(grad_hidden * scaled)
    vec[pl.ds(6, 1), :] = col_sum(grad_hidden)
    vec[pl.ds(7, 1), :] = col_sum(grad)
    gz = grad + norm_backward(grad_hidden, scaled, inverse, gain)
    gz_ref[...] = gz

    def scaled_rows(n):
        before = left_ref[n, pl.ds(left_ref.shape[1] - LEFT_ROWS, LEFT_ROWS), :]
        parts = (frames_ref[n], right_ref[n], before)
        first_gain = gains_ref[0, pl.ds(0, 1), :]
        first_bias = biases_ref[0, pl.ds(0, 1), :]
        return [norm_forward(part.astype(F32), first_gain, first_bias)[1] for part in parts]

    wait_all(attn_copies)
    attn_back_stage(
        sizes, seqs, gz, grad_mem_ref, att_ref, proj_ref, probs_ref, z_ref, qkv_ref, out_ref,
        gqkv_ref, gout_ref, go_ref, gproj_ref, branch_ref, vec, gh_ref, gmem_ref, back_left_ref,
        back_right_ref, scaled_rows,
    )
    outs = outs + start_out(
        attn_pairs(mats, halves, outs_to, gqkv_ref, gout_ref, place_ref),
        sems,
        out_at + len(outs),
    )
    parts = sizes.width // LANES
    for layer, total in enumerate((vec[...], last_vec[...] + upper_vec[...])):
        for part in range(parts):
            small_ref[pl.ds((layer * parts + part) * TILE, TILE), :] = total[
                :, part * LANES : (part + 1) * LANES
            ].astype(BF16)
    outs = outs + start_out([(ref, small_ref) for ref in small], sems, out_at + len(outs))
    wait_all(outs)


def frames_grad_kernel(
    sizes, seqs, frames_ref, gz_ref, gh_ref, gmem_ref, from_right_ref, from_left_ref, gains_ref,
    biases_ref, grad_ref
):
    gain = gains_ref[0, pl.ds(0, 1), :]
    for n in range(seqs):
        _, scaled, inverse = norm_forward(
            frames_ref[n].astype(F32), gain, biases_ref[0, pl.ds(0, 1), :]
        )
        total, mem = merge_halo(sizes, n, gh_ref, gmem_ref, from_right_ref, from_left_ref)
        grad_ref[n] = (
            gz_ref[pl.ds(n * sizes.rows, sizes.rows), :]
            + norm_backward(total, scaled, inverse, gain)
            + segment_spread(sizes.rows, sizes.width, mem * (1.0 / SEG_LEN))
        )


def shifted(value, axis, by):
    size = lax.axis_size(axis)
    pairs = [(i, i + by) for i in range(size) if 0 <= i + by < size]
    return lax.ppermute(value, axis, pairs)


def permuted(value, move):
    reps = lax.axis_size("rep")
    pairs = []
    for flat in range(lax.axis_size("seg") * reps):
        seg, rep = divmod(flat, reps)
        z, y, x, core = move(seg // CHIPS_Y, seg % CHIPS_Y, rep // 2, rep % 2)
        pairs.append((flat, (z * CHIPS_Y + y) * reps + 2 * x + core))
    return lax.ppermute(value, ("seg", "rep"), pairs)


def across_first(value):
    return permuted(value, lambda z, y, x, c: (z, y, x ^ 1, c) if c == 0 else (z, y ^ 1, x, c))


def across_second(value):
    return permuted(value, lambda z, y, x, c: (z, y ^ 1, x, c) if c == 0 else (z, y, x ^ 1, c))


def other_core(value):
    return permuted(value, lambda z, y, x, c: (z, y, x, c ^ 1))


def after(value, *others):
    return lax.optimization_barrier((value,) + others)[0]


def swap_z(blocks):
    groups = [
        [z * CHIPS_Y + y for z in range(CHIPS_Z)] for y in range(CHIPS_Y)
    ]
    return lax.all_to_all(blocks, "seg", 0, 0, axis_index_groups=groups, tiled=True)


def gather_sides(here):
    return [here, across_first(here), across_second(here)]


def both_cores(blocks):
    return blocks + [other_core(block) for block in blocks]


def summed(*parts):
    total = parts[0].astype(F32)
    for part in parts[1:]:
        total = total + part.astype(F32)
    return total.astype(BF16)


def first_rows(rows):
    return pl.BlockSpec((1, rows, LANES), lambda i: (0, 0, 0))


def sum_everywhere(value):
    count = lax.axis_size("seg") * lax.axis_size("rep")
    bit = 1
    while bit < count:
        value = value + lax.ppermute(value, ("seg", "rep"), [(i, i ^ bit) for i in range(count)])
        bit *= 2
    return value


def vmem_spec():
    return pl.BlockSpec(memory_space=pltpu.VMEM)


def smem_spec():
    return pl.BlockSpec(memory_space=pltpu.SMEM)


def hbm_spec():
    return pl.BlockSpec(memory_space=pl.ANY)


def call(body, in_specs, out_shapes, out_specs, scratch, args, flops=0, moved=0, grid=()):
    return pl.pallas_call(
        body,
        grid=grid,
        in_specs=in_specs,
        out_shape=tuple(jax.ShapeDtypeStruct(shape, kind) for shape, kind in out_shapes),
        out_specs=tuple(out_specs),
        scratch_shapes=scratch,
        compiler_params=pltpu.CompilerParams(vmem_limit_bytes=VMEM_BYTES),
        cost_estimate=pl.CostEstimate(flops=flops, bytes_accessed=moved, transcendentals=0),
    )(*args)


def on_device(
    frames,
    utt_segments,
    out_grad,
    qkv_weight,
    out_weight,
    ffn_in_weight,
    ffn_out_weight,
    norm_gains,
    biases,
    ffn_bias,
):
    micros, groups, rows, width = frames.shape
    seqs = micros * groups
    ff = ffn_bias.shape[1]
    reps = lax.axis_size("rep")
    seg_count = lax.axis_size("seg")
    mats = Matrices(width, ff)
    by_blocks = width // reps == LANES and reps == 4 and seg_count == BLOCKS
    first = Sizes(rows, width, ff, True)
    last = Sizes(rows, width, ff, False)
    own = seqs * rows
    mem_own = seqs * first.segs

    seg_at = lax.axis_index("seg")
    seg_base = seg_at * first.segs
    rep_at = lax.axis_index("rep")
    place = [seg_base, jnp.int32(first.segs * seg_count)]
    y_at, x_at, core_at = seg_at % CHIPS_Y, rep_at // 2, rep_at % 2
    for other in range(2):
        core = lax.bitwise_xor(core_at, other)
        for hop2 in range(2):
            for hop1 in range(2):
                x_hop = jnp.where(core == 0, hop1, hop2)
                y_hop = jnp.where(core == 0, hop2, hop1)
                place.append(lax.bitwise_xor(y_at, y_hop))
                place.append((lax.bitwise_xor(x_at, x_hop) * 2 + core) * LANES)
    place = jnp.stack([jnp.asarray(entry, jnp.int32) for entry in place])
    lengths = utt_segments.reshape(seqs, utt_segments.shape[2])
    starts = (jnp.cumsum(lengths, axis=1) - lengths).astype(jnp.int32)
    zero_bias = jnp.zeros((width,), F32)
    row_bias = jnp.stack(
        [jnp.concatenate([biases[l, 1], zero_bias, biases[l, 2]]) for l in range(LAYERS)]
    ).reshape(LAYERS, 1, 3 * width)

    frames_own = frames.reshape(seqs, rows, width)
    grads_own = out_grad.reshape(seqs, rows, width)
    far = MEM_LEN * SEG_LEN
    frames_left = shifted(frames_own[:, rows - far :], "seg", 1)
    frames_right = shifted(frames_own[:, :RIGHT_ROWS], "seg", -1)

    attn_rows, ffn_rows = mats.attn_rows, mats.ffn_rows
    if by_blocks:
        qkv_t, out_t, down_t = (
            jnp.swapaxes(member, 1, 2) for member in (qkv_weight, out_weight, ffn_out_weight)
        )
        all_rows = attn_rows + ffn_rows
        spots, halves = Spots(mats, False), Spots(mats, True)
        shards = call(
            lambda *refs: pack_kernel(spots, *refs),
            [vmem_spec()] * 4,
            [((CHIPS_Z, all_rows, LANES), BF16)] * LAYERS,
            [vmem_spec()] * LAYERS,
            [],
            (qkv_t, out_t, ffn_in_weight, down_t),
        )
        sides0 = gather_sides(after(swap_z(shards[0]), frames_left, frames_right))
        place, starts, row_bias, sent = lax.optimization_barrier(
            (place, starts, row_bias, after(shards[1], sides0[0]))
        )
        sides1 = gather_sides(swap_z(sent))
        first_all = both_cores(sides0 + [across_second(after(sides0[1], sides1[0]))])
        classes = len(first_all) // 2
        half_rows = CHIPS_Z * all_rows // 2
        grad_outs0 = [((classes, 2 * half_rows + SMALL_ROWS, LANES), BF16)] * 2
        grad_outs1 = [((classes, CHIPS_Z, all_rows, LANES), BF16)] * 2
        copies_in = len(first_all) * (3 + mats.down_parts)
    else:
        whole = []
        for member, shape in zip(
            (qkv_weight, out_weight, ffn_in_weight, ffn_out_weight),
            (mats.qkv, mats.out, mats.up, mats.down),
        ):
            member = lax.all_gather(member, "rep", axis=1, tiled=True)
            member = lax.all_gather(member, "seg", axis=2, tiled=True)
            whole.append(jnp.swapaxes(member, 1, 2).reshape((LAYERS,) + shape))
        first_all = [member[0] for member in whole]
        last_all = [member[1] for member in whole]
        spots = halves = None
        grad_outs0 = grad_outs1 = [
            (shape, BF16) for shape in (mats.qkv, mats.out, mats.up, mats.down)
        ]
        copies_in = 4
    dma = pltpu.SemaphoreType.DMA

    matrices = [pltpu.VMEM(shape, BF16) for shape in (mats.qkv, mats.out, mats.up, mats.down)]

    (
        z0, proj0, probs0, att0, mixed0, mem1, x1, active0, slope0, low1, send_right, send_left,
    ) = call(
        lambda *refs: first_layer_kernel(
            first, seqs, mats, spots, len(first_all), *refs
        ),
        [smem_spec()] * 2 + [vmem_spec()] * 7 + [hbm_spec()] * len(first_all),
        [
            ((seqs * first.ext, width), BF16),
            ((seqs * first.ext, 3 * width), BF16),
            ((seqs * first.pairs, 2 * first.queries, first.keys), BF16),
            ((seqs * first.queries, width), BF16),
            ((own, width), F32),
            ((mem_own, width), F32),
            ((own, width), F32),
            ((own, ff), BF16),
            ((own, ff), BF16),
            ((own, width), BF16),
            ((seqs, BACK_ROWS, width), BF16),
            ((seqs, RIGHT_ROWS, width), BF16),
        ],
        [vmem_spec()] * 12,
        matrices
        + [
            pltpu.VMEM((seqs, first.queries, first.keys), F32),
            pltpu.VMEM((own, width), BF16),
            dma((copies_in,)),
        ],
        (place, starts, frames_own, frames_left, frames_right, norm_gains, biases, ffn_bias,
         row_bias[0]) + tuple(first_all),
        flops=24 * own * (4 * width * width + 2 * width * ff) // 2,
        moved=2 * (4 * width * width + 2 * width * ff),
    )
    left1 = shifted(send_right, "seg", 1)
    right1 = shifted(send_left, "seg", -1)
    if by_blocks:
        last_side = across_second(after(sides1[1], sides1[2], low1))
        last_all = both_cores(sides1 + [last_side])
        last_all[-1] = other_core(after(last_side, left1, right1))

    vec_shape = (TILE, width)
    outs = call(
        lambda *refs: last_layer_kernel(
            last, seqs, mats, spots, len(last_all), len(grad_outs1), *refs
        ),
        [smem_spec()] * 2 + [vmem_spec()] * 10 + [hbm_spec()] * len(last_all),
        [
            ((seqs, rows, width), F32),
            ((own, width), F32),
            ((own, width), F32),
            ((mem_own, width), F32),
            ((seqs, BACK_ROWS, width), BF16),
            ((seqs, RIGHT_ROWS, width), BF16),
            (vec_shape, F32),
        ]
        + grad_outs1,
        [vmem_spec()] * 7 + [hbm_spec()] * len(grad_outs1),
        matrices
        + matrices
        + [
            pltpu.VMEM((seqs, last.queries, last.keys), F32),
            pltpu.VMEM((seqs * last.ext, width), BF16),
            pltpu.VMEM((seqs * last.ext, 3 * width), BF16),
            pltpu.VMEM((seqs * last.pairs, 2 * last.queries, last.keys), BF16),
            pltpu.VMEM((seqs * last.queries, width), BF16),
            pltpu.VMEM((own, width), BF16),
            pltpu.VMEM((seqs * last.queries, width), BF16),
            pltpu.VMEM((seqs * last.ext, 3 * width), BF16),
            pltpu.VMEM((seqs * last.queries, width), BF16),
            pltpu.VMEM((own, width), BF16),
            pltpu.VMEM((own, width), F32),
            dma((2 * copies_in,)),
        ],
        (place, starts, low1, left1, right1, mem1, x1, grads_own, norm_gains, biases, ffn_bias,
         row_bias[1]) + tuple(last_all),
        flops=30 * own * (4 * width * width + 2 * width * ff),
        moved=4 * (4 * width * width + 2 * width * ff),
    )
    encoded, gz1, gh1, gmem1, back_left1, back_right1, vec1 = outs[:7]
    grad_blocks1 = outs[7:]
    from_right1 = shifted(back_left1, "seg", -1)
    from_left1 = shifted(back_right1, "seg", 1)

    gh1_tied = gh1
    if by_blocks:
        mine1, theirs1 = grad_blocks1[0], other_core(grad_blocks1[1])
        far1 = summed(mine1[2:], theirs1[2:])
        gh1_tied = after(gh1, far1)
    gz0, gh0, gmem0, back_left0, back_right0, upper_vec, vec0, *grad_blocks0 = call(
        lambda *refs: first_back_kernel(
            last, first, seqs, mats, spots, halves, len(first_all), len(grad_outs0), *refs
        ),
        [smem_spec()] + [vmem_spec()] * 19 + [hbm_spec()] * len(first_all),
        [
            ((own, width), F32),
            ((own, width), F32),
            ((mem_own, width), F32),
            ((seqs, BACK_ROWS, width), BF16),
            ((seqs, RIGHT_ROWS, width), BF16),
            (vec_shape, F32),
            (vec_shape, F32),
        ]
        + grad_outs0,
        [vmem_spec()] * 7 + [hbm_spec()] * len(grad_outs0),
        matrices
        + matrices
        + [
            pltpu.VMEM((own, width), BF16),
            pltpu.VMEM((own, width), BF16),
            pltpu.VMEM((own, width), F32),
            pltpu.VMEM((own, width), F32),
            pltpu.VMEM((mem_own, width), F32),
            pltpu.VMEM((seqs * first.queries, width), BF16),
            pltpu.VMEM((seqs * first.ext, 3 * width), BF16),
            pltpu.VMEM((seqs * first.queries, width), BF16),
            pltpu.VMEM((SMALL_ROWS, LANES), BF16),
            dma((2 * copies_in + 8,)),
        ],
        (place, x1, gz1, gh1_tied, gmem1, from_right1, from_left1, mixed0, active0, slope0, att0,
         probs0, proj0, z0, frames_own, frames_left, frames_right, norm_gains, biases, vec1)
        + tuple(first_all),
        flops=28 * own * (4 * width * width + 2 * width * ff),
        moved=4 * (4 * width * width + 2 * width * ff),
    )
    from_right0 = shifted(back_left0, "seg", -1)
    from_left0 = shifted(back_right0, "seg", 1)
    gz0_last = gz0
    if by_blocks:
        second1 = across_second(far1)
        near1 = summed(mine1[1], theirs1[1], second1[1])
        first1 = across_first(near1)
        mine0, theirs0 = grad_blocks0[0], other_core(after(grad_blocks0[1], second1))
        far0 = after(summed(mine0[2:], theirs0[2:]), near1)
        second0 = across_second(far0)
        total1 = summed(mine1[0], theirs1[0], second1[0], after(first1, far0))
        last_parts = swap_z(total1)
        tail = half_rows + SMALL_ROWS
        half_a, half_b = slice(tail, None), slice(0, tail)
        second0 = after(second0, total1)
        mid_a = summed(mine0[1, half_a], theirs0[1, half_a], second0[1, half_a])
        mid_b = summed(mine0[1, half_b], theirs0[1, half_b], second0[1, half_b])
        first_a, first_b = across_first(mid_a), across_first(mid_b)
        near_a = summed(
            mine0[0, half_a], theirs0[0, half_a], second0[0, half_a], after(first_a, last_parts)
        )
        parts_a = swap_z(near_a.reshape(CHIPS_Z, -1, LANES))
        near_b = call(
            lambda *refs: near_small_kernel(CHIPS_Z, *refs),
            [first_rows(tail)] * 3 + [vmem_spec()],
            [((CHIPS_Z, half_rows // CHIPS_Z + SMALL_ROWS, LANES), BF16)],
            [vmem_spec()],
            [],
            [mine0, theirs0, second0, first_b],
            grid=(1,),
        )[0]
        parts_b = swap_z(near_b)
        gz0_last = after(gz0, near_b)
    frames_grad = call(
        lambda *refs: frames_grad_kernel(first, seqs, *refs),
        [vmem_spec()] * 8,
        [((seqs, rows, width), F32)],
        [vmem_spec()],
        [],
        (frames_own, gz0_last, gh0, gmem0, from_right0, from_left0, norm_gains, biases),
    )[0]

    if by_blocks:
        shapes = [member.shape for member in (qkv_t, out_t, ffn_in_weight, down_t)]
        shapes += [norm_gains.shape, (biases.shape[1], LAYERS, width), ffn_bias.shape]
        reduced = call(
            lambda *refs: unpack_kernel(
                [halves, spots], (1, half_rows // CHIPS_Z), *refs
            ),
            [vmem_spec()] * 3,
            [(shape, F32) for shape in shapes],
            [vmem_spec()] * len(shapes),
            [],
            [parts_a, after(parts_b, frames_grad), last_parts],
        )
        small = reduced[4], jnp.swapaxes(reduced[5], 0, 1), reduced[6]
        reduced = [
            jnp.swapaxes(reduced[0], 1, 2),
            jnp.swapaxes(reduced[1], 1, 2),
            reduced[2],
            jnp.swapaxes(reduced[3], 1, 2),
        ]
    else:
        reduced = []
        for member0, member1 in zip(grad_blocks0, grad_blocks1):
            both = jnp.stack([member0, member1]).reshape(LAYERS, -1, member0.shape[3])
            both = jnp.swapaxes(both, 1, 2)
            both = lax.psum_scatter(both, "seg", scatter_dimension=2, tiled=True)
            both = lax.psum_scatter(both, "rep", scatter_dimension=1, tiled=True)
            reduced.append(both.astype(F32))
        small = sum_everywhere(jnp.stack([vec0, vec1 + upper_vec]))
        small = small[:, 0:2], small[:, 2:8], small[:, 8:12].reshape(ffn_bias.shape)

    return (
        encoded.reshape(frames.shape),
        frames_grad.reshape(frames.shape),
        reduced[0],
        reduced[1],
        reduced[2],
        reduced[3],
        small[0],
        small[1],
        small[2],
    )


def solution(mesh):
    in_specs = (
        P(None, "rep", "seg", None),
        P(None, "rep", None),
        P(None, "rep", "seg", None),
        P(None, "rep", "seg"),
        P(None, "rep", "seg"),
        P(None, "rep", "seg"),
        P(None, "rep", "seg"),
        P(),
        P(),
        P(),
    )
    out_specs = (
        P(None, "rep", "seg", None),
        P(None, "rep", "seg", None),
        P(None, "rep", "seg"),
        P(None, "rep", "seg"),
        P(None, "rep", "seg"),
        P(None, "rep", "seg"),
        P(),
        P(),
        P(),
    )
    return jax.shard_map(
        on_device, mesh=mesh, in_specs=in_specs, out_specs=out_specs, check_vma=False
    )
```

```python
import jax
import jax.numpy as jnp
from jax import lax
from jax.experimental import pallas as pl
from jax.experimental.pallas import tpu as pltpu
from jax.sharding import PartitionSpec as P

HEADS = 8
SEG_LEN = 16
LEFT_LEN = 30
RIGHT_LEN = 4
MEM_LEN = 4
LAYERS = 2

EPS = 1e-05
ROOT_HALF = 0.7071067811865476
INV_ROOT_TWO_PI = 0.3989422804014327

LANES = 128
TILE = 16
RIGHT_ROWS = 16
LEFT_ROWS = 32
MEM_ROWS = 16
BACK_ROWS = LEFT_ROWS + MEM_ROWS
CHIPS_Z = 4
CHIPS_Y = 2
BLOCKS = CHIPS_Z * CHIPS_Y
SMALL_ROWS = 128
VMEM_BYTES = 56 * 1024 * 1024

BF16 = jnp.bfloat16
F32 = jnp.float32


def nn(a, b):
    return lax.dot_general(a, b, (((1,), (0,)), ((), ())), preferred_element_type=F32)


def nt(a, b):
    return lax.dot_general(a, b, (((1,), (1,)), ((), ())), preferred_element_type=F32)


def tn(a, b):
    return lax.dot_general(a, b, (((0,), (0,)), ((), ())), preferred_element_type=F32)


def col_sum(value):
    return jnp.sum(value, axis=0, keepdims=True)


def norm_forward(inputs, gain, bias):
    center = inputs - jnp.mean(inputs, axis=1, keepdims=True)
    inverse = lax.rsqrt(jnp.mean(center * center, axis=1, keepdims=True) + EPS)
    scaled = center * inverse
    return scaled * gain + bias, scaled, inverse


def norm_backward(grad_in, scaled, inverse, gain):
    grad_scaled = grad_in * gain
    return inverse * (
        grad_scaled
        - jnp.mean(grad_scaled, axis=1, keepdims=True)
        - scaled * jnp.mean(grad_scaled * scaled, axis=1, keepdims=True)
    )


def segment_mean(inputs):
    rows, width = inputs.shape
    return jnp.mean(inputs.reshape(rows // SEG_LEN, SEG_LEN, width), axis=1)


def segment_spread(rows, width, per_segment):
    segs = rows // SEG_LEN
    return jnp.broadcast_to(per_segment[:, None, :], (segs, SEG_LEN, width)).reshape(rows, width)


def identity(size):
    row = lax.broadcasted_iota(jnp.int32, (size, size), 0)
    col = lax.broadcasted_iota(jnp.int32, (size, size), 1)
    return (row == col).astype(F32).astype(BF16)


class Sizes:
    def __init__(self, rows, width, ff, with_summary):
        self.rows = rows
        self.width = width
        self.ff = ff
        self.segs = rows // SEG_LEN
        self.top = TILE if with_summary else 0
        self.keys = rows + RIGHT_ROWS + LEFT_ROWS + MEM_ROWS
        self.ext = self.top + self.keys
        self.queries = self.top + rows
        self.right_at = self.top + rows
        self.left_at = self.right_at + RIGHT_ROWS
        self.mem_at = self.left_at + LEFT_ROWS
        self.pairs = width // LANES


class Matrices:
    def __init__(self, width, ff):
        self.qkv = (CHIPS_Z, CHIPS_Y, 3 * width // BLOCKS, width)
        self.out = (CHIPS_Z, CHIPS_Y, width // BLOCKS, width)
        self.up = (CHIPS_Z, CHIPS_Y, ff // BLOCKS, width)
        self.down = (CHIPS_Z, CHIPS_Y, width // BLOCKS, ff)
        self.down_parts = ff // width
        self.attn_rows = self.qkv[2] + self.out[2]
        self.ffn_rows = self.up[2] + self.down_parts * self.down[2]


class Spots:
    def __init__(self, mats):
        high, wide, up, low = mats.qkv[2], mats.out[2], mats.up[2], mats.down[2]
        self.qkv = (0, 0)
        self.out = (0, high)
        self.up = (0, high + wide)
        self.down = [(0, high + wide + up + low * part) for part in range(mats.down_parts)]


def attn_pairs(mats, spots, groups, qkv_ref, out_ref, place_ref):
    if spots is None:
        return [(groups[0], qkv_ref), (groups[1], out_ref)]
    pairs = []
    for k in range(len(groups[0])):
        row = place_ref[2 + 2 * k]
        lane = pl.multiple_of(place_ref[3 + 2 * k], LANES)
        for (group, first), ref, shape in (
            (spots.qkv, qkv_ref, mats.qkv),
            (spots.out, out_ref, mats.out),
        ):
            block = groups[group][k]
            pairs.append(
                (
                    block.at[:, pl.ds(first, shape[2]), :],
                    ref.at[:, row, :, pl.ds(lane, LANES)],
                )
            )
    return pairs


def ffn_pairs(mats, spots, groups, up_ref, down_ref, place_ref):
    if spots is None:
        return [(groups[2], up_ref), (groups[3], down_ref)]
    pairs = []
    for k in range(len(groups[0])):
        row = place_ref[2 + 2 * k]
        lane = pl.multiple_of(place_ref[3 + 2 * k], LANES)
        group, first = spots.up
        block = groups[group][k]
        pairs.append(
            (block.at[:, pl.ds(first, mats.up[2]), :], up_ref.at[:, row, :, pl.ds(lane, LANES)])
        )
        for part, (group, first) in enumerate(spots.down):
            there = pl.multiple_of(
                place_ref[3 + 2 * k] * mats.down_parts + part * LANES, LANES
            )
            block = groups[group][k]
            pairs.append(
                (
                    block.at[:, pl.ds(first, mats.down[2]), :],
                    down_ref.at[:, row, :, pl.ds(there, LANES)],
                )
            )
    return pairs


def start_in(pairs, sems, at):
    copies = [pltpu.make_async_copy(s, d, sems.at[at + i]) for i, (s, d) in enumerate(pairs)]
    for copy in copies:
        copy.start()
    return copies


def start_out(pairs, sems, at):
    copies = [pltpu.make_async_copy(d, s, sems.at[at + i]) for i, (s, d) in enumerate(pairs)]
    for copy in copies:
        copy.start()
    return copies


def in_groups(spots, refs):
    return refs if spots is None else [refs]


def wait_all(copies):
    for copy in copies:
        copy.wait()


def fill_mask(sizes, seqs, starts_ref, place_ref, mask_ref):
    shape = (sizes.queries, sizes.keys)
    row = lax.broadcasted_iota(jnp.int32, shape, 0)
    col = lax.broadcasted_iota(jnp.int32, shape, 1)
    base = place_ref[0]
    total = place_ref[1]
    query = jnp.where(row < sizes.top, row, lax.shift_right_arithmetic(row - sizes.top, 4))
    left_at = sizes.rows + RIGHT_ROWS
    mem_at = left_at + LEFT_ROWS
    spot = jnp.where(col < left_at, col, col - mem_at)
    mem_seg = jnp.where(col < mem_at + sizes.segs, col - mem_at, col - mem_at - 2 * sizes.segs)
    key_seg = jnp.where(col < mem_at, lax.shift_right_arithmetic(spot, 4), mem_seg)
    near = (
        (key_seg == query)
        | ((spot >= query * SEG_LEN - LEFT_LEN) & (spot < query * SEG_LEN))
        | ((key_seg == query + 1) & (spot < query * SEG_LEN + SEG_LEN + RIGHT_LEN))
    )
    recent = (key_seg >= query - MEM_LEN) & (key_seg < query) & (row >= sizes.top)
    allowed = ((col < mem_at) & near) | ((col >= mem_at) & recent)
    key_abs = key_seg + base
    query_abs = query + base
    allowed = allowed & (key_abs >= 0) & (key_abs < total)
    if sizes.top:
        allowed = allowed & ((row < sizes.segs) | (row >= sizes.top))
    for n in range(seqs):
        key_owner = jnp.zeros(shape, jnp.int32)
        query_owner = jnp.zeros(shape, jnp.int32)
        for u in range(starts_ref.shape[1]):
            first = starts_ref[n, u]
            key_owner = key_owner + (key_abs >= first).astype(jnp.int32)
            query_owner = query_owner + (query_abs >= first).astype(jnp.int32)
        mask_ref[n] = jnp.where(allowed & (key_owner == query_owner), 0.0, -1e30)


def half_masks():
    lane = lax.broadcasted_iota(jnp.int32, (1, LANES), 1)
    even = (lane < LANES // 2).astype(F32)
    return even.astype(BF16), (1.0 - even).astype(BF16), lane < LANES // 2


def project(sizes, z_ref, qkv_ref, row_bias_ref, proj_ref):
    step = CHIPS_Z // 2
    for c in range(2):
        block = qkv_ref[pl.ds(c * step, step)].reshape(-1, sizes.width)
        wide = block.shape[0]
        made = nt(z_ref[...], block) + row_bias_ref[:, pl.ds(c * wide, wide)]
        proj_ref[:, pl.ds(c * wide, wide)] = made.astype(BF16)


def attend(sizes, seqs, proj_ref, mask_ref, probs_ref, att_ref):
    even, odd, is_even = half_masks()
    scale = (sizes.width // HEADS) ** (-0.5)
    count = sizes.queries

    def body(p, carry):
        for n in range(seqs):
            lane = pl.multiple_of(p * LANES, LANES)
            query = proj_ref[pl.ds(n * sizes.ext, count), pl.ds(lane, LANES)]
            first = n * sizes.ext + sizes.top
            key = proj_ref[pl.ds(first, sizes.keys), pl.ds(sizes.width + lane, LANES)]
            value = proj_ref[pl.ds(first, sizes.keys), pl.ds(2 * sizes.width + lane, LANES)]
            scores = nt(jnp.concatenate([query * even, query * odd], axis=0), key) * scale
            outs = []
            for half in range(2):
                part = scores[half * count : (half + 1) * count] + mask_ref[n]
                part = jnp.exp(part - jnp.max(part, axis=1, keepdims=True))
                part = (part * (1.0 / jnp.sum(part, axis=1, keepdims=True))).astype(BF16)
                probs_ref[n * sizes.pairs + p, pl.ds(half * count, count), :] = part
                outs.append(nn(part, value))
            att_ref[pl.ds(n * count, count), pl.ds(lane, LANES)] = jnp.where(
                is_even, outs[0], outs[1]
            ).astype(BF16)
        return carry

    lax.fori_loop(0, sizes.pairs, body, 0)


def attend_back(sizes, seqs, proj_ref, probs_ref, go_ref, gproj_ref):
    even, odd, is_even = half_masks()
    scale = (sizes.width // HEADS) ** (-0.5)
    count = sizes.queries
    wide = sizes.width
    for n in range(seqs):
        base = n * sizes.ext
        rest = sizes.ext - count
        gproj_ref[pl.ds(base + count, rest), pl.ds(0, wide)] = jnp.zeros((rest, wide), BF16)
        if sizes.top:
            gproj_ref[pl.ds(base, sizes.top), pl.ds(wide, 2 * wide)] = jnp.zeros(
                (sizes.top, 2 * wide), BF16
            )

    def body(p, carry):
        for n in range(seqs):
            lane = pl.multiple_of(p * LANES, LANES)
            base = n * sizes.ext
            first = base + sizes.top
            query = proj_ref[pl.ds(base, count), pl.ds(lane, LANES)]
            key = proj_ref[pl.ds(first, sizes.keys), pl.ds(wide + lane, LANES)]
            value = proj_ref[pl.ds(first, sizes.keys), pl.ds(2 * wide + lane, LANES)]
            grad = go_ref[pl.ds(n * count, count), pl.ds(lane, LANES)]
            queries = jnp.concatenate([query * even, query * odd], axis=0)
            grads = jnp.concatenate([grad * even, grad * odd], axis=0)
            probs_low = probs_ref[n * sizes.pairs + p]
            grad_values = tn(probs_low, grads)
            probs = probs_low.astype(F32)
            grad_probs = nt(grads, value)
            weighted = grad_probs * probs
            grad_scores = (
                (weighted - probs * jnp.sum(weighted, axis=1, keepdims=True)) * scale
            ).astype(BF16)
            grad_keys = tn(grad_scores, queries)
            grad_query = jnp.where(
                is_even, nn(grad_scores[:count], key), nn(grad_scores[count:], key)
            )
            gproj_ref[pl.ds(base, count), pl.ds(lane, LANES)] = grad_query.astype(BF16)
            gproj_ref[pl.ds(first, sizes.keys), pl.ds(wide + lane, LANES)] = grad_keys.astype(BF16)
            gproj_ref[pl.ds(first, sizes.keys), pl.ds(2 * wide + lane, LANES)] = (
                grad_values.astype(BF16)
            )
        return carry

    lax.fori_loop(0, sizes.pairs, body, 0)


def gelu_both(upward):
    half = 0.5 * (1.0 + lax.erf(upward * ROOT_HALF))
    slope = half + upward * jnp.exp(-0.5 * upward * upward) * INV_ROOT_TWO_PI
    return upward * half, slope


def up_block(up_ref, c, wide):
    step = wide // (up_ref.shape[1] * up_ref.shape[2])
    return up_ref[pl.ds(c * step, step)].reshape(-1, up_ref.shape[3])


def down_block(down_ref, c, wide):
    at = pl.multiple_of(c * wide, wide)
    return down_ref[:, :, :, pl.ds(at, wide)].reshape(-1, wide)


def ffn_back_step(
    sizes, c, wide, grad_low, hidden_low, active, slope, up_ref, down_ref, gup_ref, gdown_ref, vec
):
    at = pl.multiple_of(c * wide, wide)
    up = up_block(up_ref, c, wide)
    down = down_block(down_ref, c, wide)
    grad_active = nn(grad_low, down)
    grad_up_f = grad_active * slope
    grad_up = grad_up_f.astype(BF16)
    gdown_ref[:, :, :, pl.ds(at, wide)] = (
        tn(grad_low, active).astype(BF16).reshape(gdown_ref.shape[:3] + (wide,))
    )
    step = wide // (gup_ref.shape[1] * gup_ref.shape[2])
    gup_ref[pl.ds(c * step, step)] = (
        tn(grad_up, hidden_low).astype(BF16).reshape((step,) + gup_ref.shape[1:])
    )
    vec[pl.ds(8 + c, 1), :] = col_sum(grad_up.astype(F32))
    return nn(grad_up, up)


def attn_back_stage(
    sizes, seqs, gz, grad_mem_ref, att_ref, proj_ref, probs_ref, z_ref, qkv_ref, out_ref,
    gqkv_ref, gout_ref, go_ref, gproj_ref, branch_ref, vec, gh_ref, gmem_ref, back_left_ref,
    back_right_ref, scaled_rows=None,
):
    wide = sizes.width
    count = sizes.queries
    bias_out = col_sum(gz)
    for n in range(seqs):
        if sizes.top:
            mem_grad = grad_mem_ref[pl.ds(n * sizes.segs, sizes.segs), :]
            bias_out = bias_out + col_sum(mem_grad)
            branch_ref[pl.ds(n * count, sizes.top), :] = jnp.concatenate(
                [mem_grad, jnp.zeros((sizes.top - sizes.segs, wide), F32)], axis=0
            ).astype(BF16)
        branch_ref[pl.ds(n * count + sizes.top, sizes.rows), :] = gz[
            n * sizes.rows : (n + 1) * sizes.rows
        ].astype(BF16)
    vec[pl.ds(5, 1), :] = bias_out
    branch = branch_ref[...]
    gout_ref[...] = tn(branch, att_ref[...]).astype(BF16).reshape(gout_ref.shape)
    go_ref[...] = nn(branch, out_ref[...].reshape(-1, wide)).astype(BF16)
    attend_back(sizes, seqs, proj_ref, probs_ref, go_ref, gproj_ref)
    vec[pl.ds(3, 1), :] = col_sum(gproj_ref[:, pl.ds(0, wide)].astype(F32))
    vec[pl.ds(4, 1), :] = col_sum(gproj_ref[:, pl.ds(2 * wide, wide)].astype(F32))
    grad_ext = nn(gproj_ref[...], qkv_ref[...].reshape(-1, wide))
    gain_sum = jnp.zeros((1, wide), F32)
    bias_sum = jnp.zeros((1, wide), F32)
    for n in range(seqs):
        base = n * sizes.ext
        own = grad_ext[base + sizes.top : base + sizes.top + sizes.rows]
        if sizes.top:
            spread = grad_ext[base : base + sizes.segs] * (1.0 / SEG_LEN)
            own = own + segment_spread(sizes.rows, wide, spread)
        gh_ref[pl.ds(n * sizes.rows, sizes.rows), :] = own
        mem = base + sizes.mem_at
        gmem_ref[pl.ds(n * sizes.segs, sizes.segs), :] = grad_ext[mem : mem + sizes.segs]
        left = base + sizes.left_at
        back_left_ref[n] = grad_ext[left : left + BACK_ROWS].astype(BF16)
        right = base + sizes.right_at
        back_right_ref[n] = grad_ext[right : right + RIGHT_ROWS].astype(BF16)
        if scaled_rows is not None:
            grads = (
                own,
                grad_ext[right : right + RIGHT_ROWS],
                grad_ext[left : left + LEFT_ROWS],
            )
            for rows, scaled in zip(grads, scaled_rows(n)):
                gain_sum = gain_sum + col_sum(rows * scaled)
                bias_sum = bias_sum + col_sum(rows)
    if scaled_rows is not None:
        vec[pl.ds(0, 1), :] = gain_sum
        vec[pl.ds(2, 1), :] = bias_sum
    step = CHIPS_Z // 2
    part = gqkv_ref.shape[1] * gqkv_ref.shape[2] * step
    for c in range(2):
        gqkv_ref[pl.ds(c * step, step)] = (
            tn(gproj_ref[:, pl.ds(c * part, part)], z_ref[...])
            .astype(BF16)
            .reshape((step,) + gqkv_ref.shape[1:])
        )


def merge_halo(sizes, n, gh_ref, gmem_ref, from_right_ref, from_left_ref):
    first = n * sizes.rows
    back = from_right_ref[n].astype(F32)
    head = gh_ref[pl.ds(first, RIGHT_ROWS), :] + from_left_ref[n].astype(F32)
    middle = gh_ref[pl.ds(first + RIGHT_ROWS, sizes.rows - RIGHT_ROWS - LEFT_ROWS), :]
    tail = gh_ref[pl.ds(first + sizes.rows - LEFT_ROWS, LEFT_ROWS), :] + back[:LEFT_ROWS]
    mem = gmem_ref[pl.ds(n * sizes.segs, sizes.segs), :] + back[LEFT_ROWS + sizes.segs :]
    return jnp.concatenate([head, middle, tail], axis=0), mem


def pack_kernel(spots, qkv_ref, out_ref, up_ref, down_ref, *packed):
    eye = identity(LANES)
    high, wide, low = qkv_ref.shape[1], out_ref.shape[1], down_ref.shape[1]
    for layer, ref in enumerate(packed):
        up = tn(up_ref[layer], eye).astype(BF16)
        for z in range(ref.shape[0]):
            ref[z, pl.ds(spots.qkv[1], high), :] = qkv_ref[layer]
            ref[z, pl.ds(spots.out[1], wide), :] = out_ref[layer]
            ref[z, pl.ds(spots.up[1], up_ref.shape[2]), :] = up
            for part, (_, first) in enumerate(spots.down):
                ref[z, pl.ds(first, low), :] = down_ref[layer, :, pl.ds(part * LANES, LANES)]


def unpack_kernel(layers, small_at, *refs):
    sources, outs = refs[:-7], refs[-7:]
    qkv_ref, out_ref, up_ref, down_ref, gains_ref, biases_ref, ffn_bias_ref = outs
    eye = identity(LANES)
    high, wide, low = qkv_ref.shape[1], out_ref.shape[1], down_ref.shape[1]

    def total(source, first, rows):
        ref = sources[source]
        value = ref[0, pl.ds(first, rows), :].astype(F32)
        for z in range(1, ref.shape[0]):
            value = value + ref[z, pl.ds(first, rows), :].astype(F32)
        return value

    base = 0
    for layer, spots in enumerate(layers):
        qkv_ref[layer] = total(base + spots.qkv[0], spots.qkv[1], high)
        out_ref[layer] = total(base + spots.out[0], spots.out[1], wide)
        up_ref[layer] = nt(
            eye, total(base + spots.up[0], spots.up[1], up_ref.shape[2]).astype(BF16)
        )
        for part, (group, first) in enumerate(spots.down):
            down_ref[layer, :, pl.ds(part * LANES, LANES)] = total(base + group, first, low)
        base += 1 + max(group for group, _ in spots.down)
    sums = total(small_at[0], small_at[1], SMALL_ROWS)
    parts = gains_ref.shape[2] // LANES
    for layer in range(gains_ref.shape[0]):
        for part in range(parts):
            lanes = pl.ds(part * LANES, LANES)
            block = sums[(layer * parts + part) * TILE : (layer * parts + part + 1) * TILE]
            gains_ref[layer, :, lanes] = block[0:2]
            for row in range(biases_ref.shape[0]):
                biases_ref[row, pl.ds(layer, 1), lanes] = block[2 + row : 3 + row]
            for row in range(ffn_bias_ref.shape[1] // gains_ref.shape[2]):
                at = row * gains_ref.shape[2] + part * LANES
                ffn_bias_ref[pl.ds(layer, 1), pl.ds(at, LANES)] = block[8 + row : 9 + row]


def near_small_kernel(count, mine_ref, theirs_ref, second_ref, first_ref, out_ref):
    rows = out_ref.shape[1] - SMALL_ROWS

    def total(at, size):
        group = pl.ds(at, size)
        value = mine_ref[0, group, :].astype(F32) + theirs_ref[0, group, :].astype(F32)
        return (
            value + second_ref[0, group, :].astype(F32) + first_ref[group, :].astype(F32)
        ).astype(BF16)

    small = total(count * rows, SMALL_ROWS)
    for z in range(count):
        out_ref[z, pl.ds(0, rows), :] = total(z * rows, rows)
        out_ref[z, pl.ds(rows, SMALL_ROWS), :] = small


def first_layer_kernel(
    sizes, seqs, mats, spots, count_in, place_ref, starts_ref, frames_ref, left_ref, right_ref,
    gains_ref, biases_ref, ffn_bias_ref, row_bias_ref, *refs
):
    groups = in_groups(spots, refs[:count_in])
    (
        z_ref, proj_ref, probs_ref, att_ref, mixed_ref, mem_ref, next_ref, active_ref, slope_ref,
        low_ref, send_right_ref, send_left_ref, qkv_ref, out_ref, up_ref, down_ref, mask_ref,
        hidden_ref, sems,
    ) = refs[count_in:]
    wide = sizes.width
    copies = start_in(attn_pairs(mats, spots, groups, qkv_ref, out_ref, place_ref), sems, 0)
    ffn_copies = start_in(
        ffn_pairs(mats, spots, groups, up_ref, down_ref, place_ref), sems, len(copies)
    )
    gain = gains_ref[0, pl.ds(0, 1), :]
    bias = biases_ref[0, pl.ds(0, 1), :]
    pad = jnp.zeros((TILE - sizes.segs, wide), F32)
    for n in range(seqs):
        own = frames_ref[n].astype(F32)
        before = left_ref[n].astype(F32)
        hidden = norm_forward(own, gain, bias)[0]
        halo = norm_forward(before[before.shape[0] - LEFT_ROWS :], gain, bias)[0]
        after = norm_forward(right_ref[n].astype(F32), gain, bias)[0]
        memory = jnp.concatenate(
            [
                segment_mean(own),
                jnp.zeros((sizes.segs - before.shape[0] // SEG_LEN, wide), F32),
                segment_mean(before),
            ],
            axis=0,
        )
        base = n * sizes.ext
        z_ref[pl.ds(base, sizes.top), :] = jnp.concatenate(
            [segment_mean(hidden), pad], axis=0
        ).astype(BF16)
        z_ref[pl.ds(base + sizes.top, sizes.rows), :] = hidden.astype(BF16)
        z_ref[pl.ds(base + sizes.right_at, RIGHT_ROWS), :] = after.astype(BF16)
        z_ref[pl.ds(base + sizes.left_at, LEFT_ROWS), :] = halo.astype(BF16)
        z_ref[pl.ds(base + sizes.mem_at, MEM_ROWS), :] = memory.astype(BF16)
    fill_mask(sizes, seqs, starts_ref, place_ref, mask_ref)
    wait_all(copies)
    project(sizes, z_ref, qkv_ref, row_bias_ref, proj_ref)
    attend(sizes, seqs, proj_ref, mask_ref, probs_ref, att_ref)
    mixed = nt(att_ref[...], out_ref[...].reshape(-1, wide)) + biases_ref[0, pl.ds(3, 1), :]
    for n in range(seqs):
        base = n * sizes.queries
        mem_ref[pl.ds(n * sizes.segs, sizes.segs), :] = mixed[base : base + sizes.segs]
        mixed_ref[pl.ds(n * sizes.rows, sizes.rows), :] = (
            frames_ref[n].astype(F32) + mixed[base + sizes.top : base + sizes.top + sizes.rows]
        )
    mixed = mixed_ref[...]
    hidden, _, _ = norm_forward(mixed, gains_ref[0, pl.ds(1, 1), :], biases_ref[0, pl.ds(4, 1), :])
    hidden_ref[...] = hidden.astype(BF16)
    next_ref[...] = mixed + biases_ref[0, pl.ds(5, 1), :]
    wait_all(ffn_copies)

    def body(c, carry):
        at_lane = pl.multiple_of(c * wide, wide)
        upward = nt(hidden_ref[...], up_block(up_ref, c, wide))
        upward = upward + ffn_bias_ref[pl.ds(0, 1), pl.ds(at_lane, wide)]
        active, slope = gelu_both(upward)
        active = active.astype(BF16)
        active_ref[:, pl.ds(at_lane, wide)] = active
        slope_ref[:, pl.ds(at_lane, wide)] = slope.astype(BF16)
        next_ref[...] += nt(active, down_block(down_ref, c, wide))
        return carry

    lax.fori_loop(0, sizes.ff // wide, body, 0)
    low, _, _ = norm_forward(
        next_ref[...], gains_ref[1, pl.ds(0, 1), :], biases_ref[1, pl.ds(0, 1), :]
    )
    low = low.astype(BF16)
    low_ref[...] = low
    for n in range(seqs):
        base = n * sizes.rows
        send_right_ref[n, pl.ds(0, LEFT_ROWS), :] = low[
            base + sizes.rows - LEFT_ROWS : base + sizes.rows
        ]
        send_right_ref[n, pl.ds(LEFT_ROWS, MEM_ROWS), :] = jnp.concatenate(
            [
                mem_ref[pl.ds(n * sizes.segs, sizes.segs), :],
                jnp.zeros((MEM_ROWS - sizes.segs, wide), F32),
            ],
            axis=0,
        ).astype(BF16)
        send_left_ref[n] = low[base : base + RIGHT_ROWS]


def last_layer_kernel(
    sizes, seqs, mats, spots, count_in, count_out, place_ref, starts_ref, low_ref, left_ref,
    right_ref, mem_ref, inputs_ref, out_grad_ref, gains_ref, biases_ref, ffn_bias_ref,
    row_bias_ref, *refs
):
    groups = in_groups(spots, refs[:count_in])
    (encoded_ref, gz_ref, gh_ref, gmem_ref, back_left_ref, back_right_ref, vec) = refs[
        count_in : count_in + 7
    ]
    hbm_out = refs[count_in + 7 : count_in + 7 + count_out]
    (
        qkv_ref, out_ref, up_ref, down_ref, gqkv_ref, gout_ref, gup_ref, gdown_ref, mask_ref,
        z_ref, proj_ref, probs_ref, att_ref, hidden_ref, go_ref, gproj_ref, branch_ref,
        grad_low_ref, grad_hidden_ref, sems,
    ) = refs[count_in + 7 + count_out :]
    outs_to = hbm_out
    if spots is not None:
        outs_to = [[ref.at[k] for ref in hbm_out for k in range(ref.shape[0])]]
    wide = sizes.width
    attn_copies = start_in(attn_pairs(mats, spots, groups, qkv_ref, out_ref, place_ref), sems, 0)
    ffn_copies = start_in(
        ffn_pairs(mats, spots, groups, up_ref, down_ref, place_ref), sems, len(attn_copies)
    )
    vec[...] = jnp.zeros_like(vec)
    for n in range(seqs):
        base = n * sizes.ext
        z_ref[pl.ds(base, sizes.rows), :] = low_ref[pl.ds(n * sizes.rows, sizes.rows), :]
        z_ref[pl.ds(base + sizes.right_at, RIGHT_ROWS), :] = right_ref[n]
        z_ref[pl.ds(base + sizes.left_at, LEFT_ROWS), :] = left_ref[n, pl.ds(0, LEFT_ROWS), :]
        memory = jnp.concatenate(
            [
                mem_ref[pl.ds(n * sizes.segs, sizes.segs), :],
                left_ref[n, pl.ds(LEFT_ROWS, MEM_ROWS), :].astype(F32)[: sizes.segs],
            ],
            axis=0,
        )
        z_ref[pl.ds(base + sizes.mem_at, MEM_ROWS), :] = memory.astype(BF16)
        grad_low_ref[pl.ds(n * sizes.rows, sizes.rows), :] = out_grad_ref[n]
    fill_mask(sizes, seqs, starts_ref, place_ref, mask_ref)
    wait_all(attn_copies)
    project(sizes, z_ref, qkv_ref, row_bias_ref, proj_ref)
    attend(sizes, seqs, proj_ref, mask_ref, probs_ref, att_ref)
    mixed = (
        inputs_ref[...]
        + nt(att_ref[...], out_ref[...].reshape(-1, wide))
        + biases_ref[1, pl.ds(3, 1), :]
    )
    gain = gains_ref[1, pl.ds(1, 1), :]
    hidden, scaled, inverse = norm_forward(mixed, gain, biases_ref[1, pl.ds(4, 1), :])
    hidden_ref[...] = hidden.astype(BF16)
    for n in range(seqs):
        encoded_ref[n] = mixed[n * sizes.rows : (n + 1) * sizes.rows] + biases_ref[
            1, pl.ds(5, 1), :
        ]
    grad_hidden_ref[...] = jnp.zeros_like(grad_hidden_ref)
    wait_all(ffn_copies)

    def body(c, carry):
        at_lane = pl.multiple_of(c * wide, wide)
        upward = nt(hidden_ref[...], up_block(up_ref, c, wide))
        upward = upward + ffn_bias_ref[pl.ds(1, 1), pl.ds(at_lane, wide)]
        active, slope = gelu_both(upward)
        active = active.astype(BF16)
        made = nt(active, down_block(down_ref, c, wide))
        for n in range(seqs):
            encoded_ref[n] += made[n * sizes.rows : (n + 1) * sizes.rows]
        grad_hidden_ref[...] += ffn_back_step(
            sizes, c, wide, grad_low_ref[...], hidden_ref[...], active, slope, up_ref, down_ref,
            gup_ref, gdown_ref, vec,
        )
        return carry

    lax.fori_loop(0, sizes.ff // wide, body, 0)
    out_at = len(attn_copies) + len(ffn_copies)
    outs = start_out(
        ffn_pairs(mats, spots, outs_to, gup_ref, gdown_ref, place_ref), sems, out_at
    )
    grad = grad_low_ref[...].astype(F32)
    grad_hidden = grad_hidden_ref[...]
    vec[pl.ds(1, 1), :] = col_sum(grad_hidden * scaled)
    vec[pl.ds(6, 1), :] = col_sum(grad_hidden)
    vec[pl.ds(7, 1), :] = col_sum(grad)
    gz = grad + norm_backward(grad_hidden, scaled, inverse, gain)
    gz_ref[...] = gz
    attn_back_stage(
        sizes, seqs, gz, None, att_ref, proj_ref, probs_ref, z_ref, qkv_ref, out_ref, gqkv_ref,
        gout_ref, go_ref, gproj_ref, branch_ref, vec, gh_ref, gmem_ref, back_left_ref,
        back_right_ref,
    )
    outs = outs + start_out(
        attn_pairs(mats, spots, outs_to, gqkv_ref, gout_ref, place_ref),
        sems,
        out_at + len(outs),
    )
    wait_all(outs)


def first_back_kernel(
    last, sizes, seqs, mats, spots, count_in, count_out, place_ref, inputs_ref, gz_in_ref,
    gh_in_ref, gmem_in_ref, from_right_ref, from_left_ref, mixed_ref, active_ref, slope_ref,
    att_ref, probs_ref, proj_ref, z_ref, frames_ref, left_ref, right_ref, gains_ref, biases_ref,
    last_vec, *refs
):
    groups = in_groups(spots, refs[:count_in])
    gz_ref, gh_ref, gmem_ref, back_left_ref, back_right_ref, upper_vec, vec = refs[
        count_in : count_in + 7
    ]
    refs = refs[count_in + 7 :]
    hbm_out = refs[:count_out]
    (
        qkv_ref, out_ref, up_ref, down_ref, gqkv_ref, gout_ref, gup_ref, gdown_ref, hidden_ref,
        grad_low_ref, grad_ref, grad_hidden_ref, grad_mem_ref, go_ref, gproj_ref, branch_ref,
        small_ref, sems,
    ) = refs[count_out:]
    wide = sizes.width
    small = []
    outs_to = hbm_out
    if spots is not None:
        classes = count_in // 2
        rows = mats.attn_rows + mats.ffn_rows
        end = CHIPS_Z * rows
        each = [ref.at[k] for ref in hbm_out for k in range(classes)]
        small = [ref.at[pl.ds(end, SMALL_ROWS), :] for ref in each]
        outs_to = [[ref.at[pl.ds(0, end), :].reshape(CHIPS_Z, rows, LANES) for ref in each]]
    ffn_copies = start_in(ffn_pairs(mats, spots, groups, up_ref, down_ref, place_ref), sems, 0)
    attn_copies = start_in(
        attn_pairs(mats, spots, groups, qkv_ref, out_ref, place_ref), sems, len(ffn_copies)
    )
    vec[...] = jnp.zeros_like(vec)
    upper_vec[...] = jnp.zeros_like(upper_vec)
    gain = gains_ref[1, pl.ds(0, 1), :]
    gain_sum = jnp.zeros((1, wide), F32)
    bias_sum = jnp.zeros((1, wide), F32)
    for n in range(seqs):
        rows = pl.ds(n * sizes.rows, sizes.rows)
        _, scaled, inverse = norm_forward(
            inputs_ref[rows, :], gain, biases_ref[1, pl.ds(0, 1), :]
        )
        total, mem = merge_halo(last, n, gh_in_ref, gmem_in_ref, from_right_ref, from_left_ref)
        gain_sum = gain_sum + col_sum(total * scaled)
        bias_sum = bias_sum + col_sum(total)
        grad = gz_in_ref[rows, :] + norm_backward(total, scaled, inverse, gain)
        grad_ref[rows, :] = grad
        grad_low_ref[rows, :] = grad.astype(BF16)
        grad_mem_ref[pl.ds(n * sizes.segs, sizes.segs), :] = mem
    upper_vec[pl.ds(0, 1), :] = gain_sum
    upper_vec[pl.ds(2, 1), :] = bias_sum
    gain = gains_ref[0, pl.ds(1, 1), :]
    hidden, scaled, inverse = norm_forward(
        mixed_ref[...], gain, biases_ref[0, pl.ds(4, 1), :]
    )
    hidden_ref[...] = hidden.astype(BF16)
    grad_hidden_ref[...] = jnp.zeros_like(grad_hidden_ref)
    wait_all(ffn_copies)

    def body(c, carry):
        at_lane = pl.multiple_of(c * wide, wide)
        grad_hidden_ref[...] += ffn_back_step(
            sizes, c, wide, grad_low_ref[...], hidden_ref[...],
            active_ref[:, pl.ds(at_lane, wide)], slope_ref[:, pl.ds(at_lane, wide)].astype(F32),
            up_ref, down_ref, gup_ref, gdown_ref, vec,
        )
        return carry

    lax.fori_loop(0, sizes.ff // wide, body, 0)
    out_at = len(ffn_copies) + len(attn_copies)
    outs = start_out(
        ffn_pairs(mats, spots, outs_to, gup_ref, gdown_ref, place_ref), sems, out_at
    )
    grad_hidden = grad_hidden_ref[...]
    grad = grad_ref[...]
    vec[pl.ds(1, 1), :] = col_sum(grad_hidden * scaled)
    vec[pl.ds(6, 1), :] = col_sum(grad_hidden)
    vec[pl.ds(7, 1), :] = col_sum(grad)
    gz = grad + norm_backward(grad_hidden, scaled, inverse, gain)
    gz_ref[...] = gz

    def scaled_rows(n):
        before = left_ref[n, pl.ds(left_ref.shape[1] - LEFT_ROWS, LEFT_ROWS), :]
        parts = (frames_ref[n], right_ref[n], before)
        first_gain = gains_ref[0, pl.ds(0, 1), :]
        first_bias = biases_ref[0, pl.ds(0, 1), :]
        return [norm_forward(part.astype(F32), first_gain, first_bias)[1] for part in parts]

    wait_all(attn_copies)
    attn_back_stage(
        sizes, seqs, gz, grad_mem_ref, att_ref, proj_ref, probs_ref, z_ref, qkv_ref, out_ref,
        gqkv_ref, gout_ref, go_ref, gproj_ref, branch_ref, vec, gh_ref, gmem_ref, back_left_ref,
        back_right_ref, scaled_rows,
    )
    outs = outs + start_out(
        attn_pairs(mats, spots, outs_to, gqkv_ref, gout_ref, place_ref),
        sems,
        out_at + len(outs),
    )
    parts = sizes.width // LANES
    for layer, total in enumerate((vec[...], last_vec[...] + upper_vec[...])):
        for part in range(parts):
            small_ref[pl.ds((layer * parts + part) * TILE, TILE), :] = total[
                :, part * LANES : (part + 1) * LANES
            ].astype(BF16)
    outs = outs + start_out([(ref, small_ref) for ref in small], sems, out_at + len(outs))
    wait_all(outs)


def frames_grad_kernel(
    sizes, seqs, frames_ref, gz_ref, gh_ref, gmem_ref, from_right_ref, from_left_ref, gains_ref,
    biases_ref, grad_ref
):
    gain = gains_ref[0, pl.ds(0, 1), :]
    for n in range(seqs):
        _, scaled, inverse = norm_forward(
            frames_ref[n].astype(F32), gain, biases_ref[0, pl.ds(0, 1), :]
        )
        total, mem = merge_halo(sizes, n, gh_ref, gmem_ref, from_right_ref, from_left_ref)
        grad_ref[n] = (
            gz_ref[pl.ds(n * sizes.rows, sizes.rows), :]
            + norm_backward(total, scaled, inverse, gain)
            + segment_spread(sizes.rows, sizes.width, mem * (1.0 / SEG_LEN))
        )


def shifted(value, axis, by):
    size = lax.axis_size(axis)
    pairs = [(i, i + by) for i in range(size) if 0 <= i + by < size]
    return lax.ppermute(value, axis, pairs)


def permuted(value, move):
    reps = lax.axis_size("rep")
    pairs = []
    for flat in range(lax.axis_size("seg") * reps):
        seg, rep = divmod(flat, reps)
        z, y, x, core = move(seg // CHIPS_Y, seg % CHIPS_Y, rep // 2, rep % 2)
        pairs.append((flat, (z * CHIPS_Y + y) * reps + 2 * x + core))
    return lax.ppermute(value, ("seg", "rep"), pairs)


def across_first(value):
    return permuted(value, lambda z, y, x, c: (z, y, x ^ 1, c) if c == 0 else (z, y ^ 1, x, c))


def across_second(value):
    return permuted(value, lambda z, y, x, c: (z, y ^ 1, x, c) if c == 0 else (z, y, x ^ 1, c))


def other_core(value):
    return permuted(value, lambda z, y, x, c: (z, y, x, c ^ 1))


def after(value, *others):
    return lax.optimization_barrier((value,) + others)[0]


def swap_z(blocks):
    groups = [
        [z * CHIPS_Y + y for z in range(CHIPS_Z)] for y in range(CHIPS_Y)
    ]
    return lax.all_to_all(blocks, "seg", 0, 0, axis_index_groups=groups, tiled=True)


def gather_sides(here):
    return [here, across_first(here), across_second(here)]


def both_cores(blocks):
    return blocks + [other_core(block) for block in blocks]


def summed(*parts):
    total = parts[0].astype(F32)
    for part in parts[1:]:
        total = total + part.astype(F32)
    return total.astype(BF16)


def first_rows(rows):
    return pl.BlockSpec((1, rows, LANES), lambda i: (0, 0, 0))


def sum_everywhere(value):
    count = lax.axis_size("seg") * lax.axis_size("rep")
    bit = 1
    while bit < count:
        value = value + lax.ppermute(value, ("seg", "rep"), [(i, i ^ bit) for i in range(count)])
        bit *= 2
    return value


def vmem_spec():
    return pl.BlockSpec(memory_space=pltpu.VMEM)


def smem_spec():
    return pl.BlockSpec(memory_space=pltpu.SMEM)


def hbm_spec():
    return pl.BlockSpec(memory_space=pl.ANY)


def call(body, in_specs, out_shapes, out_specs, scratch, args, flops=0, moved=0, grid=()):
    return pl.pallas_call(
        body,
        grid=grid,
        in_specs=in_specs,
        out_shape=tuple(jax.ShapeDtypeStruct(shape, kind) for shape, kind in out_shapes),
        out_specs=tuple(out_specs),
        scratch_shapes=scratch,
        compiler_params=pltpu.CompilerParams(vmem_limit_bytes=VMEM_BYTES),
        cost_estimate=pl.CostEstimate(flops=flops, bytes_accessed=moved, transcendentals=0),
    )(*args)


def on_device(
    frames,
    utt_segments,
    out_grad,
    qkv_weight,
    out_weight,
    ffn_in_weight,
    ffn_out_weight,
    norm_gains,
    biases,
    ffn_bias,
):
    micros, groups, rows, width = frames.shape
    seqs = micros * groups
    ff = ffn_bias.shape[1]
    reps = lax.axis_size("rep")
    seg_count = lax.axis_size("seg")
    mats = Matrices(width, ff)
    by_blocks = width // reps == LANES and reps == 4 and seg_count == BLOCKS
    first = Sizes(rows, width, ff, True)
    last = Sizes(rows, width, ff, False)
    own = seqs * rows
    mem_own = seqs * first.segs

    seg_at = lax.axis_index("seg")
    seg_base = seg_at * first.segs
    rep_at = lax.axis_index("rep")
    place = [seg_base, jnp.int32(first.segs * seg_count)]
    y_at, x_at, core_at = seg_at % CHIPS_Y, rep_at // 2, rep_at % 2
    for other in range(2):
        core = lax.bitwise_xor(core_at, other)
        for hop2 in range(2):
            for hop1 in range(2):
                x_hop = jnp.where(core == 0, hop1, hop2)
                y_hop = jnp.where(core == 0, hop2, hop1)
                place.append(lax.bitwise_xor(y_at, y_hop))
                place.append((lax.bitwise_xor(x_at, x_hop) * 2 + core) * LANES)
    place = jnp.stack([jnp.asarray(entry, jnp.int32) for entry in place])
    lengths = utt_segments.reshape(seqs, utt_segments.shape[2])
    starts = (jnp.cumsum(lengths, axis=1) - lengths).astype(jnp.int32)
    zero_bias = jnp.zeros((width,), F32)
    row_bias = jnp.stack(
        [jnp.concatenate([biases[l, 1], zero_bias, biases[l, 2]]) for l in range(LAYERS)]
    ).reshape(LAYERS, 1, 3 * width)

    frames_own = frames.reshape(seqs, rows, width)
    grads_own = out_grad.reshape(seqs, rows, width)
    far = MEM_LEN * SEG_LEN
    frames_left = shifted(frames_own[:, rows - far :], "seg", 1)
    frames_right = shifted(frames_own[:, :RIGHT_ROWS], "seg", -1)

    attn_rows, ffn_rows = mats.attn_rows, mats.ffn_rows
    if by_blocks:
        qkv_t, out_t, down_t = (
            jnp.swapaxes(member, 1, 2) for member in (qkv_weight, out_weight, ffn_out_weight)
        )
        all_rows = attn_rows + ffn_rows
        spots = Spots(mats)
        shards = call(
            lambda *refs: pack_kernel(spots, *refs),
            [vmem_spec()] * 4,
            [((CHIPS_Z, all_rows, LANES), BF16)] * LAYERS,
            [vmem_spec()] * LAYERS,
            [],
            (qkv_t, out_t, ffn_in_weight, down_t),
        )
        sides0 = gather_sides(after(swap_z(shards[0]), frames_left, frames_right))
        place, starts, row_bias, sent = lax.optimization_barrier(
            (place, starts, row_bias, after(shards[1], sides0[0]))
        )
        sides1 = gather_sides(swap_z(sent))
        first_all = both_cores(sides0 + [across_second(after(sides0[1], sides1[0]))])
        classes = len(first_all) // 2
        grad_outs0 = [((classes, CHIPS_Z * all_rows + SMALL_ROWS, LANES), BF16)] * 2
        grad_outs1 = [((classes, CHIPS_Z, all_rows, LANES), BF16)] * 2
        copies_in = len(first_all) * (3 + mats.down_parts)
    else:
        whole = []
        for member, shape in zip(
            (qkv_weight, out_weight, ffn_in_weight, ffn_out_weight),
            (mats.qkv, mats.out, mats.up, mats.down),
        ):
            member = lax.all_gather(member, "rep", axis=1, tiled=True)
            member = lax.all_gather(member, "seg", axis=2, tiled=True)
            whole.append(jnp.swapaxes(member, 1, 2).reshape((LAYERS,) + shape))
        first_all = [member[0] for member in whole]
        last_all = [member[1] for member in whole]
        spots = None
        grad_outs0 = grad_outs1 = [
            (shape, BF16) for shape in (mats.qkv, mats.out, mats.up, mats.down)
        ]
        copies_in = 4
    dma = pltpu.SemaphoreType.DMA

    matrices = [pltpu.VMEM(shape, BF16) for shape in (mats.qkv, mats.out, mats.up, mats.down)]

    (
        z0, proj0, probs0, att0, mixed0, mem1, x1, active0, slope0, low1, send_right, send_left,
    ) = call(
        lambda *refs: first_layer_kernel(
            first, seqs, mats, spots, len(first_all), *refs
        ),
        [smem_spec()] * 2 + [vmem_spec()] * 7 + [hbm_spec()] * len(first_all),
        [
            ((seqs * first.ext, width), BF16),
            ((seqs * first.ext, 3 * width), BF16),
            ((seqs * first.pairs, 2 * first.queries, first.keys), BF16),
            ((seqs * first.queries, width), BF16),
            ((own, width), F32),
            ((mem_own, width), F32),
            ((own, width), F32),
            ((own, ff), BF16),
            ((own, ff), BF16),
            ((own, width), BF16),
            ((seqs, BACK_ROWS, width), BF16),
            ((seqs, RIGHT_ROWS, width), BF16),
        ],
        [vmem_spec()] * 12,
        matrices
        + [
            pltpu.VMEM((seqs, first.queries, first.keys), F32),
            pltpu.VMEM((own, width), BF16),
            dma((copies_in,)),
        ],
        (place, starts, frames_own, frames_left, frames_right, norm_gains, biases, ffn_bias,
         row_bias[0]) + tuple(first_all),
        flops=24 * own * (4 * width * width + 2 * width * ff) // 2,
        moved=2 * (4 * width * width + 2 * width * ff),
    )
    left1 = shifted(send_right, "seg", 1)
    right1 = shifted(send_left, "seg", -1)
    if by_blocks:
        last_side = across_second(after(sides1[1], sides1[2], low1))
        last_all = both_cores(sides1 + [last_side])
        last_all[-1] = other_core(after(last_side, left1, right1))

    vec_shape = (TILE, width)
    outs = call(
        lambda *refs: last_layer_kernel(
            last, seqs, mats, spots, len(last_all), len(grad_outs1), *refs
        ),
        [smem_spec()] * 2 + [vmem_spec()] * 10 + [hbm_spec()] * len(last_all),
        [
            ((seqs, rows, width), F32),
            ((own, width), F32),
            ((own, width), F32),
            ((mem_own, width), F32),
            ((seqs, BACK_ROWS, width), BF16),
            ((seqs, RIGHT_ROWS, width), BF16),
            (vec_shape, F32),
        ]
        + grad_outs1,
        [vmem_spec()] * 7 + [hbm_spec()] * len(grad_outs1),
        matrices
        + matrices
        + [
            pltpu.VMEM((seqs, last.queries, last.keys), F32),
            pltpu.VMEM((seqs * last.ext, width), BF16),
            pltpu.VMEM((seqs * last.ext, 3 * width), BF16),
            pltpu.VMEM((seqs * last.pairs, 2 * last.queries, last.keys), BF16),
            pltpu.VMEM((seqs * last.queries, width), BF16),
            pltpu.VMEM((own, width), BF16),
            pltpu.VMEM((seqs * last.queries, width), BF16),
            pltpu.VMEM((seqs * last.ext, 3 * width), BF16),
            pltpu.VMEM((seqs * last.queries, width), BF16),
            pltpu.VMEM((own, width), BF16),
            pltpu.VMEM((own, width), F32),
            dma((2 * copies_in,)),
        ],
        (place, starts, low1, left1, right1, mem1, x1, grads_own, norm_gains, biases, ffn_bias,
         row_bias[1]) + tuple(last_all),
        flops=30 * own * (4 * width * width + 2 * width * ff),
        moved=4 * (4 * width * width + 2 * width * ff),
    )
    encoded, gz1, gh1, gmem1, back_left1, back_right1, vec1 = outs[:7]
    grad_blocks1 = outs[7:]
    from_right1 = shifted(back_left1, "seg", -1)
    from_left1 = shifted(back_right1, "seg", 1)

    gh1_tied = gh1
    if by_blocks:
        mine1, theirs1 = grad_blocks1[0], other_core(grad_blocks1[1])
        far1 = summed(mine1[2:], theirs1[2:])
        gh1_tied = after(gh1, far1)
    gz0, gh0, gmem0, back_left0, back_right0, upper_vec, vec0, *grad_blocks0 = call(
        lambda *refs: first_back_kernel(
            last, first, seqs, mats, spots, len(first_all), len(grad_outs0), *refs
        ),
        [smem_spec()] + [vmem_spec()] * 19 + [hbm_spec()] * len(first_all),
        [
            ((own, width), F32),
            ((own, width), F32),
            ((mem_own, width), F32),
            ((seqs, BACK_ROWS, width), BF16),
            ((seqs, RIGHT_ROWS, width), BF16),
            (vec_shape, F32),
            (vec_shape, F32),
        ]
        + grad_outs0,
        [vmem_spec()] * 7 + [hbm_spec()] * len(grad_outs0),
        matrices
        + matrices
        + [
            pltpu.VMEM((own, width), BF16),
            pltpu.VMEM((own, width), BF16),
            pltpu.VMEM((own, width), F32),
            pltpu.VMEM((own, width), F32),
            pltpu.VMEM((mem_own, width), F32),
            pltpu.VMEM((seqs * first.queries, width), BF16),
            pltpu.VMEM((seqs * first.ext, 3 * width), BF16),
            pltpu.VMEM((seqs * first.queries, width), BF16),
            pltpu.VMEM((SMALL_ROWS, LANES), BF16),
            dma((2 * copies_in + 8,)),
        ],
        (place, x1, gz1, gh1_tied, gmem1, from_right1, from_left1, mixed0, active0, slope0, att0,
         probs0, proj0, z0, frames_own, frames_left, frames_right, norm_gains, biases, vec1)
        + tuple(first_all),
        flops=28 * own * (4 * width * width + 2 * width * ff),
        moved=4 * (4 * width * width + 2 * width * ff),
    )
    from_right0 = shifted(back_left0, "seg", -1)
    from_left0 = shifted(back_right0, "seg", 1)
    gz0_last = gz0
    if by_blocks:
        second1 = across_second(far1)
        near1 = summed(mine1[1], theirs1[1], second1[1])
        first1 = across_first(near1)
        mine0, theirs0 = grad_blocks0[0], other_core(after(grad_blocks0[1], second1))
        far0 = after(summed(mine0[2:], theirs0[2:]), first1)
        second0 = across_second(far0)
        total1 = summed(mine1[0], theirs1[0], second1[0], after(first1, far0))
        last_parts = swap_z(total1)
        mid0 = summed(mine0[1], theirs0[1], after(second0, total1)[1])
        first0 = after(across_first(mid0), last_parts)
        near0 = call(
            lambda *refs: near_small_kernel(CHIPS_Z, *refs),
            [first_rows(mine0.shape[1])] * 3 + [vmem_spec()],
            [((CHIPS_Z, all_rows + SMALL_ROWS, LANES), BF16)],
            [vmem_spec()],
            [],
            [mine0, theirs0, second0, first0],
            grid=(1,),
        )[0]
        first_parts = swap_z(near0)
        gz0_last = after(gz0, near0)
    frames_grad = call(
        lambda *refs: frames_grad_kernel(first, seqs, *refs),
        [vmem_spec()] * 8,
        [((seqs, rows, width), F32)],
        [vmem_spec()],
        [],
        (frames_own, gz0_last, gh0, gmem0, from_right0, from_left0, norm_gains, biases),
    )[0]

    if by_blocks:
        shapes = [member.shape for member in (qkv_t, out_t, ffn_in_weight, down_t)]
        shapes += [norm_gains.shape, (biases.shape[1], LAYERS, width), ffn_bias.shape]
        reduced = call(
            lambda *refs: unpack_kernel([spots, spots], (0, all_rows), *refs),
            [vmem_spec()] * LAYERS,
            [(shape, F32) for shape in shapes],
            [vmem_spec()] * len(shapes),
            [],
            [after(first_parts, frames_grad), last_parts],
        )
        small = reduced[4], jnp.swapaxes(reduced[5], 0, 1), reduced[6]
        reduced = [
            jnp.swapaxes(reduced[0], 1, 2),
            jnp.swapaxes(reduced[1], 1, 2),
            reduced[2],
            jnp.swapaxes(reduced[3], 1, 2),
        ]
    else:
        reduced = []
        for member0, member1 in zip(grad_blocks0, grad_blocks1):
            both = jnp.stack([member0, member1]).reshape(LAYERS, -1, member0.shape[3])
            both = jnp.swapaxes(both, 1, 2)
            both = lax.psum_scatter(both, "seg", scatter_dimension=2, tiled=True)
            both = lax.psum_scatter(both, "rep", scatter_dimension=1, tiled=True)
            reduced.append(both.astype(F32))
        small = sum_everywhere(jnp.stack([vec0, vec1 + upper_vec]))
        small = small[:, 0:2], small[:, 2:8], small[:, 8:12].reshape(ffn_bias.shape)

    return (
        encoded.reshape(frames.shape),
        frames_grad.reshape(frames.shape),
        reduced[0],
        reduced[1],
        reduced[2],
        reduced[3],
        small[0],
        small[1],
        small[2],
    )


def solution(mesh):
    in_specs = (
        P(None, "rep", "seg", None),
        P(None, "rep", None),
        P(None, "rep", "seg", None),
        P(None, "rep", "seg"),
        P(None, "rep", "seg"),
        P(None, "rep", "seg"),
        P(None, "rep", "seg"),
        P(),
        P(),
        P(),
    )
    out_specs = (
        P(None, "rep", "seg", None),
        P(None, "rep", "seg", None),
        P(None, "rep", "seg"),
        P(None, "rep", "seg"),
        P(None, "rep", "seg"),
        P(None, "rep", "seg"),
        P(),
        P(),
        P(),
    )
    return jax.shard_map(
        on_device, mesh=mesh, in_specs=in_specs, out_specs=out_specs, check_vma=False
    )
```

```python
import jax
import jax.numpy as jnp
from jax import lax
from jax.experimental import pallas as pl
from jax.experimental.pallas import tpu as pltpu
from jax.sharding import PartitionSpec as P

HEADS = 8
SEG_LEN = 16
LEFT_LEN = 30
RIGHT_LEN = 4
MEM_LEN = 4
LAYERS = 2

EPS = 1e-05
ROOT_HALF = 0.7071067811865476
INV_ROOT_TWO_PI = 0.3989422804014327

LANES = 128
TILE = 16
RIGHT_ROWS = 16
LEFT_ROWS = 32
MEM_ROWS = 16
BACK_ROWS = LEFT_ROWS + MEM_ROWS
CHIPS_Z = 4
CHIPS_Y = 2
BLOCKS = CHIPS_Z * CHIPS_Y
SMALL_ROWS = 128
VMEM_BYTES = 56 * 1024 * 1024

BF16 = jnp.bfloat16
F32 = jnp.float32


def nn(a, b):
    return lax.dot_general(a, b, (((1,), (0,)), ((), ())), preferred_element_type=F32)


def nt(a, b):
    return lax.dot_general(a, b, (((1,), (1,)), ((), ())), preferred_element_type=F32)


def tn(a, b):
    return lax.dot_general(a, b, (((0,), (0,)), ((), ())), preferred_element_type=F32)


def col_sum(value):
    return jnp.sum(value, axis=0, keepdims=True)


def norm_forward(inputs, gain, bias):
    center = inputs - jnp.mean(inputs, axis=1, keepdims=True)
    inverse = lax.rsqrt(jnp.mean(center * center, axis=1, keepdims=True) + EPS)
    scaled = center * inverse
    return scaled * gain + bias, scaled, inverse


def norm_backward(grad_in, scaled, inverse, gain):
    grad_scaled = grad_in * gain
    return inverse * (
        grad_scaled
        - jnp.mean(grad_scaled, axis=1, keepdims=True)
        - scaled * jnp.mean(grad_scaled * scaled, axis=1, keepdims=True)
    )


def segment_mean(inputs):
    rows, width = inputs.shape
    return jnp.mean(inputs.reshape(rows // SEG_LEN, SEG_LEN, width), axis=1)


def segment_spread(rows, width, per_segment):
    segs = rows // SEG_LEN
    return jnp.broadcast_to(per_segment[:, None, :], (segs, SEG_LEN, width)).reshape(rows, width)


def identity(size):
    row = lax.broadcasted_iota(jnp.int32, (size, size), 0)
    col = lax.broadcasted_iota(jnp.int32, (size, size), 1)
    return (row == col).astype(F32).astype(BF16)


class Sizes:
    def __init__(self, rows, width, ff, with_summary):
        self.rows = rows
        self.width = width
        self.ff = ff
        self.segs = rows // SEG_LEN
        self.top = TILE if with_summary else 0
        self.keys = rows + RIGHT_ROWS + LEFT_ROWS + MEM_ROWS
        self.ext = self.top + self.keys
        self.queries = self.top + rows
        self.right_at = self.top + rows
        self.left_at = self.right_at + RIGHT_ROWS
        self.mem_at = self.left_at + LEFT_ROWS
        self.pairs = width // LANES


class Matrices:
    def __init__(self, width, ff):
        self.qkv = (CHIPS_Z, CHIPS_Y, 3 * width // BLOCKS, width)
        self.out = (CHIPS_Z, CHIPS_Y, width // BLOCKS, width)
        self.up = (CHIPS_Z, CHIPS_Y, ff // BLOCKS, width)
        self.down = (CHIPS_Z, CHIPS_Y, width // BLOCKS, ff)
        self.down_parts = ff // width
        self.attn_rows = self.qkv[2] + self.out[2]
        self.ffn_rows = self.up[2] + self.down_parts * self.down[2]


class Spots:
    def __init__(self, mats):
        high, wide, up, low = mats.qkv[2], mats.out[2], mats.up[2], mats.down[2]
        self.qkv = (0, 0)
        self.out = (0, high)
        self.up = (0, high + wide)
        self.down = [(0, high + wide + up + low * part) for part in range(mats.down_parts)]


def attn_pairs(mats, spots, groups, qkv_ref, out_ref, place_ref):
    if spots is None:
        return [(groups[0], qkv_ref), (groups[1], out_ref)]
    pairs = []
    for k in range(len(groups[0])):
        row = place_ref[2 + 2 * k]
        lane = pl.multiple_of(place_ref[3 + 2 * k], LANES)
        for (group, first), ref, shape in (
            (spots.qkv, qkv_ref, mats.qkv),
            (spots.out, out_ref, mats.out),
        ):
            block = groups[group][k]
            pairs.append(
                (
                    block.at[:, pl.ds(first, shape[2]), :],
                    ref.at[:, row, :, pl.ds(lane, LANES)],
                )
            )
    return pairs


def ffn_pairs(mats, spots, groups, up_ref, down_ref, place_ref):
    if spots is None:
        return [(groups[2], up_ref), (groups[3], down_ref)]
    pairs = []
    for k in range(len(groups[0])):
        row = place_ref[2 + 2 * k]
        lane = pl.multiple_of(place_ref[3 + 2 * k], LANES)
        group, first = spots.up
        block = groups[group][k]
        pairs.append(
            (block.at[:, pl.ds(first, mats.up[2]), :], up_ref.at[:, row, :, pl.ds(lane, LANES)])
        )
        for part, (group, first) in enumerate(spots.down):
            there = pl.multiple_of(
                place_ref[3 + 2 * k] * mats.down_parts + part * LANES, LANES
            )
            block = groups[group][k]
            pairs.append(
                (
                    block.at[:, pl.ds(first, mats.down[2]), :],
                    down_ref.at[:, row, :, pl.ds(there, LANES)],
                )
            )
    return pairs


def start_in(pairs, sems, at):
    copies = [pltpu.make_async_copy(s, d, sems.at[at + i]) for i, (s, d) in enumerate(pairs)]
    for copy in copies:
        copy.start()
    return copies


def start_out(pairs, sems, at):
    copies = [pltpu.make_async_copy(d, s, sems.at[at + i]) for i, (s, d) in enumerate(pairs)]
    for copy in copies:
        copy.start()
    return copies


def in_groups(spots, refs):
    return refs if spots is None else [refs]


def wait_all(copies):
    for copy in copies:
        copy.wait()


def fill_mask(sizes, seqs, starts_ref, place_ref, mask_ref):
    shape = (sizes.queries, sizes.keys)
    row = lax.broadcasted_iota(jnp.int32, shape, 0)
    col = lax.broadcasted_iota(jnp.int32, shape, 1)
    base = place_ref[0]
    total = place_ref[1]
    query = jnp.where(row < sizes.top, row, lax.shift_right_arithmetic(row - sizes.top, 4))
    left_at = sizes.rows + RIGHT_ROWS
    mem_at = left_at + LEFT_ROWS
    spot = jnp.where(col < left_at, col, col - mem_at)
    mem_seg = jnp.where(col < mem_at + sizes.segs, col - mem_at, col - mem_at - 2 * sizes.segs)
    key_seg = jnp.where(col < mem_at, lax.shift_right_arithmetic(spot, 4), mem_seg)
    near = (
        (key_seg == query)
        | ((spot >= query * SEG_LEN - LEFT_LEN) & (spot < query * SEG_LEN))
        | ((key_seg == query + 1) & (spot < query * SEG_LEN + SEG_LEN + RIGHT_LEN))
    )
    recent = (key_seg >= query - MEM_LEN) & (key_seg < query) & (row >= sizes.top)
    allowed = ((col < mem_at) & near) | ((col >= mem_at) & recent)
    key_abs = key_seg + base
    query_abs = query + base
    allowed = allowed & (key_abs >= 0) & (key_abs < total)
    if sizes.top:
        allowed = allowed & ((row < sizes.segs) | (row >= sizes.top))
    for n in range(seqs):
        key_owner = jnp.zeros(shape, jnp.int32)
        query_owner = jnp.zeros(shape, jnp.int32)
        for u in range(starts_ref.shape[1]):
            first = starts_ref[n, u]
            key_owner = key_owner + (key_abs >= first).astype(jnp.int32)
            query_owner = query_owner + (query_abs >= first).astype(jnp.int32)
        mask_ref[n] = jnp.where(allowed & (key_owner == query_owner), 0.0, -1e30)


def half_masks():
    lane = lax.broadcasted_iota(jnp.int32, (1, LANES), 1)
    even = (lane < LANES // 2).astype(F32)
    return even.astype(BF16), (1.0 - even).astype(BF16), lane < LANES // 2


def project(sizes, z_ref, qkv_ref, row_bias_ref, proj_ref):
    step = CHIPS_Z // 2
    for c in range(2):
        block = qkv_ref[pl.ds(c * step, step)].reshape(-1, sizes.width)
        wide = block.shape[0]
        made = nt(z_ref[...], block) + row_bias_ref[:, pl.ds(c * wide, wide)]
        proj_ref[:, pl.ds(c * wide, wide)] = made.astype(BF16)


def attend(sizes, seqs, proj_ref, mask_ref, probs_ref, att_ref):
    even, odd, is_even = half_masks()
    scale = (sizes.width // HEADS) ** (-0.5)
    count = sizes.queries

    def body(p, carry):
        for n in range(seqs):
            lane = pl.multiple_of(p * LANES, LANES)
            query = proj_ref[pl.ds(n * sizes.ext, count), pl.ds(lane, LANES)]
            first = n * sizes.ext + sizes.top
            key = proj_ref[pl.ds(first, sizes.keys), pl.ds(sizes.width + lane, LANES)]
            value = proj_ref[pl.ds(first, sizes.keys), pl.ds(2 * sizes.width + lane, LANES)]
            scores = nt(jnp.concatenate([query * even, query * odd], axis=0), key) * scale
            outs = []
            for half in range(2):
                part = scores[half * count : (half + 1) * count] + mask_ref[n]
                part = jnp.exp(part - jnp.max(part, axis=1, keepdims=True))
                part = (part * (1.0 / jnp.sum(part, axis=1, keepdims=True))).astype(BF16)
                probs_ref[n * sizes.pairs + p, pl.ds(half * count, count), :] = part
                outs.append(nn(part, value))
            att_ref[pl.ds(n * count, count), pl.ds(lane, LANES)] = jnp.where(
                is_even, outs[0], outs[1]
            ).astype(BF16)
        return carry

    lax.fori_loop(0, sizes.pairs, body, 0, unroll=True)


def attend_back(sizes, seqs, proj_ref, probs_ref, go_ref, gproj_ref):
    even, odd, is_even = half_masks()
    scale = (sizes.width // HEADS) ** (-0.5)
    count = sizes.queries
    wide = sizes.width
    for n in range(seqs):
        base = n * sizes.ext
        rest = sizes.ext - count
        gproj_ref[pl.ds(base + count, rest), pl.ds(0, wide)] = jnp.zeros((rest, wide), BF16)
        if sizes.top:
            gproj_ref[pl.ds(base, sizes.top), pl.ds(wide, 2 * wide)] = jnp.zeros(
                (sizes.top, 2 * wide), BF16
            )

    def body(p, carry):
        for n in range(seqs):
            lane = pl.multiple_of(p * LANES, LANES)
            base = n * sizes.ext
            first = base + sizes.top
            query = proj_ref[pl.ds(base, count), pl.ds(lane, LANES)]
            key = proj_ref[pl.ds(first, sizes.keys), pl.ds(wide + lane, LANES)]
            value = proj_ref[pl.ds(first, sizes.keys), pl.ds(2 * wide + lane, LANES)]
            grad = go_ref[pl.ds(n * count, count), pl.ds(lane, LANES)]
            queries = jnp.concatenate([query * even, query * odd], axis=0)
            grads = jnp.concatenate([grad * even, grad * odd], axis=0)
            probs_low = probs_ref[n * sizes.pairs + p]
            grad_values = tn(probs_low, grads)
            probs = probs_low.astype(F32)
            grad_probs = nt(grads, value)
            weighted = grad_probs * probs
            grad_scores = (
                (weighted - probs * jnp.sum(weighted, axis=1, keepdims=True)) * scale
            ).astype(BF16)
            grad_keys = tn(grad_scores, queries)
            grad_query = jnp.where(
                is_even, nn(grad_scores[:count], key), nn(grad_scores[count:], key)
            )
            gproj_ref[pl.ds(base, count), pl.ds(lane, LANES)] = grad_query.astype(BF16)
            gproj_ref[pl.ds(first, sizes.keys), pl.ds(wide + lane, LANES)] = grad_keys.astype(BF16)
            gproj_ref[pl.ds(first, sizes.keys), pl.ds(2 * wide + lane, LANES)] = (
                grad_values.astype(BF16)
            )
        return carry

    lax.fori_loop(0, sizes.pairs, body, 0, unroll=True)


def gelu_both(upward):
    half = 0.5 * (1.0 + lax.erf(upward * ROOT_HALF))
    slope = half + upward * jnp.exp(-0.5 * upward * upward) * INV_ROOT_TWO_PI
    return upward * half, slope


def up_block(up_ref, c, wide):
    step = wide // (up_ref.shape[1] * up_ref.shape[2])
    return up_ref[pl.ds(c * step, step)].reshape(-1, up_ref.shape[3])


def down_block(down_ref, c, wide):
    at = pl.multiple_of(c * wide, wide)
    return down_ref[:, :, :, pl.ds(at, wide)].reshape(-1, wide)


def ffn_back_step(
    sizes, c, wide, grad_low, hidden_low, active, slope, up_ref, down_ref, gup_ref, gdown_ref, vec
):
    at = pl.multiple_of(c * wide, wide)
    up = up_block(up_ref, c, wide)
    down = down_block(down_ref, c, wide)
    grad_active = nn(grad_low, down)
    grad_up_f = grad_active * slope
    grad_up = grad_up_f.astype(BF16)
    gdown_ref[:, :, :, pl.ds(at, wide)] = (
        tn(grad_low, active).astype(BF16).reshape(gdown_ref.shape[:3] + (wide,))
    )
    step = wide // (gup_ref.shape[1] * gup_ref.shape[2])
    gup_ref[pl.ds(c * step, step)] = (
        tn(grad_up, hidden_low).astype(BF16).reshape((step,) + gup_ref.shape[1:])
    )
    vec[pl.ds(8 + c, 1), :] = col_sum(grad_up.astype(F32))
    return nn(grad_up, up)


def attn_back_stage(
    sizes, seqs, gz, grad_mem_ref, att_ref, proj_ref, probs_ref, z_ref, qkv_ref, out_ref,
    gqkv_ref, gout_ref, go_ref, gproj_ref, branch_ref, vec, gh_ref, gmem_ref, back_left_ref,
    back_right_ref, scaled_rows=None,
):
    wide = sizes.width
    count = sizes.queries
    bias_out = col_sum(gz)
    for n in range(seqs):
        if sizes.top:
            mem_grad = grad_mem_ref[pl.ds(n * sizes.segs, sizes.segs), :]
            bias_out = bias_out + col_sum(mem_grad)
            branch_ref[pl.ds(n * count, sizes.top), :] = jnp.concatenate(
                [mem_grad, jnp.zeros((sizes.top - sizes.segs, wide), F32)], axis=0
            ).astype(BF16)
        branch_ref[pl.ds(n * count + sizes.top, sizes.rows), :] = gz[
            n * sizes.rows : (n + 1) * sizes.rows
        ].astype(BF16)
    vec[pl.ds(5, 1), :] = bias_out
    branch = branch_ref[...]
    gout_ref[...] = tn(branch, att_ref[...]).astype(BF16).reshape(gout_ref.shape)
    go_ref[...] = nn(branch, out_ref[...].reshape(-1, wide)).astype(BF16)
    attend_back(sizes, seqs, proj_ref, probs_ref, go_ref, gproj_ref)
    vec[pl.ds(3, 1), :] = col_sum(gproj_ref[:, pl.ds(0, wide)].astype(F32))
    vec[pl.ds(4, 1), :] = col_sum(gproj_ref[:, pl.ds(2 * wide, wide)].astype(F32))
    grad_ext = nn(gproj_ref[...], qkv_ref[...].reshape(-1, wide))
    gain_sum = jnp.zeros((1, wide), F32)
    bias_sum = jnp.zeros((1, wide), F32)
    for n in range(seqs):
        base = n * sizes.ext
        own = grad_ext[base + sizes.top : base + sizes.top + sizes.rows]
        if sizes.top:
            spread = grad_ext[base : base + sizes.segs] * (1.0 / SEG_LEN)
            own = own + segment_spread(sizes.rows, wide, spread)
        gh_ref[pl.ds(n * sizes.rows, sizes.rows), :] = own
        mem = base + sizes.mem_at
        gmem_ref[pl.ds(n * sizes.segs, sizes.segs), :] = grad_ext[mem : mem + sizes.segs]
        left = base + sizes.left_at
        back_left_ref[n] = grad_ext[left : left + BACK_ROWS].astype(BF16)
        right = base + sizes.right_at
        back_right_ref[n] = grad_ext[right : right + RIGHT_ROWS].astype(BF16)
        if scaled_rows is not None:
            grads = (
                own,
                grad_ext[right : right + RIGHT_ROWS],
                grad_ext[left : left + LEFT_ROWS],
            )
            for rows, scaled in zip(grads, scaled_rows(n)):
                gain_sum = gain_sum + col_sum(rows * scaled)
                bias_sum = bias_sum + col_sum(rows)
    if scaled_rows is not None:
        vec[pl.ds(0, 1), :] = gain_sum
        vec[pl.ds(2, 1), :] = bias_sum
    step = CHIPS_Z // 2
    part = gqkv_ref.shape[1] * gqkv_ref.shape[2] * step
    for c in range(2):
        gqkv_ref[pl.ds(c * step, step)] = (
            tn(gproj_ref[:, pl.ds(c * part, part)], z_ref[...])
            .astype(BF16)
            .reshape((step,) + gqkv_ref.shape[1:])
        )


def merge_halo(sizes, n, gh_ref, gmem_ref, from_right_ref, from_left_ref):
    first = n * sizes.rows
    back = from_right_ref[n].astype(F32)
    head = gh_ref[pl.ds(first, RIGHT_ROWS), :] + from_left_ref[n].astype(F32)
    middle = gh_ref[pl.ds(first + RIGHT_ROWS, sizes.rows - RIGHT_ROWS - LEFT_ROWS), :]
    tail = gh_ref[pl.ds(first + sizes.rows - LEFT_ROWS, LEFT_ROWS), :] + back[:LEFT_ROWS]
    mem = gmem_ref[pl.ds(n * sizes.segs, sizes.segs), :] + back[LEFT_ROWS + sizes.segs :]
    return jnp.concatenate([head, middle, tail], axis=0), mem


def pack_kernel(spots, qkv_ref, out_ref, up_ref, down_ref, *packed):
    eye = identity(LANES)
    high, wide, low = qkv_ref.shape[1], out_ref.shape[1], down_ref.shape[1]
    for layer, ref in enumerate(packed):
        up = tn(up_ref[layer], eye).astype(BF16)
        for z in range(ref.shape[0]):
            ref[z, pl.ds(spots.qkv[1], high), :] = qkv_ref[layer]
            ref[z, pl.ds(spots.out[1], wide), :] = out_ref[layer]
            ref[z, pl.ds(spots.up[1], up_ref.shape[2]), :] = up
            for part, (_, first) in enumerate(spots.down):
                ref[z, pl.ds(first, low), :] = down_ref[layer, :, pl.ds(part * LANES, LANES)]


def unpack_kernel(layers, small_at, *refs):
    sources, outs = refs[:-7], refs[-7:]
    qkv_ref, out_ref, up_ref, down_ref, gains_ref, biases_ref, ffn_bias_ref = outs
    eye = identity(LANES)
    high, wide, low = qkv_ref.shape[1], out_ref.shape[1], down_ref.shape[1]

    def total(source, first, rows):
        ref = sources[source]
        value = ref[0, pl.ds(first, rows), :].astype(F32)
        for z in range(1, ref.shape[0]):
            value = value + ref[z, pl.ds(first, rows), :].astype(F32)
        return value

    base = 0
    for layer, spots in enumerate(layers):
        qkv_ref[layer] = total(base + spots.qkv[0], spots.qkv[1], high)
        out_ref[layer] = total(base + spots.out[0], spots.out[1], wide)
        up_ref[layer] = nt(
            eye, total(base + spots.up[0], spots.up[1], up_ref.shape[2]).astype(BF16)
        )
        for part, (group, first) in enumerate(spots.down):
            down_ref[layer, :, pl.ds(part * LANES, LANES)] = total(base + group, first, low)
        base += 1 + max(group for group, _ in spots.down)
    sums = total(small_at[0], small_at[1], SMALL_ROWS)
    parts = gains_ref.shape[2] // LANES
    for layer in range(gains_ref.shape[0]):
        for part in range(parts):
            lanes = pl.ds(part * LANES, LANES)
            block = sums[(layer * parts + part) * TILE : (layer * parts + part + 1) * TILE]
            gains_ref[layer, :, lanes] = block[0:2]
            for row in range(biases_ref.shape[0]):
                biases_ref[row, pl.ds(layer, 1), lanes] = block[2 + row : 3 + row]
            for row in range(ffn_bias_ref.shape[1] // gains_ref.shape[2]):
                at = row * gains_ref.shape[2] + part * LANES
                ffn_bias_ref[pl.ds(layer, 1), pl.ds(at, LANES)] = block[8 + row : 9 + row]


def sum_kernel(*refs):
    total = refs[0][...].astype(F32)
    for ref in refs[1:-1]:
        total = total + ref[...].astype(F32)
    refs[-1][...] = total.astype(BF16)


def near_small_kernel(*refs):
    count = (len(refs) - 1) // 2
    out_ref = refs[-1]
    rows = out_ref.shape[1] - SMALL_ROWS
    for sources, at, size in ((refs[:count], 0, rows), (refs[count:-1], rows, SMALL_ROWS)):
        total = sources[0][0].astype(F32)
        for ref in sources[1:]:
            total = total + ref[0].astype(F32)
        out_ref[0, pl.ds(at, size), :] = total.astype(BF16)


def first_layer_kernel(
    sizes, seqs, mats, spots, count_in, place_ref, starts_ref, frames_ref, left_ref, right_ref,
    gains_ref, biases_ref, ffn_bias_ref, row_bias_ref, *refs
):
    groups = in_groups(spots, refs[:count_in])
    (
        z_ref, proj_ref, probs_ref, att_ref, mixed_ref, mem_ref, next_ref, active_ref, slope_ref,
        low_ref, send_right_ref, send_left_ref, qkv_ref, out_ref, up_ref, down_ref, mask_ref,
        hidden_ref, sems,
    ) = refs[count_in:]
    wide = sizes.width
    copies = start_in(attn_pairs(mats, spots, groups, qkv_ref, out_ref, place_ref), sems, 0)
    ffn_copies = start_in(
        ffn_pairs(mats, spots, groups, up_ref, down_ref, place_ref), sems, len(copies)
    )
    gain = gains_ref[0, pl.ds(0, 1), :]
    bias = biases_ref[0, pl.ds(0, 1), :]
    pad = jnp.zeros((TILE - sizes.segs, wide), F32)
    for n in range(seqs):
        own = frames_ref[n].astype(F32)
        before = left_ref[n].astype(F32)
        hidden = norm_forward(own, gain, bias)[0]
        halo = norm_forward(before[before.shape[0] - LEFT_ROWS :], gain, bias)[0]
        after = norm_forward(right_ref[n].astype(F32), gain, bias)[0]
        memory = jnp.concatenate(
            [
                segment_mean(own),
                jnp.zeros((sizes.segs - before.shape[0] // SEG_LEN, wide), F32),
                segment_mean(before),
            ],
            axis=0,
        )
        base = n * sizes.ext
        z_ref[pl.ds(base, sizes.top), :] = jnp.concatenate(
            [segment_mean(hidden), pad], axis=0
        ).astype(BF16)
        z_ref[pl.ds(base + sizes.top, sizes.rows), :] = hidden.astype(BF16)
        z_ref[pl.ds(base + sizes.right_at, RIGHT_ROWS), :] = after.astype(BF16)
        z_ref[pl.ds(base + sizes.left_at, LEFT_ROWS), :] = halo.astype(BF16)
        z_ref[pl.ds(base + sizes.mem_at, MEM_ROWS), :] = memory.astype(BF16)
    fill_mask(sizes, seqs, starts_ref, place_ref, mask_ref)
    wait_all(copies)
    project(sizes, z_ref, qkv_ref, row_bias_ref, proj_ref)
    attend(sizes, seqs, proj_ref, mask_ref, probs_ref, att_ref)
    mixed = nt(att_ref[...], out_ref[...].reshape(-1, wide)) + biases_ref[0, pl.ds(3, 1), :]
    for n in range(seqs):
        base = n * sizes.queries
        mem_ref[pl.ds(n * sizes.segs, sizes.segs), :] = mixed[base : base + sizes.segs]
        mixed_ref[pl.ds(n * sizes.rows, sizes.rows), :] = (
            frames_ref[n].astype(F32) + mixed[base + sizes.top : base + sizes.top + sizes.rows]
        )
    mixed = mixed_ref[...]
    hidden, _, _ = norm_forward(mixed, gains_ref[0, pl.ds(1, 1), :], biases_ref[0, pl.ds(4, 1), :])
    hidden_ref[...] = hidden.astype(BF16)
    next_ref[...] = mixed + biases_ref[0, pl.ds(5, 1), :]
    wait_all(ffn_copies)

    def body(c, carry):
        at_lane = pl.multiple_of(c * wide, wide)
        upward = nt(hidden_ref[...], up_block(up_ref, c, wide))
        upward = upward + ffn_bias_ref[pl.ds(0, 1), pl.ds(at_lane, wide)]
        active, slope = gelu_both(upward)
        active = active.astype(BF16)
        active_ref[:, pl.ds(at_lane, wide)] = active
        slope_ref[:, pl.ds(at_lane, wide)] = slope.astype(BF16)
        next_ref[...] += nt(active, down_block(down_ref, c, wide))
        return carry

    lax.fori_loop(0, sizes.ff // wide, body, 0)
    low, _, _ = norm_forward(
        next_ref[...], gains_ref[1, pl.ds(0, 1), :], biases_ref[1, pl.ds(0, 1), :]
    )
    low = low.astype(BF16)
    low_ref[...] = low
    for n in range(seqs):
        base = n * sizes.rows
        send_right_ref[n, pl.ds(0, LEFT_ROWS), :] = low[
            base + sizes.rows - LEFT_ROWS : base + sizes.rows
        ]
        send_right_ref[n, pl.ds(LEFT_ROWS, MEM_ROWS), :] = jnp.concatenate(
            [
                mem_ref[pl.ds(n * sizes.segs, sizes.segs), :],
                jnp.zeros((MEM_ROWS - sizes.segs, wide), F32),
            ],
            axis=0,
        ).astype(BF16)
        send_left_ref[n] = low[base : base + RIGHT_ROWS]


def last_layer_kernel(
    sizes, seqs, mats, spots, count_in, count_out, place_ref, starts_ref, low_ref, left_ref,
    right_ref, mem_ref, inputs_ref, out_grad_ref, gains_ref, biases_ref, ffn_bias_ref,
    row_bias_ref, *refs
):
    groups = in_groups(spots, refs[:count_in])
    (encoded_ref, gz_ref, gh_ref, gmem_ref, back_left_ref, back_right_ref, vec) = refs[
        count_in : count_in + 7
    ]
    hbm_out = refs[count_in + 7 : count_in + 7 + count_out]
    (
        qkv_ref, out_ref, up_ref, down_ref, gqkv_ref, gout_ref, gup_ref, gdown_ref, mask_ref,
        z_ref, proj_ref, probs_ref, att_ref, hidden_ref, go_ref, gproj_ref, branch_ref,
        grad_low_ref, grad_hidden_ref, sems,
    ) = refs[count_in + 7 + count_out :]
    outs_to = hbm_out
    if spots is not None:
        outs_to = [[ref.at[k] for ref in hbm_out for k in range(ref.shape[0])]]
    wide = sizes.width
    attn_copies = start_in(attn_pairs(mats, spots, groups, qkv_ref, out_ref, place_ref), sems, 0)
    ffn_copies = start_in(
        ffn_pairs(mats, spots, groups, up_ref, down_ref, place_ref), sems, len(attn_copies)
    )
    vec[...] = jnp.zeros_like(vec)
    for n in range(seqs):
        base = n * sizes.ext
        z_ref[pl.ds(base, sizes.rows), :] = low_ref[pl.ds(n * sizes.rows, sizes.rows), :]
        z_ref[pl.ds(base + sizes.right_at, RIGHT_ROWS), :] = right_ref[n]
        z_ref[pl.ds(base + sizes.left_at, LEFT_ROWS), :] = left_ref[n, pl.ds(0, LEFT_ROWS), :]
        memory = jnp.concatenate(
            [
                mem_ref[pl.ds(n * sizes.segs, sizes.segs), :],
                left_ref[n, pl.ds(LEFT_ROWS, MEM_ROWS), :].astype(F32)[: sizes.segs],
            ],
            axis=0,
        )
        z_ref[pl.ds(base + sizes.mem_at, MEM_ROWS), :] = memory.astype(BF16)
        grad_low_ref[pl.ds(n * sizes.rows, sizes.rows), :] = out_grad_ref[n]
    fill_mask(sizes, seqs, starts_ref, place_ref, mask_ref)
    wait_all(attn_copies)
    project(sizes, z_ref, qkv_ref, row_bias_ref, proj_ref)
    attend(sizes, seqs, proj_ref, mask_ref, probs_ref, att_ref)
    mixed = (
        inputs_ref[...]
        + nt(att_ref[...], out_ref[...].reshape(-1, wide))
        + biases_ref[1, pl.ds(3, 1), :]
    )
    gain = gains_ref[1, pl.ds(1, 1), :]
    hidden, scaled, inverse = norm_forward(mixed, gain, biases_ref[1, pl.ds(4, 1), :])
    hidden_ref[...] = hidden.astype(BF16)
    for n in range(seqs):
        encoded_ref[n] = mixed[n * sizes.rows : (n + 1) * sizes.rows] + biases_ref[
            1, pl.ds(5, 1), :
        ]
    grad_hidden_ref[...] = jnp.zeros_like(grad_hidden_ref)
    wait_all(ffn_copies)

    def body(c, carry):
        at_lane = pl.multiple_of(c * wide, wide)
        upward = nt(hidden_ref[...], up_block(up_ref, c, wide))
        upward = upward + ffn_bias_ref[pl.ds(1, 1), pl.ds(at_lane, wide)]
        active, slope = gelu_both(upward)
        active = active.astype(BF16)
        made = nt(active, down_block(down_ref, c, wide))
        for n in range(seqs):
            encoded_ref[n] += made[n * sizes.rows : (n + 1) * sizes.rows]
        grad_hidden_ref[...] += ffn_back_step(
            sizes, c, wide, grad_low_ref[...], hidden_ref[...], active, slope, up_ref, down_ref,
            gup_ref, gdown_ref, vec,
        )
        return carry

    lax.fori_loop(0, sizes.ff // wide, body, 0)
    out_at = len(attn_copies) + len(ffn_copies)
    outs = start_out(
        ffn_pairs(mats, spots, outs_to, gup_ref, gdown_ref, place_ref), sems, out_at
    )
    grad = grad_low_ref[...].astype(F32)
    grad_hidden = grad_hidden_ref[...]
    vec[pl.ds(1, 1), :] = col_sum(grad_hidden * scaled)
    vec[pl.ds(6, 1), :] = col_sum(grad_hidden)
    vec[pl.ds(7, 1), :] = col_sum(grad)
    gz = grad + norm_backward(grad_hidden, scaled, inverse, gain)
    gz_ref[...] = gz
    attn_back_stage(
        sizes, seqs, gz, None, att_ref, proj_ref, probs_ref, z_ref, qkv_ref, out_ref, gqkv_ref,
        gout_ref, go_ref, gproj_ref, branch_ref, vec, gh_ref, gmem_ref, back_left_ref,
        back_right_ref,
    )
    outs = outs + start_out(
        attn_pairs(mats, spots, outs_to, gqkv_ref, gout_ref, place_ref),
        sems,
        out_at + len(outs),
    )
    wait_all(outs)


def first_back_kernel(
    last, sizes, seqs, mats, spots, count_in, count_out, place_ref, inputs_ref, gz_in_ref,
    gh_in_ref, gmem_in_ref, from_right_ref, from_left_ref, mixed_ref, active_ref, slope_ref,
    att_ref, probs_ref, proj_ref, z_ref, frames_ref, left_ref, right_ref, gains_ref, biases_ref,
    last_vec, *refs
):
    groups = in_groups(spots, refs[:count_in])
    gz_ref, gh_ref, gmem_ref, back_left_ref, back_right_ref, upper_vec, vec = refs[
        count_in : count_in + 7
    ]
    refs = refs[count_in + 7 :]
    hbm_out = refs[:count_out]
    (
        qkv_ref, out_ref, up_ref, down_ref, gqkv_ref, gout_ref, gup_ref, gdown_ref, hidden_ref,
        grad_low_ref, grad_ref, grad_hidden_ref, grad_mem_ref, go_ref, gproj_ref, branch_ref,
        small_ref, sems,
    ) = refs[count_out:]
    wide = sizes.width
    small = []
    outs_to = hbm_out
    if spots is not None:
        classes = count_in // 2
        rows = mats.attn_rows + mats.ffn_rows
        end = CHIPS_Z * rows
        each = [ref.at[k] for ref in hbm_out for k in range(classes)]
        small = [ref.at[pl.ds(end, SMALL_ROWS), :] for ref in each]
        outs_to = [[ref.at[pl.ds(0, end), :].reshape(CHIPS_Z, rows, LANES) for ref in each]]
    ffn_copies = start_in(ffn_pairs(mats, spots, groups, up_ref, down_ref, place_ref), sems, 0)
    attn_copies = start_in(
        attn_pairs(mats, spots, groups, qkv_ref, out_ref, place_ref), sems, len(ffn_copies)
    )
    vec[...] = jnp.zeros_like(vec)
    upper_vec[...] = jnp.zeros_like(upper_vec)
    gain = gains_ref[1, pl.ds(0, 1), :]
    gain_sum = jnp.zeros((1, wide), F32)
    bias_sum = jnp.zeros((1, wide), F32)
    for n in range(seqs):
        rows = pl.ds(n * sizes.rows, sizes.rows)
        _, scaled, inverse = norm_forward(
            inputs_ref[rows, :], gain, biases_ref[1, pl.ds(0, 1), :]
        )
        total, mem = merge_halo(last, n, gh_in_ref, gmem_in_ref, from_right_ref, from_left_ref)
        gain_sum = gain_sum + col_sum(total * scaled)
        bias_sum = bias_sum + col_sum(total)
        grad = gz_in_ref[rows, :] + norm_backward(total, scaled, inverse, gain)
        grad_ref[rows, :] = grad
        grad_low_ref[rows, :] = grad.astype(BF16)
        grad_mem_ref[pl.ds(n * sizes.segs, sizes.segs), :] = mem
    upper_vec[pl.ds(0, 1), :] = gain_sum
    upper_vec[pl.ds(2, 1), :] = bias_sum
    gain = gains_ref[0, pl.ds(1, 1), :]
    hidden, scaled, inverse = norm_forward(
        mixed_ref[...], gain, biases_ref[0, pl.ds(4, 1), :]
    )
    hidden_ref[...] = hidden.astype(BF16)
    grad_hidden_ref[...] = jnp.zeros_like(grad_hidden_ref)
    wait_all(ffn_copies)

    def body(c, carry):
        at_lane = pl.multiple_of(c * wide, wide)
        grad_hidden_ref[...] += ffn_back_step(
            sizes, c, wide, grad_low_ref[...], hidden_ref[...],
            active_ref[:, pl.ds(at_lane, wide)], slope_ref[:, pl.ds(at_lane, wide)].astype(F32),
            up_ref, down_ref, gup_ref, gdown_ref, vec,
        )
        return carry

    lax.fori_loop(0, sizes.ff // wide, body, 0)
    out_at = len(ffn_copies) + len(attn_copies)
    outs = start_out(
        ffn_pairs(mats, spots, outs_to, gup_ref, gdown_ref, place_ref), sems, out_at
    )
    grad_hidden = grad_hidden_ref[...]
    grad = grad_ref[...]
    vec[pl.ds(1, 1), :] = col_sum(grad_hidden * scaled)
    vec[pl.ds(6, 1), :] = col_sum(grad_hidden)
    vec[pl.ds(7, 1), :] = col_sum(grad)
    gz = grad + norm_backward(grad_hidden, scaled, inverse, gain)
    gz_ref[...] = gz

    def scaled_rows(n):
        before = left_ref[n, pl.ds(left_ref.shape[1] - LEFT_ROWS, LEFT_ROWS), :]
        parts = (frames_ref[n], right_ref[n], before)
        first_gain = gains_ref[0, pl.ds(0, 1), :]
        first_bias = biases_ref[0, pl.ds(0, 1), :]
        return [norm_forward(part.astype(F32), first_gain, first_bias)[1] for part in parts]

    wait_all(attn_copies)
    attn_back_stage(
        sizes, seqs, gz, grad_mem_ref, att_ref, proj_ref, probs_ref, z_ref, qkv_ref, out_ref,
        gqkv_ref, gout_ref, go_ref, gproj_ref, branch_ref, vec, gh_ref, gmem_ref, back_left_ref,
        back_right_ref, scaled_rows,
    )
    outs = outs + start_out(
        attn_pairs(mats, spots, outs_to, gqkv_ref, gout_ref, place_ref),
        sems,
        out_at + len(outs),
    )
    parts = sizes.width // LANES
    for layer, total in enumerate((vec[...], last_vec[...] + upper_vec[...])):
        for part in range(parts):
            small_ref[pl.ds((layer * parts + part) * TILE, TILE), :] = total[
                :, part * LANES : (part + 1) * LANES
            ].astype(BF16)
    outs = outs + start_out([(ref, small_ref) for ref in small], sems, out_at + len(outs))
    wait_all(outs)


def frames_grad_kernel(
    sizes, seqs, frames_ref, gz_ref, gh_ref, gmem_ref, from_right_ref, from_left_ref, gains_ref,
    biases_ref, grad_ref
):
    gain = gains_ref[0, pl.ds(0, 1), :]
    for n in range(seqs):
        _, scaled, inverse = norm_forward(
            frames_ref[n].astype(F32), gain, biases_ref[0, pl.ds(0, 1), :]
        )
        total, mem = merge_halo(sizes, n, gh_ref, gmem_ref, from_right_ref, from_left_ref)
        grad_ref[n] = (
            gz_ref[pl.ds(n * sizes.rows, sizes.rows), :]
            + norm_backward(total, scaled, inverse, gain)
            + segment_spread(sizes.rows, sizes.width, mem * (1.0 / SEG_LEN))
        )


def shifted(value, axis, by):
    size = lax.axis_size(axis)
    pairs = [(i, i + by) for i in range(size) if 0 <= i + by < size]
    return lax.ppermute(value, axis, pairs)


def permuted(value, move):
    reps = lax.axis_size("rep")
    pairs = []
    for flat in range(lax.axis_size("seg") * reps):
        seg, rep = divmod(flat, reps)
        z, y, x, core = move(seg // CHIPS_Y, seg % CHIPS_Y, rep // 2, rep % 2)
        pairs.append((flat, (z * CHIPS_Y + y) * reps + 2 * x + core))
    return lax.ppermute(value, ("seg", "rep"), pairs)


def across_first(value):
    return permuted(value, lambda z, y, x, c: (z, y, x ^ 1, c) if c == 0 else (z, y ^ 1, x, c))


def across_second(value):
    return permuted(value, lambda z, y, x, c: (z, y ^ 1, x, c) if c == 0 else (z, y, x ^ 1, c))


def other_core(value):
    return permuted(value, lambda z, y, x, c: (z, y, x, c ^ 1))


def after(value, *others):
    return lax.optimization_barrier((value,) + others)[0]


def swap_z(blocks):
    groups = [
        [z * CHIPS_Y + y for z in range(CHIPS_Z)] for y in range(CHIPS_Y)
    ]
    return lax.all_to_all(blocks, "seg", 0, 0, axis_index_groups=groups, tiled=True)


def gather_sides(here):
    return [here, across_first(here), across_second(here)]


def both_cores(blocks):
    return blocks + [other_core(block) for block in blocks]


def summed(*parts):
    total = parts[0].astype(F32)
    for part in parts[1:]:
        total = total + part.astype(F32)
    return total.astype(BF16)


def block_rows(rows, lead, at=None):
    if at is not None:
        return pl.BlockSpec((1, rows, LANES), lambda i: (lead, at, 0))
    return pl.BlockSpec((1, rows, LANES), lambda i: (lead, i, 0))


def piped_sum(parts, count, steps):
    rows = parts[0][0].shape[1]
    size = rows // steps

    def spec(first):
        return pl.BlockSpec((1, size, LANES), lambda l, i: (first + l, i, 0))

    return call(
        sum_kernel,
        [spec(first) for _, first in parts],
        [((count, rows, LANES), BF16)],
        [spec(0)],
        [],
        [array for array, _ in parts],
        grid=(count, steps),
    )[0]


def sum_everywhere(value):
    count = lax.axis_size("seg") * lax.axis_size("rep")
    bit = 1
    while bit < count:
        value = value + lax.ppermute(value, ("seg", "rep"), [(i, i ^ bit) for i in range(count)])
        bit *= 2
    return value


def vmem_spec():
    return pl.BlockSpec(memory_space=pltpu.VMEM)


def smem_spec():
    return pl.BlockSpec(memory_space=pltpu.SMEM)


def hbm_spec():
    return pl.BlockSpec(memory_space=pl.ANY)


def call(body, in_specs, out_shapes, out_specs, scratch, args, flops=0, moved=0, grid=()):
    return pl.pallas_call(
        body,
        grid=grid,
        in_specs=in_specs,
        out_shape=tuple(jax.ShapeDtypeStruct(shape, kind) for shape, kind in out_shapes),
        out_specs=tuple(out_specs),
        scratch_shapes=scratch,
        compiler_params=pltpu.CompilerParams(vmem_limit_bytes=VMEM_BYTES),
        cost_estimate=pl.CostEstimate(flops=flops, bytes_accessed=moved, transcendentals=0),
    )(*args)


def on_device(
    frames,
    utt_segments,
    out_grad,
    qkv_weight,
    out_weight,
    ffn_in_weight,
    ffn_out_weight,
    norm_gains,
    biases,
    ffn_bias,
):
    micros, groups, rows, width = frames.shape
    seqs = micros * groups
    ff = ffn_bias.shape[1]
    reps = lax.axis_size("rep")
    seg_count = lax.axis_size("seg")
    mats = Matrices(width, ff)
    by_blocks = width // reps == LANES and reps == 4 and seg_count == BLOCKS
    first = Sizes(rows, width, ff, True)
    last = Sizes(rows, width, ff, False)
    own = seqs * rows
    mem_own = seqs * first.segs

    seg_at = lax.axis_index("seg")
    seg_base = seg_at * first.segs
    rep_at = lax.axis_index("rep")
    place = [seg_base, jnp.int32(first.segs * seg_count)]
    y_at, x_at, core_at = seg_at % CHIPS_Y, rep_at // 2, rep_at % 2
    for other in range(2):
        core = lax.bitwise_xor(core_at, other)
        for hop2 in range(2):
            for hop1 in range(2):
                x_hop = jnp.where(core == 0, hop1, hop2)
                y_hop = jnp.where(core == 0, hop2, hop1)
                place.append(lax.bitwise_xor(y_at, y_hop))
                place.append((lax.bitwise_xor(x_at, x_hop) * 2 + core) * LANES)
    place = jnp.stack([jnp.asarray(entry, jnp.int32) for entry in place])
    lengths = utt_segments.reshape(seqs, utt_segments.shape[2])
    starts = (jnp.cumsum(lengths, axis=1) - lengths).astype(jnp.int32)
    zero_bias = jnp.zeros((width,), F32)
    row_bias = jnp.stack(
        [jnp.concatenate([biases[l, 1], zero_bias, biases[l, 2]]) for l in range(LAYERS)]
    ).reshape(LAYERS, 1, 3 * width)

    frames_own = frames.reshape(seqs, rows, width)
    grads_own = out_grad.reshape(seqs, rows, width)
    far = MEM_LEN * SEG_LEN
    frames_left = shifted(frames_own[:, rows - far :], "seg", 1)
    frames_right = shifted(frames_own[:, :RIGHT_ROWS], "seg", -1)

    attn_rows, ffn_rows = mats.attn_rows, mats.ffn_rows
    if by_blocks:
        qkv_t, out_t, down_t = (
            jnp.swapaxes(member, 1, 2) for member in (qkv_weight, out_weight, ffn_out_weight)
        )
        all_rows = attn_rows + ffn_rows
        spots = Spots(mats)
        shards = call(
            lambda *refs: pack_kernel(spots, *refs),
            [vmem_spec()] * 4,
            [((CHIPS_Z, all_rows, LANES), BF16)] * LAYERS,
            [vmem_spec()] * LAYERS,
            [],
            (qkv_t, out_t, ffn_in_weight, down_t),
        )
        sides0 = gather_sides(after(swap_z(shards[0]), frames_left, frames_right))
        place, starts, row_bias, sent = lax.optimization_barrier(
            (place, starts, row_bias, after(shards[1], sides0[0]))
        )
        sides1 = gather_sides(swap_z(sent))
        first_all = both_cores(sides0 + [across_second(after(sides0[1], sides1[0]))])
        classes = len(first_all) // 2
        grad_outs0 = [((classes, CHIPS_Z * all_rows + SMALL_ROWS, LANES), BF16)] * 2
        grad_outs1 = [((classes, CHIPS_Z, all_rows, LANES), BF16)] * 2
        copies_in = len(first_all) * (3 + mats.down_parts)
    else:
        whole = []
        for member, shape in zip(
            (qkv_weight, out_weight, ffn_in_weight, ffn_out_weight),
            (mats.qkv, mats.out, mats.up, mats.down),
        ):
            member = lax.all_gather(member, "rep", axis=1, tiled=True)
            member = lax.all_gather(member, "seg", axis=2, tiled=True)
            whole.append(jnp.swapaxes(member, 1, 2).reshape((LAYERS,) + shape))
        first_all = [member[0] for member in whole]
        last_all = [member[1] for member in whole]
        spots = None
        grad_outs0 = grad_outs1 = [
            (shape, BF16) for shape in (mats.qkv, mats.out, mats.up, mats.down)
        ]
        copies_in = 4
    dma = pltpu.SemaphoreType.DMA

    matrices = [pltpu.VMEM(shape, BF16) for shape in (mats.qkv, mats.out, mats.up, mats.down)]

    (
        z0, proj0, probs0, att0, mixed0, mem1, x1, active0, slope0, low1, send_right, send_left,
    ) = call(
        lambda *refs: first_layer_kernel(
            first, seqs, mats, spots, len(first_all), *refs
        ),
        [smem_spec()] * 2 + [vmem_spec()] * 7 + [hbm_spec()] * len(first_all),
        [
            ((seqs * first.ext, width), BF16),
            ((seqs * first.ext, 3 * width), BF16),
            ((seqs * first.pairs, 2 * first.queries, first.keys), BF16),
            ((seqs * first.queries, width), BF16),
            ((own, width), F32),
            ((mem_own, width), F32),
            ((own, width), F32),
            ((own, ff), BF16),
            ((own, ff), BF16),
            ((own, width), BF16),
            ((seqs, BACK_ROWS, width), BF16),
            ((seqs, RIGHT_ROWS, width), BF16),
        ],
        [vmem_spec()] * 12,
        matrices
        + [
            pltpu.VMEM((seqs, first.queries, first.keys), F32),
            pltpu.VMEM((own, width), BF16),
            dma((copies_in,)),
        ],
        (place, starts, frames_own, frames_left, frames_right, norm_gains, biases, ffn_bias,
         row_bias[0]) + tuple(first_all),
        flops=24 * own * (4 * width * width + 2 * width * ff) // 2,
        moved=2 * (4 * width * width + 2 * width * ff),
    )
    left1 = shifted(send_right, "seg", 1)
    right1 = shifted(send_left, "seg", -1)
    if by_blocks:
        last_side = across_second(after(sides1[1], sides1[2], low1))
        last_all = both_cores(sides1 + [last_side])
        last_all[-1] = other_core(after(last_side, left1, right1))

    vec_shape = (TILE, width)
    outs = call(
        lambda *refs: last_layer_kernel(
            last, seqs, mats, spots, len(last_all), len(grad_outs1), *refs
        ),
        [smem_spec()] * 2 + [vmem_spec()] * 10 + [hbm_spec()] * len(last_all),
        [
            ((seqs, rows, width), F32),
            ((own, width), F32),
            ((own, width), F32),
            ((mem_own, width), F32),
            ((seqs, BACK_ROWS, width), BF16),
            ((seqs, RIGHT_ROWS, width), BF16),
            (vec_shape, F32),
        ]
        + grad_outs1,
        [vmem_spec()] * 7 + [hbm_spec()] * len(grad_outs1),
        matrices
        + matrices
        + [
            pltpu.VMEM((seqs, last.queries, last.keys), F32),
            pltpu.VMEM((seqs * last.ext, width), BF16),
            pltpu.VMEM((seqs * last.ext, 3 * width), BF16),
            pltpu.VMEM((seqs * last.pairs, 2 * last.queries, last.keys), BF16),
            pltpu.VMEM((seqs * last.queries, width), BF16),
            pltpu.VMEM((own, width), BF16),
            pltpu.VMEM((seqs * last.queries, width), BF16),
            pltpu.VMEM((seqs * last.ext, 3 * width), BF16),
            pltpu.VMEM((seqs * last.queries, width), BF16),
            pltpu.VMEM((own, width), BF16),
            pltpu.VMEM((own, width), F32),
            dma((2 * copies_in,)),
        ],
        (place, starts, low1, left1, right1, mem1, x1, grads_own, norm_gains, biases, ffn_bias,
         row_bias[1]) + tuple(last_all),
        flops=30 * own * (4 * width * width + 2 * width * ff),
        moved=4 * (4 * width * width + 2 * width * ff),
    )
    encoded, gz1, gh1, gmem1, back_left1, back_right1, vec1 = outs[:7]
    grad_blocks1 = outs[7:]
    from_right1 = shifted(back_left1, "seg", -1)
    from_left1 = shifted(back_right1, "seg", 1)

    gh1_tied = gh1
    if by_blocks:
        mine1, theirs1 = grad_blocks1[0], other_core(grad_blocks1[1])
        half = classes // 2
        far1 = piped_sum(
            [
                (member.reshape(classes, -1, LANES), half)
                for member in (mine1, theirs1)
            ],
            half,
            2,
        ).reshape((half,) + mine1.shape[1:])
        gh1_tied = after(gh1, far1)
    gz0, gh0, gmem0, back_left0, back_right0, upper_vec, vec0, *grad_blocks0 = call(
        lambda *refs: first_back_kernel(
            last, first, seqs, mats, spots, len(first_all), len(grad_outs0), *refs
        ),
        [smem_spec()] + [vmem_spec()] * 19 + [hbm_spec()] * len(first_all),
        [
            ((own, width), F32),
            ((own, width), F32),
            ((mem_own, width), F32),
            ((seqs, BACK_ROWS, width), BF16),
            ((seqs, RIGHT_ROWS, width), BF16),
            (vec_shape, F32),
            (vec_shape, F32),
        ]
        + grad_outs0,
        [vmem_spec()] * 7 + [hbm_spec()] * len(grad_outs0),
        matrices
        + matrices
        + [
            pltpu.VMEM((own, width), BF16),
            pltpu.VMEM((own, width), BF16),
            pltpu.VMEM((own, width), F32),
            pltpu.VMEM((own, width), F32),
            pltpu.VMEM((mem_own, width), F32),
            pltpu.VMEM((seqs * first.queries, width), BF16),
            pltpu.VMEM((seqs * first.ext, 3 * width), BF16),
            pltpu.VMEM((seqs * first.queries, width), BF16),
            pltpu.VMEM((SMALL_ROWS, LANES), BF16),
            dma((2 * copies_in + 8,)),
        ],
        (place, x1, gz1, gh1_tied, gmem1, from_right1, from_left1, mixed0, active0, slope0, att0,
         probs0, proj0, z0, frames_own, frames_left, frames_right, norm_gains, biases, vec1)
        + tuple(first_all),
        flops=28 * own * (4 * width * width + 2 * width * ff),
        moved=4 * (4 * width * width + 2 * width * ff),
    )
    from_right0 = shifted(back_left0, "seg", -1)
    from_left0 = shifted(back_right0, "seg", 1)
    gz0_last = gz0
    if by_blocks:
        second1 = across_second(far1)
        near1 = summed(mine1[1], theirs1[1], second1[1])
        first1 = across_first(near1)
        mine0, theirs0 = grad_blocks0[0], other_core(after(grad_blocks0[1], second1))
        half = classes // 2
        far0 = after(piped_sum([(mine0, half), (theirs0, half)], half, 2), first1)
        second0 = across_second(far0)
        total1 = summed(mine1[0], theirs1[0], second1[0], after(first1, far0))
        last_parts = swap_z(total1)
        mid0 = piped_sum([(mine0, 1), (theirs0, 1), (after(second0, total1), 1)], 1, 4)
        first0 = after(across_first(mid0), last_parts)
        near0 = call(
            near_small_kernel,
            [block_rows(all_rows, 0)] * 4
            + [block_rows(SMALL_ROWS, 0, CHIPS_Z * all_rows // SMALL_ROWS)] * 4,
            [((CHIPS_Z, all_rows + SMALL_ROWS, LANES), BF16)],
            [pl.BlockSpec((1, all_rows + SMALL_ROWS, LANES), lambda i: (i, 0, 0))],
            [],
            [mine0, theirs0, second0, first0] * 2,
            grid=(CHIPS_Z,),
        )[0]
        first_parts = swap_z(near0)
        gz0_last = after(gz0, near0)
    frames_grad = call(
        lambda *refs: frames_grad_kernel(first, seqs, *refs),
        [vmem_spec()] * 8,
        [((seqs, rows, width), F32)],
        [vmem_spec()],
        [],
        (frames_own, gz0_last, gh0, gmem0, from_right0, from_left0, norm_gains, biases),
    )[0]

    if by_blocks:
        shapes = [member.shape for member in (qkv_t, out_t, ffn_in_weight, down_t)]
        shapes += [norm_gains.shape, (biases.shape[1], LAYERS, width), ffn_bias.shape]
        reduced = call(
            lambda *refs: unpack_kernel([spots, spots], (0, all_rows), *refs),
            [vmem_spec()] * LAYERS,
            [(shape, F32) for shape in shapes],
            [vmem_spec()] * len(shapes),
            [],
            [after(first_parts, frames_grad), last_parts],
        )
        small = reduced[4], jnp.swapaxes(reduced[5], 0, 1), reduced[6]
        reduced = [
            jnp.swapaxes(reduced[0], 1, 2),
            jnp.swapaxes(reduced[1], 1, 2),
            reduced[2],
            jnp.swapaxes(reduced[3], 1, 2),
        ]
    else:
        reduced = []
        for member0, member1 in zip(grad_blocks0, grad_blocks1):
            both = jnp.stack([member0, member1]).reshape(LAYERS, -1, member0.shape[3])
            both = jnp.swapaxes(both, 1, 2)
            both = lax.psum_scatter(both, "seg", scatter_dimension=2, tiled=True)
            both = lax.psum_scatter(both, "rep", scatter_dimension=1, tiled=True)
            reduced.append(both.astype(F32))
        small = sum_everywhere(jnp.stack([vec0, vec1 + upper_vec]))
        small = small[:, 0:2], small[:, 2:8], small[:, 8:12].reshape(ffn_bias.shape)

    return (
        encoded.reshape(frames.shape),
        frames_grad.reshape(frames.shape),
        reduced[0],
        reduced[1],
        reduced[2],
        reduced[3],
        small[0],
        small[1],
        small[2],
    )


def solution(mesh):
    in_specs = (
        P(None, "rep", "seg", None),
        P(None, "rep", None),
        P(None, "rep", "seg", None),
        P(None, "rep", "seg"),
        P(None, "rep", "seg"),
        P(None, "rep", "seg"),
        P(None, "rep", "seg"),
        P(),
        P(),
        P(),
    )
    out_specs = (
        P(None, "rep", "seg", None),
        P(None, "rep", "seg", None),
        P(None, "rep", "seg"),
        P(None, "rep", "seg"),
        P(None, "rep", "seg"),
        P(None, "rep", "seg"),
        P(),
        P(),
        P(),
    )
    return jax.shard_map(
        on_device, mesh=mesh, in_specs=in_specs, out_specs=out_specs, check_vma=False
    )
```

```python
import jax
import jax.numpy as jnp
from jax import lax
from jax.experimental import pallas as pl
from jax.experimental.pallas import tpu as pltpu
from jax.sharding import PartitionSpec as P

HEADS = 8
SEG_LEN = 16
LEFT_LEN = 30
RIGHT_LEN = 4
MEM_LEN = 4
LAYERS = 2

EPS = 1e-05
ROOT_HALF = 0.7071067811865476
INV_ROOT_TWO_PI = 0.3989422804014327

LANES = 128
TILE = 16
RIGHT_ROWS = 16
LEFT_ROWS = 32
MEM_ROWS = 16
BACK_ROWS = LEFT_ROWS + MEM_ROWS
CHIPS_Z = 4
CHIPS_Y = 2
BLOCKS = CHIPS_Z * CHIPS_Y
SMALL_ROWS = 128
VMEM_BYTES = 56 * 1024 * 1024

BF16 = jnp.bfloat16
F32 = jnp.float32


def nn(a, b):
    return lax.dot_general(a, b, (((1,), (0,)), ((), ())), preferred_element_type=F32)


def nt(a, b):
    return lax.dot_general(a, b, (((1,), (1,)), ((), ())), preferred_element_type=F32)


def tn(a, b):
    return lax.dot_general(a, b, (((0,), (0,)), ((), ())), preferred_element_type=F32)


def col_sum(value):
    return jnp.sum(value, axis=0, keepdims=True)


def norm_forward(inputs, gain, bias):
    center = inputs - jnp.mean(inputs, axis=1, keepdims=True)
    inverse = lax.rsqrt(jnp.mean(center * center, axis=1, keepdims=True) + EPS)
    scaled = center * inverse
    return scaled * gain + bias, scaled, inverse


def norm_backward(grad_in, scaled, inverse, gain):
    grad_scaled = grad_in * gain
    return inverse * (
        grad_scaled
        - jnp.mean(grad_scaled, axis=1, keepdims=True)
        - scaled * jnp.mean(grad_scaled * scaled, axis=1, keepdims=True)
    )


def segment_mean(inputs):
    rows, width = inputs.shape
    return jnp.mean(inputs.reshape(rows // SEG_LEN, SEG_LEN, width), axis=1)


def segment_spread(rows, width, per_segment):
    segs = rows // SEG_LEN
    return jnp.broadcast_to(per_segment[:, None, :], (segs, SEG_LEN, width)).reshape(rows, width)


def identity(size):
    row = lax.broadcasted_iota(jnp.int32, (size, size), 0)
    col = lax.broadcasted_iota(jnp.int32, (size, size), 1)
    return (row == col).astype(F32).astype(BF16)


class Sizes:
    def __init__(self, rows, width, ff, with_summary):
        self.rows = rows
        self.width = width
        self.ff = ff
        self.segs = rows // SEG_LEN
        self.top = TILE if with_summary else 0
        self.keys = rows + RIGHT_ROWS + LEFT_ROWS + MEM_ROWS
        self.ext = self.top + self.keys
        self.queries = self.top + rows
        self.right_at = self.top + rows
        self.left_at = self.right_at + RIGHT_ROWS
        self.mem_at = self.left_at + LEFT_ROWS
        self.pairs = width // LANES


class Matrices:
    def __init__(self, width, ff):
        self.qkv = (CHIPS_Z, CHIPS_Y, 3 * width // BLOCKS, width)
        self.out = (CHIPS_Z, CHIPS_Y, width // BLOCKS, width)
        self.up = (CHIPS_Z, CHIPS_Y, ff // BLOCKS, width)
        self.down = (CHIPS_Z, CHIPS_Y, width // BLOCKS, ff)
        self.down_parts = ff // width
        self.attn_rows = self.qkv[2] + self.out[2]
        self.ffn_rows = self.up[2] + self.down_parts * self.down[2]


class Spots:
    def __init__(self, mats, cut=False):
        high, wide, up, low = mats.qkv[2], mats.out[2], mats.up[2], mats.down[2]
        sizes = [high, wide, up] + [low] * mats.down_parts
        rows = [0, 0]
        found = []
        for part, size in enumerate(sizes):
            group = int(cut and part in (1, 3))
            found.append((group, rows[group]))
            rows[group] += size
        self.qkv, self.out, self.up = found[:3]
        self.down = found[3:]
        self.rows = rows


def attn_pairs(mats, spots, groups, qkv_ref, out_ref, place_ref):
    if spots is None:
        return [(groups[0], qkv_ref), (groups[1], out_ref)]
    pairs = []
    for k in range(len(groups[0])):
        row = place_ref[2 + 2 * k]
        lane = pl.multiple_of(place_ref[3 + 2 * k], LANES)
        for (group, first), ref, shape in (
            (spots.qkv, qkv_ref, mats.qkv),
            (spots.out, out_ref, mats.out),
        ):
            block = groups[group][k]
            pairs.append(
                (
                    block.at[:, pl.ds(first, shape[2]), :],
                    ref.at[:, row, :, pl.ds(lane, LANES)],
                )
            )
    return pairs


def ffn_pairs(mats, spots, groups, up_ref, down_ref, place_ref):
    if spots is None:
        return [(groups[2], up_ref), (groups[3], down_ref)]
    pairs = []
    for k in range(len(groups[0])):
        row = place_ref[2 + 2 * k]
        lane = pl.multiple_of(place_ref[3 + 2 * k], LANES)
        group, first = spots.up
        block = groups[group][k]
        pairs.append(
            (block.at[:, pl.ds(first, mats.up[2]), :], up_ref.at[:, row, :, pl.ds(lane, LANES)])
        )
        for part, (group, first) in enumerate(spots.down):
            there = pl.multiple_of(
                place_ref[3 + 2 * k] * mats.down_parts + part * LANES, LANES
            )
            block = groups[group][k]
            pairs.append(
                (
                    block.at[:, pl.ds(first, mats.down[2]), :],
                    down_ref.at[:, row, :, pl.ds(there, LANES)],
                )
            )
    return pairs


def start_in(pairs, sems, at):
    copies = [pltpu.make_async_copy(s, d, sems.at[at + i]) for i, (s, d) in enumerate(pairs)]
    for copy in copies:
        copy.start()
    return copies


def start_out(pairs, sems, at):
    copies = [pltpu.make_async_copy(d, s, sems.at[at + i]) for i, (s, d) in enumerate(pairs)]
    for copy in copies:
        copy.start()
    return copies


def in_groups(spots, refs):
    return refs if spots is None else [refs]


def wait_all(copies):
    for copy in copies:
        copy.wait()


def fill_mask(sizes, seqs, starts_ref, place_ref, mask_ref):
    shape = (sizes.queries, sizes.keys)
    row = lax.broadcasted_iota(jnp.int32, shape, 0)
    col = lax.broadcasted_iota(jnp.int32, shape, 1)
    base = place_ref[0]
    total = place_ref[1]
    query = jnp.where(row < sizes.top, row, lax.shift_right_arithmetic(row - sizes.top, 4))
    left_at = sizes.rows + RIGHT_ROWS
    mem_at = left_at + LEFT_ROWS
    spot = jnp.where(col < left_at, col, col - mem_at)
    mem_seg = jnp.where(col < mem_at + sizes.segs, col - mem_at, col - mem_at - 2 * sizes.segs)
    key_seg = jnp.where(col < mem_at, lax.shift_right_arithmetic(spot, 4), mem_seg)
    near = (
        (key_seg == query)
        | ((spot >= query * SEG_LEN - LEFT_LEN) & (spot < query * SEG_LEN))
        | ((key_seg == query + 1) & (spot < query * SEG_LEN + SEG_LEN + RIGHT_LEN))
    )
    recent = (key_seg >= query - MEM_LEN) & (key_seg < query) & (row >= sizes.top)
    allowed = ((col < mem_at) & near) | ((col >= mem_at) & recent)
    key_abs = key_seg + base
    query_abs = query + base
    allowed = allowed & (key_abs >= 0) & (key_abs < total)
    if sizes.top:
        allowed = allowed & ((row < sizes.segs) | (row >= sizes.top))
    for n in range(seqs):
        key_owner = jnp.zeros(shape, jnp.int32)
        query_owner = jnp.zeros(shape, jnp.int32)
        for u in range(starts_ref.shape[1]):
            first = starts_ref[n, u]
            key_owner = key_owner + (key_abs >= first).astype(jnp.int32)
            query_owner = query_owner + (query_abs >= first).astype(jnp.int32)
        mask_ref[n] = jnp.where(allowed & (key_owner == query_owner), 0.0, -1e30)


def half_masks():
    lane = lax.broadcasted_iota(jnp.int32, (1, LANES), 1)
    even = (lane < LANES // 2).astype(F32)
    return even.astype(BF16), (1.0 - even).astype(BF16), lane < LANES // 2


def project(sizes, z_ref, qkv_ref, row_bias_ref, proj_ref):
    step = CHIPS_Z // 2
    for c in range(2):
        block = qkv_ref[pl.ds(c * step, step)].reshape(-1, sizes.width)
        wide = block.shape[0]
        made = nt(z_ref[...], block) + row_bias_ref[:, pl.ds(c * wide, wide)]
        proj_ref[:, pl.ds(c * wide, wide)] = made.astype(BF16)


def attend(sizes, seqs, proj_ref, mask_ref, probs_ref, att_ref):
    even, odd, is_even = half_masks()
    scale = (sizes.width // HEADS) ** (-0.5)
    count = sizes.queries

    def body(p, carry):
        for n in range(seqs):
            lane = pl.multiple_of(p * LANES, LANES)
            query = proj_ref[pl.ds(n * sizes.ext, count), pl.ds(lane, LANES)]
            first = n * sizes.ext + sizes.top
            key = proj_ref[pl.ds(first, sizes.keys), pl.ds(sizes.width + lane, LANES)]
            value = proj_ref[pl.ds(first, sizes.keys), pl.ds(2 * sizes.width + lane, LANES)]
            scores = nt(jnp.concatenate([query * even, query * odd], axis=0), key) * scale
            outs = []
            for half in range(2):
                part = scores[half * count : (half + 1) * count] + mask_ref[n]
                part = jnp.exp(part - jnp.max(part, axis=1, keepdims=True))
                part = (part * (1.0 / jnp.sum(part, axis=1, keepdims=True))).astype(BF16)
                probs_ref[n * sizes.pairs + p, pl.ds(half * count, count), :] = part
                outs.append(nn(part, value))
            att_ref[pl.ds(n * count, count), pl.ds(lane, LANES)] = jnp.where(
                is_even, outs[0], outs[1]
            ).astype(BF16)
        return carry

    lax.fori_loop(0, sizes.pairs, body, 0, unroll=True)


def attend_back(sizes, seqs, proj_ref, probs_ref, go_ref, gproj_ref):
    even, odd, is_even = half_masks()
    scale = (sizes.width // HEADS) ** (-0.5)
    count = sizes.queries
    wide = sizes.width
    for n in range(seqs):
        base = n * sizes.ext
        rest = sizes.ext - count
        gproj_ref[pl.ds(base + count, rest), pl.ds(0, wide)] = jnp.zeros((rest, wide), BF16)
        if sizes.top:
            gproj_ref[pl.ds(base, sizes.top), pl.ds(wide, 2 * wide)] = jnp.zeros(
                (sizes.top, 2 * wide), BF16
            )

    def body(p, carry):
        for n in range(seqs):
            lane = pl.multiple_of(p * LANES, LANES)
            base = n * sizes.ext
            first = base + sizes.top
            query = proj_ref[pl.ds(base, count), pl.ds(lane, LANES)]
            key = proj_ref[pl.ds(first, sizes.keys), pl.ds(wide + lane, LANES)]
            value = proj_ref[pl.ds(first, sizes.keys), pl.ds(2 * wide + lane, LANES)]
            grad = go_ref[pl.ds(n * count, count), pl.ds(lane, LANES)]
            queries = jnp.concatenate([query * even, query * odd], axis=0)
            grads = jnp.concatenate([grad * even, grad * odd], axis=0)
            probs_low = probs_ref[n * sizes.pairs + p]
            grad_values = tn(probs_low, grads)
            probs = probs_low.astype(F32)
            grad_probs = nt(grads, value)
            weighted = grad_probs * probs
            grad_scores = (
                (weighted - probs * jnp.sum(weighted, axis=1, keepdims=True)) * scale
            ).astype(BF16)
            grad_keys = tn(grad_scores, queries)
            grad_query = jnp.where(
                is_even, nn(grad_scores[:count], key), nn(grad_scores[count:], key)
            )
            gproj_ref[pl.ds(base, count), pl.ds(lane, LANES)] = grad_query.astype(BF16)
            gproj_ref[pl.ds(first, sizes.keys), pl.ds(wide + lane, LANES)] = grad_keys.astype(BF16)
            gproj_ref[pl.ds(first, sizes.keys), pl.ds(2 * wide + lane, LANES)] = (
                grad_values.astype(BF16)
            )
        return carry

    lax.fori_loop(0, sizes.pairs, body, 0)


def gelu_both(upward):
    half = 0.5 * (1.0 + lax.erf(upward * ROOT_HALF))
    slope = half + upward * jnp.exp(-0.5 * upward * upward) * INV_ROOT_TWO_PI
    return upward * half, slope


def up_block(up_ref, c, wide):
    step = wide // (up_ref.shape[1] * up_ref.shape[2])
    return up_ref[pl.ds(c * step, step)].reshape(-1, up_ref.shape[3])


def down_block(down_ref, c, wide):
    at = pl.multiple_of(c * wide, wide)
    return down_ref[:, :, :, pl.ds(at, wide)].reshape(-1, wide)


def ffn_back_step(
    sizes, c, wide, grad_low, hidden_low, active, slope, up_ref, down_ref, gup_ref, gdown_ref, vec
):
    at = pl.multiple_of(c * wide, wide)
    up = up_block(up_ref, c, wide)
    down = down_block(down_ref, c, wide)
    grad_active = nn(grad_low, down)
    grad_up_f = grad_active * slope
    grad_up = grad_up_f.astype(BF16)
    gdown_ref[:, :, :, pl.ds(at, wide)] = (
        tn(grad_low, active).astype(BF16).reshape(gdown_ref.shape[:3] + (wide,))
    )
    step = wide // (gup_ref.shape[1] * gup_ref.shape[2])
    gup_ref[pl.ds(c * step, step)] = (
        tn(grad_up, hidden_low).astype(BF16).reshape((step,) + gup_ref.shape[1:])
    )
    vec[pl.ds(8 + c, 1), :] = col_sum(grad_up.astype(F32))
    return nn(grad_up, up)


def attn_back_stage(
    sizes, seqs, gz, grad_mem_ref, att_ref, proj_ref, probs_ref, z_ref, qkv_ref, out_ref,
    gqkv_ref, gout_ref, go_ref, gproj_ref, branch_ref, vec, gh_ref, gmem_ref, back_left_ref,
    back_right_ref, scaled_rows=None,
):
    wide = sizes.width
    count = sizes.queries
    bias_out = col_sum(gz)
    for n in range(seqs):
        if sizes.top:
            mem_grad = grad_mem_ref[pl.ds(n * sizes.segs, sizes.segs), :]
            bias_out = bias_out + col_sum(mem_grad)
            branch_ref[pl.ds(n * count, sizes.top), :] = jnp.concatenate(
                [mem_grad, jnp.zeros((sizes.top - sizes.segs, wide), F32)], axis=0
            ).astype(BF16)
        branch_ref[pl.ds(n * count + sizes.top, sizes.rows), :] = gz[
            n * sizes.rows : (n + 1) * sizes.rows
        ].astype(BF16)
    vec[pl.ds(5, 1), :] = bias_out
    branch = branch_ref[...]
    gout_ref[...] = tn(branch, att_ref[...]).astype(BF16).reshape(gout_ref.shape)
    go_ref[...] = nn(branch, out_ref[...].reshape(-1, wide)).astype(BF16)
    attend_back(sizes, seqs, proj_ref, probs_ref, go_ref, gproj_ref)
    vec[pl.ds(3, 1), :] = col_sum(gproj_ref[:, pl.ds(0, wide)].astype(F32))
    vec[pl.ds(4, 1), :] = col_sum(gproj_ref[:, pl.ds(2 * wide, wide)].astype(F32))
    grad_ext = nn(gproj_ref[...], qkv_ref[...].reshape(-1, wide))
    gain_sum = jnp.zeros((1, wide), F32)
    bias_sum = jnp.zeros((1, wide), F32)
    for n in range(seqs):
        base = n * sizes.ext
        own = grad_ext[base + sizes.top : base + sizes.top + sizes.rows]
        if sizes.top:
            spread = grad_ext[base : base + sizes.segs] * (1.0 / SEG_LEN)
            own = own + segment_spread(sizes.rows, wide, spread)
        gh_ref[pl.ds(n * sizes.rows, sizes.rows), :] = own
        mem = base + sizes.mem_at
        gmem_ref[pl.ds(n * sizes.segs, sizes.segs), :] = grad_ext[mem : mem + sizes.segs]
        left = base + sizes.left_at
        back_left_ref[n] = grad_ext[left : left + BACK_ROWS].astype(BF16)
        right = base + sizes.right_at
        back_right_ref[n] = grad_ext[right : right + RIGHT_ROWS].astype(BF16)
        if scaled_rows is not None:
            grads = (
                own,
                grad_ext[right : right + RIGHT_ROWS],
                grad_ext[left : left + LEFT_ROWS],
            )
            for rows, scaled in zip(grads, scaled_rows(n)):
                gain_sum = gain_sum + col_sum(rows * scaled)
                bias_sum = bias_sum + col_sum(rows)
    if scaled_rows is not None:
        vec[pl.ds(0, 1), :] = gain_sum
        vec[pl.ds(2, 1), :] = bias_sum
    step = CHIPS_Z // 2
    part = gqkv_ref.shape[1] * gqkv_ref.shape[2] * step
    for c in range(2):
        gqkv_ref[pl.ds(c * step, step)] = (
            tn(gproj_ref[:, pl.ds(c * part, part)], z_ref[...])
            .astype(BF16)
            .reshape((step,) + gqkv_ref.shape[1:])
        )


def merge_halo(sizes, n, gh_ref, gmem_ref, from_right_ref, from_left_ref):
    first = n * sizes.rows
    back = from_right_ref[n].astype(F32)
    head = gh_ref[pl.ds(first, RIGHT_ROWS), :] + from_left_ref[n].astype(F32)
    middle = gh_ref[pl.ds(first + RIGHT_ROWS, sizes.rows - RIGHT_ROWS - LEFT_ROWS), :]
    tail = gh_ref[pl.ds(first + sizes.rows - LEFT_ROWS, LEFT_ROWS), :] + back[:LEFT_ROWS]
    mem = gmem_ref[pl.ds(n * sizes.segs, sizes.segs), :] + back[LEFT_ROWS + sizes.segs :]
    return jnp.concatenate([head, middle, tail], axis=0), mem


def pack_kernel(layers, qkv_ref, out_ref, up_ref, down_ref, *packed):
    eye = identity(LANES)
    high, wide, low = qkv_ref.shape[1], out_ref.shape[1], down_ref.shape[1]
    base = 0
    for layer, spots in enumerate(layers):
        parts = [
            (spots.qkv, high, qkv_ref[layer]),
            (spots.out, wide, out_ref[layer]),
            (spots.up, up_ref.shape[2], tn(up_ref[layer], eye).astype(BF16)),
        ] + [
            (spot, low, down_ref[layer, :, pl.ds(part * LANES, LANES)])
            for part, spot in enumerate(spots.down)
        ]
        for (group, first), rows, value in parts:
            ref = packed[base + group]
            for z in range(ref.shape[0]):
                ref[z, pl.ds(first, rows), :] = value
        base += 1 + int(spots.rows[1] > 0)


def unpack_kernel(layers, small_at, *refs):
    sources, outs = refs[:-7], refs[-7:]
    qkv_ref, out_ref, up_ref, down_ref, gains_ref, biases_ref, ffn_bias_ref = outs
    eye = identity(LANES)
    high, wide, low = qkv_ref.shape[1], out_ref.shape[1], down_ref.shape[1]

    def total(source, first, rows):
        ref = sources[source]
        value = ref[0, pl.ds(first, rows), :].astype(F32)
        for z in range(1, ref.shape[0]):
            value = value + ref[z, pl.ds(first, rows), :].astype(F32)
        return value

    base = 0
    for layer, spots in enumerate(layers):
        qkv_ref[layer] = total(base + spots.qkv[0], spots.qkv[1], high)
        out_ref[layer] = total(base + spots.out[0], spots.out[1], wide)
        up_ref[layer] = nt(
            eye, total(base + spots.up[0], spots.up[1], up_ref.shape[2]).astype(BF16)
        )
        for part, (group, first) in enumerate(spots.down):
            down_ref[layer, :, pl.ds(part * LANES, LANES)] = total(base + group, first, low)
        base += 1 + max(group for group, _ in spots.down)
    sums = total(small_at[0], small_at[1], SMALL_ROWS)
    parts = gains_ref.shape[2] // LANES
    for layer in range(gains_ref.shape[0]):
        for part in range(parts):
            lanes = pl.ds(part * LANES, LANES)
            block = sums[(layer * parts + part) * TILE : (layer * parts + part + 1) * TILE]
            gains_ref[layer, :, lanes] = block[0:2]
            for row in range(biases_ref.shape[0]):
                biases_ref[row, pl.ds(layer, 1), lanes] = block[2 + row : 3 + row]
            for row in range(ffn_bias_ref.shape[1] // gains_ref.shape[2]):
                at = row * gains_ref.shape[2] + part * LANES
                ffn_bias_ref[pl.ds(layer, 1), pl.ds(at, LANES)] = block[8 + row : 9 + row]


def near_small_kernel(count, mine_ref, theirs_ref, second_ref, first_ref, out_ref):
    rows = out_ref.shape[1] - SMALL_ROWS

    def total(at, size):
        group = pl.ds(at, size)
        value = mine_ref[0, group, :].astype(F32) + theirs_ref[0, group, :].astype(F32)
        return (
            value + second_ref[0, group, :].astype(F32) + first_ref[group, :].astype(F32)
        ).astype(BF16)

    small = total(count * rows, SMALL_ROWS)
    for z in range(count):
        out_ref[z, pl.ds(0, rows), :] = total(z * rows, rows)
        out_ref[z, pl.ds(rows, SMALL_ROWS), :] = small


def first_layer_kernel(
    sizes, seqs, mats, spots, count_in, place_ref, starts_ref, frames_ref, left_ref, right_ref,
    gains_ref, biases_ref, ffn_bias_ref, row_bias_ref, *refs
):
    groups = in_groups(spots, refs[:count_in])
    (
        z_ref, proj_ref, probs_ref, att_ref, mixed_ref, mem_ref, next_ref, active_ref, slope_ref,
        low_ref, send_right_ref, send_left_ref, qkv_ref, out_ref, up_ref, down_ref, mask_ref,
        hidden_ref, sems,
    ) = refs[count_in:]
    wide = sizes.width
    copies = start_in(attn_pairs(mats, spots, groups, qkv_ref, out_ref, place_ref), sems, 0)
    ffn_copies = start_in(
        ffn_pairs(mats, spots, groups, up_ref, down_ref, place_ref), sems, len(copies)
    )
    gain = gains_ref[0, pl.ds(0, 1), :]
    bias = biases_ref[0, pl.ds(0, 1), :]
    pad = jnp.zeros((TILE - sizes.segs, wide), F32)
    for n in range(seqs):
        own = frames_ref[n].astype(F32)
        before = left_ref[n].astype(F32)
        hidden = norm_forward(own, gain, bias)[0]
        halo = norm_forward(before[before.shape[0] - LEFT_ROWS :], gain, bias)[0]
        after = norm_forward(right_ref[n].astype(F32), gain, bias)[0]
        memory = jnp.concatenate(
            [
                segment_mean(own),
                jnp.zeros((sizes.segs - before.shape[0] // SEG_LEN, wide), F32),
                segment_mean(before),
            ],
            axis=0,
        )
        base = n * sizes.ext
        z_ref[pl.ds(base, sizes.top), :] = jnp.concatenate(
            [segment_mean(hidden), pad], axis=0
        ).astype(BF16)
        z_ref[pl.ds(base + sizes.top, sizes.rows), :] = hidden.astype(BF16)
        z_ref[pl.ds(base + sizes.right_at, RIGHT_ROWS), :] = after.astype(BF16)
        z_ref[pl.ds(base + sizes.left_at, LEFT_ROWS), :] = halo.astype(BF16)
        z_ref[pl.ds(base + sizes.mem_at, MEM_ROWS), :] = memory.astype(BF16)
    fill_mask(sizes, seqs, starts_ref, place_ref, mask_ref)
    wait_all(copies)
    project(sizes, z_ref, qkv_ref, row_bias_ref, proj_ref)
    attend(sizes, seqs, proj_ref, mask_ref, probs_ref, att_ref)
    mixed = nt(att_ref[...], out_ref[...].reshape(-1, wide)) + biases_ref[0, pl.ds(3, 1), :]
    for n in range(seqs):
        base = n * sizes.queries
        mem_ref[pl.ds(n * sizes.segs, sizes.segs), :] = mixed[base : base + sizes.segs]
        mixed_ref[pl.ds(n * sizes.rows, sizes.rows), :] = (
            frames_ref[n].astype(F32) + mixed[base + sizes.top : base + sizes.top + sizes.rows]
        )
    mixed = mixed_ref[...]
    hidden, _, _ = norm_forward(mixed, gains_ref[0, pl.ds(1, 1), :], biases_ref[0, pl.ds(4, 1), :])
    hidden_ref[...] = hidden.astype(BF16)
    next_ref[...] = mixed + biases_ref[0, pl.ds(5, 1), :]
    wait_all(ffn_copies)

    def body(c, carry):
        at_lane = pl.multiple_of(c * wide, wide)
        upward = nt(hidden_ref[...], up_block(up_ref, c, wide))
        upward = upward + ffn_bias_ref[pl.ds(0, 1), pl.ds(at_lane, wide)]
        active, slope = gelu_both(upward)
        active = active.astype(BF16)
        active_ref[:, pl.ds(at_lane, wide)] = active
        slope_ref[:, pl.ds(at_lane, wide)] = slope.astype(BF16)
        next_ref[...] += nt(active, down_block(down_ref, c, wide))
        return carry

    lax.fori_loop(0, sizes.ff // wide, body, 0)
    low, _, _ = norm_forward(
        next_ref[...], gains_ref[1, pl.ds(0, 1), :], biases_ref[1, pl.ds(0, 1), :]
    )
    low = low.astype(BF16)
    low_ref[...] = low
    for n in range(seqs):
        base = n * sizes.rows
        send_right_ref[n, pl.ds(0, LEFT_ROWS), :] = low[
            base + sizes.rows - LEFT_ROWS : base + sizes.rows
        ]
        send_right_ref[n, pl.ds(LEFT_ROWS, MEM_ROWS), :] = jnp.concatenate(
            [
                mem_ref[pl.ds(n * sizes.segs, sizes.segs), :],
                jnp.zeros((MEM_ROWS - sizes.segs, wide), F32),
            ],
            axis=0,
        ).astype(BF16)
        send_left_ref[n] = low[base : base + RIGHT_ROWS]


def last_layer_kernel(
    sizes, seqs, mats, cut, spots, count_in, count_out, place_ref, starts_ref, low_ref, left_ref,
    right_ref, mem_ref, inputs_ref, out_grad_ref, gains_ref, biases_ref, ffn_bias_ref,
    row_bias_ref, *refs
):
    groups = in_groups(spots, refs[:count_in])
    if cut is not None:
        classes = (count_in - 2) // 2
        rows = cut.rows[1]
        groups = [
            refs[: 2 * classes],
            [
                refs[2 * classes + core].at[:, pl.ds(k * rows, rows), :]
                for core in range(2)
                for k in range(classes)
            ],
        ]
    (encoded_ref, gz_ref, gh_ref, gmem_ref, back_left_ref, back_right_ref, vec) = refs[
        count_in : count_in + 7
    ]
    hbm_out = refs[count_in + 7 : count_in + 7 + count_out]
    (
        qkv_ref, out_ref, up_ref, down_ref, gqkv_ref, gout_ref, gup_ref, gdown_ref, mask_ref,
        z_ref, proj_ref, probs_ref, att_ref, hidden_ref, go_ref, gproj_ref, branch_ref,
        grad_low_ref, grad_hidden_ref, sems,
    ) = refs[count_in + 7 + count_out :]
    outs_to = hbm_out
    if spots is not None:
        outs_to = [[ref.at[k] for ref in hbm_out for k in range(ref.shape[0])]]
    wide = sizes.width
    attn_copies = start_in(attn_pairs(mats, cut, groups, qkv_ref, out_ref, place_ref), sems, 0)
    ffn_copies = start_in(
        ffn_pairs(mats, cut, groups, up_ref, down_ref, place_ref), sems, len(attn_copies)
    )
    vec[...] = jnp.zeros_like(vec)
    for n in range(seqs):
        base = n * sizes.ext
        z_ref[pl.ds(base, sizes.rows), :] = low_ref[pl.ds(n * sizes.rows, sizes.rows), :]
        z_ref[pl.ds(base + sizes.right_at, RIGHT_ROWS), :] = right_ref[n]
        z_ref[pl.ds(base + sizes.left_at, LEFT_ROWS), :] = left_ref[n, pl.ds(0, LEFT_ROWS), :]
        memory = jnp.concatenate(
            [
                mem_ref[pl.ds(n * sizes.segs, sizes.segs), :],
                left_ref[n, pl.ds(LEFT_ROWS, MEM_ROWS), :].astype(F32)[: sizes.segs],
            ],
            axis=0,
        )
        z_ref[pl.ds(base + sizes.mem_at, MEM_ROWS), :] = memory.astype(BF16)
        grad_low_ref[pl.ds(n * sizes.rows, sizes.rows), :] = out_grad_ref[n]
    fill_mask(sizes, seqs, starts_ref, place_ref, mask_ref)
    wait_all(attn_copies)
    project(sizes, z_ref, qkv_ref, row_bias_ref, proj_ref)
    attend(sizes, seqs, proj_ref, mask_ref, probs_ref, att_ref)
    mixed = (
        inputs_ref[...]
        + nt(att_ref[...], out_ref[...].reshape(-1, wide))
        + biases_ref[1, pl.ds(3, 1), :]
    )
    gain = gains_ref[1, pl.ds(1, 1), :]
    hidden, scaled, inverse = norm_forward(mixed, gain, biases_ref[1, pl.ds(4, 1), :])
    hidden_ref[...] = hidden.astype(BF16)
    for n in range(seqs):
        encoded_ref[n] = mixed[n * sizes.rows : (n + 1) * sizes.rows] + biases_ref[
            1, pl.ds(5, 1), :
        ]
    grad_hidden_ref[...] = jnp.zeros_like(grad_hidden_ref)
    wait_all(ffn_copies)

    def body(c, carry):
        at_lane = pl.multiple_of(c * wide, wide)
        upward = nt(hidden_ref[...], up_block(up_ref, c, wide))
        upward = upward + ffn_bias_ref[pl.ds(1, 1), pl.ds(at_lane, wide)]
        active, slope = gelu_both(upward)
        active = active.astype(BF16)
        made = nt(active, down_block(down_ref, c, wide))
        for n in range(seqs):
            encoded_ref[n] += made[n * sizes.rows : (n + 1) * sizes.rows]
        grad_hidden_ref[...] += ffn_back_step(
            sizes, c, wide, grad_low_ref[...], hidden_ref[...], active, slope, up_ref, down_ref,
            gup_ref, gdown_ref, vec,
        )
        return carry

    lax.fori_loop(0, sizes.ff // wide, body, 0)
    out_at = len(attn_copies) + len(ffn_copies)
    outs = start_out(
        ffn_pairs(mats, spots, outs_to, gup_ref, gdown_ref, place_ref), sems, out_at
    )
    grad = grad_low_ref[...].astype(F32)
    grad_hidden = grad_hidden_ref[...]
    vec[pl.ds(1, 1), :] = col_sum(grad_hidden * scaled)
    vec[pl.ds(6, 1), :] = col_sum(grad_hidden)
    vec[pl.ds(7, 1), :] = col_sum(grad)
    gz = grad + norm_backward(grad_hidden, scaled, inverse, gain)
    gz_ref[...] = gz
    attn_back_stage(
        sizes, seqs, gz, None, att_ref, proj_ref, probs_ref, z_ref, qkv_ref, out_ref, gqkv_ref,
        gout_ref, go_ref, gproj_ref, branch_ref, vec, gh_ref, gmem_ref, back_left_ref,
        back_right_ref,
    )
    outs = outs + start_out(
        attn_pairs(mats, spots, outs_to, gqkv_ref, gout_ref, place_ref),
        sems,
        out_at + len(outs),
    )
    wait_all(outs)


def first_back_kernel(
    last, sizes, seqs, mats, spots, count_in, count_out, place_ref, inputs_ref, gz_in_ref,
    gh_in_ref, gmem_in_ref, from_right_ref, from_left_ref, mixed_ref, active_ref, slope_ref,
    att_ref, probs_ref, proj_ref, z_ref, frames_ref, left_ref, right_ref, gains_ref, biases_ref,
    last_vec, *refs
):
    groups = in_groups(spots, refs[:count_in])
    gz_ref, gh_ref, gmem_ref, back_left_ref, back_right_ref, upper_vec, vec = refs[
        count_in : count_in + 7
    ]
    refs = refs[count_in + 7 :]
    hbm_out = refs[:count_out]
    (
        qkv_ref, out_ref, up_ref, down_ref, gqkv_ref, gout_ref, gup_ref, gdown_ref, hidden_ref,
        grad_low_ref, grad_ref, grad_hidden_ref, grad_mem_ref, go_ref, gproj_ref, branch_ref,
        small_ref, sems,
    ) = refs[count_out:]
    wide = sizes.width
    small = []
    outs_to = hbm_out
    if spots is not None:
        classes = count_in // 2
        rows = mats.attn_rows + mats.ffn_rows
        end = CHIPS_Z * rows
        each = [ref.at[k] for ref in hbm_out for k in range(classes)]
        small = [ref.at[pl.ds(end, SMALL_ROWS), :] for ref in each]
        outs_to = [[ref.at[pl.ds(0, end), :].reshape(CHIPS_Z, rows, LANES) for ref in each]]
    ffn_copies = start_in(ffn_pairs(mats, spots, groups, up_ref, down_ref, place_ref), sems, 0)
    attn_copies = start_in(
        attn_pairs(mats, spots, groups, qkv_ref, out_ref, place_ref), sems, len(ffn_copies)
    )
    vec[...] = jnp.zeros_like(vec)
    upper_vec[...] = jnp.zeros_like(upper_vec)
    gain = gains_ref[1, pl.ds(0, 1), :]
    gain_sum = jnp.zeros((1, wide), F32)
    bias_sum = jnp.zeros((1, wide), F32)
    for n in range(seqs):
        rows = pl.ds(n * sizes.rows, sizes.rows)
        _, scaled, inverse = norm_forward(
            inputs_ref[rows, :], gain, biases_ref[1, pl.ds(0, 1), :]
        )
        total, mem = merge_halo(last, n, gh_in_ref, gmem_in_ref, from_right_ref, from_left_ref)
        gain_sum = gain_sum + col_sum(total * scaled)
        bias_sum = bias_sum + col_sum(total)
        grad = gz_in_ref[rows, :] + norm_backward(total, scaled, inverse, gain)
        grad_ref[rows, :] = grad
        grad_low_ref[rows, :] = grad.astype(BF16)
        grad_mem_ref[pl.ds(n * sizes.segs, sizes.segs), :] = mem
    upper_vec[pl.ds(0, 1), :] = gain_sum
    upper_vec[pl.ds(2, 1), :] = bias_sum
    gain = gains_ref[0, pl.ds(1, 1), :]
    hidden, scaled, inverse = norm_forward(
        mixed_ref[...], gain, biases_ref[0, pl.ds(4, 1), :]
    )
    hidden_ref[...] = hidden.astype(BF16)
    grad_hidden_ref[...] = jnp.zeros_like(grad_hidden_ref)
    wait_all(ffn_copies)

    def body(c, carry):
        at_lane = pl.multiple_of(c * wide, wide)
        grad_hidden_ref[...] += ffn_back_step(
            sizes, c, wide, grad_low_ref[...], hidden_ref[...],
            active_ref[:, pl.ds(at_lane, wide)], slope_ref[:, pl.ds(at_lane, wide)].astype(F32),
            up_ref, down_ref, gup_ref, gdown_ref, vec,
        )
        return carry

    lax.fori_loop(0, sizes.ff // wide, body, 0)
    out_at = len(ffn_copies) + len(attn_copies)
    outs = start_out(
        ffn_pairs(mats, spots, outs_to, gup_ref, gdown_ref, place_ref), sems, out_at
    )
    grad_hidden = grad_hidden_ref[...]
    grad = grad_ref[...]
    vec[pl.ds(1, 1), :] = col_sum(grad_hidden * scaled)
    vec[pl.ds(6, 1), :] = col_sum(grad_hidden)
    vec[pl.ds(7, 1), :] = col_sum(grad)
    gz = grad + norm_backward(grad_hidden, scaled, inverse, gain)
    gz_ref[...] = gz

    def scaled_rows(n):
        before = left_ref[n, pl.ds(left_ref.shape[1] - LEFT_ROWS, LEFT_ROWS), :]
        parts = (frames_ref[n], right_ref[n], before)
        first_gain = gains_ref[0, pl.ds(0, 1), :]
        first_bias = biases_ref[0, pl.ds(0, 1), :]
        return [norm_forward(part.astype(F32), first_gain, first_bias)[1] for part in parts]

    wait_all(attn_copies)
    attn_back_stage(
        sizes, seqs, gz, grad_mem_ref, att_ref, proj_ref, probs_ref, z_ref, qkv_ref, out_ref,
        gqkv_ref, gout_ref, go_ref, gproj_ref, branch_ref, vec, gh_ref, gmem_ref, back_left_ref,
        back_right_ref, scaled_rows,
    )
    outs = outs + start_out(
        attn_pairs(mats, spots, outs_to, gqkv_ref, gout_ref, place_ref),
        sems,
        out_at + len(outs),
    )
    parts = sizes.width // LANES
    for layer, total in enumerate((vec[...], last_vec[...] + upper_vec[...])):
        for part in range(parts):
            small_ref[pl.ds((layer * parts + part) * TILE, TILE), :] = total[
                :, part * LANES : (part + 1) * LANES
            ].astype(BF16)
    outs = outs + start_out([(ref, small_ref) for ref in small], sems, out_at + len(outs))
    wait_all(outs)


def frames_grad_kernel(
    sizes, seqs, frames_ref, gz_ref, gh_ref, gmem_ref, from_right_ref, from_left_ref, gains_ref,
    biases_ref, grad_ref
):
    gain = gains_ref[0, pl.ds(0, 1), :]
    for n in range(seqs):
        _, scaled, inverse = norm_forward(
            frames_ref[n].astype(F32), gain, biases_ref[0, pl.ds(0, 1), :]
        )
        total, mem = merge_halo(sizes, n, gh_ref, gmem_ref, from_right_ref, from_left_ref)
        grad_ref[n] = (
            gz_ref[pl.ds(n * sizes.rows, sizes.rows), :]
            + norm_backward(total, scaled, inverse, gain)
            + segment_spread(sizes.rows, sizes.width, mem * (1.0 / SEG_LEN))
        )


def shifted(value, axis, by):
    size = lax.axis_size(axis)
    pairs = [(i, i + by) for i in range(size) if 0 <= i + by < size]
    return lax.ppermute(value, axis, pairs)


def permuted(value, move):
    reps = lax.axis_size("rep")
    pairs = []
    for flat in range(lax.axis_size("seg") * reps):
        seg, rep = divmod(flat, reps)
        z, y, x, core = move(seg // CHIPS_Y, seg % CHIPS_Y, rep // 2, rep % 2)
        pairs.append((flat, (z * CHIPS_Y + y) * reps + 2 * x + core))
    return lax.ppermute(value, ("seg", "rep"), pairs)


def across_first(value):
    return permuted(value, lambda z, y, x, c: (z, y, x ^ 1, c) if c == 0 else (z, y ^ 1, x, c))


def across_second(value):
    return permuted(value, lambda z, y, x, c: (z, y ^ 1, x, c) if c == 0 else (z, y, x ^ 1, c))


def other_core(value):
    return permuted(value, lambda z, y, x, c: (z, y, x, c ^ 1))


def after(value, *others):
    return lax.optimization_barrier((value,) + others)[0]


def swap_z(blocks):
    groups = [
        [z * CHIPS_Y + y for z in range(CHIPS_Z)] for y in range(CHIPS_Y)
    ]
    return lax.all_to_all(blocks, "seg", 0, 0, axis_index_groups=groups, tiled=True)


def gather_sides(here):
    return [here, across_first(here), across_second(here)]


def both_cores(blocks):
    return blocks + [other_core(block) for block in blocks]


def summed(*parts):
    total = parts[0].astype(F32)
    for part in parts[1:]:
        total = total + part.astype(F32)
    return total.astype(BF16)


def first_rows(rows):
    return pl.BlockSpec((1, rows, LANES), lambda i: (0, 0, 0))


def sum_everywhere(value):
    count = lax.axis_size("seg") * lax.axis_size("rep")
    bit = 1
    while bit < count:
        value = value + lax.ppermute(value, ("seg", "rep"), [(i, i ^ bit) for i in range(count)])
        bit *= 2
    return value


def vmem_spec():
    return pl.BlockSpec(memory_space=pltpu.VMEM)


def smem_spec():
    return pl.BlockSpec(memory_space=pltpu.SMEM)


def hbm_spec():
    return pl.BlockSpec(memory_space=pl.ANY)


def call(body, in_specs, out_shapes, out_specs, scratch, args, flops=0, moved=0, grid=()):
    return pl.pallas_call(
        body,
        grid=grid,
        in_specs=in_specs,
        out_shape=tuple(jax.ShapeDtypeStruct(shape, kind) for shape, kind in out_shapes),
        out_specs=tuple(out_specs),
        scratch_shapes=scratch,
        compiler_params=pltpu.CompilerParams(vmem_limit_bytes=VMEM_BYTES),
        cost_estimate=pl.CostEstimate(flops=flops, bytes_accessed=moved, transcendentals=0),
    )(*args)


def on_device(
    frames,
    utt_segments,
    out_grad,
    qkv_weight,
    out_weight,
    ffn_in_weight,
    ffn_out_weight,
    norm_gains,
    biases,
    ffn_bias,
):
    micros, groups, rows, width = frames.shape
    seqs = micros * groups
    ff = ffn_bias.shape[1]
    reps = lax.axis_size("rep")
    seg_count = lax.axis_size("seg")
    mats = Matrices(width, ff)
    by_blocks = width // reps == LANES and reps == 4 and seg_count == BLOCKS
    first = Sizes(rows, width, ff, True)
    last = Sizes(rows, width, ff, False)
    own = seqs * rows
    mem_own = seqs * first.segs

    seg_at = lax.axis_index("seg")
    seg_base = seg_at * first.segs
    rep_at = lax.axis_index("rep")
    place = [seg_base, jnp.int32(first.segs * seg_count)]
    y_at, x_at, core_at = seg_at % CHIPS_Y, rep_at // 2, rep_at % 2
    for other in range(2):
        core = lax.bitwise_xor(core_at, other)
        for hop2 in range(2):
            for hop1 in range(2):
                x_hop = jnp.where(core == 0, hop1, hop2)
                y_hop = jnp.where(core == 0, hop2, hop1)
                place.append(lax.bitwise_xor(y_at, y_hop))
                place.append((lax.bitwise_xor(x_at, x_hop) * 2 + core) * LANES)
    place = jnp.stack([jnp.asarray(entry, jnp.int32) for entry in place])
    lengths = utt_segments.reshape(seqs, utt_segments.shape[2])
    starts = (jnp.cumsum(lengths, axis=1) - lengths).astype(jnp.int32)
    zero_bias = jnp.zeros((width,), F32)
    row_bias = jnp.stack(
        [jnp.concatenate([biases[l, 1], zero_bias, biases[l, 2]]) for l in range(LAYERS)]
    ).reshape(LAYERS, 1, 3 * width)

    frames_own = frames.reshape(seqs, rows, width)
    grads_own = out_grad.reshape(seqs, rows, width)
    far = MEM_LEN * SEG_LEN
    frames_left = shifted(frames_own[:, rows - far :], "seg", 1)
    frames_right = shifted(frames_own[:, :RIGHT_ROWS], "seg", -1)

    attn_rows, ffn_rows = mats.attn_rows, mats.ffn_rows
    if by_blocks:
        qkv_t, out_t, down_t = (
            jnp.swapaxes(member, 1, 2) for member in (qkv_weight, out_weight, ffn_out_weight)
        )
        all_rows = attn_rows + ffn_rows
        spots, cut = Spots(mats), Spots(mats, True)
        shard0, shard1, shard_cut = call(
            lambda *refs: pack_kernel([spots, cut], *refs),
            [vmem_spec()] * 4,
            [
                ((CHIPS_Z, all_rows, LANES), BF16),
                ((CHIPS_Z, cut.rows[0], LANES), BF16),
                ((1, cut.rows[1], LANES), BF16),
            ],
            [vmem_spec()] * 3,
            [],
            (qkv_t, out_t, ffn_in_weight, down_t),
        )
        sides_cut = gather_sides(shard_cut)
        sides_cut.append(across_second(sides_cut[1]))
        plane = jnp.concatenate(sides_cut, axis=1)
        plane = jnp.broadcast_to(plane, (CHIPS_Z,) + plane.shape[1:])
        sides0 = gather_sides(after(swap_z(shard0), frames_left, frames_right, plane))
        place, starts, row_bias, sent = lax.optimization_barrier(
            (place, starts, row_bias, after(shard1, sides0[0]))
        )
        sides1 = gather_sides(swap_z(sent))
        lines = swap_z(after(plane, sides1[0]))
        first_all = both_cores(sides0 + [across_second(after(sides0[1], sides1[0]))])
        first_all[-1] = after(first_all[-1], lines)
        classes = len(first_all) // 2
        grad_outs0 = [((classes, CHIPS_Z * all_rows + SMALL_ROWS, LANES), BF16)] * 2
        grad_outs1 = [((classes, CHIPS_Z, all_rows, LANES), BF16)] * 2
        copies_in = len(first_all) * (3 + mats.down_parts)
    else:
        whole = []
        for member, shape in zip(
            (qkv_weight, out_weight, ffn_in_weight, ffn_out_weight),
            (mats.qkv, mats.out, mats.up, mats.down),
        ):
            member = lax.all_gather(member, "rep", axis=1, tiled=True)
            member = lax.all_gather(member, "seg", axis=2, tiled=True)
            whole.append(jnp.swapaxes(member, 1, 2).reshape((LAYERS,) + shape))
        first_all = [member[0] for member in whole]
        last_all = [member[1] for member in whole]
        spots = cut = None
        grad_outs0 = grad_outs1 = [
            (shape, BF16) for shape in (mats.qkv, mats.out, mats.up, mats.down)
        ]
        copies_in = 4
    dma = pltpu.SemaphoreType.DMA

    matrices = [pltpu.VMEM(shape, BF16) for shape in (mats.qkv, mats.out, mats.up, mats.down)]

    (
        z0, proj0, probs0, att0, mixed0, mem1, x1, active0, slope0, low1, send_right, send_left,
    ) = call(
        lambda *refs: first_layer_kernel(
            first, seqs, mats, spots, len(first_all), *refs
        ),
        [smem_spec()] * 2 + [vmem_spec()] * 7 + [hbm_spec()] * len(first_all),
        [
            ((seqs * first.ext, width), BF16),
            ((seqs * first.ext, 3 * width), BF16),
            ((seqs * first.pairs, 2 * first.queries, first.keys), BF16),
            ((seqs * first.queries, width), BF16),
            ((own, width), F32),
            ((mem_own, width), F32),
            ((own, width), F32),
            ((own, ff), BF16),
            ((own, ff), BF16),
            ((own, width), BF16),
            ((seqs, BACK_ROWS, width), BF16),
            ((seqs, RIGHT_ROWS, width), BF16),
        ],
        [vmem_spec()] * 12,
        matrices
        + [
            pltpu.VMEM((seqs, first.queries, first.keys), F32),
            pltpu.VMEM((own, width), BF16),
            dma((copies_in,)),
        ],
        (place, starts, frames_own, frames_left, frames_right, norm_gains, biases, ffn_bias,
         row_bias[0]) + tuple(first_all),
        flops=24 * own * (4 * width * width + 2 * width * ff) // 2,
        moved=2 * (4 * width * width + 2 * width * ff),
    )
    left1 = shifted(send_right, "seg", 1)
    right1 = shifted(send_left, "seg", -1)
    if by_blocks:
        last_side = across_second(after(sides1[1], sides1[2], low1))
        last_all = both_cores(sides1 + [last_side])
        last_all[-1] = other_core(after(last_side, left1, right1))
        last_all += [lines, other_core(lines)]

    vec_shape = (TILE, width)
    outs = call(
        lambda *refs: last_layer_kernel(
            last, seqs, mats, cut, spots, len(last_all), len(grad_outs1), *refs
        ),
        [smem_spec()] * 2 + [vmem_spec()] * 10 + [hbm_spec()] * len(last_all),
        [
            ((seqs, rows, width), F32),
            ((own, width), F32),
            ((own, width), F32),
            ((mem_own, width), F32),
            ((seqs, BACK_ROWS, width), BF16),
            ((seqs, RIGHT_ROWS, width), BF16),
            (vec_shape, F32),
        ]
        + grad_outs1,
        [vmem_spec()] * 7 + [hbm_spec()] * len(grad_outs1),
        matrices
        + matrices
        + [
            pltpu.VMEM((seqs, last.queries, last.keys), F32),
            pltpu.VMEM((seqs * last.ext, width), BF16),
            pltpu.VMEM((seqs * last.ext, 3 * width), BF16),
            pltpu.VMEM((seqs * last.pairs, 2 * last.queries, last.keys), BF16),
            pltpu.VMEM((seqs * last.queries, width), BF16),
            pltpu.VMEM((own, width), BF16),
            pltpu.VMEM((seqs * last.queries, width), BF16),
            pltpu.VMEM((seqs * last.ext, 3 * width), BF16),
            pltpu.VMEM((seqs * last.queries, width), BF16),
            pltpu.VMEM((own, width), BF16),
            pltpu.VMEM((own, width), F32),
            dma((2 * copies_in,)),
        ],
        (place, starts, low1, left1, right1, mem1, x1, grads_own, norm_gains, biases, ffn_bias,
         row_bias[1]) + tuple(last_all),
        flops=30 * own * (4 * width * width + 2 * width * ff),
        moved=4 * (4 * width * width + 2 * width * ff),
    )
    encoded, gz1, gh1, gmem1, back_left1, back_right1, vec1 = outs[:7]
    grad_blocks1 = outs[7:]
    from_right1 = shifted(back_left1, "seg", -1)
    from_left1 = shifted(back_right1, "seg", 1)

    gh1_tied = gh1
    if by_blocks:
        mine1, theirs1 = grad_blocks1[0], other_core(grad_blocks1[1])
        far1 = summed(mine1[2:], theirs1[2:])
        gh1_tied = after(gh1, far1)
    gz0, gh0, gmem0, back_left0, back_right0, upper_vec, vec0, *grad_blocks0 = call(
        lambda *refs: first_back_kernel(
            last, first, seqs, mats, spots, len(first_all), len(grad_outs0), *refs
        ),
        [smem_spec()] + [vmem_spec()] * 19 + [hbm_spec()] * len(first_all),
        [
            ((own, width), F32),
            ((own, width), F32),
            ((mem_own, width), F32),
            ((seqs, BACK_ROWS, width), BF16),
            ((seqs, RIGHT_ROWS, width), BF16),
            (vec_shape, F32),
            (vec_shape, F32),
        ]
        + grad_outs0,
        [vmem_spec()] * 7 + [hbm_spec()] * len(grad_outs0),
        matrices
        + matrices
        + [
            pltpu.VMEM((own, width), BF16),
            pltpu.VMEM((own, width), BF16),
            pltpu.VMEM((own, width), F32),
            pltpu.VMEM((own, width), F32),
            pltpu.VMEM((mem_own, width), F32),
            pltpu.VMEM((seqs * first.queries, width), BF16),
            pltpu.VMEM((seqs * first.ext, 3 * width), BF16),
            pltpu.VMEM((seqs * first.queries, width), BF16),
            pltpu.VMEM((SMALL_ROWS, LANES), BF16),
            dma((2 * copies_in + 8,)),
        ],
        (place, x1, gz1, gh1_tied, gmem1, from_right1, from_left1, mixed0, active0, slope0, att0,
         probs0, proj0, z0, frames_own, frames_left, frames_right, norm_gains, biases, vec1)
        + tuple(first_all),
        flops=28 * own * (4 * width * width + 2 * width * ff),
        moved=4 * (4 * width * width + 2 * width * ff),
    )
    from_right0 = shifted(back_left0, "seg", -1)
    from_left0 = shifted(back_right0, "seg", 1)
    gz0_last = gz0
    if by_blocks:
        second1 = across_second(far1)
        near1 = summed(mine1[1], theirs1[1], second1[1])
        first1 = across_first(near1)
        mine0, theirs0 = grad_blocks0[0], other_core(after(grad_blocks0[1], second1))
        quarters = (classes, CHIPS_Z, -1, LANES)
        far0 = summed(mine0.reshape(quarters)[2:], theirs0.reshape(quarters)[2:])
        far0 = after(far0.reshape((-1,) + mine0.shape[1:]), first1)
        second0 = across_second(far0)
        total1 = summed(mine1[0], theirs1[0], second1[0], after(first1, far0))
        last_parts = swap_z(total1)
        mid0 = summed(mine0[1], theirs0[1], after(second0, total1)[1])
        first0 = after(across_first(mid0), last_parts)
        near0 = call(
            lambda *refs: near_small_kernel(CHIPS_Z, *refs),
            [first_rows(mine0.shape[1])] * 3 + [vmem_spec()],
            [((CHIPS_Z, all_rows + SMALL_ROWS, LANES), BF16)],
            [vmem_spec()],
            [],
            [mine0, theirs0, second0, first0],
            grid=(1,),
        )[0]
        first_parts = swap_z(near0)
        gz0_last = after(gz0, near0)
    frames_grad = call(
        lambda *refs: frames_grad_kernel(first, seqs, *refs),
        [vmem_spec()] * 8,
        [((seqs, rows, width), F32)],
        [vmem_spec()],
        [],
        (frames_own, gz0_last, gh0, gmem0, from_right0, from_left0, norm_gains, biases),
    )[0]

    if by_blocks:
        shapes = [member.shape for member in (qkv_t, out_t, ffn_in_weight, down_t)]
        shapes += [norm_gains.shape, (biases.shape[1], LAYERS, width), ffn_bias.shape]
        reduced = call(
            lambda *refs: unpack_kernel([spots, spots], (0, all_rows), *refs),
            [vmem_spec()] * LAYERS,
            [(shape, F32) for shape in shapes],
            [vmem_spec()] * len(shapes),
            [],
            [after(first_parts, frames_grad), last_parts],
        )
        small = reduced[4], jnp.swapaxes(reduced[5], 0, 1), reduced[6]
        reduced = [
            jnp.swapaxes(reduced[0], 1, 2),
            jnp.swapaxes(reduced[1], 1, 2),
            reduced[2],
            jnp.swapaxes(reduced[3], 1, 2),
        ]
    else:
        reduced = []
        for member0, member1 in zip(grad_blocks0, grad_blocks1):
            both = jnp.stack([member0, member1]).reshape(LAYERS, -1, member0.shape[3])
            both = jnp.swapaxes(both, 1, 2)
            both = lax.psum_scatter(both, "seg", scatter_dimension=2, tiled=True)
            both = lax.psum_scatter(both, "rep", scatter_dimension=1, tiled=True)
            reduced.append(both.astype(F32))
        small = sum_everywhere(jnp.stack([vec0, vec1 + upper_vec]))
        small = small[:, 0:2], small[:, 2:8], small[:, 8:12].reshape(ffn_bias.shape)

    return (
        encoded.reshape(frames.shape),
        frames_grad.reshape(frames.shape),
        reduced[0],
        reduced[1],
        reduced[2],
        reduced[3],
        small[0],
        small[1],
        small[2],
    )


def solution(mesh):
    in_specs = (
        P(None, "rep", "seg", None),
        P(None, "rep", None),
        P(None, "rep", "seg", None),
        P(None, "rep", "seg"),
        P(None, "rep", "seg"),
        P(None, "rep", "seg"),
        P(None, "rep", "seg"),
        P(),
        P(),
        P(),
    )
    out_specs = (
        P(None, "rep", "seg", None),
        P(None, "rep", "seg", None),
        P(None, "rep", "seg"),
        P(None, "rep", "seg"),
        P(None, "rep", "seg"),
        P(None, "rep", "seg"),
        P(),
        P(),
        P(),
    )
    return jax.shard_map(
        on_device, mesh=mesh, in_specs=in_specs, out_specs=out_specs, check_vma=False
    )
```

```python
import jax
import jax.numpy as jnp
from jax import lax
from jax.experimental import pallas as pl
from jax.experimental.pallas import tpu as pltpu
from jax.sharding import PartitionSpec as P

HEADS = 8
SEG_LEN = 16
LEFT_LEN = 30
RIGHT_LEN = 4
MEM_LEN = 4
LAYERS = 2

EPS = 1e-05
ROOT_HALF = 0.7071067811865476
INV_ROOT_TWO_PI = 0.3989422804014327

LANES = 128
TILE = 16
RIGHT_ROWS = 16
LEFT_ROWS = 32
MEM_ROWS = 16
BACK_ROWS = LEFT_ROWS + MEM_ROWS
CHIPS_Z = 4
CHIPS_Y = 2
BLOCKS = CHIPS_Z * CHIPS_Y
SMALL_ROWS = 128
VMEM_BYTES = 56 * 1024 * 1024

BF16 = jnp.bfloat16
F32 = jnp.float32


def nn(a, b):
    return lax.dot_general(a, b, (((1,), (0,)), ((), ())), preferred_element_type=F32)


def nt(a, b):
    return lax.dot_general(a, b, (((1,), (1,)), ((), ())), preferred_element_type=F32)


def tn(a, b):
    return lax.dot_general(a, b, (((0,), (0,)), ((), ())), preferred_element_type=F32)


def col_sum(value):
    return jnp.sum(value, axis=0, keepdims=True)


def norm_forward(inputs, gain, bias):
    center = inputs - jnp.mean(inputs, axis=1, keepdims=True)
    inverse = lax.rsqrt(jnp.mean(center * center, axis=1, keepdims=True) + EPS)
    scaled = center * inverse
    return scaled * gain + bias, scaled, inverse


def norm_backward(grad_in, scaled, inverse, gain):
    grad_scaled = grad_in * gain
    return inverse * (
        grad_scaled
        - jnp.mean(grad_scaled, axis=1, keepdims=True)
        - scaled * jnp.mean(grad_scaled * scaled, axis=1, keepdims=True)
    )


def segment_mean(inputs):
    rows, width = inputs.shape
    return jnp.mean(inputs.reshape(rows // SEG_LEN, SEG_LEN, width), axis=1)


def segment_spread(rows, width, per_segment):
    segs = rows // SEG_LEN
    return jnp.broadcast_to(per_segment[:, None, :], (segs, SEG_LEN, width)).reshape(rows, width)


def identity(size):
    row = lax.broadcasted_iota(jnp.int32, (size, size), 0)
    col = lax.broadcasted_iota(jnp.int32, (size, size), 1)
    return (row == col).astype(F32).astype(BF16)


class Sizes:
    def __init__(self, rows, width, ff, with_summary):
        self.rows = rows
        self.width = width
        self.ff = ff
        self.segs = rows // SEG_LEN
        self.top = TILE if with_summary else 0
        self.keys = rows + RIGHT_ROWS + LEFT_ROWS + MEM_ROWS
        self.ext = self.top + self.keys
        self.queries = self.top + rows
        self.right_at = self.top + rows
        self.left_at = self.right_at + RIGHT_ROWS
        self.mem_at = self.left_at + LEFT_ROWS
        self.pairs = width // LANES


class Matrices:
    def __init__(self, width, ff):
        self.qkv = (CHIPS_Z, CHIPS_Y, 3 * width // BLOCKS, width)
        self.out = (CHIPS_Z, CHIPS_Y, width // BLOCKS, width)
        self.up = (CHIPS_Z, CHIPS_Y, ff // BLOCKS, width)
        self.down = (CHIPS_Z, CHIPS_Y, width // BLOCKS, ff)
        self.down_parts = ff // width
        self.attn_rows = self.qkv[2] + self.out[2]
        self.ffn_rows = self.up[2] + self.down_parts * self.down[2]


class Spots:
    def __init__(self, mats, cut=False):
        high, wide, up, low = mats.qkv[2], mats.out[2], mats.up[2], mats.down[2]
        sizes = [high, wide, up] + [low] * mats.down_parts
        rows = [0, 0]
        found = []
        for part, size in enumerate(sizes):
            group = int(cut and part in (1, 3))
            found.append((group, rows[group]))
            rows[group] += size
        self.qkv, self.out, self.up = found[:3]
        self.down = found[3:]
        self.rows = rows


def attn_pairs(mats, spots, groups, qkv_ref, out_ref, place_ref):
    if spots is None:
        return [(groups[0], qkv_ref), (groups[1], out_ref)]
    pairs = []
    for k in range(len(groups[0])):
        row = place_ref[2 + 2 * k]
        lane = pl.multiple_of(place_ref[3 + 2 * k], LANES)
        for (group, first), ref, shape in (
            (spots.qkv, qkv_ref, mats.qkv),
            (spots.out, out_ref, mats.out),
        ):
            block = groups[group][k]
            pairs.append(
                (
                    block.at[:, pl.ds(first, shape[2]), :],
                    ref.at[:, row, :, pl.ds(lane, LANES)],
                )
            )
    return pairs


def ffn_pairs(mats, spots, groups, up_ref, down_ref, place_ref):
    if spots is None:
        return [(groups[2], up_ref), (groups[3], down_ref)]
    pairs = []
    for k in range(len(groups[0])):
        row = place_ref[2 + 2 * k]
        lane = pl.multiple_of(place_ref[3 + 2 * k], LANES)
        group, first = spots.up
        block = groups[group][k]
        pairs.append(
            (block.at[:, pl.ds(first, mats.up[2]), :], up_ref.at[:, row, :, pl.ds(lane, LANES)])
        )
        for part, (group, first) in enumerate(spots.down):
            there = pl.multiple_of(
                place_ref[3 + 2 * k] * mats.down_parts + part * LANES, LANES
            )
            block = groups[group][k]
            pairs.append(
                (
                    block.at[:, pl.ds(first, mats.down[2]), :],
                    down_ref.at[:, row, :, pl.ds(there, LANES)],
                )
            )
    return pairs


def start_in(pairs, sems, at):
    copies = [pltpu.make_async_copy(s, d, sems.at[at + i]) for i, (s, d) in enumerate(pairs)]
    for copy in copies:
        copy.start()
    return copies


def start_out(pairs, sems, at):
    copies = [pltpu.make_async_copy(d, s, sems.at[at + i]) for i, (s, d) in enumerate(pairs)]
    for copy in copies:
        copy.start()
    return copies


def in_groups(spots, refs):
    return refs if spots is None else [refs]


def wait_all(copies):
    for copy in copies:
        copy.wait()


def fill_mask(sizes, seqs, starts_ref, place_ref, mask_ref):
    shape = (sizes.queries, sizes.keys)
    row = lax.broadcasted_iota(jnp.int32, shape, 0)
    col = lax.broadcasted_iota(jnp.int32, shape, 1)
    base = place_ref[0]
    total = place_ref[1]
    query = jnp.where(row < sizes.top, row, lax.shift_right_arithmetic(row - sizes.top, 4))
    left_at = sizes.rows + RIGHT_ROWS
    mem_at = left_at + LEFT_ROWS
    spot = jnp.where(col < left_at, col, col - mem_at)
    mem_seg = jnp.where(col < mem_at + sizes.segs, col - mem_at, col - mem_at - 2 * sizes.segs)
    key_seg = jnp.where(col < mem_at, lax.shift_right_arithmetic(spot, 4), mem_seg)
    near = (
        (key_seg == query)
        | ((spot >= query * SEG_LEN - LEFT_LEN) & (spot < query * SEG_LEN))
        | ((key_seg == query + 1) & (spot < query * SEG_LEN + SEG_LEN + RIGHT_LEN))
    )
    recent = (key_seg >= query - MEM_LEN) & (key_seg < query) & (row >= sizes.top)
    allowed = ((col < mem_at) & near) | ((col >= mem_at) & recent)
    key_abs = key_seg + base
    query_abs = query + base
    allowed = allowed & (key_abs >= 0) & (key_abs < total)
    if sizes.top:
        allowed = allowed & ((row < sizes.segs) | (row >= sizes.top))
    for n in range(seqs):
        key_owner = jnp.zeros(shape, jnp.int32)
        query_owner = jnp.zeros(shape, jnp.int32)
        for u in range(starts_ref.shape[1]):
            first = starts_ref[n, u]
            key_owner = key_owner + (key_abs >= first).astype(jnp.int32)
            query_owner = query_owner + (query_abs >= first).astype(jnp.int32)
        mask_ref[n] = jnp.where(allowed & (key_owner == query_owner), 0.0, -1e30)


def half_masks():
    lane = lax.broadcasted_iota(jnp.int32, (1, LANES), 1)
    even = (lane < LANES // 2).astype(F32)
    return even.astype(BF16), (1.0 - even).astype(BF16), lane < LANES // 2


def project(sizes, z_ref, qkv_ref, row_bias_ref, proj_ref):
    step = CHIPS_Z // 2
    for c in range(2):
        block = qkv_ref[pl.ds(c * step, step)].reshape(-1, sizes.width)
        wide = block.shape[0]
        made = nt(z_ref[...], block) + row_bias_ref[:, pl.ds(c * wide, wide)]
        proj_ref[:, pl.ds(c * wide, wide)] = made.astype(BF16)


def attend(sizes, seqs, proj_ref, mask_ref, probs_ref, att_ref):
    even, odd, is_even = half_masks()
    scale = (sizes.width // HEADS) ** (-0.5)
    count = sizes.queries

    def body(p, carry):
        for n in range(seqs):
            lane = pl.multiple_of(p * LANES, LANES)
            query = proj_ref[pl.ds(n * sizes.ext, count), pl.ds(lane, LANES)]
            first = n * sizes.ext + sizes.top
            key = proj_ref[pl.ds(first, sizes.keys), pl.ds(sizes.width + lane, LANES)]
            value = proj_ref[pl.ds(first, sizes.keys), pl.ds(2 * sizes.width + lane, LANES)]
            scores = nt(jnp.concatenate([query * even, query * odd], axis=0), key) * scale
            outs = []
            for half in range(2):
                part = scores[half * count : (half + 1) * count] + mask_ref[n]
                part = jnp.exp(part - jnp.max(part, axis=1, keepdims=True))
                part = (part * (1.0 / jnp.sum(part, axis=1, keepdims=True))).astype(BF16)
                probs_ref[n * sizes.pairs + p, pl.ds(half * count, count), :] = part
                outs.append(nn(part, value))
            att_ref[pl.ds(n * count, count), pl.ds(lane, LANES)] = jnp.where(
                is_even, outs[0], outs[1]
            ).astype(BF16)
        return carry

    lax.fori_loop(0, sizes.pairs, body, 0, unroll=True)


def attend_back(sizes, seqs, proj_ref, probs_ref, go_ref, gproj_ref):
    even, odd, is_even = half_masks()
    scale = (sizes.width // HEADS) ** (-0.5)
    count = sizes.queries
    wide = sizes.width
    for n in range(seqs):
        base = n * sizes.ext
        rest = sizes.ext - count
        gproj_ref[pl.ds(base + count, rest), pl.ds(0, wide)] = jnp.zeros((rest, wide), BF16)
        if sizes.top:
            gproj_ref[pl.ds(base, sizes.top), pl.ds(wide, 2 * wide)] = jnp.zeros(
                (sizes.top, 2 * wide), BF16
            )

    def body(p, carry):
        for n in range(seqs):
            lane = pl.multiple_of(p * LANES, LANES)
            base = n * sizes.ext
            first = base + sizes.top
            query = proj_ref[pl.ds(base, count), pl.ds(lane, LANES)]
            key = proj_ref[pl.ds(first, sizes.keys), pl.ds(wide + lane, LANES)]
            value = proj_ref[pl.ds(first, sizes.keys), pl.ds(2 * wide + lane, LANES)]
            grad = go_ref[pl.ds(n * count, count), pl.ds(lane, LANES)]
            queries = jnp.concatenate([query * even, query * odd], axis=0)
            grads = jnp.concatenate([grad * even, grad * odd], axis=0)
            probs_low = probs_ref[n * sizes.pairs + p]
            grad_values = tn(probs_low, grads)
            probs = probs_low.astype(F32)
            grad_probs = nt(grads, value)
            weighted = grad_probs * probs
            grad_scores = (
                (weighted - probs * jnp.sum(weighted, axis=1, keepdims=True)) * scale
            ).astype(BF16)
            grad_keys = tn(grad_scores, queries)
            grad_query = jnp.where(
                is_even, nn(grad_scores[:count], key), nn(grad_scores[count:], key)
            )
            gproj_ref[pl.ds(base, count), pl.ds(lane, LANES)] = grad_query.astype(BF16)
            gproj_ref[pl.ds(first, sizes.keys), pl.ds(wide + lane, LANES)] = grad_keys.astype(BF16)
            gproj_ref[pl.ds(first, sizes.keys), pl.ds(2 * wide + lane, LANES)] = (
                grad_values.astype(BF16)
            )
        return carry

    lax.fori_loop(0, sizes.pairs, body, 0)


def gelu_both(upward):
    half = 0.5 * (1.0 + lax.erf(upward * ROOT_HALF))
    slope = half + upward * jnp.exp(-0.5 * upward * upward) * INV_ROOT_TWO_PI
    return upward * half, slope


def up_block(up_ref, c, wide):
    step = wide // (up_ref.shape[1] * up_ref.shape[2])
    return up_ref[pl.ds(c * step, step)].reshape(-1, up_ref.shape[3])


def down_block(down_ref, c, wide):
    at = pl.multiple_of(c * wide, wide)
    return down_ref[:, :, :, pl.ds(at, wide)].reshape(-1, wide)


def ffn_back_step(
    sizes, c, wide, grad_low, hidden_low, active, slope, up_ref, down_ref, gup_ref, gdown_ref, vec
):
    at = pl.multiple_of(c * wide, wide)
    up = up_block(up_ref, c, wide)
    down = down_block(down_ref, c, wide)
    grad_active = nn(grad_low, down)
    grad_up_f = grad_active * slope
    grad_up = grad_up_f.astype(BF16)
    gdown_ref[:, :, :, pl.ds(at, wide)] = (
        tn(grad_low, active).astype(BF16).reshape(gdown_ref.shape[:3] + (wide,))
    )
    step = wide // (gup_ref.shape[1] * gup_ref.shape[2])
    gup_ref[pl.ds(c * step, step)] = (
        tn(grad_up, hidden_low).astype(BF16).reshape((step,) + gup_ref.shape[1:])
    )
    vec[pl.ds(8 + c, 1), :] = col_sum(grad_up.astype(F32))
    return nn(grad_up, up)


def attn_back_stage(
    sizes, seqs, gz, grad_mem_ref, att_ref, proj_ref, probs_ref, z_ref, qkv_ref, out_ref,
    gqkv_ref, gout_ref, go_ref, gproj_ref, branch_ref, vec, gh_ref, gmem_ref, back_left_ref,
    back_right_ref, scaled_rows=None,
):
    wide = sizes.width
    count = sizes.queries
    bias_out = col_sum(gz)
    for n in range(seqs):
        if sizes.top:
            mem_grad = grad_mem_ref[pl.ds(n * sizes.segs, sizes.segs), :]
            bias_out = bias_out + col_sum(mem_grad)
            branch_ref[pl.ds(n * count, sizes.top), :] = jnp.concatenate(
                [mem_grad, jnp.zeros((sizes.top - sizes.segs, wide), F32)], axis=0
            ).astype(BF16)
        branch_ref[pl.ds(n * count + sizes.top, sizes.rows), :] = gz[
            n * sizes.rows : (n + 1) * sizes.rows
        ].astype(BF16)
    vec[pl.ds(5, 1), :] = bias_out
    branch = branch_ref[...]
    gout_ref[...] = tn(branch, att_ref[...]).astype(BF16).reshape(gout_ref.shape)
    go_ref[...] = nn(branch, out_ref[...].reshape(-1, wide)).astype(BF16)
    attend_back(sizes, seqs, proj_ref, probs_ref, go_ref, gproj_ref)
    vec[pl.ds(3, 1), :] = col_sum(gproj_ref[:, pl.ds(0, wide)].astype(F32))
    vec[pl.ds(4, 1), :] = col_sum(gproj_ref[:, pl.ds(2 * wide, wide)].astype(F32))
    grad_ext = nn(gproj_ref[...], qkv_ref[...].reshape(-1, wide))
    gain_sum = jnp.zeros((1, wide), F32)
    bias_sum = jnp.zeros((1, wide), F32)
    for n in range(seqs):
        base = n * sizes.ext
        own = grad_ext[base + sizes.top : base + sizes.top + sizes.rows]
        if sizes.top:
            spread = grad_ext[base : base + sizes.segs] * (1.0 / SEG_LEN)
            own = own + segment_spread(sizes.rows, wide, spread)
        gh_ref[pl.ds(n * sizes.rows, sizes.rows), :] = own
        mem = base + sizes.mem_at
        gmem_ref[pl.ds(n * sizes.segs, sizes.segs), :] = grad_ext[mem : mem + sizes.segs]
        left = base + sizes.left_at
        back_left_ref[n] = grad_ext[left : left + BACK_ROWS].astype(BF16)
        right = base + sizes.right_at
        back_right_ref[n] = grad_ext[right : right + RIGHT_ROWS].astype(BF16)
        if scaled_rows is not None:
            grads = (
                own,
                grad_ext[right : right + RIGHT_ROWS],
                grad_ext[left : left + LEFT_ROWS],
            )
            for rows, scaled in zip(grads, scaled_rows(n)):
                gain_sum = gain_sum + col_sum(rows * scaled)
                bias_sum = bias_sum + col_sum(rows)
    if scaled_rows is not None:
        vec[pl.ds(0, 1), :] = gain_sum
        vec[pl.ds(2, 1), :] = bias_sum
    step = CHIPS_Z // 2
    part = gqkv_ref.shape[1] * gqkv_ref.shape[2] * step
    for c in range(2):
        gqkv_ref[pl.ds(c * step, step)] = (
            tn(gproj_ref[:, pl.ds(c * part, part)], z_ref[...])
            .astype(BF16)
            .reshape((step,) + gqkv_ref.shape[1:])
        )


def merge_halo(sizes, n, gh_ref, gmem_ref, from_right_ref, from_left_ref):
    first = n * sizes.rows
    back = from_right_ref[n].astype(F32)
    head = gh_ref[pl.ds(first, RIGHT_ROWS), :] + from_left_ref[n].astype(F32)
    middle = gh_ref[pl.ds(first + RIGHT_ROWS, sizes.rows - RIGHT_ROWS - LEFT_ROWS), :]
    tail = gh_ref[pl.ds(first + sizes.rows - LEFT_ROWS, LEFT_ROWS), :] + back[:LEFT_ROWS]
    mem = gmem_ref[pl.ds(n * sizes.segs, sizes.segs), :] + back[LEFT_ROWS + sizes.segs :]
    return jnp.concatenate([head, middle, tail], axis=0), mem


def pack_kernel(layers, qkv_ref, out_ref, up_ref, down_ref, *packed):
    eye = identity(LANES)
    high, wide, low = qkv_ref.shape[1], out_ref.shape[1], down_ref.shape[1]
    base = 0
    for layer, spots in enumerate(layers):
        parts = [
            (spots.qkv, high, qkv_ref[layer]),
            (spots.out, wide, out_ref[layer]),
            (spots.up, up_ref.shape[2], tn(up_ref[layer], eye).astype(BF16)),
        ] + [
            (spot, low, down_ref[layer, :, pl.ds(part * LANES, LANES)])
            for part, spot in enumerate(spots.down)
        ]
        for (group, first), rows, value in parts:
            ref = packed[base + group]
            for z in range(ref.shape[0]):
                ref[z, pl.ds(first, rows), :] = value
        base += 1 + int(spots.rows[1] > 0)


def unpack_kernel(layers, small_at, *refs):
    sources, outs = refs[:-7], refs[-7:]
    qkv_ref, out_ref, up_ref, down_ref, gains_ref, biases_ref, ffn_bias_ref = outs
    eye = identity(LANES)
    high, wide, low = qkv_ref.shape[1], out_ref.shape[1], down_ref.shape[1]

    def total(source, first, rows):
        ref = sources[source]
        value = ref[0, pl.ds(first, rows), :].astype(F32)
        for z in range(1, ref.shape[0]):
            value = value + ref[z, pl.ds(first, rows), :].astype(F32)
        return value

    base = 0
    for layer, spots in enumerate(layers):
        qkv_ref[layer] = total(base + spots.qkv[0], spots.qkv[1], high)
        out_ref[layer] = total(base + spots.out[0], spots.out[1], wide)
        up_ref[layer] = nt(
            eye, total(base + spots.up[0], spots.up[1], up_ref.shape[2]).astype(BF16)
        )
        for part, (group, first) in enumerate(spots.down):
            down_ref[layer, :, pl.ds(part * LANES, LANES)] = total(base + group, first, low)
        base += 1 + max(group for group, _ in spots.down)
    sums = total(small_at[0], small_at[1], SMALL_ROWS)
    parts = gains_ref.shape[2] // LANES
    for layer in range(gains_ref.shape[0]):
        for part in range(parts):
            lanes = pl.ds(part * LANES, LANES)
            block = sums[(layer * parts + part) * TILE : (layer * parts + part + 1) * TILE]
            gains_ref[layer, :, lanes] = block[0:2]
            for row in range(biases_ref.shape[0]):
                biases_ref[row, pl.ds(layer, 1), lanes] = block[2 + row : 3 + row]
            for row in range(ffn_bias_ref.shape[1] // gains_ref.shape[2]):
                at = row * gains_ref.shape[2] + part * LANES
                ffn_bias_ref[pl.ds(layer, 1), pl.ds(at, LANES)] = block[8 + row : 9 + row]


def near_small_kernel(count, mine_ref, theirs_ref, second_ref, first_ref, out_ref):
    rows = out_ref.shape[1] - SMALL_ROWS

    def total(at, size):
        group = pl.ds(at, size)
        value = mine_ref[0, group, :].astype(F32) + theirs_ref[0, group, :].astype(F32)
        return (
            value + second_ref[0, group, :].astype(F32) + first_ref[group, :].astype(F32)
        ).astype(BF16)

    small = total(count * rows, SMALL_ROWS)
    for z in range(count):
        out_ref[z, pl.ds(0, rows), :] = total(z * rows, rows)
        out_ref[z, pl.ds(rows, SMALL_ROWS), :] = small


def first_layer_kernel(
    sizes, seqs, mats, spots, count_in, place_ref, starts_ref, frames_ref, left_ref, right_ref,
    gains_ref, biases_ref, ffn_bias_ref, row_bias_ref, *refs
):
    groups = in_groups(spots, refs[:count_in])
    (
        z_ref, proj_ref, probs_ref, att_ref, mixed_ref, mem_ref, next_ref, active_ref, slope_ref,
        low_ref, send_right_ref, send_left_ref, qkv_ref, out_ref, up_ref, down_ref, mask_ref,
        hidden_ref, sems,
    ) = refs[count_in:]
    wide = sizes.width
    copies = start_in(attn_pairs(mats, spots, groups, qkv_ref, out_ref, place_ref), sems, 0)
    ffn_copies = start_in(
        ffn_pairs(mats, spots, groups, up_ref, down_ref, place_ref), sems, len(copies)
    )
    gain = gains_ref[0, pl.ds(0, 1), :]
    bias = biases_ref[0, pl.ds(0, 1), :]
    pad = jnp.zeros((TILE - sizes.segs, wide), F32)
    for n in range(seqs):
        own = frames_ref[n].astype(F32)
        before = left_ref[n].astype(F32)
        hidden = norm_forward(own, gain, bias)[0]
        halo = norm_forward(before[before.shape[0] - LEFT_ROWS :], gain, bias)[0]
        after = norm_forward(right_ref[n].astype(F32), gain, bias)[0]
        memory = jnp.concatenate(
            [
                segment_mean(own),
                jnp.zeros((sizes.segs - before.shape[0] // SEG_LEN, wide), F32),
                segment_mean(before),
            ],
            axis=0,
        )
        base = n * sizes.ext
        z_ref[pl.ds(base, sizes.top), :] = jnp.concatenate(
            [segment_mean(hidden), pad], axis=0
        ).astype(BF16)
        z_ref[pl.ds(base + sizes.top, sizes.rows), :] = hidden.astype(BF16)
        z_ref[pl.ds(base + sizes.right_at, RIGHT_ROWS), :] = after.astype(BF16)
        z_ref[pl.ds(base + sizes.left_at, LEFT_ROWS), :] = halo.astype(BF16)
        z_ref[pl.ds(base + sizes.mem_at, MEM_ROWS), :] = memory.astype(BF16)
    fill_mask(sizes, seqs, starts_ref, place_ref, mask_ref)
    wait_all(copies)
    project(sizes, z_ref, qkv_ref, row_bias_ref, proj_ref)
    attend(sizes, seqs, proj_ref, mask_ref, probs_ref, att_ref)
    mixed = nt(att_ref[...], out_ref[...].reshape(-1, wide)) + biases_ref[0, pl.ds(3, 1), :]
    for n in range(seqs):
        base = n * sizes.queries
        mem_ref[pl.ds(n * sizes.segs, sizes.segs), :] = mixed[base : base + sizes.segs]
        mixed_ref[pl.ds(n * sizes.rows, sizes.rows), :] = (
            frames_ref[n].astype(F32) + mixed[base + sizes.top : base + sizes.top + sizes.rows]
        )
    mixed = mixed_ref[...]
    hidden, _, _ = norm_forward(mixed, gains_ref[0, pl.ds(1, 1), :], biases_ref[0, pl.ds(4, 1), :])
    hidden_ref[...] = hidden.astype(BF16)
    next_ref[...] = mixed + biases_ref[0, pl.ds(5, 1), :]
    wait_all(ffn_copies)

    def body(c, carry):
        at_lane = pl.multiple_of(c * wide, wide)
        upward = nt(hidden_ref[...], up_block(up_ref, c, wide))
        upward = upward + ffn_bias_ref[pl.ds(0, 1), pl.ds(at_lane, wide)]
        active, slope = gelu_both(upward)
        active = active.astype(BF16)
        active_ref[:, pl.ds(at_lane, wide)] = active
        slope_ref[:, pl.ds(at_lane, wide)] = slope.astype(BF16)
        next_ref[...] += nt(active, down_block(down_ref, c, wide))
        return carry

    lax.fori_loop(0, sizes.ff // wide, body, 0)
    low, _, _ = norm_forward(
        next_ref[...], gains_ref[1, pl.ds(0, 1), :], biases_ref[1, pl.ds(0, 1), :]
    )
    low = low.astype(BF16)
    low_ref[...] = low
    for n in range(seqs):
        base = n * sizes.rows
        send_right_ref[n, pl.ds(0, LEFT_ROWS), :] = low[
            base + sizes.rows - LEFT_ROWS : base + sizes.rows
        ]
        send_right_ref[n, pl.ds(LEFT_ROWS, MEM_ROWS), :] = jnp.concatenate(
            [
                mem_ref[pl.ds(n * sizes.segs, sizes.segs), :],
                jnp.zeros((MEM_ROWS - sizes.segs, wide), F32),
            ],
            axis=0,
        ).astype(BF16)
        send_left_ref[n] = low[base : base + RIGHT_ROWS]


def last_layer_kernel(
    sizes, seqs, mats, cut, spots, count_in, count_out, place_ref, starts_ref, low_ref, left_ref,
    right_ref, mem_ref, inputs_ref, out_grad_ref, gains_ref, biases_ref, ffn_bias_ref,
    row_bias_ref, *refs
):
    groups = in_groups(spots, refs[:count_in])
    if cut is not None:
        classes = (count_in - 2) // 2
        rows = cut.rows[1]
        groups = [
            refs[: 2 * classes],
            [
                refs[2 * classes + core].at[:, pl.ds(k * rows, rows), :]
                for core in range(2)
                for k in range(classes)
            ],
        ]
    (encoded_ref, gz_ref, gh_ref, gmem_ref, back_left_ref, back_right_ref, vec) = refs[
        count_in : count_in + 7
    ]
    hbm_out = refs[count_in + 7 : count_in + 7 + count_out]
    (
        qkv_ref, out_ref, up_ref, down_ref, gqkv_ref, gout_ref, gup_ref, gdown_ref, mask_ref,
        z_ref, proj_ref, probs_ref, att_ref, hidden_ref, go_ref, gproj_ref, branch_ref,
        grad_low_ref, grad_hidden_ref, sems,
    ) = refs[count_in + 7 + count_out :]
    outs_to = hbm_out
    if spots is not None:
        outs_to = [[ref.at[k] for ref in hbm_out for k in range(ref.shape[0])]]
    wide = sizes.width
    attn_copies = start_in(attn_pairs(mats, cut, groups, qkv_ref, out_ref, place_ref), sems, 0)
    ffn_copies = start_in(
        ffn_pairs(mats, cut, groups, up_ref, down_ref, place_ref), sems, len(attn_copies)
    )
    vec[...] = jnp.zeros_like(vec)
    for n in range(seqs):
        base = n * sizes.ext
        z_ref[pl.ds(base, sizes.rows), :] = low_ref[pl.ds(n * sizes.rows, sizes.rows), :]
        z_ref[pl.ds(base + sizes.right_at, RIGHT_ROWS), :] = right_ref[n]
        z_ref[pl.ds(base + sizes.left_at, LEFT_ROWS), :] = left_ref[n, pl.ds(0, LEFT_ROWS), :]
        memory = jnp.concatenate(
            [
                mem_ref[pl.ds(n * sizes.segs, sizes.segs), :],
                left_ref[n, pl.ds(LEFT_ROWS, MEM_ROWS), :].astype(F32)[: sizes.segs],
            ],
            axis=0,
        )
        z_ref[pl.ds(base + sizes.mem_at, MEM_ROWS), :] = memory.astype(BF16)
        grad_low_ref[pl.ds(n * sizes.rows, sizes.rows), :] = out_grad_ref[n]
    fill_mask(sizes, seqs, starts_ref, place_ref, mask_ref)
    wait_all(attn_copies)
    project(sizes, z_ref, qkv_ref, row_bias_ref, proj_ref)
    attend(sizes, seqs, proj_ref, mask_ref, probs_ref, att_ref)
    mixed = (
        inputs_ref[...]
        + nt(att_ref[...], out_ref[...].reshape(-1, wide))
        + biases_ref[1, pl.ds(3, 1), :]
    )
    gain = gains_ref[1, pl.ds(1, 1), :]
    hidden, scaled, inverse = norm_forward(mixed, gain, biases_ref[1, pl.ds(4, 1), :])
    hidden_ref[...] = hidden.astype(BF16)
    for n in range(seqs):
        encoded_ref[n] = mixed[n * sizes.rows : (n + 1) * sizes.rows] + biases_ref[
            1, pl.ds(5, 1), :
        ]
    grad_hidden_ref[...] = jnp.zeros_like(grad_hidden_ref)
    wait_all(ffn_copies)

    def body(c, carry):
        at_lane = pl.multiple_of(c * wide, wide)
        upward = nt(hidden_ref[...], up_block(up_ref, c, wide))
        upward = upward + ffn_bias_ref[pl.ds(1, 1), pl.ds(at_lane, wide)]
        active, slope = gelu_both(upward)
        active = active.astype(BF16)
        made = nt(active, down_block(down_ref, c, wide))
        for n in range(seqs):
            encoded_ref[n] += made[n * sizes.rows : (n + 1) * sizes.rows]
        grad_hidden_ref[...] += ffn_back_step(
            sizes, c, wide, grad_low_ref[...], hidden_ref[...], active, slope, up_ref, down_ref,
            gup_ref, gdown_ref, vec,
        )
        return carry

    lax.fori_loop(0, sizes.ff // wide, body, 0)
    out_at = len(attn_copies) + len(ffn_copies)
    outs = start_out(
        ffn_pairs(mats, spots, outs_to, gup_ref, gdown_ref, place_ref), sems, out_at
    )
    grad = grad_low_ref[...].astype(F32)
    grad_hidden = grad_hidden_ref[...]
    vec[pl.ds(1, 1), :] = col_sum(grad_hidden * scaled)
    vec[pl.ds(6, 1), :] = col_sum(grad_hidden)
    vec[pl.ds(7, 1), :] = col_sum(grad)
    gz = grad + norm_backward(grad_hidden, scaled, inverse, gain)
    gz_ref[...] = gz
    attn_back_stage(
        sizes, seqs, gz, None, att_ref, proj_ref, probs_ref, z_ref, qkv_ref, out_ref, gqkv_ref,
        gout_ref, go_ref, gproj_ref, branch_ref, vec, gh_ref, gmem_ref, back_left_ref,
        back_right_ref,
    )
    outs = outs + start_out(
        attn_pairs(mats, spots, outs_to, gqkv_ref, gout_ref, place_ref),
        sems,
        out_at + len(outs),
    )
    wait_all(outs)


def first_back_kernel(
    last, sizes, seqs, mats, spots, count_in, count_out, place_ref, inputs_ref, gz_in_ref,
    gh_in_ref, gmem_in_ref, from_right_ref, from_left_ref, mixed_ref, active_ref, slope_ref,
    att_ref, probs_ref, proj_ref, z_ref, frames_ref, left_ref, right_ref, gains_ref, biases_ref,
    last_vec, *refs
):
    groups = in_groups(spots, refs[:count_in])
    gz_ref, gh_ref, gmem_ref, back_left_ref, back_right_ref, upper_vec, vec = refs[
        count_in : count_in + 7
    ]
    refs = refs[count_in + 7 :]
    hbm_out = refs[:count_out]
    (
        qkv_ref, out_ref, up_ref, down_ref, gqkv_ref, gout_ref, gup_ref, gdown_ref, hidden_ref,
        grad_low_ref, grad_ref, grad_hidden_ref, grad_mem_ref, go_ref, gproj_ref, branch_ref,
        small_ref, sems,
    ) = refs[count_out:]
    wide = sizes.width
    small = []
    outs_to = hbm_out
    if spots is not None:
        classes = count_in // 2
        rows = mats.attn_rows + mats.ffn_rows
        end = CHIPS_Z * rows
        each = [ref.at[k] for ref in hbm_out for k in range(classes)]
        small = [ref.at[pl.ds(end, SMALL_ROWS), :] for ref in each]
        outs_to = [[ref.at[pl.ds(0, end), :].reshape(CHIPS_Z, rows, LANES) for ref in each]]
    ffn_copies = start_in(ffn_pairs(mats, spots, groups, up_ref, down_ref, place_ref), sems, 0)
    attn_copies = start_in(
        attn_pairs(mats, spots, groups, qkv_ref, out_ref, place_ref), sems, len(ffn_copies)
    )
    vec[...] = jnp.zeros_like(vec)
    upper_vec[...] = jnp.zeros_like(upper_vec)
    gain = gains_ref[1, pl.ds(0, 1), :]
    gain_sum = jnp.zeros((1, wide), F32)
    bias_sum = jnp.zeros((1, wide), F32)
    for n in range(seqs):
        rows = pl.ds(n * sizes.rows, sizes.rows)
        _, scaled, inverse = norm_forward(
            inputs_ref[rows, :], gain, biases_ref[1, pl.ds(0, 1), :]
        )
        total, mem = merge_halo(last, n, gh_in_ref, gmem_in_ref, from_right_ref, from_left_ref)
        gain_sum = gain_sum + col_sum(total * scaled)
        bias_sum = bias_sum + col_sum(total)
        grad = gz_in_ref[rows, :] + norm_backward(total, scaled, inverse, gain)
        grad_ref[rows, :] = grad
        grad_low_ref[rows, :] = grad.astype(BF16)
        grad_mem_ref[pl.ds(n * sizes.segs, sizes.segs), :] = mem
    upper_vec[pl.ds(0, 1), :] = gain_sum
    upper_vec[pl.ds(2, 1), :] = bias_sum
    gain = gains_ref[0, pl.ds(1, 1), :]
    hidden, scaled, inverse = norm_forward(
        mixed_ref[...], gain, biases_ref[0, pl.ds(4, 1), :]
    )
    hidden_ref[...] = hidden.astype(BF16)
    grad_hidden_ref[...] = jnp.zeros_like(grad_hidden_ref)
    wait_all(ffn_copies)

    def body(c, carry):
        at_lane = pl.multiple_of(c * wide, wide)
        grad_hidden_ref[...] += ffn_back_step(
            sizes, c, wide, grad_low_ref[...], hidden_ref[...],
            active_ref[:, pl.ds(at_lane, wide)], slope_ref[:, pl.ds(at_lane, wide)].astype(F32),
            up_ref, down_ref, gup_ref, gdown_ref, vec,
        )
        return carry

    lax.fori_loop(0, sizes.ff // wide, body, 0)
    out_at = len(ffn_copies) + len(attn_copies)
    outs = start_out(
        ffn_pairs(mats, spots, outs_to, gup_ref, gdown_ref, place_ref), sems, out_at
    )
    grad_hidden = grad_hidden_ref[...]
    grad = grad_ref[...]
    vec[pl.ds(1, 1), :] = col_sum(grad_hidden * scaled)
    vec[pl.ds(6, 1), :] = col_sum(grad_hidden)
    vec[pl.ds(7, 1), :] = col_sum(grad)
    gz = grad + norm_backward(grad_hidden, scaled, inverse, gain)
    gz_ref[...] = gz

    def scaled_rows(n):
        before = left_ref[n, pl.ds(left_ref.shape[1] - LEFT_ROWS, LEFT_ROWS), :]
        parts = (frames_ref[n], right_ref[n], before)
        first_gain = gains_ref[0, pl.ds(0, 1), :]
        first_bias = biases_ref[0, pl.ds(0, 1), :]
        return [norm_forward(part.astype(F32), first_gain, first_bias)[1] for part in parts]

    wait_all(attn_copies)
    attn_back_stage(
        sizes, seqs, gz, grad_mem_ref, att_ref, proj_ref, probs_ref, z_ref, qkv_ref, out_ref,
        gqkv_ref, gout_ref, go_ref, gproj_ref, branch_ref, vec, gh_ref, gmem_ref, back_left_ref,
        back_right_ref, scaled_rows,
    )
    outs = outs + start_out(
        attn_pairs(mats, spots, outs_to, gqkv_ref, gout_ref, place_ref),
        sems,
        out_at + len(outs),
    )
    parts = sizes.width // LANES
    for layer, total in enumerate((vec[...], last_vec[...] + upper_vec[...])):
        for part in range(parts):
            small_ref[pl.ds((layer * parts + part) * TILE, TILE), :] = total[
                :, part * LANES : (part + 1) * LANES
            ].astype(BF16)
    outs = outs + start_out([(ref, small_ref) for ref in small], sems, out_at + len(outs))
    wait_all(outs)


def frames_grad_kernel(
    sizes, seqs, frames_ref, gz_ref, gh_ref, gmem_ref, from_right_ref, from_left_ref, gains_ref,
    biases_ref, grad_ref
):
    gain = gains_ref[0, pl.ds(0, 1), :]
    for n in range(seqs):
        _, scaled, inverse = norm_forward(
            frames_ref[n].astype(F32), gain, biases_ref[0, pl.ds(0, 1), :]
        )
        total, mem = merge_halo(sizes, n, gh_ref, gmem_ref, from_right_ref, from_left_ref)
        grad_ref[n] = (
            gz_ref[pl.ds(n * sizes.rows, sizes.rows), :]
            + norm_backward(total, scaled, inverse, gain)
            + segment_spread(sizes.rows, sizes.width, mem * (1.0 / SEG_LEN))
        )


def shifted(value, axis, by):
    size = lax.axis_size(axis)
    pairs = [(i, i + by) for i in range(size) if 0 <= i + by < size]
    return lax.ppermute(value, axis, pairs)


def permuted(value, move):
    reps = lax.axis_size("rep")
    pairs = []
    for flat in range(lax.axis_size("seg") * reps):
        seg, rep = divmod(flat, reps)
        z, y, x, core = move(seg // CHIPS_Y, seg % CHIPS_Y, rep // 2, rep % 2)
        pairs.append((flat, (z * CHIPS_Y + y) * reps + 2 * x + core))
    return lax.ppermute(value, ("seg", "rep"), pairs)


def across_first(value):
    return permuted(value, lambda z, y, x, c: (z, y, x ^ 1, c) if c == 0 else (z, y ^ 1, x, c))


def across_second(value):
    return permuted(value, lambda z, y, x, c: (z, y ^ 1, x, c) if c == 0 else (z, y, x ^ 1, c))


def other_core(value):
    return permuted(value, lambda z, y, x, c: (z, y, x, c ^ 1))


def after(value, *others):
    return lax.optimization_barrier((value,) + others)[0]


def swap_z(blocks):
    groups = [
        [z * CHIPS_Y + y for z in range(CHIPS_Z)] for y in range(CHIPS_Y)
    ]
    return lax.all_to_all(blocks, "seg", 0, 0, axis_index_groups=groups, tiled=True)


def gather_sides(here):
    return [here, across_first(here), across_second(here)]


def both_cores(blocks):
    return blocks + [other_core(block) for block in blocks]


def summed(*parts):
    total = parts[0].astype(F32)
    for part in parts[1:]:
        total = total + part.astype(F32)
    return total.astype(BF16)


def first_rows(rows):
    return pl.BlockSpec((1, rows, LANES), lambda i: (0, 0, 0))


def sum_everywhere(value):
    count = lax.axis_size("seg") * lax.axis_size("rep")
    bit = 1
    while bit < count:
        value = value + lax.ppermute(value, ("seg", "rep"), [(i, i ^ bit) for i in range(count)])
        bit *= 2
    return value


def vmem_spec():
    return pl.BlockSpec(memory_space=pltpu.VMEM)


def smem_spec():
    return pl.BlockSpec(memory_space=pltpu.SMEM)


def hbm_spec():
    return pl.BlockSpec(memory_space=pl.ANY)


def call(body, in_specs, out_shapes, out_specs, scratch, args, flops=0, moved=0, grid=()):
    return pl.pallas_call(
        body,
        grid=grid,
        in_specs=in_specs,
        out_shape=tuple(jax.ShapeDtypeStruct(shape, kind) for shape, kind in out_shapes),
        out_specs=tuple(out_specs),
        scratch_shapes=scratch,
        compiler_params=pltpu.CompilerParams(vmem_limit_bytes=VMEM_BYTES),
        cost_estimate=pl.CostEstimate(flops=flops, bytes_accessed=moved, transcendentals=0),
    )(*args)


def on_device(
    frames,
    utt_segments,
    out_grad,
    qkv_weight,
    out_weight,
    ffn_in_weight,
    ffn_out_weight,
    norm_gains,
    biases,
    ffn_bias,
):
    micros, groups, rows, width = frames.shape
    seqs = micros * groups
    ff = ffn_bias.shape[1]
    reps = lax.axis_size("rep")
    seg_count = lax.axis_size("seg")
    mats = Matrices(width, ff)
    by_blocks = width // reps == LANES and reps == 4 and seg_count == BLOCKS
    first = Sizes(rows, width, ff, True)
    last = Sizes(rows, width, ff, False)
    own = seqs * rows
    mem_own = seqs * first.segs

    seg_at = lax.axis_index("seg")
    seg_base = seg_at * first.segs
    rep_at = lax.axis_index("rep")
    place = [seg_base, jnp.int32(first.segs * seg_count)]
    y_at, x_at, core_at = seg_at % CHIPS_Y, rep_at // 2, rep_at % 2
    for other in range(2):
        core = lax.bitwise_xor(core_at, other)
        for hop2 in range(2):
            for hop1 in range(2):
                x_hop = jnp.where(core == 0, hop1, hop2)
                y_hop = jnp.where(core == 0, hop2, hop1)
                place.append(lax.bitwise_xor(y_at, y_hop))
                place.append((lax.bitwise_xor(x_at, x_hop) * 2 + core) * LANES)
    place = jnp.stack([jnp.asarray(entry, jnp.int32) for entry in place])
    lengths = utt_segments.reshape(seqs, utt_segments.shape[2])
    starts = (jnp.cumsum(lengths, axis=1) - lengths).astype(jnp.int32)
    zero_bias = jnp.zeros((width,), F32)
    row_bias = jnp.stack(
        [jnp.concatenate([biases[l, 1], zero_bias, biases[l, 2]]) for l in range(LAYERS)]
    ).reshape(LAYERS, 1, 3 * width)

    frames_own = frames.reshape(seqs, rows, width)
    grads_own = out_grad.reshape(seqs, rows, width)
    far = MEM_LEN * SEG_LEN
    frames_left = shifted(frames_own[:, rows - far :], "seg", 1)
    frames_right = shifted(frames_own[:, :RIGHT_ROWS], "seg", -1)

    attn_rows, ffn_rows = mats.attn_rows, mats.ffn_rows
    if by_blocks:
        qkv_t, out_t, down_t = (
            jnp.swapaxes(member, 1, 2) for member in (qkv_weight, out_weight, ffn_out_weight)
        )
        all_rows = attn_rows + ffn_rows
        spots, cut = Spots(mats), Spots(mats, True)
        shard0, shard1, shard_cut = call(
            lambda *refs: pack_kernel([spots, cut], *refs),
            [vmem_spec()] * 4,
            [
                ((CHIPS_Z, all_rows, LANES), BF16),
                ((CHIPS_Z, cut.rows[0], LANES), BF16),
                ((1, cut.rows[1], LANES), BF16),
            ],
            [vmem_spec()] * 3,
            [],
            (qkv_t, out_t, ffn_in_weight, down_t),
        )
        sides_cut = gather_sides(shard_cut)
        sides_cut.append(across_second(sides_cut[1]))
        plane = jnp.concatenate(sides_cut, axis=1)
        plane = jnp.broadcast_to(plane, (CHIPS_Z,) + plane.shape[1:])
        sides0 = gather_sides(after(swap_z(shard0), frames_left, frames_right, plane))
        place, starts, row_bias, sent = lax.optimization_barrier(
            (place, starts, row_bias, after(shard1, sides0[0]))
        )
        sides1 = gather_sides(swap_z(sent))
        lines = swap_z(after(plane, sides1[0]))
        first_all = both_cores(sides0 + [across_second(after(sides0[1], sides1[0]))])
        classes = len(first_all) // 2
        grad_outs0 = [((classes, CHIPS_Z * all_rows + SMALL_ROWS, LANES), BF16)] * 2
        grad_outs1 = [((classes, CHIPS_Z, all_rows, LANES), BF16)] * 2
        copies_in = len(first_all) * (3 + mats.down_parts)
    else:
        whole = []
        for member, shape in zip(
            (qkv_weight, out_weight, ffn_in_weight, ffn_out_weight),
            (mats.qkv, mats.out, mats.up, mats.down),
        ):
            member = lax.all_gather(member, "rep", axis=1, tiled=True)
            member = lax.all_gather(member, "seg", axis=2, tiled=True)
            whole.append(jnp.swapaxes(member, 1, 2).reshape((LAYERS,) + shape))
        first_all = [member[0] for member in whole]
        last_all = [member[1] for member in whole]
        spots = cut = None
        grad_outs0 = grad_outs1 = [
            (shape, BF16) for shape in (mats.qkv, mats.out, mats.up, mats.down)
        ]
        copies_in = 4
    dma = pltpu.SemaphoreType.DMA

    matrices = [pltpu.VMEM(shape, BF16) for shape in (mats.qkv, mats.out, mats.up, mats.down)]

    (
        z0, proj0, probs0, att0, mixed0, mem1, x1, active0, slope0, low1, send_right, send_left,
    ) = call(
        lambda *refs: first_layer_kernel(
            first, seqs, mats, spots, len(first_all), *refs
        ),
        [smem_spec()] * 2 + [vmem_spec()] * 7 + [hbm_spec()] * len(first_all),
        [
            ((seqs * first.ext, width), BF16),
            ((seqs * first.ext, 3 * width), BF16),
            ((seqs * first.pairs, 2 * first.queries, first.keys), BF16),
            ((seqs * first.queries, width), BF16),
            ((own, width), F32),
            ((mem_own, width), F32),
            ((own, width), F32),
            ((own, ff), BF16),
            ((own, ff), BF16),
            ((own, width), BF16),
            ((seqs, BACK_ROWS, width), BF16),
            ((seqs, RIGHT_ROWS, width), BF16),
        ],
        [vmem_spec()] * 12,
        matrices
        + [
            pltpu.VMEM((seqs, first.queries, first.keys), F32),
            pltpu.VMEM((own, width), BF16),
            dma((copies_in,)),
        ],
        (place, starts, frames_own, frames_left, frames_right, norm_gains, biases, ffn_bias,
         row_bias[0]) + tuple(first_all),
        flops=24 * own * (4 * width * width + 2 * width * ff) // 2,
        moved=2 * (4 * width * width + 2 * width * ff),
    )
    left1 = shifted(send_right, "seg", 1)
    right1 = shifted(send_left, "seg", -1)
    if by_blocks:
        last_side = across_second(after(sides1[1], sides1[2], low1, lines))
        last_all = both_cores(sides1 + [last_side])
        last_all[-1] = other_core(after(last_side, left1, right1))
        last_all += [lines, other_core(lines)]

    vec_shape = (TILE, width)
    outs = call(
        lambda *refs: last_layer_kernel(
            last, seqs, mats, cut, spots, len(last_all), len(grad_outs1), *refs
        ),
        [smem_spec()] * 2 + [vmem_spec()] * 10 + [hbm_spec()] * len(last_all),
        [
            ((seqs, rows, width), F32),
            ((own, width), F32),
            ((own, width), F32),
            ((mem_own, width), F32),
            ((seqs, BACK_ROWS, width), BF16),
            ((seqs, RIGHT_ROWS, width), BF16),
            (vec_shape, F32),
        ]
        + grad_outs1,
        [vmem_spec()] * 7 + [hbm_spec()] * len(grad_outs1),
        matrices
        + matrices
        + [
            pltpu.VMEM((seqs, last.queries, last.keys), F32),
            pltpu.VMEM((seqs * last.ext, width), BF16),
            pltpu.VMEM((seqs * last.ext, 3 * width), BF16),
            pltpu.VMEM((seqs * last.pairs, 2 * last.queries, last.keys), BF16),
            pltpu.VMEM((seqs * last.queries, width), BF16),
            pltpu.VMEM((own, width), BF16),
            pltpu.VMEM((seqs * last.queries, width), BF16),
            pltpu.VMEM((seqs * last.ext, 3 * width), BF16),
            pltpu.VMEM((seqs * last.queries, width), BF16),
            pltpu.VMEM((own, width), BF16),
            pltpu.VMEM((own, width), F32),
            dma((2 * copies_in,)),
        ],
        (place, starts, low1, left1, right1, mem1, x1, grads_own, norm_gains, biases, ffn_bias,
         row_bias[1]) + tuple(last_all),
        flops=30 * own * (4 * width * width + 2 * width * ff),
        moved=4 * (4 * width * width + 2 * width * ff),
    )
    encoded, gz1, gh1, gmem1, back_left1, back_right1, vec1 = outs[:7]
    grad_blocks1 = outs[7:]
    from_right1 = shifted(back_left1, "seg", -1)
    from_left1 = shifted(back_right1, "seg", 1)

    gh1_tied = gh1
    if by_blocks:
        mine1, theirs1 = grad_blocks1[0], other_core(grad_blocks1[1])
        far1 = summed(mine1[2:], theirs1[2:])
        gh1_tied = after(gh1, far1)
    gz0, gh0, gmem0, back_left0, back_right0, upper_vec, vec0, *grad_blocks0 = call(
        lambda *refs: first_back_kernel(
            last, first, seqs, mats, spots, len(first_all), len(grad_outs0), *refs
        ),
        [smem_spec()] + [vmem_spec()] * 19 + [hbm_spec()] * len(first_all),
        [
            ((own, width), F32),
            ((own, width), F32),
            ((mem_own, width), F32),
            ((seqs, BACK_ROWS, width), BF16),
            ((seqs, RIGHT_ROWS, width), BF16),
            (vec_shape, F32),
            (vec_shape, F32),
        ]
        + grad_outs0,
        [vmem_spec()] * 7 + [hbm_spec()] * len(grad_outs0),
        matrices
        + matrices
        + [
            pltpu.VMEM((own, width), BF16),
            pltpu.VMEM((own, width), BF16),
            pltpu.VMEM((own, width), F32),
            pltpu.VMEM((own, width), F32),
            pltpu.VMEM((mem_own, width), F32),
            pltpu.VMEM((seqs * first.queries, width), BF16),
            pltpu.VMEM((seqs * first.ext, 3 * width), BF16),
            pltpu.VMEM((seqs * first.queries, width), BF16),
            pltpu.VMEM((SMALL_ROWS, LANES), BF16),
            dma((2 * copies_in + 8,)),
        ],
        (place, x1, gz1, gh1_tied, gmem1, from_right1, from_left1, mixed0, active0, slope0, att0,
         probs0, proj0, z0, frames_own, frames_left, frames_right, norm_gains, biases, vec1)
        + tuple(first_all),
        flops=28 * own * (4 * width * width + 2 * width * ff),
        moved=4 * (4 * width * width + 2 * width * ff),
    )
    from_right0 = shifted(back_left0, "seg", -1)
    from_left0 = shifted(back_right0, "seg", 1)
    gz0_last = gz0
    if by_blocks:
        second1 = across_second(far1)
        near1 = summed(mine1[1], theirs1[1], second1[1])
        first1 = across_first(near1)
        mine0, theirs0 = grad_blocks0[0], other_core(after(grad_blocks0[1], second1))
        far0 = after(summed(mine0[2:], theirs0[2:]), first1)
        second0 = across_second(far0)
        total1 = summed(mine1[0], theirs1[0], second1[0], after(first1, far0))
        last_parts = swap_z(total1)
        mid0 = summed(mine0[1], theirs0[1], after(second0, total1)[1])
        first0 = after(across_first(mid0), last_parts)
        near0 = call(
            lambda *refs: near_small_kernel(CHIPS_Z, *refs),
            [first_rows(mine0.shape[1])] * 3 + [vmem_spec()],
            [((CHIPS_Z, all_rows + SMALL_ROWS, LANES), BF16)],
            [vmem_spec()],
            [],
            [mine0, theirs0, second0, first0],
            grid=(1,),
        )[0]
        first_parts = swap_z(near0)
        gz0_last = after(gz0, near0)
    frames_grad = call(
        lambda *refs: frames_grad_kernel(first, seqs, *refs),
        [vmem_spec()] * 8,
        [((seqs, rows, width), F32)],
        [vmem_spec()],
        [],
        (frames_own, gz0_last, gh0, gmem0, from_right0, from_left0, norm_gains, biases),
    )[0]

    if by_blocks:
        shapes = [member.shape for member in (qkv_t, out_t, ffn_in_weight, down_t)]
        shapes += [norm_gains.shape, (biases.shape[1], LAYERS, width), ffn_bias.shape]
        reduced = call(
            lambda *refs: unpack_kernel([spots, spots], (0, all_rows), *refs),
            [vmem_spec()] * LAYERS,
            [(shape, F32) for shape in shapes],
            [vmem_spec()] * len(shapes),
            [],
            [after(first_parts, frames_grad), last_parts],
        )
        small = reduced[4], jnp.swapaxes(reduced[5], 0, 1), reduced[6]
        reduced = [
            jnp.swapaxes(reduced[0], 1, 2),
            jnp.swapaxes(reduced[1], 1, 2),
            reduced[2],
            jnp.swapaxes(reduced[3], 1, 2),
        ]
    else:
        reduced = []
        for member0, member1 in zip(grad_blocks0, grad_blocks1):
            both = jnp.stack([member0, member1]).reshape(LAYERS, -1, member0.shape[3])
            both = jnp.swapaxes(both, 1, 2)
            both = lax.psum_scatter(both, "seg", scatter_dimension=2, tiled=True)
            both = lax.psum_scatter(both, "rep", scatter_dimension=1, tiled=True)
            reduced.append(both.astype(F32))
        small = sum_everywhere(jnp.stack([vec0, vec1 + upper_vec]))
        small = small[:, 0:2], small[:, 2:8], small[:, 8:12].reshape(ffn_bias.shape)

    return (
        encoded.reshape(frames.shape),
        frames_grad.reshape(frames.shape),
        reduced[0],
        reduced[1],
        reduced[2],
        reduced[3],
        small[0],
        small[1],
        small[2],
    )


def solution(mesh):
    in_specs = (
        P(None, "rep", "seg", None),
        P(None, "rep", None),
        P(None, "rep", "seg", None),
        P(None, "rep", "seg"),
        P(None, "rep", "seg"),
        P(None, "rep", "seg"),
        P(None, "rep", "seg"),
        P(),
        P(),
        P(),
    )
    out_specs = (
        P(None, "rep", "seg", None),
        P(None, "rep", "seg", None),
        P(None, "rep", "seg"),
        P(None, "rep", "seg"),
        P(None, "rep", "seg"),
        P(None, "rep", "seg"),
        P(),
        P(),
        P(),
    )
    return jax.shard_map(
        on_device, mesh=mesh, in_specs=in_specs, out_specs=out_specs, check_vma=False
    )
```

```python
import jax
import jax.numpy as jnp
from jax import lax
from jax.experimental import pallas as pl
from jax.experimental.pallas import tpu as pltpu
from jax.sharding import PartitionSpec as P

HEADS = 8
SEG_LEN = 16
LEFT_LEN = 30
RIGHT_LEN = 4
MEM_LEN = 4
LAYERS = 2

EPS = 1e-05
ROOT_HALF = 0.7071067811865476
INV_ROOT_TWO_PI = 0.3989422804014327

LANES = 128
TILE = 16
RIGHT_ROWS = 16
LEFT_ROWS = 32
MEM_ROWS = 16
BACK_ROWS = LEFT_ROWS + MEM_ROWS
CHIPS_Z = 4
CHIPS_Y = 2
BLOCKS = CHIPS_Z * CHIPS_Y
SMALL_ROWS = 128
VMEM_BYTES = 56 * 1024 * 1024

BF16 = jnp.bfloat16
F32 = jnp.float32


def nn(a, b):
    return lax.dot_general(a, b, (((1,), (0,)), ((), ())), preferred_element_type=F32)


def nt(a, b):
    return lax.dot_general(a, b, (((1,), (1,)), ((), ())), preferred_element_type=F32)


def tn(a, b):
    return lax.dot_general(a, b, (((0,), (0,)), ((), ())), preferred_element_type=F32)


def col_sum(value):
    return jnp.sum(value, axis=0, keepdims=True)


def norm_forward(inputs, gain, bias):
    center = inputs - jnp.mean(inputs, axis=1, keepdims=True)
    inverse = lax.rsqrt(jnp.mean(center * center, axis=1, keepdims=True) + EPS)
    scaled = center * inverse
    return scaled * gain + bias, scaled, inverse


def norm_backward(grad_in, scaled, inverse, gain):
    grad_scaled = grad_in * gain
    return inverse * (
        grad_scaled
        - jnp.mean(grad_scaled, axis=1, keepdims=True)
        - scaled * jnp.mean(grad_scaled * scaled, axis=1, keepdims=True)
    )


def segment_mean(inputs):
    rows, width = inputs.shape
    return jnp.mean(inputs.reshape(rows // SEG_LEN, SEG_LEN, width), axis=1)


def segment_spread(rows, width, per_segment):
    segs = rows // SEG_LEN
    return jnp.broadcast_to(per_segment[:, None, :], (segs, SEG_LEN, width)).reshape(rows, width)


def identity(size):
    row = lax.broadcasted_iota(jnp.int32, (size, size), 0)
    col = lax.broadcasted_iota(jnp.int32, (size, size), 1)
    return (row == col).astype(F32).astype(BF16)


class Sizes:
    def __init__(self, rows, width, ff, with_summary):
        self.rows = rows
        self.width = width
        self.ff = ff
        self.segs = rows // SEG_LEN
        self.top = TILE if with_summary else 0
        self.keys = rows + RIGHT_ROWS + LEFT_ROWS + MEM_ROWS
        self.ext = self.top + self.keys
        self.queries = self.top + rows
        self.right_at = self.top + rows
        self.left_at = self.right_at + RIGHT_ROWS
        self.mem_at = self.left_at + LEFT_ROWS
        self.pairs = width // LANES


class Matrices:
    def __init__(self, width, ff):
        self.qkv = (CHIPS_Z, CHIPS_Y, 3 * width // BLOCKS, width)
        self.out = (CHIPS_Z, CHIPS_Y, width // BLOCKS, width)
        self.up = (CHIPS_Z, CHIPS_Y, ff // BLOCKS, width)
        self.down = (CHIPS_Z, CHIPS_Y, width // BLOCKS, ff)
        self.down_parts = ff // width
        self.attn_rows = self.qkv[2] + self.out[2]
        self.ffn_rows = self.up[2] + self.down_parts * self.down[2]


class Spots:
    def __init__(self, mats):
        high, wide, up, low = mats.qkv[2], mats.out[2], mats.up[2], mats.down[2]
        self.qkv = (0, 0)
        self.out = (0, high)
        self.up = (0, high + wide)
        self.down = [(0, high + wide + up + low * part) for part in range(mats.down_parts)]


def attn_pairs(mats, spots, groups, qkv_ref, out_ref, place_ref):
    if spots is None:
        return [(groups[0], qkv_ref), (groups[1], out_ref)]
    pairs = []
    for k in range(len(groups[0])):
        row = place_ref[2 + 2 * k]
        lane = pl.multiple_of(place_ref[3 + 2 * k], LANES)
        for (group, first), ref, shape in (
            (spots.qkv, qkv_ref, mats.qkv),
            (spots.out, out_ref, mats.out),
        ):
            block = groups[group][k]
            pairs.append(
                (
                    block.at[:, pl.ds(first, shape[2]), :],
                    ref.at[:, row, :, pl.ds(lane, LANES)],
                )
            )
    return pairs


def ffn_pairs(mats, spots, groups, up_ref, down_ref, place_ref):
    if spots is None:
        return [(groups[2], up_ref), (groups[3], down_ref)]
    pairs = []
    for k in range(len(groups[0])):
        row = place_ref[2 + 2 * k]
        lane = pl.multiple_of(place_ref[3 + 2 * k], LANES)
        group, first = spots.up
        block = groups[group][k]
        pairs.append(
            (block.at[:, pl.ds(first, mats.up[2]), :], up_ref.at[:, row, :, pl.ds(lane, LANES)])
        )
        for part, (group, first) in enumerate(spots.down):
            there = pl.multiple_of(
                place_ref[3 + 2 * k] * mats.down_parts + part * LANES, LANES
            )
            block = groups[group][k]
            pairs.append(
                (
                    block.at[:, pl.ds(first, mats.down[2]), :],
                    down_ref.at[:, row, :, pl.ds(there, LANES)],
                )
            )
    return pairs


def start_in(pairs, sems, at):
    copies = [pltpu.make_async_copy(s, d, sems.at[at + i]) for i, (s, d) in enumerate(pairs)]
    for copy in copies:
        copy.start()
    return copies


def start_out(pairs, sems, at):
    copies = [pltpu.make_async_copy(d, s, sems.at[at + i]) for i, (s, d) in enumerate(pairs)]
    for copy in copies:
        copy.start()
    return copies


def in_groups(spots, refs):
    return refs if spots is None else [refs]


def wait_all(copies):
    for copy in copies:
        copy.wait()


def fill_mask(sizes, seqs, starts_ref, place_ref, mask_ref):
    shape = (sizes.queries, sizes.keys)
    row = lax.broadcasted_iota(jnp.int32, shape, 0)
    col = lax.broadcasted_iota(jnp.int32, shape, 1)
    base = place_ref[0]
    total = place_ref[1]
    query = jnp.where(row < sizes.top, row, lax.shift_right_arithmetic(row - sizes.top, 4))
    left_at = sizes.rows + RIGHT_ROWS
    mem_at = left_at + LEFT_ROWS
    spot = jnp.where(col < left_at, col, col - mem_at)
    mem_seg = jnp.where(col < mem_at + sizes.segs, col - mem_at, col - mem_at - 2 * sizes.segs)
    key_seg = jnp.where(col < mem_at, lax.shift_right_arithmetic(spot, 4), mem_seg)
    near = (
        (key_seg == query)
        | ((spot >= query * SEG_LEN - LEFT_LEN) & (spot < query * SEG_LEN))
        | ((key_seg == query + 1) & (spot < query * SEG_LEN + SEG_LEN + RIGHT_LEN))
    )
    recent = (key_seg >= query - MEM_LEN) & (key_seg < query) & (row >= sizes.top)
    allowed = ((col < mem_at) & near) | ((col >= mem_at) & recent)
    key_abs = key_seg + base
    query_abs = query + base
    allowed = allowed & (key_abs >= 0) & (key_abs < total)
    if sizes.top:
        allowed = allowed & ((row < sizes.segs) | (row >= sizes.top))
    for n in range(seqs):
        key_owner = jnp.zeros(shape, jnp.int32)
        query_owner = jnp.zeros(shape, jnp.int32)
        for u in range(starts_ref.shape[1]):
            first = starts_ref[n, u]
            key_owner = key_owner + (key_abs >= first).astype(jnp.int32)
            query_owner = query_owner + (query_abs >= first).astype(jnp.int32)
        mask_ref[n] = jnp.where(allowed & (key_owner == query_owner), 0.0, -1e30)


def half_masks():
    lane = lax.broadcasted_iota(jnp.int32, (1, LANES), 1)
    even = (lane < LANES // 2).astype(F32)
    return even.astype(BF16), (1.0 - even).astype(BF16), lane < LANES // 2


def project(sizes, z_ref, qkv_ref, row_bias_ref, proj_ref):
    step = CHIPS_Z // 2
    for c in range(2):
        block = qkv_ref[pl.ds(c * step, step)].reshape(-1, sizes.width)
        wide = block.shape[0]
        made = nt(z_ref[...], block) + row_bias_ref[:, pl.ds(c * wide, wide)]
        proj_ref[:, pl.ds(c * wide, wide)] = made.astype(BF16)


def attend(sizes, seqs, proj_ref, mask_ref, probs_ref, att_ref):
    even, odd, is_even = half_masks()
    scale = (sizes.width // HEADS) ** (-0.5)
    count = sizes.queries

    def body(p, carry):
        for n in range(seqs):
            lane = pl.multiple_of(p * LANES, LANES)
            query = proj_ref[pl.ds(n * sizes.ext, count), pl.ds(lane, LANES)]
            first = n * sizes.ext + sizes.top
            key = proj_ref[pl.ds(first, sizes.keys), pl.ds(sizes.width + lane, LANES)]
            value = proj_ref[pl.ds(first, sizes.keys), pl.ds(2 * sizes.width + lane, LANES)]
            scores = nt(jnp.concatenate([query * even, query * odd], axis=0), key) * scale
            outs = []
            for half in range(2):
                part = scores[half * count : (half + 1) * count] + mask_ref[n]
                part = jnp.exp(part - jnp.max(part, axis=1, keepdims=True))
                part = (part * (1.0 / jnp.sum(part, axis=1, keepdims=True))).astype(BF16)
                probs_ref[n * sizes.pairs + p, pl.ds(half * count, count), :] = part
                outs.append(nn(part, value))
            att_ref[pl.ds(n * count, count), pl.ds(lane, LANES)] = jnp.where(
                is_even, outs[0], outs[1]
            ).astype(BF16)
        return carry

    lax.fori_loop(0, sizes.pairs, body, 0, unroll=True)


def attend_back(sizes, seqs, proj_ref, probs_ref, go_ref, gproj_ref):
    even, odd, is_even = half_masks()
    scale = (sizes.width // HEADS) ** (-0.5)
    count = sizes.queries
    wide = sizes.width
    for n in range(seqs):
        base = n * sizes.ext
        rest = sizes.ext - count
        gproj_ref[pl.ds(base + count, rest), pl.ds(0, wide)] = jnp.zeros((rest, wide), BF16)
        if sizes.top:
            gproj_ref[pl.ds(base, sizes.top), pl.ds(wide, 2 * wide)] = jnp.zeros(
                (sizes.top, 2 * wide), BF16
            )

    def body(p, carry):
        for n in range(seqs):
            lane = pl.multiple_of(p * LANES, LANES)
            base = n * sizes.ext
            first = base + sizes.top
            query = proj_ref[pl.ds(base, count), pl.ds(lane, LANES)]
            key = proj_ref[pl.ds(first, sizes.keys), pl.ds(wide + lane, LANES)]
            value = proj_ref[pl.ds(first, sizes.keys), pl.ds(2 * wide + lane, LANES)]
            grad = go_ref[pl.ds(n * count, count), pl.ds(lane, LANES)]
            queries = jnp.concatenate([query * even, query * odd], axis=0)
            grads = jnp.concatenate([grad * even, grad * odd], axis=0)
            probs_low = probs_ref[n * sizes.pairs + p]
            grad_values = tn(probs_low, grads)
            probs = probs_low.astype(F32)
            grad_probs = nt(grads, value)
            weighted = grad_probs * probs
            grad_scores = (
                (weighted - probs * jnp.sum(weighted, axis=1, keepdims=True)) * scale
            ).astype(BF16)
            grad_keys = tn(grad_scores, queries)
            grad_query = jnp.where(
                is_even, nn(grad_scores[:count], key), nn(grad_scores[count:], key)
            )
            gproj_ref[pl.ds(base, count), pl.ds(lane, LANES)] = grad_query.astype(BF16)
            gproj_ref[pl.ds(first, sizes.keys), pl.ds(wide + lane, LANES)] = grad_keys.astype(BF16)
            gproj_ref[pl.ds(first, sizes.keys), pl.ds(2 * wide + lane, LANES)] = (
                grad_values.astype(BF16)
            )
        return carry

    lax.fori_loop(0, sizes.pairs, body, 0)


def gelu_both(upward):
    half = 0.5 * (1.0 + lax.erf(upward * ROOT_HALF))
    slope = half + upward * jnp.exp(-0.5 * upward * upward) * INV_ROOT_TWO_PI
    return upward * half, slope


def up_block(up_ref, c, wide):
    step = wide // (up_ref.shape[1] * up_ref.shape[2])
    return up_ref[pl.ds(c * step, step)].reshape(-1, up_ref.shape[3])


def down_block(down_ref, c, wide):
    at = pl.multiple_of(c * wide, wide)
    return down_ref[:, :, :, pl.ds(at, wide)].reshape(-1, wide)


def ffn_back_step(
    sizes, c, wide, grad_low, hidden_low, active, slope, up_ref, down_ref, gup_ref, gdown_ref, vec
):
    at = pl.multiple_of(c * wide, wide)
    up = up_block(up_ref, c, wide)
    down = down_block(down_ref, c, wide)
    grad_active = nn(grad_low, down)
    grad_up_f = grad_active * slope
    grad_up = grad_up_f.astype(BF16)
    gdown_ref[:, :, :, pl.ds(at, wide)] = (
        tn(grad_low, active).astype(BF16).reshape(gdown_ref.shape[:3] + (wide,))
    )
    step = wide // (gup_ref.shape[1] * gup_ref.shape[2])
    gup_ref[pl.ds(c * step, step)] = (
        tn(grad_up, hidden_low).astype(BF16).reshape((step,) + gup_ref.shape[1:])
    )
    vec[pl.ds(8 + c, 1), :] = col_sum(grad_up.astype(F32))
    return nn(grad_up, up)


def attn_back_stage(
    sizes, seqs, gz, grad_mem_ref, att_ref, proj_ref, probs_ref, z_ref, qkv_ref, out_ref,
    gqkv_ref, gout_ref, go_ref, gproj_ref, branch_ref, vec, gh_ref, gmem_ref, back_left_ref,
    back_right_ref, scaled_rows=None,
):
    wide = sizes.width
    count = sizes.queries
    bias_out = col_sum(gz)
    for n in range(seqs):
        if sizes.top:
            mem_grad = grad_mem_ref[pl.ds(n * sizes.segs, sizes.segs), :]
            bias_out = bias_out + col_sum(mem_grad)
            branch_ref[pl.ds(n * count, sizes.top), :] = jnp.concatenate(
                [mem_grad, jnp.zeros((sizes.top - sizes.segs, wide), F32)], axis=0
            ).astype(BF16)
        branch_ref[pl.ds(n * count + sizes.top, sizes.rows), :] = gz[
            n * sizes.rows : (n + 1) * sizes.rows
        ].astype(BF16)
    vec[pl.ds(5, 1), :] = bias_out
    branch = branch_ref[...]
    gout_ref[...] = tn(branch, att_ref[...]).astype(BF16).reshape(gout_ref.shape)
    go_ref[...] = nn(branch, out_ref[...].reshape(-1, wide)).astype(BF16)
    attend_back(sizes, seqs, proj_ref, probs_ref, go_ref, gproj_ref)
    vec[pl.ds(3, 1), :] = col_sum(gproj_ref[:, pl.ds(0, wide)].astype(F32))
    vec[pl.ds(4, 1), :] = col_sum(gproj_ref[:, pl.ds(2 * wide, wide)].astype(F32))
    grad_ext = nn(gproj_ref[...], qkv_ref[...].reshape(-1, wide))
    gain_sum = jnp.zeros((1, wide), F32)
    bias_sum = jnp.zeros((1, wide), F32)
    for n in range(seqs):
        base = n * sizes.ext
        own = grad_ext[base + sizes.top : base + sizes.top + sizes.rows]
        if sizes.top:
            spread = grad_ext[base : base + sizes.segs] * (1.0 / SEG_LEN)
            own = own + segment_spread(sizes.rows, wide, spread)
        gh_ref[pl.ds(n * sizes.rows, sizes.rows), :] = own
        mem = base + sizes.mem_at
        gmem_ref[pl.ds(n * sizes.segs, sizes.segs), :] = grad_ext[mem : mem + sizes.segs]
        left = base + sizes.left_at
        back_left_ref[n] = grad_ext[left : left + BACK_ROWS].astype(BF16)
        right = base + sizes.right_at
        back_right_ref[n] = grad_ext[right : right + RIGHT_ROWS].astype(BF16)
        if scaled_rows is not None:
            grads = (
                own,
                grad_ext[right : right + RIGHT_ROWS],
                grad_ext[left : left + LEFT_ROWS],
            )
            for rows, scaled in zip(grads, scaled_rows(n)):
                gain_sum = gain_sum + col_sum(rows * scaled)
                bias_sum = bias_sum + col_sum(rows)
    if scaled_rows is not None:
        vec[pl.ds(0, 1), :] = gain_sum
        vec[pl.ds(2, 1), :] = bias_sum
    step = CHIPS_Z // 2
    part = gqkv_ref.shape[1] * gqkv_ref.shape[2] * step
    for c in range(2):
        gqkv_ref[pl.ds(c * step, step)] = (
            tn(gproj_ref[:, pl.ds(c * part, part)], z_ref[...])
            .astype(BF16)
            .reshape((step,) + gqkv_ref.shape[1:])
        )


def merge_halo(sizes, n, gh_ref, gmem_ref, from_right_ref, from_left_ref):
    first = n * sizes.rows
    back = from_right_ref[n].astype(F32)
    head = gh_ref[pl.ds(first, RIGHT_ROWS), :] + from_left_ref[n].astype(F32)
    middle = gh_ref[pl.ds(first + RIGHT_ROWS, sizes.rows - RIGHT_ROWS - LEFT_ROWS), :]
    tail = gh_ref[pl.ds(first + sizes.rows - LEFT_ROWS, LEFT_ROWS), :] + back[:LEFT_ROWS]
    mem = gmem_ref[pl.ds(n * sizes.segs, sizes.segs), :] + back[LEFT_ROWS + sizes.segs :]
    return jnp.concatenate([head, middle, tail], axis=0), mem


def pack_kernel(spots, qkv_ref, out_ref, up_ref, down_ref, *packed):
    eye = identity(LANES)
    high, wide, low = qkv_ref.shape[1], out_ref.shape[1], down_ref.shape[1]
    for layer, ref in enumerate(packed):
        up = tn(up_ref[layer], eye).astype(BF16)
        for z in range(ref.shape[0]):
            ref[z, pl.ds(spots.qkv[1], high), :] = qkv_ref[layer]
            ref[z, pl.ds(spots.out[1], wide), :] = out_ref[layer]
            ref[z, pl.ds(spots.up[1], up_ref.shape[2]), :] = up
            for part, (_, first) in enumerate(spots.down):
                ref[z, pl.ds(first, low), :] = down_ref[layer, :, pl.ds(part * LANES, LANES)]


def unpack_kernel(layers, sources_of, small_at, *refs):
    sources, outs = refs[:-7], refs[-7:]
    qkv_ref, out_ref, up_ref, down_ref, gains_ref, biases_ref, ffn_bias_ref = outs
    eye = identity(LANES)
    high, wide, low = qkv_ref.shape[1], out_ref.shape[1], down_ref.shape[1]

    def total(indices, first, rows):
        parts = [
            sources[i][z, pl.ds(first, rows), :] for i in indices for z in range(sources[i].shape[0])
        ]
        value = parts[0].astype(F32)
        for part in parts[1:]:
            value = value + part.astype(F32)
        return value

    for layer, spots in enumerate(layers):
        which = sources_of[layer]
        qkv_ref[layer] = total(which, spots.qkv[1], high)
        out_ref[layer] = total(which, spots.out[1], wide)
        up_ref[layer] = nt(eye, total(which, spots.up[1], up_ref.shape[2]).astype(BF16))
        for part, (_, first) in enumerate(spots.down):
            down_ref[layer, :, pl.ds(part * LANES, LANES)] = total(which, first, low)
    sums = total([small_at[0]], small_at[1], SMALL_ROWS)
    parts = gains_ref.shape[2] // LANES
    for layer in range(gains_ref.shape[0]):
        for part in range(parts):
            lanes = pl.ds(part * LANES, LANES)
            block = sums[(layer * parts + part) * TILE : (layer * parts + part + 1) * TILE]
            gains_ref[layer, :, lanes] = block[0:2]
            for row in range(biases_ref.shape[0]):
                biases_ref[row, pl.ds(layer, 1), lanes] = block[2 + row : 3 + row]
            for row in range(ffn_bias_ref.shape[1] // gains_ref.shape[2]):
                at = row * gains_ref.shape[2] + part * LANES
                ffn_bias_ref[pl.ds(layer, 1), pl.ds(at, LANES)] = block[8 + row : 9 + row]


def near_small_kernel(count, mine_ref, theirs_ref, second_ref, first_ref, out_ref):
    rows = out_ref.shape[1] - SMALL_ROWS

    def total(at, size):
        group = pl.ds(at, size)
        value = mine_ref[0, group, :].astype(F32) + theirs_ref[0, group, :].astype(F32)
        return (
            value + second_ref[0, group, :].astype(F32) + first_ref[group, :].astype(F32)
        ).astype(BF16)

    small = total(count * rows, SMALL_ROWS)
    for z in range(count):
        out_ref[z, pl.ds(0, rows), :] = total(z * rows, rows)
        out_ref[z, pl.ds(rows, SMALL_ROWS), :] = small


def first_layer_kernel(
    sizes, seqs, mats, spots, count_in, place_ref, starts_ref, frames_ref, left_ref, right_ref,
    gains_ref, biases_ref, ffn_bias_ref, row_bias_ref, *refs
):
    groups = in_groups(spots, refs[:count_in])
    (
        z_ref, proj_ref, probs_ref, att_ref, mixed_ref, mem_ref, next_ref, active_ref, slope_ref,
        low_ref, send_right_ref, send_left_ref, qkv_ref, out_ref, up_ref, down_ref, mask_ref,
        hidden_ref, sems,
    ) = refs[count_in:]
    wide = sizes.width
    copies = start_in(attn_pairs(mats, spots, groups, qkv_ref, out_ref, place_ref), sems, 0)
    ffn_copies = start_in(
        ffn_pairs(mats, spots, groups, up_ref, down_ref, place_ref), sems, len(copies)
    )
    gain = gains_ref[0, pl.ds(0, 1), :]
    bias = biases_ref[0, pl.ds(0, 1), :]
    pad = jnp.zeros((TILE - sizes.segs, wide), F32)
    for n in range(seqs):
        own = frames_ref[n].astype(F32)
        before = left_ref[n].astype(F32)
        hidden = norm_forward(own, gain, bias)[0]
        halo = norm_forward(before[before.shape[0] - LEFT_ROWS :], gain, bias)[0]
        after = norm_forward(right_ref[n].astype(F32), gain, bias)[0]
        memory = jnp.concatenate(
            [
                segment_mean(own),
                jnp.zeros((sizes.segs - before.shape[0] // SEG_LEN, wide), F32),
                segment_mean(before),
            ],
            axis=0,
        )
        base = n * sizes.ext
        z_ref[pl.ds(base, sizes.top), :] = jnp.concatenate(
            [segment_mean(hidden), pad], axis=0
        ).astype(BF16)
        z_ref[pl.ds(base + sizes.top, sizes.rows), :] = hidden.astype(BF16)
        z_ref[pl.ds(base + sizes.right_at, RIGHT_ROWS), :] = after.astype(BF16)
        z_ref[pl.ds(base + sizes.left_at, LEFT_ROWS), :] = halo.astype(BF16)
        z_ref[pl.ds(base + sizes.mem_at, MEM_ROWS), :] = memory.astype(BF16)
    fill_mask(sizes, seqs, starts_ref, place_ref, mask_ref)
    wait_all(copies)
    project(sizes, z_ref, qkv_ref, row_bias_ref, proj_ref)
    attend(sizes, seqs, proj_ref, mask_ref, probs_ref, att_ref)
    mixed = nt(att_ref[...], out_ref[...].reshape(-1, wide)) + biases_ref[0, pl.ds(3, 1), :]
    for n in range(seqs):
        base = n * sizes.queries
        mem_ref[pl.ds(n * sizes.segs, sizes.segs), :] = mixed[base : base + sizes.segs]
        mixed_ref[pl.ds(n * sizes.rows, sizes.rows), :] = (
            frames_ref[n].astype(F32) + mixed[base + sizes.top : base + sizes.top + sizes.rows]
        )
    mixed = mixed_ref[...]
    hidden, _, _ = norm_forward(mixed, gains_ref[0, pl.ds(1, 1), :], biases_ref[0, pl.ds(4, 1), :])
    hidden_ref[...] = hidden.astype(BF16)
    next_ref[...] = mixed + biases_ref[0, pl.ds(5, 1), :]
    wait_all(ffn_copies)

    def body(c, carry):
        at_lane = pl.multiple_of(c * wide, wide)
        upward = nt(hidden_ref[...], up_block(up_ref, c, wide))
        upward = upward + ffn_bias_ref[pl.ds(0, 1), pl.ds(at_lane, wide)]
        active, slope = gelu_both(upward)
        active = active.astype(BF16)
        active_ref[:, pl.ds(at_lane, wide)] = active
        slope_ref[:, pl.ds(at_lane, wide)] = slope.astype(BF16)
        next_ref[...] += nt(active, down_block(down_ref, c, wide))
        return carry

    lax.fori_loop(0, sizes.ff // wide, body, 0)
    low, _, _ = norm_forward(
        next_ref[...], gains_ref[1, pl.ds(0, 1), :], biases_ref[1, pl.ds(0, 1), :]
    )
    low = low.astype(BF16)
    low_ref[...] = low
    for n in range(seqs):
        base = n * sizes.rows
        send_right_ref[n, pl.ds(0, LEFT_ROWS), :] = low[
            base + sizes.rows - LEFT_ROWS : base + sizes.rows
        ]
        send_right_ref[n, pl.ds(LEFT_ROWS, MEM_ROWS), :] = jnp.concatenate(
            [
                mem_ref[pl.ds(n * sizes.segs, sizes.segs), :],
                jnp.zeros((MEM_ROWS - sizes.segs, wide), F32),
            ],
            axis=0,
        ).astype(BF16)
        send_left_ref[n] = low[base : base + RIGHT_ROWS]


def last_layer_kernel(
    sizes, seqs, mats, spots, count_in, count_out, place_ref, starts_ref, low_ref, left_ref,
    right_ref, mem_ref, inputs_ref, out_grad_ref, gains_ref, biases_ref, ffn_bias_ref,
    row_bias_ref, *refs
):
    groups = in_groups(spots, refs[:count_in])
    (encoded_ref, gz_ref, gh_ref, gmem_ref, back_left_ref, back_right_ref, vec) = refs[
        count_in : count_in + 7
    ]
    hbm_out = refs[count_in + 7 : count_in + 7 + count_out]
    (
        qkv_ref, out_ref, up_ref, down_ref, gqkv_ref, gout_ref, gup_ref, gdown_ref, mask_ref,
        z_ref, proj_ref, probs_ref, att_ref, hidden_ref, go_ref, gproj_ref, branch_ref,
        grad_low_ref, grad_hidden_ref, sems,
    ) = refs[count_in + 7 + count_out :]
    outs_to = hbm_out
    if spots is not None:
        rows = mats.attn_rows + mats.ffn_rows
        outs_to = [
            [
                ref.at[hop2, :, pl.ds(hop1 * rows, rows), :]
                for ref in hbm_out
                for hop2 in range(2)
                for hop1 in range(2)
            ]
        ]
    wide = sizes.width
    attn_copies = start_in(attn_pairs(mats, spots, groups, qkv_ref, out_ref, place_ref), sems, 0)
    ffn_copies = start_in(
        ffn_pairs(mats, spots, groups, up_ref, down_ref, place_ref), sems, len(attn_copies)
    )
    vec[...] = jnp.zeros_like(vec)
    for n in range(seqs):
        base = n * sizes.ext
        z_ref[pl.ds(base, sizes.rows), :] = low_ref[pl.ds(n * sizes.rows, sizes.rows), :]
        z_ref[pl.ds(base + sizes.right_at, RIGHT_ROWS), :] = right_ref[n]
        z_ref[pl.ds(base + sizes.left_at, LEFT_ROWS), :] = left_ref[n, pl.ds(0, LEFT_ROWS), :]
        memory = jnp.concatenate(
            [
                mem_ref[pl.ds(n * sizes.segs, sizes.segs), :],
                left_ref[n, pl.ds(LEFT_ROWS, MEM_ROWS), :].astype(F32)[: sizes.segs],
            ],
            axis=0,
        )
        z_ref[pl.ds(base + sizes.mem_at, MEM_ROWS), :] = memory.astype(BF16)
        grad_low_ref[pl.ds(n * sizes.rows, sizes.rows), :] = out_grad_ref[n]
    fill_mask(sizes, seqs, starts_ref, place_ref, mask_ref)
    wait_all(attn_copies)
    project(sizes, z_ref, qkv_ref, row_bias_ref, proj_ref)
    attend(sizes, seqs, proj_ref, mask_ref, probs_ref, att_ref)
    mixed = (
        inputs_ref[...]
        + nt(att_ref[...], out_ref[...].reshape(-1, wide))
        + biases_ref[1, pl.ds(3, 1), :]
    )
    gain = gains_ref[1, pl.ds(1, 1), :]
    hidden, scaled, inverse = norm_forward(mixed, gain, biases_ref[1, pl.ds(4, 1), :])
    hidden_ref[...] = hidden.astype(BF16)
    for n in range(seqs):
        encoded_ref[n] = mixed[n * sizes.rows : (n + 1) * sizes.rows] + biases_ref[
            1, pl.ds(5, 1), :
        ]
    grad_hidden_ref[...] = jnp.zeros_like(grad_hidden_ref)
    wait_all(ffn_copies)

    def body(c, carry):
        at_lane = pl.multiple_of(c * wide, wide)
        upward = nt(hidden_ref[...], up_block(up_ref, c, wide))
        upward = upward + ffn_bias_ref[pl.ds(1, 1), pl.ds(at_lane, wide)]
        active, slope = gelu_both(upward)
        active = active.astype(BF16)
        made = nt(active, down_block(down_ref, c, wide))
        for n in range(seqs):
            encoded_ref[n] += made[n * sizes.rows : (n + 1) * sizes.rows]
        grad_hidden_ref[...] += ffn_back_step(
            sizes, c, wide, grad_low_ref[...], hidden_ref[...], active, slope, up_ref, down_ref,
            gup_ref, gdown_ref, vec,
        )
        return carry

    lax.fori_loop(0, sizes.ff // wide, body, 0)
    out_at = len(attn_copies) + len(ffn_copies)
    outs = start_out(
        ffn_pairs(mats, spots, outs_to, gup_ref, gdown_ref, place_ref), sems, out_at
    )
    grad = grad_low_ref[...].astype(F32)
    grad_hidden = grad_hidden_ref[...]
    vec[pl.ds(1, 1), :] = col_sum(grad_hidden * scaled)
    vec[pl.ds(6, 1), :] = col_sum(grad_hidden)
    vec[pl.ds(7, 1), :] = col_sum(grad)
    gz = grad + norm_backward(grad_hidden, scaled, inverse, gain)
    gz_ref[...] = gz
    attn_back_stage(
        sizes, seqs, gz, None, att_ref, proj_ref, probs_ref, z_ref, qkv_ref, out_ref, gqkv_ref,
        gout_ref, go_ref, gproj_ref, branch_ref, vec, gh_ref, gmem_ref, back_left_ref,
        back_right_ref,
    )
    outs = outs + start_out(
        attn_pairs(mats, spots, outs_to, gqkv_ref, gout_ref, place_ref),
        sems,
        out_at + len(outs),
    )
    wait_all(outs)


def first_back_kernel(
    last, sizes, seqs, mats, spots, count_in, count_out, place_ref, inputs_ref, gz_in_ref,
    gh_in_ref, gmem_in_ref, from_right_ref, from_left_ref, mixed_ref, active_ref, slope_ref,
    att_ref, probs_ref, proj_ref, z_ref, frames_ref, left_ref, right_ref, gains_ref, biases_ref,
    last_vec, *refs
):
    groups = in_groups(spots, refs[:count_in])
    gz_ref, gh_ref, gmem_ref, back_left_ref, back_right_ref, upper_vec, vec = refs[
        count_in : count_in + 7
    ]
    refs = refs[count_in + 7 :]
    hbm_out = refs[:count_out]
    (
        qkv_ref, out_ref, up_ref, down_ref, gqkv_ref, gout_ref, gup_ref, gdown_ref, hidden_ref,
        grad_low_ref, grad_ref, grad_hidden_ref, grad_mem_ref, go_ref, gproj_ref, branch_ref,
        small_ref, sems,
    ) = refs[count_out:]
    wide = sizes.width
    small = []
    outs_to = hbm_out
    if spots is not None:
        classes = count_in // 2
        rows = mats.attn_rows + mats.ffn_rows
        end = CHIPS_Z * rows
        each = [ref.at[k] for ref in hbm_out for k in range(classes)]
        small = [ref.at[pl.ds(end, SMALL_ROWS), :] for ref in each]
        outs_to = [[ref.at[pl.ds(0, end), :].reshape(CHIPS_Z, rows, LANES) for ref in each]]
    ffn_copies = start_in(ffn_pairs(mats, spots, groups, up_ref, down_ref, place_ref), sems, 0)
    attn_copies = start_in(
        attn_pairs(mats, spots, groups, qkv_ref, out_ref, place_ref), sems, len(ffn_copies)
    )
    vec[...] = jnp.zeros_like(vec)
    upper_vec[...] = jnp.zeros_like(upper_vec)
    gain = gains_ref[1, pl.ds(0, 1), :]
    gain_sum = jnp.zeros((1, wide), F32)
    bias_sum = jnp.zeros((1, wide), F32)
    for n in range(seqs):
        rows = pl.ds(n * sizes.rows, sizes.rows)
        _, scaled, inverse = norm_forward(
            inputs_ref[rows, :], gain, biases_ref[1, pl.ds(0, 1), :]
        )
        total, mem = merge_halo(last, n, gh_in_ref, gmem_in_ref, from_right_ref, from_left_ref)
        gain_sum = gain_sum + col_sum(total * scaled)
        bias_sum = bias_sum + col_sum(total)
        grad = gz_in_ref[rows, :] + norm_backward(total, scaled, inverse, gain)
        grad_ref[rows, :] = grad
        grad_low_ref[rows, :] = grad.astype(BF16)
        grad_mem_ref[pl.ds(n * sizes.segs, sizes.segs), :] = mem
    upper_vec[pl.ds(0, 1), :] = gain_sum
    upper_vec[pl.ds(2, 1), :] = bias_sum
    gain = gains_ref[0, pl.ds(1, 1), :]
    hidden, scaled, inverse = norm_forward(
        mixed_ref[...], gain, biases_ref[0, pl.ds(4, 1), :]
    )
    hidden_ref[...] = hidden.astype(BF16)
    grad_hidden_ref[...] = jnp.zeros_like(grad_hidden_ref)
    wait_all(ffn_copies)

    def body(c, carry):
        at_lane = pl.multiple_of(c * wide, wide)
        grad_hidden_ref[...] += ffn_back_step(
            sizes, c, wide, grad_low_ref[...], hidden_ref[...],
            active_ref[:, pl.ds(at_lane, wide)], slope_ref[:, pl.ds(at_lane, wide)].astype(F32),
            up_ref, down_ref, gup_ref, gdown_ref, vec,
        )
        return carry

    lax.fori_loop(0, sizes.ff // wide, body, 0)
    out_at = len(ffn_copies) + len(attn_copies)
    outs = start_out(
        ffn_pairs(mats, spots, outs_to, gup_ref, gdown_ref, place_ref), sems, out_at
    )
    grad_hidden = grad_hidden_ref[...]
    grad = grad_ref[...]
    vec[pl.ds(1, 1), :] = col_sum(grad_hidden * scaled)
    vec[pl.ds(6, 1), :] = col_sum(grad_hidden)
    vec[pl.ds(7, 1), :] = col_sum(grad)
    gz = grad + norm_backward(grad_hidden, scaled, inverse, gain)
    gz_ref[...] = gz

    def scaled_rows(n):
        before = left_ref[n, pl.ds(left_ref.shape[1] - LEFT_ROWS, LEFT_ROWS), :]
        parts = (frames_ref[n], right_ref[n], before)
        first_gain = gains_ref[0, pl.ds(0, 1), :]
        first_bias = biases_ref[0, pl.ds(0, 1), :]
        return [norm_forward(part.astype(F32), first_gain, first_bias)[1] for part in parts]

    wait_all(attn_copies)
    attn_back_stage(
        sizes, seqs, gz, grad_mem_ref, att_ref, proj_ref, probs_ref, z_ref, qkv_ref, out_ref,
        gqkv_ref, gout_ref, go_ref, gproj_ref, branch_ref, vec, gh_ref, gmem_ref, back_left_ref,
        back_right_ref, scaled_rows,
    )
    outs = outs + start_out(
        attn_pairs(mats, spots, outs_to, gqkv_ref, gout_ref, place_ref),
        sems,
        out_at + len(outs),
    )
    parts = sizes.width // LANES
    for layer, total in enumerate((vec[...], last_vec[...] + upper_vec[...])):
        for part in range(parts):
            small_ref[pl.ds((layer * parts + part) * TILE, TILE), :] = total[
                :, part * LANES : (part + 1) * LANES
            ].astype(BF16)
    outs = outs + start_out([(ref, small_ref) for ref in small], sems, out_at + len(outs))
    wait_all(outs)


def frames_grad_kernel(
    sizes, seqs, frames_ref, gz_ref, gh_ref, gmem_ref, from_right_ref, from_left_ref, gains_ref,
    biases_ref, grad_ref
):
    gain = gains_ref[0, pl.ds(0, 1), :]
    for n in range(seqs):
        _, scaled, inverse = norm_forward(
            frames_ref[n].astype(F32), gain, biases_ref[0, pl.ds(0, 1), :]
        )
        total, mem = merge_halo(sizes, n, gh_ref, gmem_ref, from_right_ref, from_left_ref)
        grad_ref[n] = (
            gz_ref[pl.ds(n * sizes.rows, sizes.rows), :]
            + norm_backward(total, scaled, inverse, gain)
            + segment_spread(sizes.rows, sizes.width, mem * (1.0 / SEG_LEN))
        )


def shifted(value, axis, by):
    size = lax.axis_size(axis)
    pairs = [(i, i + by) for i in range(size) if 0 <= i + by < size]
    return lax.ppermute(value, axis, pairs)


def permuted(value, move):
    reps = lax.axis_size("rep")
    pairs = []
    for flat in range(lax.axis_size("seg") * reps):
        seg, rep = divmod(flat, reps)
        z, y, x, core = move(seg // CHIPS_Y, seg % CHIPS_Y, rep // 2, rep % 2)
        pairs.append((flat, (z * CHIPS_Y + y) * reps + 2 * x + core))
    return lax.ppermute(value, ("seg", "rep"), pairs)


def across_first(value):
    return permuted(value, lambda z, y, x, c: (z, y, x ^ 1, c) if c == 0 else (z, y ^ 1, x, c))


def across_second(value):
    return permuted(value, lambda z, y, x, c: (z, y ^ 1, x, c) if c == 0 else (z, y, x ^ 1, c))


def other_core(value):
    return permuted(value, lambda z, y, x, c: (z, y, x, c ^ 1))


def after(value, *others):
    return lax.optimization_barrier((value,) + others)[0]


def swap_z(blocks):
    groups = [
        [z * CHIPS_Y + y for z in range(CHIPS_Z)] for y in range(CHIPS_Y)
    ]
    return lax.all_to_all(blocks, "seg", 0, 0, axis_index_groups=groups, tiled=True)


def gather_sides(here):
    return [here, across_first(here), across_second(here)]


def both_cores(blocks):
    return blocks + [other_core(block) for block in blocks]


def summed(*parts):
    total = parts[0].astype(F32)
    for part in parts[1:]:
        total = total + part.astype(F32)
    return total.astype(BF16)


def first_rows(rows):
    return pl.BlockSpec((1, rows, LANES), lambda i: (0, 0, 0))


def sum_everywhere(value):
    count = lax.axis_size("seg") * lax.axis_size("rep")
    bit = 1
    while bit < count:
        value = value + lax.ppermute(value, ("seg", "rep"), [(i, i ^ bit) for i in range(count)])
        bit *= 2
    return value


def vmem_spec():
    return pl.BlockSpec(memory_space=pltpu.VMEM)


def smem_spec():
    return pl.BlockSpec(memory_space=pltpu.SMEM)


def hbm_spec():
    return pl.BlockSpec(memory_space=pl.ANY)


def call(body, in_specs, out_shapes, out_specs, scratch, args, flops=0, moved=0, grid=()):
    return pl.pallas_call(
        body,
        grid=grid,
        in_specs=in_specs,
        out_shape=tuple(jax.ShapeDtypeStruct(shape, kind) for shape, kind in out_shapes),
        out_specs=tuple(out_specs),
        scratch_shapes=scratch,
        compiler_params=pltpu.CompilerParams(vmem_limit_bytes=VMEM_BYTES),
        cost_estimate=pl.CostEstimate(flops=flops, bytes_accessed=moved, transcendentals=0),
    )(*args)


def on_device(
    frames,
    utt_segments,
    out_grad,
    qkv_weight,
    out_weight,
    ffn_in_weight,
    ffn_out_weight,
    norm_gains,
    biases,
    ffn_bias,
):
    micros, groups, rows, width = frames.shape
    seqs = micros * groups
    ff = ffn_bias.shape[1]
    reps = lax.axis_size("rep")
    seg_count = lax.axis_size("seg")
    mats = Matrices(width, ff)
    by_blocks = width // reps == LANES and reps == 4 and seg_count == BLOCKS
    first = Sizes(rows, width, ff, True)
    last = Sizes(rows, width, ff, False)
    own = seqs * rows
    mem_own = seqs * first.segs

    seg_at = lax.axis_index("seg")
    seg_base = seg_at * first.segs
    rep_at = lax.axis_index("rep")
    place = [seg_base, jnp.int32(first.segs * seg_count)]
    y_at, x_at, core_at = seg_at % CHIPS_Y, rep_at // 2, rep_at % 2
    for other in range(2):
        core = lax.bitwise_xor(core_at, other)
        for hop2 in range(2):
            for hop1 in range(2):
                x_hop = jnp.where(core == 0, hop1, hop2)
                y_hop = jnp.where(core == 0, hop2, hop1)
                place.append(lax.bitwise_xor(y_at, y_hop))
                place.append((lax.bitwise_xor(x_at, x_hop) * 2 + core) * LANES)
    place = jnp.stack([jnp.asarray(entry, jnp.int32) for entry in place])
    lengths = utt_segments.reshape(seqs, utt_segments.shape[2])
    starts = (jnp.cumsum(lengths, axis=1) - lengths).astype(jnp.int32)
    zero_bias = jnp.zeros((width,), F32)
    row_bias = jnp.stack(
        [jnp.concatenate([biases[l, 1], zero_bias, biases[l, 2]]) for l in range(LAYERS)]
    ).reshape(LAYERS, 1, 3 * width)

    frames_own = frames.reshape(seqs, rows, width)
    grads_own = out_grad.reshape(seqs, rows, width)
    far = MEM_LEN * SEG_LEN
    frames_left = shifted(frames_own[:, rows - far :], "seg", 1)
    frames_right = shifted(frames_own[:, :RIGHT_ROWS], "seg", -1)

    attn_rows, ffn_rows = mats.attn_rows, mats.ffn_rows
    if by_blocks:
        qkv_t, out_t, down_t = (
            jnp.swapaxes(member, 1, 2) for member in (qkv_weight, out_weight, ffn_out_weight)
        )
        all_rows = attn_rows + ffn_rows
        spots = Spots(mats)
        shards = call(
            lambda *refs: pack_kernel(spots, *refs),
            [vmem_spec()] * 4,
            [((CHIPS_Z, all_rows, LANES), BF16)] * LAYERS,
            [vmem_spec()] * LAYERS,
            [],
            (qkv_t, out_t, ffn_in_weight, down_t),
        )
        sides0 = gather_sides(after(swap_z(shards[0]), frames_left, frames_right))
        place, starts, row_bias, sent = lax.optimization_barrier(
            (place, starts, row_bias, after(shards[1], sides0[0]))
        )
        sides1 = gather_sides(swap_z(sent))
        first_all = both_cores(sides0 + [across_second(after(sides0[1], sides1[0]))])
        classes = len(first_all) // 2
        grad_outs0 = [((classes, CHIPS_Z * all_rows + SMALL_ROWS, LANES), BF16)] * 2
        grad_outs1 = [((2, CHIPS_Z, 2 * all_rows, LANES), BF16)] * 2
        copies_in = len(first_all) * (3 + mats.down_parts)
    else:
        whole = []
        for member, shape in zip(
            (qkv_weight, out_weight, ffn_in_weight, ffn_out_weight),
            (mats.qkv, mats.out, mats.up, mats.down),
        ):
            member = lax.all_gather(member, "rep", axis=1, tiled=True)
            member = lax.all_gather(member, "seg", axis=2, tiled=True)
            whole.append(jnp.swapaxes(member, 1, 2).reshape((LAYERS,) + shape))
        first_all = [member[0] for member in whole]
        last_all = [member[1] for member in whole]
        spots = None
        grad_outs0 = grad_outs1 = [
            (shape, BF16) for shape in (mats.qkv, mats.out, mats.up, mats.down)
        ]
        copies_in = 4
    dma = pltpu.SemaphoreType.DMA

    matrices = [pltpu.VMEM(shape, BF16) for shape in (mats.qkv, mats.out, mats.up, mats.down)]

    (
        z0, proj0, probs0, att0, mixed0, mem1, x1, active0, slope0, low1, send_right, send_left,
    ) = call(
        lambda *refs: first_layer_kernel(
            first, seqs, mats, spots, len(first_all), *refs
        ),
        [smem_spec()] * 2 + [vmem_spec()] * 7 + [hbm_spec()] * len(first_all),
        [
            ((seqs * first.ext, width), BF16),
            ((seqs * first.ext, 3 * width), BF16),
            ((seqs * first.pairs, 2 * first.queries, first.keys), BF16),
            ((seqs * first.queries, width), BF16),
            ((own, width), F32),
            ((mem_own, width), F32),
            ((own, width), F32),
            ((own, ff), BF16),
            ((own, ff), BF16),
            ((own, width), BF16),
            ((seqs, BACK_ROWS, width), BF16),
            ((seqs, RIGHT_ROWS, width), BF16),
        ],
        [vmem_spec()] * 12,
        matrices
        + [
            pltpu.VMEM((seqs, first.queries, first.keys), F32),
            pltpu.VMEM((own, width), BF16),
            dma((copies_in,)),
        ],
        (place, starts, frames_own, frames_left, frames_right, norm_gains, biases, ffn_bias,
         row_bias[0]) + tuple(first_all),
        flops=24 * own * (4 * width * width + 2 * width * ff) // 2,
        moved=2 * (4 * width * width + 2 * width * ff),
    )
    left1 = shifted(send_right, "seg", 1)
    right1 = shifted(send_left, "seg", -1)
    if by_blocks:
        last_side = across_second(after(sides1[1], sides1[2], low1))
        last_all = both_cores(sides1 + [last_side])
        last_all[-1] = other_core(after(last_side, left1, right1))

    vec_shape = (TILE, width)
    outs = call(
        lambda *refs: last_layer_kernel(
            last, seqs, mats, spots, len(last_all), len(grad_outs1), *refs
        ),
        [smem_spec()] * 2 + [vmem_spec()] * 10 + [hbm_spec()] * len(last_all),
        [
            ((seqs, rows, width), F32),
            ((own, width), F32),
            ((own, width), F32),
            ((mem_own, width), F32),
            ((seqs, BACK_ROWS, width), BF16),
            ((seqs, RIGHT_ROWS, width), BF16),
            (vec_shape, F32),
        ]
        + grad_outs1,
        [vmem_spec()] * 7 + [hbm_spec()] * len(grad_outs1),
        matrices
        + matrices
        + [
            pltpu.VMEM((seqs, last.queries, last.keys), F32),
            pltpu.VMEM((seqs * last.ext, width), BF16),
            pltpu.VMEM((seqs * last.ext, 3 * width), BF16),
            pltpu.VMEM((seqs * last.pairs, 2 * last.queries, last.keys), BF16),
            pltpu.VMEM((seqs * last.queries, width), BF16),
            pltpu.VMEM((own, width), BF16),
            pltpu.VMEM((seqs * last.queries, width), BF16),
            pltpu.VMEM((seqs * last.ext, 3 * width), BF16),
            pltpu.VMEM((seqs * last.queries, width), BF16),
            pltpu.VMEM((own, width), BF16),
            pltpu.VMEM((own, width), F32),
            dma((2 * copies_in,)),
        ],
        (place, starts, low1, left1, right1, mem1, x1, grads_own, norm_gains, biases, ffn_bias,
         row_bias[1]) + tuple(last_all),
        flops=30 * own * (4 * width * width + 2 * width * ff),
        moved=4 * (4 * width * width + 2 * width * ff),
    )
    encoded, gz1, gh1, gmem1, back_left1, back_right1, vec1 = outs[:7]
    grad_blocks1 = outs[7:]
    from_right1 = shifted(back_left1, "seg", -1)
    from_left1 = shifted(back_right1, "seg", 1)

    gh1_tied = gh1
    if by_blocks:
        mine1, theirs1 = grad_blocks1[0], other_core(grad_blocks1[1])
        far1 = summed(mine1[1], theirs1[1])
        gh1_tied = after(gh1, far1)
    gz0, gh0, gmem0, back_left0, back_right0, upper_vec, vec0, *grad_blocks0 = call(
        lambda *refs: first_back_kernel(
            last, first, seqs, mats, spots, len(first_all), len(grad_outs0), *refs
        ),
        [smem_spec()] + [vmem_spec()] * 19 + [hbm_spec()] * len(first_all),
        [
            ((own, width), F32),
            ((own, width), F32),
            ((mem_own, width), F32),
            ((seqs, BACK_ROWS, width), BF16),
            ((seqs, RIGHT_ROWS, width), BF16),
            (vec_shape, F32),
            (vec_shape, F32),
        ]
        + grad_outs0,
        [vmem_spec()] * 7 + [hbm_spec()] * len(grad_outs0),
        matrices
        + matrices
        + [
            pltpu.VMEM((own, width), BF16),
            pltpu.VMEM((own, width), BF16),
            pltpu.VMEM((own, width), F32),
            pltpu.VMEM((own, width), F32),
            pltpu.VMEM((mem_own, width), F32),
            pltpu.VMEM((seqs * first.queries, width), BF16),
            pltpu.VMEM((seqs * first.ext, 3 * width), BF16),
            pltpu.VMEM((seqs * first.queries, width), BF16),
            pltpu.VMEM((SMALL_ROWS, LANES), BF16),
            dma((2 * copies_in + 8,)),
        ],
        (place, x1, gz1, gh1_tied, gmem1, from_right1, from_left1, mixed0, active0, slope0, att0,
         probs0, proj0, z0, frames_own, frames_left, frames_right, norm_gains, biases, vec1)
        + tuple(first_all),
        flops=28 * own * (4 * width * width + 2 * width * ff),
        moved=4 * (4 * width * width + 2 * width * ff),
    )
    from_right0 = shifted(back_left0, "seg", -1)
    from_left0 = shifted(back_right0, "seg", 1)
    gz0_last = gz0
    if by_blocks:
        second1 = across_second(far1)
        mine0, theirs0 = grad_blocks0[0], other_core(after(grad_blocks0[1], second1))
        far0 = summed(mine0[2:], theirs0[2:])
        second0 = across_second(far0)
        both1 = summed(mine1[0], theirs1[0], after(second1, far0))
        lines1 = swap_z(both1)
        mid0 = summed(mine0[1], theirs0[1], after(second0, both1)[1])
        first0 = across_first(mid0)
        near0 = call(
            lambda *refs: near_small_kernel(CHIPS_Z, *refs),
            [first_rows(mine0.shape[1])] * 3 + [vmem_spec()],
            [((CHIPS_Z, all_rows + SMALL_ROWS, LANES), BF16)],
            [vmem_spec()],
            [],
            [mine0, theirs0, second0, first0],
            grid=(1,),
        )[0]
        first_parts = swap_z(near0)
        gz0_last, lines1 = lax.optimization_barrier((after(gz0, near0), lines1))
        cross1 = jnp.sum(lines1[:, all_rows:].astype(F32), axis=0, keepdims=True).astype(BF16)
        first1 = across_first(cross1)
    frames_grad = call(
        lambda *refs: frames_grad_kernel(first, seqs, *refs),
        [vmem_spec()] * 8,
        [((seqs, rows, width), F32)],
        [vmem_spec()],
        [],
        (frames_own, gz0_last, gh0, gmem0, from_right0, from_left0, norm_gains, biases),
    )[0]

    if by_blocks:
        shapes = [member.shape for member in (qkv_t, out_t, ffn_in_weight, down_t)]
        shapes += [norm_gains.shape, (biases.shape[1], LAYERS, width), ffn_bias.shape]
        reduced = call(
            lambda *refs: unpack_kernel([spots, spots], [[0], [1, 2]], (0, all_rows), *refs),
            [
                pl.BlockSpec((high, rows_in, LANES), lambda i: (0, 0, 0))
                for high, rows_in in (
                    (CHIPS_Z, all_rows + SMALL_ROWS),
                    (CHIPS_Z, all_rows),
                    (1, all_rows),
                )
            ],
            [(shape, F32) for shape in shapes],
            [vmem_spec()] * len(shapes),
            [],
            [after(first_parts, frames_grad), lines1, first1],
            grid=(1,),
        )
        small = reduced[4], jnp.swapaxes(reduced[5], 0, 1), reduced[6]
        reduced = [
            jnp.swapaxes(reduced[0], 1, 2),
            jnp.swapaxes(reduced[1], 1, 2),
            reduced[2],
            jnp.swapaxes(reduced[3], 1, 2),
        ]
    else:
        reduced = []
        for member0, member1 in zip(grad_blocks0, grad_blocks1):
            both = jnp.stack([member0, member1]).reshape(LAYERS, -1, member0.shape[3])
            both = jnp.swapaxes(both, 1, 2)
            both = lax.psum_scatter(both, "seg", scatter_dimension=2, tiled=True)
            both = lax.psum_scatter(both, "rep", scatter_dimension=1, tiled=True)
            reduced.append(both.astype(F32))
        small = sum_everywhere(jnp.stack([vec0, vec1 + upper_vec]))
        small = small[:, 0:2], small[:, 2:8], small[:, 8:12].reshape(ffn_bias.shape)

    return (
        encoded.reshape(frames.shape),
        frames_grad.reshape(frames.shape),
        reduced[0],
        reduced[1],
        reduced[2],
        reduced[3],
        small[0],
        small[1],
        small[2],
    )


def solution(mesh):
    in_specs = (
        P(None, "rep", "seg", None),
        P(None, "rep", None),
        P(None, "rep", "seg", None),
        P(None, "rep", "seg"),
        P(None, "rep", "seg"),
        P(None, "rep", "seg"),
        P(None, "rep", "seg"),
        P(),
        P(),
        P(),
    )
    out_specs = (
        P(None, "rep", "seg", None),
        P(None, "rep", "seg", None),
        P(None, "rep", "seg"),
        P(None, "rep", "seg"),
        P(None, "rep", "seg"),
        P(None, "rep", "seg"),
        P(),
        P(),
        P(),
    )
    return jax.shard_map(
        on_device, mesh=mesh, in_specs=in_specs, out_specs=out_specs, check_vma=False
    )
```

```python
import jax
import jax.numpy as jnp
from jax import lax
from jax.experimental import pallas as pl
from jax.experimental.pallas import tpu as pltpu
from jax.sharding import PartitionSpec as P

HEADS = 8
SEG_LEN = 16
LEFT_LEN = 30
RIGHT_LEN = 4
MEM_LEN = 4
LAYERS = 2

EPS = 1e-05
ROOT_HALF = 0.7071067811865476
INV_ROOT_TWO_PI = 0.3989422804014327

LANES = 128
TILE = 16
RIGHT_ROWS = 16
LEFT_ROWS = 32
MEM_ROWS = 16
BACK_ROWS = LEFT_ROWS + MEM_ROWS
CHIPS_Z = 4
CHIPS_Y = 2
BLOCKS = CHIPS_Z * CHIPS_Y
SMALL_ROWS = 128
VMEM_BYTES = 56 * 1024 * 1024

BF16 = jnp.bfloat16
F32 = jnp.float32


def nn(a, b):
    return lax.dot_general(a, b, (((1,), (0,)), ((), ())), preferred_element_type=F32)


def nt(a, b):
    return lax.dot_general(a, b, (((1,), (1,)), ((), ())), preferred_element_type=F32)


def tn(a, b):
    return lax.dot_general(a, b, (((0,), (0,)), ((), ())), preferred_element_type=F32)


def col_sum(value):
    return jnp.sum(value, axis=0, keepdims=True)


def norm_forward(inputs, gain, bias):
    center = inputs - jnp.mean(inputs, axis=1, keepdims=True)
    inverse = lax.rsqrt(jnp.mean(center * center, axis=1, keepdims=True) + EPS)
    scaled = center * inverse
    return scaled * gain + bias, scaled, inverse


def norm_backward(grad_in, scaled, inverse, gain):
    grad_scaled = grad_in * gain
    return inverse * (
        grad_scaled
        - jnp.mean(grad_scaled, axis=1, keepdims=True)
        - scaled * jnp.mean(grad_scaled * scaled, axis=1, keepdims=True)
    )


def segment_mean(inputs):
    rows, width = inputs.shape
    return jnp.mean(inputs.reshape(rows // SEG_LEN, SEG_LEN, width), axis=1)


def segment_spread(rows, width, per_segment):
    segs = rows // SEG_LEN
    return jnp.broadcast_to(per_segment[:, None, :], (segs, SEG_LEN, width)).reshape(rows, width)


def identity(size):
    row = lax.broadcasted_iota(jnp.int32, (size, size), 0)
    col = lax.broadcasted_iota(jnp.int32, (size, size), 1)
    return (row == col).astype(F32).astype(BF16)


class Sizes:
    def __init__(self, rows, width, ff, with_summary):
        self.rows = rows
        self.width = width
        self.ff = ff
        self.segs = rows // SEG_LEN
        self.top = TILE if with_summary else 0
        self.keys = rows + RIGHT_ROWS + LEFT_ROWS + MEM_ROWS
        self.ext = self.top + self.keys
        self.queries = self.top + rows
        self.right_at = self.top + rows
        self.left_at = self.right_at + RIGHT_ROWS
        self.mem_at = self.left_at + LEFT_ROWS
        self.pairs = width // LANES


class Matrices:
    def __init__(self, width, ff):
        self.qkv = (CHIPS_Z, CHIPS_Y, 3 * width // BLOCKS, width)
        self.out = (CHIPS_Z, CHIPS_Y, width // BLOCKS, width)
        self.up = (CHIPS_Z, CHIPS_Y, ff // BLOCKS, width)
        self.down = (CHIPS_Z, CHIPS_Y, width // BLOCKS, ff)
        self.down_parts = ff // width
        self.attn_rows = self.qkv[2] + self.out[2]
        self.ffn_rows = self.up[2] + self.down_parts * self.down[2]


class Spots:
    def __init__(self, mats):
        high, wide, up, low = mats.qkv[2], mats.out[2], mats.up[2], mats.down[2]
        self.qkv = (0, 0)
        self.out = (0, high)
        self.up = (0, high + wide)
        self.down = [(0, high + wide + up + low * part) for part in range(mats.down_parts)]


def attn_pairs(mats, spots, groups, qkv_ref, out_ref, place_ref):
    if spots is None:
        return [(groups[0], qkv_ref), (groups[1], out_ref)]
    pairs = []
    for k in range(len(groups[0])):
        row = place_ref[2 + 2 * k]
        lane = pl.multiple_of(place_ref[3 + 2 * k], LANES)
        for (group, first), ref, shape in (
            (spots.qkv, qkv_ref, mats.qkv),
            (spots.out, out_ref, mats.out),
        ):
            block = groups[group][k]
            pairs.append(
                (
                    block.at[:, pl.ds(first, shape[2]), :],
                    ref.at[:, row, :, pl.ds(lane, LANES)],
                )
            )
    return pairs


def ffn_pairs(mats, spots, groups, up_ref, down_ref, place_ref):
    if spots is None:
        return [(groups[2], up_ref), (groups[3], down_ref)]
    pairs = []
    for k in range(len(groups[0])):
        row = place_ref[2 + 2 * k]
        lane = pl.multiple_of(place_ref[3 + 2 * k], LANES)
        group, first = spots.up
        block = groups[group][k]
        pairs.append(
            (block.at[:, pl.ds(first, mats.up[2]), :], up_ref.at[:, row, :, pl.ds(lane, LANES)])
        )
        for part, (group, first) in enumerate(spots.down):
            there = pl.multiple_of(
                place_ref[3 + 2 * k] * mats.down_parts + part * LANES, LANES
            )
            block = groups[group][k]
            pairs.append(
                (
                    block.at[:, pl.ds(first, mats.down[2]), :],
                    down_ref.at[:, row, :, pl.ds(there, LANES)],
                )
            )
    return pairs


def start_in(pairs, sems, at):
    copies = [pltpu.make_async_copy(s, d, sems.at[at + i]) for i, (s, d) in enumerate(pairs)]
    for copy in copies:
        copy.start()
    return copies


def start_out(pairs, sems, at):
    copies = [pltpu.make_async_copy(d, s, sems.at[at + i]) for i, (s, d) in enumerate(pairs)]
    for copy in copies:
        copy.start()
    return copies


def in_groups(spots, refs):
    return refs if spots is None else [refs]


def wait_all(copies):
    for copy in copies:
        copy.wait()


def fill_mask(sizes, seqs, starts_ref, place_ref, mask_ref):
    shape = (sizes.queries, sizes.keys)
    row = lax.broadcasted_iota(jnp.int32, shape, 0)
    col = lax.broadcasted_iota(jnp.int32, shape, 1)
    base = place_ref[0]
    total = place_ref[1]
    query = jnp.where(row < sizes.top, row, lax.shift_right_arithmetic(row - sizes.top, 4))
    left_at = sizes.rows + RIGHT_ROWS
    mem_at = left_at + LEFT_ROWS
    spot = jnp.where(col < left_at, col, col - mem_at)
    mem_seg = jnp.where(col < mem_at + sizes.segs, col - mem_at, col - mem_at - 2 * sizes.segs)
    key_seg = jnp.where(col < mem_at, lax.shift_right_arithmetic(spot, 4), mem_seg)
    near = (
        (key_seg == query)
        | ((spot >= query * SEG_LEN - LEFT_LEN) & (spot < query * SEG_LEN))
        | ((key_seg == query + 1) & (spot < query * SEG_LEN + SEG_LEN + RIGHT_LEN))
    )
    recent = (key_seg >= query - MEM_LEN) & (key_seg < query) & (row >= sizes.top)
    allowed = ((col < mem_at) & near) | ((col >= mem_at) & recent)
    key_abs = key_seg + base
    query_abs = query + base
    allowed = allowed & (key_abs >= 0) & (key_abs < total)
    if sizes.top:
        allowed = allowed & ((row < sizes.segs) | (row >= sizes.top))
    for n in range(seqs):
        key_owner = jnp.zeros(shape, jnp.int32)
        query_owner = jnp.zeros(shape, jnp.int32)
        for u in range(starts_ref.shape[1]):
            first = starts_ref[n, u]
            key_owner = key_owner + (key_abs >= first).astype(jnp.int32)
            query_owner = query_owner + (query_abs >= first).astype(jnp.int32)
        mask_ref[n] = jnp.where(allowed & (key_owner == query_owner), 0.0, -1e30)


def half_masks():
    lane = lax.broadcasted_iota(jnp.int32, (1, LANES), 1)
    even = (lane < LANES // 2).astype(F32)
    return even.astype(BF16), (1.0 - even).astype(BF16), lane < LANES // 2


def project(sizes, z_ref, qkv_ref, row_bias_ref, proj_ref):
    step = CHIPS_Z // 2
    for c in range(2):
        block = qkv_ref[pl.ds(c * step, step)].reshape(-1, sizes.width)
        wide = block.shape[0]
        made = nt(z_ref[...], block) + row_bias_ref[:, pl.ds(c * wide, wide)]
        proj_ref[:, pl.ds(c * wide, wide)] = made.astype(BF16)


def attend(sizes, seqs, proj_ref, mask_ref, probs_ref, att_ref):
    even, odd, is_even = half_masks()
    scale = (sizes.width // HEADS) ** (-0.5)
    count = sizes.queries

    def body(p, carry):
        for n in range(seqs):
            lane = pl.multiple_of(p * LANES, LANES)
            query = proj_ref[pl.ds(n * sizes.ext, count), pl.ds(lane, LANES)]
            first = n * sizes.ext + sizes.top
            key = proj_ref[pl.ds(first, sizes.keys), pl.ds(sizes.width + lane, LANES)]
            value = proj_ref[pl.ds(first, sizes.keys), pl.ds(2 * sizes.width + lane, LANES)]
            scores = nt(jnp.concatenate([query * even, query * odd], axis=0), key) * scale
            outs = []
            for half in range(2):
                part = scores[half * count : (half + 1) * count] + mask_ref[n]
                part = jnp.exp(part - jnp.max(part, axis=1, keepdims=True))
                part = (part * (1.0 / jnp.sum(part, axis=1, keepdims=True))).astype(BF16)
                probs_ref[n * sizes.pairs + p, pl.ds(half * count, count), :] = part
                outs.append(nn(part, value))
            att_ref[pl.ds(n * count, count), pl.ds(lane, LANES)] = jnp.where(
                is_even, outs[0], outs[1]
            ).astype(BF16)
        return carry

    lax.fori_loop(0, sizes.pairs, body, 0, unroll=True)


def attend_back(sizes, seqs, proj_ref, probs_ref, go_ref, gproj_ref):
    even, odd, is_even = half_masks()
    scale = (sizes.width // HEADS) ** (-0.5)
    count = sizes.queries
    wide = sizes.width
    for n in range(seqs):
        base = n * sizes.ext
        rest = sizes.ext - count
        gproj_ref[pl.ds(base + count, rest), pl.ds(0, wide)] = jnp.zeros((rest, wide), BF16)
        if sizes.top:
            gproj_ref[pl.ds(base, sizes.top), pl.ds(wide, 2 * wide)] = jnp.zeros(
                (sizes.top, 2 * wide), BF16
            )

    def body(p, carry):
        for n in range(seqs):
            lane = pl.multiple_of(p * LANES, LANES)
            base = n * sizes.ext
            first = base + sizes.top
            query = proj_ref[pl.ds(base, count), pl.ds(lane, LANES)]
            key = proj_ref[pl.ds(first, sizes.keys), pl.ds(wide + lane, LANES)]
            value = proj_ref[pl.ds(first, sizes.keys), pl.ds(2 * wide + lane, LANES)]
            grad = go_ref[pl.ds(n * count, count), pl.ds(lane, LANES)]
            queries = jnp.concatenate([query * even, query * odd], axis=0)
            grads = jnp.concatenate([grad * even, grad * odd], axis=0)
            probs_low = probs_ref[n * sizes.pairs + p]
            grad_values = tn(probs_low, grads)
            probs = probs_low.astype(F32)
            grad_probs = nt(grads, value)
            weighted = grad_probs * probs
            grad_scores = (
                (weighted - probs * jnp.sum(weighted, axis=1, keepdims=True)) * scale
            ).astype(BF16)
            grad_keys = tn(grad_scores, queries)
            grad_query = jnp.where(
                is_even, nn(grad_scores[:count], key), nn(grad_scores[count:], key)
            )
            gproj_ref[pl.ds(base, count), pl.ds(lane, LANES)] = grad_query.astype(BF16)
            gproj_ref[pl.ds(first, sizes.keys), pl.ds(wide + lane, LANES)] = grad_keys.astype(BF16)
            gproj_ref[pl.ds(first, sizes.keys), pl.ds(2 * wide + lane, LANES)] = (
                grad_values.astype(BF16)
            )
        return carry

    lax.fori_loop(0, sizes.pairs, body, 0)


def gelu_both(upward):
    half = 0.5 * (1.0 + lax.erf(upward * ROOT_HALF))
    slope = half + upward * jnp.exp(-0.5 * upward * upward) * INV_ROOT_TWO_PI
    return upward * half, slope


def up_block(up_ref, c, wide):
    step = wide // (up_ref.shape[1] * up_ref.shape[2])
    return up_ref[pl.ds(c * step, step)].reshape(-1, up_ref.shape[3])


def down_block(down_ref, c, wide):
    at = pl.multiple_of(c * wide, wide)
    return down_ref[:, :, :, pl.ds(at, wide)].reshape(-1, wide)


def ffn_back_step(
    sizes, c, wide, grad_low, hidden_low, active, slope, up_ref, down_ref, gup_ref, gdown_ref, vec
):
    at = pl.multiple_of(c * wide, wide)
    up = up_block(up_ref, c, wide)
    down = down_block(down_ref, c, wide)
    grad_active = nn(grad_low, down)
    grad_up_f = grad_active * slope
    grad_up = grad_up_f.astype(BF16)
    gdown_ref[:, :, :, pl.ds(at, wide)] = (
        tn(grad_low, active).astype(BF16).reshape(gdown_ref.shape[:3] + (wide,))
    )
    step = wide // (gup_ref.shape[1] * gup_ref.shape[2])
    gup_ref[pl.ds(c * step, step)] = (
        tn(grad_up, hidden_low).astype(BF16).reshape((step,) + gup_ref.shape[1:])
    )
    vec[pl.ds(8 + c, 1), :] = col_sum(grad_up.astype(F32))
    return nn(grad_up, up)


def attn_back_stage(
    sizes, seqs, gz, grad_mem_ref, att_ref, proj_ref, probs_ref, z_ref, qkv_ref, out_ref,
    gqkv_ref, gout_ref, go_ref, gproj_ref, branch_ref, vec, gh_ref, gmem_ref, back_left_ref,
    back_right_ref, scaled_rows=None,
):
    wide = sizes.width
    count = sizes.queries
    bias_out = col_sum(gz)
    for n in range(seqs):
        if sizes.top:
            mem_grad = grad_mem_ref[pl.ds(n * sizes.segs, sizes.segs), :]
            bias_out = bias_out + col_sum(mem_grad)
            branch_ref[pl.ds(n * count, sizes.top), :] = jnp.concatenate(
                [mem_grad, jnp.zeros((sizes.top - sizes.segs, wide), F32)], axis=0
            ).astype(BF16)
        branch_ref[pl.ds(n * count + sizes.top, sizes.rows), :] = gz[
            n * sizes.rows : (n + 1) * sizes.rows
        ].astype(BF16)
    vec[pl.ds(5, 1), :] = bias_out
    branch = branch_ref[...]
    gout_ref[...] = tn(branch, att_ref[...]).astype(BF16).reshape(gout_ref.shape)
    go_ref[...] = nn(branch, out_ref[...].reshape(-1, wide)).astype(BF16)
    attend_back(sizes, seqs, proj_ref, probs_ref, go_ref, gproj_ref)
    vec[pl.ds(3, 1), :] = col_sum(gproj_ref[:, pl.ds(0, wide)].astype(F32))
    vec[pl.ds(4, 1), :] = col_sum(gproj_ref[:, pl.ds(2 * wide, wide)].astype(F32))
    grad_ext = nn(gproj_ref[...], qkv_ref[...].reshape(-1, wide))
    gain_sum = jnp.zeros((1, wide), F32)
    bias_sum = jnp.zeros((1, wide), F32)
    for n in range(seqs):
        base = n * sizes.ext
        own = grad_ext[base + sizes.top : base + sizes.top + sizes.rows]
        if sizes.top:
            spread = grad_ext[base : base + sizes.segs] * (1.0 / SEG_LEN)
            own = own + segment_spread(sizes.rows, wide, spread)
        gh_ref[pl.ds(n * sizes.rows, sizes.rows), :] = own
        mem = base + sizes.mem_at
        gmem_ref[pl.ds(n * sizes.segs, sizes.segs), :] = grad_ext[mem : mem + sizes.segs]
        left = base + sizes.left_at
        back_left_ref[n] = grad_ext[left : left + BACK_ROWS].astype(BF16)
        right = base + sizes.right_at
        back_right_ref[n] = grad_ext[right : right + RIGHT_ROWS].astype(BF16)
        if scaled_rows is not None:
            grads = (
                own,
                grad_ext[right : right + RIGHT_ROWS],
                grad_ext[left : left + LEFT_ROWS],
            )
            for rows, scaled in zip(grads, scaled_rows(n)):
                gain_sum = gain_sum + col_sum(rows * scaled)
                bias_sum = bias_sum + col_sum(rows)
    if scaled_rows is not None:
        vec[pl.ds(0, 1), :] = gain_sum
        vec[pl.ds(2, 1), :] = bias_sum
    step = CHIPS_Z // 2
    part = gqkv_ref.shape[1] * gqkv_ref.shape[2] * step
    for c in range(2):
        gqkv_ref[pl.ds(c * step, step)] = (
            tn(gproj_ref[:, pl.ds(c * part, part)], z_ref[...])
            .astype(BF16)
            .reshape((step,) + gqkv_ref.shape[1:])
        )


def merge_halo(sizes, n, gh_ref, gmem_ref, from_right_ref, from_left_ref):
    first = n * sizes.rows
    back = from_right_ref[n].astype(F32)
    head = gh_ref[pl.ds(first, RIGHT_ROWS), :] + from_left_ref[n].astype(F32)
    middle = gh_ref[pl.ds(first + RIGHT_ROWS, sizes.rows - RIGHT_ROWS - LEFT_ROWS), :]
    tail = gh_ref[pl.ds(first + sizes.rows - LEFT_ROWS, LEFT_ROWS), :] + back[:LEFT_ROWS]
    mem = gmem_ref[pl.ds(n * sizes.segs, sizes.segs), :] + back[LEFT_ROWS + sizes.segs :]
    return jnp.concatenate([head, middle, tail], axis=0), mem


def pack_kernel(spots, qkv_ref, out_ref, up_ref, down_ref, *packed):
    eye = identity(LANES)
    high, wide, low = qkv_ref.shape[1], out_ref.shape[1], down_ref.shape[1]
    for layer, ref in enumerate(packed):
        up = tn(up_ref[layer], eye).astype(BF16)
        for z in range(ref.shape[0]):
            ref[z, pl.ds(spots.qkv[1], high), :] = qkv_ref[layer]
            ref[z, pl.ds(spots.out[1], wide), :] = out_ref[layer]
            ref[z, pl.ds(spots.up[1], up_ref.shape[2]), :] = up
            for part, (_, first) in enumerate(spots.down):
                ref[z, pl.ds(first, low), :] = down_ref[layer, :, pl.ds(part * LANES, LANES)]


def unpack_kernel(layers, sources_of, small_at, *refs):
    sources, outs = refs[:-7], refs[-7:]
    qkv_ref, out_ref, up_ref, down_ref, gains_ref, biases_ref, ffn_bias_ref = outs
    eye = identity(LANES)
    high, wide, low = qkv_ref.shape[1], out_ref.shape[1], down_ref.shape[1]

    def total(indices, first, rows):
        parts = [
            sources[i][z, pl.ds(first, rows), :] for i in indices for z in range(sources[i].shape[0])
        ]
        value = parts[0].astype(F32)
        for part in parts[1:]:
            value = value + part.astype(F32)
        return value

    for layer, spots in enumerate(layers):
        which = sources_of[layer]
        qkv_ref[layer] = total(which, spots.qkv[1], high)
        out_ref[layer] = total(which, spots.out[1], wide)
        up_ref[layer] = nt(eye, total(which, spots.up[1], up_ref.shape[2]).astype(BF16))
        for part, (_, first) in enumerate(spots.down):
            down_ref[layer, :, pl.ds(part * LANES, LANES)] = total(which, first, low)
    sums = total([small_at[0]], small_at[1], SMALL_ROWS)
    parts = gains_ref.shape[2] // LANES
    for layer in range(gains_ref.shape[0]):
        for part in range(parts):
            lanes = pl.ds(part * LANES, LANES)
            block = sums[(layer * parts + part) * TILE : (layer * parts + part + 1) * TILE]
            gains_ref[layer, :, lanes] = block[0:2]
            for row in range(biases_ref.shape[0]):
                biases_ref[row, pl.ds(layer, 1), lanes] = block[2 + row : 3 + row]
            for row in range(ffn_bias_ref.shape[1] // gains_ref.shape[2]):
                at = row * gains_ref.shape[2] + part * LANES
                ffn_bias_ref[pl.ds(layer, 1), pl.ds(at, LANES)] = block[8 + row : 9 + row]


def near_small_kernel(count, mine_ref, theirs_ref, second_ref, first_ref, out_ref):
    rows = out_ref.shape[1] - SMALL_ROWS

    def total(at, size):
        group = pl.ds(at, size)
        value = mine_ref[group, :].astype(F32) + theirs_ref[group, :].astype(F32)
        return (
            value + second_ref[group, :].astype(F32) + first_ref[group, :].astype(F32)
        ).astype(BF16)

    small = total(count * rows, SMALL_ROWS)
    for z in range(count):
        out_ref[z, pl.ds(0, rows), :] = total(z * rows, rows)
        out_ref[z, pl.ds(rows, SMALL_ROWS), :] = small


def first_layer_kernel(
    sizes, seqs, mats, spots, count_in, place_ref, starts_ref, frames_ref, left_ref, right_ref,
    gains_ref, biases_ref, ffn_bias_ref, row_bias_ref, *refs
):
    groups = in_groups(spots, refs[:count_in])
    (
        z_ref, proj_ref, probs_ref, att_ref, mixed_ref, mem_ref, next_ref, active_ref, slope_ref,
        low_ref, send_right_ref, send_left_ref, qkv_ref, out_ref, up_ref, down_ref, mask_ref,
        hidden_ref, sems,
    ) = refs[count_in:]
    wide = sizes.width
    copies = start_in(attn_pairs(mats, spots, groups, qkv_ref, out_ref, place_ref), sems, 0)
    ffn_copies = start_in(
        ffn_pairs(mats, spots, groups, up_ref, down_ref, place_ref), sems, len(copies)
    )
    gain = gains_ref[0, pl.ds(0, 1), :]
    bias = biases_ref[0, pl.ds(0, 1), :]
    pad = jnp.zeros((TILE - sizes.segs, wide), F32)
    for n in range(seqs):
        own = frames_ref[n].astype(F32)
        before = left_ref[n].astype(F32)
        hidden = norm_forward(own, gain, bias)[0]
        halo = norm_forward(before[before.shape[0] - LEFT_ROWS :], gain, bias)[0]
        after = norm_forward(right_ref[n].astype(F32), gain, bias)[0]
        memory = jnp.concatenate(
            [
                segment_mean(own),
                jnp.zeros((sizes.segs - before.shape[0] // SEG_LEN, wide), F32),
                segment_mean(before),
            ],
            axis=0,
        )
        base = n * sizes.ext
        z_ref[pl.ds(base, sizes.top), :] = jnp.concatenate(
            [segment_mean(hidden), pad], axis=0
        ).astype(BF16)
        z_ref[pl.ds(base + sizes.top, sizes.rows), :] = hidden.astype(BF16)
        z_ref[pl.ds(base + sizes.right_at, RIGHT_ROWS), :] = after.astype(BF16)
        z_ref[pl.ds(base + sizes.left_at, LEFT_ROWS), :] = halo.astype(BF16)
        z_ref[pl.ds(base + sizes.mem_at, MEM_ROWS), :] = memory.astype(BF16)
    fill_mask(sizes, seqs, starts_ref, place_ref, mask_ref)
    wait_all(copies)
    project(sizes, z_ref, qkv_ref, row_bias_ref, proj_ref)
    attend(sizes, seqs, proj_ref, mask_ref, probs_ref, att_ref)
    mixed = nt(att_ref[...], out_ref[...].reshape(-1, wide)) + biases_ref[3, pl.ds(0, 1), :]
    for n in range(seqs):
        base = n * sizes.queries
        mem_ref[pl.ds(n * sizes.segs, sizes.segs), :] = mixed[base : base + sizes.segs]
        mixed_ref[pl.ds(n * sizes.rows, sizes.rows), :] = (
            frames_ref[n].astype(F32) + mixed[base + sizes.top : base + sizes.top + sizes.rows]
        )
    mixed = mixed_ref[...]
    hidden, _, _ = norm_forward(mixed, gains_ref[0, pl.ds(1, 1), :], biases_ref[4, pl.ds(0, 1), :])
    hidden_ref[...] = hidden.astype(BF16)
    next_ref[...] = mixed + biases_ref[5, pl.ds(0, 1), :]
    wait_all(ffn_copies)

    def body(c, carry):
        at_lane = pl.multiple_of(c * wide, wide)
        upward = nt(hidden_ref[...], up_block(up_ref, c, wide))
        upward = upward + ffn_bias_ref[pl.ds(0, 1), pl.ds(at_lane, wide)]
        active, slope = gelu_both(upward)
        active = active.astype(BF16)
        active_ref[:, pl.ds(at_lane, wide)] = active
        slope_ref[:, pl.ds(at_lane, wide)] = slope.astype(BF16)
        next_ref[...] += nt(active, down_block(down_ref, c, wide))
        return carry

    lax.fori_loop(0, sizes.ff // wide, body, 0)
    low, _, _ = norm_forward(
        next_ref[...], gains_ref[1, pl.ds(0, 1), :], biases_ref[0, pl.ds(1, 1), :]
    )
    low = low.astype(BF16)
    low_ref[...] = low
    for n in range(seqs):
        base = n * sizes.rows
        send_right_ref[n, pl.ds(0, LEFT_ROWS), :] = low[
            base + sizes.rows - LEFT_ROWS : base + sizes.rows
        ]
        send_right_ref[n, pl.ds(LEFT_ROWS, MEM_ROWS), :] = jnp.concatenate(
            [
                mem_ref[pl.ds(n * sizes.segs, sizes.segs), :],
                jnp.zeros((MEM_ROWS - sizes.segs, wide), F32),
            ],
            axis=0,
        ).astype(BF16)
        send_left_ref[n] = low[base : base + RIGHT_ROWS]


def last_layer_kernel(
    sizes, seqs, mats, spots, count_in, count_out, place_ref, starts_ref, low_ref, left_ref,
    right_ref, mem_ref, inputs_ref, out_grad_ref, gains_ref, biases_ref, ffn_bias_ref,
    row_bias_ref, *refs
):
    groups = in_groups(spots, refs[:count_in])
    (encoded_ref, gz_ref, gh_ref, gmem_ref, back_left_ref, back_right_ref, vec) = refs[
        count_in : count_in + 7
    ]
    hbm_out = refs[count_in + 7 : count_in + 7 + count_out]
    (
        qkv_ref, out_ref, up_ref, down_ref, gqkv_ref, gout_ref, gup_ref, gdown_ref, mask_ref,
        z_ref, proj_ref, probs_ref, att_ref, hidden_ref, go_ref, gproj_ref, branch_ref,
        grad_low_ref, grad_hidden_ref, sems,
    ) = refs[count_in + 7 + count_out :]
    outs_to = hbm_out
    if spots is not None:
        rows = mats.attn_rows + mats.ffn_rows
        outs_to = [
            [
                ref.at[hop2, :, pl.ds(hop1 * rows, rows), :]
                for ref in hbm_out
                for hop2 in range(2)
                for hop1 in range(2)
            ]
        ]
    wide = sizes.width
    attn_copies = start_in(attn_pairs(mats, spots, groups, qkv_ref, out_ref, place_ref), sems, 0)
    ffn_copies = start_in(
        ffn_pairs(mats, spots, groups, up_ref, down_ref, place_ref), sems, len(attn_copies)
    )
    vec[...] = jnp.zeros_like(vec)
    for n in range(seqs):
        base = n * sizes.ext
        z_ref[pl.ds(base, sizes.rows), :] = low_ref[pl.ds(n * sizes.rows, sizes.rows), :]
        z_ref[pl.ds(base + sizes.right_at, RIGHT_ROWS), :] = right_ref[n]
        z_ref[pl.ds(base + sizes.left_at, LEFT_ROWS), :] = left_ref[n, pl.ds(0, LEFT_ROWS), :]
        memory = jnp.concatenate(
            [
                mem_ref[pl.ds(n * sizes.segs, sizes.segs), :],
                left_ref[n, pl.ds(LEFT_ROWS, MEM_ROWS), :].astype(F32)[: sizes.segs],
            ],
            axis=0,
        )
        z_ref[pl.ds(base + sizes.mem_at, MEM_ROWS), :] = memory.astype(BF16)
        grad_low_ref[pl.ds(n * sizes.rows, sizes.rows), :] = out_grad_ref[n]
    fill_mask(sizes, seqs, starts_ref, place_ref, mask_ref)
    wait_all(attn_copies)
    project(sizes, z_ref, qkv_ref, row_bias_ref, proj_ref)
    attend(sizes, seqs, proj_ref, mask_ref, probs_ref, att_ref)
    mixed = (
        inputs_ref[...]
        + nt(att_ref[...], out_ref[...].reshape(-1, wide))
        + biases_ref[3, pl.ds(1, 1), :]
    )
    gain = gains_ref[1, pl.ds(1, 1), :]
    hidden, scaled, inverse = norm_forward(mixed, gain, biases_ref[4, pl.ds(1, 1), :])
    hidden_ref[...] = hidden.astype(BF16)
    for n in range(seqs):
        encoded_ref[n] = mixed[n * sizes.rows : (n + 1) * sizes.rows] + biases_ref[5, pl.ds(1, 1), :]
    grad_hidden_ref[...] = jnp.zeros_like(grad_hidden_ref)
    wait_all(ffn_copies)

    def body(c, carry):
        at_lane = pl.multiple_of(c * wide, wide)
        upward = nt(hidden_ref[...], up_block(up_ref, c, wide))
        upward = upward + ffn_bias_ref[pl.ds(1, 1), pl.ds(at_lane, wide)]
        active, slope = gelu_both(upward)
        active = active.astype(BF16)
        made = nt(active, down_block(down_ref, c, wide))
        for n in range(seqs):
            encoded_ref[n] += made[n * sizes.rows : (n + 1) * sizes.rows]
        grad_hidden_ref[...] += ffn_back_step(
            sizes, c, wide, grad_low_ref[...], hidden_ref[...], active, slope, up_ref, down_ref,
            gup_ref, gdown_ref, vec,
        )
        return carry

    lax.fori_loop(0, sizes.ff // wide, body, 0)
    out_at = len(attn_copies) + len(ffn_copies)
    outs = start_out(
        ffn_pairs(mats, spots, outs_to, gup_ref, gdown_ref, place_ref), sems, out_at
    )
    grad = grad_low_ref[...].astype(F32)
    grad_hidden = grad_hidden_ref[...]
    vec[pl.ds(1, 1), :] = col_sum(grad_hidden * scaled)
    vec[pl.ds(6, 1), :] = col_sum(grad_hidden)
    vec[pl.ds(7, 1), :] = col_sum(grad)
    gz = grad + norm_backward(grad_hidden, scaled, inverse, gain)
    gz_ref[...] = gz
    attn_back_stage(
        sizes, seqs, gz, None, att_ref, proj_ref, probs_ref, z_ref, qkv_ref, out_ref, gqkv_ref,
        gout_ref, go_ref, gproj_ref, branch_ref, vec, gh_ref, gmem_ref, back_left_ref,
        back_right_ref,
    )
    outs = outs + start_out(
        attn_pairs(mats, spots, outs_to, gqkv_ref, gout_ref, place_ref),
        sems,
        out_at + len(outs),
    )
    wait_all(outs)


def first_back_kernel(
    last, sizes, seqs, mats, spots, count_in, count_out, place_ref, inputs_ref, gz_in_ref,
    gh_in_ref, gmem_in_ref, from_right_ref, from_left_ref, mixed_ref, active_ref, slope_ref,
    att_ref, probs_ref, proj_ref, z_ref, frames_ref, left_ref, right_ref, gains_ref, biases_ref,
    last_vec, *refs
):
    groups = in_groups(spots, refs[:count_in])
    gz_ref, gh_ref, gmem_ref, back_left_ref, back_right_ref, upper_vec, vec = refs[
        count_in : count_in + 7
    ]
    refs = refs[count_in + 7 :]
    hbm_out = refs[:count_out]
    (
        qkv_ref, out_ref, up_ref, down_ref, gqkv_ref, gout_ref, gup_ref, gdown_ref, hidden_ref,
        grad_low_ref, grad_ref, grad_hidden_ref, grad_mem_ref, go_ref, gproj_ref, branch_ref,
        small_ref, sems,
    ) = refs[count_out:]
    wide = sizes.width
    small = []
    outs_to = hbm_out
    if spots is not None:
        rows = mats.attn_rows + mats.ffn_rows
        end = CHIPS_Z * rows
        each = [
            ref.at[hop2, hop1] for ref in hbm_out for hop2 in range(2) for hop1 in range(2)
        ]
        small = [ref.at[pl.ds(end, SMALL_ROWS), :] for ref in each]
        outs_to = [[ref.at[pl.ds(0, end), :].reshape(CHIPS_Z, rows, LANES) for ref in each]]
    ffn_copies = start_in(ffn_pairs(mats, spots, groups, up_ref, down_ref, place_ref), sems, 0)
    attn_copies = start_in(
        attn_pairs(mats, spots, groups, qkv_ref, out_ref, place_ref), sems, len(ffn_copies)
    )
    vec[...] = jnp.zeros_like(vec)
    upper_vec[...] = jnp.zeros_like(upper_vec)
    gain = gains_ref[1, pl.ds(0, 1), :]
    gain_sum = jnp.zeros((1, wide), F32)
    bias_sum = jnp.zeros((1, wide), F32)
    for n in range(seqs):
        rows = pl.ds(n * sizes.rows, sizes.rows)
        _, scaled, inverse = norm_forward(
            inputs_ref[rows, :], gain, biases_ref[0, pl.ds(1, 1), :]
        )
        total, mem = merge_halo(last, n, gh_in_ref, gmem_in_ref, from_right_ref, from_left_ref)
        gain_sum = gain_sum + col_sum(total * scaled)
        bias_sum = bias_sum + col_sum(total)
        grad = gz_in_ref[rows, :] + norm_backward(total, scaled, inverse, gain)
        grad_ref[rows, :] = grad
        grad_low_ref[rows, :] = grad.astype(BF16)
        grad_mem_ref[pl.ds(n * sizes.segs, sizes.segs), :] = mem
    upper_vec[pl.ds(0, 1), :] = gain_sum
    upper_vec[pl.ds(2, 1), :] = bias_sum
    gain = gains_ref[0, pl.ds(1, 1), :]
    hidden, scaled, inverse = norm_forward(
        mixed_ref[...], gain, biases_ref[4, pl.ds(0, 1), :]
    )
    hidden_ref[...] = hidden.astype(BF16)
    grad_hidden_ref[...] = jnp.zeros_like(grad_hidden_ref)
    wait_all(ffn_copies)

    def body(c, carry):
        at_lane = pl.multiple_of(c * wide, wide)
        grad_hidden_ref[...] += ffn_back_step(
            sizes, c, wide, grad_low_ref[...], hidden_ref[...],
            active_ref[:, pl.ds(at_lane, wide)], slope_ref[:, pl.ds(at_lane, wide)].astype(F32),
            up_ref, down_ref, gup_ref, gdown_ref, vec,
        )
        return carry

    lax.fori_loop(0, sizes.ff // wide, body, 0)
    out_at = len(ffn_copies) + len(attn_copies)
    outs = start_out(
        ffn_pairs(mats, spots, outs_to, gup_ref, gdown_ref, place_ref), sems, out_at
    )
    grad_hidden = grad_hidden_ref[...]
    grad = grad_ref[...]
    vec[pl.ds(1, 1), :] = col_sum(grad_hidden * scaled)
    vec[pl.ds(6, 1), :] = col_sum(grad_hidden)
    vec[pl.ds(7, 1), :] = col_sum(grad)
    gz = grad + norm_backward(grad_hidden, scaled, inverse, gain)
    gz_ref[...] = gz

    def scaled_rows(n):
        before = left_ref[n, pl.ds(left_ref.shape[1] - LEFT_ROWS, LEFT_ROWS), :]
        parts = (frames_ref[n], right_ref[n], before)
        first_gain = gains_ref[0, pl.ds(0, 1), :]
        first_bias = biases_ref[0, pl.ds(0, 1), :]
        return [norm_forward(part.astype(F32), first_gain, first_bias)[1] for part in parts]

    wait_all(attn_copies)
    attn_back_stage(
        sizes, seqs, gz, grad_mem_ref, att_ref, proj_ref, probs_ref, z_ref, qkv_ref, out_ref,
        gqkv_ref, gout_ref, go_ref, gproj_ref, branch_ref, vec, gh_ref, gmem_ref, back_left_ref,
        back_right_ref, scaled_rows,
    )
    outs = outs + start_out(
        attn_pairs(mats, spots, outs_to, gqkv_ref, gout_ref, place_ref),
        sems,
        out_at + len(outs),
    )
    parts = sizes.width // LANES
    for layer, total in enumerate((vec[...], last_vec[...] + upper_vec[...])):
        for part in range(parts):
            small_ref[pl.ds((layer * parts + part) * TILE, TILE), :] = total[
                :, part * LANES : (part + 1) * LANES
            ].astype(BF16)
    outs = outs + start_out([(ref, small_ref) for ref in small], sems, out_at + len(outs))
    wait_all(outs)


def frames_grad_kernel(
    sizes, seqs, frames_ref, gz_ref, gh_ref, gmem_ref, from_right_ref, from_left_ref, gains_ref,
    biases_ref, grad_ref
):
    gain = gains_ref[0, pl.ds(0, 1), :]
    for n in range(seqs):
        _, scaled, inverse = norm_forward(
            frames_ref[n].astype(F32), gain, biases_ref[0, pl.ds(0, 1), :]
        )
        total, mem = merge_halo(sizes, n, gh_ref, gmem_ref, from_right_ref, from_left_ref)
        grad_ref[n] = (
            gz_ref[pl.ds(n * sizes.rows, sizes.rows), :]
            + norm_backward(total, scaled, inverse, gain)
            + segment_spread(sizes.rows, sizes.width, mem * (1.0 / SEG_LEN))
        )


def shifted(value, axis, by):
    size = lax.axis_size(axis)
    pairs = [(i, i + by) for i in range(size) if 0 <= i + by < size]
    return lax.ppermute(value, axis, pairs)


def permuted(value, move):
    reps = lax.axis_size("rep")
    pairs = []
    for flat in range(lax.axis_size("seg") * reps):
        seg, rep = divmod(flat, reps)
        z, y, x, core = move(seg // CHIPS_Y, seg % CHIPS_Y, rep // 2, rep % 2)
        pairs.append((flat, (z * CHIPS_Y + y) * reps + 2 * x + core))
    return lax.ppermute(value, ("seg", "rep"), pairs)


def across_first(value):
    return permuted(value, lambda z, y, x, c: (z, y, x ^ 1, c) if c == 0 else (z, y ^ 1, x, c))


def across_second(value):
    return permuted(value, lambda z, y, x, c: (z, y ^ 1, x, c) if c == 0 else (z, y, x ^ 1, c))


def other_core(value):
    return permuted(value, lambda z, y, x, c: (z, y, x, c ^ 1))


def after(value, *others):
    return lax.optimization_barrier((value,) + others)[0]


def swap_z(blocks):
    groups = [
        [z * CHIPS_Y + y for z in range(CHIPS_Z)] for y in range(CHIPS_Y)
    ]
    return lax.all_to_all(blocks, "seg", 0, 0, axis_index_groups=groups, tiled=True)


def gather_sides(here):
    return [here, across_first(here), across_second(here)]


def both_cores(blocks):
    return blocks + [other_core(block) for block in blocks]


def summed(*parts):
    total = parts[0].astype(F32)
    for part in parts[1:]:
        total = total + part.astype(F32)
    return total.astype(BF16)


def first_rows(array):
    lead = array.ndim - 2
    shape = (None,) * lead + tuple(array.shape[-2:])
    return pl.BlockSpec(shape, lambda i: (0,) * array.ndim)


def sum_everywhere(value):
    count = lax.axis_size("seg") * lax.axis_size("rep")
    bit = 1
    while bit < count:
        value = value + lax.ppermute(value, ("seg", "rep"), [(i, i ^ bit) for i in range(count)])
        bit *= 2
    return value


def vmem_spec():
    return pl.BlockSpec(memory_space=pltpu.VMEM)


def smem_spec():
    return pl.BlockSpec(memory_space=pltpu.SMEM)


def hbm_spec():
    return pl.BlockSpec(memory_space=pl.ANY)


def call(body, in_specs, out_shapes, out_specs, scratch, args, flops=0, moved=0, grid=()):
    return pl.pallas_call(
        body,
        grid=grid,
        in_specs=in_specs,
        out_shape=tuple(jax.ShapeDtypeStruct(shape, kind) for shape, kind in out_shapes),
        out_specs=tuple(out_specs),
        scratch_shapes=scratch,
        compiler_params=pltpu.CompilerParams(vmem_limit_bytes=VMEM_BYTES),
        cost_estimate=pl.CostEstimate(flops=flops, bytes_accessed=moved, transcendentals=0),
    )(*args)


def on_device(
    frames,
    utt_segments,
    out_grad,
    qkv_weight,
    out_weight,
    ffn_in_weight,
    ffn_out_weight,
    norm_gains,
    biases,
    ffn_bias,
):
    micros, groups, rows, width = frames.shape
    seqs = micros * groups
    ff = ffn_bias.shape[1]
    reps = lax.axis_size("rep")
    seg_count = lax.axis_size("seg")
    mats = Matrices(width, ff)
    by_blocks = width // reps == LANES and reps == 4 and seg_count == BLOCKS
    first = Sizes(rows, width, ff, True)
    last = Sizes(rows, width, ff, False)
    own = seqs * rows
    mem_own = seqs * first.segs

    seg_at = lax.axis_index("seg")
    seg_base = seg_at * first.segs
    rep_at = lax.axis_index("rep")
    place = [seg_base, jnp.int32(first.segs * seg_count)]
    y_at, x_at, core_at = seg_at % CHIPS_Y, rep_at // 2, rep_at % 2
    for other in range(2):
        core = lax.bitwise_xor(core_at, other)
        for hop2 in range(2):
            for hop1 in range(2):
                x_hop = jnp.where(core == 0, hop1, hop2)
                y_hop = jnp.where(core == 0, hop2, hop1)
                place.append(lax.bitwise_xor(y_at, y_hop))
                place.append((lax.bitwise_xor(x_at, x_hop) * 2 + core) * LANES)
    place = jnp.stack([jnp.asarray(entry, jnp.int32) for entry in place])
    lengths = utt_segments.reshape(seqs, utt_segments.shape[2])
    starts = (jnp.cumsum(lengths, axis=1) - lengths).astype(jnp.int32)
    zero_bias = jnp.zeros((1, width), F32)
    row_biases = [
        jnp.concatenate([biases[l : l + 1, 1], zero_bias, biases[l : l + 1, 2]], axis=1)
        for l in range(LAYERS)
    ]
    biases_by_row = jnp.swapaxes(biases, 0, 1)

    frames_own = frames.reshape(seqs, rows, width)
    grads_own = out_grad.reshape(seqs, rows, width)
    far = MEM_LEN * SEG_LEN
    frames_left = shifted(frames_own[:, rows - far :], "seg", 1)
    frames_right = shifted(frames_own[:, :RIGHT_ROWS], "seg", -1)

    attn_rows, ffn_rows = mats.attn_rows, mats.ffn_rows
    if by_blocks:
        qkv_t, out_t, down_t = (
            jnp.swapaxes(member, 1, 2) for member in (qkv_weight, out_weight, ffn_out_weight)
        )
        all_rows = attn_rows + ffn_rows
        spots = Spots(mats)
        shards = call(
            lambda *refs: pack_kernel(spots, *refs),
            [vmem_spec()] * 4,
            [((CHIPS_Z, all_rows, LANES), BF16)] * LAYERS,
            [vmem_spec()] * LAYERS,
            [],
            (qkv_t, out_t, ffn_in_weight, down_t),
        )
        sides0 = gather_sides(after(swap_z(shards[0]), frames_left, frames_right))
        place, starts, row_biases, sent = lax.optimization_barrier(
            (place, starts, row_biases, after(shards[1], sides0[0]))
        )
        sides1 = gather_sides(swap_z(sent))
        first_all = both_cores(sides0 + [across_second(after(sides0[1], sides1[0]))])
        classes = len(first_all) // 2
        grad_outs0 = [((2, 2, CHIPS_Z * all_rows + SMALL_ROWS, LANES), BF16)] * 2
        grad_outs1 = [((2, CHIPS_Z, 2 * all_rows, LANES), BF16)] * 2
        copies_in = len(first_all) * (3 + mats.down_parts)
    else:
        whole = []
        for member, shape in zip(
            (qkv_weight, out_weight, ffn_in_weight, ffn_out_weight),
            (mats.qkv, mats.out, mats.up, mats.down),
        ):
            member = lax.all_gather(member, "rep", axis=1, tiled=True)
            member = lax.all_gather(member, "seg", axis=2, tiled=True)
            whole.append(jnp.swapaxes(member, 1, 2).reshape((LAYERS,) + shape))
        first_all = [member[0] for member in whole]
        last_all = [member[1] for member in whole]
        spots = None
        grad_outs0 = grad_outs1 = [
            (shape, BF16) for shape in (mats.qkv, mats.out, mats.up, mats.down)
        ]
        copies_in = 4
    dma = pltpu.SemaphoreType.DMA

    matrices = [pltpu.VMEM(shape, BF16) for shape in (mats.qkv, mats.out, mats.up, mats.down)]

    (
        z0, proj0, probs0, att0, mixed0, mem1, x1, active0, slope0, low1, send_right, send_left,
    ) = call(
        lambda *refs: first_layer_kernel(
            first, seqs, mats, spots, len(first_all), *refs
        ),
        [smem_spec()] * 2 + [vmem_spec()] * 7 + [hbm_spec()] * len(first_all),
        [
            ((seqs * first.ext, width), BF16),
            ((seqs * first.ext, 3 * width), BF16),
            ((seqs * first.pairs, 2 * first.queries, first.keys), BF16),
            ((seqs * first.queries, width), BF16),
            ((own, width), F32),
            ((mem_own, width), F32),
            ((own, width), F32),
            ((own, ff), BF16),
            ((own, ff), BF16),
            ((own, width), BF16),
            ((seqs, BACK_ROWS, width), BF16),
            ((seqs, RIGHT_ROWS, width), BF16),
        ],
        [vmem_spec()] * 12,
        matrices
        + [
            pltpu.VMEM((seqs, first.queries, first.keys), F32),
            pltpu.VMEM((own, width), BF16),
            dma((copies_in,)),
        ],
        (place, starts, frames_own, frames_left, frames_right, norm_gains, biases_by_row, ffn_bias,
         row_biases[0]) + tuple(first_all),
        flops=24 * own * (4 * width * width + 2 * width * ff) // 2,
        moved=2 * (4 * width * width + 2 * width * ff),
    )
    left1 = shifted(send_right, "seg", 1)
    right1 = shifted(send_left, "seg", -1)
    if by_blocks:
        last_side = across_second(after(sides1[1], sides1[2], low1))
        last_all = both_cores(sides1 + [last_side])
        last_all[-1] = other_core(after(last_side, left1, right1))

    vec_shape = (TILE, width)
    outs = call(
        lambda *refs: last_layer_kernel(
            last, seqs, mats, spots, len(last_all), len(grad_outs1), *refs
        ),
        [smem_spec()] * 2 + [vmem_spec()] * 10 + [hbm_spec()] * len(last_all),
        [
            ((seqs, rows, width), F32),
            ((own, width), F32),
            ((own, width), F32),
            ((mem_own, width), F32),
            ((seqs, BACK_ROWS, width), BF16),
            ((seqs, RIGHT_ROWS, width), BF16),
            (vec_shape, F32),
        ]
        + grad_outs1,
        [vmem_spec()] * 7 + [hbm_spec()] * len(grad_outs1),
        matrices
        + matrices
        + [
            pltpu.VMEM((seqs, last.queries, last.keys), F32),
            pltpu.VMEM((seqs * last.ext, width), BF16),
            pltpu.VMEM((seqs * last.ext, 3 * width), BF16),
            pltpu.VMEM((seqs * last.pairs, 2 * last.queries, last.keys), BF16),
            pltpu.VMEM((seqs * last.queries, width), BF16),
            pltpu.VMEM((own, width), BF16),
            pltpu.VMEM((seqs * last.queries, width), BF16),
            pltpu.VMEM((seqs * last.ext, 3 * width), BF16),
            pltpu.VMEM((seqs * last.queries, width), BF16),
            pltpu.VMEM((own, width), BF16),
            pltpu.VMEM((own, width), F32),
            dma((2 * copies_in,)),
        ],
        (place, starts, low1, left1, right1, mem1, x1, grads_own, norm_gains, biases_by_row, ffn_bias,
         row_biases[1]) + tuple(last_all),
        flops=30 * own * (4 * width * width + 2 * width * ff),
        moved=4 * (4 * width * width + 2 * width * ff),
    )
    encoded, gz1, gh1, gmem1, back_left1, back_right1, vec1 = outs[:7]
    grad_blocks1 = outs[7:]
    from_right1 = shifted(back_left1, "seg", -1)
    from_left1 = shifted(back_right1, "seg", 1)

    gh1_tied = gh1
    if by_blocks:
        mine1, theirs1 = grad_blocks1[0], other_core(grad_blocks1[1])
        far1 = summed(mine1[1], theirs1[1])
        gh1_tied = after(gh1, far1)
    gz0, gh0, gmem0, back_left0, back_right0, upper_vec, vec0, *grad_blocks0 = call(
        lambda *refs: first_back_kernel(
            last, first, seqs, mats, spots, len(first_all), len(grad_outs0), *refs
        ),
        [smem_spec()] + [vmem_spec()] * 19 + [hbm_spec()] * len(first_all),
        [
            ((own, width), F32),
            ((own, width), F32),
            ((mem_own, width), F32),
            ((seqs, BACK_ROWS, width), BF16),
            ((seqs, RIGHT_ROWS, width), BF16),
            (vec_shape, F32),
            (vec_shape, F32),
        ]
        + grad_outs0,
        [vmem_spec()] * 7 + [hbm_spec()] * len(grad_outs0),
        matrices
        + matrices
        + [
            pltpu.VMEM((own, width), BF16),
            pltpu.VMEM((own, width), BF16),
            pltpu.VMEM((own, width), F32),
            pltpu.VMEM((own, width), F32),
            pltpu.VMEM((mem_own, width), F32),
            pltpu.VMEM((seqs * first.queries, width), BF16),
            pltpu.VMEM((seqs * first.ext, 3 * width), BF16),
            pltpu.VMEM((seqs * first.queries, width), BF16),
            pltpu.VMEM((SMALL_ROWS, LANES), BF16),
            dma((2 * copies_in + 8,)),
        ],
        (place, x1, gz1, gh1_tied, gmem1, from_right1, from_left1, mixed0, active0, slope0, att0,
         probs0, proj0, z0, frames_own, frames_left, frames_right, norm_gains, biases_by_row, vec1)
        + tuple(first_all),
        flops=28 * own * (4 * width * width + 2 * width * ff),
        moved=4 * (4 * width * width + 2 * width * ff),
    )
    from_right0 = shifted(back_left0, "seg", -1)
    from_left0 = shifted(back_right0, "seg", 1)
    gz0_last = gz0
    if by_blocks:
        second1 = across_second(far1)
        mine0, theirs0 = grad_blocks0[0], other_core(after(grad_blocks0[1], second1))
        both1 = summed(mine1[0], theirs1[0], second1)
        lines1 = swap_z(both1)
        far0 = summed(mine0[1], after(theirs0, both1)[1])
        second0 = across_second(far0)
        mid0 = summed(mine0[0, 1], theirs0[0, 1], second0[1])
        first0 = across_first(mid0)
        near0 = call(
            lambda *refs: near_small_kernel(CHIPS_Z, *refs),
            [first_rows(mine0), first_rows(theirs0), first_rows(second0), vmem_spec()],
            [((CHIPS_Z, all_rows + SMALL_ROWS, LANES), BF16)],
            [vmem_spec()],
            [],
            [mine0, theirs0, second0, first0],
            grid=(1,),
        )[0]
        first_parts = swap_z(near0)
        gz0_last, lines1 = lax.optimization_barrier((after(gz0, near0), lines1))
        cross1 = jnp.sum(lines1[:, all_rows:].astype(F32), axis=0, keepdims=True).astype(BF16)
        first1 = across_first(cross1)
    frames_grad = call(
        lambda *refs: frames_grad_kernel(first, seqs, *refs),
        [vmem_spec()] * 8,
        [((seqs, rows, width), F32)],
        [vmem_spec()],
        [],
        (frames_own, gz0_last, gh0, gmem0, from_right0, from_left0, norm_gains, biases_by_row),
    )[0]

    if by_blocks:
        shapes = [member.shape for member in (qkv_t, out_t, ffn_in_weight, down_t)]
        shapes += [norm_gains.shape, (biases.shape[1], LAYERS, width), ffn_bias.shape]
        reduced = call(
            lambda *refs: unpack_kernel([spots, spots], [[0], [1, 2]], (0, all_rows), *refs),
            [
                pl.BlockSpec((high, rows_in, LANES), lambda i: (0, 0, 0))
                for high, rows_in in (
                    (CHIPS_Z, all_rows + SMALL_ROWS),
                    (CHIPS_Z, all_rows),
                    (1, all_rows),
                )
            ],
            [(shape, F32) for shape in shapes],
            [vmem_spec()] * len(shapes),
            [],
            [after(first_parts, frames_grad), lines1, first1],
            grid=(1,),
        )
        small = reduced[4], jnp.swapaxes(reduced[5], 0, 1), reduced[6]
        reduced = [
            jnp.swapaxes(reduced[0], 1, 2),
            jnp.swapaxes(reduced[1], 1, 2),
            reduced[2],
            jnp.swapaxes(reduced[3], 1, 2),
        ]
    else:
        reduced = []
        for member0, member1 in zip(grad_blocks0, grad_blocks1):
            both = jnp.stack([member0, member1]).reshape(LAYERS, -1, member0.shape[3])
            both = jnp.swapaxes(both, 1, 2)
            both = lax.psum_scatter(both, "seg", scatter_dimension=2, tiled=True)
            both = lax.psum_scatter(both, "rep", scatter_dimension=1, tiled=True)
            reduced.append(both.astype(F32))
        small = sum_everywhere(jnp.stack([vec0, vec1 + upper_vec]))
        small = small[:, 0:2], small[:, 2:8], small[:, 8:12].reshape(ffn_bias.shape)

    return (
        encoded.reshape(frames.shape),
        frames_grad.reshape(frames.shape),
        reduced[0],
        reduced[1],
        reduced[2],
        reduced[3],
        small[0],
        small[1],
        small[2],
    )


def solution(mesh):
    in_specs = (
        P(None, "rep", "seg", None),
        P(None, "rep", None),
        P(None, "rep", "seg", None),
        P(None, "rep", "seg"),
        P(None, "rep", "seg"),
        P(None, "rep", "seg"),
        P(None, "rep", "seg"),
        P(),
        P(),
        P(),
    )
    out_specs = (
        P(None, "rep", "seg", None),
        P(None, "rep", "seg", None),
        P(None, "rep", "seg"),
        P(None, "rep", "seg"),
        P(None, "rep", "seg"),
        P(None, "rep", "seg"),
        P(),
        P(),
        P(),
    )
    return jax.shard_map(
        on_device, mesh=mesh, in_specs=in_specs, out_specs=out_specs, check_vma=False
    )
```

```python
import jax
import jax.numpy as jnp
from jax import lax
from jax.experimental import pallas as pl
from jax.experimental.pallas import tpu as pltpu
from jax.sharding import PartitionSpec as P

HEADS = 8
SEG_LEN = 16
LEFT_LEN = 30
RIGHT_LEN = 4
MEM_LEN = 4
LAYERS = 2

EPS = 1e-05
ROOT_HALF = 0.7071067811865476
INV_ROOT_TWO_PI = 0.3989422804014327

LANES = 128
TILE = 16
RIGHT_ROWS = 16
LEFT_ROWS = 32
MEM_ROWS = 16
BACK_ROWS = LEFT_ROWS + MEM_ROWS
CHIPS_Z = 4
CHIPS_Y = 2
BLOCKS = CHIPS_Z * CHIPS_Y
SMALL_ROWS = 128
VMEM_BYTES = 56 * 1024 * 1024

BF16 = jnp.bfloat16
F32 = jnp.float32


def nn(a, b):
    return lax.dot_general(a, b, (((1,), (0,)), ((), ())), preferred_element_type=F32)


def nt(a, b):
    return lax.dot_general(a, b, (((1,), (1,)), ((), ())), preferred_element_type=F32)


def tn(a, b):
    return lax.dot_general(a, b, (((0,), (0,)), ((), ())), preferred_element_type=F32)


def col_sum(value):
    return jnp.sum(value, axis=0, keepdims=True)


def norm_forward(inputs, gain, bias):
    center = inputs - jnp.mean(inputs, axis=1, keepdims=True)
    inverse = lax.rsqrt(jnp.mean(center * center, axis=1, keepdims=True) + EPS)
    scaled = center * inverse
    return scaled * gain + bias, scaled, inverse


def norm_backward(grad_in, scaled, inverse, gain):
    grad_scaled = grad_in * gain
    return inverse * (
        grad_scaled
        - jnp.mean(grad_scaled, axis=1, keepdims=True)
        - scaled * jnp.mean(grad_scaled * scaled, axis=1, keepdims=True)
    )


def segment_mean(inputs):
    rows, width = inputs.shape
    return jnp.mean(inputs.reshape(rows // SEG_LEN, SEG_LEN, width), axis=1)


def segment_spread(rows, width, per_segment):
    segs = rows // SEG_LEN
    return jnp.broadcast_to(per_segment[:, None, :], (segs, SEG_LEN, width)).reshape(rows, width)


def identity(size):
    row = lax.broadcasted_iota(jnp.int32, (size, size), 0)
    col = lax.broadcasted_iota(jnp.int32, (size, size), 1)
    return (row == col).astype(F32).astype(BF16)


class Sizes:
    def __init__(self, rows, width, ff, with_summary):
        self.rows = rows
        self.width = width
        self.ff = ff
        self.segs = rows // SEG_LEN
        self.top = TILE if with_summary else 0
        self.keys = rows + RIGHT_ROWS + LEFT_ROWS + MEM_ROWS
        self.ext = self.top + self.keys
        self.queries = self.top + rows
        self.right_at = self.top + rows
        self.left_at = self.right_at + RIGHT_ROWS
        self.mem_at = self.left_at + LEFT_ROWS
        self.pairs = width // LANES


class Matrices:
    def __init__(self, width, ff):
        self.qkv = (CHIPS_Z, CHIPS_Y, 3 * width // BLOCKS, width)
        self.out = (CHIPS_Z, CHIPS_Y, width // BLOCKS, width)
        self.up = (CHIPS_Z, CHIPS_Y, ff // BLOCKS, width)
        self.down = (CHIPS_Z, CHIPS_Y, width // BLOCKS, ff)
        self.down_parts = ff // width
        self.attn_rows = self.qkv[2] + self.out[2]
        self.ffn_rows = self.up[2] + self.down_parts * self.down[2]


class Spots:
    def __init__(self, mats):
        high, wide, up, low = mats.qkv[2], mats.out[2], mats.up[2], mats.down[2]
        self.qkv = (0, 0)
        self.out = (0, high)
        self.up = (0, high + wide)
        self.down = [(0, high + wide + up + low * part) for part in range(mats.down_parts)]


def attn_pairs(mats, spots, groups, qkv_ref, out_ref, place_ref):
    if spots is None:
        return [(groups[0], qkv_ref), (groups[1], out_ref)]
    pairs = []
    for k in range(len(groups[0])):
        row = place_ref[2 + 2 * k]
        lane = pl.multiple_of(place_ref[3 + 2 * k], LANES)
        for (group, first), ref, shape in (
            (spots.qkv, qkv_ref, mats.qkv),
            (spots.out, out_ref, mats.out),
        ):
            block = groups[group][k]
            pairs.append(
                (
                    block.at[:, pl.ds(first, shape[2]), :],
                    ref.at[:, row, :, pl.ds(lane, LANES)],
                )
            )
    return pairs


def ffn_pairs(mats, spots, groups, up_ref, down_ref, place_ref):
    if spots is None:
        return [(groups[2], up_ref), (groups[3], down_ref)]
    pairs = []
    for k in range(len(groups[0])):
        row = place_ref[2 + 2 * k]
        lane = pl.multiple_of(place_ref[3 + 2 * k], LANES)
        group, first = spots.up
        block = groups[group][k]
        pairs.append(
            (block.at[:, pl.ds(first, mats.up[2]), :], up_ref.at[:, row, :, pl.ds(lane, LANES)])
        )
        for part, (group, first) in enumerate(spots.down):
            there = pl.multiple_of(
                place_ref[3 + 2 * k] * mats.down_parts + part * LANES, LANES
            )
            block = groups[group][k]
            pairs.append(
                (
                    block.at[:, pl.ds(first, mats.down[2]), :],
                    down_ref.at[:, row, :, pl.ds(there, LANES)],
                )
            )
    return pairs


def start_in(pairs, sems, at):
    copies = [pltpu.make_async_copy(s, d, sems.at[at + i]) for i, (s, d) in enumerate(pairs)]
    for copy in copies:
        copy.start()
    return copies


def start_out(pairs, sems, at):
    copies = [pltpu.make_async_copy(d, s, sems.at[at + i]) for i, (s, d) in enumerate(pairs)]
    for copy in copies:
        copy.start()
    return copies


def in_groups(spots, refs):
    return refs if spots is None else [refs]


def wait_all(copies):
    for copy in copies:
        copy.wait()


def fill_mask(sizes, seqs, starts_ref, place_ref, mask_ref):
    shape = (sizes.keys, 2 * sizes.queries)
    key = lax.broadcasted_iota(jnp.int32, shape, 0)
    col = lax.broadcasted_iota(jnp.int32, shape, 1)
    col = jnp.where(col < sizes.queries, col, col - sizes.queries)
    base = place_ref[0]
    total = place_ref[1]
    query = jnp.where(col < sizes.top, col, lax.shift_right_arithmetic(col - sizes.top, 4))
    left_at = sizes.rows + RIGHT_ROWS
    mem_at = left_at + LEFT_ROWS
    spot = jnp.where(key < left_at, key, key - mem_at)
    mem_seg = jnp.where(key < mem_at + sizes.segs, key - mem_at, key - mem_at - 2 * sizes.segs)
    key_seg = jnp.where(key < mem_at, lax.shift_right_arithmetic(spot, 4), mem_seg)
    near = (
        (key_seg == query)
        | ((spot >= query * SEG_LEN - LEFT_LEN) & (spot < query * SEG_LEN))
        | ((key_seg == query + 1) & (spot < query * SEG_LEN + SEG_LEN + RIGHT_LEN))
    )
    recent = (key_seg >= query - MEM_LEN) & (key_seg < query) & (col >= sizes.top)
    allowed = ((key < mem_at) & near) | ((key >= mem_at) & recent)
    key_abs = key_seg + base
    query_abs = query + base
    allowed = allowed & (key_abs >= 0) & (key_abs < total)
    if sizes.top:
        allowed = allowed & ((col < sizes.segs) | (col >= sizes.top))
    for n in range(seqs):
        key_owner = jnp.zeros(shape, jnp.int32)
        query_owner = jnp.zeros(shape, jnp.int32)
        for u in range(starts_ref.shape[1]):
            first = starts_ref[n, u]
            key_owner = key_owner + (key_abs >= first).astype(jnp.int32)
            query_owner = query_owner + (query_abs >= first).astype(jnp.int32)
        mask_ref[n] = jnp.where(allowed & (key_owner == query_owner), 0.0, -1e30)


def half_masks():
    lane = lax.broadcasted_iota(jnp.int32, (1, LANES), 1)
    even = (lane < LANES // 2).astype(F32)
    return even.astype(BF16), (1.0 - even).astype(BF16), lane < LANES // 2


def project(sizes, z_ref, qkv_ref, row_bias_ref, proj_ref):
    step = CHIPS_Z // 2
    for c in range(2):
        block = qkv_ref[pl.ds(c * step, step)].reshape(-1, sizes.width)
        wide = block.shape[0]
        made = nt(z_ref[...], block) + row_bias_ref[:, pl.ds(c * wide, wide)]
        proj_ref[:, pl.ds(c * wide, wide)] = made.astype(BF16)


def attend(sizes, seqs, proj_ref, mask_ref, probs_ref, att_ref):
    even, odd, is_even = half_masks()
    scale = (sizes.width // HEADS) ** (-0.5)
    count = sizes.queries

    def body(p, carry):
        for n in range(seqs):
            lane = pl.multiple_of(p * LANES, LANES)
            query = proj_ref[pl.ds(n * sizes.ext, count), pl.ds(lane, LANES)]
            first = n * sizes.ext + sizes.top
            key = proj_ref[pl.ds(first, sizes.keys), pl.ds(sizes.width + lane, LANES)]
            value = proj_ref[pl.ds(first, sizes.keys), pl.ds(2 * sizes.width + lane, LANES)]
            queries = jnp.concatenate([query * even, query * odd], axis=0)
            scores = nt(key, queries) * scale + mask_ref[n]
            scores = jnp.exp(scores - jnp.max(scores, axis=0, keepdims=True))
            probs = (scores * (1.0 / jnp.sum(scores, axis=0, keepdims=True))).astype(BF16)
            probs_ref[n * sizes.pairs + p] = probs
            out = tn(probs, value)
            att_ref[pl.ds(n * count, count), pl.ds(lane, LANES)] = jnp.where(
                is_even, out[:count], out[count:]
            ).astype(BF16)
        return carry

    lax.fori_loop(0, sizes.pairs, body, 0, unroll=True)


def attend_back(sizes, seqs, proj_ref, probs_ref, go_ref, gproj_ref):
    even, odd, is_even = half_masks()
    scale = (sizes.width // HEADS) ** (-0.5)
    count = sizes.queries
    wide = sizes.width
    for n in range(seqs):
        base = n * sizes.ext
        rest = sizes.ext - count
        gproj_ref[pl.ds(base + count, rest), pl.ds(0, wide)] = jnp.zeros((rest, wide), BF16)
        if sizes.top:
            gproj_ref[pl.ds(base, sizes.top), pl.ds(wide, 2 * wide)] = jnp.zeros(
                (sizes.top, 2 * wide), BF16
            )

    def body(p, carry):
        for n in range(seqs):
            lane = pl.multiple_of(p * LANES, LANES)
            base = n * sizes.ext
            first = base + sizes.top
            query = proj_ref[pl.ds(base, count), pl.ds(lane, LANES)]
            key = proj_ref[pl.ds(first, sizes.keys), pl.ds(wide + lane, LANES)]
            value = proj_ref[pl.ds(first, sizes.keys), pl.ds(2 * wide + lane, LANES)]
            grad = go_ref[pl.ds(n * count, count), pl.ds(lane, LANES)]
            queries = jnp.concatenate([query * even, query * odd], axis=0)
            grads = jnp.concatenate([grad * even, grad * odd], axis=0)
            probs_low = probs_ref[n * sizes.pairs + p]
            grad_values = nn(probs_low, grads)
            probs = probs_low.astype(F32)
            weighted = nt(value, grads) * probs
            grad_scores = (
                (weighted - probs * jnp.sum(weighted, axis=0, keepdims=True)) * scale
            ).astype(BF16)
            grad_keys = nn(grad_scores, queries)
            grad_both = tn(grad_scores, key)
            grad_query = jnp.where(is_even, grad_both[:count], grad_both[count:])
            gproj_ref[pl.ds(base, count), pl.ds(lane, LANES)] = grad_query.astype(BF16)
            gproj_ref[pl.ds(first, sizes.keys), pl.ds(wide + lane, LANES)] = grad_keys.astype(BF16)
            gproj_ref[pl.ds(first, sizes.keys), pl.ds(2 * wide + lane, LANES)] = (
                grad_values.astype(BF16)
            )
        return carry

    lax.fori_loop(0, sizes.pairs, body, 0)


def gelu_both(upward):
    half = 0.5 * (1.0 + lax.erf(upward * ROOT_HALF))
    slope = half + upward * jnp.exp(-0.5 * upward * upward) * INV_ROOT_TWO_PI
    return upward * half, slope


def up_block(up_ref, c, wide):
    step = wide // (up_ref.shape[1] * up_ref.shape[2])
    return up_ref[pl.ds(c * step, step)].reshape(-1, up_ref.shape[3])


def down_block(down_ref, c, wide):
    at = pl.multiple_of(c * wide, wide)
    return down_ref[:, :, :, pl.ds(at, wide)].reshape(-1, wide)


def ffn_back_step(
    sizes, c, wide, grad_low, hidden_low, active, slope, up_ref, down_ref, gup_ref, gdown_ref, vec
):
    at = pl.multiple_of(c * wide, wide)
    up = up_block(up_ref, c, wide)
    down = down_block(down_ref, c, wide)
    grad_active = nn(grad_low, down)
    grad_up_f = grad_active * slope
    grad_up = grad_up_f.astype(BF16)
    gdown_ref[:, :, :, pl.ds(at, wide)] = (
        tn(grad_low, active).astype(BF16).reshape(gdown_ref.shape[:3] + (wide,))
    )
    step = wide // (gup_ref.shape[1] * gup_ref.shape[2])
    gup_ref[pl.ds(c * step, step)] = (
        tn(grad_up, hidden_low).astype(BF16).reshape((step,) + gup_ref.shape[1:])
    )
    vec[pl.ds(8 + c, 1), :] = col_sum(grad_up.astype(F32))
    return nn(grad_up, up)


def attn_back_stage(
    sizes, seqs, gz, grad_mem_ref, att_ref, proj_ref, probs_ref, z_ref, qkv_ref, out_ref,
    gqkv_ref, gout_ref, go_ref, gproj_ref, branch_ref, vec, gh_ref, gmem_ref, back_left_ref,
    back_right_ref, scaled_rows=None,
):
    wide = sizes.width
    count = sizes.queries
    bias_out = col_sum(gz)
    for n in range(seqs):
        if sizes.top:
            mem_grad = grad_mem_ref[pl.ds(n * sizes.segs, sizes.segs), :]
            bias_out = bias_out + col_sum(mem_grad)
            branch_ref[pl.ds(n * count, sizes.top), :] = jnp.concatenate(
                [mem_grad, jnp.zeros((sizes.top - sizes.segs, wide), F32)], axis=0
            ).astype(BF16)
        branch_ref[pl.ds(n * count + sizes.top, sizes.rows), :] = gz[
            n * sizes.rows : (n + 1) * sizes.rows
        ].astype(BF16)
    vec[pl.ds(5, 1), :] = bias_out
    branch = branch_ref[...]
    gout_ref[...] = tn(branch, att_ref[...]).astype(BF16).reshape(gout_ref.shape)
    go_ref[...] = nn(branch, out_ref[...].reshape(-1, wide)).astype(BF16)
    attend_back(sizes, seqs, proj_ref, probs_ref, go_ref, gproj_ref)
    vec[pl.ds(3, 1), :] = col_sum(gproj_ref[:, pl.ds(0, wide)].astype(F32))
    vec[pl.ds(4, 1), :] = col_sum(gproj_ref[:, pl.ds(2 * wide, wide)].astype(F32))
    grad_ext = nn(gproj_ref[...], qkv_ref[...].reshape(-1, wide))
    gain_sum = jnp.zeros((1, wide), F32)
    bias_sum = jnp.zeros((1, wide), F32)
    for n in range(seqs):
        base = n * sizes.ext
        own = grad_ext[base + sizes.top : base + sizes.top + sizes.rows]
        if sizes.top:
            spread = grad_ext[base : base + sizes.segs] * (1.0 / SEG_LEN)
            own = own + segment_spread(sizes.rows, wide, spread)
        gh_ref[pl.ds(n * sizes.rows, sizes.rows), :] = own
        mem = base + sizes.mem_at
        gmem_ref[pl.ds(n * sizes.segs, sizes.segs), :] = grad_ext[mem : mem + sizes.segs]
        left = base + sizes.left_at
        back_left_ref[n] = grad_ext[left : left + BACK_ROWS].astype(BF16)
        right = base + sizes.right_at
        back_right_ref[n] = grad_ext[right : right + RIGHT_ROWS].astype(BF16)
        if scaled_rows is not None:
            grads = (
                own,
                grad_ext[right : right + RIGHT_ROWS],
                grad_ext[left : left + LEFT_ROWS],
            )
            for rows, scaled in zip(grads, scaled_rows(n)):
                gain_sum = gain_sum + col_sum(rows * scaled)
                bias_sum = bias_sum + col_sum(rows)
    if scaled_rows is not None:
        vec[pl.ds(0, 1), :] = gain_sum
        vec[pl.ds(2, 1), :] = bias_sum
    step = CHIPS_Z // 2
    part = gqkv_ref.shape[1] * gqkv_ref.shape[2] * step
    for c in range(2):
        gqkv_ref[pl.ds(c * step, step)] = (
            tn(gproj_ref[:, pl.ds(c * part, part)], z_ref[...])
            .astype(BF16)
            .reshape((step,) + gqkv_ref.shape[1:])
        )


def merge_halo(sizes, n, gh_ref, gmem_ref, from_right_ref, from_left_ref):
    first = n * sizes.rows
    back = from_right_ref[n].astype(F32)
    head = gh_ref[pl.ds(first, RIGHT_ROWS), :] + from_left_ref[n].astype(F32)
    middle = gh_ref[pl.ds(first + RIGHT_ROWS, sizes.rows - RIGHT_ROWS - LEFT_ROWS), :]
    tail = gh_ref[pl.ds(first + sizes.rows - LEFT_ROWS, LEFT_ROWS), :] + back[:LEFT_ROWS]
    mem = gmem_ref[pl.ds(n * sizes.segs, sizes.segs), :] + back[LEFT_ROWS + sizes.segs :]
    return jnp.concatenate([head, middle, tail], axis=0), mem


def pack_kernel(spots, qkv_ref, out_ref, up_ref, down_ref, *packed):
    eye = identity(LANES)
    high, wide, low = qkv_ref.shape[1], out_ref.shape[1], down_ref.shape[1]
    for layer, ref in enumerate(packed):
        up = tn(up_ref[layer], eye).astype(BF16)
        for z in range(ref.shape[0]):
            ref[z, pl.ds(spots.qkv[1], high), :] = qkv_ref[layer]
            ref[z, pl.ds(spots.out[1], wide), :] = out_ref[layer]
            ref[z, pl.ds(spots.up[1], up_ref.shape[2]), :] = up
            for part, (_, first) in enumerate(spots.down):
                ref[z, pl.ds(first, low), :] = down_ref[layer, :, pl.ds(part * LANES, LANES)]


def unpack_layer(spots, sources, refs):
    qkv_ref, out_ref, up_ref, down_ref = refs
    high, wide, low = qkv_ref.shape[0], out_ref.shape[0], down_ref.shape[0]

    def total(first, rows):
        parts = [ref[z, pl.ds(first, rows), :] for ref in sources for z in range(ref.shape[0])]
        value = parts[0].astype(F32)
        for part in parts[1:]:
            value = value + part.astype(F32)
        return value

    qkv_ref[...] = total(spots.qkv[1], high)
    out_ref[...] = total(spots.out[1], wide)
    up_ref[...] = nt(identity(LANES), total(spots.up[1], up_ref.shape[1]).astype(BF16))
    for part, (_, first) in enumerate(spots.down):
        down_ref[:, pl.ds(part * LANES, LANES)] = total(first, low)
    return total


def store_layer(layer, held, outs, sems):
    copies = [
        pltpu.make_async_copy(ref, out.at[layer], sems.at[i])
        for i, (ref, out) in enumerate(zip(held, outs))
    ]
    for copy in copies:
        copy.start()
    return copies


def unpack_last_kernel(spots, layer, lines_ref, first_ref, *refs):
    outs, held, sems = refs[:4], refs[4:8], refs[8]
    unpack_layer(spots, (lines_ref, first_ref), held)
    wait_all(store_layer(layer, held, outs, sems))


def unpack_first_kernel(spots, small_at, parts_ref, *refs):
    outs, (gains_ref, biases_ref, ffn_bias_ref), held, sems = (
        refs[4:8], refs[8:11], refs[11:15], refs[15],
    )
    total = unpack_layer(spots, (parts_ref,), held)
    copies = store_layer(0, held, outs, sems)
    sums = total(small_at, SMALL_ROWS)
    parts = gains_ref.shape[2] // LANES
    for layer in range(gains_ref.shape[0]):
        for part in range(parts):
            lanes = pl.ds(part * LANES, LANES)
            block = sums[(layer * parts + part) * TILE : (layer * parts + part + 1) * TILE]
            gains_ref[layer, :, lanes] = block[0:2]
            for row in range(biases_ref.shape[0]):
                biases_ref[row, pl.ds(layer, 1), lanes] = block[2 + row : 3 + row]
            for row in range(ffn_bias_ref.shape[1] // gains_ref.shape[2]):
                at = row * gains_ref.shape[2] + part * LANES
                ffn_bias_ref[pl.ds(layer, 1), pl.ds(at, LANES)] = block[8 + row : 9 + row]
    wait_all(copies)


def near_small_kernel(count, held_ref, first_ref, out_ref):
    rows = out_ref.shape[1] - SMALL_ROWS

    def total(at, size):
        group = pl.ds(at, size)
        return (held_ref[group, :].astype(F32) + first_ref[group, :].astype(F32)).astype(BF16)

    small = total(count * rows, SMALL_ROWS)
    for z in range(count):
        out_ref[z, pl.ds(0, rows), :] = total(z * rows, rows)
        out_ref[z, pl.ds(rows, SMALL_ROWS), :] = small


def first_layer_kernel(
    sizes, seqs, mats, spots, count_in, place_ref, starts_ref, frames_ref, left_ref, right_ref,
    gains_ref, biases_ref, ffn_bias_ref, row_bias_ref, *refs
):
    groups = in_groups(spots, refs[:count_in])
    (
        z_ref, proj_ref, probs_ref, att_ref, mixed_ref, mem_ref, next_ref, active_ref, slope_ref,
        low_ref, send_right_ref, send_left_ref, qkv_ref, out_ref, up_ref, down_ref, mask_ref,
        hidden_ref, sems,
    ) = refs[count_in:]
    wide = sizes.width
    copies = start_in(attn_pairs(mats, spots, groups, qkv_ref, out_ref, place_ref), sems, 0)
    ffn_copies = start_in(
        ffn_pairs(mats, spots, groups, up_ref, down_ref, place_ref), sems, len(copies)
    )
    gain = gains_ref[0, pl.ds(0, 1), :]
    bias = biases_ref[0, pl.ds(0, 1), :]
    pad = jnp.zeros((TILE - sizes.segs, wide), F32)
    for n in range(seqs):
        own = frames_ref[n].astype(F32)
        before = left_ref[n].astype(F32)
        hidden = norm_forward(own, gain, bias)[0]
        halo = norm_forward(before[before.shape[0] - LEFT_ROWS :], gain, bias)[0]
        after = norm_forward(right_ref[n].astype(F32), gain, bias)[0]
        memory = jnp.concatenate(
            [
                segment_mean(own),
                jnp.zeros((sizes.segs - before.shape[0] // SEG_LEN, wide), F32),
                segment_mean(before),
            ],
            axis=0,
        )
        base = n * sizes.ext
        z_ref[pl.ds(base, sizes.top), :] = jnp.concatenate(
            [segment_mean(hidden), pad], axis=0
        ).astype(BF16)
        z_ref[pl.ds(base + sizes.top, sizes.rows), :] = hidden.astype(BF16)
        z_ref[pl.ds(base + sizes.right_at, RIGHT_ROWS), :] = after.astype(BF16)
        z_ref[pl.ds(base + sizes.left_at, LEFT_ROWS), :] = halo.astype(BF16)
        z_ref[pl.ds(base + sizes.mem_at, MEM_ROWS), :] = memory.astype(BF16)
    fill_mask(sizes, seqs, starts_ref, place_ref, mask_ref)
    wait_all(copies)
    project(sizes, z_ref, qkv_ref, row_bias_ref, proj_ref)
    attend(sizes, seqs, proj_ref, mask_ref, probs_ref, att_ref)
    mixed = nt(att_ref[...], out_ref[...].reshape(-1, wide)) + biases_ref[3, pl.ds(0, 1), :]
    for n in range(seqs):
        base = n * sizes.queries
        mem_ref[pl.ds(n * sizes.segs, sizes.segs), :] = mixed[base : base + sizes.segs]
        mixed_ref[pl.ds(n * sizes.rows, sizes.rows), :] = (
            frames_ref[n].astype(F32) + mixed[base + sizes.top : base + sizes.top + sizes.rows]
        )
    mixed = mixed_ref[...]
    hidden, _, _ = norm_forward(mixed, gains_ref[0, pl.ds(1, 1), :], biases_ref[4, pl.ds(0, 1), :])
    hidden_ref[...] = hidden.astype(BF16)
    next_ref[...] = mixed + biases_ref[5, pl.ds(0, 1), :]
    wait_all(ffn_copies)

    def body(c, carry):
        at_lane = pl.multiple_of(c * wide, wide)
        upward = nt(hidden_ref[...], up_block(up_ref, c, wide))
        upward = upward + ffn_bias_ref[pl.ds(0, 1), pl.ds(at_lane, wide)]
        active, slope = gelu_both(upward)
        active = active.astype(BF16)
        active_ref[:, pl.ds(at_lane, wide)] = active
        slope_ref[:, pl.ds(at_lane, wide)] = slope.astype(BF16)
        next_ref[...] += nt(active, down_block(down_ref, c, wide))
        return carry

    lax.fori_loop(0, sizes.ff // wide, body, 0)
    low, _, _ = norm_forward(
        next_ref[...], gains_ref[1, pl.ds(0, 1), :], biases_ref[0, pl.ds(1, 1), :]
    )
    low = low.astype(BF16)
    low_ref[...] = low
    for n in range(seqs):
        base = n * sizes.rows
        send_right_ref[n, pl.ds(0, LEFT_ROWS), :] = low[
            base + sizes.rows - LEFT_ROWS : base + sizes.rows
        ]
        send_right_ref[n, pl.ds(LEFT_ROWS, MEM_ROWS), :] = jnp.concatenate(
            [
                mem_ref[pl.ds(n * sizes.segs, sizes.segs), :],
                jnp.zeros((MEM_ROWS - sizes.segs, wide), F32),
            ],
            axis=0,
        ).astype(BF16)
        send_left_ref[n] = low[base : base + RIGHT_ROWS]


def last_layer_kernel(
    sizes, seqs, mats, spots, count_in, count_out, place_ref, starts_ref, low_ref, left_ref,
    right_ref, mem_ref, inputs_ref, out_grad_ref, gains_ref, biases_ref, ffn_bias_ref,
    row_bias_ref, *refs
):
    groups = in_groups(spots, refs[:count_in])
    (encoded_ref, gz_ref, gh_ref, gmem_ref, back_left_ref, back_right_ref, vec) = refs[
        count_in : count_in + 7
    ]
    hbm_out = refs[count_in + 7 : count_in + 7 + count_out]
    (
        qkv_ref, out_ref, up_ref, down_ref, gqkv_ref, gout_ref, gup_ref, gdown_ref, mask_ref,
        z_ref, proj_ref, probs_ref, att_ref, hidden_ref, go_ref, gproj_ref, branch_ref,
        grad_low_ref, grad_hidden_ref, sems,
    ) = refs[count_in + 7 + count_out :]
    outs_to = hbm_out
    if spots is not None:
        rows = mats.attn_rows + mats.ffn_rows
        outs_to = [
            [
                ref.at[hop2, :, pl.ds(hop1 * rows, rows), :]
                for ref in hbm_out
                for hop2 in range(2)
                for hop1 in range(2)
            ]
        ]
    wide = sizes.width
    attn_copies = start_in(attn_pairs(mats, spots, groups, qkv_ref, out_ref, place_ref), sems, 0)
    ffn_copies = start_in(
        ffn_pairs(mats, spots, groups, up_ref, down_ref, place_ref), sems, len(attn_copies)
    )
    vec[...] = jnp.zeros_like(vec)
    for n in range(seqs):
        base = n * sizes.ext
        z_ref[pl.ds(base, sizes.rows), :] = low_ref[pl.ds(n * sizes.rows, sizes.rows), :]
        z_ref[pl.ds(base + sizes.right_at, RIGHT_ROWS), :] = right_ref[n]
        z_ref[pl.ds(base + sizes.left_at, LEFT_ROWS), :] = left_ref[n, pl.ds(0, LEFT_ROWS), :]
        memory = jnp.concatenate(
            [
                mem_ref[pl.ds(n * sizes.segs, sizes.segs), :],
                left_ref[n, pl.ds(LEFT_ROWS, MEM_ROWS), :].astype(F32)[: sizes.segs],
            ],
            axis=0,
        )
        z_ref[pl.ds(base + sizes.mem_at, MEM_ROWS), :] = memory.astype(BF16)
        grad_low_ref[pl.ds(n * sizes.rows, sizes.rows), :] = out_grad_ref[n]
    fill_mask(sizes, seqs, starts_ref, place_ref, mask_ref)
    wait_all(attn_copies)
    project(sizes, z_ref, qkv_ref, row_bias_ref, proj_ref)
    attend(sizes, seqs, proj_ref, mask_ref, probs_ref, att_ref)
    mixed = (
        inputs_ref[...]
        + nt(att_ref[...], out_ref[...].reshape(-1, wide))
        + biases_ref[3, pl.ds(1, 1), :]
    )
    gain = gains_ref[1, pl.ds(1, 1), :]
    hidden, scaled, inverse = norm_forward(mixed, gain, biases_ref[4, pl.ds(1, 1), :])
    hidden_ref[...] = hidden.astype(BF16)
    for n in range(seqs):
        encoded_ref[n] = mixed[n * sizes.rows : (n + 1) * sizes.rows] + biases_ref[5, pl.ds(1, 1), :]
    grad_hidden_ref[...] = jnp.zeros_like(grad_hidden_ref)
    wait_all(ffn_copies)

    def body(c, carry):
        at_lane = pl.multiple_of(c * wide, wide)
        upward = nt(hidden_ref[...], up_block(up_ref, c, wide))
        upward = upward + ffn_bias_ref[pl.ds(1, 1), pl.ds(at_lane, wide)]
        active, slope = gelu_both(upward)
        active = active.astype(BF16)
        made = nt(active, down_block(down_ref, c, wide))
        for n in range(seqs):
            encoded_ref[n] += made[n * sizes.rows : (n + 1) * sizes.rows]
        grad_hidden_ref[...] += ffn_back_step(
            sizes, c, wide, grad_low_ref[...], hidden_ref[...], active, slope, up_ref, down_ref,
            gup_ref, gdown_ref, vec,
        )
        return carry

    lax.fori_loop(0, sizes.ff // wide, body, 0)
    out_at = len(attn_copies) + len(ffn_copies)
    outs = start_out(
        ffn_pairs(mats, spots, outs_to, gup_ref, gdown_ref, place_ref), sems, out_at
    )
    grad = grad_low_ref[...].astype(F32)
    grad_hidden = grad_hidden_ref[...]
    vec[pl.ds(1, 1), :] = col_sum(grad_hidden * scaled)
    vec[pl.ds(6, 1), :] = col_sum(grad_hidden)
    vec[pl.ds(7, 1), :] = col_sum(grad)
    gz = grad + norm_backward(grad_hidden, scaled, inverse, gain)
    gz_ref[...] = gz
    attn_back_stage(
        sizes, seqs, gz, None, att_ref, proj_ref, probs_ref, z_ref, qkv_ref, out_ref, gqkv_ref,
        gout_ref, go_ref, gproj_ref, branch_ref, vec, gh_ref, gmem_ref, back_left_ref,
        back_right_ref,
    )
    outs = outs + start_out(
        attn_pairs(mats, spots, outs_to, gqkv_ref, gout_ref, place_ref),
        sems,
        out_at + len(outs),
    )
    wait_all(outs)


def first_back_kernel(
    last, sizes, seqs, mats, spots, count_in, count_out, place_ref, inputs_ref, gz_in_ref,
    gh_in_ref, gmem_in_ref, from_right_ref, from_left_ref, mixed_ref, active_ref, slope_ref,
    att_ref, probs_ref, proj_ref, z_ref, frames_ref, left_ref, right_ref, gains_ref, biases_ref,
    last_vec, *refs
):
    groups = in_groups(spots, refs[:count_in])
    gz_ref, gh_ref, gmem_ref, back_left_ref, back_right_ref, upper_vec, vec = refs[
        count_in : count_in + 7
    ]
    refs = refs[count_in + 7 :]
    hbm_out = refs[:count_out]
    (
        qkv_ref, out_ref, up_ref, down_ref, gqkv_ref, gout_ref, gup_ref, gdown_ref, hidden_ref,
        grad_low_ref, grad_ref, grad_hidden_ref, grad_mem_ref, go_ref, gproj_ref, branch_ref,
        small_ref, sems,
    ) = refs[count_out:]
    wide = sizes.width
    small = []
    outs_to = hbm_out
    if spots is not None:
        rows = mats.attn_rows + mats.ffn_rows
        end = CHIPS_Z * rows
        each = [
            ref.at[hop2, hop1] for ref in hbm_out for hop2 in range(2) for hop1 in range(2)
        ]
        small = [ref.at[pl.ds(end, SMALL_ROWS), :] for ref in each]
        outs_to = [[ref.at[pl.ds(0, end), :].reshape(CHIPS_Z, rows, LANES) for ref in each]]
    ffn_copies = start_in(ffn_pairs(mats, spots, groups, up_ref, down_ref, place_ref), sems, 0)
    attn_copies = start_in(
        attn_pairs(mats, spots, groups, qkv_ref, out_ref, place_ref), sems, len(ffn_copies)
    )
    vec[...] = jnp.zeros_like(vec)
    upper_vec[...] = jnp.zeros_like(upper_vec)
    gain = gains_ref[1, pl.ds(0, 1), :]
    gain_sum = jnp.zeros((1, wide), F32)
    bias_sum = jnp.zeros((1, wide), F32)
    for n in range(seqs):
        rows = pl.ds(n * sizes.rows, sizes.rows)
        _, scaled, inverse = norm_forward(
            inputs_ref[rows, :], gain, biases_ref[0, pl.ds(1, 1), :]
        )
        total, mem = merge_halo(last, n, gh_in_ref, gmem_in_ref, from_right_ref, from_left_ref)
        gain_sum = gain_sum + col_sum(total * scaled)
        bias_sum = bias_sum + col_sum(total)
        grad = gz_in_ref[rows, :] + norm_backward(total, scaled, inverse, gain)
        grad_ref[rows, :] = grad
        grad_low_ref[rows, :] = grad.astype(BF16)
        grad_mem_ref[pl.ds(n * sizes.segs, sizes.segs), :] = mem
    upper_vec[pl.ds(0, 1), :] = gain_sum
    upper_vec[pl.ds(2, 1), :] = bias_sum
    gain = gains_ref[0, pl.ds(1, 1), :]
    hidden, scaled, inverse = norm_forward(
        mixed_ref[...], gain, biases_ref[4, pl.ds(0, 1), :]
    )
    hidden_ref[...] = hidden.astype(BF16)
    grad_hidden_ref[...] = jnp.zeros_like(grad_hidden_ref)
    wait_all(ffn_copies)

    def body(c, carry):
        at_lane = pl.multiple_of(c * wide, wide)
        grad_hidden_ref[...] += ffn_back_step(
            sizes, c, wide, grad_low_ref[...], hidden_ref[...],
            active_ref[:, pl.ds(at_lane, wide)], slope_ref[:, pl.ds(at_lane, wide)].astype(F32),
            up_ref, down_ref, gup_ref, gdown_ref, vec,
        )
        return carry

    lax.fori_loop(0, sizes.ff // wide, body, 0)
    out_at = len(ffn_copies) + len(attn_copies)
    outs = start_out(
        ffn_pairs(mats, spots, outs_to, gup_ref, gdown_ref, place_ref), sems, out_at
    )
    grad_hidden = grad_hidden_ref[...]
    grad = grad_ref[...]
    vec[pl.ds(1, 1), :] = col_sum(grad_hidden * scaled)
    vec[pl.ds(6, 1), :] = col_sum(grad_hidden)
    vec[pl.ds(7, 1), :] = col_sum(grad)
    gz = grad + norm_backward(grad_hidden, scaled, inverse, gain)
    gz_ref[...] = gz

    def scaled_rows(n):
        before = left_ref[n, pl.ds(left_ref.shape[1] - LEFT_ROWS, LEFT_ROWS), :]
        parts = (frames_ref[n], right_ref[n], before)
        first_gain = gains_ref[0, pl.ds(0, 1), :]
        first_bias = biases_ref[0, pl.ds(0, 1), :]
        return [norm_forward(part.astype(F32), first_gain, first_bias)[1] for part in parts]

    wait_all(attn_copies)
    attn_back_stage(
        sizes, seqs, gz, grad_mem_ref, att_ref, proj_ref, probs_ref, z_ref, qkv_ref, out_ref,
        gqkv_ref, gout_ref, go_ref, gproj_ref, branch_ref, vec, gh_ref, gmem_ref, back_left_ref,
        back_right_ref, scaled_rows,
    )
    outs = outs + start_out(
        attn_pairs(mats, spots, outs_to, gqkv_ref, gout_ref, place_ref),
        sems,
        out_at + len(outs),
    )
    parts = sizes.width // LANES
    for layer, total in enumerate((vec[...], last_vec[...] + upper_vec[...])):
        for part in range(parts):
            small_ref[pl.ds((layer * parts + part) * TILE, TILE), :] = total[
                :, part * LANES : (part + 1) * LANES
            ].astype(BF16)
    outs = outs + start_out([(ref, small_ref) for ref in small], sems, out_at + len(outs))
    wait_all(outs)


def frames_grad_kernel(
    sizes, seqs, frames_ref, gz_ref, gh_ref, gmem_ref, from_right_ref, from_left_ref, gains_ref,
    biases_ref, grad_ref
):
    gain = gains_ref[0, pl.ds(0, 1), :]
    for n in range(seqs):
        _, scaled, inverse = norm_forward(
            frames_ref[n].astype(F32), gain, biases_ref[0, pl.ds(0, 1), :]
        )
        total, mem = merge_halo(sizes, n, gh_ref, gmem_ref, from_right_ref, from_left_ref)
        grad_ref[n] = (
            gz_ref[pl.ds(n * sizes.rows, sizes.rows), :]
            + norm_backward(total, scaled, inverse, gain)
            + segment_spread(sizes.rows, sizes.width, mem * (1.0 / SEG_LEN))
        )


def shifted(value, axis, by):
    size = lax.axis_size(axis)
    pairs = [(i, i + by) for i in range(size) if 0 <= i + by < size]
    return lax.ppermute(value, axis, pairs)


def permuted(value, move):
    reps = lax.axis_size("rep")
    pairs = []
    for flat in range(lax.axis_size("seg") * reps):
        seg, rep = divmod(flat, reps)
        z, y, x, core = move(seg // CHIPS_Y, seg % CHIPS_Y, rep // 2, rep % 2)
        pairs.append((flat, (z * CHIPS_Y + y) * reps + 2 * x + core))
    return lax.ppermute(value, ("seg", "rep"), pairs)


def across_first(value):
    return permuted(value, lambda z, y, x, c: (z, y, x ^ 1, c) if c == 0 else (z, y ^ 1, x, c))


def across_second(value):
    return permuted(value, lambda z, y, x, c: (z, y ^ 1, x, c) if c == 0 else (z, y, x ^ 1, c))


def other_core(value):
    return permuted(value, lambda z, y, x, c: (z, y, x, c ^ 1))


def after(value, *others):
    return lax.optimization_barrier((value,) + others)[0]


def swap_z(blocks):
    groups = [
        [z * CHIPS_Y + y for z in range(CHIPS_Z)] for y in range(CHIPS_Y)
    ]
    return lax.all_to_all(blocks, "seg", 0, 0, axis_index_groups=groups, tiled=True)


def gather_sides(here):
    return [here, across_first(here), across_second(here)]


def both_cores(blocks):
    return blocks + [other_core(block) for block in blocks]


def summed(*parts):
    total = parts[0].astype(F32)
    for part in parts[1:]:
        total = total + part.astype(F32)
    return total.astype(BF16)


def sum_everywhere(value):
    count = lax.axis_size("seg") * lax.axis_size("rep")
    bit = 1
    while bit < count:
        value = value + lax.ppermute(value, ("seg", "rep"), [(i, i ^ bit) for i in range(count)])
        bit *= 2
    return value


def vmem_spec():
    return pl.BlockSpec(memory_space=pltpu.VMEM)


def smem_spec():
    return pl.BlockSpec(memory_space=pltpu.SMEM)


def hbm_spec():
    return pl.BlockSpec(memory_space=pl.ANY)


def call(body, in_specs, out_shapes, out_specs, scratch, args, flops=0, moved=0, grid=(), aliases={}):
    return pl.pallas_call(
        body,
        grid=grid,
        input_output_aliases=aliases,
        in_specs=in_specs,
        out_shape=tuple(jax.ShapeDtypeStruct(shape, kind) for shape, kind in out_shapes),
        out_specs=tuple(out_specs),
        scratch_shapes=scratch,
        compiler_params=pltpu.CompilerParams(vmem_limit_bytes=VMEM_BYTES),
        cost_estimate=pl.CostEstimate(flops=flops, bytes_accessed=moved, transcendentals=0),
    )(*args)


def on_device(
    frames,
    utt_segments,
    out_grad,
    qkv_weight,
    out_weight,
    ffn_in_weight,
    ffn_out_weight,
    norm_gains,
    biases,
    ffn_bias,
):
    micros, groups, rows, width = frames.shape
    seqs = micros * groups
    ff = ffn_bias.shape[1]
    reps = lax.axis_size("rep")
    seg_count = lax.axis_size("seg")
    mats = Matrices(width, ff)
    by_blocks = width // reps == LANES and reps == 4 and seg_count == BLOCKS
    first = Sizes(rows, width, ff, True)
    last = Sizes(rows, width, ff, False)
    own = seqs * rows
    mem_own = seqs * first.segs

    seg_at = lax.axis_index("seg")
    seg_base = seg_at * first.segs
    rep_at = lax.axis_index("rep")
    place = [seg_base, jnp.int32(first.segs * seg_count)]
    y_at, x_at, core_at = seg_at % CHIPS_Y, rep_at // 2, rep_at % 2
    for other in range(2):
        core = lax.bitwise_xor(core_at, other)
        for hop2 in range(2):
            for hop1 in range(2):
                x_hop = jnp.where(core == 0, hop1, hop2)
                y_hop = jnp.where(core == 0, hop2, hop1)
                place.append(lax.bitwise_xor(y_at, y_hop))
                place.append((lax.bitwise_xor(x_at, x_hop) * 2 + core) * LANES)
    place = jnp.stack([jnp.asarray(entry, jnp.int32) for entry in place])
    lengths = utt_segments.reshape(seqs, utt_segments.shape[2])
    starts = (jnp.cumsum(lengths, axis=1) - lengths).astype(jnp.int32)
    zero_bias = jnp.zeros((1, width), F32)
    row_biases = [
        jnp.concatenate([biases[l : l + 1, 1], zero_bias, biases[l : l + 1, 2]], axis=1)
        for l in range(LAYERS)
    ]
    biases_by_row = jnp.swapaxes(biases, 0, 1)

    frames_own = frames.reshape(seqs, rows, width)
    grads_own = out_grad.reshape(seqs, rows, width)
    far = MEM_LEN * SEG_LEN
    frames_left = shifted(frames_own[:, rows - far :], "seg", 1)
    frames_right = shifted(frames_own[:, :RIGHT_ROWS], "seg", -1)

    attn_rows, ffn_rows = mats.attn_rows, mats.ffn_rows
    if by_blocks:
        qkv_t, out_t, down_t = (
            jnp.swapaxes(member, 1, 2) for member in (qkv_weight, out_weight, ffn_out_weight)
        )
        all_rows = attn_rows + ffn_rows
        spots = Spots(mats)
        shards = call(
            lambda *refs: pack_kernel(spots, *refs),
            [vmem_spec()] * 4,
            [((CHIPS_Z, all_rows, LANES), BF16)] * LAYERS,
            [vmem_spec()] * LAYERS,
            [],
            (qkv_t, out_t, ffn_in_weight, down_t),
        )
        sides0 = gather_sides(after(swap_z(shards[0]), frames_left, frames_right))
        place, starts, row_biases, sent = lax.optimization_barrier(
            (place, starts, row_biases, after(shards[1], sides0[0]))
        )
        sides1 = gather_sides(swap_z(sent))
        first_all = both_cores(sides0 + [across_second(after(sides0[1], sides1[0]))])
        classes = len(first_all) // 2
        grad_outs0 = [((2, 2, CHIPS_Z * all_rows + SMALL_ROWS, LANES), BF16)] * 2
        grad_outs1 = [((2, CHIPS_Z, 2 * all_rows, LANES), BF16)] * 2
        copies_in = len(first_all) * (3 + mats.down_parts)
    else:
        whole = []
        for member, shape in zip(
            (qkv_weight, out_weight, ffn_in_weight, ffn_out_weight),
            (mats.qkv, mats.out, mats.up, mats.down),
        ):
            member = lax.all_gather(member, "rep", axis=1, tiled=True)
            member = lax.all_gather(member, "seg", axis=2, tiled=True)
            whole.append(jnp.swapaxes(member, 1, 2).reshape((LAYERS,) + shape))
        first_all = [member[0] for member in whole]
        last_all = [member[1] for member in whole]
        spots = None
        grad_outs0 = grad_outs1 = [
            (shape, BF16) for shape in (mats.qkv, mats.out, mats.up, mats.down)
        ]
        copies_in = 4
    dma = pltpu.SemaphoreType.DMA

    matrices = [pltpu.VMEM(shape, BF16) for shape in (mats.qkv, mats.out, mats.up, mats.down)]

    (
        z0, proj0, probs0, att0, mixed0, mem1, x1, active0, slope0, low1, send_right, send_left,
    ) = call(
        lambda *refs: first_layer_kernel(
            first, seqs, mats, spots, len(first_all), *refs
        ),
        [smem_spec()] * 2 + [vmem_spec()] * 7 + [hbm_spec()] * len(first_all),
        [
            ((seqs * first.ext, width), BF16),
            ((seqs * first.ext, 3 * width), BF16),
            ((seqs * first.pairs, first.keys, 2 * first.queries), BF16),
            ((seqs * first.queries, width), BF16),
            ((own, width), F32),
            ((mem_own, width), F32),
            ((own, width), F32),
            ((own, ff), BF16),
            ((own, ff), BF16),
            ((own, width), BF16),
            ((seqs, BACK_ROWS, width), BF16),
            ((seqs, RIGHT_ROWS, width), BF16),
        ],
        [vmem_spec()] * 12,
        matrices
        + [
            pltpu.VMEM((seqs, first.keys, 2 * first.queries), F32),
            pltpu.VMEM((own, width), BF16),
            dma((copies_in,)),
        ],
        (place, starts, frames_own, frames_left, frames_right, norm_gains, biases_by_row, ffn_bias,
         row_biases[0]) + tuple(first_all),
        flops=24 * own * (4 * width * width + 2 * width * ff) // 2,
        moved=2 * (4 * width * width + 2 * width * ff),
    )
    left1 = shifted(send_right, "seg", 1)
    right1 = shifted(send_left, "seg", -1)
    if by_blocks:
        last_side = across_second(after(sides1[1], sides1[2], low1))
        last_all = both_cores(sides1 + [last_side])
        last_all[-1] = other_core(after(last_side, left1, right1))

    vec_shape = (TILE, width)
    outs = call(
        lambda *refs: last_layer_kernel(
            last, seqs, mats, spots, len(last_all), len(grad_outs1), *refs
        ),
        [smem_spec()] * 2 + [vmem_spec()] * 10 + [hbm_spec()] * len(last_all),
        [
            ((seqs, rows, width), F32),
            ((own, width), F32),
            ((own, width), F32),
            ((mem_own, width), F32),
            ((seqs, BACK_ROWS, width), BF16),
            ((seqs, RIGHT_ROWS, width), BF16),
            (vec_shape, F32),
        ]
        + grad_outs1,
        [vmem_spec()] * 7 + [hbm_spec()] * len(grad_outs1),
        matrices
        + matrices
        + [
            pltpu.VMEM((seqs, last.keys, 2 * last.queries), F32),
            pltpu.VMEM((seqs * last.ext, width), BF16),
            pltpu.VMEM((seqs * last.ext, 3 * width), BF16),
            pltpu.VMEM((seqs * last.pairs, last.keys, 2 * last.queries), BF16),
            pltpu.VMEM((seqs * last.queries, width), BF16),
            pltpu.VMEM((own, width), BF16),
            pltpu.VMEM((seqs * last.queries, width), BF16),
            pltpu.VMEM((seqs * last.ext, 3 * width), BF16),
            pltpu.VMEM((seqs * last.queries, width), BF16),
            pltpu.VMEM((own, width), BF16),
            pltpu.VMEM((own, width), F32),
            dma((2 * copies_in,)),
        ],
        (place, starts, low1, left1, right1, mem1, x1, grads_own, norm_gains, biases_by_row, ffn_bias,
         row_biases[1]) + tuple(last_all),
        flops=30 * own * (4 * width * width + 2 * width * ff),
        moved=4 * (4 * width * width + 2 * width * ff),
    )
    encoded, gz1, gh1, gmem1, back_left1, back_right1, vec1 = outs[:7]
    grad_blocks1 = outs[7:]
    from_right1 = shifted(back_left1, "seg", -1)
    from_left1 = shifted(back_right1, "seg", 1)

    gh1_tied = gh1
    if by_blocks:
        mine1, theirs1 = grad_blocks1[0], other_core(grad_blocks1[1])
        far1 = summed(mine1[1], theirs1[1])
        gh1_tied = after(gh1, far1)
    gz0, gh0, gmem0, back_left0, back_right0, upper_vec, vec0, *grad_blocks0 = call(
        lambda *refs: first_back_kernel(
            last, first, seqs, mats, spots, len(first_all), len(grad_outs0), *refs
        ),
        [smem_spec()] + [vmem_spec()] * 19 + [hbm_spec()] * len(first_all),
        [
            ((own, width), F32),
            ((own, width), F32),
            ((mem_own, width), F32),
            ((seqs, BACK_ROWS, width), BF16),
            ((seqs, RIGHT_ROWS, width), BF16),
            (vec_shape, F32),
            (vec_shape, F32),
        ]
        + grad_outs0,
        [vmem_spec()] * 7 + [hbm_spec()] * len(grad_outs0),
        matrices
        + matrices
        + [
            pltpu.VMEM((own, width), BF16),
            pltpu.VMEM((own, width), BF16),
            pltpu.VMEM((own, width), F32),
            pltpu.VMEM((own, width), F32),
            pltpu.VMEM((mem_own, width), F32),
            pltpu.VMEM((seqs * first.queries, width), BF16),
            pltpu.VMEM((seqs * first.ext, 3 * width), BF16),
            pltpu.VMEM((seqs * first.queries, width), BF16),
            pltpu.VMEM((SMALL_ROWS, LANES), BF16),
            dma((2 * copies_in + 8,)),
        ],
        (place, x1, gz1, gh1_tied, gmem1, from_right1, from_left1, mixed0, active0, slope0, att0,
         probs0, proj0, z0, frames_own, frames_left, frames_right, norm_gains, biases_by_row, vec1)
        + tuple(first_all),
        flops=28 * own * (4 * width * width + 2 * width * ff),
        moved=4 * (4 * width * width + 2 * width * ff),
    )
    from_right0 = shifted(back_left0, "seg", -1)
    from_left0 = shifted(back_right0, "seg", 1)
    gz0_last = gz0
    if by_blocks:
        second1 = across_second(far1)
        mine0, theirs0 = grad_blocks0[0], other_core(after(grad_blocks0[1], second1))
        both1 = summed(mine1[0], theirs1[0], second1)
        lines1 = swap_z(both1)
        far0 = summed(mine0[1], after(theirs0, both1)[1])
        second0 = across_second(far0)
        mid0 = summed(mine0[0, 1], theirs0[0, 1], second0[1])
        first0 = across_first(mid0)
        held0 = summed(mine0[0, 0], theirs0[0, 0], after(second0, mid0)[0])
        near0 = call(
            lambda *refs: near_small_kernel(CHIPS_Z, *refs),
            [vmem_spec()] * 2,
            [((CHIPS_Z, all_rows + SMALL_ROWS, LANES), BF16)],
            [vmem_spec()],
            [],
            [held0, first0],
        )[0]
        first_parts = swap_z(near0)
        gz0_last, lines1 = lax.optimization_barrier((after(gz0, near0), lines1))
        cross1 = jnp.sum(lines1[:, all_rows:].astype(F32), axis=0, keepdims=True).astype(BF16)
        first1 = across_first(cross1)
    frames_grad = call(
        lambda *refs: frames_grad_kernel(first, seqs, *refs),
        [vmem_spec()] * 8,
        [((seqs, rows, width), F32)],
        [vmem_spec()],
        [],
        (frames_own, gz0_last, gh0, gmem0, from_right0, from_left0, norm_gains, biases_by_row),
    )[0]

    if by_blocks:
        shapes = [member.shape for member in (qkv_t, out_t, ffn_in_weight, down_t)]
        held = [pltpu.VMEM(shape[1:], F32) for shape in shapes]
        whole = [(shape, F32) for shape in shapes]
        written = call(
            lambda *refs: unpack_last_kernel(spots, LAYERS - 1, *refs),
            [
                pl.BlockSpec((CHIPS_Z, all_rows, LANES), lambda i: (0, 0, 0)),
                pl.BlockSpec((1, all_rows, LANES), lambda i: (0, 0, 0)),
            ],
            whole,
            [hbm_spec()] * 4,
            held + [dma((4,))],
            [lines1, first1],
            grid=(1,),
        )
        small_shapes = [norm_gains.shape, (biases.shape[1], LAYERS, width), ffn_bias.shape]
        reduced = call(
            lambda *refs: unpack_first_kernel(spots, all_rows, *refs),
            [vmem_spec()] + [hbm_spec()] * 4,
            whole + [(shape, F32) for shape in small_shapes],
            [hbm_spec()] * 4 + [vmem_spec()] * 3,
            held + [dma((4,))],
            [after(first_parts, frames_grad)] + list(written),
            aliases={1 + i: i for i in range(4)},
        )
        small = reduced[4], jnp.swapaxes(reduced[5], 0, 1), reduced[6]
        reduced = [
            jnp.swapaxes(reduced[0], 1, 2),
            jnp.swapaxes(reduced[1], 1, 2),
            reduced[2],
            jnp.swapaxes(reduced[3], 1, 2),
        ]
    else:
        reduced = []
        for member0, member1 in zip(grad_blocks0, grad_blocks1):
            both = jnp.stack([member0, member1]).reshape(LAYERS, -1, member0.shape[3])
            both = jnp.swapaxes(both, 1, 2)
            both = lax.psum_scatter(both, "seg", scatter_dimension=2, tiled=True)
            both = lax.psum_scatter(both, "rep", scatter_dimension=1, tiled=True)
            reduced.append(both.astype(F32))
        small = sum_everywhere(jnp.stack([vec0, vec1 + upper_vec]))
        small = small[:, 0:2], small[:, 2:8], small[:, 8:12].reshape(ffn_bias.shape)

    return (
        encoded.reshape(frames.shape),
        frames_grad.reshape(frames.shape),
        reduced[0],
        reduced[1],
        reduced[2],
        reduced[3],
        small[0],
        small[1],
        small[2],
    )


def solution(mesh):
    in_specs = (
        P(None, "rep", "seg", None),
        P(None, "rep", None),
        P(None, "rep", "seg", None),
        P(None, "rep", "seg"),
        P(None, "rep", "seg"),
        P(None, "rep", "seg"),
        P(None, "rep", "seg"),
        P(),
        P(),
        P(),
    )
    out_specs = (
        P(None, "rep", "seg", None),
        P(None, "rep", "seg", None),
        P(None, "rep", "seg"),
        P(None, "rep", "seg"),
        P(None, "rep", "seg"),
        P(None, "rep", "seg"),
        P(),
        P(),
        P(),
    )
    return jax.shard_map(
        on_device, mesh=mesh, in_specs=in_specs, out_specs=out_specs, check_vma=False
    )
```

```python
import jax
import jax.numpy as jnp
from jax import lax
from jax.experimental import pallas as pl
from jax.experimental.pallas import tpu as pltpu
from jax.sharding import PartitionSpec as P

HEADS = 8
SEG_LEN = 16
LEFT_LEN = 30
RIGHT_LEN = 4
MEM_LEN = 4
LAYERS = 2

EPS = 1e-05
ROOT_HALF = 0.7071067811865476
INV_ROOT_TWO_PI = 0.3989422804014327

LANES = 128
TILE = 16
RIGHT_ROWS = 16
LEFT_ROWS = 32
MEM_ROWS = 16
BACK_ROWS = LEFT_ROWS + MEM_ROWS
CHIPS_Z = 4
CHIPS_Y = 2
BLOCKS = CHIPS_Z * CHIPS_Y
SMALL_ROWS = 128
VMEM_BYTES = 56 * 1024 * 1024

BF16 = jnp.bfloat16
F32 = jnp.float32


def nn(a, b):
    return lax.dot_general(a, b, (((1,), (0,)), ((), ())), preferred_element_type=F32)


def nt(a, b):
    return lax.dot_general(a, b, (((1,), (1,)), ((), ())), preferred_element_type=F32)


def tn(a, b):
    return lax.dot_general(a, b, (((0,), (0,)), ((), ())), preferred_element_type=F32)


def col_sum(value):
    return jnp.sum(value, axis=0, keepdims=True)


def norm_forward(inputs, gain, bias):
    center = inputs - jnp.mean(inputs, axis=1, keepdims=True)
    inverse = lax.rsqrt(jnp.mean(center * center, axis=1, keepdims=True) + EPS)
    scaled = center * inverse
    return scaled * gain + bias, scaled, inverse


def norm_backward(grad_in, scaled, inverse, gain):
    grad_scaled = grad_in * gain
    return inverse * (
        grad_scaled
        - jnp.mean(grad_scaled, axis=1, keepdims=True)
        - scaled * jnp.mean(grad_scaled * scaled, axis=1, keepdims=True)
    )


def segment_mean(inputs):
    rows, width = inputs.shape
    return jnp.mean(inputs.reshape(rows // SEG_LEN, SEG_LEN, width), axis=1)


def segment_spread(rows, width, per_segment):
    segs = rows // SEG_LEN
    return jnp.broadcast_to(per_segment[:, None, :], (segs, SEG_LEN, width)).reshape(rows, width)


def identity(size):
    row = lax.broadcasted_iota(jnp.int32, (size, size), 0)
    col = lax.broadcasted_iota(jnp.int32, (size, size), 1)
    return (row == col).astype(F32).astype(BF16)


class Sizes:
    def __init__(self, rows, width, ff, with_summary):
        self.rows = rows
        self.width = width
        self.ff = ff
        self.segs = rows // SEG_LEN
        self.top = TILE if with_summary else 0
        self.keys = rows + RIGHT_ROWS + LEFT_ROWS + MEM_ROWS
        self.ext = self.top + self.keys
        self.queries = self.top + rows
        self.right_at = self.top + rows
        self.left_at = self.right_at + RIGHT_ROWS
        self.mem_at = self.left_at + LEFT_ROWS
        self.pairs = width // LANES


class Matrices:
    def __init__(self, width, ff):
        self.qkv = (CHIPS_Z, CHIPS_Y, 3 * width // BLOCKS, width)
        self.out = (CHIPS_Z, CHIPS_Y, width // BLOCKS, width)
        self.up = (CHIPS_Z, CHIPS_Y, ff // BLOCKS, width)
        self.down = (CHIPS_Z, CHIPS_Y, width // BLOCKS, ff)
        self.down_parts = ff // width
        self.attn_rows = self.qkv[2] + self.out[2]
        self.ffn_rows = self.up[2] + self.down_parts * self.down[2]


class Spots:
    def __init__(self, mats):
        high, wide, up, low = mats.qkv[2], mats.out[2], mats.up[2], mats.down[2]
        self.qkv = (0, 0)
        self.out = (0, high)
        self.up = (0, high + wide)
        self.down = [(0, high + wide + up + low * part) for part in range(mats.down_parts)]


def attn_pairs(mats, spots, groups, qkv_ref, out_ref, place_ref):
    if spots is None:
        return [(groups[0], qkv_ref), (groups[1], out_ref)]
    pairs = []
    for k in range(len(groups[0])):
        row = place_ref[2 + 2 * k]
        lane = pl.multiple_of(place_ref[3 + 2 * k], LANES)
        for (group, first), ref, shape in (
            (spots.qkv, qkv_ref, mats.qkv),
            (spots.out, out_ref, mats.out),
        ):
            block = groups[group][k]
            pairs.append(
                (
                    block.at[:, pl.ds(first, shape[2]), :],
                    ref.at[:, row, :, pl.ds(lane, LANES)],
                )
            )
    return pairs


def ffn_pairs(mats, spots, groups, up_ref, down_ref, place_ref):
    if spots is None:
        return [(groups[2], up_ref), (groups[3], down_ref)]
    pairs = []
    for k in range(len(groups[0])):
        row = place_ref[2 + 2 * k]
        lane = pl.multiple_of(place_ref[3 + 2 * k], LANES)
        group, first = spots.up
        block = groups[group][k]
        pairs.append(
            (block.at[:, pl.ds(first, mats.up[2]), :], up_ref.at[:, row, :, pl.ds(lane, LANES)])
        )
        for part, (group, first) in enumerate(spots.down):
            there = pl.multiple_of(
                place_ref[3 + 2 * k] * mats.down_parts + part * LANES, LANES
            )
            block = groups[group][k]
            pairs.append(
                (
                    block.at[:, pl.ds(first, mats.down[2]), :],
                    down_ref.at[:, row, :, pl.ds(there, LANES)],
                )
            )
    return pairs


def start_in(pairs, sems, at):
    copies = [pltpu.make_async_copy(s, d, sems.at[at + i]) for i, (s, d) in enumerate(pairs)]
    for copy in copies:
        copy.start()
    return copies


def start_out(pairs, sems, at):
    copies = [pltpu.make_async_copy(d, s, sems.at[at + i]) for i, (s, d) in enumerate(pairs)]
    for copy in copies:
        copy.start()
    return copies


def in_groups(spots, refs):
    return refs if spots is None else [refs]


def wait_all(copies):
    for copy in copies:
        copy.wait()


def fill_mask(sizes, seqs, starts_ref, place_ref, mask_ref):
    shape = (sizes.keys, 2 * sizes.queries)
    key = lax.broadcasted_iota(jnp.int32, shape, 0)
    col = lax.broadcasted_iota(jnp.int32, shape, 1)
    col = jnp.where(col < sizes.queries, col, col - sizes.queries)
    base = place_ref[0]
    total = place_ref[1]
    query = jnp.where(col < sizes.top, col, lax.shift_right_arithmetic(col - sizes.top, 4))
    left_at = sizes.rows + RIGHT_ROWS
    mem_at = left_at + LEFT_ROWS
    spot = jnp.where(key < left_at, key, key - mem_at)
    mem_seg = jnp.where(key < mem_at + sizes.segs, key - mem_at, key - mem_at - 2 * sizes.segs)
    key_seg = jnp.where(key < mem_at, lax.shift_right_arithmetic(spot, 4), mem_seg)
    near = (
        (key_seg == query)
        | ((spot >= query * SEG_LEN - LEFT_LEN) & (spot < query * SEG_LEN))
        | ((key_seg == query + 1) & (spot < query * SEG_LEN + SEG_LEN + RIGHT_LEN))
    )
    recent = (key_seg >= query - MEM_LEN) & (key_seg < query) & (col >= sizes.top)
    allowed = ((key < mem_at) & near) | ((key >= mem_at) & recent)
    key_abs = key_seg + base
    query_abs = query + base
    allowed = allowed & (key_abs >= 0) & (key_abs < total)
    if sizes.top:
        allowed = allowed & ((col < sizes.segs) | (col >= sizes.top))
    for n in range(seqs):
        key_owner = jnp.zeros(shape, jnp.int32)
        query_owner = jnp.zeros(shape, jnp.int32)
        for u in range(starts_ref.shape[1]):
            first = starts_ref[n, u]
            key_owner = key_owner + (key_abs >= first).astype(jnp.int32)
            query_owner = query_owner + (query_abs >= first).astype(jnp.int32)
        mask_ref[n] = jnp.where(allowed & (key_owner == query_owner), 0.0, -1e30)


def half_masks():
    lane = lax.broadcasted_iota(jnp.int32, (1, LANES), 1)
    even = (lane < LANES // 2).astype(F32)
    return even.astype(BF16), (1.0 - even).astype(BF16), lane < LANES // 2


def project(sizes, z_ref, qkv_ref, row_bias_ref, proj_ref):
    step = CHIPS_Z // 2
    for c in range(2):
        block = qkv_ref[pl.ds(c * step, step)].reshape(-1, sizes.width)
        wide = block.shape[0]
        made = nt(z_ref[...], block) + row_bias_ref[:, pl.ds(c * wide, wide)]
        proj_ref[:, pl.ds(c * wide, wide)] = made.astype(BF16)


def attend(sizes, seqs, proj_ref, mask_ref, probs_ref, att_ref):
    even, odd, is_even = half_masks()
    scale = (sizes.width // HEADS) ** (-0.5)
    count = sizes.queries

    def body(p, carry):
        for n in range(seqs):
            lane = pl.multiple_of(p * LANES, LANES)
            query = proj_ref[pl.ds(n * sizes.ext, count), pl.ds(lane, LANES)]
            first = n * sizes.ext + sizes.top
            key = proj_ref[pl.ds(first, sizes.keys), pl.ds(sizes.width + lane, LANES)]
            value = proj_ref[pl.ds(first, sizes.keys), pl.ds(2 * sizes.width + lane, LANES)]
            queries = jnp.concatenate([query * even, query * odd], axis=0)
            scores = nt(key, queries) * scale + mask_ref[n]
            scores = jnp.exp(scores - jnp.max(scores, axis=0, keepdims=True))
            probs = (scores * (1.0 / jnp.sum(scores, axis=0, keepdims=True))).astype(BF16)
            probs_ref[n * sizes.pairs + p] = probs
            out = tn(probs, value)
            att_ref[pl.ds(n * count, count), pl.ds(lane, LANES)] = jnp.where(
                is_even, out[:count], out[count:]
            ).astype(BF16)
        return carry

    lax.fori_loop(0, sizes.pairs, body, 0, unroll=True)


def attend_back(sizes, seqs, proj_ref, probs_ref, go_ref, gproj_ref):
    even, odd, is_even = half_masks()
    scale = (sizes.width // HEADS) ** (-0.5)
    count = sizes.queries
    wide = sizes.width
    for n in range(seqs):
        base = n * sizes.ext
        rest = sizes.ext - count
        gproj_ref[pl.ds(base + count, rest), pl.ds(0, wide)] = jnp.zeros((rest, wide), BF16)
        if sizes.top:
            gproj_ref[pl.ds(base, sizes.top), pl.ds(wide, 2 * wide)] = jnp.zeros(
                (sizes.top, 2 * wide), BF16
            )

    def body(p, carry):
        for n in range(seqs):
            lane = pl.multiple_of(p * LANES, LANES)
            base = n * sizes.ext
            first = base + sizes.top
            query = proj_ref[pl.ds(base, count), pl.ds(lane, LANES)]
            key = proj_ref[pl.ds(first, sizes.keys), pl.ds(wide + lane, LANES)]
            value = proj_ref[pl.ds(first, sizes.keys), pl.ds(2 * wide + lane, LANES)]
            grad = go_ref[pl.ds(n * count, count), pl.ds(lane, LANES)]
            queries = jnp.concatenate([query * even, query * odd], axis=0)
            grads = jnp.concatenate([grad * even, grad * odd], axis=0)
            probs_low = probs_ref[n * sizes.pairs + p]
            grad_values = nn(probs_low, grads)
            probs = probs_low.astype(F32)
            weighted = nt(value, grads) * probs
            grad_scores = (
                (weighted - probs * jnp.sum(weighted, axis=0, keepdims=True)) * scale
            ).astype(BF16)
            grad_keys = nn(grad_scores, queries)
            grad_both = tn(grad_scores, key)
            grad_query = jnp.where(is_even, grad_both[:count], grad_both[count:])
            gproj_ref[pl.ds(base, count), pl.ds(lane, LANES)] = grad_query.astype(BF16)
            gproj_ref[pl.ds(first, sizes.keys), pl.ds(wide + lane, LANES)] = grad_keys.astype(BF16)
            gproj_ref[pl.ds(first, sizes.keys), pl.ds(2 * wide + lane, LANES)] = (
                grad_values.astype(BF16)
            )
        return carry

    lax.fori_loop(0, sizes.pairs, body, 0)


def gelu_both(upward):
    half = 0.5 * (1.0 + lax.erf(upward * ROOT_HALF))
    slope = half + upward * jnp.exp(-0.5 * upward * upward) * INV_ROOT_TWO_PI
    return upward * half, slope


def up_block(up_ref, c, wide):
    step = wide // (up_ref.shape[1] * up_ref.shape[2])
    return up_ref[pl.ds(c * step, step)].reshape(-1, up_ref.shape[3])


def down_block(down_ref, c, wide):
    at = pl.multiple_of(c * wide, wide)
    return down_ref[:, :, :, pl.ds(at, wide)].reshape(-1, wide)


def ffn_back_step(
    sizes, c, wide, grad_low, hidden_low, active, slope, up_ref, down_ref, gup_ref, gdown_ref, vec
):
    at = pl.multiple_of(c * wide, wide)
    up = up_block(up_ref, c, wide)
    down = down_block(down_ref, c, wide)
    grad_active = nn(grad_low, down)
    grad_up_f = grad_active * slope
    grad_up = grad_up_f.astype(BF16)
    gdown_ref[:, :, :, pl.ds(at, wide)] = (
        tn(grad_low, active).astype(BF16).reshape(gdown_ref.shape[:3] + (wide,))
    )
    step = wide // (gup_ref.shape[1] * gup_ref.shape[2])
    gup_ref[pl.ds(c * step, step)] = (
        tn(grad_up, hidden_low).astype(BF16).reshape((step,) + gup_ref.shape[1:])
    )
    vec[pl.ds(8 + c, 1), :] = col_sum(grad_up.astype(F32))
    return nn(grad_up, up)


def attn_back_stage(
    sizes, seqs, gz, grad_mem_ref, att_ref, proj_ref, probs_ref, z_ref, qkv_ref, out_ref,
    gqkv_ref, gout_ref, go_ref, gproj_ref, branch_ref, vec, gh_ref, gmem_ref, back_left_ref,
    back_right_ref, scaled_rows=None,
):
    wide = sizes.width
    count = sizes.queries
    bias_out = col_sum(gz)
    for n in range(seqs):
        if sizes.top:
            mem_grad = grad_mem_ref[pl.ds(n * sizes.segs, sizes.segs), :]
            bias_out = bias_out + col_sum(mem_grad)
            branch_ref[pl.ds(n * count, sizes.top), :] = jnp.concatenate(
                [mem_grad, jnp.zeros((sizes.top - sizes.segs, wide), F32)], axis=0
            ).astype(BF16)
        branch_ref[pl.ds(n * count + sizes.top, sizes.rows), :] = gz[
            n * sizes.rows : (n + 1) * sizes.rows
        ].astype(BF16)
    vec[pl.ds(5, 1), :] = bias_out
    branch = branch_ref[...]
    gout_ref[...] = tn(branch, att_ref[...]).astype(BF16).reshape(gout_ref.shape)
    go_ref[...] = nn(branch, out_ref[...].reshape(-1, wide)).astype(BF16)
    attend_back(sizes, seqs, proj_ref, probs_ref, go_ref, gproj_ref)
    vec[pl.ds(3, 1), :] = col_sum(gproj_ref[:, pl.ds(0, wide)].astype(F32))
    vec[pl.ds(4, 1), :] = col_sum(gproj_ref[:, pl.ds(2 * wide, wide)].astype(F32))
    grad_ext = nn(gproj_ref[...], qkv_ref[...].reshape(-1, wide))
    gain_sum = jnp.zeros((1, wide), F32)
    bias_sum = jnp.zeros((1, wide), F32)
    for n in range(seqs):
        base = n * sizes.ext
        own = grad_ext[base + sizes.top : base + sizes.top + sizes.rows]
        if sizes.top:
            spread = grad_ext[base : base + sizes.segs] * (1.0 / SEG_LEN)
            own = own + segment_spread(sizes.rows, wide, spread)
        gh_ref[pl.ds(n * sizes.rows, sizes.rows), :] = own
        mem = base + sizes.mem_at
        gmem_ref[pl.ds(n * sizes.segs, sizes.segs), :] = grad_ext[mem : mem + sizes.segs]
        left = base + sizes.left_at
        back_left_ref[n] = grad_ext[left : left + BACK_ROWS].astype(BF16)
        right = base + sizes.right_at
        back_right_ref[n] = grad_ext[right : right + RIGHT_ROWS].astype(BF16)
        if scaled_rows is not None:
            grads = (
                own,
                grad_ext[right : right + RIGHT_ROWS],
                grad_ext[left : left + LEFT_ROWS],
            )
            for rows, scaled in zip(grads, scaled_rows(n)):
                gain_sum = gain_sum + col_sum(rows * scaled)
                bias_sum = bias_sum + col_sum(rows)
    if scaled_rows is not None:
        vec[pl.ds(0, 1), :] = gain_sum
        vec[pl.ds(2, 1), :] = bias_sum
    step = CHIPS_Z // 2
    part = gqkv_ref.shape[1] * gqkv_ref.shape[2] * step
    for c in range(2):
        gqkv_ref[pl.ds(c * step, step)] = (
            tn(gproj_ref[:, pl.ds(c * part, part)], z_ref[...])
            .astype(BF16)
            .reshape((step,) + gqkv_ref.shape[1:])
        )


def merge_halo(sizes, n, gh_ref, gmem_ref, from_right_ref, from_left_ref):
    first = n * sizes.rows
    back = from_right_ref[n].astype(F32)
    head = gh_ref[pl.ds(first, RIGHT_ROWS), :] + from_left_ref[n].astype(F32)
    middle = gh_ref[pl.ds(first + RIGHT_ROWS, sizes.rows - RIGHT_ROWS - LEFT_ROWS), :]
    tail = gh_ref[pl.ds(first + sizes.rows - LEFT_ROWS, LEFT_ROWS), :] + back[:LEFT_ROWS]
    mem = gmem_ref[pl.ds(n * sizes.segs, sizes.segs), :] + back[LEFT_ROWS + sizes.segs :]
    return jnp.concatenate([head, middle, tail], axis=0), mem


def pack_kernel(spots, qkv_ref, out_ref, up_ref, down_ref, *packed):
    eye = identity(LANES)
    high, wide, low = qkv_ref.shape[1], out_ref.shape[1], down_ref.shape[1]
    for layer, ref in enumerate(packed):
        up = tn(up_ref[layer], eye).astype(BF16)
        for z in range(ref.shape[0]):
            ref[z, pl.ds(spots.qkv[1], high), :] = qkv_ref[layer]
            ref[z, pl.ds(spots.out[1], wide), :] = out_ref[layer]
            ref[z, pl.ds(spots.up[1], up_ref.shape[2]), :] = up
            for part, (_, first) in enumerate(spots.down):
                ref[z, pl.ds(first, low), :] = down_ref[layer, :, pl.ds(part * LANES, LANES)]


def unpack_layer(spots, sources, refs):
    qkv_ref, out_ref, up_ref, down_ref = refs
    high, wide, low = qkv_ref.shape[0], out_ref.shape[0], down_ref.shape[0]

    def total(first, rows):
        parts = [ref[z, pl.ds(first, rows), :] for ref in sources for z in range(ref.shape[0])]
        value = parts[0].astype(F32)
        for part in parts[1:]:
            value = value + part.astype(F32)
        return value

    qkv_ref[...] = total(spots.qkv[1], high)
    out_ref[...] = total(spots.out[1], wide)
    up_ref[...] = nt(identity(LANES), total(spots.up[1], up_ref.shape[1]).astype(BF16))
    for part, (_, first) in enumerate(spots.down):
        down_ref[:, pl.ds(part * LANES, LANES)] = total(first, low)
    return total


def store_layer(layer, held, outs, sems):
    copies = [
        pltpu.make_async_copy(ref, out.at[layer], sems.at[i])
        for i, (ref, out) in enumerate(zip(held, outs))
    ]
    for copy in copies:
        copy.start()
    return copies


def unpack_last_kernel(spots, layer, lines_ref, first_ref, *refs):
    outs, held, sems = refs[:4], refs[4:8], refs[8]
    unpack_layer(spots, (lines_ref, first_ref), held)
    wait_all(store_layer(layer, held, outs, sems))


def unpack_first_kernel(spots, small_at, parts_ref, *refs):
    outs, (gains_ref, biases_ref, ffn_bias_ref), held, sems = (
        refs[4:8], refs[8:11], refs[11:15], refs[15],
    )
    total = unpack_layer(spots, (parts_ref,), held)
    copies = store_layer(0, held, outs, sems)
    sums = total(small_at, SMALL_ROWS)
    parts = gains_ref.shape[2] // LANES
    for layer in range(gains_ref.shape[0]):
        for part in range(parts):
            lanes = pl.ds(part * LANES, LANES)
            block = sums[(layer * parts + part) * TILE : (layer * parts + part + 1) * TILE]
            gains_ref[layer, :, lanes] = block[0:2]
            for row in range(biases_ref.shape[0]):
                biases_ref[row, pl.ds(layer, 1), lanes] = block[2 + row : 3 + row]
            for row in range(ffn_bias_ref.shape[1] // gains_ref.shape[2]):
                at = row * gains_ref.shape[2] + part * LANES
                ffn_bias_ref[pl.ds(layer, 1), pl.ds(at, LANES)] = block[8 + row : 9 + row]
    wait_all(copies)


def near_small_kernel(count, held_ref, first_ref, out_ref):
    rows = out_ref.shape[1] - SMALL_ROWS

    def total(at, size):
        group = pl.ds(at, size)
        return (held_ref[group, :].astype(F32) + first_ref[group, :].astype(F32)).astype(BF16)

    small = total(count * rows, SMALL_ROWS)
    for z in range(count):
        out_ref[z, pl.ds(0, rows), :] = total(z * rows, rows)
        out_ref[z, pl.ds(rows, SMALL_ROWS), :] = small


def first_layer_kernel(
    sizes, seqs, mats, spots, count_in, place_ref, starts_ref, frames_ref, left_ref, right_ref,
    gains_ref, biases_ref, ffn_bias_ref, row_bias_ref, *refs
):
    groups = in_groups(spots, refs[:count_in])
    (
        z_ref, proj_ref, probs_ref, att_ref, mixed_ref, mem_ref, next_ref, active_ref, slope_ref,
        low_ref, send_right_ref, send_left_ref, qkv_ref, out_ref, up_ref, down_ref, mask_ref,
        hidden_ref, sems,
    ) = refs[count_in:]
    wide = sizes.width
    copies = start_in(attn_pairs(mats, spots, groups, qkv_ref, out_ref, place_ref), sems, 0)
    ffn_copies = start_in(
        ffn_pairs(mats, spots, groups, up_ref, down_ref, place_ref), sems, len(copies)
    )
    gain = gains_ref[0, pl.ds(0, 1), :]
    bias = biases_ref[0, pl.ds(0, 1), :]
    pad = jnp.zeros((TILE - sizes.segs, wide), F32)
    for n in range(seqs):
        own = frames_ref[n].astype(F32)
        before = left_ref[n].astype(F32)
        hidden = norm_forward(own, gain, bias)[0]
        halo = norm_forward(before[before.shape[0] - LEFT_ROWS :], gain, bias)[0]
        after = norm_forward(right_ref[n].astype(F32), gain, bias)[0]
        memory = jnp.concatenate(
            [
                segment_mean(own),
                jnp.zeros((sizes.segs - before.shape[0] // SEG_LEN, wide), F32),
                segment_mean(before),
            ],
            axis=0,
        )
        base = n * sizes.ext
        z_ref[pl.ds(base, sizes.top), :] = jnp.concatenate(
            [segment_mean(hidden), pad], axis=0
        ).astype(BF16)
        z_ref[pl.ds(base + sizes.top, sizes.rows), :] = hidden.astype(BF16)
        z_ref[pl.ds(base + sizes.right_at, RIGHT_ROWS), :] = after.astype(BF16)
        z_ref[pl.ds(base + sizes.left_at, LEFT_ROWS), :] = halo.astype(BF16)
        z_ref[pl.ds(base + sizes.mem_at, MEM_ROWS), :] = memory.astype(BF16)
    fill_mask(sizes, seqs, starts_ref, place_ref, mask_ref)
    wait_all(copies)
    project(sizes, z_ref, qkv_ref, row_bias_ref, proj_ref)
    attend(sizes, seqs, proj_ref, mask_ref, probs_ref, att_ref)
    mixed = nt(att_ref[...], out_ref[...].reshape(-1, wide)) + biases_ref[3, pl.ds(0, 1), :]
    for n in range(seqs):
        base = n * sizes.queries
        mem_ref[pl.ds(n * sizes.segs, sizes.segs), :] = mixed[base : base + sizes.segs]
        mixed_ref[pl.ds(n * sizes.rows, sizes.rows), :] = (
            frames_ref[n].astype(F32) + mixed[base + sizes.top : base + sizes.top + sizes.rows]
        )
    mixed = mixed_ref[...]
    hidden, _, _ = norm_forward(mixed, gains_ref[0, pl.ds(1, 1), :], biases_ref[4, pl.ds(0, 1), :])
    hidden_ref[...] = hidden.astype(BF16)
    next_ref[...] = mixed + biases_ref[5, pl.ds(0, 1), :]
    wait_all(ffn_copies)

    def body(c, carry):
        at_lane = pl.multiple_of(c * wide, wide)
        upward = nt(hidden_ref[...], up_block(up_ref, c, wide))
        upward = upward + ffn_bias_ref[pl.ds(0, 1), pl.ds(at_lane, wide)]
        active, slope = gelu_both(upward)
        active = active.astype(BF16)
        active_ref[:, pl.ds(at_lane, wide)] = active
        slope_ref[:, pl.ds(at_lane, wide)] = slope.astype(BF16)
        next_ref[...] += nt(active, down_block(down_ref, c, wide))
        return carry

    lax.fori_loop(0, sizes.ff // wide, body, 0)
    low, _, _ = norm_forward(
        next_ref[...], gains_ref[1, pl.ds(0, 1), :], biases_ref[0, pl.ds(1, 1), :]
    )
    low = low.astype(BF16)
    low_ref[...] = low
    for n in range(seqs):
        base = n * sizes.rows
        send_right_ref[n, pl.ds(0, LEFT_ROWS), :] = low[
            base + sizes.rows - LEFT_ROWS : base + sizes.rows
        ]
        send_right_ref[n, pl.ds(LEFT_ROWS, MEM_ROWS), :] = jnp.concatenate(
            [
                mem_ref[pl.ds(n * sizes.segs, sizes.segs), :],
                jnp.zeros((MEM_ROWS - sizes.segs, wide), F32),
            ],
            axis=0,
        ).astype(BF16)
        send_left_ref[n] = low[base : base + RIGHT_ROWS]


def last_layer_kernel(
    sizes, seqs, mats, spots, count_in, count_out, place_ref, starts_ref, low_ref, left_ref,
    right_ref, mem_ref, inputs_ref, out_grad_ref, gains_ref, biases_ref, ffn_bias_ref,
    row_bias_ref, *refs
):
    groups = in_groups(spots, refs[:count_in])
    (encoded_ref, gz_ref, gh_ref, gmem_ref, back_left_ref, back_right_ref, vec) = refs[
        count_in : count_in + 7
    ]
    hbm_out = refs[count_in + 7 : count_in + 7 + count_out]
    (
        qkv_ref, out_ref, up_ref, down_ref, gqkv_ref, gout_ref, gup_ref, gdown_ref, mask_ref,
        z_ref, proj_ref, probs_ref, att_ref, hidden_ref, go_ref, gproj_ref, branch_ref,
        grad_low_ref, grad_hidden_ref, sems,
    ) = refs[count_in + 7 + count_out :]
    outs_to = hbm_out
    if spots is not None:
        rows = mats.attn_rows + mats.ffn_rows
        outs_to = [
            [
                ref.at[hop2, :, pl.ds(hop1 * rows, rows), :]
                for ref in hbm_out
                for hop2 in range(2)
                for hop1 in range(2)
            ]
        ]
    wide = sizes.width
    attn_copies = start_in(attn_pairs(mats, spots, groups, qkv_ref, out_ref, place_ref), sems, 0)
    ffn_copies = start_in(
        ffn_pairs(mats, spots, groups, up_ref, down_ref, place_ref), sems, len(attn_copies)
    )
    vec[...] = jnp.zeros_like(vec)
    for n in range(seqs):
        base = n * sizes.ext
        z_ref[pl.ds(base, sizes.rows), :] = low_ref[pl.ds(n * sizes.rows, sizes.rows), :]
        z_ref[pl.ds(base + sizes.right_at, RIGHT_ROWS), :] = right_ref[n]
        z_ref[pl.ds(base + sizes.left_at, LEFT_ROWS), :] = left_ref[n, pl.ds(0, LEFT_ROWS), :]
        memory = jnp.concatenate(
            [
                mem_ref[pl.ds(n * sizes.segs, sizes.segs), :],
                left_ref[n, pl.ds(LEFT_ROWS, MEM_ROWS), :].astype(F32)[: sizes.segs],
            ],
            axis=0,
        )
        z_ref[pl.ds(base + sizes.mem_at, MEM_ROWS), :] = memory.astype(BF16)
        grad_low_ref[pl.ds(n * sizes.rows, sizes.rows), :] = out_grad_ref[n]
    fill_mask(sizes, seqs, starts_ref, place_ref, mask_ref)
    wait_all(attn_copies)
    project(sizes, z_ref, qkv_ref, row_bias_ref, proj_ref)
    attend(sizes, seqs, proj_ref, mask_ref, probs_ref, att_ref)
    mixed = (
        inputs_ref[...]
        + nt(att_ref[...], out_ref[...].reshape(-1, wide))
        + biases_ref[3, pl.ds(1, 1), :]
    )
    gain = gains_ref[1, pl.ds(1, 1), :]
    hidden, scaled, inverse = norm_forward(mixed, gain, biases_ref[4, pl.ds(1, 1), :])
    hidden_ref[...] = hidden.astype(BF16)
    for n in range(seqs):
        encoded_ref[n] = mixed[n * sizes.rows : (n + 1) * sizes.rows] + biases_ref[5, pl.ds(1, 1), :]
    grad_hidden_ref[...] = jnp.zeros_like(grad_hidden_ref)
    wait_all(ffn_copies)

    def body(c, carry):
        at_lane = pl.multiple_of(c * wide, wide)
        upward = nt(hidden_ref[...], up_block(up_ref, c, wide))
        upward = upward + ffn_bias_ref[pl.ds(1, 1), pl.ds(at_lane, wide)]
        active, slope = gelu_both(upward)
        active = active.astype(BF16)
        made = nt(active, down_block(down_ref, c, wide))
        for n in range(seqs):
            encoded_ref[n] += made[n * sizes.rows : (n + 1) * sizes.rows]
        grad_hidden_ref[...] += ffn_back_step(
            sizes, c, wide, grad_low_ref[...], hidden_ref[...], active, slope, up_ref, down_ref,
            gup_ref, gdown_ref, vec,
        )
        return carry

    lax.fori_loop(0, sizes.ff // wide, body, 0)
    out_at = len(attn_copies) + len(ffn_copies)
    outs = start_out(
        ffn_pairs(mats, spots, outs_to, gup_ref, gdown_ref, place_ref), sems, out_at
    )
    grad = grad_low_ref[...].astype(F32)
    grad_hidden = grad_hidden_ref[...]
    vec[pl.ds(1, 1), :] = col_sum(grad_hidden * scaled)
    vec[pl.ds(6, 1), :] = col_sum(grad_hidden)
    vec[pl.ds(7, 1), :] = col_sum(grad)
    gz = grad + norm_backward(grad_hidden, scaled, inverse, gain)
    gz_ref[...] = gz
    attn_back_stage(
        sizes, seqs, gz, None, att_ref, proj_ref, probs_ref, z_ref, qkv_ref, out_ref, gqkv_ref,
        gout_ref, go_ref, gproj_ref, branch_ref, vec, gh_ref, gmem_ref, back_left_ref,
        back_right_ref,
    )
    outs = outs + start_out(
        attn_pairs(mats, spots, outs_to, gqkv_ref, gout_ref, place_ref),
        sems,
        out_at + len(outs),
    )
    wait_all(outs)


def first_back_kernel(
    last, sizes, seqs, mats, spots, count_in, count_out, place_ref, inputs_ref, gz_in_ref,
    gh_in_ref, gmem_in_ref, from_right_ref, from_left_ref, mixed_ref, active_ref, slope_ref,
    att_ref, probs_ref, proj_ref, z_ref, frames_ref, left_ref, right_ref, gains_ref, biases_ref,
    last_vec, *refs
):
    groups = in_groups(spots, refs[:count_in])
    gz_ref, gh_ref, gmem_ref, back_left_ref, back_right_ref, upper_vec, vec = refs[
        count_in : count_in + 7
    ]
    refs = refs[count_in + 7 :]
    hbm_out = refs[:count_out]
    (
        qkv_ref, out_ref, up_ref, down_ref, gqkv_ref, gout_ref, gup_ref, gdown_ref, hidden_ref,
        grad_low_ref, grad_ref, grad_hidden_ref, grad_mem_ref, go_ref, gproj_ref, branch_ref,
        small_ref, sems,
    ) = refs[count_out:]
    wide = sizes.width
    small = []
    outs_to = hbm_out
    if spots is not None:
        rows = mats.attn_rows + mats.ffn_rows
        end = CHIPS_Z * rows
        each = [
            ref.at[hop2, hop1] for ref in hbm_out for hop2 in range(2) for hop1 in range(2)
        ]
        small = [ref.at[pl.ds(end, SMALL_ROWS), :] for ref in each]
        outs_to = [[ref.at[pl.ds(0, end), :].reshape(CHIPS_Z, rows, LANES) for ref in each]]
    ffn_copies = start_in(ffn_pairs(mats, spots, groups, up_ref, down_ref, place_ref), sems, 0)
    attn_copies = start_in(
        attn_pairs(mats, spots, groups, qkv_ref, out_ref, place_ref), sems, len(ffn_copies)
    )
    vec[...] = jnp.zeros_like(vec)
    upper_vec[...] = jnp.zeros_like(upper_vec)
    gain = gains_ref[1, pl.ds(0, 1), :]
    gain_sum = jnp.zeros((1, wide), F32)
    bias_sum = jnp.zeros((1, wide), F32)
    for n in range(seqs):
        rows = pl.ds(n * sizes.rows, sizes.rows)
        _, scaled, inverse = norm_forward(
            inputs_ref[rows, :], gain, biases_ref[0, pl.ds(1, 1), :]
        )
        total, mem = merge_halo(last, n, gh_in_ref, gmem_in_ref, from_right_ref, from_left_ref)
        gain_sum = gain_sum + col_sum(total * scaled)
        bias_sum = bias_sum + col_sum(total)
        grad = gz_in_ref[rows, :] + norm_backward(total, scaled, inverse, gain)
        grad_ref[rows, :] = grad
        grad_low_ref[rows, :] = grad.astype(BF16)
        grad_mem_ref[pl.ds(n * sizes.segs, sizes.segs), :] = mem
    upper_vec[pl.ds(0, 1), :] = gain_sum
    upper_vec[pl.ds(2, 1), :] = bias_sum
    gain = gains_ref[0, pl.ds(1, 1), :]
    hidden, scaled, inverse = norm_forward(
        mixed_ref[...], gain, biases_ref[4, pl.ds(0, 1), :]
    )
    hidden_ref[...] = hidden.astype(BF16)
    grad_hidden_ref[...] = jnp.zeros_like(grad_hidden_ref)
    wait_all(ffn_copies)

    def body(c, carry):
        at_lane = pl.multiple_of(c * wide, wide)
        grad_hidden_ref[...] += ffn_back_step(
            sizes, c, wide, grad_low_ref[...], hidden_ref[...],
            active_ref[:, pl.ds(at_lane, wide)], slope_ref[:, pl.ds(at_lane, wide)].astype(F32),
            up_ref, down_ref, gup_ref, gdown_ref, vec,
        )
        return carry

    lax.fori_loop(0, sizes.ff // wide, body, 0)
    out_at = len(ffn_copies) + len(attn_copies)
    outs = start_out(
        ffn_pairs(mats, spots, outs_to, gup_ref, gdown_ref, place_ref), sems, out_at
    )
    grad_hidden = grad_hidden_ref[...]
    grad = grad_ref[...]
    vec[pl.ds(1, 1), :] = col_sum(grad_hidden * scaled)
    vec[pl.ds(6, 1), :] = col_sum(grad_hidden)
    vec[pl.ds(7, 1), :] = col_sum(grad)
    gz = grad + norm_backward(grad_hidden, scaled, inverse, gain)
    gz_ref[...] = gz

    def scaled_rows(n):
        before = left_ref[n, pl.ds(left_ref.shape[1] - LEFT_ROWS, LEFT_ROWS), :]
        parts = (frames_ref[n], right_ref[n], before)
        first_gain = gains_ref[0, pl.ds(0, 1), :]
        first_bias = biases_ref[0, pl.ds(0, 1), :]
        return [norm_forward(part.astype(F32), first_gain, first_bias)[1] for part in parts]

    wait_all(attn_copies)
    attn_back_stage(
        sizes, seqs, gz, grad_mem_ref, att_ref, proj_ref, probs_ref, z_ref, qkv_ref, out_ref,
        gqkv_ref, gout_ref, go_ref, gproj_ref, branch_ref, vec, gh_ref, gmem_ref, back_left_ref,
        back_right_ref, scaled_rows,
    )
    outs = outs + start_out(
        attn_pairs(mats, spots, outs_to, gqkv_ref, gout_ref, place_ref),
        sems,
        out_at + len(outs),
    )
    parts = sizes.width // LANES
    for layer, total in enumerate((vec[...], last_vec[...] + upper_vec[...])):
        for part in range(parts):
            small_ref[pl.ds((layer * parts + part) * TILE, TILE), :] = total[
                :, part * LANES : (part + 1) * LANES
            ].astype(BF16)
    outs = outs + start_out([(ref, small_ref) for ref in small], sems, out_at + len(outs))
    wait_all(outs)


def frames_grad_kernel(
    sizes, seqs, frames_ref, gz_ref, gh_ref, gmem_ref, from_right_ref, from_left_ref, gains_ref,
    biases_ref, grad_ref
):
    gain = gains_ref[0, pl.ds(0, 1), :]
    for n in range(seqs):
        _, scaled, inverse = norm_forward(
            frames_ref[n].astype(F32), gain, biases_ref[0, pl.ds(0, 1), :]
        )
        total, mem = merge_halo(sizes, n, gh_ref, gmem_ref, from_right_ref, from_left_ref)
        grad_ref[n] = (
            gz_ref[pl.ds(n * sizes.rows, sizes.rows), :]
            + norm_backward(total, scaled, inverse, gain)
            + segment_spread(sizes.rows, sizes.width, mem * (1.0 / SEG_LEN))
        )


def shifted(value, axis, by):
    size = lax.axis_size(axis)
    pairs = [(i, i + by) for i in range(size) if 0 <= i + by < size]
    return lax.ppermute(value, axis, pairs)


def permuted(value, move):
    reps = lax.axis_size("rep")
    pairs = []
    for flat in range(lax.axis_size("seg") * reps):
        seg, rep = divmod(flat, reps)
        z, y, x, core = move(seg // CHIPS_Y, seg % CHIPS_Y, rep // 2, rep % 2)
        pairs.append((flat, (z * CHIPS_Y + y) * reps + 2 * x + core))
    return lax.ppermute(value, ("seg", "rep"), pairs)


def across_first(value):
    return permuted(value, lambda z, y, x, c: (z, y, x ^ 1, c) if c == 0 else (z, y ^ 1, x, c))


def across_second(value):
    return permuted(value, lambda z, y, x, c: (z, y ^ 1, x, c) if c == 0 else (z, y, x ^ 1, c))


def other_core(value):
    return permuted(value, lambda z, y, x, c: (z, y, x, c ^ 1))


def after(value, *others):
    return lax.optimization_barrier((value,) + others)[0]


def swap_z(blocks):
    groups = [
        [z * CHIPS_Y + y for z in range(CHIPS_Z)] for y in range(CHIPS_Y)
    ]
    return lax.all_to_all(blocks, "seg", 0, 0, axis_index_groups=groups, tiled=True)


def gather_sides(here):
    return [here, across_first(here), across_second(here)]


def both_cores(blocks):
    return blocks + [other_core(block) for block in blocks]


def summed(*parts):
    total = parts[0].astype(F32)
    for part in parts[1:]:
        total = total + part.astype(F32)
    return total.astype(BF16)


def sum_everywhere(value):
    count = lax.axis_size("seg") * lax.axis_size("rep")
    bit = 1
    while bit < count:
        value = value + lax.ppermute(value, ("seg", "rep"), [(i, i ^ bit) for i in range(count)])
        bit *= 2
    return value


def vmem_spec():
    return pl.BlockSpec(memory_space=pltpu.VMEM)


def smem_spec():
    return pl.BlockSpec(memory_space=pltpu.SMEM)


def hbm_spec():
    return pl.BlockSpec(memory_space=pl.ANY)


def call(body, in_specs, out_shapes, out_specs, scratch, args, flops=0, moved=0, grid=(), aliases={}):
    return pl.pallas_call(
        body,
        grid=grid,
        input_output_aliases=aliases,
        in_specs=in_specs,
        out_shape=tuple(jax.ShapeDtypeStruct(shape, kind) for shape, kind in out_shapes),
        out_specs=tuple(out_specs),
        scratch_shapes=scratch,
        compiler_params=pltpu.CompilerParams(vmem_limit_bytes=VMEM_BYTES),
        cost_estimate=pl.CostEstimate(flops=flops, bytes_accessed=moved, transcendentals=0),
    )(*args)


def on_device(
    frames,
    utt_segments,
    out_grad,
    qkv_weight,
    out_weight,
    ffn_in_weight,
    ffn_out_weight,
    norm_gains,
    biases,
    ffn_bias,
):
    micros, groups, rows, width = frames.shape
    seqs = micros * groups
    ff = ffn_bias.shape[1]
    reps = lax.axis_size("rep")
    seg_count = lax.axis_size("seg")
    mats = Matrices(width, ff)
    by_blocks = width // reps == LANES and reps == 4 and seg_count == BLOCKS
    first = Sizes(rows, width, ff, True)
    last = Sizes(rows, width, ff, False)
    own = seqs * rows
    mem_own = seqs * first.segs

    seg_at = lax.axis_index("seg")
    seg_base = seg_at * first.segs
    rep_at = lax.axis_index("rep")
    place = [seg_base, jnp.int32(first.segs * seg_count)]
    y_at, x_at, core_at = seg_at % CHIPS_Y, rep_at // 2, rep_at % 2
    for other in range(2):
        core = lax.bitwise_xor(core_at, other)
        for hop2 in range(2):
            for hop1 in range(2):
                x_hop = jnp.where(core == 0, hop1, hop2)
                y_hop = jnp.where(core == 0, hop2, hop1)
                place.append(lax.bitwise_xor(y_at, y_hop))
                place.append((lax.bitwise_xor(x_at, x_hop) * 2 + core) * LANES)
    place = jnp.stack([jnp.asarray(entry, jnp.int32) for entry in place])
    lengths = utt_segments.reshape(seqs, utt_segments.shape[2])
    starts = (jnp.cumsum(lengths, axis=1) - lengths).astype(jnp.int32)
    zero_bias = jnp.zeros((1, width), F32)
    row_biases = [
        jnp.concatenate([biases[l : l + 1, 1], zero_bias, biases[l : l + 1, 2]], axis=1)
        for l in range(LAYERS)
    ]
    biases_by_row = jnp.swapaxes(biases, 0, 1)

    frames_own = frames.reshape(seqs, rows, width)
    grads_own = out_grad.reshape(seqs, rows, width)
    far = MEM_LEN * SEG_LEN
    frames_left = shifted(frames_own[:, rows - far :], "seg", 1)
    frames_right = shifted(frames_own[:, :RIGHT_ROWS], "seg", -1)

    attn_rows, ffn_rows = mats.attn_rows, mats.ffn_rows
    if by_blocks:
        qkv_t, out_t, down_t = (
            jnp.swapaxes(member, 1, 2) for member in (qkv_weight, out_weight, ffn_out_weight)
        )
        all_rows = attn_rows + ffn_rows
        spots = Spots(mats)
        shards = call(
            lambda *refs: pack_kernel(spots, *refs),
            [vmem_spec()] * 4,
            [((CHIPS_Z, all_rows, LANES), BF16)] * LAYERS,
            [vmem_spec()] * LAYERS,
            [],
            (qkv_t, out_t, ffn_in_weight, down_t),
        )
        sides0 = gather_sides(after(swap_z(shards[0]), frames_left, frames_right))
        place, starts, row_biases, sent = lax.optimization_barrier(
            (place, starts, row_biases, after(shards[1], sides0[0]))
        )
        sides1 = gather_sides(swap_z(sent))
        first_all = both_cores(sides0 + [across_second(after(sides0[1], sides1[0]))])
        classes = len(first_all) // 2
        grad_outs0 = [((2, 2, CHIPS_Z * all_rows + SMALL_ROWS, LANES), BF16)] * 2
        grad_outs1 = [((2, CHIPS_Z, 2 * all_rows, LANES), BF16)] * 2
        copies_in = len(first_all) * (3 + mats.down_parts)
    else:
        whole = []
        for member, shape in zip(
            (qkv_weight, out_weight, ffn_in_weight, ffn_out_weight),
            (mats.qkv, mats.out, mats.up, mats.down),
        ):
            member = lax.all_gather(member, "rep", axis=1, tiled=True)
            member = lax.all_gather(member, "seg", axis=2, tiled=True)
            whole.append(jnp.swapaxes(member, 1, 2).reshape((LAYERS,) + shape))
        first_all = [member[0] for member in whole]
        last_all = [member[1] for member in whole]
        spots = None
        grad_outs0 = grad_outs1 = [
            (shape, BF16) for shape in (mats.qkv, mats.out, mats.up, mats.down)
        ]
        copies_in = 4
    dma = pltpu.SemaphoreType.DMA

    matrices = [pltpu.VMEM(shape, BF16) for shape in (mats.qkv, mats.out, mats.up, mats.down)]

    (
        z0, proj0, probs0, att0, mixed0, mem1, x1, active0, slope0, low1, send_right, send_left,
    ) = call(
        lambda *refs: first_layer_kernel(
            first, seqs, mats, spots, len(first_all), *refs
        ),
        [smem_spec()] * 2 + [vmem_spec()] * 7 + [hbm_spec()] * len(first_all),
        [
            ((seqs * first.ext, width), BF16),
            ((seqs * first.ext, 3 * width), BF16),
            ((seqs * first.pairs, first.keys, 2 * first.queries), BF16),
            ((seqs * first.queries, width), BF16),
            ((own, width), F32),
            ((mem_own, width), F32),
            ((own, width), F32),
            ((own, ff), BF16),
            ((own, ff), BF16),
            ((own, width), BF16),
            ((seqs, BACK_ROWS, width), BF16),
            ((seqs, RIGHT_ROWS, width), BF16),
        ],
        [vmem_spec()] * 12,
        matrices
        + [
            pltpu.VMEM((seqs, first.keys, 2 * first.queries), F32),
            pltpu.VMEM((own, width), BF16),
            dma((copies_in,)),
        ],
        (place, starts, frames_own, frames_left, frames_right, norm_gains, biases_by_row, ffn_bias,
         row_biases[0]) + tuple(first_all),
        flops=24 * own * (4 * width * width + 2 * width * ff) // 2,
        moved=2 * (4 * width * width + 2 * width * ff),
    )
    left1 = shifted(send_right, "seg", 1)
    right1 = shifted(send_left, "seg", -1)
    if by_blocks:
        last_side = across_second(after(sides1[1], sides1[2], low1))
        last_all = both_cores(sides1 + [last_side])
        last_all[-1] = other_core(after(last_side, left1, right1))

    vec_shape = (TILE, width)
    outs = call(
        lambda *refs: last_layer_kernel(
            last, seqs, mats, spots, len(last_all), len(grad_outs1), *refs
        ),
        [smem_spec()] * 2 + [vmem_spec()] * 10 + [hbm_spec()] * len(last_all),
        [
            ((seqs, rows, width), F32),
            ((own, width), F32),
            ((own, width), F32),
            ((mem_own, width), F32),
            ((seqs, BACK_ROWS, width), BF16),
            ((seqs, RIGHT_ROWS, width), BF16),
            (vec_shape, F32),
        ]
        + grad_outs1,
        [vmem_spec()] * 7 + [hbm_spec()] * len(grad_outs1),
        matrices
        + matrices
        + [
            pltpu.VMEM((seqs, last.keys, 2 * last.queries), F32),
            pltpu.VMEM((seqs * last.ext, width), BF16),
            pltpu.VMEM((seqs * last.ext, 3 * width), BF16),
            pltpu.VMEM((seqs * last.pairs, last.keys, 2 * last.queries), BF16),
            pltpu.VMEM((seqs * last.queries, width), BF16),
            pltpu.VMEM((own, width), BF16),
            pltpu.VMEM((seqs * last.queries, width), BF16),
            pltpu.VMEM((seqs * last.ext, 3 * width), BF16),
            pltpu.VMEM((seqs * last.queries, width), BF16),
            pltpu.VMEM((own, width), BF16),
            pltpu.VMEM((own, width), F32),
            dma((2 * copies_in,)),
        ],
        (place, starts, low1, left1, right1, mem1, x1, grads_own, norm_gains, biases_by_row, ffn_bias,
         row_biases[1]) + tuple(last_all),
        flops=30 * own * (4 * width * width + 2 * width * ff),
        moved=4 * (4 * width * width + 2 * width * ff),
    )
    encoded, gz1, gh1, gmem1, back_left1, back_right1, vec1 = outs[:7]
    grad_blocks1 = outs[7:]
    from_right1 = shifted(back_left1, "seg", -1)
    from_left1 = shifted(back_right1, "seg", 1)

    gh1_tied = gh1
    if by_blocks:
        mine1, theirs1 = grad_blocks1[0], other_core(grad_blocks1[1])
        far1 = summed(mine1[1], theirs1[1])
        gh1_tied = after(gh1, far1)
    gz0, gh0, gmem0, back_left0, back_right0, upper_vec, vec0, *grad_blocks0 = call(
        lambda *refs: first_back_kernel(
            last, first, seqs, mats, spots, len(first_all), len(grad_outs0), *refs
        ),
        [smem_spec()] + [vmem_spec()] * 19 + [hbm_spec()] * len(first_all),
        [
            ((own, width), F32),
            ((own, width), F32),
            ((mem_own, width), F32),
            ((seqs, BACK_ROWS, width), BF16),
            ((seqs, RIGHT_ROWS, width), BF16),
            (vec_shape, F32),
            (vec_shape, F32),
        ]
        + grad_outs0,
        [vmem_spec()] * 7 + [hbm_spec()] * len(grad_outs0),
        matrices
        + matrices
        + [
            pltpu.VMEM((own, width), BF16),
            pltpu.VMEM((own, width), BF16),
            pltpu.VMEM((own, width), F32),
            pltpu.VMEM((own, width), F32),
            pltpu.VMEM((mem_own, width), F32),
            pltpu.VMEM((seqs * first.queries, width), BF16),
            pltpu.VMEM((seqs * first.ext, 3 * width), BF16),
            pltpu.VMEM((seqs * first.queries, width), BF16),
            pltpu.VMEM((SMALL_ROWS, LANES), BF16),
            dma((2 * copies_in + 8,)),
        ],
        (place, x1, gz1, gh1_tied, gmem1, from_right1, from_left1, mixed0, active0, slope0, att0,
         probs0, proj0, z0, frames_own, frames_left, frames_right, norm_gains, biases_by_row, vec1)
        + tuple(first_all),
        flops=28 * own * (4 * width * width + 2 * width * ff),
        moved=4 * (4 * width * width + 2 * width * ff),
    )
    from_right0 = shifted(back_left0, "seg", -1)
    from_left0 = shifted(back_right0, "seg", 1)
    gz0_last = gz0
    if by_blocks:
        second1 = across_second(far1)
        mine0, theirs0 = grad_blocks0[0], other_core(after(grad_blocks0[1], second1))
        both1 = summed(mine1[0], theirs1[0], second1)
        lines1 = swap_z(both1)
        far0 = summed(mine0[1], after(theirs0, both1, from_right0, from_left0)[1])
        second0 = across_second(far0)
        mid0 = summed(mine0[0, 1], theirs0[0, 1], second0[1])
        first0 = across_first(mid0)
        held0 = summed(mine0[0, 0], theirs0[0, 0], after(second0, mid0)[0])
        near0 = call(
            lambda *refs: near_small_kernel(CHIPS_Z, *refs),
            [vmem_spec()] * 2,
            [((CHIPS_Z, all_rows + SMALL_ROWS, LANES), BF16)],
            [vmem_spec()],
            [],
            [held0, first0],
        )[0]
        first_parts = swap_z(near0)
        gz0_last, lines1 = lax.optimization_barrier((after(gz0, near0), lines1))
        cross1 = jnp.sum(lines1[:, all_rows:].astype(F32), axis=0, keepdims=True).astype(BF16)
        first1 = across_first(cross1)
    frames_grad = call(
        lambda *refs: frames_grad_kernel(first, seqs, *refs),
        [vmem_spec()] * 8,
        [((seqs, rows, width), F32)],
        [vmem_spec()],
        [],
        (frames_own, gz0_last, gh0, gmem0, from_right0, from_left0, norm_gains, biases_by_row),
    )[0]

    if by_blocks:
        shapes = [member.shape for member in (qkv_t, out_t, ffn_in_weight, down_t)]
        held = [pltpu.VMEM(shape[1:], F32) for shape in shapes]
        whole = [(shape, F32) for shape in shapes]
        written = call(
            lambda *refs: unpack_last_kernel(spots, LAYERS - 1, *refs),
            [
                pl.BlockSpec((CHIPS_Z, all_rows, LANES), lambda i: (0, 0, 0)),
                pl.BlockSpec((1, all_rows, LANES), lambda i: (0, 0, 0)),
            ],
            whole,
            [hbm_spec()] * 4,
            held + [dma((4,))],
            [lines1, first1],
            grid=(1,),
        )
        small_shapes = [norm_gains.shape, (biases.shape[1], LAYERS, width), ffn_bias.shape]
        reduced = call(
            lambda *refs: unpack_first_kernel(spots, all_rows, *refs),
            [vmem_spec()] + [hbm_spec()] * 4,
            whole + [(shape, F32) for shape in small_shapes],
            [hbm_spec()] * 4 + [vmem_spec()] * 3,
            held + [dma((4,))],
            [after(first_parts, frames_grad)] + list(written),
            aliases={1 + i: i for i in range(4)},
        )
        small = reduced[4], jnp.swapaxes(reduced[5], 0, 1), reduced[6]
        reduced = [
            jnp.swapaxes(reduced[0], 1, 2),
            jnp.swapaxes(reduced[1], 1, 2),
            reduced[2],
            jnp.swapaxes(reduced[3], 1, 2),
        ]
    else:
        reduced = []
        for member0, member1 in zip(grad_blocks0, grad_blocks1):
            both = jnp.stack([member0, member1]).reshape(LAYERS, -1, member0.shape[3])
            both = jnp.swapaxes(both, 1, 2)
            both = lax.psum_scatter(both, "seg", scatter_dimension=2, tiled=True)
            both = lax.psum_scatter(both, "rep", scatter_dimension=1, tiled=True)
            reduced.append(both.astype(F32))
        small = sum_everywhere(jnp.stack([vec0, vec1 + upper_vec]))
        small = small[:, 0:2], small[:, 2:8], small[:, 8:12].reshape(ffn_bias.shape)

    return (
        encoded.reshape(frames.shape),
        frames_grad.reshape(frames.shape),
        reduced[0],
        reduced[1],
        reduced[2],
        reduced[3],
        small[0],
        small[1],
        small[2],
    )


def solution(mesh):
    in_specs = (
        P(None, "rep", "seg", None),
        P(None, "rep", None),
        P(None, "rep", "seg", None),
        P(None, "rep", "seg"),
        P(None, "rep", "seg"),
        P(None, "rep", "seg"),
        P(None, "rep", "seg"),
        P(),
        P(),
        P(),
    )
    out_specs = (
        P(None, "rep", "seg", None),
        P(None, "rep", "seg", None),
        P(None, "rep", "seg"),
        P(None, "rep", "seg"),
        P(None, "rep", "seg"),
        P(None, "rep", "seg"),
        P(),
        P(),
        P(),
    )
    return jax.shard_map(
        on_device, mesh=mesh, in_specs=in_specs, out_specs=out_specs, check_vma=False
    )
```

```python
import jax
import jax.numpy as jnp
from jax import lax
from jax.experimental import pallas as pl
from jax.experimental.pallas import tpu as pltpu
from jax.sharding import PartitionSpec as P

HEADS = 8
SEG_LEN = 16
LEFT_LEN = 30
RIGHT_LEN = 4
MEM_LEN = 4
LAYERS = 2

EPS = 1e-05
ROOT_HALF = 0.7071067811865476
INV_ROOT_TWO_PI = 0.3989422804014327

LANES = 128
TILE = 16
RIGHT_ROWS = 16
LEFT_ROWS = 32
MEM_ROWS = 16
BACK_ROWS = LEFT_ROWS + MEM_ROWS
CHIPS_Z = 4
CHIPS_Y = 2
BLOCKS = CHIPS_Z * CHIPS_Y
SMALL_ROWS = 128
MIB = 1024 * 1024

BF16 = jnp.bfloat16
F32 = jnp.float32


def nn(a, b):
    return lax.dot_general(a, b, (((1,), (0,)), ((), ())), preferred_element_type=F32)


def nt(a, b):
    return lax.dot_general(a, b, (((1,), (1,)), ((), ())), preferred_element_type=F32)


def tn(a, b):
    return lax.dot_general(a, b, (((0,), (0,)), ((), ())), preferred_element_type=F32)


def col_sum(value):
    return jnp.sum(value, axis=0, keepdims=True)


def norm_forward(inputs, gain, bias):
    center = inputs - jnp.mean(inputs, axis=1, keepdims=True)
    inverse = lax.rsqrt(jnp.mean(center * center, axis=1, keepdims=True) + EPS)
    scaled = center * inverse
    return scaled * gain + bias, scaled, inverse


def norm_backward(grad_in, scaled, inverse, gain):
    grad_scaled = grad_in * gain
    return inverse * (
        grad_scaled
        - jnp.mean(grad_scaled, axis=1, keepdims=True)
        - scaled * jnp.mean(grad_scaled * scaled, axis=1, keepdims=True)
    )


def segment_mean(inputs):
    rows, width = inputs.shape
    return jnp.mean(inputs.reshape(rows // SEG_LEN, SEG_LEN, width), axis=1)


def segment_spread(rows, width, per_segment):
    segs = rows // SEG_LEN
    return jnp.broadcast_to(per_segment[:, None, :], (segs, SEG_LEN, width)).reshape(rows, width)


def identity(size):
    row = lax.broadcasted_iota(jnp.int32, (size, size), 0)
    col = lax.broadcasted_iota(jnp.int32, (size, size), 1)
    return (row == col).astype(F32).astype(BF16)


class Sizes:
    def __init__(self, rows, width, ff, with_summary):
        self.rows = rows
        self.width = width
        self.ff = ff
        self.segs = rows // SEG_LEN
        self.top = TILE if with_summary else 0
        self.keys = rows + RIGHT_ROWS + LEFT_ROWS + MEM_ROWS
        self.ext = self.top + self.keys
        self.queries = self.top + rows
        self.right_at = self.top + rows
        self.left_at = self.right_at + RIGHT_ROWS
        self.mem_at = self.left_at + LEFT_ROWS
        self.pairs = width // LANES


class Matrices:
    def __init__(self, width, ff):
        self.qkv = (CHIPS_Z, CHIPS_Y, 3 * width // BLOCKS, width)
        self.out = (CHIPS_Z, CHIPS_Y, width // BLOCKS, width)
        self.up = (CHIPS_Z, CHIPS_Y, ff // BLOCKS, width)
        self.down = (CHIPS_Z, CHIPS_Y, width // BLOCKS, ff)
        self.down_parts = ff // width
        self.attn_rows = self.qkv[2] + self.out[2]
        self.ffn_rows = self.up[2] + self.down_parts * self.down[2]


class Spots:
    def __init__(self, mats):
        high, wide, up, low = mats.qkv[2], mats.out[2], mats.up[2], mats.down[2]
        self.qkv = (0, 0)
        self.out = (0, high)
        self.up = (0, high + wide)
        self.down = [(0, high + wide + up + low * part) for part in range(mats.down_parts)]


def attn_pairs(mats, spots, groups, qkv_ref, out_ref, place_ref):
    if spots is None:
        return [(groups[0], qkv_ref), (groups[1], out_ref)]
    pairs = []
    for k in range(len(groups[0])):
        row = place_ref[2 + 2 * k]
        lane = pl.multiple_of(place_ref[3 + 2 * k], LANES)
        for (group, first), ref, shape in (
            (spots.qkv, qkv_ref, mats.qkv),
            (spots.out, out_ref, mats.out),
        ):
            block = groups[group][k]
            pairs.append(
                (
                    block.at[:, pl.ds(first, shape[2]), :],
                    ref.at[:, row, :, pl.ds(lane, LANES)],
                )
            )
    return pairs


def ffn_pairs(mats, spots, groups, up_ref, down_ref, place_ref):
    if spots is None:
        return [(groups[2], up_ref), (groups[3], down_ref)]
    pairs = []
    for k in range(len(groups[0])):
        row = place_ref[2 + 2 * k]
        lane = pl.multiple_of(place_ref[3 + 2 * k], LANES)
        group, first = spots.up
        block = groups[group][k]
        pairs.append(
            (block.at[:, pl.ds(first, mats.up[2]), :], up_ref.at[:, row, :, pl.ds(lane, LANES)])
        )
        for part, (group, first) in enumerate(spots.down):
            there = pl.multiple_of(
                place_ref[3 + 2 * k] * mats.down_parts + part * LANES, LANES
            )
            block = groups[group][k]
            pairs.append(
                (
                    block.at[:, pl.ds(first, mats.down[2]), :],
                    down_ref.at[:, row, :, pl.ds(there, LANES)],
                )
            )
    return pairs


def start_in(pairs, sems, at):
    copies = [pltpu.make_async_copy(s, d, sems.at[at + i]) for i, (s, d) in enumerate(pairs)]
    for copy in copies:
        copy.start()
    return copies


def start_out(pairs, sems, at):
    copies = [pltpu.make_async_copy(d, s, sems.at[at + i]) for i, (s, d) in enumerate(pairs)]
    for copy in copies:
        copy.start()
    return copies


def in_groups(spots, refs):
    return refs if spots is None else [refs]


def wait_all(copies):
    for copy in copies:
        copy.wait()


def fill_mask(sizes, seqs, starts_ref, place_ref, mask_ref):
    shape = (sizes.keys, 2 * sizes.queries)
    key = lax.broadcasted_iota(jnp.int32, shape, 0)
    col = lax.broadcasted_iota(jnp.int32, shape, 1)
    col = jnp.where(col < sizes.queries, col, col - sizes.queries)
    base = place_ref[0]
    total = place_ref[1]
    query = jnp.where(col < sizes.top, col, lax.shift_right_arithmetic(col - sizes.top, 4))
    left_at = sizes.rows + RIGHT_ROWS
    mem_at = left_at + LEFT_ROWS
    spot = jnp.where(key < left_at, key, key - mem_at)
    mem_seg = jnp.where(key < mem_at + sizes.segs, key - mem_at, key - mem_at - 2 * sizes.segs)
    key_seg = jnp.where(key < mem_at, lax.shift_right_arithmetic(spot, 4), mem_seg)
    near = (
        (key_seg == query)
        | ((spot >= query * SEG_LEN - LEFT_LEN) & (spot < query * SEG_LEN))
        | ((key_seg == query + 1) & (spot < query * SEG_LEN + SEG_LEN + RIGHT_LEN))
    )
    recent = (key_seg >= query - MEM_LEN) & (key_seg < query) & (col >= sizes.top)
    allowed = ((key < mem_at) & near) | ((key >= mem_at) & recent)
    key_abs = key_seg + base
    query_abs = query + base
    allowed = allowed & (key_abs >= 0) & (key_abs < total)
    if sizes.top:
        allowed = allowed & ((col < sizes.segs) | (col >= sizes.top))
    for n in range(seqs):
        key_owner = jnp.zeros(shape, jnp.int32)
        query_owner = jnp.zeros(shape, jnp.int32)
        for u in range(starts_ref.shape[1]):
            first = starts_ref[n, u]
            key_owner = key_owner + (key_abs >= first).astype(jnp.int32)
            query_owner = query_owner + (query_abs >= first).astype(jnp.int32)
        mask_ref[n] = jnp.where(allowed & (key_owner == query_owner), 0.0, -1e30)


def half_masks():
    lane = lax.broadcasted_iota(jnp.int32, (1, LANES), 1)
    even = (lane < LANES // 2).astype(F32)
    return even.astype(BF16), (1.0 - even).astype(BF16), lane < LANES // 2


def project(sizes, z_ref, qkv_ref, row_bias_ref, proj_ref):
    step = CHIPS_Z // 2
    for c in range(2):
        block = qkv_ref[pl.ds(c * step, step)].reshape(-1, sizes.width)
        wide = block.shape[0]
        made = nt(z_ref[...], block) + row_bias_ref[:, pl.ds(c * wide, wide)]
        proj_ref[:, pl.ds(c * wide, wide)] = made.astype(BF16)


def attend(sizes, seqs, proj_ref, mask_ref, probs_ref, att_ref):
    even, odd, is_even = half_masks()
    scale = (sizes.width // HEADS) ** (-0.5)
    count = sizes.queries

    def body(p, carry):
        for n in range(seqs):
            lane = pl.multiple_of(p * LANES, LANES)
            query = proj_ref[pl.ds(n * sizes.ext, count), pl.ds(lane, LANES)]
            first = n * sizes.ext + sizes.top
            key = proj_ref[pl.ds(first, sizes.keys), pl.ds(sizes.width + lane, LANES)]
            value = proj_ref[pl.ds(first, sizes.keys), pl.ds(2 * sizes.width + lane, LANES)]
            queries = jnp.concatenate([query * even, query * odd], axis=0)
            scores = nt(key, queries) * scale + mask_ref[n]
            scores = jnp.exp(scores - jnp.max(scores, axis=0, keepdims=True))
            probs = (scores * (1.0 / jnp.sum(scores, axis=0, keepdims=True))).astype(BF16)
            probs_ref[n * sizes.pairs + p] = probs
            out = tn(probs, value)
            att_ref[pl.ds(n * count, count), pl.ds(lane, LANES)] = jnp.where(
                is_even, out[:count], out[count:]
            ).astype(BF16)
        return carry

    lax.fori_loop(0, sizes.pairs, body, 0, unroll=True)


def attend_back(sizes, seqs, proj_ref, probs_ref, go_ref, gproj_ref):
    even, odd, is_even = half_masks()
    scale = (sizes.width // HEADS) ** (-0.5)
    count = sizes.queries
    wide = sizes.width
    for n in range(seqs):
        base = n * sizes.ext
        rest = sizes.ext - count
        gproj_ref[pl.ds(base + count, rest), pl.ds(0, wide)] = jnp.zeros((rest, wide), BF16)
        if sizes.top:
            gproj_ref[pl.ds(base, sizes.top), pl.ds(wide, 2 * wide)] = jnp.zeros(
                (sizes.top, 2 * wide), BF16
            )

    def body(p, carry):
        for n in range(seqs):
            lane = pl.multiple_of(p * LANES, LANES)
            base = n * sizes.ext
            first = base + sizes.top
            query = proj_ref[pl.ds(base, count), pl.ds(lane, LANES)]
            key = proj_ref[pl.ds(first, sizes.keys), pl.ds(wide + lane, LANES)]
            value = proj_ref[pl.ds(first, sizes.keys), pl.ds(2 * wide + lane, LANES)]
            grad = go_ref[pl.ds(n * count, count), pl.ds(lane, LANES)]
            queries = jnp.concatenate([query * even, query * odd], axis=0)
            grads = jnp.concatenate([grad * even, grad * odd], axis=0)
            probs_low = probs_ref[n * sizes.pairs + p]
            grad_values = nn(probs_low, grads)
            probs = probs_low.astype(F32)
            weighted = nt(value, grads) * probs
            grad_scores = (
                (weighted - probs * jnp.sum(weighted, axis=0, keepdims=True)) * scale
            ).astype(BF16)
            grad_keys = nn(grad_scores, queries)
            grad_both = tn(grad_scores, key)
            grad_query = jnp.where(is_even, grad_both[:count], grad_both[count:])
            gproj_ref[pl.ds(base, count), pl.ds(lane, LANES)] = grad_query.astype(BF16)
            gproj_ref[pl.ds(first, sizes.keys), pl.ds(wide + lane, LANES)] = grad_keys.astype(BF16)
            gproj_ref[pl.ds(first, sizes.keys), pl.ds(2 * wide + lane, LANES)] = (
                grad_values.astype(BF16)
            )
        return carry

    lax.fori_loop(0, sizes.pairs, body, 0)


def gelu_both(upward):
    half = 0.5 * (1.0 + lax.erf(upward * ROOT_HALF))
    slope = half + upward * jnp.exp(-0.5 * upward * upward) * INV_ROOT_TWO_PI
    return upward * half, slope


def up_block(up_ref, c, wide):
    step = wide // (up_ref.shape[1] * up_ref.shape[2])
    return up_ref[pl.ds(c * step, step)].reshape(-1, up_ref.shape[3])


def down_block(down_ref, c, wide):
    at = pl.multiple_of(c * wide, wide)
    return down_ref[:, :, :, pl.ds(at, wide)].reshape(-1, wide)


def ffn_back_step(
    sizes, c, wide, grad_low, hidden_low, active, slope, up_ref, down_ref, gup_ref, gdown_ref, vec
):
    at = pl.multiple_of(c * wide, wide)
    up = up_block(up_ref, c, wide)
    down = down_block(down_ref, c, wide)
    grad_active = nn(grad_low, down)
    grad_up_f = grad_active * slope
    grad_up = grad_up_f.astype(BF16)
    gdown_ref[:, :, :, pl.ds(at, wide)] = (
        tn(grad_low, active).astype(BF16).reshape(gdown_ref.shape[:3] + (wide,))
    )
    step = wide // (gup_ref.shape[1] * gup_ref.shape[2])
    gup_ref[pl.ds(c * step, step)] = (
        tn(grad_up, hidden_low).astype(BF16).reshape((step,) + gup_ref.shape[1:])
    )
    vec[pl.ds(8 + c, 1), :] = col_sum(grad_up.astype(F32))
    return nn(grad_up, up)


def attn_back_stage(
    sizes, seqs, gz, grad_mem_ref, att_ref, proj_ref, probs_ref, z_ref, qkv_ref, out_ref,
    gqkv_ref, gout_ref, go_ref, gproj_ref, branch_ref, vec, gh_ref, gmem_ref, back_left_ref,
    back_right_ref, scaled_rows=None,
):
    wide = sizes.width
    count = sizes.queries
    bias_out = col_sum(gz)
    for n in range(seqs):
        if sizes.top:
            mem_grad = grad_mem_ref[pl.ds(n * sizes.segs, sizes.segs), :]
            bias_out = bias_out + col_sum(mem_grad)
            branch_ref[pl.ds(n * count, sizes.top), :] = jnp.concatenate(
                [mem_grad, jnp.zeros((sizes.top - sizes.segs, wide), F32)], axis=0
            ).astype(BF16)
        branch_ref[pl.ds(n * count + sizes.top, sizes.rows), :] = gz[
            n * sizes.rows : (n + 1) * sizes.rows
        ].astype(BF16)
    vec[pl.ds(5, 1), :] = bias_out
    branch = branch_ref[...]
    gout_ref[...] = tn(branch, att_ref[...]).astype(BF16).reshape(gout_ref.shape)
    go_ref[...] = nn(branch, out_ref[...].reshape(-1, wide)).astype(BF16)
    attend_back(sizes, seqs, proj_ref, probs_ref, go_ref, gproj_ref)
    vec[pl.ds(3, 1), :] = col_sum(gproj_ref[:, pl.ds(0, wide)].astype(F32))
    vec[pl.ds(4, 1), :] = col_sum(gproj_ref[:, pl.ds(2 * wide, wide)].astype(F32))
    grad_ext = nn(gproj_ref[...], qkv_ref[...].reshape(-1, wide))
    gain_sum = jnp.zeros((1, wide), F32)
    bias_sum = jnp.zeros((1, wide), F32)
    for n in range(seqs):
        base = n * sizes.ext
        own = grad_ext[base + sizes.top : base + sizes.top + sizes.rows]
        if sizes.top:
            spread = grad_ext[base : base + sizes.segs] * (1.0 / SEG_LEN)
            own = own + segment_spread(sizes.rows, wide, spread)
        gh_ref[pl.ds(n * sizes.rows, sizes.rows), :] = own
        mem = base + sizes.mem_at
        gmem_ref[pl.ds(n * sizes.segs, sizes.segs), :] = grad_ext[mem : mem + sizes.segs]
        left = base + sizes.left_at
        back_left_ref[n] = grad_ext[left : left + BACK_ROWS].astype(BF16)
        right = base + sizes.right_at
        back_right_ref[n] = grad_ext[right : right + RIGHT_ROWS].astype(BF16)
        if scaled_rows is not None:
            grads = (
                own,
                grad_ext[right : right + RIGHT_ROWS],
                grad_ext[left : left + LEFT_ROWS],
            )
            for rows, scaled in zip(grads, scaled_rows(n)):
                gain_sum = gain_sum + col_sum(rows * scaled)
                bias_sum = bias_sum + col_sum(rows)
    if scaled_rows is not None:
        vec[pl.ds(0, 1), :] = gain_sum
        vec[pl.ds(2, 1), :] = bias_sum
    step = CHIPS_Z // 2
    part = gqkv_ref.shape[1] * gqkv_ref.shape[2] * step
    for c in range(2):
        gqkv_ref[pl.ds(c * step, step)] = (
            tn(gproj_ref[:, pl.ds(c * part, part)], z_ref[...])
            .astype(BF16)
            .reshape((step,) + gqkv_ref.shape[1:])
        )


def merge_halo(sizes, n, gh_ref, gmem_ref, from_right_ref, from_left_ref):
    first = n * sizes.rows
    back = from_right_ref[n].astype(F32)
    head = gh_ref[pl.ds(first, RIGHT_ROWS), :] + from_left_ref[n].astype(F32)
    middle = gh_ref[pl.ds(first + RIGHT_ROWS, sizes.rows - RIGHT_ROWS - LEFT_ROWS), :]
    tail = gh_ref[pl.ds(first + sizes.rows - LEFT_ROWS, LEFT_ROWS), :] + back[:LEFT_ROWS]
    mem = gmem_ref[pl.ds(n * sizes.segs, sizes.segs), :] + back[LEFT_ROWS + sizes.segs :]
    return jnp.concatenate([head, middle, tail], axis=0), mem


def pack_kernel(spots, qkv_ref, out_ref, up_ref, down_ref, *packed):
    eye = identity(LANES)
    high, wide, low = qkv_ref.shape[1], out_ref.shape[1], down_ref.shape[1]
    for layer, ref in enumerate(packed):
        up = tn(up_ref[layer], eye).astype(BF16)
        for z in range(ref.shape[0]):
            ref[z, pl.ds(spots.qkv[1], high), :] = qkv_ref[layer]
            ref[z, pl.ds(spots.out[1], wide), :] = out_ref[layer]
            ref[z, pl.ds(spots.up[1], up_ref.shape[2]), :] = up
            for part, (_, first) in enumerate(spots.down):
                ref[z, pl.ds(first, low), :] = down_ref[layer, :, pl.ds(part * LANES, LANES)]


def unpack_layer(spots, sources, refs):
    qkv_ref, out_ref, up_ref, down_ref = refs
    high, wide, low = qkv_ref.shape[0], out_ref.shape[0], down_ref.shape[0]

    def total(first, rows):
        parts = [ref[z, pl.ds(first, rows), :] for ref in sources for z in range(ref.shape[0])]
        value = parts[0].astype(F32)
        for part in parts[1:]:
            value = value + part.astype(F32)
        return value

    qkv_ref[...] = total(spots.qkv[1], high)
    out_ref[...] = total(spots.out[1], wide)
    up_ref[...] = nt(identity(LANES), total(spots.up[1], up_ref.shape[1]).astype(BF16))
    for part, (_, first) in enumerate(spots.down):
        down_ref[:, pl.ds(part * LANES, LANES)] = total(first, low)
    return total


def store_layer(layer, held, outs, sems):
    copies = [
        pltpu.make_async_copy(ref, out.at[layer], sems.at[i])
        for i, (ref, out) in enumerate(zip(held, outs))
    ]
    for copy in copies:
        copy.start()
    return copies


def unpack_last_kernel(spots, layer, lines_ref, first_ref, *refs):
    outs, held, sems = refs[:4], refs[4:8], refs[8]
    unpack_layer(spots, (lines_ref, first_ref), held)
    wait_all(store_layer(layer, held, outs, sems))


def unpack_first_kernel(spots, small_at, parts_ref, *refs):
    outs, (gains_ref, biases_ref, ffn_bias_ref), held, sems = (
        refs[4:8], refs[8:11], refs[11:15], refs[15],
    )
    total = unpack_layer(spots, (parts_ref,), held)
    copies = store_layer(0, held, outs, sems)
    sums = total(small_at, SMALL_ROWS)
    parts = gains_ref.shape[2] // LANES
    for layer in range(gains_ref.shape[0]):
        for part in range(parts):
            lanes = pl.ds(part * LANES, LANES)
            block = sums[(layer * parts + part) * TILE : (layer * parts + part + 1) * TILE]
            gains_ref[layer, :, lanes] = block[0:2]
            for row in range(biases_ref.shape[0]):
                biases_ref[row, pl.ds(layer, 1), lanes] = block[2 + row : 3 + row]
            for row in range(ffn_bias_ref.shape[1] // gains_ref.shape[2]):
                at = row * gains_ref.shape[2] + part * LANES
                ffn_bias_ref[pl.ds(layer, 1), pl.ds(at, LANES)] = block[8 + row : 9 + row]
    wait_all(copies)


def first_layer_kernel(
    sizes, seqs, mats, spots, count_in, place_ref, starts_ref, frames_ref, left_ref, right_ref,
    gains_ref, biases_ref, ffn_bias_ref, row_bias_ref, *refs
):
    groups = in_groups(spots, refs[:count_in])
    (
        z_ref, proj_ref, probs_ref, att_ref, mixed_ref, mem_ref, next_ref, active_ref, slope_ref,
        low_ref, send_right_ref, send_left_ref, qkv_ref, out_ref, up_ref, down_ref, mask_ref,
        hidden_ref, sems,
    ) = refs[count_in:]
    wide = sizes.width
    copies = start_in(attn_pairs(mats, spots, groups, qkv_ref, out_ref, place_ref), sems, 0)
    ffn_copies = start_in(
        ffn_pairs(mats, spots, groups, up_ref, down_ref, place_ref), sems, len(copies)
    )
    gain = gains_ref[0, pl.ds(0, 1), :]
    bias = biases_ref[0, pl.ds(0, 1), :]
    pad = jnp.zeros((TILE - sizes.segs, wide), F32)
    for n in range(seqs):
        own = frames_ref[n].astype(F32)
        before = left_ref[n].astype(F32)
        hidden = norm_forward(own, gain, bias)[0]
        halo = norm_forward(before[before.shape[0] - LEFT_ROWS :], gain, bias)[0]
        after = norm_forward(right_ref[n].astype(F32), gain, bias)[0]
        memory = jnp.concatenate(
            [
                segment_mean(own),
                jnp.zeros((sizes.segs - before.shape[0] // SEG_LEN, wide), F32),
                segment_mean(before),
            ],
            axis=0,
        )
        base = n * sizes.ext
        z_ref[pl.ds(base, sizes.top), :] = jnp.concatenate(
            [segment_mean(hidden), pad], axis=0
        ).astype(BF16)
        z_ref[pl.ds(base + sizes.top, sizes.rows), :] = hidden.astype(BF16)
        z_ref[pl.ds(base + sizes.right_at, RIGHT_ROWS), :] = after.astype(BF16)
        z_ref[pl.ds(base + sizes.left_at, LEFT_ROWS), :] = halo.astype(BF16)
        z_ref[pl.ds(base + sizes.mem_at, MEM_ROWS), :] = memory.astype(BF16)
    fill_mask(sizes, seqs, starts_ref, place_ref, mask_ref)
    wait_all(copies)
    project(sizes, z_ref, qkv_ref, row_bias_ref, proj_ref)
    attend(sizes, seqs, proj_ref, mask_ref, probs_ref, att_ref)
    mixed = nt(att_ref[...], out_ref[...].reshape(-1, wide)) + biases_ref[3, pl.ds(0, 1), :]
    for n in range(seqs):
        base = n * sizes.queries
        mem_ref[pl.ds(n * sizes.segs, sizes.segs), :] = mixed[base : base + sizes.segs]
        mixed_ref[pl.ds(n * sizes.rows, sizes.rows), :] = (
            frames_ref[n].astype(F32) + mixed[base + sizes.top : base + sizes.top + sizes.rows]
        )
    mixed = mixed_ref[...]
    hidden, _, _ = norm_forward(mixed, gains_ref[0, pl.ds(1, 1), :], biases_ref[4, pl.ds(0, 1), :])
    hidden_ref[...] = hidden.astype(BF16)
    next_ref[...] = mixed + biases_ref[5, pl.ds(0, 1), :]
    wait_all(ffn_copies)

    def body(c, carry):
        at_lane = pl.multiple_of(c * wide, wide)
        upward = nt(hidden_ref[...], up_block(up_ref, c, wide))
        upward = upward + ffn_bias_ref[pl.ds(0, 1), pl.ds(at_lane, wide)]
        active, slope = gelu_both(upward)
        active = active.astype(BF16)
        active_ref[:, pl.ds(at_lane, wide)] = active
        slope_ref[:, pl.ds(at_lane, wide)] = slope.astype(BF16)
        next_ref[...] += nt(active, down_block(down_ref, c, wide))
        return carry

    lax.fori_loop(0, sizes.ff // wide, body, 0)
    low, _, _ = norm_forward(
        next_ref[...], gains_ref[1, pl.ds(0, 1), :], biases_ref[0, pl.ds(1, 1), :]
    )
    low = low.astype(BF16)
    low_ref[...] = low
    for n in range(seqs):
        base = n * sizes.rows
        send_right_ref[n, pl.ds(0, LEFT_ROWS), :] = low[
            base + sizes.rows - LEFT_ROWS : base + sizes.rows
        ]
        send_right_ref[n, pl.ds(LEFT_ROWS, MEM_ROWS), :] = jnp.concatenate(
            [
                mem_ref[pl.ds(n * sizes.segs, sizes.segs), :],
                jnp.zeros((MEM_ROWS - sizes.segs, wide), F32),
            ],
            axis=0,
        ).astype(BF16)
        send_left_ref[n] = low[base : base + RIGHT_ROWS]


def last_layer_kernel(
    sizes, seqs, mats, spots, count_in, count_out, place_ref, starts_ref, low_ref, left_ref,
    right_ref, mem_ref, inputs_ref, out_grad_ref, gains_ref, biases_ref, ffn_bias_ref,
    row_bias_ref, *refs
):
    groups = in_groups(spots, refs[:count_in])
    (encoded_ref, gz_ref, gh_ref, gmem_ref, back_left_ref, back_right_ref, vec) = refs[
        count_in : count_in + 7
    ]
    hbm_out = refs[count_in + 7 : count_in + 7 + count_out]
    (
        qkv_ref, out_ref, up_ref, down_ref, gqkv_ref, gout_ref, gup_ref, gdown_ref, mask_ref,
        z_ref, proj_ref, probs_ref, att_ref, hidden_ref, go_ref, gproj_ref, branch_ref,
        grad_low_ref, grad_hidden_ref, sems,
    ) = refs[count_in + 7 + count_out :]
    outs_to = hbm_out
    if spots is not None:
        rows = mats.attn_rows + mats.ffn_rows
        outs_to = [
            [
                ref.at[hop2, :, pl.ds(hop1 * rows, rows), :]
                for ref in hbm_out
                for hop2 in range(2)
                for hop1 in range(2)
            ]
        ]
    wide = sizes.width
    attn_copies = start_in(attn_pairs(mats, spots, groups, qkv_ref, out_ref, place_ref), sems, 0)
    ffn_copies = start_in(
        ffn_pairs(mats, spots, groups, up_ref, down_ref, place_ref), sems, len(attn_copies)
    )
    vec[...] = jnp.zeros_like(vec)
    for n in range(seqs):
        base = n * sizes.ext
        z_ref[pl.ds(base, sizes.rows), :] = low_ref[pl.ds(n * sizes.rows, sizes.rows), :]
        z_ref[pl.ds(base + sizes.right_at, RIGHT_ROWS), :] = right_ref[n]
        z_ref[pl.ds(base + sizes.left_at, LEFT_ROWS), :] = left_ref[n, pl.ds(0, LEFT_ROWS), :]
        memory = jnp.concatenate(
            [
                mem_ref[pl.ds(n * sizes.segs, sizes.segs), :],
                left_ref[n, pl.ds(LEFT_ROWS, MEM_ROWS), :].astype(F32)[: sizes.segs],
            ],
            axis=0,
        )
        z_ref[pl.ds(base + sizes.mem_at, MEM_ROWS), :] = memory.astype(BF16)
        grad_low_ref[pl.ds(n * sizes.rows, sizes.rows), :] = out_grad_ref[n]
    fill_mask(sizes, seqs, starts_ref, place_ref, mask_ref)
    wait_all(attn_copies)
    project(sizes, z_ref, qkv_ref, row_bias_ref, proj_ref)
    attend(sizes, seqs, proj_ref, mask_ref, probs_ref, att_ref)
    mixed = (
        inputs_ref[...]
        + nt(att_ref[...], out_ref[...].reshape(-1, wide))
        + biases_ref[3, pl.ds(1, 1), :]
    )
    gain = gains_ref[1, pl.ds(1, 1), :]
    hidden, scaled, inverse = norm_forward(mixed, gain, biases_ref[4, pl.ds(1, 1), :])
    hidden_ref[...] = hidden.astype(BF16)
    for n in range(seqs):
        encoded_ref[n] = mixed[n * sizes.rows : (n + 1) * sizes.rows] + biases_ref[5, pl.ds(1, 1), :]
    grad_hidden_ref[...] = jnp.zeros_like(grad_hidden_ref)
    wait_all(ffn_copies)

    def body(c, carry):
        at_lane = pl.multiple_of(c * wide, wide)
        upward = nt(hidden_ref[...], up_block(up_ref, c, wide))
        upward = upward + ffn_bias_ref[pl.ds(1, 1), pl.ds(at_lane, wide)]
        active, slope = gelu_both(upward)
        active = active.astype(BF16)
        made = nt(active, down_block(down_ref, c, wide))
        for n in range(seqs):
            encoded_ref[n] += made[n * sizes.rows : (n + 1) * sizes.rows]
        grad_hidden_ref[...] += ffn_back_step(
            sizes, c, wide, grad_low_ref[...], hidden_ref[...], active, slope, up_ref, down_ref,
            gup_ref, gdown_ref, vec,
        )
        return carry

    lax.fori_loop(0, sizes.ff // wide, body, 0)
    out_at = len(attn_copies) + len(ffn_copies)
    outs = start_out(
        ffn_pairs(mats, spots, outs_to, gup_ref, gdown_ref, place_ref), sems, out_at
    )
    grad = grad_low_ref[...].astype(F32)
    grad_hidden = grad_hidden_ref[...]
    vec[pl.ds(1, 1), :] = col_sum(grad_hidden * scaled)
    vec[pl.ds(6, 1), :] = col_sum(grad_hidden)
    vec[pl.ds(7, 1), :] = col_sum(grad)
    gz = grad + norm_backward(grad_hidden, scaled, inverse, gain)
    gz_ref[...] = gz
    attn_back_stage(
        sizes, seqs, gz, None, att_ref, proj_ref, probs_ref, z_ref, qkv_ref, out_ref, gqkv_ref,
        gout_ref, go_ref, gproj_ref, branch_ref, vec, gh_ref, gmem_ref, back_left_ref,
        back_right_ref,
    )
    outs = outs + start_out(
        attn_pairs(mats, spots, outs_to, gqkv_ref, gout_ref, place_ref),
        sems,
        out_at + len(outs),
    )
    wait_all(outs)


def first_back_kernel(
    last, sizes, seqs, mats, spots, count_in, count_out, place_ref, inputs_ref, gz_in_ref,
    gh_in_ref, gmem_in_ref, from_right_ref, from_left_ref, mixed_ref, active_ref, slope_ref,
    att_ref, probs_ref, proj_ref, z_ref, frames_ref, left_ref, right_ref, gains_ref, biases_ref,
    last_vec, *refs
):
    groups = in_groups(spots, refs[:count_in])
    gz_ref, gh_ref, gmem_ref, back_left_ref, back_right_ref, upper_vec, vec = refs[
        count_in : count_in + 7
    ]
    refs = refs[count_in + 7 :]
    hbm_out = refs[:count_out]
    (
        qkv_ref, out_ref, up_ref, down_ref, gqkv_ref, gout_ref, gup_ref, gdown_ref, hidden_ref,
        grad_low_ref, grad_ref, grad_hidden_ref, grad_mem_ref, go_ref, gproj_ref, branch_ref,
        small_ref, sems,
    ) = refs[count_out:]
    wide = sizes.width
    small = []
    outs_to = hbm_out
    if spots is not None:
        rows = mats.attn_rows + mats.ffn_rows
        end = CHIPS_Z * rows
        each = [
            ref.at[hop2, hop1] for ref in hbm_out for hop2 in range(2) for hop1 in range(2)
        ]
        small = [ref.at[pl.ds(end, SMALL_ROWS), :] for ref in each]
        outs_to = [[ref.at[pl.ds(0, end), :].reshape(CHIPS_Z, rows, LANES) for ref in each]]
    ffn_copies = start_in(ffn_pairs(mats, spots, groups, up_ref, down_ref, place_ref), sems, 0)
    attn_copies = start_in(
        attn_pairs(mats, spots, groups, qkv_ref, out_ref, place_ref), sems, len(ffn_copies)
    )
    vec[...] = jnp.zeros_like(vec)
    upper_vec[...] = jnp.zeros_like(upper_vec)
    gain = gains_ref[1, pl.ds(0, 1), :]
    gain_sum = jnp.zeros((1, wide), F32)
    bias_sum = jnp.zeros((1, wide), F32)
    for n in range(seqs):
        rows = pl.ds(n * sizes.rows, sizes.rows)
        _, scaled, inverse = norm_forward(
            inputs_ref[rows, :], gain, biases_ref[0, pl.ds(1, 1), :]
        )
        total, mem = merge_halo(last, n, gh_in_ref, gmem_in_ref, from_right_ref, from_left_ref)
        gain_sum = gain_sum + col_sum(total * scaled)
        bias_sum = bias_sum + col_sum(total)
        grad = gz_in_ref[rows, :] + norm_backward(total, scaled, inverse, gain)
        grad_ref[rows, :] = grad
        grad_low_ref[rows, :] = grad.astype(BF16)
        grad_mem_ref[pl.ds(n * sizes.segs, sizes.segs), :] = mem
    upper_vec[pl.ds(0, 1), :] = gain_sum
    upper_vec[pl.ds(2, 1), :] = bias_sum
    gain = gains_ref[0, pl.ds(1, 1), :]
    hidden, scaled, inverse = norm_forward(
        mixed_ref[...], gain, biases_ref[4, pl.ds(0, 1), :]
    )
    hidden_ref[...] = hidden.astype(BF16)
    grad_hidden_ref[...] = jnp.zeros_like(grad_hidden_ref)
    wait_all(ffn_copies)

    def body(c, carry):
        at_lane = pl.multiple_of(c * wide, wide)
        grad_hidden_ref[...] += ffn_back_step(
            sizes, c, wide, grad_low_ref[...], hidden_ref[...],
            active_ref[:, pl.ds(at_lane, wide)], slope_ref[:, pl.ds(at_lane, wide)].astype(F32),
            up_ref, down_ref, gup_ref, gdown_ref, vec,
        )
        return carry

    lax.fori_loop(0, sizes.ff // wide, body, 0)
    out_at = len(ffn_copies) + len(attn_copies)
    outs = start_out(
        ffn_pairs(mats, spots, outs_to, gup_ref, gdown_ref, place_ref), sems, out_at
    )
    grad_hidden = grad_hidden_ref[...]
    grad = grad_ref[...]
    vec[pl.ds(1, 1), :] = col_sum(grad_hidden * scaled)
    vec[pl.ds(6, 1), :] = col_sum(grad_hidden)
    vec[pl.ds(7, 1), :] = col_sum(grad)
    gz = grad + norm_backward(grad_hidden, scaled, inverse, gain)
    gz_ref[...] = gz

    def scaled_rows(n):
        before = left_ref[n, pl.ds(left_ref.shape[1] - LEFT_ROWS, LEFT_ROWS), :]
        parts = (frames_ref[n], right_ref[n], before)
        first_gain = gains_ref[0, pl.ds(0, 1), :]
        first_bias = biases_ref[0, pl.ds(0, 1), :]
        return [norm_forward(part.astype(F32), first_gain, first_bias)[1] for part in parts]

    wait_all(attn_copies)
    attn_back_stage(
        sizes, seqs, gz, grad_mem_ref, att_ref, proj_ref, probs_ref, z_ref, qkv_ref, out_ref,
        gqkv_ref, gout_ref, go_ref, gproj_ref, branch_ref, vec, gh_ref, gmem_ref, back_left_ref,
        back_right_ref, scaled_rows,
    )
    outs = outs + start_out(
        attn_pairs(mats, spots, outs_to, gqkv_ref, gout_ref, place_ref),
        sems,
        out_at + len(outs),
    )
    parts = sizes.width // LANES
    for layer, total in enumerate((vec[...], last_vec[...] + upper_vec[...])):
        for part in range(parts):
            small_ref[pl.ds((layer * parts + part) * TILE, TILE), :] = total[
                :, part * LANES : (part + 1) * LANES
            ].astype(BF16)
    outs = outs + start_out([(ref, small_ref) for ref in small], sems, out_at + len(outs))
    wait_all(outs)


def frames_grad_kernel(
    sizes, seqs, frames_ref, gz_ref, gh_ref, gmem_ref, from_right_ref, from_left_ref, gains_ref,
    biases_ref, grad_ref
):
    gain = gains_ref[0, pl.ds(0, 1), :]
    for n in range(seqs):
        _, scaled, inverse = norm_forward(
            frames_ref[n].astype(F32), gain, biases_ref[0, pl.ds(0, 1), :]
        )
        total, mem = merge_halo(sizes, n, gh_ref, gmem_ref, from_right_ref, from_left_ref)
        grad_ref[n] = (
            gz_ref[pl.ds(n * sizes.rows, sizes.rows), :]
            + norm_backward(total, scaled, inverse, gain)
            + segment_spread(sizes.rows, sizes.width, mem * (1.0 / SEG_LEN))
        )


def shifted(value, axis, by):
    size = lax.axis_size(axis)
    pairs = [(i, i + by) for i in range(size) if 0 <= i + by < size]
    return lax.ppermute(value, axis, pairs)


def permuted(value, move):
    reps = lax.axis_size("rep")
    pairs = []
    for flat in range(lax.axis_size("seg") * reps):
        seg, rep = divmod(flat, reps)
        z, y, x, core = move(seg // CHIPS_Y, seg % CHIPS_Y, rep // 2, rep % 2)
        pairs.append((flat, (z * CHIPS_Y + y) * reps + 2 * x + core))
    return lax.ppermute(value, ("seg", "rep"), pairs)


def across_first(value):
    return permuted(value, lambda z, y, x, c: (z, y, x ^ 1, c) if c == 0 else (z, y ^ 1, x, c))


def across_second(value):
    return permuted(value, lambda z, y, x, c: (z, y ^ 1, x, c) if c == 0 else (z, y, x ^ 1, c))


def other_core(value):
    return permuted(value, lambda z, y, x, c: (z, y, x, c ^ 1))


def after(value, *others):
    return lax.optimization_barrier((value,) + others)[0]


def swap_z(blocks):
    groups = [
        [z * CHIPS_Y + y for z in range(CHIPS_Z)] for y in range(CHIPS_Y)
    ]
    return lax.all_to_all(blocks, "seg", 0, 0, axis_index_groups=groups, tiled=True)


def gather_sides(here):
    return [here, across_first(here), across_second(here)]


def both_cores(blocks):
    return blocks + [other_core(block) for block in blocks]


def summed(*parts):
    total = parts[0].astype(F32)
    for part in parts[1:]:
        total = total + part.astype(F32)
    return total.astype(BF16)


def sum_everywhere(value):
    count = lax.axis_size("seg") * lax.axis_size("rep")
    bit = 1
    while bit < count:
        value = value + lax.ppermute(value, ("seg", "rep"), [(i, i ^ bit) for i in range(count)])
        bit *= 2
    return value


def vmem_spec():
    return pl.BlockSpec(memory_space=pltpu.VMEM)


def smem_spec():
    return pl.BlockSpec(memory_space=pltpu.SMEM)


def hbm_spec():
    return pl.BlockSpec(memory_space=pl.ANY)


def call(body, in_specs, out_shapes, out_specs, scratch, args, flops=0, moved=0, grid=(), aliases={}, vmem=12):
    return pl.pallas_call(
        body,
        grid=grid,
        input_output_aliases=aliases,
        in_specs=in_specs,
        out_shape=tuple(jax.ShapeDtypeStruct(shape, kind) for shape, kind in out_shapes),
        out_specs=tuple(out_specs),
        scratch_shapes=scratch,
        compiler_params=pltpu.CompilerParams(vmem_limit_bytes=vmem * MIB),
        cost_estimate=pl.CostEstimate(flops=flops, bytes_accessed=moved, transcendentals=0),
    )(*args)


def on_device(
    frames,
    utt_segments,
    out_grad,
    qkv_weight,
    out_weight,
    ffn_in_weight,
    ffn_out_weight,
    norm_gains,
    biases,
    ffn_bias,
):
    micros, groups, rows, width = frames.shape
    seqs = micros * groups
    ff = ffn_bias.shape[1]
    reps = lax.axis_size("rep")
    seg_count = lax.axis_size("seg")
    mats = Matrices(width, ff)
    by_blocks = width // reps == LANES and reps == 4 and seg_count == BLOCKS
    first = Sizes(rows, width, ff, True)
    last = Sizes(rows, width, ff, False)
    own = seqs * rows
    mem_own = seqs * first.segs

    seg_at = lax.axis_index("seg")
    seg_base = seg_at * first.segs
    rep_at = lax.axis_index("rep")
    place = [seg_base, jnp.int32(first.segs * seg_count)]
    y_at, x_at, core_at = seg_at % CHIPS_Y, rep_at // 2, rep_at % 2
    for other in range(2):
        core = lax.bitwise_xor(core_at, other)
        for hop2 in range(2):
            for hop1 in range(2):
                x_hop = jnp.where(core == 0, hop1, hop2)
                y_hop = jnp.where(core == 0, hop2, hop1)
                place.append(lax.bitwise_xor(y_at, y_hop))
                place.append((lax.bitwise_xor(x_at, x_hop) * 2 + core) * LANES)
    place = jnp.stack([jnp.asarray(entry, jnp.int32) for entry in place])
    lengths = utt_segments.reshape(seqs, utt_segments.shape[2])
    starts = (jnp.cumsum(lengths, axis=1) - lengths).astype(jnp.int32)
    zero_bias = jnp.zeros((1, width), F32)
    row_biases = [
        jnp.concatenate([biases[l : l + 1, 1], zero_bias, biases[l : l + 1, 2]], axis=1)
        for l in range(LAYERS)
    ]
    biases_by_row = jnp.swapaxes(biases, 0, 1)

    frames_own = frames.reshape(seqs, rows, width)
    grads_own = out_grad.reshape(seqs, rows, width)
    far = MEM_LEN * SEG_LEN
    frames_left = shifted(frames_own[:, rows - far :], "seg", 1)
    frames_right = shifted(frames_own[:, :RIGHT_ROWS], "seg", -1)

    attn_rows, ffn_rows = mats.attn_rows, mats.ffn_rows
    if by_blocks:
        qkv_t, out_t, down_t = (
            jnp.swapaxes(member, 1, 2) for member in (qkv_weight, out_weight, ffn_out_weight)
        )
        all_rows = attn_rows + ffn_rows
        spots = Spots(mats)
        shards = call(
            lambda *refs: pack_kernel(spots, *refs),
            [vmem_spec()] * 4,
            [((CHIPS_Z, all_rows, LANES), BF16)] * LAYERS,
            [vmem_spec()] * LAYERS,
            [],
            (qkv_t, out_t, ffn_in_weight, down_t),
        )
        sides0 = gather_sides(after(swap_z(shards[0]), frames_left, frames_right))
        place, starts, row_biases, sent = lax.optimization_barrier(
            (place, starts, row_biases, after(shards[1], sides0[0]))
        )
        sides1 = gather_sides(swap_z(sent))
        first_all = both_cores(sides0 + [across_second(after(sides0[1], sides1[0]))])
        classes = len(first_all) // 2
        grad_outs0 = [((2, 2, CHIPS_Z * all_rows + SMALL_ROWS, LANES), BF16)] * 2
        grad_outs1 = [((2, CHIPS_Z, 2 * all_rows, LANES), BF16)] * 2
        copies_in = len(first_all) * (3 + mats.down_parts)
    else:
        whole = []
        for member, shape in zip(
            (qkv_weight, out_weight, ffn_in_weight, ffn_out_weight),
            (mats.qkv, mats.out, mats.up, mats.down),
        ):
            member = lax.all_gather(member, "rep", axis=1, tiled=True)
            member = lax.all_gather(member, "seg", axis=2, tiled=True)
            whole.append(jnp.swapaxes(member, 1, 2).reshape((LAYERS,) + shape))
        first_all = [member[0] for member in whole]
        last_all = [member[1] for member in whole]
        spots = None
        grad_outs0 = grad_outs1 = [
            (shape, BF16) for shape in (mats.qkv, mats.out, mats.up, mats.down)
        ]
        copies_in = 4
    dma = pltpu.SemaphoreType.DMA

    matrices = [pltpu.VMEM(shape, BF16) for shape in (mats.qkv, mats.out, mats.up, mats.down)]

    (
        z0, proj0, probs0, att0, mixed0, mem1, x1, active0, slope0, low1, send_right, send_left,
    ) = call(
        lambda *refs: first_layer_kernel(
            first, seqs, mats, spots, len(first_all), *refs
        ),
        [smem_spec()] * 2 + [vmem_spec()] * 7 + [hbm_spec()] * len(first_all),
        [
            ((seqs * first.ext, width), BF16),
            ((seqs * first.ext, 3 * width), BF16),
            ((seqs * first.pairs, first.keys, 2 * first.queries), BF16),
            ((seqs * first.queries, width), BF16),
            ((own, width), F32),
            ((mem_own, width), F32),
            ((own, width), F32),
            ((own, ff), BF16),
            ((own, ff), BF16),
            ((own, width), BF16),
            ((seqs, BACK_ROWS, width), BF16),
            ((seqs, RIGHT_ROWS, width), BF16),
        ],
        [vmem_spec()] * 12,
        matrices
        + [
            pltpu.VMEM((seqs, first.keys, 2 * first.queries), F32),
            pltpu.VMEM((own, width), BF16),
            dma((copies_in,)),
        ],
        (place, starts, frames_own, frames_left, frames_right, norm_gains, biases_by_row, ffn_bias,
         row_biases[0]) + tuple(first_all),
        flops=24 * own * (4 * width * width + 2 * width * ff) // 2,
        moved=2 * (4 * width * width + 2 * width * ff),
        vmem=24,
    )
    left1 = shifted(send_right, "seg", 1)
    right1 = shifted(send_left, "seg", -1)
    if by_blocks:
        last_side = across_second(after(sides1[1], sides1[2], left1, right1))
        last_all = both_cores(sides1 + [last_side])

    vec_shape = (TILE, width)
    outs = call(
        lambda *refs: last_layer_kernel(
            last, seqs, mats, spots, len(last_all), len(grad_outs1), *refs
        ),
        [smem_spec()] * 2 + [vmem_spec()] * 10 + [hbm_spec()] * len(last_all),
        [
            ((seqs, rows, width), F32),
            ((own, width), F32),
            ((own, width), F32),
            ((mem_own, width), F32),
            ((seqs, BACK_ROWS, width), BF16),
            ((seqs, RIGHT_ROWS, width), BF16),
            (vec_shape, F32),
        ]
        + grad_outs1,
        [vmem_spec()] * 7 + [hbm_spec()] * len(grad_outs1),
        matrices
        + matrices
        + [
            pltpu.VMEM((seqs, last.keys, 2 * last.queries), F32),
            pltpu.VMEM((seqs * last.ext, width), BF16),
            pltpu.VMEM((seqs * last.ext, 3 * width), BF16),
            pltpu.VMEM((seqs * last.pairs, last.keys, 2 * last.queries), BF16),
            pltpu.VMEM((seqs * last.queries, width), BF16),
            pltpu.VMEM((own, width), BF16),
            pltpu.VMEM((seqs * last.queries, width), BF16),
            pltpu.VMEM((seqs * last.ext, 3 * width), BF16),
            pltpu.VMEM((seqs * last.queries, width), BF16),
            pltpu.VMEM((own, width), BF16),
            pltpu.VMEM((own, width), F32),
            dma((2 * copies_in,)),
        ],
        (place, starts, low1, left1, right1, mem1, x1, grads_own, norm_gains, biases_by_row, ffn_bias,
         row_biases[1]) + tuple(last_all),
        flops=30 * own * (4 * width * width + 2 * width * ff),
        moved=4 * (4 * width * width + 2 * width * ff),
        vmem=34,
    )
    encoded, gz1, gh1, gmem1, back_left1, back_right1, vec1 = outs[:7]
    grad_blocks1 = outs[7:]
    from_right1 = shifted(back_left1, "seg", -1)
    from_left1 = shifted(back_right1, "seg", 1)

    gh1_tied = gh1
    if by_blocks:
        mine1, theirs1 = grad_blocks1[0], other_core(grad_blocks1[1])
        far1 = summed(mine1[1], theirs1[1])
        gh1_tied = after(gh1, far1)
    gz0, gh0, gmem0, back_left0, back_right0, upper_vec, vec0, *grad_blocks0 = call(
        lambda *refs: first_back_kernel(
            last, first, seqs, mats, spots, len(first_all), len(grad_outs0), *refs
        ),
        [smem_spec()] + [vmem_spec()] * 19 + [hbm_spec()] * len(first_all),
        [
            ((own, width), F32),
            ((own, width), F32),
            ((mem_own, width), F32),
            ((seqs, BACK_ROWS, width), BF16),
            ((seqs, RIGHT_ROWS, width), BF16),
            (vec_shape, F32),
            (vec_shape, F32),
        ]
        + grad_outs0,
        [vmem_spec()] * 7 + [hbm_spec()] * len(grad_outs0),
        matrices
        + matrices
        + [
            pltpu.VMEM((own, width), BF16),
            pltpu.VMEM((own, width), BF16),
            pltpu.VMEM((own, width), F32),
            pltpu.VMEM((own, width), F32),
            pltpu.VMEM((mem_own, width), F32),
            pltpu.VMEM((seqs * first.queries, width), BF16),
            pltpu.VMEM((seqs * first.ext, 3 * width), BF16),
            pltpu.VMEM((seqs * first.queries, width), BF16),
            pltpu.VMEM((SMALL_ROWS, LANES), BF16),
            dma((2 * copies_in + 8,)),
        ],
        (place, x1, gz1, gh1_tied, gmem1, from_right1, from_left1, mixed0, active0, slope0, att0,
         probs0, proj0, z0, frames_own, frames_left, frames_right, norm_gains, biases_by_row, vec1)
        + tuple(first_all),
        flops=28 * own * (4 * width * width + 2 * width * ff),
        moved=4 * (4 * width * width + 2 * width * ff),
        vmem=34,
    )
    from_right0 = shifted(back_left0, "seg", -1)
    from_left0 = shifted(back_right0, "seg", 1)
    gz0_last = gz0
    if by_blocks:
        second1 = across_second(far1)
        mine0, theirs0 = grad_blocks0[0], other_core(after(grad_blocks0[1], second1))
        both1 = summed(mine1[0], theirs1[0], second1)
        lines1 = swap_z(both1)
        far0 = summed(mine0[1], after(theirs0, both1, from_right0, from_left0)[1])
        second0 = across_second(far0)
        mid0 = summed(mine0[0, 1], theirs0[0, 1], second0[1])
        first0 = across_first(mid0)
        held0 = summed(mine0[0, 0], theirs0[0, 0], after(second0, mid0)[0])
        near0 = summed(held0, first0)
        blocks = CHIPS_Z * all_rows
        near0 = jnp.concatenate(
            [
                near0[:blocks].reshape(CHIPS_Z, all_rows, LANES),
                jnp.broadcast_to(near0[None, blocks:], (CHIPS_Z, SMALL_ROWS, LANES)),
            ],
            axis=1,
        )
        first_parts = swap_z(near0)
        gz0_last, lines1 = lax.optimization_barrier((after(gz0, near0), lines1))
        cross1 = jnp.sum(lines1[:, all_rows:].astype(F32), axis=0, keepdims=True).astype(BF16)
        first1 = across_first(cross1)
    frames_grad = call(
        lambda *refs: frames_grad_kernel(first, seqs, *refs),
        [vmem_spec()] * 8,
        [((seqs, rows, width), F32)],
        [vmem_spec()],
        [],
        (frames_own, gz0_last, gh0, gmem0, from_right0, from_left0, norm_gains, biases_by_row),
    )[0]

    if by_blocks:
        shapes = [member.shape for member in (qkv_t, out_t, ffn_in_weight, down_t)]
        held = [pltpu.VMEM(shape[1:], F32) for shape in shapes]
        whole = [(shape, F32) for shape in shapes]
        written = call(
            lambda *refs: unpack_last_kernel(spots, LAYERS - 1, *refs),
            [
                pl.BlockSpec((CHIPS_Z, all_rows, LANES), lambda i: (0, 0, 0)),
                pl.BlockSpec((1, all_rows, LANES), lambda i: (0, 0, 0)),
            ],
            whole,
            [hbm_spec()] * 4,
            held + [dma((4,))],
            [lines1, first1],
            grid=(1,),
        )
        small_shapes = [norm_gains.shape, (biases.shape[1], LAYERS, width), ffn_bias.shape]
        reduced = call(
            lambda *refs: unpack_first_kernel(spots, all_rows, *refs),
            [vmem_spec()] + [hbm_spec()] * 4,
            whole + [(shape, F32) for shape in small_shapes],
            [hbm_spec()] * 4 + [vmem_spec()] * 3,
            held + [dma((4,))],
            [after(first_parts, frames_grad)] + list(written),
            aliases={1 + i: i for i in range(4)},
        )
        small = reduced[4], jnp.swapaxes(reduced[5], 0, 1), reduced[6]
        reduced = [
            jnp.swapaxes(reduced[0], 1, 2),
            jnp.swapaxes(reduced[1], 1, 2),
            reduced[2],
            jnp.swapaxes(reduced[3], 1, 2),
        ]
    else:
        reduced = []
        for member0, member1 in zip(grad_blocks0, grad_blocks1):
            both = jnp.stack([member0, member1]).reshape(LAYERS, -1, member0.shape[3])
            both = jnp.swapaxes(both, 1, 2)
            both = lax.psum_scatter(both, "seg", scatter_dimension=2, tiled=True)
            both = lax.psum_scatter(both, "rep", scatter_dimension=1, tiled=True)
            reduced.append(both.astype(F32))
        small = sum_everywhere(jnp.stack([vec0, vec1 + upper_vec]))
        small = small[:, 0:2], small[:, 2:8], small[:, 8:12].reshape(ffn_bias.shape)

    return (
        encoded.reshape(frames.shape),
        frames_grad.reshape(frames.shape),
        reduced[0],
        reduced[1],
        reduced[2],
        reduced[3],
        small[0],
        small[1],
        small[2],
    )


def solution(mesh):
    in_specs = (
        P(None, "rep", "seg", None),
        P(None, "rep", None),
        P(None, "rep", "seg", None),
        P(None, "rep", "seg"),
        P(None, "rep", "seg"),
        P(None, "rep", "seg"),
        P(None, "rep", "seg"),
        P(),
        P(),
        P(),
    )
    out_specs = (
        P(None, "rep", "seg", None),
        P(None, "rep", "seg", None),
        P(None, "rep", "seg"),
        P(None, "rep", "seg"),
        P(None, "rep", "seg"),
        P(None, "rep", "seg"),
        P(),
        P(),
        P(),
    )
    return jax.shard_map(
        on_device, mesh=mesh, in_specs=in_specs, out_specs=out_specs, check_vma=False
    )
```

```python
import jax
import jax.numpy as jnp
from jax import lax
from jax.experimental import pallas as pl
from jax.experimental.pallas import tpu as pltpu
from jax.sharding import PartitionSpec as P

HEADS = 8
SEG_LEN = 16
LEFT_LEN = 30
RIGHT_LEN = 4
MEM_LEN = 4
LAYERS = 2

EPS = 1e-05
ROOT_HALF = 0.7071067811865476
INV_ROOT_TWO_PI = 0.3989422804014327

LANES = 128
TILE = 16
RIGHT_ROWS = 16
LEFT_ROWS = 32
MEM_ROWS = 16
BACK_ROWS = LEFT_ROWS + MEM_ROWS
CHIPS_Z = 4
CHIPS_Y = 2
BLOCKS = CHIPS_Z * CHIPS_Y
SMALL_ROWS = 128
MIB = 1024 * 1024

BF16 = jnp.bfloat16
F32 = jnp.float32


def nn(a, b):
    return lax.dot_general(a, b, (((1,), (0,)), ((), ())), preferred_element_type=F32)


def nt(a, b):
    return lax.dot_general(a, b, (((1,), (1,)), ((), ())), preferred_element_type=F32)


def tn(a, b):
    return lax.dot_general(a, b, (((0,), (0,)), ((), ())), preferred_element_type=F32)


def col_sum(value):
    return jnp.sum(value, axis=0, keepdims=True)


def norm_forward(inputs, gain, bias):
    center = inputs - jnp.mean(inputs, axis=1, keepdims=True)
    inverse = lax.rsqrt(jnp.mean(center * center, axis=1, keepdims=True) + EPS)
    scaled = center * inverse
    return scaled * gain + bias, scaled, inverse


def norm_backward(grad_in, scaled, inverse, gain):
    grad_scaled = grad_in * gain
    return inverse * (
        grad_scaled
        - jnp.mean(grad_scaled, axis=1, keepdims=True)
        - scaled * jnp.mean(grad_scaled * scaled, axis=1, keepdims=True)
    )


def segment_mean(inputs):
    rows, width = inputs.shape
    return jnp.mean(inputs.reshape(rows // SEG_LEN, SEG_LEN, width), axis=1)


def segment_spread(rows, width, per_segment):
    segs = rows // SEG_LEN
    return jnp.broadcast_to(per_segment[:, None, :], (segs, SEG_LEN, width)).reshape(rows, width)


def identity(size):
    row = lax.broadcasted_iota(jnp.int32, (size, size), 0)
    col = lax.broadcasted_iota(jnp.int32, (size, size), 1)
    return (row == col).astype(F32).astype(BF16)


class Sizes:
    def __init__(self, rows, width, ff, with_summary):
        self.rows = rows
        self.width = width
        self.ff = ff
        self.segs = rows // SEG_LEN
        self.top = TILE if with_summary else 0
        self.keys = rows + RIGHT_ROWS + LEFT_ROWS + MEM_ROWS
        self.ext = self.top + self.keys
        self.queries = self.top + rows
        self.right_at = self.top + rows
        self.left_at = self.right_at + RIGHT_ROWS
        self.mem_at = self.left_at + LEFT_ROWS
        self.pairs = width // LANES


class Matrices:
    def __init__(self, width, ff):
        self.qkv = (CHIPS_Z, CHIPS_Y, 3 * width // BLOCKS, width)
        self.out = (CHIPS_Z, CHIPS_Y, width // BLOCKS, width)
        self.up = (CHIPS_Z, CHIPS_Y, ff // BLOCKS, width)
        self.down = (CHIPS_Z, CHIPS_Y, width // BLOCKS, ff)
        self.down_parts = ff // width
        self.attn_rows = self.qkv[2] + self.out[2]
        self.ffn_rows = self.up[2] + self.down_parts * self.down[2]


class Spots:
    def __init__(self, mats):
        high, wide, up, low = mats.qkv[2], mats.out[2], mats.up[2], mats.down[2]
        self.qkv = (0, 0)
        self.out = (0, high)
        self.up = (0, high + wide)
        self.down = [(0, high + wide + up + low * part) for part in range(mats.down_parts)]


def attn_pairs(mats, spots, groups, qkv_ref, out_ref, place_ref):
    if spots is None:
        return [(groups[0], qkv_ref), (groups[1], out_ref)]
    pairs = []
    for k in range(len(groups[0])):
        row = place_ref[2 + 2 * k]
        lane = pl.multiple_of(place_ref[3 + 2 * k], LANES)
        for (group, first), ref, shape in (
            (spots.qkv, qkv_ref, mats.qkv),
            (spots.out, out_ref, mats.out),
        ):
            block = groups[group][k]
            pairs.append(
                (
                    block.at[:, pl.ds(first, shape[2]), :],
                    ref.at[:, row, :, pl.ds(lane, LANES)],
                )
            )
    return pairs


def ffn_pairs(mats, spots, groups, up_ref, down_ref, place_ref):
    if spots is None:
        return [(groups[2], up_ref), (groups[3], down_ref)]
    pairs = []
    for k in range(len(groups[0])):
        row = place_ref[2 + 2 * k]
        lane = pl.multiple_of(place_ref[3 + 2 * k], LANES)
        group, first = spots.up
        block = groups[group][k]
        pairs.append(
            (block.at[:, pl.ds(first, mats.up[2]), :], up_ref.at[:, row, :, pl.ds(lane, LANES)])
        )
        for part, (group, first) in enumerate(spots.down):
            there = pl.multiple_of(
                place_ref[3 + 2 * k] * mats.down_parts + part * LANES, LANES
            )
            block = groups[group][k]
            pairs.append(
                (
                    block.at[:, pl.ds(first, mats.down[2]), :],
                    down_ref.at[:, row, :, pl.ds(there, LANES)],
                )
            )
    return pairs


def start_in(pairs, sems, at):
    copies = [pltpu.make_async_copy(s, d, sems.at[at + i]) for i, (s, d) in enumerate(pairs)]
    for copy in copies:
        copy.start()
    return copies


def start_out(pairs, sems, at):
    copies = [pltpu.make_async_copy(d, s, sems.at[at + i]) for i, (s, d) in enumerate(pairs)]
    for copy in copies:
        copy.start()
    return copies


def in_groups(spots, refs):
    return refs if spots is None else [refs]


def wait_all(copies):
    for copy in copies:
        copy.wait()


def fill_mask(sizes, seqs, starts_ref, place_ref, mask_ref):
    shape = (sizes.keys, 2 * sizes.queries)
    key = lax.broadcasted_iota(jnp.int32, shape, 0)
    col = lax.broadcasted_iota(jnp.int32, shape, 1)
    col = jnp.where(col < sizes.queries, col, col - sizes.queries)
    base = place_ref[0]
    total = place_ref[1]
    query = jnp.where(col < sizes.top, col, lax.shift_right_arithmetic(col - sizes.top, 4))
    left_at = sizes.rows + RIGHT_ROWS
    mem_at = left_at + LEFT_ROWS
    spot = jnp.where(key < left_at, key, key - mem_at)
    mem_seg = jnp.where(key < mem_at + sizes.segs, key - mem_at, key - mem_at - 2 * sizes.segs)
    key_seg = jnp.where(key < mem_at, lax.shift_right_arithmetic(spot, 4), mem_seg)
    near = (
        (key_seg == query)
        | ((spot >= query * SEG_LEN - LEFT_LEN) & (spot < query * SEG_LEN))
        | ((key_seg == query + 1) & (spot < query * SEG_LEN + SEG_LEN + RIGHT_LEN))
    )
    recent = (key_seg >= query - MEM_LEN) & (key_seg < query) & (col >= sizes.top)
    allowed = ((key < mem_at) & near) | ((key >= mem_at) & recent)
    key_abs = key_seg + base
    query_abs = query + base
    allowed = allowed & (key_abs >= 0) & (key_abs < total)
    if sizes.top:
        allowed = allowed & ((col < sizes.segs) | (col >= sizes.top))
    for n in range(seqs):
        key_owner = jnp.zeros(shape, jnp.int32)
        query_owner = jnp.zeros(shape, jnp.int32)
        for u in range(starts_ref.shape[1]):
            first = starts_ref[n, u]
            key_owner = key_owner + (key_abs >= first).astype(jnp.int32)
            query_owner = query_owner + (query_abs >= first).astype(jnp.int32)
        mask_ref[n] = jnp.where(allowed & (key_owner == query_owner), 0.0, -1e30)


def half_masks():
    lane = lax.broadcasted_iota(jnp.int32, (1, LANES), 1)
    even = (lane < LANES // 2).astype(F32)
    return even.astype(BF16), (1.0 - even).astype(BF16), lane < LANES // 2


def project(sizes, z_ref, qkv_ref, row_bias_ref, proj_ref):
    step = CHIPS_Z // 2
    for c in range(2):
        block = qkv_ref[pl.ds(c * step, step)].reshape(-1, sizes.width)
        wide = block.shape[0]
        made = nt(z_ref[...], block) + row_bias_ref[:, pl.ds(c * wide, wide)]
        proj_ref[:, pl.ds(c * wide, wide)] = made.astype(BF16)


def attend(sizes, seqs, proj_ref, mask_ref, probs_ref, att_ref):
    even, odd, is_even = half_masks()
    scale = (sizes.width // HEADS) ** (-0.5)
    count = sizes.queries

    def body(p, carry):
        for n in range(seqs):
            lane = pl.multiple_of(p * LANES, LANES)
            query = proj_ref[pl.ds(n * sizes.ext, count), pl.ds(lane, LANES)]
            first = n * sizes.ext + sizes.top
            key = proj_ref[pl.ds(first, sizes.keys), pl.ds(sizes.width + lane, LANES)]
            value = proj_ref[pl.ds(first, sizes.keys), pl.ds(2 * sizes.width + lane, LANES)]
            queries = jnp.concatenate([query * even, query * odd], axis=0)
            scores = nt(key, queries) * scale + mask_ref[n]
            scores = jnp.exp(scores - jnp.max(scores, axis=0, keepdims=True))
            probs = (scores * (1.0 / jnp.sum(scores, axis=0, keepdims=True))).astype(BF16)
            probs_ref[n * sizes.pairs + p] = probs
            out = tn(probs, value)
            att_ref[pl.ds(n * count, count), pl.ds(lane, LANES)] = jnp.where(
                is_even, out[:count], out[count:]
            ).astype(BF16)
        return carry

    lax.fori_loop(0, sizes.pairs, body, 0, unroll=True)


def attend_back(sizes, seqs, proj_ref, probs_ref, go_ref, gproj_ref):
    even, odd, is_even = half_masks()
    scale = (sizes.width // HEADS) ** (-0.5)
    count = sizes.queries
    wide = sizes.width
    for n in range(seqs):
        base = n * sizes.ext
        rest = sizes.ext - count
        gproj_ref[pl.ds(base + count, rest), pl.ds(0, wide)] = jnp.zeros((rest, wide), BF16)
        if sizes.top:
            gproj_ref[pl.ds(base, sizes.top), pl.ds(wide, 2 * wide)] = jnp.zeros(
                (sizes.top, 2 * wide), BF16
            )

    def body(p, carry):
        for n in range(seqs):
            lane = pl.multiple_of(p * LANES, LANES)
            base = n * sizes.ext
            first = base + sizes.top
            query = proj_ref[pl.ds(base, count), pl.ds(lane, LANES)]
            key = proj_ref[pl.ds(first, sizes.keys), pl.ds(wide + lane, LANES)]
            value = proj_ref[pl.ds(first, sizes.keys), pl.ds(2 * wide + lane, LANES)]
            grad = go_ref[pl.ds(n * count, count), pl.ds(lane, LANES)]
            queries = jnp.concatenate([query * even, query * odd], axis=0)
            grads = jnp.concatenate([grad * even, grad * odd], axis=0)
            probs_low = probs_ref[n * sizes.pairs + p]
            grad_values = nn(probs_low, grads)
            probs = probs_low.astype(F32)
            weighted = nt(value, grads) * probs
            grad_scores = (
                (weighted - probs * jnp.sum(weighted, axis=0, keepdims=True)) * scale
            ).astype(BF16)
            grad_keys = nn(grad_scores, queries)
            grad_both = tn(grad_scores, key)
            grad_query = jnp.where(is_even, grad_both[:count], grad_both[count:])
            gproj_ref[pl.ds(base, count), pl.ds(lane, LANES)] = grad_query.astype(BF16)
            gproj_ref[pl.ds(first, sizes.keys), pl.ds(wide + lane, LANES)] = grad_keys.astype(BF16)
            gproj_ref[pl.ds(first, sizes.keys), pl.ds(2 * wide + lane, LANES)] = (
                grad_values.astype(BF16)
            )
        return carry

    lax.fori_loop(0, sizes.pairs, body, 0)


def gelu_both(upward):
    half = 0.5 * (1.0 + lax.erf(upward * ROOT_HALF))
    slope = half + upward * jnp.exp(-0.5 * upward * upward) * INV_ROOT_TWO_PI
    return upward * half, slope


def up_block(up_ref, c, wide):
    step = wide // (up_ref.shape[1] * up_ref.shape[2])
    return up_ref[pl.ds(c * step, step)].reshape(-1, up_ref.shape[3])


def down_block(down_ref, c, wide):
    at = pl.multiple_of(c * wide, wide)
    return down_ref[:, :, :, pl.ds(at, wide)].reshape(-1, wide)


def ffn_back_step(
    sizes, c, wide, grad_low, hidden_low, active, slope, up_ref, down_ref, gup_ref, gdown_ref, vec
):
    at = pl.multiple_of(c * wide, wide)
    up = up_block(up_ref, c, wide)
    down = down_block(down_ref, c, wide)
    grad_active = nn(grad_low, down)
    grad_up_f = grad_active * slope
    grad_up = grad_up_f.astype(BF16)
    gdown_ref[:, :, :, pl.ds(at, wide)] = (
        tn(grad_low, active).astype(BF16).reshape(gdown_ref.shape[:3] + (wide,))
    )
    step = wide // (gup_ref.shape[1] * gup_ref.shape[2])
    gup_ref[pl.ds(c * step, step)] = (
        tn(grad_up, hidden_low).astype(BF16).reshape((step,) + gup_ref.shape[1:])
    )
    vec[pl.ds(8 + c, 1), :] = col_sum(grad_up.astype(F32))
    return nn(grad_up, up)


def attn_back_stage(
    sizes, seqs, gz, grad_mem_ref, att_ref, proj_ref, probs_ref, z_ref, qkv_ref, out_ref,
    gqkv_ref, gout_ref, go_ref, gproj_ref, branch_ref, vec, gh_ref, gmem_ref, back_left_ref,
    back_right_ref, scaled_rows=None,
):
    wide = sizes.width
    count = sizes.queries
    bias_out = col_sum(gz)
    for n in range(seqs):
        if sizes.top:
            mem_grad = grad_mem_ref[pl.ds(n * sizes.segs, sizes.segs), :]
            bias_out = bias_out + col_sum(mem_grad)
            branch_ref[pl.ds(n * count, sizes.top), :] = jnp.concatenate(
                [mem_grad, jnp.zeros((sizes.top - sizes.segs, wide), F32)], axis=0
            ).astype(BF16)
        branch_ref[pl.ds(n * count + sizes.top, sizes.rows), :] = gz[
            n * sizes.rows : (n + 1) * sizes.rows
        ].astype(BF16)
    vec[pl.ds(5, 1), :] = bias_out
    branch = branch_ref[...]
    gout_ref[...] = tn(branch, att_ref[...]).astype(BF16).reshape(gout_ref.shape)
    go_ref[...] = nn(branch, out_ref[...].reshape(-1, wide)).astype(BF16)
    attend_back(sizes, seqs, proj_ref, probs_ref, go_ref, gproj_ref)
    vec[pl.ds(3, 1), :] = col_sum(gproj_ref[:, pl.ds(0, wide)].astype(F32))
    vec[pl.ds(4, 1), :] = col_sum(gproj_ref[:, pl.ds(2 * wide, wide)].astype(F32))
    grad_ext = nn(gproj_ref[...], qkv_ref[...].reshape(-1, wide))
    gain_sum = jnp.zeros((1, wide), F32)
    bias_sum = jnp.zeros((1, wide), F32)
    for n in range(seqs):
        base = n * sizes.ext
        own = grad_ext[base + sizes.top : base + sizes.top + sizes.rows]
        if sizes.top:
            spread = grad_ext[base : base + sizes.segs] * (1.0 / SEG_LEN)
            own = own + segment_spread(sizes.rows, wide, spread)
        gh_ref[pl.ds(n * sizes.rows, sizes.rows), :] = own
        mem = base + sizes.mem_at
        gmem_ref[pl.ds(n * sizes.segs, sizes.segs), :] = grad_ext[mem : mem + sizes.segs]
        left = base + sizes.left_at
        back_left_ref[n] = grad_ext[left : left + BACK_ROWS].astype(BF16)
        right = base + sizes.right_at
        back_right_ref[n] = grad_ext[right : right + RIGHT_ROWS].astype(BF16)
        if scaled_rows is not None:
            grads = (
                own,
                grad_ext[right : right + RIGHT_ROWS],
                grad_ext[left : left + LEFT_ROWS],
            )
            for rows, scaled in zip(grads, scaled_rows(n)):
                gain_sum = gain_sum + col_sum(rows * scaled)
                bias_sum = bias_sum + col_sum(rows)
    if scaled_rows is not None:
        vec[pl.ds(0, 1), :] = gain_sum
        vec[pl.ds(2, 1), :] = bias_sum
    step = CHIPS_Z // 2
    part = gqkv_ref.shape[1] * gqkv_ref.shape[2] * step
    for c in range(2):
        gqkv_ref[pl.ds(c * step, step)] = (
            tn(gproj_ref[:, pl.ds(c * part, part)], z_ref[...])
            .astype(BF16)
            .reshape((step,) + gqkv_ref.shape[1:])
        )


def merge_halo(sizes, n, gh_ref, gmem_ref, from_right_ref, from_left_ref):
    first = n * sizes.rows
    back = from_right_ref[n].astype(F32)
    head = gh_ref[pl.ds(first, RIGHT_ROWS), :] + from_left_ref[n].astype(F32)
    middle = gh_ref[pl.ds(first + RIGHT_ROWS, sizes.rows - RIGHT_ROWS - LEFT_ROWS), :]
    tail = gh_ref[pl.ds(first + sizes.rows - LEFT_ROWS, LEFT_ROWS), :] + back[:LEFT_ROWS]
    mem = gmem_ref[pl.ds(n * sizes.segs, sizes.segs), :] + back[LEFT_ROWS + sizes.segs :]
    return jnp.concatenate([head, middle, tail], axis=0), mem


def pack_kernel(spots, qkv_ref, out_ref, up_ref, down_ref, *packed):
    eye = identity(LANES)
    high, wide, low = qkv_ref.shape[1], out_ref.shape[1], down_ref.shape[1]
    for layer, ref in enumerate(packed):
        up = tn(up_ref[layer], eye).astype(BF16)
        for z in range(ref.shape[0]):
            ref[z, pl.ds(spots.qkv[1], high), :] = qkv_ref[layer]
            ref[z, pl.ds(spots.out[1], wide), :] = out_ref[layer]
            ref[z, pl.ds(spots.up[1], up_ref.shape[2]), :] = up
            for part, (_, first) in enumerate(spots.down):
                ref[z, pl.ds(first, low), :] = down_ref[layer, :, pl.ds(part * LANES, LANES)]


def unpack_layer(spots, sources, refs):
    qkv_ref, out_ref, up_ref, down_ref = refs
    high, wide, low = qkv_ref.shape[0], out_ref.shape[0], down_ref.shape[0]

    def total(first, rows):
        parts = [ref[z, pl.ds(first, rows), :] for ref in sources for z in range(ref.shape[0])]
        value = parts[0].astype(F32)
        for part in parts[1:]:
            value = value + part.astype(F32)
        return value

    qkv_ref[...] = total(spots.qkv[1], high)
    out_ref[...] = total(spots.out[1], wide)
    up_ref[...] = nt(identity(LANES), total(spots.up[1], up_ref.shape[1]).astype(BF16))
    for part, (_, first) in enumerate(spots.down):
        down_ref[:, pl.ds(part * LANES, LANES)] = total(first, low)
    return total


def store_layer(layer, held, outs, sems):
    copies = [
        pltpu.make_async_copy(ref, out.at[layer], sems.at[i])
        for i, (ref, out) in enumerate(zip(held, outs))
    ]
    for copy in copies:
        copy.start()
    return copies


def unpack_last_kernel(spots, layer, lines_ref, first_ref, *refs):
    outs, held, sems = refs[:4], refs[4:8], refs[8]
    unpack_layer(spots, (lines_ref, first_ref), held)
    wait_all(store_layer(layer, held, outs, sems))


def unpack_first_kernel(spots, small_at, parts_ref, *refs):
    outs, (gains_ref, biases_ref, ffn_bias_ref), held, sems = (
        refs[4:8], refs[8:11], refs[11:15], refs[15],
    )
    total = unpack_layer(spots, (parts_ref,), held)
    copies = store_layer(0, held, outs, sems)
    sums = total(small_at, SMALL_ROWS)
    parts = gains_ref.shape[2] // LANES
    for layer in range(gains_ref.shape[0]):
        for part in range(parts):
            lanes = pl.ds(part * LANES, LANES)
            block = sums[(layer * parts + part) * TILE : (layer * parts + part + 1) * TILE]
            gains_ref[layer, :, lanes] = block[0:2]
            for row in range(biases_ref.shape[0]):
                biases_ref[row, pl.ds(layer, 1), lanes] = block[2 + row : 3 + row]
            for row in range(ffn_bias_ref.shape[1] // gains_ref.shape[2]):
                at = row * gains_ref.shape[2] + part * LANES
                ffn_bias_ref[pl.ds(layer, 1), pl.ds(at, LANES)] = block[8 + row : 9 + row]
    wait_all(copies)


def first_layer_kernel(
    sizes, seqs, mats, spots, count_in, place_ref, starts_ref, frames_ref, left_ref, right_ref,
    gains_ref, biases_ref, ffn_bias_ref, row_bias_ref, *refs
):
    groups = in_groups(spots, refs[:count_in])
    (
        z_ref, proj_ref, probs_ref, att_ref, mixed_ref, mem_ref, next_ref, active_ref, slope_ref,
        low_ref, send_right_ref, send_left_ref, qkv_ref, out_ref, up_ref, down_ref, mask_ref,
        hidden_ref, sems,
    ) = refs[count_in:]
    wide = sizes.width
    copies = start_in(attn_pairs(mats, spots, groups, qkv_ref, out_ref, place_ref), sems, 0)
    ffn_copies = start_in(
        ffn_pairs(mats, spots, groups, up_ref, down_ref, place_ref), sems, len(copies)
    )
    gain = gains_ref[0, pl.ds(0, 1), :]
    bias = biases_ref[0, pl.ds(0, 1), :]
    pad = jnp.zeros((TILE - sizes.segs, wide), F32)
    for n in range(seqs):
        own = frames_ref[n].astype(F32)
        before = left_ref[n].astype(F32)
        hidden = norm_forward(own, gain, bias)[0]
        halo = norm_forward(before[before.shape[0] - LEFT_ROWS :], gain, bias)[0]
        after = norm_forward(right_ref[n].astype(F32), gain, bias)[0]
        memory = jnp.concatenate(
            [
                segment_mean(own),
                jnp.zeros((sizes.segs - before.shape[0] // SEG_LEN, wide), F32),
                segment_mean(before),
            ],
            axis=0,
        )
        base = n * sizes.ext
        z_ref[pl.ds(base, sizes.top), :] = jnp.concatenate(
            [segment_mean(hidden), pad], axis=0
        ).astype(BF16)
        z_ref[pl.ds(base + sizes.top, sizes.rows), :] = hidden.astype(BF16)
        z_ref[pl.ds(base + sizes.right_at, RIGHT_ROWS), :] = after.astype(BF16)
        z_ref[pl.ds(base + sizes.left_at, LEFT_ROWS), :] = halo.astype(BF16)
        z_ref[pl.ds(base + sizes.mem_at, MEM_ROWS), :] = memory.astype(BF16)
    fill_mask(sizes, seqs, starts_ref, place_ref, mask_ref)
    wait_all(copies)
    project(sizes, z_ref, qkv_ref, row_bias_ref, proj_ref)
    attend(sizes, seqs, proj_ref, mask_ref, probs_ref, att_ref)
    mixed = nt(att_ref[...], out_ref[...].reshape(-1, wide)) + biases_ref[3, pl.ds(0, 1), :]
    for n in range(seqs):
        base = n * sizes.queries
        mem_ref[pl.ds(n * sizes.segs, sizes.segs), :] = mixed[base : base + sizes.segs]
        mixed_ref[pl.ds(n * sizes.rows, sizes.rows), :] = (
            frames_ref[n].astype(F32) + mixed[base + sizes.top : base + sizes.top + sizes.rows]
        )
    mixed = mixed_ref[...]
    hidden, _, _ = norm_forward(mixed, gains_ref[0, pl.ds(1, 1), :], biases_ref[4, pl.ds(0, 1), :])
    hidden_ref[...] = hidden.astype(BF16)
    next_ref[...] = mixed + biases_ref[5, pl.ds(0, 1), :]
    wait_all(ffn_copies)

    def body(c, carry):
        at_lane = pl.multiple_of(c * wide, wide)
        upward = nt(hidden_ref[...], up_block(up_ref, c, wide))
        upward = upward + ffn_bias_ref[pl.ds(0, 1), pl.ds(at_lane, wide)]
        active, slope = gelu_both(upward)
        active = active.astype(BF16)
        active_ref[:, pl.ds(at_lane, wide)] = active
        slope_ref[:, pl.ds(at_lane, wide)] = slope.astype(BF16)
        next_ref[...] += nt(active, down_block(down_ref, c, wide))
        return carry

    lax.fori_loop(0, sizes.ff // wide, body, 0)
    low, _, _ = norm_forward(
        next_ref[...], gains_ref[1, pl.ds(0, 1), :], biases_ref[0, pl.ds(1, 1), :]
    )
    low = low.astype(BF16)
    low_ref[...] = low
    for n in range(seqs):
        base = n * sizes.rows
        send_right_ref[n, pl.ds(0, LEFT_ROWS), :] = low[
            base + sizes.rows - LEFT_ROWS : base + sizes.rows
        ]
        send_right_ref[n, pl.ds(LEFT_ROWS, MEM_ROWS), :] = jnp.concatenate(
            [
                mem_ref[pl.ds(n * sizes.segs, sizes.segs), :],
                jnp.zeros((MEM_ROWS - sizes.segs, wide), F32),
            ],
            axis=0,
        ).astype(BF16)
        send_left_ref[n] = low[base : base + RIGHT_ROWS]


def last_layer_kernel(
    sizes, seqs, mats, spots, count_in, count_out, place_ref, starts_ref, low_ref, left_ref,
    right_ref, mem_ref, inputs_ref, out_grad_ref, gains_ref, biases_ref, ffn_bias_ref,
    row_bias_ref, *refs
):
    groups = in_groups(spots, refs[:count_in])
    (encoded_ref, gz_ref, gh_ref, gmem_ref, back_left_ref, back_right_ref, vec) = refs[
        count_in : count_in + 7
    ]
    hbm_out = refs[count_in + 7 : count_in + 7 + count_out]
    (
        qkv_ref, out_ref, up_ref, down_ref, gqkv_ref, gout_ref, gup_ref, gdown_ref, mask_ref,
        z_ref, proj_ref, probs_ref, att_ref, hidden_ref, go_ref, gproj_ref, branch_ref,
        grad_low_ref, grad_hidden_ref, sems,
    ) = refs[count_in + 7 + count_out :]
    outs_to = hbm_out
    if spots is not None:
        rows = mats.attn_rows + mats.ffn_rows
        outs_to = [
            [
                ref.at[hop2, :, pl.ds(hop1 * rows, rows), :]
                for ref in hbm_out
                for hop2 in range(2)
                for hop1 in range(2)
            ]
        ]
    wide = sizes.width
    attn_copies = start_in(attn_pairs(mats, spots, groups, qkv_ref, out_ref, place_ref), sems, 0)
    ffn_copies = start_in(
        ffn_pairs(mats, spots, groups, up_ref, down_ref, place_ref), sems, len(attn_copies)
    )
    vec[...] = jnp.zeros_like(vec)
    for n in range(seqs):
        base = n * sizes.ext
        z_ref[pl.ds(base, sizes.rows), :] = low_ref[pl.ds(n * sizes.rows, sizes.rows), :]
        z_ref[pl.ds(base + sizes.right_at, RIGHT_ROWS), :] = right_ref[n]
        z_ref[pl.ds(base + sizes.left_at, LEFT_ROWS), :] = left_ref[n, pl.ds(0, LEFT_ROWS), :]
        memory = jnp.concatenate(
            [
                mem_ref[pl.ds(n * sizes.segs, sizes.segs), :],
                left_ref[n, pl.ds(LEFT_ROWS, MEM_ROWS), :].astype(F32)[: sizes.segs],
            ],
            axis=0,
        )
        z_ref[pl.ds(base + sizes.mem_at, MEM_ROWS), :] = memory.astype(BF16)
        grad_low_ref[pl.ds(n * sizes.rows, sizes.rows), :] = out_grad_ref[n]
    fill_mask(sizes, seqs, starts_ref, place_ref, mask_ref)
    wait_all(attn_copies)
    project(sizes, z_ref, qkv_ref, row_bias_ref, proj_ref)
    attend(sizes, seqs, proj_ref, mask_ref, probs_ref, att_ref)
    mixed = (
        inputs_ref[...]
        + nt(att_ref[...], out_ref[...].reshape(-1, wide))
        + biases_ref[3, pl.ds(1, 1), :]
    )
    gain = gains_ref[1, pl.ds(1, 1), :]
    hidden, scaled, inverse = norm_forward(mixed, gain, biases_ref[4, pl.ds(1, 1), :])
    hidden_ref[...] = hidden.astype(BF16)
    for n in range(seqs):
        encoded_ref[n] = mixed[n * sizes.rows : (n + 1) * sizes.rows] + biases_ref[5, pl.ds(1, 1), :]
    grad_hidden_ref[...] = jnp.zeros_like(grad_hidden_ref)
    wait_all(ffn_copies)

    def body(c, carry):
        at_lane = pl.multiple_of(c * wide, wide)
        upward = nt(hidden_ref[...], up_block(up_ref, c, wide))
        upward = upward + ffn_bias_ref[pl.ds(1, 1), pl.ds(at_lane, wide)]
        active, slope = gelu_both(upward)
        active = active.astype(BF16)
        made = nt(active, down_block(down_ref, c, wide))
        for n in range(seqs):
            encoded_ref[n] += made[n * sizes.rows : (n + 1) * sizes.rows]
        grad_hidden_ref[...] += ffn_back_step(
            sizes, c, wide, grad_low_ref[...], hidden_ref[...], active, slope, up_ref, down_ref,
            gup_ref, gdown_ref, vec,
        )
        return carry

    lax.fori_loop(0, sizes.ff // wide, body, 0)
    out_at = len(attn_copies) + len(ffn_copies)
    outs = start_out(
        ffn_pairs(mats, spots, outs_to, gup_ref, gdown_ref, place_ref), sems, out_at
    )
    grad = grad_low_ref[...].astype(F32)
    grad_hidden = grad_hidden_ref[...]
    vec[pl.ds(1, 1), :] = col_sum(grad_hidden * scaled)
    vec[pl.ds(6, 1), :] = col_sum(grad_hidden)
    vec[pl.ds(7, 1), :] = col_sum(grad)
    gz = grad + norm_backward(grad_hidden, scaled, inverse, gain)
    gz_ref[...] = gz
    attn_back_stage(
        sizes, seqs, gz, None, att_ref, proj_ref, probs_ref, z_ref, qkv_ref, out_ref, gqkv_ref,
        gout_ref, go_ref, gproj_ref, branch_ref, vec, gh_ref, gmem_ref, back_left_ref,
        back_right_ref,
    )
    outs = outs + start_out(
        attn_pairs(mats, spots, outs_to, gqkv_ref, gout_ref, place_ref),
        sems,
        out_at + len(outs),
    )
    wait_all(outs)


def first_back_kernel(
    last, sizes, seqs, mats, spots, count_in, count_out, place_ref, inputs_ref, gz_in_ref,
    gh_in_ref, gmem_in_ref, from_right_ref, from_left_ref, mixed_ref, active_ref, slope_ref,
    att_ref, probs_ref, proj_ref, z_ref, frames_ref, left_ref, right_ref, gains_ref, biases_ref,
    last_vec, *refs
):
    groups = in_groups(spots, refs[:count_in])
    gz_ref, gh_ref, gmem_ref, back_left_ref, back_right_ref, upper_vec, vec = refs[
        count_in : count_in + 7
    ]
    refs = refs[count_in + 7 :]
    hbm_out = refs[:count_out]
    (
        qkv_ref, out_ref, up_ref, down_ref, gqkv_ref, gout_ref, gup_ref, gdown_ref, hidden_ref,
        grad_low_ref, grad_ref, grad_hidden_ref, grad_mem_ref, go_ref, gproj_ref, branch_ref,
        small_ref, sems,
    ) = refs[count_out:]
    wide = sizes.width
    small = []
    outs_to = hbm_out
    if spots is not None:
        rows = mats.attn_rows + mats.ffn_rows
        end = CHIPS_Z * rows
        each = [
            ref.at[hop2, hop1] for ref in hbm_out for hop2 in range(2) for hop1 in range(2)
        ]
        small = [ref.at[pl.ds(end, SMALL_ROWS), :] for ref in each]
        outs_to = [[ref.at[pl.ds(0, end), :].reshape(CHIPS_Z, rows, LANES) for ref in each]]
    ffn_copies = start_in(ffn_pairs(mats, spots, groups, up_ref, down_ref, place_ref), sems, 0)
    attn_copies = start_in(
        attn_pairs(mats, spots, groups, qkv_ref, out_ref, place_ref), sems, len(ffn_copies)
    )
    vec[...] = jnp.zeros_like(vec)
    upper_vec[...] = jnp.zeros_like(upper_vec)
    gain = gains_ref[1, pl.ds(0, 1), :]
    gain_sum = jnp.zeros((1, wide), F32)
    bias_sum = jnp.zeros((1, wide), F32)
    for n in range(seqs):
        rows = pl.ds(n * sizes.rows, sizes.rows)
        _, scaled, inverse = norm_forward(
            inputs_ref[rows, :], gain, biases_ref[0, pl.ds(1, 1), :]
        )
        total, mem = merge_halo(last, n, gh_in_ref, gmem_in_ref, from_right_ref, from_left_ref)
        gain_sum = gain_sum + col_sum(total * scaled)
        bias_sum = bias_sum + col_sum(total)
        grad = gz_in_ref[rows, :] + norm_backward(total, scaled, inverse, gain)
        grad_ref[rows, :] = grad
        grad_low_ref[rows, :] = grad.astype(BF16)
        grad_mem_ref[pl.ds(n * sizes.segs, sizes.segs), :] = mem
    upper_vec[pl.ds(0, 1), :] = gain_sum
    upper_vec[pl.ds(2, 1), :] = bias_sum
    gain = gains_ref[0, pl.ds(1, 1), :]
    hidden, scaled, inverse = norm_forward(
        mixed_ref[...], gain, biases_ref[4, pl.ds(0, 1), :]
    )
    hidden_ref[...] = hidden.astype(BF16)
    grad_hidden_ref[...] = jnp.zeros_like(grad_hidden_ref)
    wait_all(ffn_copies)

    def body(c, carry):
        at_lane = pl.multiple_of(c * wide, wide)
        grad_hidden_ref[...] += ffn_back_step(
            sizes, c, wide, grad_low_ref[...], hidden_ref[...],
            active_ref[:, pl.ds(at_lane, wide)], slope_ref[:, pl.ds(at_lane, wide)].astype(F32),
            up_ref, down_ref, gup_ref, gdown_ref, vec,
        )
        return carry

    lax.fori_loop(0, sizes.ff // wide, body, 0)
    out_at = len(ffn_copies) + len(attn_copies)
    outs = start_out(
        ffn_pairs(mats, spots, outs_to, gup_ref, gdown_ref, place_ref), sems, out_at
    )
    grad_hidden = grad_hidden_ref[...]
    grad = grad_ref[...]
    vec[pl.ds(1, 1), :] = col_sum(grad_hidden * scaled)
    vec[pl.ds(6, 1), :] = col_sum(grad_hidden)
    vec[pl.ds(7, 1), :] = col_sum(grad)
    gz = grad + norm_backward(grad_hidden, scaled, inverse, gain)
    gz_ref[...] = gz

    def scaled_rows(n):
        before = left_ref[n, pl.ds(left_ref.shape[1] - LEFT_ROWS, LEFT_ROWS), :]
        parts = (frames_ref[n], right_ref[n], before)
        first_gain = gains_ref[0, pl.ds(0, 1), :]
        first_bias = biases_ref[0, pl.ds(0, 1), :]
        return [norm_forward(part.astype(F32), first_gain, first_bias)[1] for part in parts]

    wait_all(attn_copies)
    attn_back_stage(
        sizes, seqs, gz, grad_mem_ref, att_ref, proj_ref, probs_ref, z_ref, qkv_ref, out_ref,
        gqkv_ref, gout_ref, go_ref, gproj_ref, branch_ref, vec, gh_ref, gmem_ref, back_left_ref,
        back_right_ref, scaled_rows,
    )
    outs = outs + start_out(
        attn_pairs(mats, spots, outs_to, gqkv_ref, gout_ref, place_ref),
        sems,
        out_at + len(outs),
    )
    parts = sizes.width // LANES
    for layer, total in enumerate((vec[...], last_vec[...] + upper_vec[...])):
        for part in range(parts):
            small_ref[pl.ds((layer * parts + part) * TILE, TILE), :] = total[
                :, part * LANES : (part + 1) * LANES
            ].astype(BF16)
    outs = outs + start_out([(ref, small_ref) for ref in small], sems, out_at + len(outs))
    wait_all(outs)


def frames_grad_kernel(
    sizes, seqs, frames_ref, gz_ref, gh_ref, gmem_ref, from_right_ref, from_left_ref, gains_ref,
    biases_ref, grad_ref
):
    gain = gains_ref[0, pl.ds(0, 1), :]
    for n in range(seqs):
        _, scaled, inverse = norm_forward(
            frames_ref[n].astype(F32), gain, biases_ref[0, pl.ds(0, 1), :]
        )
        total, mem = merge_halo(sizes, n, gh_ref, gmem_ref, from_right_ref, from_left_ref)
        grad_ref[n] = (
            gz_ref[pl.ds(n * sizes.rows, sizes.rows), :]
            + norm_backward(total, scaled, inverse, gain)
            + segment_spread(sizes.rows, sizes.width, mem * (1.0 / SEG_LEN))
        )


def shifted(value, axis, by):
    size = lax.axis_size(axis)
    return lax.ppermute(value, axis, [(i, (i + by) % size) for i in range(size)])


def permuted(value, move):
    reps = lax.axis_size("rep")
    pairs = []
    for flat in range(lax.axis_size("seg") * reps):
        seg, rep = divmod(flat, reps)
        z, y, x, core = move(seg // CHIPS_Y, seg % CHIPS_Y, rep // 2, rep % 2)
        pairs.append((flat, (z * CHIPS_Y + y) * reps + 2 * x + core))
    return lax.ppermute(value, ("seg", "rep"), pairs)


def across_first(value):
    return permuted(value, lambda z, y, x, c: (z, y, x ^ 1, c) if c == 0 else (z, y ^ 1, x, c))


def across_second(value):
    return permuted(value, lambda z, y, x, c: (z, y ^ 1, x, c) if c == 0 else (z, y, x ^ 1, c))


def other_core(value):
    return permuted(value, lambda z, y, x, c: (z, y, x, c ^ 1))


def after(value, *others):
    return lax.optimization_barrier((value,) + others)[0]


def swap_z(blocks):
    groups = [
        [z * CHIPS_Y + y for z in range(CHIPS_Z)] for y in range(CHIPS_Y)
    ]
    return lax.all_to_all(blocks, "seg", 0, 0, axis_index_groups=groups, tiled=True)


def gather_sides(here):
    return [here, across_first(here), across_second(here)]


def both_cores(blocks):
    return blocks + [other_core(block) for block in blocks]


def summed(*parts):
    total = parts[0].astype(F32)
    for part in parts[1:]:
        total = total + part.astype(F32)
    return total.astype(BF16)


def sum_everywhere(value):
    count = lax.axis_size("seg") * lax.axis_size("rep")
    bit = 1
    while bit < count:
        value = value + lax.ppermute(value, ("seg", "rep"), [(i, i ^ bit) for i in range(count)])
        bit *= 2
    return value


def vmem_spec():
    return pl.BlockSpec(memory_space=pltpu.VMEM)


def smem_spec():
    return pl.BlockSpec(memory_space=pltpu.SMEM)


def hbm_spec():
    return pl.BlockSpec(memory_space=pl.ANY)


def call(body, in_specs, out_shapes, out_specs, scratch, args, flops=0, moved=0, grid=(), aliases={}, vmem=12):
    return pl.pallas_call(
        body,
        grid=grid,
        input_output_aliases=aliases,
        in_specs=in_specs,
        out_shape=tuple(jax.ShapeDtypeStruct(shape, kind) for shape, kind in out_shapes),
        out_specs=tuple(out_specs),
        scratch_shapes=scratch,
        compiler_params=pltpu.CompilerParams(vmem_limit_bytes=vmem * MIB),
        cost_estimate=pl.CostEstimate(flops=flops, bytes_accessed=moved, transcendentals=0),
    )(*args)


def on_device(
    frames,
    utt_segments,
    out_grad,
    qkv_weight,
    out_weight,
    ffn_in_weight,
    ffn_out_weight,
    norm_gains,
    biases,
    ffn_bias,
):
    micros, groups, rows, width = frames.shape
    seqs = micros * groups
    ff = ffn_bias.shape[1]
    reps = lax.axis_size("rep")
    seg_count = lax.axis_size("seg")
    mats = Matrices(width, ff)
    by_blocks = width // reps == LANES and reps == 4 and seg_count == BLOCKS
    first = Sizes(rows, width, ff, True)
    last = Sizes(rows, width, ff, False)
    own = seqs * rows
    mem_own = seqs * first.segs

    seg_at = lax.axis_index("seg")
    seg_base = seg_at * first.segs
    rep_at = lax.axis_index("rep")
    place = [seg_base, jnp.int32(first.segs * seg_count)]
    y_at, x_at, core_at = seg_at % CHIPS_Y, rep_at // 2, rep_at % 2
    for other in range(2):
        core = lax.bitwise_xor(core_at, other)
        for hop2 in range(2):
            for hop1 in range(2):
                x_hop = jnp.where(core == 0, hop1, hop2)
                y_hop = jnp.where(core == 0, hop2, hop1)
                place.append(lax.bitwise_xor(y_at, y_hop))
                place.append((lax.bitwise_xor(x_at, x_hop) * 2 + core) * LANES)
    place = jnp.stack([jnp.asarray(entry, jnp.int32) for entry in place])
    lengths = utt_segments.reshape(seqs, utt_segments.shape[2])
    starts = (jnp.cumsum(lengths, axis=1) - lengths).astype(jnp.int32)
    zero_bias = jnp.zeros((1, width), F32)
    row_biases = [
        jnp.concatenate([biases[l : l + 1, 1], zero_bias, biases[l : l + 1, 2]], axis=1)
        for l in range(LAYERS)
    ]
    biases_by_row = jnp.swapaxes(biases, 0, 1)

    frames_own = frames.reshape(seqs, rows, width)
    grads_own = out_grad.reshape(seqs, rows, width)
    far = MEM_LEN * SEG_LEN
    frames_left = shifted(frames_own[:, rows - far :], "seg", 1)
    frames_right = shifted(frames_own[:, :RIGHT_ROWS], "seg", -1)

    attn_rows, ffn_rows = mats.attn_rows, mats.ffn_rows
    if by_blocks:
        qkv_t, out_t, down_t = (
            jnp.swapaxes(member, 1, 2) for member in (qkv_weight, out_weight, ffn_out_weight)
        )
        all_rows = attn_rows + ffn_rows
        spots = Spots(mats)
        shards = call(
            lambda *refs: pack_kernel(spots, *refs),
            [vmem_spec()] * 4,
            [((CHIPS_Z, all_rows, LANES), BF16)] * LAYERS,
            [vmem_spec()] * LAYERS,
            [],
            (qkv_t, out_t, ffn_in_weight, down_t),
            vmem=56,
        )
        sides0 = gather_sides(after(swap_z(shards[0]), frames_left, frames_right))
        place, starts, row_biases, sent = lax.optimization_barrier(
            (place, starts, row_biases, after(shards[1], sides0[0]))
        )
        sides1 = gather_sides(swap_z(sent))
        first_all = both_cores(sides0 + [across_second(after(sides0[1], sides1[0]))])
        classes = len(first_all) // 2
        grad_outs0 = [((2, 2, CHIPS_Z * all_rows + SMALL_ROWS, LANES), BF16)] * 2
        grad_outs1 = [((2, CHIPS_Z, 2 * all_rows, LANES), BF16)] * 2
        copies_in = len(first_all) * (3 + mats.down_parts)
    else:
        whole = []
        for member, shape in zip(
            (qkv_weight, out_weight, ffn_in_weight, ffn_out_weight),
            (mats.qkv, mats.out, mats.up, mats.down),
        ):
            member = lax.all_gather(member, "rep", axis=1, tiled=True)
            member = lax.all_gather(member, "seg", axis=2, tiled=True)
            whole.append(jnp.swapaxes(member, 1, 2).reshape((LAYERS,) + shape))
        first_all = [member[0] for member in whole]
        last_all = [member[1] for member in whole]
        spots = None
        grad_outs0 = grad_outs1 = [
            (shape, BF16) for shape in (mats.qkv, mats.out, mats.up, mats.down)
        ]
        copies_in = 4
    dma = pltpu.SemaphoreType.DMA

    matrices = [pltpu.VMEM(shape, BF16) for shape in (mats.qkv, mats.out, mats.up, mats.down)]

    (
        z0, proj0, probs0, att0, mixed0, mem1, x1, active0, slope0, low1, send_right, send_left,
    ) = call(
        lambda *refs: first_layer_kernel(
            first, seqs, mats, spots, len(first_all), *refs
        ),
        [smem_spec()] * 2 + [vmem_spec()] * 7 + [hbm_spec()] * len(first_all),
        [
            ((seqs * first.ext, width), BF16),
            ((seqs * first.ext, 3 * width), BF16),
            ((seqs * first.pairs, first.keys, 2 * first.queries), BF16),
            ((seqs * first.queries, width), BF16),
            ((own, width), F32),
            ((mem_own, width), F32),
            ((own, width), F32),
            ((own, ff), BF16),
            ((own, ff), BF16),
            ((own, width), BF16),
            ((seqs, BACK_ROWS, width), BF16),
            ((seqs, RIGHT_ROWS, width), BF16),
        ],
        [vmem_spec()] * 12,
        matrices
        + [
            pltpu.VMEM((seqs, first.keys, 2 * first.queries), F32),
            pltpu.VMEM((own, width), BF16),
            dma((copies_in,)),
        ],
        (place, starts, frames_own, frames_left, frames_right, norm_gains, biases_by_row, ffn_bias,
         row_biases[0]) + tuple(first_all),
        flops=24 * own * (4 * width * width + 2 * width * ff) // 2,
        moved=2 * (4 * width * width + 2 * width * ff),
        vmem=24,
    )
    left1 = shifted(send_right, "seg", 1)
    right1 = shifted(send_left, "seg", -1)
    if by_blocks:
        last_side = across_second(after(sides1[1], sides1[2], left1, right1))
        last_all = both_cores(sides1 + [last_side])

    vec_shape = (TILE, width)
    outs = call(
        lambda *refs: last_layer_kernel(
            last, seqs, mats, spots, len(last_all), len(grad_outs1), *refs
        ),
        [smem_spec()] * 2 + [vmem_spec()] * 10 + [hbm_spec()] * len(last_all),
        [
            ((seqs, rows, width), F32),
            ((own, width), F32),
            ((own, width), F32),
            ((mem_own, width), F32),
            ((seqs, BACK_ROWS, width), BF16),
            ((seqs, RIGHT_ROWS, width), BF16),
            (vec_shape, F32),
        ]
        + grad_outs1,
        [vmem_spec()] * 7 + [hbm_spec()] * len(grad_outs1),
        matrices
        + matrices
        + [
            pltpu.VMEM((seqs, last.keys, 2 * last.queries), F32),
            pltpu.VMEM((seqs * last.ext, width), BF16),
            pltpu.VMEM((seqs * last.ext, 3 * width), BF16),
            pltpu.VMEM((seqs * last.pairs, last.keys, 2 * last.queries), BF16),
            pltpu.VMEM((seqs * last.queries, width), BF16),
            pltpu.VMEM((own, width), BF16),
            pltpu.VMEM((seqs * last.queries, width), BF16),
            pltpu.VMEM((seqs * last.ext, 3 * width), BF16),
            pltpu.VMEM((seqs * last.queries, width), BF16),
            pltpu.VMEM((own, width), BF16),
            pltpu.VMEM((own, width), F32),
            dma((2 * copies_in,)),
        ],
        (place, starts, low1, left1, right1, mem1, x1, grads_own, norm_gains, biases_by_row, ffn_bias,
         row_biases[1]) + tuple(last_all),
        flops=30 * own * (4 * width * width + 2 * width * ff),
        moved=4 * (4 * width * width + 2 * width * ff),
        vmem=34,
    )
    encoded, gz1, gh1, gmem1, back_left1, back_right1, vec1 = outs[:7]
    grad_blocks1 = outs[7:]
    from_right1 = shifted(back_left1, "seg", -1)
    from_left1 = shifted(back_right1, "seg", 1)

    gh1_tied = gh1
    if by_blocks:
        mine1, theirs1 = grad_blocks1[0], other_core(grad_blocks1[1])
        far1 = summed(mine1[1], theirs1[1])
        gh1_tied = after(gh1, far1)
    gz0, gh0, gmem0, back_left0, back_right0, upper_vec, vec0, *grad_blocks0 = call(
        lambda *refs: first_back_kernel(
            last, first, seqs, mats, spots, len(first_all), len(grad_outs0), *refs
        ),
        [smem_spec()] + [vmem_spec()] * 19 + [hbm_spec()] * len(first_all),
        [
            ((own, width), F32),
            ((own, width), F32),
            ((mem_own, width), F32),
            ((seqs, BACK_ROWS, width), BF16),
            ((seqs, RIGHT_ROWS, width), BF16),
            (vec_shape, F32),
            (vec_shape, F32),
        ]
        + grad_outs0,
        [vmem_spec()] * 7 + [hbm_spec()] * len(grad_outs0),
        matrices
        + matrices
        + [
            pltpu.VMEM((own, width), BF16),
            pltpu.VMEM((own, width), BF16),
            pltpu.VMEM((own, width), F32),
            pltpu.VMEM((own, width), F32),
            pltpu.VMEM((mem_own, width), F32),
            pltpu.VMEM((seqs * first.queries, width), BF16),
            pltpu.VMEM((seqs * first.ext, 3 * width), BF16),
            pltpu.VMEM((seqs * first.queries, width), BF16),
            pltpu.VMEM((SMALL_ROWS, LANES), BF16),
            dma((2 * copies_in + 8,)),
        ],
        (place, x1, gz1, gh1_tied, gmem1, from_right1, from_left1, mixed0, active0, slope0, att0,
         probs0, proj0, z0, frames_own, frames_left, frames_right, norm_gains, biases_by_row, vec1)
        + tuple(first_all),
        flops=28 * own * (4 * width * width + 2 * width * ff),
        moved=4 * (4 * width * width + 2 * width * ff),
        vmem=34,
    )
    from_right0 = shifted(back_left0, "seg", -1)
    from_left0 = shifted(back_right0, "seg", 1)
    gz0_last = gz0
    if by_blocks:
        second1 = across_second(far1)
        mine0, theirs0 = grad_blocks0[0], other_core(after(grad_blocks0[1], second1))
        both1 = summed(mine1[0], theirs1[0], second1)
        lines1 = swap_z(both1)
        far0 = summed(mine0[1], after(theirs0, both1, from_right0, from_left0)[1])
        second0 = across_second(far0)
        mid0 = summed(mine0[0, 1], theirs0[0, 1], second0[1])
        first0 = across_first(mid0)
        held0 = summed(mine0[0, 0], theirs0[0, 0], after(second0, mid0)[0])
        near0 = summed(held0, first0)
        blocks = CHIPS_Z * all_rows
        near0 = jnp.concatenate(
            [
                near0[:blocks].reshape(CHIPS_Z, all_rows, LANES),
                jnp.broadcast_to(near0[None, blocks:], (CHIPS_Z, SMALL_ROWS, LANES)),
            ],
            axis=1,
        )
        first_parts = swap_z(near0)
        gz0_last, lines1 = lax.optimization_barrier((after(gz0, near0), lines1))
        cross1 = jnp.sum(lines1[:, all_rows:].astype(F32), axis=0, keepdims=True).astype(BF16)
        first1 = across_first(cross1)
    frames_grad = call(
        lambda *refs: frames_grad_kernel(first, seqs, *refs),
        [vmem_spec()] * 8,
        [((seqs, rows, width), F32)],
        [vmem_spec()],
        [],
        (frames_own, gz0_last, gh0, gmem0, from_right0, from_left0, norm_gains, biases_by_row),
    )[0]

    if by_blocks:
        shapes = [member.shape for member in (qkv_t, out_t, ffn_in_weight, down_t)]
        held = [pltpu.VMEM(shape[1:], F32) for shape in shapes]
        whole = [(shape, F32) for shape in shapes]
        written = call(
            lambda *refs: unpack_last_kernel(spots, LAYERS - 1, *refs),
            [
                pl.BlockSpec((CHIPS_Z, all_rows, LANES), lambda i: (0, 0, 0)),
                pl.BlockSpec((1, all_rows, LANES), lambda i: (0, 0, 0)),
            ],
            whole,
            [hbm_spec()] * 4,
            held + [dma((4,))],
            [lines1, first1],
            grid=(1,),
        )
        small_shapes = [norm_gains.shape, (biases.shape[1], LAYERS, width), ffn_bias.shape]
        reduced = call(
            lambda *refs: unpack_first_kernel(spots, all_rows, *refs),
            [vmem_spec()] + [hbm_spec()] * 4,
            whole + [(shape, F32) for shape in small_shapes],
            [hbm_spec()] * 4 + [vmem_spec()] * 3,
            held + [dma((4,))],
            [after(first_parts, frames_grad)] + list(written),
            aliases={1 + i: i for i in range(4)},
        )
        small = reduced[4], jnp.swapaxes(reduced[5], 0, 1), reduced[6]
        reduced = [
            jnp.swapaxes(reduced[0], 1, 2),
            jnp.swapaxes(reduced[1], 1, 2),
            reduced[2],
            jnp.swapaxes(reduced[3], 1, 2),
        ]
    else:
        reduced = []
        for member0, member1 in zip(grad_blocks0, grad_blocks1):
            both = jnp.stack([member0, member1]).reshape(LAYERS, -1, member0.shape[3])
            both = jnp.swapaxes(both, 1, 2)
            both = lax.psum_scatter(both, "seg", scatter_dimension=2, tiled=True)
            both = lax.psum_scatter(both, "rep", scatter_dimension=1, tiled=True)
            reduced.append(both.astype(F32))
        small = sum_everywhere(jnp.stack([vec0, vec1 + upper_vec]))
        small = small[:, 0:2], small[:, 2:8], small[:, 8:12].reshape(ffn_bias.shape)

    return (
        encoded.reshape(frames.shape),
        frames_grad.reshape(frames.shape),
        reduced[0],
        reduced[1],
        reduced[2],
        reduced[3],
        small[0],
        small[1],
        small[2],
    )


def solution(mesh):
    in_specs = (
        P(None, "rep", "seg", None),
        P(None, "rep", None),
        P(None, "rep", "seg", None),
        P(None, "rep", "seg"),
        P(None, "rep", "seg"),
        P(None, "rep", "seg"),
        P(None, "rep", "seg"),
        P(),
        P(),
        P(),
    )
    out_specs = (
        P(None, "rep", "seg", None),
        P(None, "rep", "seg", None),
        P(None, "rep", "seg"),
        P(None, "rep", "seg"),
        P(None, "rep", "seg"),
        P(None, "rep", "seg"),
        P(),
        P(),
        P(),
    )
    return jax.shard_map(
        on_device, mesh=mesh, in_specs=in_specs, out_specs=out_specs, check_vma=False
    )
```

```python
import jax
import jax.numpy as jnp
from jax import lax
from jax.experimental import pallas as pl
from jax.experimental.pallas import tpu as pltpu
from jax.sharding import PartitionSpec as P

HEADS = 8
SEG_LEN = 16
LEFT_LEN = 30
RIGHT_LEN = 4
MEM_LEN = 4
LAYERS = 2

EPS = 1e-05
ROOT_HALF = 0.7071067811865476
INV_ROOT_TWO_PI = 0.3989422804014327

LANES = 128
TILE = 16
RIGHT_ROWS = 16
LEFT_ROWS = 32
MEM_ROWS = 16
BACK_ROWS = LEFT_ROWS + MEM_ROWS
CHIPS_Z = 4
CHIPS_Y = 2
BLOCKS = CHIPS_Z * CHIPS_Y
VEC_ROWS = 12
SMALL_ROWS = 96
MIB = 1024 * 1024

BF16 = jnp.bfloat16
F32 = jnp.float32


def nn(a, b):
    return lax.dot_general(a, b, (((1,), (0,)), ((), ())), preferred_element_type=F32)


def nt(a, b):
    return lax.dot_general(a, b, (((1,), (1,)), ((), ())), preferred_element_type=F32)


def tn(a, b):
    return lax.dot_general(a, b, (((0,), (0,)), ((), ())), preferred_element_type=F32)


def col_sum(value):
    return jnp.sum(value, axis=0, keepdims=True)


def norm_forward(inputs, gain, bias):
    center = inputs - jnp.mean(inputs, axis=1, keepdims=True)
    inverse = lax.rsqrt(jnp.mean(center * center, axis=1, keepdims=True) + EPS)
    scaled = center * inverse
    return scaled * gain + bias, scaled, inverse


def norm_backward(grad_in, scaled, inverse, gain):
    grad_scaled = grad_in * gain
    return inverse * (
        grad_scaled
        - jnp.mean(grad_scaled, axis=1, keepdims=True)
        - scaled * jnp.mean(grad_scaled * scaled, axis=1, keepdims=True)
    )


def segment_mean(inputs):
    rows, width = inputs.shape
    return jnp.mean(inputs.reshape(rows // SEG_LEN, SEG_LEN, width), axis=1)


def segment_spread(rows, width, per_segment):
    segs = rows // SEG_LEN
    return jnp.broadcast_to(per_segment[:, None, :], (segs, SEG_LEN, width)).reshape(rows, width)


def identity(size):
    row = lax.broadcasted_iota(jnp.int32, (size, size), 0)
    col = lax.broadcasted_iota(jnp.int32, (size, size), 1)
    return (row == col).astype(F32).astype(BF16)


class Sizes:
    def __init__(self, rows, width, ff, with_summary):
        self.rows = rows
        self.width = width
        self.ff = ff
        self.segs = rows // SEG_LEN
        self.top = TILE if with_summary else 0
        self.keys = rows + RIGHT_ROWS + LEFT_ROWS + MEM_ROWS
        self.ext = self.top + self.keys
        self.queries = self.top + rows
        self.right_at = self.top + rows
        self.left_at = self.right_at + RIGHT_ROWS
        self.mem_at = self.left_at + LEFT_ROWS
        self.pairs = width // LANES


class Matrices:
    def __init__(self, width, ff):
        self.qkv = (CHIPS_Z, CHIPS_Y, 3 * width // BLOCKS, width)
        self.out = (CHIPS_Z, CHIPS_Y, width // BLOCKS, width)
        self.up = (CHIPS_Z, CHIPS_Y, ff // BLOCKS, width)
        self.down = (CHIPS_Z, CHIPS_Y, width // BLOCKS, ff)
        self.down_parts = ff // width
        self.attn_rows = self.qkv[2] + self.out[2]
        self.ffn_rows = self.up[2] + self.down_parts * self.down[2]


class Spots:
    def __init__(self, mats):
        high, wide, up, low = mats.qkv[2], mats.out[2], mats.up[2], mats.down[2]
        self.qkv = (0, 0)
        self.out = (0, high)
        self.up = (0, high + wide)
        self.down = [(0, high + wide + up + low * part) for part in range(mats.down_parts)]


def attn_pairs(mats, spots, groups, qkv_ref, out_ref, place_ref):
    if spots is None:
        return [(groups[0], qkv_ref), (groups[1], out_ref)]
    pairs = []
    for k in range(len(groups[0])):
        row = place_ref[2 + 2 * k]
        lane = pl.multiple_of(place_ref[3 + 2 * k], LANES)
        for (group, first), ref, shape in (
            (spots.qkv, qkv_ref, mats.qkv),
            (spots.out, out_ref, mats.out),
        ):
            block = groups[group][k]
            pairs.append(
                (
                    block.at[:, pl.ds(first, shape[2]), :],
                    ref.at[:, row, :, pl.ds(lane, LANES)],
                )
            )
    return pairs


def ffn_pairs(mats, spots, groups, up_ref, down_ref, place_ref):
    if spots is None:
        return [(groups[2], up_ref), (groups[3], down_ref)]
    pairs = []
    for k in range(len(groups[0])):
        row = place_ref[2 + 2 * k]
        lane = pl.multiple_of(place_ref[3 + 2 * k], LANES)
        group, first = spots.up
        block = groups[group][k]
        pairs.append(
            (block.at[:, pl.ds(first, mats.up[2]), :], up_ref.at[:, row, :, pl.ds(lane, LANES)])
        )
        for part, (group, first) in enumerate(spots.down):
            there = pl.multiple_of(
                place_ref[3 + 2 * k] * mats.down_parts + part * LANES, LANES
            )
            block = groups[group][k]
            pairs.append(
                (
                    block.at[:, pl.ds(first, mats.down[2]), :],
                    down_ref.at[:, row, :, pl.ds(there, LANES)],
                )
            )
    return pairs


def start_in(pairs, sems, at):
    copies = [pltpu.make_async_copy(s, d, sems.at[at + i]) for i, (s, d) in enumerate(pairs)]
    for copy in copies:
        copy.start()
    return copies


def start_out(pairs, sems, at):
    copies = [pltpu.make_async_copy(d, s, sems.at[at + i]) for i, (s, d) in enumerate(pairs)]
    for copy in copies:
        copy.start()
    return copies


def in_groups(spots, refs):
    return refs if spots is None else [refs]


def wait_all(copies):
    for copy in copies:
        copy.wait()


def fill_mask(sizes, seqs, starts_ref, place_ref, mask_ref):
    shape = (sizes.keys, 2 * sizes.queries)
    key = lax.broadcasted_iota(jnp.int32, shape, 0)
    col = lax.broadcasted_iota(jnp.int32, shape, 1)
    col = jnp.where(col < sizes.queries, col, col - sizes.queries)
    base = place_ref[0]
    total = place_ref[1]
    query = jnp.where(col < sizes.top, col, lax.shift_right_arithmetic(col - sizes.top, 4))
    left_at = sizes.rows + RIGHT_ROWS
    mem_at = left_at + LEFT_ROWS
    spot = jnp.where(key < left_at, key, key - mem_at)
    mem_seg = jnp.where(key < mem_at + sizes.segs, key - mem_at, key - mem_at - 2 * sizes.segs)
    key_seg = jnp.where(key < mem_at, lax.shift_right_arithmetic(spot, 4), mem_seg)
    near = (
        (key_seg == query)
        | ((spot >= query * SEG_LEN - LEFT_LEN) & (spot < query * SEG_LEN))
        | ((key_seg == query + 1) & (spot < query * SEG_LEN + SEG_LEN + RIGHT_LEN))
    )
    recent = (key_seg >= query - MEM_LEN) & (key_seg < query) & (col >= sizes.top)
    allowed = ((key < mem_at) & near) | ((key >= mem_at) & recent)
    key_abs = key_seg + base
    query_abs = query + base
    allowed = allowed & (key_abs >= 0) & (key_abs < total)
    if sizes.top:
        allowed = allowed & ((col < sizes.segs) | (col >= sizes.top))
    for n in range(seqs):
        key_owner = jnp.zeros(shape, jnp.int32)
        query_owner = jnp.zeros(shape, jnp.int32)
        for u in range(starts_ref.shape[1]):
            first = starts_ref[n, u]
            key_owner = key_owner + (key_abs >= first).astype(jnp.int32)
            query_owner = query_owner + (query_abs >= first).astype(jnp.int32)
        mask_ref[n] = jnp.where(allowed & (key_owner == query_owner), 0.0, -1e30)


def half_masks():
    lane = lax.broadcasted_iota(jnp.int32, (1, LANES), 1)
    even = (lane < LANES // 2).astype(F32)
    return even.astype(BF16), (1.0 - even).astype(BF16), lane < LANES // 2


def project(sizes, z_ref, qkv_ref, row_bias_ref, proj_ref):
    step = CHIPS_Z // 2
    for c in range(2):
        block = qkv_ref[pl.ds(c * step, step)].reshape(-1, sizes.width)
        wide = block.shape[0]
        made = nt(z_ref[...], block) + row_bias_ref[:, pl.ds(c * wide, wide)]
        proj_ref[:, pl.ds(c * wide, wide)] = made.astype(BF16)


def attend(sizes, seqs, proj_ref, mask_ref, probs_ref, att_ref):
    even, odd, is_even = half_masks()
    scale = (sizes.width // HEADS) ** (-0.5)
    count = sizes.queries

    def body(p, carry):
        for n in range(seqs):
            lane = pl.multiple_of(p * LANES, LANES)
            query = proj_ref[pl.ds(n * sizes.ext, count), pl.ds(lane, LANES)]
            first = n * sizes.ext + sizes.top
            key = proj_ref[pl.ds(first, sizes.keys), pl.ds(sizes.width + lane, LANES)]
            value = proj_ref[pl.ds(first, sizes.keys), pl.ds(2 * sizes.width + lane, LANES)]
            queries = jnp.concatenate([query * even, query * odd], axis=0)
            scores = nt(key, queries) * scale + mask_ref[n]
            scores = jnp.exp(scores - jnp.max(scores, axis=0, keepdims=True))
            probs = (scores * (1.0 / jnp.sum(scores, axis=0, keepdims=True))).astype(BF16)
            probs_ref[n * sizes.pairs + p] = probs
            out = tn(probs, value)
            att_ref[pl.ds(n * count, count), pl.ds(lane, LANES)] = jnp.where(
                is_even, out[:count], out[count:]
            ).astype(BF16)
        return carry

    lax.fori_loop(0, sizes.pairs, body, 0, unroll=True)


def attend_back(sizes, seqs, proj_ref, probs_ref, go_ref, gproj_ref):
    even, odd, is_even = half_masks()
    scale = (sizes.width // HEADS) ** (-0.5)
    count = sizes.queries
    wide = sizes.width
    for n in range(seqs):
        base = n * sizes.ext
        rest = sizes.ext - count
        gproj_ref[pl.ds(base + count, rest), pl.ds(0, wide)] = jnp.zeros((rest, wide), BF16)
        if sizes.top:
            gproj_ref[pl.ds(base, sizes.top), pl.ds(wide, 2 * wide)] = jnp.zeros(
                (sizes.top, 2 * wide), BF16
            )

    def body(p, carry):
        for n in range(seqs):
            lane = pl.multiple_of(p * LANES, LANES)
            base = n * sizes.ext
            first = base + sizes.top
            query = proj_ref[pl.ds(base, count), pl.ds(lane, LANES)]
            key = proj_ref[pl.ds(first, sizes.keys), pl.ds(wide + lane, LANES)]
            value = proj_ref[pl.ds(first, sizes.keys), pl.ds(2 * wide + lane, LANES)]
            grad = go_ref[pl.ds(n * count, count), pl.ds(lane, LANES)]
            queries = jnp.concatenate([query * even, query * odd], axis=0)
            grads = jnp.concatenate([grad * even, grad * odd], axis=0)
            probs_low = probs_ref[n * sizes.pairs + p]
            grad_values = nn(probs_low, grads)
            probs = probs_low.astype(F32)
            weighted = nt(value, grads) * probs
            grad_scores = (
                (weighted - probs * jnp.sum(weighted, axis=0, keepdims=True)) * scale
            ).astype(BF16)
            grad_keys = nn(grad_scores, queries)
            grad_both = tn(grad_scores, key)
            grad_query = jnp.where(is_even, grad_both[:count], grad_both[count:])
            gproj_ref[pl.ds(base, count), pl.ds(lane, LANES)] = grad_query.astype(BF16)
            gproj_ref[pl.ds(first, sizes.keys), pl.ds(wide + lane, LANES)] = grad_keys.astype(BF16)
            gproj_ref[pl.ds(first, sizes.keys), pl.ds(2 * wide + lane, LANES)] = (
                grad_values.astype(BF16)
            )
        return carry

    lax.fori_loop(0, sizes.pairs, body, 0)


def gelu_both(upward):
    half = 0.5 * (1.0 + lax.erf(upward * ROOT_HALF))
    slope = half + upward * jnp.exp(-0.5 * upward * upward) * INV_ROOT_TWO_PI
    return upward * half, slope


def up_block(up_ref, c, wide):
    step = wide // (up_ref.shape[1] * up_ref.shape[2])
    return up_ref[pl.ds(c * step, step)].reshape(-1, up_ref.shape[3])


def down_block(down_ref, c, wide):
    at = pl.multiple_of(c * wide, wide)
    return down_ref[:, :, :, pl.ds(at, wide)].reshape(-1, wide)


def ffn_back_step(
    sizes, c, wide, grad_low, hidden_low, active, slope, up_ref, down_ref, gup_ref, gdown_ref, vec
):
    at = pl.multiple_of(c * wide, wide)
    up = up_block(up_ref, c, wide)
    down = down_block(down_ref, c, wide)
    grad_active = nn(grad_low, down)
    grad_up_f = grad_active * slope
    grad_up = grad_up_f.astype(BF16)
    gdown_ref[:, :, :, pl.ds(at, wide)] = (
        tn(grad_low, active).astype(BF16).reshape(gdown_ref.shape[:3] + (wide,))
    )
    step = wide // (gup_ref.shape[1] * gup_ref.shape[2])
    gup_ref[pl.ds(c * step, step)] = (
        tn(grad_up, hidden_low).astype(BF16).reshape((step,) + gup_ref.shape[1:])
    )
    vec[pl.ds(8 + c, 1), :] = col_sum(grad_up.astype(F32))
    return nn(grad_up, up)


def attn_back_stage(
    sizes, seqs, gz, grad_mem_ref, att_ref, proj_ref, probs_ref, z_ref, qkv_ref, out_ref,
    gqkv_ref, gout_ref, go_ref, gproj_ref, branch_ref, vec, gh_ref, gmem_ref, back_left_ref,
    back_right_ref, scaled_rows=None,
):
    wide = sizes.width
    count = sizes.queries
    bias_out = col_sum(gz)
    for n in range(seqs):
        if sizes.top:
            mem_grad = grad_mem_ref[pl.ds(n * sizes.segs, sizes.segs), :]
            bias_out = bias_out + col_sum(mem_grad)
            branch_ref[pl.ds(n * count, sizes.top), :] = jnp.concatenate(
                [mem_grad, jnp.zeros((sizes.top - sizes.segs, wide), F32)], axis=0
            ).astype(BF16)
        branch_ref[pl.ds(n * count + sizes.top, sizes.rows), :] = gz[
            n * sizes.rows : (n + 1) * sizes.rows
        ].astype(BF16)
    vec[pl.ds(5, 1), :] = bias_out
    branch = branch_ref[...]
    gout_ref[...] = tn(branch, att_ref[...]).astype(BF16).reshape(gout_ref.shape)
    go_ref[...] = nn(branch, out_ref[...].reshape(-1, wide)).astype(BF16)
    attend_back(sizes, seqs, proj_ref, probs_ref, go_ref, gproj_ref)
    vec[pl.ds(3, 1), :] = col_sum(gproj_ref[:, pl.ds(0, wide)].astype(F32))
    vec[pl.ds(4, 1), :] = col_sum(gproj_ref[:, pl.ds(2 * wide, wide)].astype(F32))
    grad_ext = nn(gproj_ref[...], qkv_ref[...].reshape(-1, wide))
    gain_sum = jnp.zeros((1, wide), F32)
    bias_sum = jnp.zeros((1, wide), F32)
    for n in range(seqs):
        base = n * sizes.ext
        own = grad_ext[base + sizes.top : base + sizes.top + sizes.rows]
        if sizes.top:
            spread = grad_ext[base : base + sizes.segs] * (1.0 / SEG_LEN)
            own = own + segment_spread(sizes.rows, wide, spread)
        gh_ref[pl.ds(n * sizes.rows, sizes.rows), :] = own
        mem = base + sizes.mem_at
        gmem_ref[pl.ds(n * sizes.segs, sizes.segs), :] = grad_ext[mem : mem + sizes.segs]
        left = base + sizes.left_at
        back_left_ref[n] = grad_ext[left : left + BACK_ROWS].astype(BF16)
        right = base + sizes.right_at
        back_right_ref[n] = grad_ext[right : right + RIGHT_ROWS].astype(BF16)
        if scaled_rows is not None:
            grads = (
                own,
                grad_ext[right : right + RIGHT_ROWS],
                grad_ext[left : left + LEFT_ROWS],
            )
            for rows, scaled in zip(grads, scaled_rows(n)):
                gain_sum = gain_sum + col_sum(rows * scaled)
                bias_sum = bias_sum + col_sum(rows)
    if scaled_rows is not None:
        vec[pl.ds(0, 1), :] = gain_sum
        vec[pl.ds(2, 1), :] = bias_sum
    step = CHIPS_Z // 2
    part = gqkv_ref.shape[1] * gqkv_ref.shape[2] * step
    for c in range(2):
        gqkv_ref[pl.ds(c * step, step)] = (
            tn(gproj_ref[:, pl.ds(c * part, part)], z_ref[...])
            .astype(BF16)
            .reshape((step,) + gqkv_ref.shape[1:])
        )


def merge_halo(sizes, n, gh_ref, gmem_ref, from_right_ref, from_left_ref):
    first = n * sizes.rows
    back = from_right_ref[n].astype(F32)
    head = gh_ref[pl.ds(first, RIGHT_ROWS), :] + from_left_ref[n].astype(F32)
    middle = gh_ref[pl.ds(first + RIGHT_ROWS, sizes.rows - RIGHT_ROWS - LEFT_ROWS), :]
    tail = gh_ref[pl.ds(first + sizes.rows - LEFT_ROWS, LEFT_ROWS), :] + back[:LEFT_ROWS]
    mem = gmem_ref[pl.ds(n * sizes.segs, sizes.segs), :] + back[LEFT_ROWS + sizes.segs :]
    return jnp.concatenate([head, middle, tail], axis=0), mem


def pack_kernel(spots, qkv_ref, out_ref, up_ref, down_ref, *packed):
    eye = identity(LANES)
    high, wide, low = qkv_ref.shape[1], out_ref.shape[1], down_ref.shape[1]
    for layer, ref in enumerate(packed):
        up = tn(up_ref[layer], eye).astype(BF16)
        for z in range(ref.shape[0]):
            ref[z, pl.ds(spots.qkv[1], high), :] = qkv_ref[layer]
            ref[z, pl.ds(spots.out[1], wide), :] = out_ref[layer]
            ref[z, pl.ds(spots.up[1], up_ref.shape[2]), :] = up
            for part, (_, first) in enumerate(spots.down):
                ref[z, pl.ds(first, low), :] = down_ref[layer, :, pl.ds(part * LANES, LANES)]


def unpack_layer(spots, sources, refs):
    qkv_ref, out_ref, up_ref, down_ref = refs
    high, wide, low = qkv_ref.shape[0], out_ref.shape[0], down_ref.shape[0]

    def total(first, rows):
        parts = [ref[z, pl.ds(first, rows), :] for ref in sources for z in range(ref.shape[0])]
        value = parts[0].astype(F32)
        for part in parts[1:]:
            value = value + part.astype(F32)
        return value

    qkv_ref[...] = total(spots.qkv[1], high)
    out_ref[...] = total(spots.out[1], wide)
    up_ref[...] = nt(identity(LANES), total(spots.up[1], up_ref.shape[1]).astype(BF16))
    for part, (_, first) in enumerate(spots.down):
        down_ref[:, pl.ds(part * LANES, LANES)] = total(first, low)
    return total


def store_layer(layer, held, outs, sems):
    copies = [
        pltpu.make_async_copy(ref, out.at[layer], sems.at[i])
        for i, (ref, out) in enumerate(zip(held, outs))
    ]
    for copy in copies:
        copy.start()
    return copies


def unpack_last_kernel(spots, layer, lines_ref, first_ref, *refs):
    outs, held, sems = refs[:4], refs[4:8], refs[8]
    unpack_layer(spots, (lines_ref, first_ref), held)
    wait_all(store_layer(layer, held, outs, sems))


def unpack_first_kernel(spots, small_at, parts_ref, *refs):
    outs, (gains_ref, biases_ref, ffn_bias_ref), held, sems = (
        refs[4:8], refs[8:11], refs[11:15], refs[15],
    )
    total = unpack_layer(spots, (parts_ref,), held)
    copies = store_layer(0, held, outs, sems)
    sums = total(small_at, SMALL_ROWS)
    parts = gains_ref.shape[2] // LANES
    for layer in range(gains_ref.shape[0]):
        for part in range(parts):
            lanes = pl.ds(part * LANES, LANES)
            at = (part * gains_ref.shape[0] + layer) * VEC_ROWS
            block = sums[at : at + VEC_ROWS]
            gains_ref[layer, :, lanes] = block[0:2]
            for row in range(biases_ref.shape[0]):
                biases_ref[row, pl.ds(layer, 1), lanes] = block[2 + row : 3 + row]
            for row in range(ffn_bias_ref.shape[1] // gains_ref.shape[2]):
                at = row * gains_ref.shape[2] + part * LANES
                ffn_bias_ref[pl.ds(layer, 1), pl.ds(at, LANES)] = block[8 + row : 9 + row]
    wait_all(copies)


def first_layer_kernel(
    sizes, seqs, mats, spots, count_in, place_ref, starts_ref, frames_ref, left_ref, right_ref,
    gains_ref, biases_ref, ffn_bias_ref, row_bias_ref, *refs
):
    groups = in_groups(spots, refs[:count_in])
    (
        z_ref, proj_ref, probs_ref, att_ref, mixed_ref, mem_ref, next_ref, active_ref, slope_ref,
        low_ref, send_right_ref, send_left_ref, qkv_ref, out_ref, up_ref, down_ref, mask_ref,
        hidden_ref, sems,
    ) = refs[count_in:]
    wide = sizes.width
    copies = start_in(attn_pairs(mats, spots, groups, qkv_ref, out_ref, place_ref), sems, 0)
    ffn_copies = start_in(
        ffn_pairs(mats, spots, groups, up_ref, down_ref, place_ref), sems, len(copies)
    )
    gain = gains_ref[0, pl.ds(0, 1), :]
    bias = biases_ref[0, pl.ds(0, 1), :]
    pad = jnp.zeros((TILE - sizes.segs, wide), F32)
    for n in range(seqs):
        own = frames_ref[n].astype(F32)
        before = left_ref[n].astype(F32)
        hidden = norm_forward(own, gain, bias)[0]
        halo = norm_forward(before[before.shape[0] - LEFT_ROWS :], gain, bias)[0]
        after = norm_forward(right_ref[n].astype(F32), gain, bias)[0]
        memory = jnp.concatenate(
            [
                segment_mean(own),
                jnp.zeros((sizes.segs - before.shape[0] // SEG_LEN, wide), F32),
                segment_mean(before),
            ],
            axis=0,
        )
        base = n * sizes.ext
        z_ref[pl.ds(base, sizes.top), :] = jnp.concatenate(
            [segment_mean(hidden), pad], axis=0
        ).astype(BF16)
        z_ref[pl.ds(base + sizes.top, sizes.rows), :] = hidden.astype(BF16)
        z_ref[pl.ds(base + sizes.right_at, RIGHT_ROWS), :] = after.astype(BF16)
        z_ref[pl.ds(base + sizes.left_at, LEFT_ROWS), :] = halo.astype(BF16)
        z_ref[pl.ds(base + sizes.mem_at, MEM_ROWS), :] = memory.astype(BF16)
    fill_mask(sizes, seqs, starts_ref, place_ref, mask_ref)
    wait_all(copies)
    project(sizes, z_ref, qkv_ref, row_bias_ref, proj_ref)
    attend(sizes, seqs, proj_ref, mask_ref, probs_ref, att_ref)
    mixed = nt(att_ref[...], out_ref[...].reshape(-1, wide)) + biases_ref[3, pl.ds(0, 1), :]
    for n in range(seqs):
        base = n * sizes.queries
        mem_ref[pl.ds(n * sizes.segs, sizes.segs), :] = mixed[base : base + sizes.segs]
        mixed_ref[pl.ds(n * sizes.rows, sizes.rows), :] = (
            frames_ref[n].astype(F32) + mixed[base + sizes.top : base + sizes.top + sizes.rows]
        )
    mixed = mixed_ref[...]
    hidden, _, _ = norm_forward(mixed, gains_ref[0, pl.ds(1, 1), :], biases_ref[4, pl.ds(0, 1), :])
    hidden_ref[...] = hidden.astype(BF16)
    next_ref[...] = mixed + biases_ref[5, pl.ds(0, 1), :]
    wait_all(ffn_copies)

    def body(c, carry):
        at_lane = pl.multiple_of(c * wide, wide)
        upward = nt(hidden_ref[...], up_block(up_ref, c, wide))
        upward = upward + ffn_bias_ref[pl.ds(0, 1), pl.ds(at_lane, wide)]
        active, slope = gelu_both(upward)
        active = active.astype(BF16)
        active_ref[:, pl.ds(at_lane, wide)] = active
        slope_ref[:, pl.ds(at_lane, wide)] = slope.astype(BF16)
        next_ref[...] += nt(active, down_block(down_ref, c, wide))
        return carry

    lax.fori_loop(0, sizes.ff // wide, body, 0)
    low, _, _ = norm_forward(
        next_ref[...], gains_ref[1, pl.ds(0, 1), :], biases_ref[0, pl.ds(1, 1), :]
    )
    low = low.astype(BF16)
    low_ref[...] = low
    for n in range(seqs):
        base = n * sizes.rows
        send_right_ref[n, pl.ds(0, LEFT_ROWS), :] = low[
            base + sizes.rows - LEFT_ROWS : base + sizes.rows
        ]
        send_right_ref[n, pl.ds(LEFT_ROWS, MEM_ROWS), :] = jnp.concatenate(
            [
                mem_ref[pl.ds(n * sizes.segs, sizes.segs), :],
                jnp.zeros((MEM_ROWS - sizes.segs, wide), F32),
            ],
            axis=0,
        ).astype(BF16)
        send_left_ref[n] = low[base : base + RIGHT_ROWS]


def last_layer_kernel(
    sizes, seqs, mats, spots, count_in, count_out, place_ref, starts_ref, low_ref, left_ref,
    right_ref, mem_ref, inputs_ref, out_grad_ref, gains_ref, biases_ref, ffn_bias_ref,
    row_bias_ref, *refs
):
    groups = in_groups(spots, refs[:count_in])
    (encoded_ref, gz_ref, gh_ref, gmem_ref, back_left_ref, back_right_ref, vec) = refs[
        count_in : count_in + 7
    ]
    hbm_out = refs[count_in + 7 : count_in + 7 + count_out]
    (
        qkv_ref, out_ref, up_ref, down_ref, gqkv_ref, gout_ref, gup_ref, gdown_ref, mask_ref,
        z_ref, proj_ref, probs_ref, att_ref, hidden_ref, go_ref, gproj_ref, branch_ref,
        grad_low_ref, grad_hidden_ref, sems,
    ) = refs[count_in + 7 + count_out :]
    outs_to = hbm_out
    if spots is not None:
        rows = mats.attn_rows + mats.ffn_rows
        outs_to = [
            [
                ref.at[hop2, :, pl.ds(hop1 * rows, rows), :]
                for ref in hbm_out
                for hop2 in range(2)
                for hop1 in range(2)
            ]
        ]
    wide = sizes.width
    attn_copies = start_in(attn_pairs(mats, spots, groups, qkv_ref, out_ref, place_ref), sems, 0)
    ffn_copies = start_in(
        ffn_pairs(mats, spots, groups, up_ref, down_ref, place_ref), sems, len(attn_copies)
    )
    vec[...] = jnp.zeros_like(vec)
    for n in range(seqs):
        base = n * sizes.ext
        z_ref[pl.ds(base, sizes.rows), :] = low_ref[pl.ds(n * sizes.rows, sizes.rows), :]
        z_ref[pl.ds(base + sizes.right_at, RIGHT_ROWS), :] = right_ref[n]
        z_ref[pl.ds(base + sizes.left_at, LEFT_ROWS), :] = left_ref[n, pl.ds(0, LEFT_ROWS), :]
        memory = jnp.concatenate(
            [
                mem_ref[pl.ds(n * sizes.segs, sizes.segs), :],
                left_ref[n, pl.ds(LEFT_ROWS, MEM_ROWS), :].astype(F32)[: sizes.segs],
            ],
            axis=0,
        )
        z_ref[pl.ds(base + sizes.mem_at, MEM_ROWS), :] = memory.astype(BF16)
        grad_low_ref[pl.ds(n * sizes.rows, sizes.rows), :] = out_grad_ref[n]
    fill_mask(sizes, seqs, starts_ref, place_ref, mask_ref)
    wait_all(attn_copies)
    project(sizes, z_ref, qkv_ref, row_bias_ref, proj_ref)
    attend(sizes, seqs, proj_ref, mask_ref, probs_ref, att_ref)
    mixed = (
        inputs_ref[...]
        + nt(att_ref[...], out_ref[...].reshape(-1, wide))
        + biases_ref[3, pl.ds(1, 1), :]
    )
    gain = gains_ref[1, pl.ds(1, 1), :]
    hidden, scaled, inverse = norm_forward(mixed, gain, biases_ref[4, pl.ds(1, 1), :])
    hidden_ref[...] = hidden.astype(BF16)
    for n in range(seqs):
        encoded_ref[n] = mixed[n * sizes.rows : (n + 1) * sizes.rows] + biases_ref[5, pl.ds(1, 1), :]
    grad_hidden_ref[...] = jnp.zeros_like(grad_hidden_ref)
    wait_all(ffn_copies)

    def body(c, carry):
        at_lane = pl.multiple_of(c * wide, wide)
        upward = nt(hidden_ref[...], up_block(up_ref, c, wide))
        upward = upward + ffn_bias_ref[pl.ds(1, 1), pl.ds(at_lane, wide)]
        active, slope = gelu_both(upward)
        active = active.astype(BF16)
        made = nt(active, down_block(down_ref, c, wide))
        for n in range(seqs):
            encoded_ref[n] += made[n * sizes.rows : (n + 1) * sizes.rows]
        grad_hidden_ref[...] += ffn_back_step(
            sizes, c, wide, grad_low_ref[...], hidden_ref[...], active, slope, up_ref, down_ref,
            gup_ref, gdown_ref, vec,
        )
        return carry

    lax.fori_loop(0, sizes.ff // wide, body, 0)
    out_at = len(attn_copies) + len(ffn_copies)
    outs = start_out(
        ffn_pairs(mats, spots, outs_to, gup_ref, gdown_ref, place_ref), sems, out_at
    )
    grad = grad_low_ref[...].astype(F32)
    grad_hidden = grad_hidden_ref[...]
    vec[pl.ds(1, 1), :] = col_sum(grad_hidden * scaled)
    vec[pl.ds(6, 1), :] = col_sum(grad_hidden)
    vec[pl.ds(7, 1), :] = col_sum(grad)
    gz = grad + norm_backward(grad_hidden, scaled, inverse, gain)
    gz_ref[...] = gz
    attn_back_stage(
        sizes, seqs, gz, None, att_ref, proj_ref, probs_ref, z_ref, qkv_ref, out_ref, gqkv_ref,
        gout_ref, go_ref, gproj_ref, branch_ref, vec, gh_ref, gmem_ref, back_left_ref,
        back_right_ref,
    )
    outs = outs + start_out(
        attn_pairs(mats, spots, outs_to, gqkv_ref, gout_ref, place_ref),
        sems,
        out_at + len(outs),
    )
    wait_all(outs)


def first_back_kernel(
    last, sizes, seqs, mats, spots, count_in, count_out, place_ref, inputs_ref, gz_in_ref,
    gh_in_ref, gmem_in_ref, from_right_ref, from_left_ref, mixed_ref, active_ref, slope_ref,
    att_ref, probs_ref, proj_ref, z_ref, frames_ref, left_ref, right_ref, gains_ref, biases_ref,
    last_vec, *refs
):
    groups = in_groups(spots, refs[:count_in])
    gz_ref, gh_ref, gmem_ref, back_left_ref, back_right_ref, upper_vec, vec = refs[
        count_in : count_in + 7
    ]
    refs = refs[count_in + 7 :]
    hbm_out = refs[:count_out]
    (
        qkv_ref, out_ref, up_ref, down_ref, gqkv_ref, gout_ref, gup_ref, gdown_ref, hidden_ref,
        grad_low_ref, grad_ref, grad_hidden_ref, grad_mem_ref, go_ref, gproj_ref, branch_ref,
        small_ref, sems,
    ) = refs[count_out:]
    wide = sizes.width
    small = []
    outs_to = hbm_out
    if spots is not None:
        rows = mats.attn_rows + mats.ffn_rows
        end = CHIPS_Z * rows
        each = [
            ref.at[hop2, hop1] for ref in hbm_out for hop2 in range(2) for hop1 in range(2)
        ]
        small = [ref.at[pl.ds(end, SMALL_ROWS), :] for ref in each]
        outs_to = [[ref.at[pl.ds(0, end), :].reshape(CHIPS_Z, rows, LANES) for ref in each]]
    ffn_copies = start_in(ffn_pairs(mats, spots, groups, up_ref, down_ref, place_ref), sems, 0)
    attn_copies = start_in(
        attn_pairs(mats, spots, groups, qkv_ref, out_ref, place_ref), sems, len(ffn_copies)
    )
    vec[...] = jnp.zeros_like(vec)
    upper_vec[...] = jnp.zeros_like(upper_vec)
    gain = gains_ref[1, pl.ds(0, 1), :]
    gain_sum = jnp.zeros((1, wide), F32)
    bias_sum = jnp.zeros((1, wide), F32)
    for n in range(seqs):
        rows = pl.ds(n * sizes.rows, sizes.rows)
        _, scaled, inverse = norm_forward(
            inputs_ref[rows, :], gain, biases_ref[0, pl.ds(1, 1), :]
        )
        total, mem = merge_halo(last, n, gh_in_ref, gmem_in_ref, from_right_ref, from_left_ref)
        gain_sum = gain_sum + col_sum(total * scaled)
        bias_sum = bias_sum + col_sum(total)
        grad = gz_in_ref[rows, :] + norm_backward(total, scaled, inverse, gain)
        grad_ref[rows, :] = grad
        grad_low_ref[rows, :] = grad.astype(BF16)
        grad_mem_ref[pl.ds(n * sizes.segs, sizes.segs), :] = mem
    upper_vec[pl.ds(0, 1), :] = gain_sum
    upper_vec[pl.ds(2, 1), :] = bias_sum
    gain = gains_ref[0, pl.ds(1, 1), :]
    hidden, scaled, inverse = norm_forward(
        mixed_ref[...], gain, biases_ref[4, pl.ds(0, 1), :]
    )
    hidden_ref[...] = hidden.astype(BF16)
    grad_hidden_ref[...] = jnp.zeros_like(grad_hidden_ref)
    wait_all(ffn_copies)

    def body(c, carry):
        at_lane = pl.multiple_of(c * wide, wide)
        grad_hidden_ref[...] += ffn_back_step(
            sizes, c, wide, grad_low_ref[...], hidden_ref[...],
            active_ref[:, pl.ds(at_lane, wide)], slope_ref[:, pl.ds(at_lane, wide)].astype(F32),
            up_ref, down_ref, gup_ref, gdown_ref, vec,
        )
        return carry

    lax.fori_loop(0, sizes.ff // wide, body, 0)
    out_at = len(ffn_copies) + len(attn_copies)
    outs = start_out(
        ffn_pairs(mats, spots, outs_to, gup_ref, gdown_ref, place_ref), sems, out_at
    )
    grad_hidden = grad_hidden_ref[...]
    grad = grad_ref[...]
    vec[pl.ds(1, 1), :] = col_sum(grad_hidden * scaled)
    vec[pl.ds(6, 1), :] = col_sum(grad_hidden)
    vec[pl.ds(7, 1), :] = col_sum(grad)
    gz = grad + norm_backward(grad_hidden, scaled, inverse, gain)
    gz_ref[...] = gz

    def scaled_rows(n):
        before = left_ref[n, pl.ds(left_ref.shape[1] - LEFT_ROWS, LEFT_ROWS), :]
        parts = (frames_ref[n], right_ref[n], before)
        first_gain = gains_ref[0, pl.ds(0, 1), :]
        first_bias = biases_ref[0, pl.ds(0, 1), :]
        return [norm_forward(part.astype(F32), first_gain, first_bias)[1] for part in parts]

    wait_all(attn_copies)
    attn_back_stage(
        sizes, seqs, gz, grad_mem_ref, att_ref, proj_ref, probs_ref, z_ref, qkv_ref, out_ref,
        gqkv_ref, gout_ref, go_ref, gproj_ref, branch_ref, vec, gh_ref, gmem_ref, back_left_ref,
        back_right_ref, scaled_rows,
    )
    outs = outs + start_out(
        attn_pairs(mats, spots, outs_to, gqkv_ref, gout_ref, place_ref),
        sems,
        out_at + len(outs),
    )
    totals = vec[...], last_vec[...] + upper_vec[...]
    small_ref[...] = jnp.concatenate(
        [
            total[:VEC_ROWS, part * LANES : (part + 1) * LANES]
            for part in range(sizes.pairs)
            for total in totals
        ],
        axis=0,
    ).astype(BF16)
    outs = outs + start_out([(ref, small_ref) for ref in small], sems, out_at + len(outs))
    wait_all(outs)


def frames_grad_kernel(
    sizes, seqs, frames_ref, gz_ref, gh_ref, gmem_ref, from_right_ref, from_left_ref, gains_ref,
    biases_ref, grad_ref
):
    gain = gains_ref[0, pl.ds(0, 1), :]
    for n in range(seqs):
        _, scaled, inverse = norm_forward(
            frames_ref[n].astype(F32), gain, biases_ref[0, pl.ds(0, 1), :]
        )
        total, mem = merge_halo(sizes, n, gh_ref, gmem_ref, from_right_ref, from_left_ref)
        grad_ref[n] = (
            gz_ref[pl.ds(n * sizes.rows, sizes.rows), :]
            + norm_backward(total, scaled, inverse, gain)
            + segment_spread(sizes.rows, sizes.width, mem * (1.0 / SEG_LEN))
        )


def shifted(value, axis, by):
    size = lax.axis_size(axis)
    return lax.ppermute(value, axis, [(i, (i + by) % size) for i in range(size)])


def permuted(value, move):
    reps = lax.axis_size("rep")
    pairs = []
    for flat in range(lax.axis_size("seg") * reps):
        seg, rep = divmod(flat, reps)
        z, y, x, core = move(seg // CHIPS_Y, seg % CHIPS_Y, rep // 2, rep % 2)
        pairs.append((flat, (z * CHIPS_Y + y) * reps + 2 * x + core))
    return lax.ppermute(value, ("seg", "rep"), pairs)


def across_first(value):
    return permuted(value, lambda z, y, x, c: (z, y, x ^ 1, c) if c == 0 else (z, y ^ 1, x, c))


def across_second(value):
    return permuted(value, lambda z, y, x, c: (z, y ^ 1, x, c) if c == 0 else (z, y, x ^ 1, c))


def other_core(value):
    return permuted(value, lambda z, y, x, c: (z, y, x, c ^ 1))


def after(value, *others):
    return lax.optimization_barrier((value,) + others)[0]


def swap_z(blocks):
    groups = [
        [z * CHIPS_Y + y for z in range(CHIPS_Z)] for y in range(CHIPS_Y)
    ]
    return lax.all_to_all(blocks, "seg", 0, 0, axis_index_groups=groups, tiled=True)


def gather_sides(here):
    return [here, across_first(here), across_second(here)]


def both_cores(blocks):
    return blocks + [other_core(block) for block in blocks]


def summed(*parts):
    total = parts[0].astype(F32)
    for part in parts[1:]:
        total = total + part.astype(F32)
    return total.astype(BF16)


def sum_everywhere(value):
    count = lax.axis_size("seg") * lax.axis_size("rep")
    bit = 1
    while bit < count:
        value = value + lax.ppermute(value, ("seg", "rep"), [(i, i ^ bit) for i in range(count)])
        bit *= 2
    return value


def vmem_spec():
    return pl.BlockSpec(memory_space=pltpu.VMEM)


def smem_spec():
    return pl.BlockSpec(memory_space=pltpu.SMEM)


def hbm_spec():
    return pl.BlockSpec(memory_space=pl.ANY)


def call(body, in_specs, out_shapes, out_specs, scratch, args, flops=0, moved=0, grid=(), aliases={}, vmem=12):
    return pl.pallas_call(
        body,
        grid=grid,
        input_output_aliases=aliases,
        in_specs=in_specs,
        out_shape=tuple(jax.ShapeDtypeStruct(shape, kind) for shape, kind in out_shapes),
        out_specs=tuple(out_specs),
        scratch_shapes=scratch,
        compiler_params=pltpu.CompilerParams(vmem_limit_bytes=vmem * MIB),
        cost_estimate=pl.CostEstimate(flops=flops, bytes_accessed=moved, transcendentals=0),
    )(*args)


def on_device(
    frames,
    utt_segments,
    out_grad,
    qkv_weight,
    out_weight,
    ffn_in_weight,
    ffn_out_weight,
    norm_gains,
    biases,
    ffn_bias,
):
    micros, groups, rows, width = frames.shape
    seqs = micros * groups
    ff = ffn_bias.shape[1]
    reps = lax.axis_size("rep")
    seg_count = lax.axis_size("seg")
    mats = Matrices(width, ff)
    by_blocks = width // reps == LANES and reps == 4 and seg_count == BLOCKS
    first = Sizes(rows, width, ff, True)
    last = Sizes(rows, width, ff, False)
    own = seqs * rows
    mem_own = seqs * first.segs

    seg_at = lax.axis_index("seg")
    seg_base = seg_at * first.segs
    rep_at = lax.axis_index("rep")
    place = [seg_base, jnp.int32(first.segs * seg_count)]
    y_at, x_at, core_at = seg_at % CHIPS_Y, rep_at // 2, rep_at % 2
    for other in range(2):
        core = lax.bitwise_xor(core_at, other)
        for hop2 in range(2):
            for hop1 in range(2):
                x_hop = jnp.where(core == 0, hop1, hop2)
                y_hop = jnp.where(core == 0, hop2, hop1)
                place.append(lax.bitwise_xor(y_at, y_hop))
                place.append((lax.bitwise_xor(x_at, x_hop) * 2 + core) * LANES)
    place = jnp.stack([jnp.asarray(entry, jnp.int32) for entry in place])
    lengths = utt_segments.reshape(seqs, utt_segments.shape[2])
    starts = (jnp.cumsum(lengths, axis=1) - lengths).astype(jnp.int32)
    zero_bias = jnp.zeros((1, width), F32)
    row_biases = [
        jnp.concatenate([biases[l : l + 1, 1], zero_bias, biases[l : l + 1, 2]], axis=1)
        for l in range(LAYERS)
    ]
    biases_by_row = jnp.swapaxes(biases, 0, 1)

    frames_own = frames.reshape(seqs, rows, width)
    grads_own = out_grad.reshape(seqs, rows, width)
    far = MEM_LEN * SEG_LEN
    frames_left = shifted(frames_own[:, rows - far :], "seg", 1)
    frames_right = shifted(frames_own[:, :RIGHT_ROWS], "seg", -1)

    attn_rows, ffn_rows = mats.attn_rows, mats.ffn_rows
    if by_blocks:
        qkv_t, out_t, down_t = (
            jnp.swapaxes(member, 1, 2) for member in (qkv_weight, out_weight, ffn_out_weight)
        )
        all_rows = attn_rows + ffn_rows
        spots = Spots(mats)
        shards = call(
            lambda *refs: pack_kernel(spots, *refs),
            [vmem_spec()] * 4,
            [((CHIPS_Z, all_rows, LANES), BF16)] * LAYERS,
            [vmem_spec()] * LAYERS,
            [],
            (qkv_t, out_t, ffn_in_weight, down_t),
            vmem=56,
        )
        sides0 = gather_sides(after(swap_z(shards[0]), frames_left, frames_right))
        place, starts, row_biases, sent = lax.optimization_barrier(
            (place, starts, row_biases, after(shards[1], sides0[0]))
        )
        sides1 = gather_sides(swap_z(sent))
        first_all = both_cores(sides0 + [across_second(after(sides0[1], sides1[0]))])
        classes = len(first_all) // 2
        grad_outs0 = [((2, 2, CHIPS_Z * all_rows + SMALL_ROWS, LANES), BF16)] * 2
        grad_outs1 = [((2, CHIPS_Z, 2 * all_rows, LANES), BF16)] * 2
        copies_in = len(first_all) * (3 + mats.down_parts)
    else:
        whole = []
        for member, shape in zip(
            (qkv_weight, out_weight, ffn_in_weight, ffn_out_weight),
            (mats.qkv, mats.out, mats.up, mats.down),
        ):
            member = lax.all_gather(member, "rep", axis=1, tiled=True)
            member = lax.all_gather(member, "seg", axis=2, tiled=True)
            whole.append(jnp.swapaxes(member, 1, 2).reshape((LAYERS,) + shape))
        first_all = [member[0] for member in whole]
        last_all = [member[1] for member in whole]
        spots = None
        grad_outs0 = grad_outs1 = [
            (shape, BF16) for shape in (mats.qkv, mats.out, mats.up, mats.down)
        ]
        copies_in = 4
    dma = pltpu.SemaphoreType.DMA

    matrices = [pltpu.VMEM(shape, BF16) for shape in (mats.qkv, mats.out, mats.up, mats.down)]

    (
        z0, proj0, probs0, att0, mixed0, mem1, x1, active0, slope0, low1, send_right, send_left,
    ) = call(
        lambda *refs: first_layer_kernel(
            first, seqs, mats, spots, len(first_all), *refs
        ),
        [smem_spec()] * 2 + [vmem_spec()] * 7 + [hbm_spec()] * len(first_all),
        [
            ((seqs * first.ext, width), BF16),
            ((seqs * first.ext, 3 * width), BF16),
            ((seqs * first.pairs, first.keys, 2 * first.queries), BF16),
            ((seqs * first.queries, width), BF16),
            ((own, width), F32),
            ((mem_own, width), F32),
            ((own, width), F32),
            ((own, ff), BF16),
            ((own, ff), BF16),
            ((own, width), BF16),
            ((seqs, BACK_ROWS, width), BF16),
            ((seqs, RIGHT_ROWS, width), BF16),
        ],
        [vmem_spec()] * 12,
        matrices
        + [
            pltpu.VMEM((seqs, first.keys, 2 * first.queries), F32),
            pltpu.VMEM((own, width), BF16),
            dma((copies_in,)),
        ],
        (place, starts, frames_own, frames_left, frames_right, norm_gains, biases_by_row, ffn_bias,
         row_biases[0]) + tuple(first_all),
        flops=24 * own * (4 * width * width + 2 * width * ff) // 2,
        moved=2 * (4 * width * width + 2 * width * ff),
        vmem=24,
    )
    left1 = shifted(send_right, "seg", 1)
    right1 = shifted(send_left, "seg", -1)
    if by_blocks:
        last_side = across_second(after(sides1[1], sides1[2], left1, right1))
        last_all = both_cores(sides1 + [last_side])

    vec_shape = (TILE, width)
    outs = call(
        lambda *refs: last_layer_kernel(
            last, seqs, mats, spots, len(last_all), len(grad_outs1), *refs
        ),
        [smem_spec()] * 2 + [vmem_spec()] * 10 + [hbm_spec()] * len(last_all),
        [
            ((seqs, rows, width), F32),
            ((own, width), F32),
            ((own, width), F32),
            ((mem_own, width), F32),
            ((seqs, BACK_ROWS, width), BF16),
            ((seqs, RIGHT_ROWS, width), BF16),
            (vec_shape, F32),
        ]
        + grad_outs1,
        [vmem_spec()] * 7 + [hbm_spec()] * len(grad_outs1),
        matrices
        + matrices
        + [
            pltpu.VMEM((seqs, last.keys, 2 * last.queries), F32),
            pltpu.VMEM((seqs * last.ext, width), BF16),
            pltpu.VMEM((seqs * last.ext, 3 * width), BF16),
            pltpu.VMEM((seqs * last.pairs, last.keys, 2 * last.queries), BF16),
            pltpu.VMEM((seqs * last.queries, width), BF16),
            pltpu.VMEM((own, width), BF16),
            pltpu.VMEM((seqs * last.queries, width), BF16),
            pltpu.VMEM((seqs * last.ext, 3 * width), BF16),
            pltpu.VMEM((seqs * last.queries, width), BF16),
            pltpu.VMEM((own, width), BF16),
            pltpu.VMEM((own, width), F32),
            dma((2 * copies_in,)),
        ],
        (place, starts, low1, left1, right1, mem1, x1, grads_own, norm_gains, biases_by_row, ffn_bias,
         row_biases[1]) + tuple(last_all),
        flops=30 * own * (4 * width * width + 2 * width * ff),
        moved=4 * (4 * width * width + 2 * width * ff),
        vmem=34,
    )
    encoded, gz1, gh1, gmem1, back_left1, back_right1, vec1 = outs[:7]
    grad_blocks1 = outs[7:]
    from_right1 = shifted(back_left1, "seg", -1)
    from_left1 = shifted(back_right1, "seg", 1)

    gh1_tied = gh1
    if by_blocks:
        mine1, theirs1 = grad_blocks1[0], other_core(grad_blocks1[1])
        far1 = summed(mine1[1], theirs1[1])
        gh1_tied = after(gh1, far1)
    gz0, gh0, gmem0, back_left0, back_right0, upper_vec, vec0, *grad_blocks0 = call(
        lambda *refs: first_back_kernel(
            last, first, seqs, mats, spots, len(first_all), len(grad_outs0), *refs
        ),
        [smem_spec()] + [vmem_spec()] * 19 + [hbm_spec()] * len(first_all),
        [
            ((own, width), F32),
            ((own, width), F32),
            ((mem_own, width), F32),
            ((seqs, BACK_ROWS, width), BF16),
            ((seqs, RIGHT_ROWS, width), BF16),
            (vec_shape, F32),
            (vec_shape, F32),
        ]
        + grad_outs0,
        [vmem_spec()] * 7 + [hbm_spec()] * len(grad_outs0),
        matrices
        + matrices
        + [
            pltpu.VMEM((own, width), BF16),
            pltpu.VMEM((own, width), BF16),
            pltpu.VMEM((own, width), F32),
            pltpu.VMEM((own, width), F32),
            pltpu.VMEM((mem_own, width), F32),
            pltpu.VMEM((seqs * first.queries, width), BF16),
            pltpu.VMEM((seqs * first.ext, 3 * width), BF16),
            pltpu.VMEM((seqs * first.queries, width), BF16),
            pltpu.VMEM((SMALL_ROWS, LANES), BF16),
            dma((2 * copies_in + 8,)),
        ],
        (place, x1, gz1, gh1_tied, gmem1, from_right1, from_left1, mixed0, active0, slope0, att0,
         probs0, proj0, z0, frames_own, frames_left, frames_right, norm_gains, biases_by_row, vec1)
        + tuple(first_all),
        flops=28 * own * (4 * width * width + 2 * width * ff),
        moved=4 * (4 * width * width + 2 * width * ff),
        vmem=34,
    )
    from_right0 = shifted(back_left0, "seg", -1)
    from_left0 = shifted(back_right0, "seg", 1)
    gz0_last = gz0
    if by_blocks:
        second1 = across_second(far1)
        mine0, theirs0 = grad_blocks0[0], other_core(after(grad_blocks0[1], second1))
        both1 = summed(mine1[0], theirs1[0], second1)
        lines1 = swap_z(both1)
        far0 = summed(mine0[1], after(theirs0, both1)[1])
        far0 = after(far0, from_right0, from_left0)
        second0 = across_second(far0)
        mid0 = summed(mine0[0, 1], theirs0[0, 1], second0[1])
        first0 = across_first(mid0)
        held0 = summed(mine0[0, 0], theirs0[0, 0], after(second0, mid0)[0])
        near0 = summed(held0, first0)
        blocks = CHIPS_Z * all_rows
        near0 = jnp.concatenate(
            [
                near0[:blocks].reshape(CHIPS_Z, all_rows, LANES),
                jnp.broadcast_to(near0[None, blocks:], (CHIPS_Z, SMALL_ROWS, LANES)),
            ],
            axis=1,
        )
        first_parts = swap_z(near0)
        gz0_last, lines1 = lax.optimization_barrier((after(gz0, near0), lines1))
        cross1 = jnp.sum(lines1[:, all_rows:].astype(F32), axis=0, keepdims=True).astype(BF16)
        first1 = across_first(cross1)
    frames_grad = call(
        lambda *refs: frames_grad_kernel(first, seqs, *refs),
        [vmem_spec()] * 8,
        [((seqs, rows, width), F32)],
        [vmem_spec()],
        [],
        (frames_own, gz0_last, gh0, gmem0, from_right0, from_left0, norm_gains, biases_by_row),
    )[0]

    if by_blocks:
        shapes = [member.shape for member in (qkv_t, out_t, ffn_in_weight, down_t)]
        held = [pltpu.VMEM(shape[1:], F32) for shape in shapes]
        whole = [(shape, F32) for shape in shapes]
        written = call(
            lambda *refs: unpack_last_kernel(spots, LAYERS - 1, *refs),
            [
                pl.BlockSpec((CHIPS_Z, all_rows, LANES), lambda i: (0, 0, 0)),
                pl.BlockSpec((1, all_rows, LANES), lambda i: (0, 0, 0)),
            ],
            whole,
            [hbm_spec()] * 4,
            held + [dma((4,))],
            [lines1, first1],
            grid=(1,),
        )
        small_shapes = [norm_gains.shape, (biases.shape[1], LAYERS, width), ffn_bias.shape]
        reduced = call(
            lambda *refs: unpack_first_kernel(spots, all_rows, *refs),
            [vmem_spec()] + [hbm_spec()] * 4,
            whole + [(shape, F32) for shape in small_shapes],
            [hbm_spec()] * 4 + [vmem_spec()] * 3,
            held + [dma((4,))],
            [after(first_parts, frames_grad)] + list(written),
            aliases={1 + i: i for i in range(4)},
        )
        small = reduced[4], jnp.swapaxes(reduced[5], 0, 1), reduced[6]
        reduced = [
            jnp.swapaxes(reduced[0], 1, 2),
            jnp.swapaxes(reduced[1], 1, 2),
            reduced[2],
            jnp.swapaxes(reduced[3], 1, 2),
        ]
    else:
        reduced = []
        for member0, member1 in zip(grad_blocks0, grad_blocks1):
            both = jnp.stack([member0, member1]).reshape(LAYERS, -1, member0.shape[3])
            both = jnp.swapaxes(both, 1, 2)
            both = lax.psum_scatter(both, "seg", scatter_dimension=2, tiled=True)
            both = lax.psum_scatter(both, "rep", scatter_dimension=1, tiled=True)
            reduced.append(both.astype(F32))
        small = sum_everywhere(jnp.stack([vec0, vec1 + upper_vec]))
        small = small[:, 0:2], small[:, 2:8], small[:, 8:12].reshape(ffn_bias.shape)

    return (
        encoded.reshape(frames.shape),
        frames_grad.reshape(frames.shape),
        reduced[0],
        reduced[1],
        reduced[2],
        reduced[3],
        small[0],
        small[1],
        small[2],
    )


def solution(mesh):
    in_specs = (
        P(None, "rep", "seg", None),
        P(None, "rep", None),
        P(None, "rep", "seg", None),
        P(None, "rep", "seg"),
        P(None, "rep", "seg"),
        P(None, "rep", "seg"),
        P(None, "rep", "seg"),
        P(),
        P(),
        P(),
    )
    out_specs = (
        P(None, "rep", "seg", None),
        P(None, "rep", "seg", None),
        P(None, "rep", "seg"),
        P(None, "rep", "seg"),
        P(None, "rep", "seg"),
        P(None, "rep", "seg"),
        P(),
        P(),
        P(),
    )
    return jax.shard_map(
        on_device, mesh=mesh, in_specs=in_specs, out_specs=out_specs, check_vma=False
    )
```

```python
import jax
import jax.numpy as jnp
from jax import lax
from jax.experimental import pallas as pl
from jax.experimental.pallas import tpu as pltpu
from jax.sharding import PartitionSpec as P

HEADS = 8
SEG_LEN = 16
LEFT_LEN = 30
RIGHT_LEN = 4
MEM_LEN = 4
LAYERS = 2

EPS = 1e-05
ROOT_HALF = 0.7071067811865476
INV_ROOT_TWO_PI = 0.3989422804014327

LANES = 128
TILE = 16
RIGHT_ROWS = 16
LEFT_ROWS = 32
MEM_ROWS = 16
BACK_ROWS = LEFT_ROWS + MEM_ROWS
CHIPS_Z = 4
CHIPS_Y = 2
BLOCKS = CHIPS_Z * CHIPS_Y
VEC_ROWS = 12
SMALL_ROWS = 96
MIB = 1024 * 1024

BF16 = jnp.bfloat16
F32 = jnp.float32


def nn(a, b):
    return lax.dot_general(a, b, (((1,), (0,)), ((), ())), preferred_element_type=F32)


def nt(a, b):
    return lax.dot_general(a, b, (((1,), (1,)), ((), ())), preferred_element_type=F32)


def tn(a, b):
    return lax.dot_general(a, b, (((0,), (0,)), ((), ())), preferred_element_type=F32)


def col_sum(value):
    return jnp.sum(value, axis=0, keepdims=True)


def norm_forward(inputs, gain, bias):
    center = inputs - jnp.mean(inputs, axis=1, keepdims=True)
    inverse = lax.rsqrt(jnp.mean(center * center, axis=1, keepdims=True) + EPS)
    scaled = center * inverse
    return scaled * gain + bias, scaled, inverse


def norm_backward(grad_in, scaled, inverse, gain):
    grad_scaled = grad_in * gain
    return inverse * (
        grad_scaled
        - jnp.mean(grad_scaled, axis=1, keepdims=True)
        - scaled * jnp.mean(grad_scaled * scaled, axis=1, keepdims=True)
    )


def segment_mean(inputs):
    rows, width = inputs.shape
    return jnp.mean(inputs.reshape(rows // SEG_LEN, SEG_LEN, width), axis=1)


def segment_spread(rows, width, per_segment):
    segs = rows // SEG_LEN
    return jnp.broadcast_to(per_segment[:, None, :], (segs, SEG_LEN, width)).reshape(rows, width)


def identity(size):
    row = lax.broadcasted_iota(jnp.int32, (size, size), 0)
    col = lax.broadcasted_iota(jnp.int32, (size, size), 1)
    return (row == col).astype(F32).astype(BF16)


class Sizes:
    def __init__(self, rows, width, ff, with_summary):
        self.rows = rows
        self.width = width
        self.ff = ff
        self.segs = rows // SEG_LEN
        self.top = TILE if with_summary else 0
        self.keys = rows + RIGHT_ROWS + LEFT_ROWS + MEM_ROWS
        self.ext = self.top + self.keys
        self.queries = self.top + rows
        self.right_at = self.top + rows
        self.left_at = self.right_at + RIGHT_ROWS
        self.mem_at = self.left_at + LEFT_ROWS
        self.pairs = width // LANES


class Matrices:
    def __init__(self, width, ff):
        self.qkv = (CHIPS_Z, CHIPS_Y, 3 * width // BLOCKS, width)
        self.out = (CHIPS_Z, CHIPS_Y, width // BLOCKS, width)
        self.up = (CHIPS_Z, CHIPS_Y, ff // BLOCKS, width)
        self.down = (CHIPS_Z, CHIPS_Y, width // BLOCKS, ff)
        self.down_parts = ff // width
        self.attn_rows = self.qkv[2] + self.out[2]
        self.ffn_rows = self.up[2] + self.down_parts * self.down[2]


class Spots:
    def __init__(self, mats):
        high, wide, up, low = mats.qkv[2], mats.out[2], mats.up[2], mats.down[2]
        self.qkv = (0, 0)
        self.out = (0, high)
        self.up = (0, high + wide)
        self.down = [(0, high + wide + up + low * part) for part in range(mats.down_parts)]


def attn_pairs(mats, spots, groups, qkv_ref, out_ref, place_ref):
    if spots is None:
        return [(groups[0], qkv_ref), (groups[1], out_ref)]
    pairs = []
    for k in range(len(groups[0])):
        row = place_ref[2 + 2 * k]
        lane = pl.multiple_of(place_ref[3 + 2 * k], LANES)
        for (group, first), ref, shape in (
            (spots.qkv, qkv_ref, mats.qkv),
            (spots.out, out_ref, mats.out),
        ):
            block = groups[group][k]
            pairs.append(
                (
                    block.at[:, pl.ds(first, shape[2]), :],
                    ref.at[:, row, :, pl.ds(lane, LANES)],
                )
            )
    return pairs


def ffn_pairs(mats, spots, groups, up_ref, down_ref, place_ref):
    if spots is None:
        return [(groups[2], up_ref), (groups[3], down_ref)]
    pairs = []
    for k in range(len(groups[0])):
        row = place_ref[2 + 2 * k]
        lane = pl.multiple_of(place_ref[3 + 2 * k], LANES)
        group, first = spots.up
        block = groups[group][k]
        pairs.append(
            (block.at[:, pl.ds(first, mats.up[2]), :], up_ref.at[:, row, :, pl.ds(lane, LANES)])
        )
        for part, (group, first) in enumerate(spots.down):
            there = pl.multiple_of(
                place_ref[3 + 2 * k] * mats.down_parts + part * LANES, LANES
            )
            block = groups[group][k]
            pairs.append(
                (
                    block.at[:, pl.ds(first, mats.down[2]), :],
                    down_ref.at[:, row, :, pl.ds(there, LANES)],
                )
            )
    return pairs


def start_in(pairs, sems, at):
    copies = [pltpu.make_async_copy(s, d, sems.at[at + i]) for i, (s, d) in enumerate(pairs)]
    for copy in copies:
        copy.start()
    return copies


def start_out(pairs, sems, at):
    copies = [pltpu.make_async_copy(d, s, sems.at[at + i]) for i, (s, d) in enumerate(pairs)]
    for copy in copies:
        copy.start()
    return copies


def in_groups(spots, refs):
    return refs if spots is None else [refs]


def wait_all(copies):
    for copy in copies:
        copy.wait()


def fill_mask(sizes, seqs, starts_ref, place_ref, mask_ref):
    shape = (sizes.keys, 2 * sizes.queries)
    key = lax.broadcasted_iota(jnp.int32, shape, 0)
    col = lax.broadcasted_iota(jnp.int32, shape, 1)
    col = jnp.where(col < sizes.queries, col, col - sizes.queries)
    base = place_ref[0]
    total = place_ref[1]
    query = jnp.where(col < sizes.top, col, lax.shift_right_arithmetic(col - sizes.top, 4))
    left_at = sizes.rows + RIGHT_ROWS
    mem_at = left_at + LEFT_ROWS
    spot = jnp.where(key < left_at, key, key - mem_at)
    mem_seg = jnp.where(key < mem_at + sizes.segs, key - mem_at, key - mem_at - 2 * sizes.segs)
    key_seg = jnp.where(key < mem_at, lax.shift_right_arithmetic(spot, 4), mem_seg)
    near = (
        (key_seg == query)
        | ((spot >= query * SEG_LEN - LEFT_LEN) & (spot < query * SEG_LEN))
        | ((key_seg == query + 1) & (spot < query * SEG_LEN + SEG_LEN + RIGHT_LEN))
    )
    recent = (key_seg >= query - MEM_LEN) & (key_seg < query) & (col >= sizes.top)
    allowed = ((key < mem_at) & near) | ((key >= mem_at) & recent)
    key_abs = key_seg + base
    query_abs = query + base
    allowed = allowed & (key_abs >= 0) & (key_abs < total)
    if sizes.top:
        allowed = allowed & ((col < sizes.segs) | (col >= sizes.top))
    for n in range(seqs):
        key_owner = jnp.zeros(shape, jnp.int32)
        query_owner = jnp.zeros(shape, jnp.int32)
        for u in range(starts_ref.shape[1]):
            first = starts_ref[n, u]
            key_owner = key_owner + (key_abs >= first).astype(jnp.int32)
            query_owner = query_owner + (query_abs >= first).astype(jnp.int32)
        mask_ref[n] = jnp.where(allowed & (key_owner == query_owner), 0.0, -1e30)


def half_masks():
    lane = lax.broadcasted_iota(jnp.int32, (1, LANES), 1)
    even = (lane < LANES // 2).astype(F32)
    return even.astype(BF16), (1.0 - even).astype(BF16), lane < LANES // 2


def project(sizes, z_ref, qkv_ref, row_bias_ref, proj_ref):
    step = CHIPS_Z // 2
    for c in range(2):
        block = qkv_ref[pl.ds(c * step, step)].reshape(-1, sizes.width)
        wide = block.shape[0]
        made = nt(z_ref[...], block) + row_bias_ref[:, pl.ds(c * wide, wide)]
        proj_ref[:, pl.ds(c * wide, wide)] = made.astype(BF16)


def attend(sizes, seqs, proj_ref, mask_ref, probs_ref, att_ref):
    even, odd, is_even = half_masks()
    scale = (sizes.width // HEADS) ** (-0.5)
    count = sizes.queries

    def body(p, carry):
        for n in range(seqs):
            lane = pl.multiple_of(p * LANES, LANES)
            query = proj_ref[pl.ds(n * sizes.ext, count), pl.ds(lane, LANES)]
            first = n * sizes.ext + sizes.top
            key = proj_ref[pl.ds(first, sizes.keys), pl.ds(sizes.width + lane, LANES)]
            value = proj_ref[pl.ds(first, sizes.keys), pl.ds(2 * sizes.width + lane, LANES)]
            queries = jnp.concatenate([query * even, query * odd], axis=0)
            scores = nt(key, queries) * scale + mask_ref[n]
            scores = jnp.exp(scores - jnp.max(scores, axis=0, keepdims=True))
            probs = (scores * (1.0 / jnp.sum(scores, axis=0, keepdims=True))).astype(BF16)
            probs_ref[n * sizes.pairs + p] = probs
            out = tn(probs, value)
            att_ref[pl.ds(n * count, count), pl.ds(lane, LANES)] = jnp.where(
                is_even, out[:count], out[count:]
            ).astype(BF16)
        return carry

    lax.fori_loop(0, sizes.pairs, body, 0, unroll=True)


def attend_back(sizes, seqs, proj_ref, probs_ref, go_ref, gproj_ref):
    even, odd, is_even = half_masks()
    scale = (sizes.width // HEADS) ** (-0.5)
    count = sizes.queries
    wide = sizes.width
    for n in range(seqs):
        base = n * sizes.ext
        rest = sizes.ext - count
        gproj_ref[pl.ds(base + count, rest), pl.ds(0, wide)] = jnp.zeros((rest, wide), BF16)
        if sizes.top:
            gproj_ref[pl.ds(base, sizes.top), pl.ds(wide, 2 * wide)] = jnp.zeros(
                (sizes.top, 2 * wide), BF16
            )

    def body(p, carry):
        for n in range(seqs):
            lane = pl.multiple_of(p * LANES, LANES)
            base = n * sizes.ext
            first = base + sizes.top
            query = proj_ref[pl.ds(base, count), pl.ds(lane, LANES)]
            key = proj_ref[pl.ds(first, sizes.keys), pl.ds(wide + lane, LANES)]
            value = proj_ref[pl.ds(first, sizes.keys), pl.ds(2 * wide + lane, LANES)]
            grad = go_ref[pl.ds(n * count, count), pl.ds(lane, LANES)]
            queries = jnp.concatenate([query * even, query * odd], axis=0)
            grads = jnp.concatenate([grad * even, grad * odd], axis=0)
            probs_low = probs_ref[n * sizes.pairs + p]
            grad_values = nn(probs_low, grads)
            probs = probs_low.astype(F32)
            weighted = nt(value, grads) * probs
            grad_scores = (
                (weighted - probs * jnp.sum(weighted, axis=0, keepdims=True)) * scale
            ).astype(BF16)
            grad_keys = nn(grad_scores, queries)
            grad_both = tn(grad_scores, key)
            grad_query = jnp.where(is_even, grad_both[:count], grad_both[count:])
            gproj_ref[pl.ds(base, count), pl.ds(lane, LANES)] = grad_query.astype(BF16)
            gproj_ref[pl.ds(first, sizes.keys), pl.ds(wide + lane, LANES)] = grad_keys.astype(BF16)
            gproj_ref[pl.ds(first, sizes.keys), pl.ds(2 * wide + lane, LANES)] = (
                grad_values.astype(BF16)
            )
        return carry

    lax.fori_loop(0, sizes.pairs, body, 0)


def gelu_both(upward):
    half = 0.5 * (1.0 + lax.erf(upward * ROOT_HALF))
    slope = half + upward * jnp.exp(-0.5 * upward * upward) * INV_ROOT_TWO_PI
    return upward * half, slope


def up_block(up_ref, c, wide):
    step = wide // (up_ref.shape[1] * up_ref.shape[2])
    return up_ref[pl.ds(c * step, step)].reshape(-1, up_ref.shape[3])


def down_block(down_ref, c, wide):
    at = pl.multiple_of(c * wide, wide)
    return down_ref[:, :, :, pl.ds(at, wide)].reshape(-1, wide)


def ffn_back_step(
    sizes, c, wide, grad_low, hidden_low, active, slope, up_ref, down_ref, gup_ref, gdown_ref, vec
):
    at = pl.multiple_of(c * wide, wide)
    up = up_block(up_ref, c, wide)
    down = down_block(down_ref, c, wide)
    grad_active = nn(grad_low, down)
    grad_up_f = grad_active * slope
    grad_up = grad_up_f.astype(BF16)
    gdown_ref[:, :, :, pl.ds(at, wide)] = (
        tn(grad_low, active).astype(BF16).reshape(gdown_ref.shape[:3] + (wide,))
    )
    step = wide // (gup_ref.shape[1] * gup_ref.shape[2])
    gup_ref[pl.ds(c * step, step)] = (
        tn(grad_up, hidden_low).astype(BF16).reshape((step,) + gup_ref.shape[1:])
    )
    vec[pl.ds(8 + c, 1), :] = col_sum(grad_up.astype(F32))
    return nn(grad_up, up)


def attn_back_stage(
    sizes, seqs, gz, grad_mem_ref, att_ref, proj_ref, probs_ref, z_ref, qkv_ref, out_ref,
    gqkv_ref, gout_ref, go_ref, gproj_ref, branch_ref, vec, gh_ref, gmem_ref, back_left_ref,
    back_right_ref, scaled_rows=None,
):
    wide = sizes.width
    count = sizes.queries
    bias_out = col_sum(gz)
    for n in range(seqs):
        if sizes.top:
            mem_grad = grad_mem_ref[pl.ds(n * sizes.segs, sizes.segs), :]
            bias_out = bias_out + col_sum(mem_grad)
            branch_ref[pl.ds(n * count, sizes.top), :] = jnp.concatenate(
                [mem_grad, jnp.zeros((sizes.top - sizes.segs, wide), F32)], axis=0
            ).astype(BF16)
        branch_ref[pl.ds(n * count + sizes.top, sizes.rows), :] = gz[
            n * sizes.rows : (n + 1) * sizes.rows
        ].astype(BF16)
    vec[pl.ds(5, 1), :] = bias_out
    branch = branch_ref[...]
    gout_ref[...] = tn(branch, att_ref[...]).astype(BF16).reshape(gout_ref.shape)
    go_ref[...] = nn(branch, out_ref[...].reshape(-1, wide)).astype(BF16)
    attend_back(sizes, seqs, proj_ref, probs_ref, go_ref, gproj_ref)
    vec[pl.ds(3, 1), :] = col_sum(gproj_ref[:, pl.ds(0, wide)].astype(F32))
    vec[pl.ds(4, 1), :] = col_sum(gproj_ref[:, pl.ds(2 * wide, wide)].astype(F32))
    grad_ext = nn(gproj_ref[...], qkv_ref[...].reshape(-1, wide))
    gain_sum = jnp.zeros((1, wide), F32)
    bias_sum = jnp.zeros((1, wide), F32)
    for n in range(seqs):
        base = n * sizes.ext
        own = grad_ext[base + sizes.top : base + sizes.top + sizes.rows]
        if sizes.top:
            spread = grad_ext[base : base + sizes.segs] * (1.0 / SEG_LEN)
            own = own + segment_spread(sizes.rows, wide, spread)
        gh_ref[pl.ds(n * sizes.rows, sizes.rows), :] = own
        mem = base + sizes.mem_at
        gmem_ref[pl.ds(n * sizes.segs, sizes.segs), :] = grad_ext[mem : mem + sizes.segs]
        left = base + sizes.left_at
        back_left_ref[n] = grad_ext[left : left + BACK_ROWS].astype(BF16)
        right = base + sizes.right_at
        back_right_ref[n] = grad_ext[right : right + RIGHT_ROWS].astype(BF16)
        if scaled_rows is not None:
            grads = (
                own,
                grad_ext[right : right + RIGHT_ROWS],
                grad_ext[left : left + LEFT_ROWS],
            )
            for rows, scaled in zip(grads, scaled_rows(n)):
                gain_sum = gain_sum + col_sum(rows * scaled)
                bias_sum = bias_sum + col_sum(rows)
    if scaled_rows is not None:
        vec[pl.ds(0, 1), :] = gain_sum
        vec[pl.ds(2, 1), :] = bias_sum
    step = CHIPS_Z // 2
    part = gqkv_ref.shape[1] * gqkv_ref.shape[2] * step
    for c in range(2):
        gqkv_ref[pl.ds(c * step, step)] = (
            tn(gproj_ref[:, pl.ds(c * part, part)], z_ref[...])
            .astype(BF16)
            .reshape((step,) + gqkv_ref.shape[1:])
        )


def merge_halo(sizes, n, gh_ref, gmem_ref, from_right_ref, from_left_ref):
    first = n * sizes.rows
    back = from_right_ref[n].astype(F32)
    head = gh_ref[pl.ds(first, RIGHT_ROWS), :] + from_left_ref[n].astype(F32)
    middle = gh_ref[pl.ds(first + RIGHT_ROWS, sizes.rows - RIGHT_ROWS - LEFT_ROWS), :]
    tail = gh_ref[pl.ds(first + sizes.rows - LEFT_ROWS, LEFT_ROWS), :] + back[:LEFT_ROWS]
    mem = gmem_ref[pl.ds(n * sizes.segs, sizes.segs), :] + back[LEFT_ROWS + sizes.segs :]
    return jnp.concatenate([head, middle, tail], axis=0), mem


def pack_kernel(spots, qkv_ref, out_ref, up_ref, down_ref, *packed):
    eye = identity(LANES)
    high, wide, low = qkv_ref.shape[1], out_ref.shape[1], down_ref.shape[1]
    for layer, ref in enumerate(packed):
        up = tn(up_ref[layer], eye).astype(BF16)
        for z in range(ref.shape[0]):
            ref[z, pl.ds(spots.qkv[1], high), :] = qkv_ref[layer]
            ref[z, pl.ds(spots.out[1], wide), :] = out_ref[layer]
            ref[z, pl.ds(spots.up[1], up_ref.shape[2]), :] = up
            for part, (_, first) in enumerate(spots.down):
                ref[z, pl.ds(first, low), :] = down_ref[layer, :, pl.ds(part * LANES, LANES)]


def unpack_layer(spots, sources, refs):
    qkv_ref, out_ref, up_ref, down_ref = refs
    high, wide, low = qkv_ref.shape[0], out_ref.shape[0], down_ref.shape[0]

    def total(first, rows):
        parts = [ref[z, pl.ds(first, rows), :] for ref in sources for z in range(ref.shape[0])]
        value = parts[0].astype(F32)
        for part in parts[1:]:
            value = value + part.astype(F32)
        return value

    qkv_ref[...] = total(spots.qkv[1], high)
    out_ref[...] = total(spots.out[1], wide)
    up_ref[...] = nt(identity(LANES), total(spots.up[1], up_ref.shape[1]).astype(BF16))
    for part, (_, first) in enumerate(spots.down):
        down_ref[:, pl.ds(part * LANES, LANES)] = total(first, low)
    return total


def store_layer(layer, held, outs, sems):
    copies = [
        pltpu.make_async_copy(ref, out.at[layer], sems.at[i])
        for i, (ref, out) in enumerate(zip(held, outs))
    ]
    for copy in copies:
        copy.start()
    return copies


def unpack_last_kernel(spots, layer, lines_ref, first_ref, *refs):
    outs, held, sems = refs[:4], refs[4:8], refs[8]
    unpack_layer(spots, (lines_ref, first_ref), held)
    wait_all(store_layer(layer, held, outs, sems))


def unpack_first_kernel(spots, small_at, parts_ref, *refs):
    outs, (gains_ref, biases_ref, ffn_bias_ref), held, sems = (
        refs[4:8], refs[8:11], refs[11:15], refs[15],
    )
    total = unpack_layer(spots, (parts_ref,), held)
    copies = store_layer(0, held, outs, sems)
    sums = total(small_at, SMALL_ROWS)
    parts = gains_ref.shape[2] // LANES
    for layer in range(gains_ref.shape[0]):
        for part in range(parts):
            lanes = pl.ds(part * LANES, LANES)
            at = (part * gains_ref.shape[0] + layer) * VEC_ROWS
            block = sums[at : at + VEC_ROWS]
            gains_ref[layer, :, lanes] = block[0:2]
            for row in range(biases_ref.shape[0]):
                biases_ref[row, pl.ds(layer, 1), lanes] = block[2 + row : 3 + row]
            for row in range(ffn_bias_ref.shape[1] // gains_ref.shape[2]):
                at = row * gains_ref.shape[2] + part * LANES
                ffn_bias_ref[pl.ds(layer, 1), pl.ds(at, LANES)] = block[8 + row : 9 + row]
    wait_all(copies)


def first_layer_kernel(
    sizes, seqs, mats, spots, count_in, place_ref, starts_ref, frames_ref, left_ref, right_ref,
    gains_ref, biases_ref, ffn_bias_ref, row_bias_ref, *refs
):
    groups = in_groups(spots, refs[:count_in])
    (
        z_ref, proj_ref, probs_ref, att_ref, mixed_ref, mem_ref, next_ref, active_ref, slope_ref,
        low_ref, send_right_ref, send_left_ref, qkv_ref, out_ref, up_ref, down_ref, mask_ref,
        hidden_ref, sems,
    ) = refs[count_in:]
    wide = sizes.width
    copies = start_in(attn_pairs(mats, spots, groups, qkv_ref, out_ref, place_ref), sems, 0)
    ffn_copies = start_in(
        ffn_pairs(mats, spots, groups, up_ref, down_ref, place_ref), sems, len(copies)
    )
    gain = gains_ref[0, pl.ds(0, 1), :]
    bias = biases_ref[0, pl.ds(0, 1), :]
    pad = jnp.zeros((TILE - sizes.segs, wide), F32)
    for n in range(seqs):
        own = frames_ref[n].astype(F32)
        before = left_ref[n].astype(F32)
        hidden = norm_forward(own, gain, bias)[0]
        halo = norm_forward(before[before.shape[0] - LEFT_ROWS :], gain, bias)[0]
        after = norm_forward(right_ref[n].astype(F32), gain, bias)[0]
        memory = jnp.concatenate(
            [
                segment_mean(own),
                jnp.zeros((sizes.segs - before.shape[0] // SEG_LEN, wide), F32),
                segment_mean(before),
            ],
            axis=0,
        )
        base = n * sizes.ext
        z_ref[pl.ds(base, sizes.top), :] = jnp.concatenate(
            [segment_mean(hidden), pad], axis=0
        ).astype(BF16)
        z_ref[pl.ds(base + sizes.top, sizes.rows), :] = hidden.astype(BF16)
        z_ref[pl.ds(base + sizes.right_at, RIGHT_ROWS), :] = after.astype(BF16)
        z_ref[pl.ds(base + sizes.left_at, LEFT_ROWS), :] = halo.astype(BF16)
        z_ref[pl.ds(base + sizes.mem_at, MEM_ROWS), :] = memory.astype(BF16)
    fill_mask(sizes, seqs, starts_ref, place_ref, mask_ref)
    wait_all(copies)
    project(sizes, z_ref, qkv_ref, row_bias_ref, proj_ref)
    attend(sizes, seqs, proj_ref, mask_ref, probs_ref, att_ref)
    mixed = nt(att_ref[...], out_ref[...].reshape(-1, wide)) + biases_ref[3, pl.ds(0, 1), :]
    for n in range(seqs):
        base = n * sizes.queries
        mem_ref[pl.ds(n * sizes.segs, sizes.segs), :] = mixed[base : base + sizes.segs]
        mixed_ref[pl.ds(n * sizes.rows, sizes.rows), :] = (
            frames_ref[n].astype(F32) + mixed[base + sizes.top : base + sizes.top + sizes.rows]
        )
    mixed = mixed_ref[...]
    hidden, _, _ = norm_forward(mixed, gains_ref[0, pl.ds(1, 1), :], biases_ref[4, pl.ds(0, 1), :])
    hidden_ref[...] = hidden.astype(BF16)
    next_ref[...] = mixed + biases_ref[5, pl.ds(0, 1), :]
    wait_all(ffn_copies)

    def body(c, carry):
        at_lane = pl.multiple_of(c * wide, wide)
        upward = nt(hidden_ref[...], up_block(up_ref, c, wide))
        upward = upward + ffn_bias_ref[pl.ds(0, 1), pl.ds(at_lane, wide)]
        active, slope = gelu_both(upward)
        active = active.astype(BF16)
        active_ref[:, pl.ds(at_lane, wide)] = active
        slope_ref[:, pl.ds(at_lane, wide)] = slope.astype(BF16)
        next_ref[...] += nt(active, down_block(down_ref, c, wide))
        return carry

    lax.fori_loop(0, sizes.ff // wide, body, 0)
    low, _, _ = norm_forward(
        next_ref[...], gains_ref[1, pl.ds(0, 1), :], biases_ref[0, pl.ds(1, 1), :]
    )
    low = low.astype(BF16)
    low_ref[...] = low
    for n in range(seqs):
        base = n * sizes.rows
        send_right_ref[n, pl.ds(0, LEFT_ROWS), :] = low[
            base + sizes.rows - LEFT_ROWS : base + sizes.rows
        ]
        send_right_ref[n, pl.ds(LEFT_ROWS, MEM_ROWS), :] = jnp.concatenate(
            [
                mem_ref[pl.ds(n * sizes.segs, sizes.segs), :],
                jnp.zeros((MEM_ROWS - sizes.segs, wide), F32),
            ],
            axis=0,
        ).astype(BF16)
        send_left_ref[n] = low[base : base + RIGHT_ROWS]


def last_layer_kernel(
    sizes, seqs, mats, spots, count_in, count_out, place_ref, starts_ref, low_ref, left_ref,
    right_ref, mem_ref, inputs_ref, out_grad_ref, gains_ref, biases_ref, ffn_bias_ref,
    row_bias_ref, *refs
):
    groups = in_groups(spots, refs[:count_in])
    (encoded_ref, gz_ref, gh_ref, gmem_ref, back_left_ref, back_right_ref, vec) = refs[
        count_in : count_in + 7
    ]
    hbm_out = refs[count_in + 7 : count_in + 7 + count_out]
    (
        qkv_ref, out_ref, up_ref, down_ref, gqkv_ref, gout_ref, gup_ref, gdown_ref, mask_ref,
        z_ref, proj_ref, probs_ref, att_ref, hidden_ref, go_ref, gproj_ref, branch_ref,
        grad_low_ref, grad_hidden_ref, sems,
    ) = refs[count_in + 7 + count_out :]
    outs_to = hbm_out
    if spots is not None:
        rows = mats.attn_rows + mats.ffn_rows
        outs_to = [
            [ref.at[:, pl.ds(hop1 * rows, rows), :] for ref in hbm_out for hop1 in range(2)]
        ]
    wide = sizes.width
    attn_copies = start_in(attn_pairs(mats, spots, groups, qkv_ref, out_ref, place_ref), sems, 0)
    ffn_copies = start_in(
        ffn_pairs(mats, spots, groups, up_ref, down_ref, place_ref), sems, len(attn_copies)
    )
    vec[...] = jnp.zeros_like(vec)
    for n in range(seqs):
        base = n * sizes.ext
        z_ref[pl.ds(base, sizes.rows), :] = low_ref[pl.ds(n * sizes.rows, sizes.rows), :]
        z_ref[pl.ds(base + sizes.right_at, RIGHT_ROWS), :] = right_ref[n]
        z_ref[pl.ds(base + sizes.left_at, LEFT_ROWS), :] = left_ref[n, pl.ds(0, LEFT_ROWS), :]
        memory = jnp.concatenate(
            [
                mem_ref[pl.ds(n * sizes.segs, sizes.segs), :],
                left_ref[n, pl.ds(LEFT_ROWS, MEM_ROWS), :].astype(F32)[: sizes.segs],
            ],
            axis=0,
        )
        z_ref[pl.ds(base + sizes.mem_at, MEM_ROWS), :] = memory.astype(BF16)
        grad_low_ref[pl.ds(n * sizes.rows, sizes.rows), :] = out_grad_ref[n]
    fill_mask(sizes, seqs, starts_ref, place_ref, mask_ref)
    wait_all(attn_copies)
    project(sizes, z_ref, qkv_ref, row_bias_ref, proj_ref)
    attend(sizes, seqs, proj_ref, mask_ref, probs_ref, att_ref)
    mixed = (
        inputs_ref[...]
        + nt(att_ref[...], out_ref[...].reshape(-1, wide))
        + biases_ref[3, pl.ds(1, 1), :]
    )
    gain = gains_ref[1, pl.ds(1, 1), :]
    hidden, scaled, inverse = norm_forward(mixed, gain, biases_ref[4, pl.ds(1, 1), :])
    hidden_ref[...] = hidden.astype(BF16)
    for n in range(seqs):
        encoded_ref[n] = mixed[n * sizes.rows : (n + 1) * sizes.rows] + biases_ref[5, pl.ds(1, 1), :]
    grad_hidden_ref[...] = jnp.zeros_like(grad_hidden_ref)
    wait_all(ffn_copies)

    def body(c, carry):
        at_lane = pl.multiple_of(c * wide, wide)
        upward = nt(hidden_ref[...], up_block(up_ref, c, wide))
        upward = upward + ffn_bias_ref[pl.ds(1, 1), pl.ds(at_lane, wide)]
        active, slope = gelu_both(upward)
        active = active.astype(BF16)
        made = nt(active, down_block(down_ref, c, wide))
        for n in range(seqs):
            encoded_ref[n] += made[n * sizes.rows : (n + 1) * sizes.rows]
        grad_hidden_ref[...] += ffn_back_step(
            sizes, c, wide, grad_low_ref[...], hidden_ref[...], active, slope, up_ref, down_ref,
            gup_ref, gdown_ref, vec,
        )
        return carry

    lax.fori_loop(0, sizes.ff // wide, body, 0)
    out_at = len(attn_copies) + len(ffn_copies)
    outs = start_out(
        ffn_pairs(mats, spots, outs_to, gup_ref, gdown_ref, place_ref), sems, out_at
    )
    grad = grad_low_ref[...].astype(F32)
    grad_hidden = grad_hidden_ref[...]
    vec[pl.ds(1, 1), :] = col_sum(grad_hidden * scaled)
    vec[pl.ds(6, 1), :] = col_sum(grad_hidden)
    vec[pl.ds(7, 1), :] = col_sum(grad)
    gz = grad + norm_backward(grad_hidden, scaled, inverse, gain)
    gz_ref[...] = gz
    attn_back_stage(
        sizes, seqs, gz, None, att_ref, proj_ref, probs_ref, z_ref, qkv_ref, out_ref, gqkv_ref,
        gout_ref, go_ref, gproj_ref, branch_ref, vec, gh_ref, gmem_ref, back_left_ref,
        back_right_ref,
    )
    outs = outs + start_out(
        attn_pairs(mats, spots, outs_to, gqkv_ref, gout_ref, place_ref),
        sems,
        out_at + len(outs),
    )
    wait_all(outs)


def first_back_kernel(
    last, sizes, seqs, mats, spots, count_in, count_out, place_ref, inputs_ref, gz_in_ref,
    gh_in_ref, gmem_in_ref, from_right_ref, from_left_ref, mixed_ref, active_ref, slope_ref,
    att_ref, probs_ref, proj_ref, z_ref, frames_ref, left_ref, right_ref, gains_ref, biases_ref,
    last_vec, *refs
):
    groups = in_groups(spots, refs[:count_in])
    gz_ref, gh_ref, gmem_ref, back_left_ref, back_right_ref, upper_vec, vec = refs[
        count_in : count_in + 7
    ]
    refs = refs[count_in + 7 :]
    hbm_out = refs[:count_out]
    (
        qkv_ref, out_ref, up_ref, down_ref, gqkv_ref, gout_ref, gup_ref, gdown_ref, hidden_ref,
        grad_low_ref, grad_ref, grad_hidden_ref, grad_mem_ref, go_ref, gproj_ref, branch_ref,
        small_ref, sems,
    ) = refs[count_out:]
    wide = sizes.width
    small = []
    outs_to = hbm_out
    if spots is not None:
        rows = mats.attn_rows + mats.ffn_rows
        end = CHIPS_Z * rows
        each = [
            ref.at[hop2, hop1] for ref in hbm_out for hop2 in range(2) for hop1 in range(2)
        ]
        small = [ref.at[pl.ds(end, SMALL_ROWS), :] for ref in each]
        outs_to = [[ref.at[pl.ds(0, end), :].reshape(CHIPS_Z, rows, LANES) for ref in each]]
    ffn_copies = start_in(ffn_pairs(mats, spots, groups, up_ref, down_ref, place_ref), sems, 0)
    attn_copies = start_in(
        attn_pairs(mats, spots, groups, qkv_ref, out_ref, place_ref), sems, len(ffn_copies)
    )
    vec[...] = jnp.zeros_like(vec)
    upper_vec[...] = jnp.zeros_like(upper_vec)
    gain = gains_ref[1, pl.ds(0, 1), :]
    gain_sum = jnp.zeros((1, wide), F32)
    bias_sum = jnp.zeros((1, wide), F32)
    for n in range(seqs):
        rows = pl.ds(n * sizes.rows, sizes.rows)
        _, scaled, inverse = norm_forward(
            inputs_ref[rows, :], gain, biases_ref[0, pl.ds(1, 1), :]
        )
        total, mem = merge_halo(last, n, gh_in_ref, gmem_in_ref, from_right_ref, from_left_ref)
        gain_sum = gain_sum + col_sum(total * scaled)
        bias_sum = bias_sum + col_sum(total)
        grad = gz_in_ref[rows, :] + norm_backward(total, scaled, inverse, gain)
        grad_ref[rows, :] = grad
        grad_low_ref[rows, :] = grad.astype(BF16)
        grad_mem_ref[pl.ds(n * sizes.segs, sizes.segs), :] = mem
    upper_vec[pl.ds(0, 1), :] = gain_sum
    upper_vec[pl.ds(2, 1), :] = bias_sum
    gain = gains_ref[0, pl.ds(1, 1), :]
    hidden, scaled, inverse = norm_forward(
        mixed_ref[...], gain, biases_ref[4, pl.ds(0, 1), :]
    )
    hidden_ref[...] = hidden.astype(BF16)
    grad_hidden_ref[...] = jnp.zeros_like(grad_hidden_ref)
    wait_all(ffn_copies)

    def body(c, carry):
        at_lane = pl.multiple_of(c * wide, wide)
        grad_hidden_ref[...] += ffn_back_step(
            sizes, c, wide, grad_low_ref[...], hidden_ref[...],
            active_ref[:, pl.ds(at_lane, wide)], slope_ref[:, pl.ds(at_lane, wide)].astype(F32),
            up_ref, down_ref, gup_ref, gdown_ref, vec,
        )
        return carry

    lax.fori_loop(0, sizes.ff // wide, body, 0)
    out_at = len(ffn_copies) + len(attn_copies)
    outs = start_out(
        ffn_pairs(mats, spots, outs_to, gup_ref, gdown_ref, place_ref), sems, out_at
    )
    grad_hidden = grad_hidden_ref[...]
    grad = grad_ref[...]
    vec[pl.ds(1, 1), :] = col_sum(grad_hidden * scaled)
    vec[pl.ds(6, 1), :] = col_sum(grad_hidden)
    vec[pl.ds(7, 1), :] = col_sum(grad)
    gz = grad + norm_backward(grad_hidden, scaled, inverse, gain)
    gz_ref[...] = gz

    def scaled_rows(n):
        before = left_ref[n, pl.ds(left_ref.shape[1] - LEFT_ROWS, LEFT_ROWS), :]
        parts = (frames_ref[n], right_ref[n], before)
        first_gain = gains_ref[0, pl.ds(0, 1), :]
        first_bias = biases_ref[0, pl.ds(0, 1), :]
        return [norm_forward(part.astype(F32), first_gain, first_bias)[1] for part in parts]

    wait_all(attn_copies)
    attn_back_stage(
        sizes, seqs, gz, grad_mem_ref, att_ref, proj_ref, probs_ref, z_ref, qkv_ref, out_ref,
        gqkv_ref, gout_ref, go_ref, gproj_ref, branch_ref, vec, gh_ref, gmem_ref, back_left_ref,
        back_right_ref, scaled_rows,
    )
    outs = outs + start_out(
        attn_pairs(mats, spots, outs_to, gqkv_ref, gout_ref, place_ref),
        sems,
        out_at + len(outs),
    )
    totals = vec[...], last_vec[...] + upper_vec[...]
    small_ref[...] = jnp.concatenate(
        [
            total[:VEC_ROWS, part * LANES : (part + 1) * LANES]
            for part in range(sizes.pairs)
            for total in totals
        ],
        axis=0,
    ).astype(BF16)
    outs = outs + start_out([(ref, small_ref) for ref in small], sems, out_at + len(outs))
    wait_all(outs)


def frames_grad_kernel(
    sizes, seqs, frames_ref, gz_ref, gh_ref, gmem_ref, from_right_ref, from_left_ref, gains_ref,
    biases_ref, grad_ref
):
    gain = gains_ref[0, pl.ds(0, 1), :]
    for n in range(seqs):
        _, scaled, inverse = norm_forward(
            frames_ref[n].astype(F32), gain, biases_ref[0, pl.ds(0, 1), :]
        )
        total, mem = merge_halo(sizes, n, gh_ref, gmem_ref, from_right_ref, from_left_ref)
        grad_ref[n] = (
            gz_ref[pl.ds(n * sizes.rows, sizes.rows), :]
            + norm_backward(total, scaled, inverse, gain)
            + segment_spread(sizes.rows, sizes.width, mem * (1.0 / SEG_LEN))
        )


def shifted(value, axis, by):
    size = lax.axis_size(axis)
    return lax.ppermute(value, axis, [(i, (i + by) % size) for i in range(size)])


def permuted(value, move):
    reps = lax.axis_size("rep")
    pairs = []
    for flat in range(lax.axis_size("seg") * reps):
        seg, rep = divmod(flat, reps)
        z, y, x, core = move(seg // CHIPS_Y, seg % CHIPS_Y, rep // 2, rep % 2)
        pairs.append((flat, (z * CHIPS_Y + y) * reps + 2 * x + core))
    return lax.ppermute(value, ("seg", "rep"), pairs)


def across_first(value):
    return permuted(value, lambda z, y, x, c: (z, y, x ^ 1, c) if c == 0 else (z, y ^ 1, x, c))


def across_second(value):
    return permuted(value, lambda z, y, x, c: (z, y ^ 1, x, c) if c == 0 else (z, y, x ^ 1, c))


def other_core(value):
    return permuted(value, lambda z, y, x, c: (z, y, x, c ^ 1))


def after(value, *others):
    return lax.optimization_barrier((value,) + others)[0]


def swap_z(blocks):
    groups = [
        [z * CHIPS_Y + y for z in range(CHIPS_Z)] for y in range(CHIPS_Y)
    ]
    return lax.all_to_all(blocks, "seg", 0, 0, axis_index_groups=groups, tiled=True)


def gather_sides(here):
    return [here, across_first(here), across_second(here)]


def both_cores(blocks):
    return blocks + [other_core(block) for block in blocks]


def summed(*parts):
    total = parts[0].astype(F32)
    for part in parts[1:]:
        total = total + part.astype(F32)
    return total.astype(BF16)


def sum_everywhere(value):
    count = lax.axis_size("seg") * lax.axis_size("rep")
    bit = 1
    while bit < count:
        value = value + lax.ppermute(value, ("seg", "rep"), [(i, i ^ bit) for i in range(count)])
        bit *= 2
    return value


def vmem_spec():
    return pl.BlockSpec(memory_space=pltpu.VMEM)


def smem_spec():
    return pl.BlockSpec(memory_space=pltpu.SMEM)


def hbm_spec():
    return pl.BlockSpec(memory_space=pl.ANY)


def call(body, in_specs, out_shapes, out_specs, scratch, args, flops=0, moved=0, grid=(), aliases={}, vmem=12):
    return pl.pallas_call(
        body,
        grid=grid,
        input_output_aliases=aliases,
        in_specs=in_specs,
        out_shape=tuple(jax.ShapeDtypeStruct(shape, kind) for shape, kind in out_shapes),
        out_specs=tuple(out_specs),
        scratch_shapes=scratch,
        compiler_params=pltpu.CompilerParams(vmem_limit_bytes=vmem * MIB),
        cost_estimate=pl.CostEstimate(flops=flops, bytes_accessed=moved, transcendentals=0),
    )(*args)


def on_device(
    frames,
    utt_segments,
    out_grad,
    qkv_weight,
    out_weight,
    ffn_in_weight,
    ffn_out_weight,
    norm_gains,
    biases,
    ffn_bias,
):
    micros, groups, rows, width = frames.shape
    seqs = micros * groups
    ff = ffn_bias.shape[1]
    reps = lax.axis_size("rep")
    seg_count = lax.axis_size("seg")
    mats = Matrices(width, ff)
    by_blocks = width // reps == LANES and reps == 4 and seg_count == BLOCKS
    first = Sizes(rows, width, ff, True)
    last = Sizes(rows, width, ff, False)
    own = seqs * rows
    mem_own = seqs * first.segs

    seg_at = lax.axis_index("seg")
    seg_base = seg_at * first.segs
    rep_at = lax.axis_index("rep")
    place = [seg_base, jnp.int32(first.segs * seg_count)]
    y_at, x_at, core_at = seg_at % CHIPS_Y, rep_at // 2, rep_at % 2
    for other in range(2):
        core = lax.bitwise_xor(core_at, other)
        for hop2 in range(2):
            for hop1 in range(2):
                x_hop = jnp.where(core == 0, hop1, hop2)
                y_hop = jnp.where(core == 0, hop2, hop1)
                place.append(lax.bitwise_xor(y_at, y_hop))
                place.append((lax.bitwise_xor(x_at, x_hop) * 2 + core) * LANES)
    place = jnp.stack([jnp.asarray(entry, jnp.int32) for entry in place])
    lengths = utt_segments.reshape(seqs, utt_segments.shape[2])
    starts = (jnp.cumsum(lengths, axis=1) - lengths).astype(jnp.int32)
    zero_bias = jnp.zeros((1, width), F32)
    row_biases = [
        jnp.concatenate([biases[l : l + 1, 1], zero_bias, biases[l : l + 1, 2]], axis=1)
        for l in range(LAYERS)
    ]
    biases_by_row = jnp.swapaxes(biases, 0, 1)

    frames_own = frames.reshape(seqs, rows, width)
    grads_own = out_grad.reshape(seqs, rows, width)
    far = MEM_LEN * SEG_LEN
    frames_left = shifted(frames_own[:, rows - far :], "seg", 1)
    frames_right = shifted(frames_own[:, :RIGHT_ROWS], "seg", -1)

    attn_rows, ffn_rows = mats.attn_rows, mats.ffn_rows
    if by_blocks:
        qkv_t, out_t, down_t = (
            jnp.swapaxes(member, 1, 2) for member in (qkv_weight, out_weight, ffn_out_weight)
        )
        all_rows = attn_rows + ffn_rows
        spots = Spots(mats)
        shards = call(
            lambda *refs: pack_kernel(spots, *refs),
            [vmem_spec()] * 4,
            [((CHIPS_Z, all_rows, LANES), BF16)] * LAYERS,
            [vmem_spec()] * LAYERS,
            [],
            (qkv_t, out_t, ffn_in_weight, down_t),
            vmem=56,
        )
        sides0 = gather_sides(after(swap_z(shards[0]), frames_left, frames_right))
        place, starts, row_biases, sent = lax.optimization_barrier(
            (place, starts, row_biases, after(shards[1], sides0[0]))
        )
        sides1 = gather_sides(swap_z(sent))
        first_all = both_cores(sides0 + [across_second(after(sides0[1], sides1[0]))])
        classes = len(first_all) // 2
        grad_outs0 = [((2, 2, CHIPS_Z * all_rows + SMALL_ROWS, LANES), BF16)] * 2
        grad_outs1 = [((CHIPS_Z, 2 * all_rows, LANES), BF16)] * 4
        copies_in = len(first_all) * (3 + mats.down_parts)
    else:
        whole = []
        for member, shape in zip(
            (qkv_weight, out_weight, ffn_in_weight, ffn_out_weight),
            (mats.qkv, mats.out, mats.up, mats.down),
        ):
            member = lax.all_gather(member, "rep", axis=1, tiled=True)
            member = lax.all_gather(member, "seg", axis=2, tiled=True)
            whole.append(jnp.swapaxes(member, 1, 2).reshape((LAYERS,) + shape))
        first_all = [member[0] for member in whole]
        last_all = [member[1] for member in whole]
        spots = None
        grad_outs0 = grad_outs1 = [
            (shape, BF16) for shape in (mats.qkv, mats.out, mats.up, mats.down)
        ]
        copies_in = 4
    dma = pltpu.SemaphoreType.DMA

    matrices = [pltpu.VMEM(shape, BF16) for shape in (mats.qkv, mats.out, mats.up, mats.down)]

    (
        z0, proj0, probs0, att0, mixed0, mem1, x1, active0, slope0, low1, send_right, send_left,
    ) = call(
        lambda *refs: first_layer_kernel(
            first, seqs, mats, spots, len(first_all), *refs
        ),
        [smem_spec()] * 2 + [vmem_spec()] * 7 + [hbm_spec()] * len(first_all),
        [
            ((seqs * first.ext, width), BF16),
            ((seqs * first.ext, 3 * width), BF16),
            ((seqs * first.pairs, first.keys, 2 * first.queries), BF16),
            ((seqs * first.queries, width), BF16),
            ((own, width), F32),
            ((mem_own, width), F32),
            ((own, width), F32),
            ((own, ff), BF16),
            ((own, ff), BF16),
            ((own, width), BF16),
            ((seqs, BACK_ROWS, width), BF16),
            ((seqs, RIGHT_ROWS, width), BF16),
        ],
        [vmem_spec()] * 12,
        matrices
        + [
            pltpu.VMEM((seqs, first.keys, 2 * first.queries), F32),
            pltpu.VMEM((own, width), BF16),
            dma((copies_in,)),
        ],
        (place, starts, frames_own, frames_left, frames_right, norm_gains, biases_by_row, ffn_bias,
         row_biases[0]) + tuple(first_all),
        flops=24 * own * (4 * width * width + 2 * width * ff) // 2,
        moved=2 * (4 * width * width + 2 * width * ff),
        vmem=20,
    )
    left1 = shifted(send_right, "seg", 1)
    right1 = shifted(send_left, "seg", -1)
    if by_blocks:
        last_side = across_second(after(sides1[1], sides1[2], left1, right1))
        last_all = both_cores(sides1 + [last_side])

    vec_shape = (TILE, width)
    outs = call(
        lambda *refs: last_layer_kernel(
            last, seqs, mats, spots, len(last_all), len(grad_outs1), *refs
        ),
        [smem_spec()] * 2 + [vmem_spec()] * 10 + [hbm_spec()] * len(last_all),
        [
            ((seqs, rows, width), F32),
            ((own, width), F32),
            ((own, width), F32),
            ((mem_own, width), F32),
            ((seqs, BACK_ROWS, width), BF16),
            ((seqs, RIGHT_ROWS, width), BF16),
            (vec_shape, F32),
        ]
        + grad_outs1,
        [vmem_spec()] * 7 + [hbm_spec()] * len(grad_outs1),
        matrices
        + matrices
        + [
            pltpu.VMEM((seqs, last.keys, 2 * last.queries), F32),
            pltpu.VMEM((seqs * last.ext, width), BF16),
            pltpu.VMEM((seqs * last.ext, 3 * width), BF16),
            pltpu.VMEM((seqs * last.pairs, last.keys, 2 * last.queries), BF16),
            pltpu.VMEM((seqs * last.queries, width), BF16),
            pltpu.VMEM((own, width), BF16),
            pltpu.VMEM((seqs * last.queries, width), BF16),
            pltpu.VMEM((seqs * last.ext, 3 * width), BF16),
            pltpu.VMEM((seqs * last.queries, width), BF16),
            pltpu.VMEM((own, width), BF16),
            pltpu.VMEM((own, width), F32),
            dma((2 * copies_in,)),
        ],
        (place, starts, low1, left1, right1, mem1, x1, grads_own, norm_gains, biases_by_row, ffn_bias,
         row_biases[1]) + tuple(last_all),
        flops=30 * own * (4 * width * width + 2 * width * ff),
        moved=4 * (4 * width * width + 2 * width * ff),
        vmem=26,
    )
    encoded, gz1, gh1, gmem1, back_left1, back_right1, vec1 = outs[:7]
    grad_blocks1 = outs[7:]
    from_right1 = shifted(back_left1, "seg", -1)
    from_left1 = shifted(back_right1, "seg", 1)

    gh1_tied = gh1
    if by_blocks:
        near1, far1, near1_other, far1_other = grad_blocks1
        far1 = summed(far1, other_core(far1_other))
        near1_theirs = other_core(near1_other)
        gh1_tied = after(gh1, far1, near1_theirs)
    gz0, gh0, gmem0, back_left0, back_right0, upper_vec, vec0, *grad_blocks0 = call(
        lambda *refs: first_back_kernel(
            last, first, seqs, mats, spots, len(first_all), len(grad_outs0), *refs
        ),
        [smem_spec()] + [vmem_spec()] * 19 + [hbm_spec()] * len(first_all),
        [
            ((own, width), F32),
            ((own, width), F32),
            ((mem_own, width), F32),
            ((seqs, BACK_ROWS, width), BF16),
            ((seqs, RIGHT_ROWS, width), BF16),
            (vec_shape, F32),
            (vec_shape, F32),
        ]
        + grad_outs0,
        [vmem_spec()] * 7 + [hbm_spec()] * len(grad_outs0),
        matrices
        + matrices
        + [
            pltpu.VMEM((own, width), BF16),
            pltpu.VMEM((own, width), BF16),
            pltpu.VMEM((own, width), F32),
            pltpu.VMEM((own, width), F32),
            pltpu.VMEM((mem_own, width), F32),
            pltpu.VMEM((seqs * first.queries, width), BF16),
            pltpu.VMEM((seqs * first.ext, 3 * width), BF16),
            pltpu.VMEM((seqs * first.queries, width), BF16),
            pltpu.VMEM((SMALL_ROWS, LANES), BF16),
            dma((2 * copies_in + 8,)),
        ],
        (place, x1, gz1, gh1_tied, gmem1, from_right1, from_left1, mixed0, active0, slope0, att0,
         probs0, proj0, z0, frames_own, frames_left, frames_right, norm_gains, biases_by_row, vec1)
        + tuple(first_all),
        flops=28 * own * (4 * width * width + 2 * width * ff),
        moved=4 * (4 * width * width + 2 * width * ff),
        vmem=28,
    )
    from_right0 = shifted(back_left0, "seg", -1)
    from_left0 = shifted(back_right0, "seg", 1)
    gz0_last = gz0
    if by_blocks:
        second1 = across_second(far1)
        mine0, theirs0 = grad_blocks0[0], other_core(after(grad_blocks0[1], second1))
        both1 = summed(near1, near1_theirs, second1)
        lines1 = swap_z(both1)
        far0 = summed(mine0[1], after(theirs0, both1)[1])
        far0 = after(far0, from_right0, from_left0)
        second0 = across_second(far0)
        mid0 = summed(mine0[0, 1], theirs0[0, 1], second0[1])
        first0 = across_first(mid0)
        held0 = summed(mine0[0, 0], theirs0[0, 0], after(second0, mid0)[0])
        near0 = summed(held0, first0)
        blocks = CHIPS_Z * all_rows
        near0 = jnp.concatenate(
            [
                near0[:blocks].reshape(CHIPS_Z, all_rows, LANES),
                jnp.broadcast_to(near0[None, blocks:], (CHIPS_Z, SMALL_ROWS, LANES)),
            ],
            axis=1,
        )
        first_parts = swap_z(near0)
        gz0_last, lines1 = lax.optimization_barrier((after(gz0, near0), lines1))
        cross1 = jnp.sum(lines1[:, all_rows:].astype(F32), axis=0, keepdims=True).astype(BF16)
        first1 = across_first(cross1)
    frames_grad = call(
        lambda *refs: frames_grad_kernel(first, seqs, *refs),
        [vmem_spec()] * 8,
        [((seqs, rows, width), F32)],
        [vmem_spec()],
        [],
        (frames_own, gz0_last, gh0, gmem0, from_right0, from_left0, norm_gains, biases_by_row),
    )[0]

    if by_blocks:
        shapes = [member.shape for member in (qkv_t, out_t, ffn_in_weight, down_t)]
        held = [pltpu.VMEM(shape[1:], F32) for shape in shapes]
        whole = [(shape, F32) for shape in shapes]
        written = call(
            lambda *refs: unpack_last_kernel(spots, LAYERS - 1, *refs),
            [
                pl.BlockSpec((CHIPS_Z, all_rows, LANES), lambda i: (0, 0, 0)),
                pl.BlockSpec((1, all_rows, LANES), lambda i: (0, 0, 0)),
            ],
            whole,
            [hbm_spec()] * 4,
            held + [dma((4,))],
            [lines1, first1],
            grid=(1,),
        )
        small_shapes = [norm_gains.shape, (biases.shape[1], LAYERS, width), ffn_bias.shape]
        reduced = call(
            lambda *refs: unpack_first_kernel(spots, all_rows, *refs),
            [vmem_spec()] + [hbm_spec()] * 4,
            whole + [(shape, F32) for shape in small_shapes],
            [hbm_spec()] * 4 + [vmem_spec()] * 3,
            held + [dma((4,))],
            [after(first_parts, frames_grad)] + list(written),
            aliases={1 + i: i for i in range(4)},
        )
        small = reduced[4], jnp.swapaxes(reduced[5], 0, 1), reduced[6]
        reduced = [
            jnp.swapaxes(reduced[0], 1, 2),
            jnp.swapaxes(reduced[1], 1, 2),
            reduced[2],
            jnp.swapaxes(reduced[3], 1, 2),
        ]
    else:
        reduced = []
        for member0, member1 in zip(grad_blocks0, grad_blocks1):
            both = jnp.stack([member0, member1]).reshape(LAYERS, -1, member0.shape[3])
            both = jnp.swapaxes(both, 1, 2)
            both = lax.psum_scatter(both, "seg", scatter_dimension=2, tiled=True)
            both = lax.psum_scatter(both, "rep", scatter_dimension=1, tiled=True)
            reduced.append(both.astype(F32))
        small = sum_everywhere(jnp.stack([vec0, vec1 + upper_vec]))
        small = small[:, 0:2], small[:, 2:8], small[:, 8:12].reshape(ffn_bias.shape)

    return (
        encoded.reshape(frames.shape),
        frames_grad.reshape(frames.shape),
        reduced[0],
        reduced[1],
        reduced[2],
        reduced[3],
        small[0],
        small[1],
        small[2],
    )


def solution(mesh):
    in_specs = (
        P(None, "rep", "seg", None),
        P(None, "rep", None),
        P(None, "rep", "seg", None),
        P(None, "rep", "seg"),
        P(None, "rep", "seg"),
        P(None, "rep", "seg"),
        P(None, "rep", "seg"),
        P(),
        P(),
        P(),
    )
    out_specs = (
        P(None, "rep", "seg", None),
        P(None, "rep", "seg", None),
        P(None, "rep", "seg"),
        P(None, "rep", "seg"),
        P(None, "rep", "seg"),
        P(None, "rep", "seg"),
        P(),
        P(),
        P(),
    )
    return jax.shard_map(
        on_device, mesh=mesh, in_specs=in_specs, out_specs=out_specs, check_vma=False
    )
```

```python
import jax
import jax.numpy as jnp
from jax import lax
from jax.experimental import pallas as pl
from jax.experimental.pallas import tpu as pltpu
from jax.sharding import PartitionSpec as P

HEADS = 8
SEG_LEN = 16
LEFT_LEN = 30
RIGHT_LEN = 4
MEM_LEN = 4
LAYERS = 2

EPS = 1e-05
ROOT_HALF = 0.7071067811865476
INV_ROOT_TWO_PI = 0.3989422804014327

LANES = 128
TILE = 16
RIGHT_ROWS = 16
LEFT_ROWS = 32
MEM_ROWS = 16
BACK_ROWS = LEFT_ROWS + MEM_ROWS
CHIPS_Z = 4
CHIPS_Y = 2
BLOCKS = CHIPS_Z * CHIPS_Y
VEC_ROWS = 12
SMALL_ROWS = 96
MIB = 1024 * 1024

BF16 = jnp.bfloat16
F32 = jnp.float32


def nn(a, b):
    return lax.dot_general(a, b, (((1,), (0,)), ((), ())), preferred_element_type=F32)


def nt(a, b):
    return lax.dot_general(a, b, (((1,), (1,)), ((), ())), preferred_element_type=F32)


def tn(a, b):
    return lax.dot_general(a, b, (((0,), (0,)), ((), ())), preferred_element_type=F32)


def col_sum(value):
    return jnp.sum(value, axis=0, keepdims=True)


def norm_forward(inputs, gain, bias):
    center = inputs - jnp.mean(inputs, axis=1, keepdims=True)
    inverse = lax.rsqrt(jnp.mean(center * center, axis=1, keepdims=True) + EPS)
    scaled = center * inverse
    return scaled * gain + bias, scaled, inverse


def norm_backward(grad_in, scaled, inverse, gain):
    grad_scaled = grad_in * gain
    return inverse * (
        grad_scaled
        - jnp.mean(grad_scaled, axis=1, keepdims=True)
        - scaled * jnp.mean(grad_scaled * scaled, axis=1, keepdims=True)
    )


def segment_mean(inputs):
    rows, width = inputs.shape
    return jnp.mean(inputs.reshape(rows // SEG_LEN, SEG_LEN, width), axis=1)


def segment_spread(rows, width, per_segment):
    segs = rows // SEG_LEN
    return jnp.broadcast_to(per_segment[:, None, :], (segs, SEG_LEN, width)).reshape(rows, width)


def identity(size):
    row = lax.broadcasted_iota(jnp.int32, (size, size), 0)
    col = lax.broadcasted_iota(jnp.int32, (size, size), 1)
    return (row == col).astype(F32).astype(BF16)


class Sizes:
    def __init__(self, rows, width, ff, with_summary):
        self.rows = rows
        self.width = width
        self.ff = ff
        self.segs = rows // SEG_LEN
        self.top = TILE if with_summary else 0
        self.keys = rows + RIGHT_ROWS + LEFT_ROWS + MEM_ROWS
        self.ext = self.top + self.keys
        self.queries = self.top + rows
        self.right_at = self.top + rows
        self.left_at = self.right_at + RIGHT_ROWS
        self.mem_at = self.left_at + LEFT_ROWS
        self.pairs = width // LANES


class Matrices:
    def __init__(self, width, ff):
        self.qkv = (CHIPS_Z, CHIPS_Y, 3 * width // BLOCKS, width)
        self.out = (CHIPS_Z, CHIPS_Y, width // BLOCKS, width)
        self.up = (CHIPS_Z, CHIPS_Y, ff // BLOCKS, width)
        self.down = (CHIPS_Z, CHIPS_Y, width // BLOCKS, ff)
        self.down_parts = ff // width
        self.attn_rows = self.qkv[2] + self.out[2]
        self.ffn_rows = self.up[2] + self.down_parts * self.down[2]


class Spots:
    def __init__(self, mats):
        high, wide, up, low = mats.qkv[2], mats.out[2], mats.up[2], mats.down[2]
        self.qkv = (0, 0)
        self.out = (0, high)
        self.up = (0, high + wide)
        self.down = [(0, high + wide + up + low * part) for part in range(mats.down_parts)]


def attn_pairs(mats, spots, groups, qkv_ref, out_ref, place_ref):
    if spots is None:
        return [(groups[0], qkv_ref), (groups[1], out_ref)]
    pairs = []
    for k in range(len(groups[0])):
        row = place_ref[2 + 2 * k]
        lane = pl.multiple_of(place_ref[3 + 2 * k], LANES)
        for (group, first), ref, shape in (
            (spots.qkv, qkv_ref, mats.qkv),
            (spots.out, out_ref, mats.out),
        ):
            block = groups[group][k]
            pairs.append(
                (
                    block.at[:, pl.ds(first, shape[2]), :],
                    ref.at[:, row, :, pl.ds(lane, LANES)],
                )
            )
    return pairs


def ffn_pairs(mats, spots, groups, up_ref, down_ref, place_ref):
    if spots is None:
        return [(groups[2], up_ref), (groups[3], down_ref)]
    pairs = []
    for k in range(len(groups[0])):
        row = place_ref[2 + 2 * k]
        lane = pl.multiple_of(place_ref[3 + 2 * k], LANES)
        group, first = spots.up
        block = groups[group][k]
        pairs.append(
            (block.at[:, pl.ds(first, mats.up[2]), :], up_ref.at[:, row, :, pl.ds(lane, LANES)])
        )
        for part, (group, first) in enumerate(spots.down):
            there = pl.multiple_of(
                place_ref[3 + 2 * k] * mats.down_parts + part * LANES, LANES
            )
            block = groups[group][k]
            pairs.append(
                (
                    block.at[:, pl.ds(first, mats.down[2]), :],
                    down_ref.at[:, row, :, pl.ds(there, LANES)],
                )
            )
    return pairs


def start_in(pairs, sems, at):
    copies = [pltpu.make_async_copy(s, d, sems.at[at + i]) for i, (s, d) in enumerate(pairs)]
    for copy in copies:
        copy.start()
    return copies


def start_out(pairs, sems, at):
    copies = [pltpu.make_async_copy(d, s, sems.at[at + i]) for i, (s, d) in enumerate(pairs)]
    for copy in copies:
        copy.start()
    return copies


def in_groups(spots, refs):
    return refs if spots is None else [refs]


def wait_all(copies):
    for copy in copies:
        copy.wait()


def fill_mask(sizes, seqs, starts_ref, place_ref, mask_ref):
    shape = (sizes.keys, 2 * sizes.queries)
    key = lax.broadcasted_iota(jnp.int32, shape, 0)
    col = lax.broadcasted_iota(jnp.int32, shape, 1)
    col = jnp.where(col < sizes.queries, col, col - sizes.queries)
    base = place_ref[0]
    total = place_ref[1]
    query = jnp.where(col < sizes.top, col, lax.shift_right_arithmetic(col - sizes.top, 4))
    left_at = sizes.rows + RIGHT_ROWS
    mem_at = left_at + LEFT_ROWS
    spot = jnp.where(key < left_at, key, key - mem_at)
    mem_seg = jnp.where(key < mem_at + sizes.segs, key - mem_at, key - mem_at - 2 * sizes.segs)
    key_seg = jnp.where(key < mem_at, lax.shift_right_arithmetic(spot, 4), mem_seg)
    near = (
        (key_seg == query)
        | ((spot >= query * SEG_LEN - LEFT_LEN) & (spot < query * SEG_LEN))
        | ((key_seg == query + 1) & (spot < query * SEG_LEN + SEG_LEN + RIGHT_LEN))
    )
    recent = (key_seg >= query - MEM_LEN) & (key_seg < query) & (col >= sizes.top)
    allowed = ((key < mem_at) & near) | ((key >= mem_at) & recent)
    key_abs = key_seg + base
    query_abs = query + base
    allowed = allowed & (key_abs >= 0) & (key_abs < total)
    if sizes.top:
        allowed = allowed & ((col < sizes.segs) | (col >= sizes.top))
    for n in range(seqs):
        key_owner = jnp.zeros(shape, jnp.int32)
        query_owner = jnp.zeros(shape, jnp.int32)
        for u in range(starts_ref.shape[1]):
            first = starts_ref[n, u]
            key_owner = key_owner + (key_abs >= first).astype(jnp.int32)
            query_owner = query_owner + (query_abs >= first).astype(jnp.int32)
        mask_ref[n] = jnp.where(allowed & (key_owner == query_owner), 0.0, -1e30)


def half_masks():
    lane = lax.broadcasted_iota(jnp.int32, (1, LANES), 1)
    even = (lane < LANES // 2).astype(F32)
    return even.astype(BF16), (1.0 - even).astype(BF16), lane < LANES // 2


def project(sizes, z_ref, qkv_ref, row_bias_ref, proj_ref):
    step = CHIPS_Z // 2
    for c in range(2):
        block = qkv_ref[pl.ds(c * step, step)].reshape(-1, sizes.width)
        wide = block.shape[0]
        made = nt(z_ref[...], block) + row_bias_ref[:, pl.ds(c * wide, wide)]
        proj_ref[:, pl.ds(c * wide, wide)] = made.astype(BF16)


def attend(sizes, seqs, proj_ref, mask_ref, probs_ref, att_ref):
    even, odd, is_even = half_masks()
    scale = (sizes.width // HEADS) ** (-0.5)
    count = sizes.queries

    def body(p, carry):
        for n in range(seqs):
            lane = pl.multiple_of(p * LANES, LANES)
            query = proj_ref[pl.ds(n * sizes.ext, count), pl.ds(lane, LANES)]
            first = n * sizes.ext + sizes.top
            key = proj_ref[pl.ds(first, sizes.keys), pl.ds(sizes.width + lane, LANES)]
            value = proj_ref[pl.ds(first, sizes.keys), pl.ds(2 * sizes.width + lane, LANES)]
            queries = jnp.concatenate([query * even, query * odd], axis=0)
            scores = nt(key, queries) * scale + mask_ref[n]
            scores = jnp.exp(scores - jnp.max(scores, axis=0, keepdims=True))
            probs = (scores * (1.0 / jnp.sum(scores, axis=0, keepdims=True))).astype(BF16)
            probs_ref[n * sizes.pairs + p] = probs
            out = tn(probs, value)
            att_ref[pl.ds(n * count, count), pl.ds(lane, LANES)] = jnp.where(
                is_even, out[:count], out[count:]
            ).astype(BF16)
        return carry

    lax.fori_loop(0, sizes.pairs, body, 0, unroll=True)


def attend_back(sizes, seqs, proj_ref, probs_ref, go_ref, gproj_ref):
    even, odd, is_even = half_masks()
    scale = (sizes.width // HEADS) ** (-0.5)
    count = sizes.queries
    wide = sizes.width
    for n in range(seqs):
        base = n * sizes.ext
        rest = sizes.ext - count
        gproj_ref[pl.ds(base + count, rest), pl.ds(0, wide)] = jnp.zeros((rest, wide), BF16)
        if sizes.top:
            gproj_ref[pl.ds(base, sizes.top), pl.ds(wide, 2 * wide)] = jnp.zeros(
                (sizes.top, 2 * wide), BF16
            )

    def body(p, carry):
        for n in range(seqs):
            lane = pl.multiple_of(p * LANES, LANES)
            base = n * sizes.ext
            first = base + sizes.top
            query = proj_ref[pl.ds(base, count), pl.ds(lane, LANES)]
            key = proj_ref[pl.ds(first, sizes.keys), pl.ds(wide + lane, LANES)]
            value = proj_ref[pl.ds(first, sizes.keys), pl.ds(2 * wide + lane, LANES)]
            grad = go_ref[pl.ds(n * count, count), pl.ds(lane, LANES)]
            queries = jnp.concatenate([query * even, query * odd], axis=0)
            grads = jnp.concatenate([grad * even, grad * odd], axis=0)
            probs_low = probs_ref[n * sizes.pairs + p]
            grad_values = nn(probs_low, grads)
            probs = probs_low.astype(F32)
            weighted = nt(value, grads) * probs
            grad_scores = (
                (weighted - probs * jnp.sum(weighted, axis=0, keepdims=True)) * scale
            ).astype(BF16)
            grad_keys = nn(grad_scores, queries)
            grad_both = tn(grad_scores, key)
            grad_query = jnp.where(is_even, grad_both[:count], grad_both[count:])
            gproj_ref[pl.ds(base, count), pl.ds(lane, LANES)] = grad_query.astype(BF16)
            gproj_ref[pl.ds(first, sizes.keys), pl.ds(wide + lane, LANES)] = grad_keys.astype(BF16)
            gproj_ref[pl.ds(first, sizes.keys), pl.ds(2 * wide + lane, LANES)] = (
                grad_values.astype(BF16)
            )
        return carry

    lax.fori_loop(0, sizes.pairs, body, 0, unroll=sizes.pairs if sizes.top == 0 else 1)


def gelu_both(upward):
    half = 0.5 * (1.0 + lax.erf(upward * ROOT_HALF))
    slope = half + upward * jnp.exp(-0.5 * upward * upward) * INV_ROOT_TWO_PI
    return upward * half, slope


def up_block(up_ref, c, wide):
    step = wide // (up_ref.shape[1] * up_ref.shape[2])
    return up_ref[pl.ds(c * step, step)].reshape(-1, up_ref.shape[3])


def down_block(down_ref, c, wide):
    at = pl.multiple_of(c * wide, wide)
    return down_ref[:, :, :, pl.ds(at, wide)].reshape(-1, wide)


def ffn_back_step(
    sizes, c, wide, grad_low, hidden_low, active, slope, up_ref, down_ref, gup_ref, gdown_ref, vec
):
    at = pl.multiple_of(c * wide, wide)
    up = up_block(up_ref, c, wide)
    down = down_block(down_ref, c, wide)
    grad_active = nn(grad_low, down)
    grad_up_f = grad_active * slope
    grad_up = grad_up_f.astype(BF16)
    gdown_ref[:, :, :, pl.ds(at, wide)] = (
        tn(grad_low, active).astype(BF16).reshape(gdown_ref.shape[:3] + (wide,))
    )
    step = wide // (gup_ref.shape[1] * gup_ref.shape[2])
    gup_ref[pl.ds(c * step, step)] = (
        tn(grad_up, hidden_low).astype(BF16).reshape((step,) + gup_ref.shape[1:])
    )
    vec[pl.ds(8 + c, 1), :] = col_sum(grad_up.astype(F32))
    return nn(grad_up, up)


def attn_back_stage(
    sizes, seqs, gz, grad_mem_ref, att_ref, proj_ref, probs_ref, z_ref, qkv_ref, out_ref,
    gqkv_ref, gout_ref, go_ref, gproj_ref, branch_ref, vec, gh_ref, gmem_ref, back_left_ref,
    back_right_ref, scaled_rows=None,
):
    wide = sizes.width
    count = sizes.queries
    bias_out = col_sum(gz)
    for n in range(seqs):
        if sizes.top:
            mem_grad = grad_mem_ref[pl.ds(n * sizes.segs, sizes.segs), :]
            bias_out = bias_out + col_sum(mem_grad)
            branch_ref[pl.ds(n * count, sizes.top), :] = jnp.concatenate(
                [mem_grad, jnp.zeros((sizes.top - sizes.segs, wide), F32)], axis=0
            ).astype(BF16)
        branch_ref[pl.ds(n * count + sizes.top, sizes.rows), :] = gz[
            n * sizes.rows : (n + 1) * sizes.rows
        ].astype(BF16)
    vec[pl.ds(5, 1), :] = bias_out
    branch = branch_ref[...]
    gout_ref[...] = tn(branch, att_ref[...]).astype(BF16).reshape(gout_ref.shape)
    go_ref[...] = nn(branch, out_ref[...].reshape(-1, wide)).astype(BF16)
    attend_back(sizes, seqs, proj_ref, probs_ref, go_ref, gproj_ref)
    vec[pl.ds(3, 1), :] = col_sum(gproj_ref[:, pl.ds(0, wide)].astype(F32))
    vec[pl.ds(4, 1), :] = col_sum(gproj_ref[:, pl.ds(2 * wide, wide)].astype(F32))
    grad_ext = nn(gproj_ref[...], qkv_ref[...].reshape(-1, wide))
    gain_sum = jnp.zeros((1, wide), F32)
    bias_sum = jnp.zeros((1, wide), F32)
    for n in range(seqs):
        base = n * sizes.ext
        own = grad_ext[base + sizes.top : base + sizes.top + sizes.rows]
        if sizes.top:
            spread = grad_ext[base : base + sizes.segs] * (1.0 / SEG_LEN)
            own = own + segment_spread(sizes.rows, wide, spread)
        gh_ref[pl.ds(n * sizes.rows, sizes.rows), :] = own
        mem = base + sizes.mem_at
        gmem_ref[pl.ds(n * sizes.segs, sizes.segs), :] = grad_ext[mem : mem + sizes.segs]
        left = base + sizes.left_at
        back_left_ref[n] = grad_ext[left : left + BACK_ROWS].astype(BF16)
        right = base + sizes.right_at
        back_right_ref[n] = grad_ext[right : right + RIGHT_ROWS].astype(BF16)
        if scaled_rows is not None:
            grads = (
                own,
                grad_ext[right : right + RIGHT_ROWS],
                grad_ext[left : left + LEFT_ROWS],
            )
            for rows, scaled in zip(grads, scaled_rows(n)):
                gain_sum = gain_sum + col_sum(rows * scaled)
                bias_sum = bias_sum + col_sum(rows)
    if scaled_rows is not None:
        vec[pl.ds(0, 1), :] = gain_sum
        vec[pl.ds(2, 1), :] = bias_sum
    step = CHIPS_Z // 2
    part = gqkv_ref.shape[1] * gqkv_ref.shape[2] * step
    for c in range(2):
        gqkv_ref[pl.ds(c * step, step)] = (
            tn(gproj_ref[:, pl.ds(c * part, part)], z_ref[...])
            .astype(BF16)
            .reshape((step,) + gqkv_ref.shape[1:])
        )


def merge_halo(sizes, n, gh_ref, gmem_ref, from_right_ref, from_left_ref):
    first = n * sizes.rows
    back = from_right_ref[n].astype(F32)
    head = gh_ref[pl.ds(first, RIGHT_ROWS), :] + from_left_ref[n].astype(F32)
    middle = gh_ref[pl.ds(first + RIGHT_ROWS, sizes.rows - RIGHT_ROWS - LEFT_ROWS), :]
    tail = gh_ref[pl.ds(first + sizes.rows - LEFT_ROWS, LEFT_ROWS), :] + back[:LEFT_ROWS]
    mem = gmem_ref[pl.ds(n * sizes.segs, sizes.segs), :] + back[LEFT_ROWS + sizes.segs :]
    return jnp.concatenate([head, middle, tail], axis=0), mem


def pack_kernel(spots, qkv_ref, out_ref, up_ref, down_ref, *packed):
    eye = identity(LANES)
    high, wide, low = qkv_ref.shape[1], out_ref.shape[1], down_ref.shape[1]
    for layer, ref in enumerate(packed):
        up = tn(up_ref[layer], eye).astype(BF16)
        for z in range(ref.shape[0]):
            ref[z, pl.ds(spots.qkv[1], high), :] = qkv_ref[layer]
            ref[z, pl.ds(spots.out[1], wide), :] = out_ref[layer]
            ref[z, pl.ds(spots.up[1], up_ref.shape[2]), :] = up
            for part, (_, first) in enumerate(spots.down):
                ref[z, pl.ds(first, low), :] = down_ref[layer, :, pl.ds(part * LANES, LANES)]


def unpack_layer(spots, sources, refs):
    qkv_ref, out_ref, up_ref, down_ref = refs
    high, wide, low = qkv_ref.shape[0], out_ref.shape[0], down_ref.shape[0]

    def total(first, rows):
        parts = [ref[z, pl.ds(first, rows), :] for ref in sources for z in range(ref.shape[0])]
        value = parts[0].astype(F32)
        for part in parts[1:]:
            value = value + part.astype(F32)
        return value

    qkv_ref[...] = total(spots.qkv[1], high)
    out_ref[...] = total(spots.out[1], wide)
    up_ref[...] = nt(identity(LANES), total(spots.up[1], up_ref.shape[1]).astype(BF16))
    for part, (_, first) in enumerate(spots.down):
        down_ref[:, pl.ds(part * LANES, LANES)] = total(first, low)
    return total


def store_layer(layer, held, outs, sems):
    copies = [
        pltpu.make_async_copy(ref, out.at[layer], sems.at[i])
        for i, (ref, out) in enumerate(zip(held, outs))
    ]
    for copy in copies:
        copy.start()
    return copies


def unpack_last_kernel(spots, layer, lines_ref, first_ref, *refs):
    outs, held, sems = refs[:4], refs[4:8], refs[8]
    unpack_layer(spots, (lines_ref, first_ref), held)
    wait_all(store_layer(layer, held, outs, sems))


def unpack_first_kernel(spots, small_at, parts_ref, *refs):
    outs, (gains_ref, biases_ref, ffn_bias_ref), held, sems = (
        refs[4:8], refs[8:11], refs[11:15], refs[15],
    )
    total = unpack_layer(spots, (parts_ref,), held)
    copies = store_layer(0, held, outs, sems)
    sums = total(small_at, SMALL_ROWS)
    parts = gains_ref.shape[2] // LANES
    for layer in range(gains_ref.shape[0]):
        for part in range(parts):
            lanes = pl.ds(part * LANES, LANES)
            at = (part * gains_ref.shape[0] + layer) * VEC_ROWS
            block = sums[at : at + VEC_ROWS]
            gains_ref[layer, :, lanes] = block[0:2]
            for row in range(biases_ref.shape[0]):
                biases_ref[row, pl.ds(layer, 1), lanes] = block[2 + row : 3 + row]
            for row in range(ffn_bias_ref.shape[1] // gains_ref.shape[2]):
                at = row * gains_ref.shape[2] + part * LANES
                ffn_bias_ref[pl.ds(layer, 1), pl.ds(at, LANES)] = block[8 + row : 9 + row]
    wait_all(copies)


def first_layer_kernel(
    sizes, seqs, mats, spots, count_in, place_ref, starts_ref, frames_ref, left_ref, right_ref,
    gains_ref, biases_ref, ffn_bias_ref, row_bias_ref, *refs
):
    groups = in_groups(spots, refs[:count_in])
    (
        z_ref, proj_ref, probs_ref, att_ref, mixed_ref, mem_ref, next_ref, active_ref, slope_ref,
        low_ref, send_right_ref, send_left_ref, qkv_ref, out_ref, up_ref, down_ref, mask_ref,
        hidden_ref, sems,
    ) = refs[count_in:]
    wide = sizes.width
    copies = start_in(attn_pairs(mats, spots, groups, qkv_ref, out_ref, place_ref), sems, 0)
    ffn_copies = start_in(
        ffn_pairs(mats, spots, groups, up_ref, down_ref, place_ref), sems, len(copies)
    )
    gain = gains_ref[0, pl.ds(0, 1), :]
    bias = biases_ref[0, pl.ds(0, 1), :]
    pad = jnp.zeros((TILE - sizes.segs, wide), F32)
    for n in range(seqs):
        own = frames_ref[n].astype(F32)
        before = left_ref[n].astype(F32)
        hidden = norm_forward(own, gain, bias)[0]
        halo = norm_forward(before[before.shape[0] - LEFT_ROWS :], gain, bias)[0]
        after = norm_forward(right_ref[n].astype(F32), gain, bias)[0]
        memory = jnp.concatenate(
            [
                segment_mean(own),
                jnp.zeros((sizes.segs - before.shape[0] // SEG_LEN, wide), F32),
                segment_mean(before),
            ],
            axis=0,
        )
        base = n * sizes.ext
        z_ref[pl.ds(base, sizes.top), :] = jnp.concatenate(
            [segment_mean(hidden), pad], axis=0
        ).astype(BF16)
        z_ref[pl.ds(base + sizes.top, sizes.rows), :] = hidden.astype(BF16)
        z_ref[pl.ds(base + sizes.right_at, RIGHT_ROWS), :] = after.astype(BF16)
        z_ref[pl.ds(base + sizes.left_at, LEFT_ROWS), :] = halo.astype(BF16)
        z_ref[pl.ds(base + sizes.mem_at, MEM_ROWS), :] = memory.astype(BF16)
    fill_mask(sizes, seqs, starts_ref, place_ref, mask_ref)
    wait_all(copies)
    project(sizes, z_ref, qkv_ref, row_bias_ref, proj_ref)
    attend(sizes, seqs, proj_ref, mask_ref, probs_ref, att_ref)
    mixed = nt(att_ref[...], out_ref[...].reshape(-1, wide)) + biases_ref[3, pl.ds(0, 1), :]
    for n in range(seqs):
        base = n * sizes.queries
        mem_ref[pl.ds(n * sizes.segs, sizes.segs), :] = mixed[base : base + sizes.segs]
        mixed_ref[pl.ds(n * sizes.rows, sizes.rows), :] = (
            frames_ref[n].astype(F32) + mixed[base + sizes.top : base + sizes.top + sizes.rows]
        )
    mixed = mixed_ref[...]
    hidden, _, _ = norm_forward(mixed, gains_ref[0, pl.ds(1, 1), :], biases_ref[4, pl.ds(0, 1), :])
    hidden_ref[...] = hidden.astype(BF16)
    next_ref[...] = mixed + biases_ref[5, pl.ds(0, 1), :]
    wait_all(ffn_copies)

    def body(c, carry):
        at_lane = pl.multiple_of(c * wide, wide)
        upward = nt(hidden_ref[...], up_block(up_ref, c, wide))
        upward = upward + ffn_bias_ref[pl.ds(0, 1), pl.ds(at_lane, wide)]
        active, slope = gelu_both(upward)
        active = active.astype(BF16)
        active_ref[:, pl.ds(at_lane, wide)] = active
        slope_ref[:, pl.ds(at_lane, wide)] = slope.astype(BF16)
        next_ref[...] += nt(active, down_block(down_ref, c, wide))
        return carry

    lax.fori_loop(0, sizes.ff // wide, body, 0)
    low, _, _ = norm_forward(
        next_ref[...], gains_ref[1, pl.ds(0, 1), :], biases_ref[0, pl.ds(1, 1), :]
    )
    low = low.astype(BF16)
    low_ref[...] = low
    for n in range(seqs):
        base = n * sizes.rows
        send_right_ref[n, pl.ds(0, LEFT_ROWS), :] = low[
            base + sizes.rows - LEFT_ROWS : base + sizes.rows
        ]
        send_right_ref[n, pl.ds(LEFT_ROWS, MEM_ROWS), :] = jnp.concatenate(
            [
                mem_ref[pl.ds(n * sizes.segs, sizes.segs), :],
                jnp.zeros((MEM_ROWS - sizes.segs, wide), F32),
            ],
            axis=0,
        ).astype(BF16)
        send_left_ref[n] = low[base : base + RIGHT_ROWS]


def last_layer_kernel(
    sizes, seqs, mats, spots, count_in, count_out, place_ref, starts_ref, low_ref, left_ref,
    right_ref, mem_ref, inputs_ref, out_grad_ref, gains_ref, biases_ref, ffn_bias_ref,
    row_bias_ref, *refs
):
    groups = in_groups(spots, refs[:count_in])
    (encoded_ref, gz_ref, gh_ref, gmem_ref, back_left_ref, back_right_ref, vec) = refs[
        count_in : count_in + 7
    ]
    hbm_out = refs[count_in + 7 : count_in + 7 + count_out]
    (
        qkv_ref, out_ref, up_ref, down_ref, gqkv_ref, gout_ref, gup_ref, gdown_ref, mask_ref,
        z_ref, proj_ref, probs_ref, att_ref, hidden_ref, go_ref, gproj_ref, branch_ref,
        grad_low_ref, grad_hidden_ref, sems,
    ) = refs[count_in + 7 + count_out :]
    outs_to = hbm_out
    if spots is not None:
        rows = mats.attn_rows + mats.ffn_rows
        outs_to = [
            [ref.at[:, pl.ds(hop1 * rows, rows), :] for ref in hbm_out for hop1 in range(2)]
        ]
    wide = sizes.width
    attn_copies = start_in(attn_pairs(mats, spots, groups, qkv_ref, out_ref, place_ref), sems, 0)
    ffn_copies = start_in(
        ffn_pairs(mats, spots, groups, up_ref, down_ref, place_ref), sems, len(attn_copies)
    )
    vec[...] = jnp.zeros_like(vec)
    for n in range(seqs):
        base = n * sizes.ext
        z_ref[pl.ds(base, sizes.rows), :] = low_ref[pl.ds(n * sizes.rows, sizes.rows), :]
        z_ref[pl.ds(base + sizes.right_at, RIGHT_ROWS), :] = right_ref[n]
        z_ref[pl.ds(base + sizes.left_at, LEFT_ROWS), :] = left_ref[n, pl.ds(0, LEFT_ROWS), :]
        memory = jnp.concatenate(
            [
                mem_ref[pl.ds(n * sizes.segs, sizes.segs), :],
                left_ref[n, pl.ds(LEFT_ROWS, MEM_ROWS), :].astype(F32)[: sizes.segs],
            ],
            axis=0,
        )
        z_ref[pl.ds(base + sizes.mem_at, MEM_ROWS), :] = memory.astype(BF16)
        grad_low_ref[pl.ds(n * sizes.rows, sizes.rows), :] = out_grad_ref[n]
    fill_mask(sizes, seqs, starts_ref, place_ref, mask_ref)
    wait_all(attn_copies)
    project(sizes, z_ref, qkv_ref, row_bias_ref, proj_ref)
    attend(sizes, seqs, proj_ref, mask_ref, probs_ref, att_ref)
    mixed = (
        inputs_ref[...]
        + nt(att_ref[...], out_ref[...].reshape(-1, wide))
        + biases_ref[3, pl.ds(1, 1), :]
    )
    gain = gains_ref[1, pl.ds(1, 1), :]
    hidden, scaled, inverse = norm_forward(mixed, gain, biases_ref[4, pl.ds(1, 1), :])
    hidden_ref[...] = hidden.astype(BF16)
    for n in range(seqs):
        encoded_ref[n] = mixed[n * sizes.rows : (n + 1) * sizes.rows] + biases_ref[5, pl.ds(1, 1), :]
    grad_hidden_ref[...] = jnp.zeros_like(grad_hidden_ref)
    wait_all(ffn_copies)

    def body(c, carry):
        at_lane = pl.multiple_of(c * wide, wide)
        upward = nt(hidden_ref[...], up_block(up_ref, c, wide))
        upward = upward + ffn_bias_ref[pl.ds(1, 1), pl.ds(at_lane, wide)]
        active, slope = gelu_both(upward)
        active = active.astype(BF16)
        made = nt(active, down_block(down_ref, c, wide))
        for n in range(seqs):
            encoded_ref[n] += made[n * sizes.rows : (n + 1) * sizes.rows]
        grad_hidden_ref[...] += ffn_back_step(
            sizes, c, wide, grad_low_ref[...], hidden_ref[...], active, slope, up_ref, down_ref,
            gup_ref, gdown_ref, vec,
        )
        return carry

    lax.fori_loop(0, sizes.ff // wide, body, 0, unroll=True)
    out_at = len(attn_copies) + len(ffn_copies)
    outs = start_out(
        ffn_pairs(mats, spots, outs_to, gup_ref, gdown_ref, place_ref), sems, out_at
    )
    grad = grad_low_ref[...].astype(F32)
    grad_hidden = grad_hidden_ref[...]
    vec[pl.ds(1, 1), :] = col_sum(grad_hidden * scaled)
    vec[pl.ds(6, 1), :] = col_sum(grad_hidden)
    vec[pl.ds(7, 1), :] = col_sum(grad)
    gz = grad + norm_backward(grad_hidden, scaled, inverse, gain)
    gz_ref[...] = gz
    attn_back_stage(
        sizes, seqs, gz, None, att_ref, proj_ref, probs_ref, z_ref, qkv_ref, out_ref, gqkv_ref,
        gout_ref, go_ref, gproj_ref, branch_ref, vec, gh_ref, gmem_ref, back_left_ref,
        back_right_ref,
    )
    outs = outs + start_out(
        attn_pairs(mats, spots, outs_to, gqkv_ref, gout_ref, place_ref),
        sems,
        out_at + len(outs),
    )
    wait_all(outs)


def first_back_kernel(
    last, sizes, seqs, mats, spots, count_in, count_out, place_ref, inputs_ref, gz_in_ref,
    gh_in_ref, gmem_in_ref, from_right_ref, from_left_ref, mixed_ref, active_ref, slope_ref,
    att_ref, probs_ref, proj_ref, z_ref, frames_ref, left_ref, right_ref, gains_ref, biases_ref,
    last_vec, *refs
):
    groups = in_groups(spots, refs[:count_in])
    gz_ref, gh_ref, gmem_ref, back_left_ref, back_right_ref, upper_vec, vec = refs[
        count_in : count_in + 7
    ]
    refs = refs[count_in + 7 :]
    hbm_out = refs[:count_out]
    (
        qkv_ref, out_ref, up_ref, down_ref, gqkv_ref, gout_ref, gup_ref, gdown_ref, hidden_ref,
        grad_low_ref, grad_ref, grad_hidden_ref, grad_mem_ref, go_ref, gproj_ref, branch_ref,
        small_ref, sems,
    ) = refs[count_out:]
    wide = sizes.width
    small = []
    outs_to = hbm_out
    if spots is not None:
        rows = mats.attn_rows + mats.ffn_rows
        end = CHIPS_Z * rows
        each = [
            ref.at[hop2, hop1] for ref in hbm_out for hop2 in range(2) for hop1 in range(2)
        ]
        small = [ref.at[pl.ds(end, SMALL_ROWS), :] for ref in each]
        outs_to = [[ref.at[pl.ds(0, end), :].reshape(CHIPS_Z, rows, LANES) for ref in each]]
    ffn_copies = start_in(ffn_pairs(mats, spots, groups, up_ref, down_ref, place_ref), sems, 0)
    attn_copies = start_in(
        attn_pairs(mats, spots, groups, qkv_ref, out_ref, place_ref), sems, len(ffn_copies)
    )
    vec[...] = jnp.zeros_like(vec)
    upper_vec[...] = jnp.zeros_like(upper_vec)
    gain = gains_ref[1, pl.ds(0, 1), :]
    gain_sum = jnp.zeros((1, wide), F32)
    bias_sum = jnp.zeros((1, wide), F32)
    for n in range(seqs):
        rows = pl.ds(n * sizes.rows, sizes.rows)
        _, scaled, inverse = norm_forward(
            inputs_ref[rows, :], gain, biases_ref[0, pl.ds(1, 1), :]
        )
        total, mem = merge_halo(last, n, gh_in_ref, gmem_in_ref, from_right_ref, from_left_ref)
        gain_sum = gain_sum + col_sum(total * scaled)
        bias_sum = bias_sum + col_sum(total)
        grad = gz_in_ref[rows, :] + norm_backward(total, scaled, inverse, gain)
        grad_ref[rows, :] = grad
        grad_low_ref[rows, :] = grad.astype(BF16)
        grad_mem_ref[pl.ds(n * sizes.segs, sizes.segs), :] = mem
    upper_vec[pl.ds(0, 1), :] = gain_sum
    upper_vec[pl.ds(2, 1), :] = bias_sum
    gain = gains_ref[0, pl.ds(1, 1), :]
    hidden, scaled, inverse = norm_forward(
        mixed_ref[...], gain, biases_ref[4, pl.ds(0, 1), :]
    )
    hidden_ref[...] = hidden.astype(BF16)
    grad_hidden_ref[...] = jnp.zeros_like(grad_hidden_ref)
    wait_all(ffn_copies)

    def body(c, carry):
        at_lane = pl.multiple_of(c * wide, wide)
        grad_hidden_ref[...] += ffn_back_step(
            sizes, c, wide, grad_low_ref[...], hidden_ref[...],
            active_ref[:, pl.ds(at_lane, wide)], slope_ref[:, pl.ds(at_lane, wide)].astype(F32),
            up_ref, down_ref, gup_ref, gdown_ref, vec,
        )
        return carry

    lax.fori_loop(0, sizes.ff // wide, body, 0)
    out_at = len(ffn_copies) + len(attn_copies)
    outs = start_out(
        ffn_pairs(mats, spots, outs_to, gup_ref, gdown_ref, place_ref), sems, out_at
    )
    grad_hidden = grad_hidden_ref[...]
    grad = grad_ref[...]
    vec[pl.ds(1, 1), :] = col_sum(grad_hidden * scaled)
    vec[pl.ds(6, 1), :] = col_sum(grad_hidden)
    vec[pl.ds(7, 1), :] = col_sum(grad)
    gz = grad + norm_backward(grad_hidden, scaled, inverse, gain)
    gz_ref[...] = gz

    def scaled_rows(n):
        before = left_ref[n, pl.ds(left_ref.shape[1] - LEFT_ROWS, LEFT_ROWS), :]
        parts = (frames_ref[n], right_ref[n], before)
        first_gain = gains_ref[0, pl.ds(0, 1), :]
        first_bias = biases_ref[0, pl.ds(0, 1), :]
        return [norm_forward(part.astype(F32), first_gain, first_bias)[1] for part in parts]

    wait_all(attn_copies)
    attn_back_stage(
        sizes, seqs, gz, grad_mem_ref, att_ref, proj_ref, probs_ref, z_ref, qkv_ref, out_ref,
        gqkv_ref, gout_ref, go_ref, gproj_ref, branch_ref, vec, gh_ref, gmem_ref, back_left_ref,
        back_right_ref, scaled_rows,
    )
    outs = outs + start_out(
        attn_pairs(mats, spots, outs_to, gqkv_ref, gout_ref, place_ref),
        sems,
        out_at + len(outs),
    )
    totals = vec[...], last_vec[...] + upper_vec[...]
    small_ref[...] = jnp.concatenate(
        [
            total[:VEC_ROWS, part * LANES : (part + 1) * LANES]
            for part in range(sizes.pairs)
            for total in totals
        ],
        axis=0,
    ).astype(BF16)
    outs = outs + start_out([(ref, small_ref) for ref in small], sems, out_at + len(outs))
    wait_all(outs)


def frames_grad_kernel(
    sizes, seqs, frames_ref, gz_ref, gh_ref, gmem_ref, from_right_ref, from_left_ref, gains_ref,
    biases_ref, grad_ref
):
    gain = gains_ref[0, pl.ds(0, 1), :]
    for n in range(seqs):
        _, scaled, inverse = norm_forward(
            frames_ref[n].astype(F32), gain, biases_ref[0, pl.ds(0, 1), :]
        )
        total, mem = merge_halo(sizes, n, gh_ref, gmem_ref, from_right_ref, from_left_ref)
        grad_ref[n] = (
            gz_ref[pl.ds(n * sizes.rows, sizes.rows), :]
            + norm_backward(total, scaled, inverse, gain)
            + segment_spread(sizes.rows, sizes.width, mem * (1.0 / SEG_LEN))
        )


def shifted(value, axis, by):
    size = lax.axis_size(axis)
    return lax.ppermute(value, axis, [(i, (i + by) % size) for i in range(size)])


def permuted(value, move):
    reps = lax.axis_size("rep")
    pairs = []
    for flat in range(lax.axis_size("seg") * reps):
        seg, rep = divmod(flat, reps)
        z, y, x, core = move(seg // CHIPS_Y, seg % CHIPS_Y, rep // 2, rep % 2)
        pairs.append((flat, (z * CHIPS_Y + y) * reps + 2 * x + core))
    return lax.ppermute(value, ("seg", "rep"), pairs)


def across_first(value):
    return permuted(value, lambda z, y, x, c: (z, y, x ^ 1, c) if c == 0 else (z, y ^ 1, x, c))


def across_second(value):
    return permuted(value, lambda z, y, x, c: (z, y ^ 1, x, c) if c == 0 else (z, y, x ^ 1, c))


def other_core(value):
    return permuted(value, lambda z, y, x, c: (z, y, x, c ^ 1))


def after(value, *others):
    return lax.optimization_barrier((value,) + others)[0]


def swap_z(blocks):
    groups = [
        [z * CHIPS_Y + y for z in range(CHIPS_Z)] for y in range(CHIPS_Y)
    ]
    return lax.all_to_all(blocks, "seg", 0, 0, axis_index_groups=groups, tiled=True)


def gather_sides(here):
    return [here, across_first(here), across_second(here)]


def both_cores(blocks):
    return blocks + [other_core(block) for block in blocks]


def summed(*parts):
    total = parts[0].astype(F32)
    for part in parts[1:]:
        total = total + part.astype(F32)
    return total.astype(BF16)


def sum_everywhere(value):
    count = lax.axis_size("seg") * lax.axis_size("rep")
    bit = 1
    while bit < count:
        value = value + lax.ppermute(value, ("seg", "rep"), [(i, i ^ bit) for i in range(count)])
        bit *= 2
    return value


def vmem_spec():
    return pl.BlockSpec(memory_space=pltpu.VMEM)


def smem_spec():
    return pl.BlockSpec(memory_space=pltpu.SMEM)


def hbm_spec():
    return pl.BlockSpec(memory_space=pl.ANY)


def call(body, in_specs, out_shapes, out_specs, scratch, args, flops=0, moved=0, grid=(), aliases={}, vmem=12):
    return pl.pallas_call(
        body,
        grid=grid,
        input_output_aliases=aliases,
        in_specs=in_specs,
        out_shape=tuple(jax.ShapeDtypeStruct(shape, kind) for shape, kind in out_shapes),
        out_specs=tuple(out_specs),
        scratch_shapes=scratch,
        compiler_params=pltpu.CompilerParams(vmem_limit_bytes=vmem * MIB),
        cost_estimate=pl.CostEstimate(flops=flops, bytes_accessed=moved, transcendentals=0),
    )(*args)


def on_device(
    frames,
    utt_segments,
    out_grad,
    qkv_weight,
    out_weight,
    ffn_in_weight,
    ffn_out_weight,
    norm_gains,
    biases,
    ffn_bias,
):
    micros, groups, rows, width = frames.shape
    seqs = micros * groups
    ff = ffn_bias.shape[1]
    reps = lax.axis_size("rep")
    seg_count = lax.axis_size("seg")
    mats = Matrices(width, ff)
    by_blocks = width // reps == LANES and reps == 4 and seg_count == BLOCKS
    first = Sizes(rows, width, ff, True)
    last = Sizes(rows, width, ff, False)
    own = seqs * rows
    mem_own = seqs * first.segs

    seg_at = lax.axis_index("seg")
    seg_base = seg_at * first.segs
    rep_at = lax.axis_index("rep")
    place = [seg_base, jnp.int32(first.segs * seg_count)]
    y_at, x_at, core_at = seg_at % CHIPS_Y, rep_at // 2, rep_at % 2
    for other in range(2):
        core = lax.bitwise_xor(core_at, other)
        for hop2 in range(2):
            for hop1 in range(2):
                x_hop = jnp.where(core == 0, hop1, hop2)
                y_hop = jnp.where(core == 0, hop2, hop1)
                place.append(lax.bitwise_xor(y_at, y_hop))
                place.append((lax.bitwise_xor(x_at, x_hop) * 2 + core) * LANES)
    place = jnp.stack([jnp.asarray(entry, jnp.int32) for entry in place])
    lengths = utt_segments.reshape(seqs, utt_segments.shape[2])
    starts = (jnp.cumsum(lengths, axis=1) - lengths).astype(jnp.int32)
    zero_bias = jnp.zeros((1, width), F32)
    row_biases = [
        jnp.concatenate([biases[l : l + 1, 1], zero_bias, biases[l : l + 1, 2]], axis=1)
        for l in range(LAYERS)
    ]
    biases_by_row = jnp.swapaxes(biases, 0, 1)

    frames_own = frames.reshape(seqs, rows, width)
    grads_own = out_grad.reshape(seqs, rows, width)
    far = MEM_LEN * SEG_LEN
    frames_left = shifted(frames_own[:, rows - far :], "seg", 1)
    frames_right = shifted(frames_own[:, :RIGHT_ROWS], "seg", -1)

    attn_rows, ffn_rows = mats.attn_rows, mats.ffn_rows
    if by_blocks:
        qkv_t, out_t, down_t = (
            jnp.swapaxes(member, 1, 2) for member in (qkv_weight, out_weight, ffn_out_weight)
        )
        all_rows = attn_rows + ffn_rows
        spots = Spots(mats)
        shards = call(
            lambda *refs: pack_kernel(spots, *refs),
            [vmem_spec()] * 4,
            [((CHIPS_Z, all_rows, LANES), BF16)] * LAYERS,
            [vmem_spec()] * LAYERS,
            [],
            (qkv_t, out_t, ffn_in_weight, down_t),
            vmem=56,
        )
        sides0 = gather_sides(after(swap_z(shards[0]), frames_left, frames_right))
        place, starts, row_biases, sent = lax.optimization_barrier(
            (place, starts, row_biases, after(shards[1], sides0[0]))
        )
        sides1 = gather_sides(swap_z(sent))
        first_all = both_cores(sides0 + [across_second(after(sides0[1], sides1[0]))])
        classes = len(first_all) // 2
        grad_outs0 = [((2, 2, CHIPS_Z * all_rows + SMALL_ROWS, LANES), BF16)] * 2
        grad_outs1 = [((CHIPS_Z, 2 * all_rows, LANES), BF16)] * 4
        copies_in = len(first_all) * (3 + mats.down_parts)
    else:
        whole = []
        for member, shape in zip(
            (qkv_weight, out_weight, ffn_in_weight, ffn_out_weight),
            (mats.qkv, mats.out, mats.up, mats.down),
        ):
            member = lax.all_gather(member, "rep", axis=1, tiled=True)
            member = lax.all_gather(member, "seg", axis=2, tiled=True)
            whole.append(jnp.swapaxes(member, 1, 2).reshape((LAYERS,) + shape))
        first_all = [member[0] for member in whole]
        last_all = [member[1] for member in whole]
        spots = None
        grad_outs0 = grad_outs1 = [
            (shape, BF16) for shape in (mats.qkv, mats.out, mats.up, mats.down)
        ]
        copies_in = 4
    dma = pltpu.SemaphoreType.DMA

    matrices = [pltpu.VMEM(shape, BF16) for shape in (mats.qkv, mats.out, mats.up, mats.down)]

    (
        z0, proj0, probs0, att0, mixed0, mem1, x1, active0, slope0, low1, send_right, send_left,
    ) = call(
        lambda *refs: first_layer_kernel(
            first, seqs, mats, spots, len(first_all), *refs
        ),
        [smem_spec()] * 2 + [vmem_spec()] * 7 + [hbm_spec()] * len(first_all),
        [
            ((seqs * first.ext, width), BF16),
            ((seqs * first.ext, 3 * width), BF16),
            ((seqs * first.pairs, first.keys, 2 * first.queries), BF16),
            ((seqs * first.queries, width), BF16),
            ((own, width), F32),
            ((mem_own, width), F32),
            ((own, width), F32),
            ((own, ff), BF16),
            ((own, ff), BF16),
            ((own, width), BF16),
            ((seqs, BACK_ROWS, width), BF16),
            ((seqs, RIGHT_ROWS, width), BF16),
        ],
        [vmem_spec()] * 12,
        matrices
        + [
            pltpu.VMEM((seqs, first.keys, 2 * first.queries), F32),
            pltpu.VMEM((own, width), BF16),
            dma((copies_in,)),
        ],
        (place, starts, frames_own, frames_left, frames_right, norm_gains, biases_by_row, ffn_bias,
         row_biases[0]) + tuple(first_all),
        flops=24 * own * (4 * width * width + 2 * width * ff) // 2,
        moved=2 * (4 * width * width + 2 * width * ff),
        vmem=20,
    )
    left1 = shifted(send_right, "seg", 1)
    right1 = shifted(send_left, "seg", -1)
    if by_blocks:
        last_side = across_second(after(sides1[1], sides1[2], left1, right1))
        last_all = both_cores(sides1 + [last_side])

    vec_shape = (TILE, width)
    outs = call(
        lambda *refs: last_layer_kernel(
            last, seqs, mats, spots, len(last_all), len(grad_outs1), *refs
        ),
        [smem_spec()] * 2 + [vmem_spec()] * 10 + [hbm_spec()] * len(last_all),
        [
            ((seqs, rows, width), F32),
            ((own, width), F32),
            ((own, width), F32),
            ((mem_own, width), F32),
            ((seqs, BACK_ROWS, width), BF16),
            ((seqs, RIGHT_ROWS, width), BF16),
            (vec_shape, F32),
        ]
        + grad_outs1,
        [vmem_spec()] * 7 + [hbm_spec()] * len(grad_outs1),
        matrices
        + matrices
        + [
            pltpu.VMEM((seqs, last.keys, 2 * last.queries), F32),
            pltpu.VMEM((seqs * last.ext, width), BF16),
            pltpu.VMEM((seqs * last.ext, 3 * width), BF16),
            pltpu.VMEM((seqs * last.pairs, last.keys, 2 * last.queries), BF16),
            pltpu.VMEM((seqs * last.queries, width), BF16),
            pltpu.VMEM((own, width), BF16),
            pltpu.VMEM((seqs * last.queries, width), BF16),
            pltpu.VMEM((seqs * last.ext, 3 * width), BF16),
            pltpu.VMEM((seqs * last.queries, width), BF16),
            pltpu.VMEM((own, width), BF16),
            pltpu.VMEM((own, width), F32),
            dma((2 * copies_in,)),
        ],
        (place, starts, low1, left1, right1, mem1, x1, grads_own, norm_gains, biases_by_row, ffn_bias,
         row_biases[1]) + tuple(last_all),
        flops=30 * own * (4 * width * width + 2 * width * ff),
        moved=4 * (4 * width * width + 2 * width * ff),
        vmem=26,
    )
    encoded, gz1, gh1, gmem1, back_left1, back_right1, vec1 = outs[:7]
    grad_blocks1 = outs[7:]
    from_right1 = shifted(back_left1, "seg", -1)
    from_left1 = shifted(back_right1, "seg", 1)

    gh1_tied = gh1
    if by_blocks:
        near1, far1, near1_other, far1_other = grad_blocks1
        far1 = summed(far1, other_core(far1_other))
        near1_theirs = other_core(near1_other)
        gh1_tied = after(gh1, far1, near1_theirs)
    gz0, gh0, gmem0, back_left0, back_right0, upper_vec, vec0, *grad_blocks0 = call(
        lambda *refs: first_back_kernel(
            last, first, seqs, mats, spots, len(first_all), len(grad_outs0), *refs
        ),
        [smem_spec()] + [vmem_spec()] * 19 + [hbm_spec()] * len(first_all),
        [
            ((own, width), F32),
            ((own, width), F32),
            ((mem_own, width), F32),
            ((seqs, BACK_ROWS, width), BF16),
            ((seqs, RIGHT_ROWS, width), BF16),
            (vec_shape, F32),
            (vec_shape, F32),
        ]
        + grad_outs0,
        [vmem_spec()] * 7 + [hbm_spec()] * len(grad_outs0),
        matrices
        + matrices
        + [
            pltpu.VMEM((own, width), BF16),
            pltpu.VMEM((own, width), BF16),
            pltpu.VMEM((own, width), F32),
            pltpu.VMEM((own, width), F32),
            pltpu.VMEM((mem_own, width), F32),
            pltpu.VMEM((seqs * first.queries, width), BF16),
            pltpu.VMEM((seqs * first.ext, 3 * width), BF16),
            pltpu.VMEM((seqs * first.queries, width), BF16),
            pltpu.VMEM((SMALL_ROWS, LANES), BF16),
            dma((2 * copies_in + 8,)),
        ],
        (place, x1, gz1, gh1_tied, gmem1, from_right1, from_left1, mixed0, active0, slope0, att0,
         probs0, proj0, z0, frames_own, frames_left, frames_right, norm_gains, biases_by_row, vec1)
        + tuple(first_all),
        flops=28 * own * (4 * width * width + 2 * width * ff),
        moved=4 * (4 * width * width + 2 * width * ff),
        vmem=28,
    )
    from_right0 = shifted(back_left0, "seg", -1)
    from_left0 = shifted(back_right0, "seg", 1)
    gz0_last = gz0
    if by_blocks:
        second1 = across_second(far1)
        mine0, theirs0 = grad_blocks0[0], other_core(after(grad_blocks0[1], second1))
        both1 = summed(near1, near1_theirs, second1)
        lines1 = swap_z(both1)
        far0 = summed(mine0[1], after(theirs0, both1)[1])
        far0 = after(far0, from_right0, from_left0)
        second0 = across_second(far0)
        mid0 = summed(mine0[0, 1], theirs0[0, 1], second0[1])
        first0 = across_first(mid0)
        held0 = summed(mine0[0, 0], theirs0[0, 0], after(second0, mid0)[0])
        near0 = summed(held0, first0)
        blocks = CHIPS_Z * all_rows
        near0 = jnp.concatenate(
            [
                near0[:blocks].reshape(CHIPS_Z, all_rows, LANES),
                jnp.broadcast_to(near0[None, blocks:], (CHIPS_Z, SMALL_ROWS, LANES)),
            ],
            axis=1,
        )
        first_parts = swap_z(near0)
        gz0_last, lines1 = lax.optimization_barrier((after(gz0, near0), lines1))
        cross1 = jnp.sum(lines1[:, all_rows:].astype(F32), axis=0, keepdims=True).astype(BF16)
        first1 = across_first(cross1)
    frames_grad = call(
        lambda *refs: frames_grad_kernel(first, seqs, *refs),
        [vmem_spec()] * 8,
        [((seqs, rows, width), F32)],
        [vmem_spec()],
        [],
        (frames_own, gz0_last, gh0, gmem0, from_right0, from_left0, norm_gains, biases_by_row),
    )[0]

    if by_blocks:
        shapes = [member.shape for member in (qkv_t, out_t, ffn_in_weight, down_t)]
        held = [pltpu.VMEM(shape[1:], F32) for shape in shapes]
        whole = [(shape, F32) for shape in shapes]
        written = call(
            lambda *refs: unpack_last_kernel(spots, LAYERS - 1, *refs),
            [
                pl.BlockSpec((CHIPS_Z, all_rows, LANES), lambda i: (0, 0, 0)),
                pl.BlockSpec((1, all_rows, LANES), lambda i: (0, 0, 0)),
            ],
            whole,
            [hbm_spec()] * 4,
            held + [dma((4,))],
            [lines1, first1],
            grid=(1,),
        )
        small_shapes = [norm_gains.shape, (biases.shape[1], LAYERS, width), ffn_bias.shape]
        reduced = call(
            lambda *refs: unpack_first_kernel(spots, all_rows, *refs),
            [vmem_spec()] + [hbm_spec()] * 4,
            whole + [(shape, F32) for shape in small_shapes],
            [hbm_spec()] * 4 + [vmem_spec()] * 3,
            held + [dma((4,))],
            [after(first_parts, frames_grad)] + list(written),
            aliases={1 + i: i for i in range(4)},
        )
        small = reduced[4], jnp.swapaxes(reduced[5], 0, 1), reduced[6]
        reduced = [
            jnp.swapaxes(reduced[0], 1, 2),
            jnp.swapaxes(reduced[1], 1, 2),
            reduced[2],
            jnp.swapaxes(reduced[3], 1, 2),
        ]
    else:
        reduced = []
        for member0, member1 in zip(grad_blocks0, grad_blocks1):
            both = jnp.stack([member0, member1]).reshape(LAYERS, -1, member0.shape[3])
            both = jnp.swapaxes(both, 1, 2)
            both = lax.psum_scatter(both, "seg", scatter_dimension=2, tiled=True)
            both = lax.psum_scatter(both, "rep", scatter_dimension=1, tiled=True)
            reduced.append(both.astype(F32))
        small = sum_everywhere(jnp.stack([vec0, vec1 + upper_vec]))
        small = small[:, 0:2], small[:, 2:8], small[:, 8:12].reshape(ffn_bias.shape)

    return (
        encoded.reshape(frames.shape),
        frames_grad.reshape(frames.shape),
        reduced[0],
        reduced[1],
        reduced[2],
        reduced[3],
        small[0],
        small[1],
        small[2],
    )


def solution(mesh):
    in_specs = (
        P(None, "rep", "seg", None),
        P(None, "rep", None),
        P(None, "rep", "seg", None),
        P(None, "rep", "seg"),
        P(None, "rep", "seg"),
        P(None, "rep", "seg"),
        P(None, "rep", "seg"),
        P(),
        P(),
        P(),
    )
    out_specs = (
        P(None, "rep", "seg", None),
        P(None, "rep", "seg", None),
        P(None, "rep", "seg"),
        P(None, "rep", "seg"),
        P(None, "rep", "seg"),
        P(None, "rep", "seg"),
        P(),
        P(),
        P(),
    )
    return jax.shard_map(
        on_device, mesh=mesh, in_specs=in_specs, out_specs=out_specs, check_vma=False
    )
```

```python
import jax
import jax.numpy as jnp
from jax import lax
from jax.experimental import pallas as pl
from jax.experimental.pallas import tpu as pltpu
from jax.sharding import PartitionSpec as P

HEADS = 8
SEG_LEN = 16
LEFT_LEN = 30
RIGHT_LEN = 4
MEM_LEN = 4
LAYERS = 2

EPS = 1e-05
ROOT_HALF = 0.7071067811865476
INV_ROOT_TWO_PI = 0.3989422804014327

LANES = 128
TILE = 16
RIGHT_ROWS = 16
LEFT_ROWS = 32
MEM_ROWS = 16
BACK_ROWS = LEFT_ROWS + MEM_ROWS
CHIPS_Z = 4
CHIPS_Y = 2
BLOCKS = CHIPS_Z * CHIPS_Y
VEC_ROWS = 12
SMALL_ROWS = 96
MIB = 1024 * 1024

BF16 = jnp.bfloat16
F32 = jnp.float32


def nn(a, b):
    return lax.dot_general(a, b, (((1,), (0,)), ((), ())), preferred_element_type=F32)


def nt(a, b):
    return lax.dot_general(a, b, (((1,), (1,)), ((), ())), preferred_element_type=F32)


def tn(a, b):
    return lax.dot_general(a, b, (((0,), (0,)), ((), ())), preferred_element_type=F32)


def col_sum(value):
    return jnp.sum(value, axis=0, keepdims=True)


def norm_forward(inputs, gain, bias):
    center = inputs - jnp.mean(inputs, axis=1, keepdims=True)
    inverse = lax.rsqrt(jnp.mean(center * center, axis=1, keepdims=True) + EPS)
    scaled = center * inverse
    return scaled * gain + bias, scaled, inverse


def norm_backward(grad_in, scaled, inverse, gain):
    grad_scaled = grad_in * gain
    return inverse * (
        grad_scaled
        - jnp.mean(grad_scaled, axis=1, keepdims=True)
        - scaled * jnp.mean(grad_scaled * scaled, axis=1, keepdims=True)
    )


def segment_mean(inputs):
    rows, width = inputs.shape
    return jnp.mean(inputs.reshape(rows // SEG_LEN, SEG_LEN, width), axis=1)


def segment_spread(rows, width, per_segment):
    segs = rows // SEG_LEN
    return jnp.broadcast_to(per_segment[:, None, :], (segs, SEG_LEN, width)).reshape(rows, width)


def identity(size):
    row = lax.broadcasted_iota(jnp.int32, (size, size), 0)
    col = lax.broadcasted_iota(jnp.int32, (size, size), 1)
    return (row == col).astype(F32).astype(BF16)


class Sizes:
    def __init__(self, rows, width, ff, with_summary):
        self.rows = rows
        self.width = width
        self.ff = ff
        self.segs = rows // SEG_LEN
        self.top = TILE if with_summary else 0
        self.keys = rows + RIGHT_ROWS + LEFT_ROWS + MEM_ROWS
        self.ext = self.top + self.keys
        self.queries = self.top + rows
        self.right_at = self.top + rows
        self.left_at = self.right_at + RIGHT_ROWS
        self.mem_at = self.left_at + LEFT_ROWS
        self.pairs = width // LANES


class Matrices:
    def __init__(self, width, ff):
        self.qkv = (CHIPS_Z, CHIPS_Y, 3 * width // BLOCKS, width)
        self.out = (CHIPS_Z, CHIPS_Y, width // BLOCKS, width)
        self.up = (CHIPS_Z, CHIPS_Y, ff // BLOCKS, width)
        self.down = (CHIPS_Z, CHIPS_Y, width // BLOCKS, ff)
        self.down_parts = ff // width
        self.attn_rows = self.qkv[2] + self.out[2]
        self.ffn_rows = self.up[2] + self.down_parts * self.down[2]


class Spots:
    def __init__(self, mats):
        high, wide, up, low = mats.qkv[2], mats.out[2], mats.up[2], mats.down[2]
        self.qkv = (0, 0)
        self.out = (0, high)
        self.up = (0, high + wide)
        self.down = [(0, high + wide + up + low * part) for part in range(mats.down_parts)]


def attn_pairs(mats, spots, groups, qkv_ref, out_ref, place_ref):
    if spots is None:
        return [(groups[0], qkv_ref), (groups[1], out_ref)]
    pairs = []
    for k in range(len(groups[0])):
        row = place_ref[2 + 2 * k]
        lane = pl.multiple_of(place_ref[3 + 2 * k], LANES)
        for (group, first), ref, shape in (
            (spots.qkv, qkv_ref, mats.qkv),
            (spots.out, out_ref, mats.out),
        ):
            block = groups[group][k]
            pairs.append(
                (
                    block.at[:, pl.ds(first, shape[2]), :],
                    ref.at[:, row, :, pl.ds(lane, LANES)],
                )
            )
    return pairs


def ffn_pairs(mats, spots, groups, up_ref, down_ref, place_ref):
    if spots is None:
        return [(groups[2], up_ref), (groups[3], down_ref)]
    pairs = []
    for k in range(len(groups[0])):
        row = place_ref[2 + 2 * k]
        lane = pl.multiple_of(place_ref[3 + 2 * k], LANES)
        group, first = spots.up
        block = groups[group][k]
        pairs.append(
            (block.at[:, pl.ds(first, mats.up[2]), :], up_ref.at[:, row, :, pl.ds(lane, LANES)])
        )
        for part, (group, first) in enumerate(spots.down):
            there = pl.multiple_of(
                place_ref[3 + 2 * k] * mats.down_parts + part * LANES, LANES
            )
            block = groups[group][k]
            pairs.append(
                (
                    block.at[:, pl.ds(first, mats.down[2]), :],
                    down_ref.at[:, row, :, pl.ds(there, LANES)],
                )
            )
    return pairs


def start_in(pairs, sems, at):
    copies = [pltpu.make_async_copy(s, d, sems.at[at + i]) for i, (s, d) in enumerate(pairs)]
    for copy in copies:
        copy.start()
    return copies


def start_out(pairs, sems, at):
    copies = [pltpu.make_async_copy(d, s, sems.at[at + i]) for i, (s, d) in enumerate(pairs)]
    for copy in copies:
        copy.start()
    return copies


def in_groups(spots, refs):
    return refs if spots is None else [refs]


def wait_all(copies):
    for copy in copies:
        copy.wait()


def fill_mask(sizes, seqs, starts_ref, place_ref, mask_ref):
    shape = (sizes.keys, 2 * sizes.queries)
    key = lax.broadcasted_iota(jnp.int32, shape, 0)
    col = lax.broadcasted_iota(jnp.int32, shape, 1)
    col = jnp.where(col < sizes.queries, col, col - sizes.queries)
    base = place_ref[0]
    total = place_ref[1]
    query = jnp.where(col < sizes.top, col, lax.shift_right_arithmetic(col - sizes.top, 4))
    left_at = sizes.rows + RIGHT_ROWS
    mem_at = left_at + LEFT_ROWS
    spot = jnp.where(key < left_at, key, key - mem_at)
    mem_seg = jnp.where(key < mem_at + sizes.segs, key - mem_at, key - mem_at - 2 * sizes.segs)
    key_seg = jnp.where(key < mem_at, lax.shift_right_arithmetic(spot, 4), mem_seg)
    near = (
        (key_seg == query)
        | ((spot >= query * SEG_LEN - LEFT_LEN) & (spot < query * SEG_LEN))
        | ((key_seg == query + 1) & (spot < query * SEG_LEN + SEG_LEN + RIGHT_LEN))
    )
    recent = (key_seg >= query - MEM_LEN) & (key_seg < query) & (col >= sizes.top)
    allowed = ((key < mem_at) & near) | ((key >= mem_at) & recent)
    key_abs = key_seg + base
    query_abs = query + base
    allowed = allowed & (key_abs >= 0) & (key_abs < total)
    if sizes.top:
        allowed = allowed & ((col < sizes.segs) | (col >= sizes.top))
    for n in range(seqs):
        key_owner = jnp.zeros(shape, jnp.int32)
        query_owner = jnp.zeros(shape, jnp.int32)
        for u in range(starts_ref.shape[1]):
            first = starts_ref[n, u]
            key_owner = key_owner + (key_abs >= first).astype(jnp.int32)
            query_owner = query_owner + (query_abs >= first).astype(jnp.int32)
        mask_ref[n] = jnp.where(allowed & (key_owner == query_owner), 0.0, -1e30)


def half_masks():
    lane = lax.broadcasted_iota(jnp.int32, (1, LANES), 1)
    even = (lane < LANES // 2).astype(F32)
    return even.astype(BF16), (1.0 - even).astype(BF16), lane < LANES // 2


def project(sizes, z_ref, qkv_ref, row_bias_ref, proj_ref):
    step = CHIPS_Z // 2
    for c in range(2):
        block = qkv_ref[pl.ds(c * step, step)].reshape(-1, sizes.width)
        wide = block.shape[0]
        made = nt(z_ref[...], block) + row_bias_ref[:, pl.ds(c * wide, wide)]
        proj_ref[:, pl.ds(c * wide, wide)] = made.astype(BF16)


def attend(sizes, seqs, proj_ref, mask_ref, probs_ref, att_ref):
    even, odd, is_even = half_masks()
    scale = (sizes.width // HEADS) ** (-0.5)
    count = sizes.queries

    def body(p, carry):
        for n in range(seqs):
            lane = pl.multiple_of(p * LANES, LANES)
            query = proj_ref[pl.ds(n * sizes.ext, count), pl.ds(lane, LANES)]
            first = n * sizes.ext + sizes.top
            key = proj_ref[pl.ds(first, sizes.keys), pl.ds(sizes.width + lane, LANES)]
            value = proj_ref[pl.ds(first, sizes.keys), pl.ds(2 * sizes.width + lane, LANES)]
            queries = jnp.concatenate([query * even, query * odd], axis=0)
            scores = nt(key, queries) * scale + mask_ref[n]
            scores = jnp.exp(scores - jnp.max(scores, axis=0, keepdims=True))
            probs = (scores * (1.0 / jnp.sum(scores, axis=0, keepdims=True))).astype(BF16)
            probs_ref[n * sizes.pairs + p] = probs
            out = tn(probs, value)
            att_ref[pl.ds(n * count, count), pl.ds(lane, LANES)] = jnp.where(
                is_even, out[:count], out[count:]
            ).astype(BF16)
        return carry

    lax.fori_loop(0, sizes.pairs, body, 0, unroll=True)


def attend_back(sizes, seqs, proj_ref, probs_ref, go_ref, gproj_ref):
    even, odd, is_even = half_masks()
    scale = (sizes.width // HEADS) ** (-0.5)
    count = sizes.queries
    wide = sizes.width
    for n in range(seqs):
        base = n * sizes.ext
        rest = sizes.ext - count
        gproj_ref[pl.ds(base + count, rest), pl.ds(0, wide)] = jnp.zeros((rest, wide), BF16)
        if sizes.top:
            gproj_ref[pl.ds(base, sizes.top), pl.ds(wide, 2 * wide)] = jnp.zeros(
                (sizes.top, 2 * wide), BF16
            )

    def body(p, carry):
        for n in range(seqs):
            lane = pl.multiple_of(p * LANES, LANES)
            base = n * sizes.ext
            first = base + sizes.top
            query = proj_ref[pl.ds(base, count), pl.ds(lane, LANES)]
            key = proj_ref[pl.ds(first, sizes.keys), pl.ds(wide + lane, LANES)]
            value = proj_ref[pl.ds(first, sizes.keys), pl.ds(2 * wide + lane, LANES)]
            grad = go_ref[pl.ds(n * count, count), pl.ds(lane, LANES)]
            queries = jnp.concatenate([query * even, query * odd], axis=0)
            grads = jnp.concatenate([grad * even, grad * odd], axis=0)
            probs_low = probs_ref[n * sizes.pairs + p]
            grad_values = nn(probs_low, grads)
            probs = probs_low.astype(F32)
            weighted = nt(value, grads) * probs
            grad_scores = (
                (weighted - probs * jnp.sum(weighted, axis=0, keepdims=True)) * scale
            ).astype(BF16)
            grad_keys = nn(grad_scores, queries)
            grad_both = tn(grad_scores, key)
            grad_query = jnp.where(is_even, grad_both[:count], grad_both[count:])
            gproj_ref[pl.ds(base, count), pl.ds(lane, LANES)] = grad_query.astype(BF16)
            gproj_ref[pl.ds(first, sizes.keys), pl.ds(wide + lane, LANES)] = grad_keys.astype(BF16)
            gproj_ref[pl.ds(first, sizes.keys), pl.ds(2 * wide + lane, LANES)] = (
                grad_values.astype(BF16)
            )
        return carry

    lax.fori_loop(0, sizes.pairs, body, 0, unroll=sizes.pairs if sizes.top == 0 else 1)


def gelu_both(upward):
    half = 0.5 * (1.0 + lax.erf(upward * ROOT_HALF))
    slope = half + upward * jnp.exp(-0.5 * upward * upward) * INV_ROOT_TWO_PI
    return upward * half, slope


def up_block(up_ref, c, wide):
    step = wide // (up_ref.shape[1] * up_ref.shape[2])
    return up_ref[pl.ds(c * step, step)].reshape(-1, up_ref.shape[3])


def down_block(down_ref, c, wide):
    at = pl.multiple_of(c * wide, wide)
    return down_ref[:, :, :, pl.ds(at, wide)].reshape(-1, wide)


def ffn_back_step(
    sizes, c, wide, grad_low, hidden_low, active, slope, up_ref, down_ref, gup_ref, gdown_ref, vec
):
    at = pl.multiple_of(c * wide, wide)
    up = up_block(up_ref, c, wide)
    down = down_block(down_ref, c, wide)
    grad_active = nn(grad_low, down)
    grad_up_f = grad_active * slope
    grad_up = grad_up_f.astype(BF16)
    gdown_ref[:, :, :, pl.ds(at, wide)] = (
        tn(grad_low, active).astype(BF16).reshape(gdown_ref.shape[:3] + (wide,))
    )
    step = wide // (gup_ref.shape[1] * gup_ref.shape[2])
    gup_ref[pl.ds(c * step, step)] = (
        tn(grad_up, hidden_low).astype(BF16).reshape((step,) + gup_ref.shape[1:])
    )
    vec[pl.ds(8 + c, 1), :] = col_sum(grad_up.astype(F32))
    return nn(grad_up, up)


def attn_back_stage(
    sizes, seqs, gz, grad_mem_ref, att_ref, proj_ref, probs_ref, z_ref, qkv_ref, out_ref,
    gqkv_ref, gout_ref, go_ref, gproj_ref, branch_ref, vec, gh_ref, gmem_ref, back_left_ref,
    back_right_ref, scaled_rows=None,
):
    wide = sizes.width
    count = sizes.queries
    bias_out = col_sum(gz)
    for n in range(seqs):
        if sizes.top:
            mem_grad = grad_mem_ref[pl.ds(n * sizes.segs, sizes.segs), :]
            bias_out = bias_out + col_sum(mem_grad)
            branch_ref[pl.ds(n * count, sizes.top), :] = jnp.concatenate(
                [mem_grad, jnp.zeros((sizes.top - sizes.segs, wide), F32)], axis=0
            ).astype(BF16)
        branch_ref[pl.ds(n * count + sizes.top, sizes.rows), :] = gz[
            n * sizes.rows : (n + 1) * sizes.rows
        ].astype(BF16)
    vec[pl.ds(5, 1), :] = bias_out
    branch = branch_ref[...]
    gout_ref[...] = tn(branch, att_ref[...]).astype(BF16).reshape(gout_ref.shape)
    go_ref[...] = nn(branch, out_ref[...].reshape(-1, wide)).astype(BF16)
    attend_back(sizes, seqs, proj_ref, probs_ref, go_ref, gproj_ref)
    vec[pl.ds(3, 1), :] = col_sum(gproj_ref[:, pl.ds(0, wide)].astype(F32))
    vec[pl.ds(4, 1), :] = col_sum(gproj_ref[:, pl.ds(2 * wide, wide)].astype(F32))
    grad_ext = nn(gproj_ref[...], qkv_ref[...].reshape(-1, wide))
    gain_sum = jnp.zeros((1, wide), F32)
    bias_sum = jnp.zeros((1, wide), F32)
    for n in range(seqs):
        base = n * sizes.ext
        own = grad_ext[base + sizes.top : base + sizes.top + sizes.rows]
        if sizes.top:
            spread = grad_ext[base : base + sizes.segs] * (1.0 / SEG_LEN)
            own = own + segment_spread(sizes.rows, wide, spread)
        gh_ref[pl.ds(n * sizes.rows, sizes.rows), :] = own
        mem = base + sizes.mem_at
        gmem_ref[pl.ds(n * sizes.segs, sizes.segs), :] = grad_ext[mem : mem + sizes.segs]
        left = base + sizes.left_at
        back_left_ref[n] = grad_ext[left : left + BACK_ROWS].astype(BF16)
        right = base + sizes.right_at
        back_right_ref[n] = grad_ext[right : right + RIGHT_ROWS].astype(BF16)
        if scaled_rows is not None:
            grads = (
                own,
                grad_ext[right : right + RIGHT_ROWS],
                grad_ext[left : left + LEFT_ROWS],
            )
            for rows, scaled in zip(grads, scaled_rows(n)):
                gain_sum = gain_sum + col_sum(rows * scaled)
                bias_sum = bias_sum + col_sum(rows)
    if scaled_rows is not None:
        vec[pl.ds(0, 1), :] = gain_sum
        vec[pl.ds(2, 1), :] = bias_sum
    step = CHIPS_Z // 2
    part = gqkv_ref.shape[1] * gqkv_ref.shape[2] * step
    for c in range(2):
        gqkv_ref[pl.ds(c * step, step)] = (
            tn(gproj_ref[:, pl.ds(c * part, part)], z_ref[...])
            .astype(BF16)
            .reshape((step,) + gqkv_ref.shape[1:])
        )


def merge_halo(sizes, n, gh_ref, gmem_ref, from_right_ref, from_left_ref):
    first = n * sizes.rows
    back = from_right_ref[n].astype(F32)
    head = gh_ref[pl.ds(first, RIGHT_ROWS), :] + from_left_ref[n].astype(F32)
    middle = gh_ref[pl.ds(first + RIGHT_ROWS, sizes.rows - RIGHT_ROWS - LEFT_ROWS), :]
    tail = gh_ref[pl.ds(first + sizes.rows - LEFT_ROWS, LEFT_ROWS), :] + back[:LEFT_ROWS]
    mem = gmem_ref[pl.ds(n * sizes.segs, sizes.segs), :] + back[LEFT_ROWS + sizes.segs :]
    return jnp.concatenate([head, middle, tail], axis=0), mem


def pack_kernel(spots, qkv_ref, out_ref, up_ref, down_ref, *packed):
    eye = identity(LANES)
    high, wide, low = qkv_ref.shape[1], out_ref.shape[1], down_ref.shape[1]
    for layer, ref in enumerate(packed):
        up = tn(up_ref[layer], eye).astype(BF16)
        for z in range(ref.shape[0]):
            ref[z, pl.ds(spots.qkv[1], high), :] = qkv_ref[layer]
            ref[z, pl.ds(spots.out[1], wide), :] = out_ref[layer]
            ref[z, pl.ds(spots.up[1], up_ref.shape[2]), :] = up
            for part, (_, first) in enumerate(spots.down):
                ref[z, pl.ds(first, low), :] = down_ref[layer, :, pl.ds(part * LANES, LANES)]


def unpack_layer(spots, sources, refs):
    qkv_ref, out_ref, up_ref, down_ref = refs
    high, wide, low = qkv_ref.shape[0], out_ref.shape[0], down_ref.shape[0]

    def total(first, rows):
        parts = [ref[z, pl.ds(first, rows), :] for ref in sources for z in range(ref.shape[0])]
        value = parts[0].astype(F32)
        for part in parts[1:]:
            value = value + part.astype(F32)
        return value

    qkv_ref[...] = total(spots.qkv[1], high)
    out_ref[...] = total(spots.out[1], wide)
    up_ref[...] = nt(identity(LANES), total(spots.up[1], up_ref.shape[1]).astype(BF16))
    for part, (_, first) in enumerate(spots.down):
        down_ref[:, pl.ds(part * LANES, LANES)] = total(first, low)
    return total


def store_layer(layer, held, outs, sems):
    copies = [
        pltpu.make_async_copy(ref, out.at[layer], sems.at[i])
        for i, (ref, out) in enumerate(zip(held, outs))
    ]
    for copy in copies:
        copy.start()
    return copies


def unpack_last_kernel(spots, layer, lines_ref, first_ref, *refs):
    outs, held, sems = refs[:4], refs[4:8], refs[8]
    unpack_layer(spots, (lines_ref, first_ref), held)
    wait_all(store_layer(layer, held, outs, sems))


def unpack_first_kernel(spots, small_at, parts_ref, *refs):
    outs, (gains_ref, biases_ref, ffn_bias_ref), held, sems = (
        refs[4:8], refs[8:11], refs[11:15], refs[15],
    )
    total = unpack_layer(spots, (parts_ref,), held)
    copies = store_layer(0, held, outs, sems)
    sums = total(small_at, SMALL_ROWS)
    parts = gains_ref.shape[2] // LANES
    for layer in range(gains_ref.shape[0]):
        for part in range(parts):
            lanes = pl.ds(part * LANES, LANES)
            at = (part * gains_ref.shape[0] + layer) * VEC_ROWS
            block = sums[at : at + VEC_ROWS]
            gains_ref[layer, :, lanes] = block[0:2]
            for row in range(biases_ref.shape[0]):
                biases_ref[row, pl.ds(layer, 1), lanes] = block[2 + row : 3 + row]
            for row in range(ffn_bias_ref.shape[1] // gains_ref.shape[2]):
                at = row * gains_ref.shape[2] + part * LANES
                ffn_bias_ref[pl.ds(layer, 1), pl.ds(at, LANES)] = block[8 + row : 9 + row]
    wait_all(copies)


def first_layer_kernel(
    sizes, seqs, mats, spots, count_in, place_ref, starts_ref, frames_ref, left_ref, right_ref,
    gains_ref, biases_ref, ffn_bias_ref, row_bias_ref, *refs
):
    groups = in_groups(spots, refs[:count_in])
    (
        z_ref, proj_ref, probs_ref, att_ref, mixed_ref, mem_ref, next_ref, active_ref, slope_ref,
        low_ref, send_right_ref, send_left_ref, qkv_ref, out_ref, up_ref, down_ref, mask_ref,
        hidden_ref, sems,
    ) = refs[count_in:]
    wide = sizes.width
    copies = start_in(attn_pairs(mats, spots, groups, qkv_ref, out_ref, place_ref), sems, 0)
    ffn_copies = start_in(
        ffn_pairs(mats, spots, groups, up_ref, down_ref, place_ref), sems, len(copies)
    )
    gain = gains_ref[0, pl.ds(0, 1), :]
    bias = biases_ref[0, pl.ds(0, 1), :]
    pad = jnp.zeros((TILE - sizes.segs, wide), F32)
    for n in range(seqs):
        own = frames_ref[n].astype(F32)
        before = left_ref[n].astype(F32)
        hidden = norm_forward(own, gain, bias)[0]
        halo = norm_forward(before[before.shape[0] - LEFT_ROWS :], gain, bias)[0]
        after = norm_forward(right_ref[n].astype(F32), gain, bias)[0]
        memory = jnp.concatenate(
            [
                segment_mean(own),
                jnp.zeros((sizes.segs - before.shape[0] // SEG_LEN, wide), F32),
                segment_mean(before),
            ],
            axis=0,
        )
        base = n * sizes.ext
        z_ref[pl.ds(base, sizes.top), :] = jnp.concatenate(
            [segment_mean(hidden), pad], axis=0
        ).astype(BF16)
        z_ref[pl.ds(base + sizes.top, sizes.rows), :] = hidden.astype(BF16)
        z_ref[pl.ds(base + sizes.right_at, RIGHT_ROWS), :] = after.astype(BF16)
        z_ref[pl.ds(base + sizes.left_at, LEFT_ROWS), :] = halo.astype(BF16)
        z_ref[pl.ds(base + sizes.mem_at, MEM_ROWS), :] = memory.astype(BF16)
    fill_mask(sizes, seqs, starts_ref, place_ref, mask_ref)
    wait_all(copies)
    project(sizes, z_ref, qkv_ref, row_bias_ref, proj_ref)
    attend(sizes, seqs, proj_ref, mask_ref, probs_ref, att_ref)
    mixed = nt(att_ref[...], out_ref[...].reshape(-1, wide)) + biases_ref[3, pl.ds(0, 1), :]
    for n in range(seqs):
        base = n * sizes.queries
        mem_ref[pl.ds(n * sizes.segs, sizes.segs), :] = mixed[base : base + sizes.segs]
        mixed_ref[pl.ds(n * sizes.rows, sizes.rows), :] = (
            frames_ref[n].astype(F32) + mixed[base + sizes.top : base + sizes.top + sizes.rows]
        )
    mixed = mixed_ref[...]
    hidden, _, _ = norm_forward(mixed, gains_ref[0, pl.ds(1, 1), :], biases_ref[4, pl.ds(0, 1), :])
    hidden_ref[...] = hidden.astype(BF16)
    next_ref[...] = mixed + biases_ref[5, pl.ds(0, 1), :]
    wait_all(ffn_copies)

    def body(c, carry):
        at_lane = pl.multiple_of(c * wide, wide)
        upward = nt(hidden_ref[...], up_block(up_ref, c, wide))
        upward = upward + ffn_bias_ref[pl.ds(0, 1), pl.ds(at_lane, wide)]
        active, slope = gelu_both(upward)
        active = active.astype(BF16)
        active_ref[:, pl.ds(at_lane, wide)] = active
        slope_ref[:, pl.ds(at_lane, wide)] = slope.astype(BF16)
        next_ref[...] += nt(active, down_block(down_ref, c, wide))
        return carry

    lax.fori_loop(0, sizes.ff // wide, body, 0)
    low, _, _ = norm_forward(
        next_ref[...], gains_ref[1, pl.ds(0, 1), :], biases_ref[0, pl.ds(1, 1), :]
    )
    low = low.astype(BF16)
    low_ref[...] = low
    for n in range(seqs):
        base = n * sizes.rows
        send_right_ref[n, pl.ds(0, LEFT_ROWS), :] = low[
            base + sizes.rows - LEFT_ROWS : base + sizes.rows
        ]
        send_right_ref[n, pl.ds(LEFT_ROWS, MEM_ROWS), :] = jnp.concatenate(
            [
                mem_ref[pl.ds(n * sizes.segs, sizes.segs), :],
                jnp.zeros((MEM_ROWS - sizes.segs, wide), F32),
            ],
            axis=0,
        ).astype(BF16)
        send_left_ref[n] = low[base : base + RIGHT_ROWS]


def last_layer_kernel(
    sizes, seqs, mats, spots, count_in, count_out, place_ref, starts_ref, low_ref, left_ref,
    right_ref, mem_ref, inputs_ref, out_grad_ref, gains_ref, biases_ref, ffn_bias_ref,
    row_bias_ref, *refs
):
    groups = in_groups(spots, refs[:count_in])
    (encoded_ref, gz_ref, gh_ref, gmem_ref, back_left_ref, back_right_ref, vec) = refs[
        count_in : count_in + 7
    ]
    hbm_out = refs[count_in + 7 : count_in + 7 + count_out]
    (
        qkv_ref, out_ref, up_ref, down_ref, gqkv_ref, gout_ref, gup_ref, gdown_ref, mask_ref,
        z_ref, proj_ref, probs_ref, att_ref, hidden_ref, go_ref, gproj_ref, branch_ref,
        grad_low_ref, grad_hidden_ref, sems,
    ) = refs[count_in + 7 + count_out :]
    outs_to = hbm_out
    if spots is not None:
        rows = mats.attn_rows + mats.ffn_rows
        outs_to = [
            [ref.at[:, pl.ds(hop1 * rows, rows), :] for ref in hbm_out for hop1 in range(2)]
        ]
    wide = sizes.width
    attn_copies = start_in(attn_pairs(mats, spots, groups, qkv_ref, out_ref, place_ref), sems, 0)
    ffn_copies = start_in(
        ffn_pairs(mats, spots, groups, up_ref, down_ref, place_ref), sems, len(attn_copies)
    )
    vec[...] = jnp.zeros_like(vec)
    for n in range(seqs):
        base = n * sizes.ext
        z_ref[pl.ds(base, sizes.rows), :] = low_ref[pl.ds(n * sizes.rows, sizes.rows), :]
        z_ref[pl.ds(base + sizes.right_at, RIGHT_ROWS), :] = right_ref[n]
        z_ref[pl.ds(base + sizes.left_at, LEFT_ROWS), :] = left_ref[n, pl.ds(0, LEFT_ROWS), :]
        memory = jnp.concatenate(
            [
                mem_ref[pl.ds(n * sizes.segs, sizes.segs), :],
                left_ref[n, pl.ds(LEFT_ROWS, MEM_ROWS), :].astype(F32)[: sizes.segs],
            ],
            axis=0,
        )
        z_ref[pl.ds(base + sizes.mem_at, MEM_ROWS), :] = memory.astype(BF16)
        grad_low_ref[pl.ds(n * sizes.rows, sizes.rows), :] = out_grad_ref[n]
    fill_mask(sizes, seqs, starts_ref, place_ref, mask_ref)
    wait_all(attn_copies)
    project(sizes, z_ref, qkv_ref, row_bias_ref, proj_ref)
    attend(sizes, seqs, proj_ref, mask_ref, probs_ref, att_ref)
    mixed = (
        inputs_ref[...]
        + nt(att_ref[...], out_ref[...].reshape(-1, wide))
        + biases_ref[3, pl.ds(1, 1), :]
    )
    gain = gains_ref[1, pl.ds(1, 1), :]
    hidden, scaled, inverse = norm_forward(mixed, gain, biases_ref[4, pl.ds(1, 1), :])
    hidden_ref[...] = hidden.astype(BF16)
    for n in range(seqs):
        encoded_ref[n] = mixed[n * sizes.rows : (n + 1) * sizes.rows] + biases_ref[5, pl.ds(1, 1), :]
    grad_hidden_ref[...] = jnp.zeros_like(grad_hidden_ref)
    wait_all(ffn_copies)

    def body(c, carry):
        at_lane = pl.multiple_of(c * wide, wide)
        upward = nt(hidden_ref[...], up_block(up_ref, c, wide))
        upward = upward + ffn_bias_ref[pl.ds(1, 1), pl.ds(at_lane, wide)]
        active, slope = gelu_both(upward)
        active = active.astype(BF16)
        made = nt(active, down_block(down_ref, c, wide))
        for n in range(seqs):
            encoded_ref[n] += made[n * sizes.rows : (n + 1) * sizes.rows]
        grad_hidden_ref[...] += ffn_back_step(
            sizes, c, wide, grad_low_ref[...], hidden_ref[...], active, slope, up_ref, down_ref,
            gup_ref, gdown_ref, vec,
        )
        return carry

    lax.fori_loop(0, sizes.ff // wide, body, 0, unroll=True)
    out_at = len(attn_copies) + len(ffn_copies)
    outs = start_out(
        ffn_pairs(mats, spots, outs_to, gup_ref, gdown_ref, place_ref), sems, out_at
    )
    grad = grad_low_ref[...].astype(F32)
    grad_hidden = grad_hidden_ref[...]
    vec[pl.ds(1, 1), :] = col_sum(grad_hidden * scaled)
    vec[pl.ds(6, 1), :] = col_sum(grad_hidden)
    vec[pl.ds(7, 1), :] = col_sum(grad)
    gz = grad + norm_backward(grad_hidden, scaled, inverse, gain)
    gz_ref[...] = gz
    attn_back_stage(
        sizes, seqs, gz, None, att_ref, proj_ref, probs_ref, z_ref, qkv_ref, out_ref, gqkv_ref,
        gout_ref, go_ref, gproj_ref, branch_ref, vec, gh_ref, gmem_ref, back_left_ref,
        back_right_ref,
    )
    outs = outs + start_out(
        attn_pairs(mats, spots, outs_to, gqkv_ref, gout_ref, place_ref),
        sems,
        out_at + len(outs),
    )
    wait_all(outs)


def first_back_kernel(
    last, sizes, seqs, mats, spots, count_in, count_out, place_ref, inputs_ref, gz_in_ref,
    gh_in_ref, gmem_in_ref, from_right_ref, from_left_ref, mixed_ref, active_ref, slope_ref,
    att_ref, probs_ref, proj_ref, z_ref, frames_ref, left_ref, right_ref, gains_ref, biases_ref,
    last_vec, *refs
):
    groups = in_groups(spots, refs[:count_in])
    gz_ref, gh_ref, gmem_ref, back_left_ref, back_right_ref, upper_vec, vec = refs[
        count_in : count_in + 7
    ]
    refs = refs[count_in + 7 :]
    hbm_out = refs[:count_out]
    (
        qkv_ref, out_ref, up_ref, down_ref, gqkv_ref, gout_ref, gup_ref, gdown_ref, hidden_ref,
        grad_low_ref, grad_ref, grad_hidden_ref, grad_mem_ref, go_ref, gproj_ref, branch_ref,
        small_ref, sems,
    ) = refs[count_out:]
    wide = sizes.width
    small = []
    outs_to = hbm_out
    if spots is not None:
        rows = mats.attn_rows + mats.ffn_rows
        end = CHIPS_Z * rows
        each = [
            ref.at[hop2, hop1] for ref in hbm_out for hop2 in range(2) for hop1 in range(2)
        ]
        small = [ref.at[pl.ds(end, SMALL_ROWS), :] for ref in each]
        outs_to = [[ref.at[pl.ds(0, end), :].reshape(CHIPS_Z, rows, LANES) for ref in each]]
    ffn_copies = start_in(ffn_pairs(mats, spots, groups, up_ref, down_ref, place_ref), sems, 0)
    attn_copies = start_in(
        attn_pairs(mats, spots, groups, qkv_ref, out_ref, place_ref), sems, len(ffn_copies)
    )
    vec[...] = jnp.zeros_like(vec)
    upper_vec[...] = jnp.zeros_like(upper_vec)
    gain = gains_ref[1, pl.ds(0, 1), :]
    gain_sum = jnp.zeros((1, wide), F32)
    bias_sum = jnp.zeros((1, wide), F32)
    for n in range(seqs):
        rows = pl.ds(n * sizes.rows, sizes.rows)
        _, scaled, inverse = norm_forward(
            inputs_ref[rows, :], gain, biases_ref[0, pl.ds(1, 1), :]
        )
        total, mem = merge_halo(last, n, gh_in_ref, gmem_in_ref, from_right_ref, from_left_ref)
        gain_sum = gain_sum + col_sum(total * scaled)
        bias_sum = bias_sum + col_sum(total)
        grad = gz_in_ref[rows, :] + norm_backward(total, scaled, inverse, gain)
        grad_ref[rows, :] = grad
        grad_low_ref[rows, :] = grad.astype(BF16)
        grad_mem_ref[pl.ds(n * sizes.segs, sizes.segs), :] = mem
    upper_vec[pl.ds(0, 1), :] = gain_sum
    upper_vec[pl.ds(2, 1), :] = bias_sum
    gain = gains_ref[0, pl.ds(1, 1), :]
    hidden, scaled, inverse = norm_forward(
        mixed_ref[...], gain, biases_ref[4, pl.ds(0, 1), :]
    )
    hidden_ref[...] = hidden.astype(BF16)
    grad_hidden_ref[...] = jnp.zeros_like(grad_hidden_ref)
    wait_all(ffn_copies)

    def body(c, carry):
        at_lane = pl.multiple_of(c * wide, wide)
        grad_hidden_ref[...] += ffn_back_step(
            sizes, c, wide, grad_low_ref[...], hidden_ref[...],
            active_ref[:, pl.ds(at_lane, wide)], slope_ref[:, pl.ds(at_lane, wide)].astype(F32),
            up_ref, down_ref, gup_ref, gdown_ref, vec,
        )
        return carry

    lax.fori_loop(0, sizes.ff // wide, body, 0)
    out_at = len(ffn_copies) + len(attn_copies)
    outs = start_out(
        ffn_pairs(mats, spots, outs_to, gup_ref, gdown_ref, place_ref), sems, out_at
    )
    grad_hidden = grad_hidden_ref[...]
    grad = grad_ref[...]
    vec[pl.ds(1, 1), :] = col_sum(grad_hidden * scaled)
    vec[pl.ds(6, 1), :] = col_sum(grad_hidden)
    vec[pl.ds(7, 1), :] = col_sum(grad)
    gz = grad + norm_backward(grad_hidden, scaled, inverse, gain)
    gz_ref[...] = gz

    def scaled_rows(n):
        before = left_ref[n, pl.ds(left_ref.shape[1] - LEFT_ROWS, LEFT_ROWS), :]
        parts = (frames_ref[n], right_ref[n], before)
        first_gain = gains_ref[0, pl.ds(0, 1), :]
        first_bias = biases_ref[0, pl.ds(0, 1), :]
        return [norm_forward(part.astype(F32), first_gain, first_bias)[1] for part in parts]

    wait_all(attn_copies)
    attn_back_stage(
        sizes, seqs, gz, grad_mem_ref, att_ref, proj_ref, probs_ref, z_ref, qkv_ref, out_ref,
        gqkv_ref, gout_ref, go_ref, gproj_ref, branch_ref, vec, gh_ref, gmem_ref, back_left_ref,
        back_right_ref, scaled_rows,
    )
    outs = outs + start_out(
        attn_pairs(mats, spots, outs_to, gqkv_ref, gout_ref, place_ref),
        sems,
        out_at + len(outs),
    )
    totals = vec[...], last_vec[...] + upper_vec[...]
    small_ref[...] = jnp.concatenate(
        [
            total[:VEC_ROWS, part * LANES : (part + 1) * LANES]
            for part in range(sizes.pairs)
            for total in totals
        ],
        axis=0,
    ).astype(BF16)
    outs = outs + start_out([(ref, small_ref) for ref in small], sems, out_at + len(outs))
    wait_all(outs)


def frames_grad_kernel(
    sizes, seqs, frames_ref, gz_ref, gh_ref, gmem_ref, from_right_ref, from_left_ref, gains_ref,
    biases_ref, grad_ref
):
    gain = gains_ref[0, pl.ds(0, 1), :]
    for n in range(seqs):
        _, scaled, inverse = norm_forward(
            frames_ref[n].astype(F32), gain, biases_ref[0, pl.ds(0, 1), :]
        )
        total, mem = merge_halo(sizes, n, gh_ref, gmem_ref, from_right_ref, from_left_ref)
        grad_ref[n] = (
            gz_ref[pl.ds(n * sizes.rows, sizes.rows), :]
            + norm_backward(total, scaled, inverse, gain)
            + segment_spread(sizes.rows, sizes.width, mem * (1.0 / SEG_LEN))
        )


def shifted(value, axis, by):
    size = lax.axis_size(axis)
    return lax.ppermute(value, axis, [(i, (i + by) % size) for i in range(size)])


def permuted(value, move):
    reps = lax.axis_size("rep")
    pairs = []
    for flat in range(lax.axis_size("seg") * reps):
        seg, rep = divmod(flat, reps)
        z, y, x, core = move(seg // CHIPS_Y, seg % CHIPS_Y, rep // 2, rep % 2)
        pairs.append((flat, (z * CHIPS_Y + y) * reps + 2 * x + core))
    return lax.ppermute(value, ("seg", "rep"), pairs)


def across_first(value):
    return permuted(value, lambda z, y, x, c: (z, y, x ^ 1, c) if c == 0 else (z, y ^ 1, x, c))


def across_second(value):
    return permuted(value, lambda z, y, x, c: (z, y ^ 1, x, c) if c == 0 else (z, y, x ^ 1, c))


def other_core(value):
    return permuted(value, lambda z, y, x, c: (z, y, x, c ^ 1))


def after(value, *others):
    return lax.optimization_barrier((value,) + others)[0]


def swap_z(blocks):
    groups = [
        [z * CHIPS_Y + y for z in range(CHIPS_Z)] for y in range(CHIPS_Y)
    ]
    return lax.all_to_all(blocks, "seg", 0, 0, axis_index_groups=groups, tiled=True)


def gather_sides(here):
    return [here, across_first(here), across_second(here)]


def both_cores(blocks):
    return blocks + [other_core(block) for block in blocks]


def summed(*parts):
    total = parts[0].astype(F32)
    for part in parts[1:]:
        total = total + part.astype(F32)
    return total.astype(BF16)


def sum_everywhere(value):
    count = lax.axis_size("seg") * lax.axis_size("rep")
    bit = 1
    while bit < count:
        value = value + lax.ppermute(value, ("seg", "rep"), [(i, i ^ bit) for i in range(count)])
        bit *= 2
    return value


def vmem_spec():
    return pl.BlockSpec(memory_space=pltpu.VMEM)


def smem_spec():
    return pl.BlockSpec(memory_space=pltpu.SMEM)


def hbm_spec():
    return pl.BlockSpec(memory_space=pl.ANY)


def call(body, in_specs, out_shapes, out_specs, scratch, args, flops=0, moved=0, grid=(), aliases={}, vmem=12):
    return pl.pallas_call(
        body,
        grid=grid,
        input_output_aliases=aliases,
        in_specs=in_specs,
        out_shape=tuple(jax.ShapeDtypeStruct(shape, kind) for shape, kind in out_shapes),
        out_specs=tuple(out_specs),
        scratch_shapes=scratch,
        compiler_params=pltpu.CompilerParams(vmem_limit_bytes=vmem * MIB),
        cost_estimate=pl.CostEstimate(flops=flops, bytes_accessed=moved, transcendentals=0),
    )(*args)


def on_device(
    frames,
    utt_segments,
    out_grad,
    qkv_weight,
    out_weight,
    ffn_in_weight,
    ffn_out_weight,
    norm_gains,
    biases,
    ffn_bias,
):
    micros, groups, rows, width = frames.shape
    seqs = micros * groups
    ff = ffn_bias.shape[1]
    reps = lax.axis_size("rep")
    seg_count = lax.axis_size("seg")
    mats = Matrices(width, ff)
    by_blocks = width // reps == LANES and reps == 4 and seg_count == BLOCKS
    first = Sizes(rows, width, ff, True)
    last = Sizes(rows, width, ff, False)
    own = seqs * rows
    mem_own = seqs * first.segs

    seg_at = lax.axis_index("seg")
    seg_base = seg_at * first.segs
    rep_at = lax.axis_index("rep")
    place = [seg_base, jnp.int32(first.segs * seg_count)]
    y_at, x_at, core_at = seg_at % CHIPS_Y, rep_at // 2, rep_at % 2
    for other in range(2):
        core = lax.bitwise_xor(core_at, other)
        for hop2 in range(2):
            for hop1 in range(2):
                x_hop = jnp.where(core == 0, hop1, hop2)
                y_hop = jnp.where(core == 0, hop2, hop1)
                place.append(lax.bitwise_xor(y_at, y_hop))
                place.append((lax.bitwise_xor(x_at, x_hop) * 2 + core) * LANES)
    place = jnp.stack([jnp.asarray(entry, jnp.int32) for entry in place])
    lengths = utt_segments.reshape(seqs, utt_segments.shape[2])
    starts = (jnp.cumsum(lengths, axis=1) - lengths).astype(jnp.int32)
    zero_bias = jnp.zeros((1, width), F32)
    row_biases = [
        jnp.concatenate([biases[l : l + 1, 1], zero_bias, biases[l : l + 1, 2]], axis=1)
        for l in range(LAYERS)
    ]
    biases_by_row = jnp.swapaxes(biases, 0, 1)

    frames_own = frames.reshape(seqs, rows, width)
    grads_own = out_grad.reshape(seqs, rows, width)
    far = MEM_LEN * SEG_LEN
    frames_left = shifted(frames_own[:, rows - far :], "seg", 1)
    frames_right = shifted(frames_own[:, :RIGHT_ROWS], "seg", -1)

    attn_rows, ffn_rows = mats.attn_rows, mats.ffn_rows
    if by_blocks:
        qkv_t, out_t, down_t = (
            jnp.swapaxes(member, 1, 2) for member in (qkv_weight, out_weight, ffn_out_weight)
        )
        all_rows = attn_rows + ffn_rows
        spots = Spots(mats)
        shards = call(
            lambda *refs: pack_kernel(spots, *refs),
            [vmem_spec()] * 4,
            [((CHIPS_Z, all_rows, LANES), BF16)] * LAYERS,
            [vmem_spec()] * LAYERS,
            [],
            (qkv_t, out_t, ffn_in_weight, down_t),
            vmem=56,
        )
        sides0 = gather_sides(after(swap_z(shards[0]), frames_left, frames_right))
        place, starts, row_biases, sent = lax.optimization_barrier(
            (place, starts, row_biases, after(shards[1], sides0[0]))
        )
        sides1 = gather_sides(swap_z(sent))
        first_all = both_cores(sides0 + [across_second(after(sides0[1], sides1[0]))])
        classes = len(first_all) // 2
        grad_outs0 = [((2, 2, CHIPS_Z * all_rows + SMALL_ROWS, LANES), BF16)] * 2
        grad_outs1 = [((CHIPS_Z, 2 * all_rows, LANES), BF16)] * 4
        copies_in = len(first_all) * (3 + mats.down_parts)
    else:
        whole = []
        for member, shape in zip(
            (qkv_weight, out_weight, ffn_in_weight, ffn_out_weight),
            (mats.qkv, mats.out, mats.up, mats.down),
        ):
            member = lax.all_gather(member, "rep", axis=1, tiled=True)
            member = lax.all_gather(member, "seg", axis=2, tiled=True)
            whole.append(jnp.swapaxes(member, 1, 2).reshape((LAYERS,) + shape))
        first_all = [member[0] for member in whole]
        last_all = [member[1] for member in whole]
        spots = None
        grad_outs0 = grad_outs1 = [
            (shape, BF16) for shape in (mats.qkv, mats.out, mats.up, mats.down)
        ]
        copies_in = 4
    dma = pltpu.SemaphoreType.DMA

    matrices = [pltpu.VMEM(shape, BF16) for shape in (mats.qkv, mats.out, mats.up, mats.down)]

    (
        z0, proj0, probs0, att0, mixed0, mem1, x1, active0, slope0, low1, send_right, send_left,
    ) = call(
        lambda *refs: first_layer_kernel(
            first, seqs, mats, spots, len(first_all), *refs
        ),
        [smem_spec()] * 2 + [vmem_spec()] * 7 + [hbm_spec()] * len(first_all),
        [
            ((seqs * first.ext, width), BF16),
            ((seqs * first.ext, 3 * width), BF16),
            ((seqs * first.pairs, first.keys, 2 * first.queries), BF16),
            ((seqs * first.queries, width), BF16),
            ((own, width), F32),
            ((mem_own, width), F32),
            ((own, width), F32),
            ((own, ff), BF16),
            ((own, ff), BF16),
            ((own, width), BF16),
            ((seqs, BACK_ROWS, width), BF16),
            ((seqs, RIGHT_ROWS, width), BF16),
        ],
        [vmem_spec()] * 12,
        matrices
        + [
            pltpu.VMEM((seqs, first.keys, 2 * first.queries), F32),
            pltpu.VMEM((own, width), BF16),
            dma((copies_in,)),
        ],
        (place, starts, frames_own, frames_left, frames_right, norm_gains, biases_by_row, ffn_bias,
         row_biases[0]) + tuple(first_all),
        flops=24 * own * (4 * width * width + 2 * width * ff) // 2,
        moved=2 * (4 * width * width + 2 * width * ff),
        vmem=20,
    )
    left1 = shifted(send_right, "seg", 1)
    right1 = shifted(send_left, "seg", -1)
    if by_blocks:
        last_side = across_second(after(sides1[1], sides1[2], left1, right1))
        last_all = both_cores(sides1 + [last_side])

    vec_shape = (TILE, width)
    outs = call(
        lambda *refs: last_layer_kernel(
            last, seqs, mats, spots, len(last_all), len(grad_outs1), *refs
        ),
        [smem_spec()] * 2 + [vmem_spec()] * 10 + [hbm_spec()] * len(last_all),
        [
            ((seqs, rows, width), F32),
            ((own, width), F32),
            ((own, width), F32),
            ((mem_own, width), F32),
            ((seqs, BACK_ROWS, width), BF16),
            ((seqs, RIGHT_ROWS, width), BF16),
            (vec_shape, F32),
        ]
        + grad_outs1,
        [vmem_spec()] * 7 + [hbm_spec()] * len(grad_outs1),
        matrices
        + matrices
        + [
            pltpu.VMEM((seqs, last.keys, 2 * last.queries), F32),
            pltpu.VMEM((seqs * last.ext, width), BF16),
            pltpu.VMEM((seqs * last.ext, 3 * width), BF16),
            pltpu.VMEM((seqs * last.pairs, last.keys, 2 * last.queries), BF16),
            pltpu.VMEM((seqs * last.queries, width), BF16),
            pltpu.VMEM((own, width), BF16),
            pltpu.VMEM((seqs * last.queries, width), BF16),
            pltpu.VMEM((seqs * last.ext, 3 * width), BF16),
            pltpu.VMEM((seqs * last.queries, width), BF16),
            pltpu.VMEM((own, width), BF16),
            pltpu.VMEM((own, width), F32),
            dma((2 * copies_in,)),
        ],
        (place, starts, low1, left1, right1, mem1, x1, grads_own, norm_gains, biases_by_row, ffn_bias,
         row_biases[1]) + tuple(last_all),
        flops=30 * own * (4 * width * width + 2 * width * ff),
        moved=4 * (4 * width * width + 2 * width * ff),
        vmem=26,
    )
    encoded, gz1, gh1, gmem1, back_left1, back_right1, vec1 = outs[:7]
    grad_blocks1 = outs[7:]
    from_right1 = shifted(back_left1, "seg", -1)
    from_left1 = shifted(back_right1, "seg", 1)

    gh1_tied = gh1
    if by_blocks:
        near1, far1, near1_other, far1_other = grad_blocks1
        far1 = summed(far1, other_core(far1_other))
        near1_theirs = other_core(near1_other)
        gh1_tied = after(gh1, far1, near1_theirs)
    gz0, gh0, gmem0, back_left0, back_right0, upper_vec, vec0, *grad_blocks0 = call(
        lambda *refs: first_back_kernel(
            last, first, seqs, mats, spots, len(first_all), len(grad_outs0), *refs
        ),
        [smem_spec()] + [vmem_spec()] * 19 + [hbm_spec()] * len(first_all),
        [
            ((own, width), F32),
            ((own, width), F32),
            ((mem_own, width), F32),
            ((seqs, BACK_ROWS, width), BF16),
            ((seqs, RIGHT_ROWS, width), BF16),
            (vec_shape, F32),
            (vec_shape, F32),
        ]
        + grad_outs0,
        [vmem_spec()] * 7 + [hbm_spec()] * len(grad_outs0),
        matrices
        + matrices
        + [
            pltpu.VMEM((own, width), BF16),
            pltpu.VMEM((own, width), BF16),
            pltpu.VMEM((own, width), F32),
            pltpu.VMEM((own, width), F32),
            pltpu.VMEM((mem_own, width), F32),
            pltpu.VMEM((seqs * first.queries, width), BF16),
            pltpu.VMEM((seqs * first.ext, 3 * width), BF16),
            pltpu.VMEM((seqs * first.queries, width), BF16),
            pltpu.VMEM((SMALL_ROWS, LANES), BF16),
            dma((2 * copies_in + 8,)),
        ],
        (place, x1, gz1, gh1_tied, gmem1, from_right1, from_left1, mixed0, active0, slope0, att0,
         probs0, proj0, z0, frames_own, frames_left, frames_right, norm_gains, biases_by_row, vec1)
        + tuple(first_all),
        flops=28 * own * (4 * width * width + 2 * width * ff),
        moved=4 * (4 * width * width + 2 * width * ff),
        vmem=28,
    )
    from_right0 = shifted(back_left0, "seg", -1)
    from_left0 = shifted(back_right0, "seg", 1)
    gz0_last = gz0
    if by_blocks:
        second1 = across_second(far1)
        mine0, theirs0 = grad_blocks0[0], other_core(after(grad_blocks0[1], second1))
        both1 = summed(near1, near1_theirs, second1)
        lines1 = swap_z(both1)
        far0 = summed(mine0[1], after(theirs0, both1)[1])
        second0 = across_second(far0)
        mid0 = summed(mine0[0, 1], theirs0[0, 1], second0[1])
        first0 = across_first(mid0)
        held0 = summed(mine0[0, 0], theirs0[0, 0], after(second0, mid0)[0])
        near0 = summed(held0, first0)
        blocks = CHIPS_Z * all_rows
        near0 = jnp.concatenate(
            [
                near0[:blocks].reshape(CHIPS_Z, all_rows, LANES),
                jnp.broadcast_to(near0[None, blocks:], (CHIPS_Z, SMALL_ROWS, LANES)),
            ],
            axis=1,
        )
        first_parts = swap_z(after(near0, from_right0, from_left0))
        gz0_last, lines1 = lax.optimization_barrier((after(gz0, near0), lines1))
        cross1 = jnp.sum(lines1[:, all_rows:].astype(F32), axis=0, keepdims=True).astype(BF16)
        first1 = across_first(cross1)
    frames_grad = call(
        lambda *refs: frames_grad_kernel(first, seqs, *refs),
        [vmem_spec()] * 8,
        [((seqs, rows, width), F32)],
        [vmem_spec()],
        [],
        (frames_own, gz0_last, gh0, gmem0, from_right0, from_left0, norm_gains, biases_by_row),
    )[0]

    if by_blocks:
        shapes = [member.shape for member in (qkv_t, out_t, ffn_in_weight, down_t)]
        held = [pltpu.VMEM(shape[1:], F32) for shape in shapes]
        whole = [(shape, F32) for shape in shapes]
        written = call(
            lambda *refs: unpack_last_kernel(spots, LAYERS - 1, *refs),
            [
                pl.BlockSpec((CHIPS_Z, all_rows, LANES), lambda i: (0, 0, 0)),
                pl.BlockSpec((1, all_rows, LANES), lambda i: (0, 0, 0)),
            ],
            whole,
            [hbm_spec()] * 4,
            held + [dma((4,))],
            [lines1, first1],
            grid=(1,),
        )
        small_shapes = [norm_gains.shape, (biases.shape[1], LAYERS, width), ffn_bias.shape]
        reduced = call(
            lambda *refs: unpack_first_kernel(spots, all_rows, *refs),
            [vmem_spec()] + [hbm_spec()] * 4,
            whole + [(shape, F32) for shape in small_shapes],
            [hbm_spec()] * 4 + [vmem_spec()] * 3,
            held + [dma((4,))],
            [after(first_parts, frames_grad)] + list(written),
            aliases={1 + i: i for i in range(4)},
        )
        small = reduced[4], jnp.swapaxes(reduced[5], 0, 1), reduced[6]
        reduced = [
            jnp.swapaxes(reduced[0], 1, 2),
            jnp.swapaxes(reduced[1], 1, 2),
            reduced[2],
            jnp.swapaxes(reduced[3], 1, 2),
        ]
    else:
        reduced = []
        for member0, member1 in zip(grad_blocks0, grad_blocks1):
            both = jnp.stack([member0, member1]).reshape(LAYERS, -1, member0.shape[3])
            both = jnp.swapaxes(both, 1, 2)
            both = lax.psum_scatter(both, "seg", scatter_dimension=2, tiled=True)
            both = lax.psum_scatter(both, "rep", scatter_dimension=1, tiled=True)
            reduced.append(both.astype(F32))
        small = sum_everywhere(jnp.stack([vec0, vec1 + upper_vec]))
        small = small[:, 0:2], small[:, 2:8], small[:, 8:12].reshape(ffn_bias.shape)

    return (
        encoded.reshape(frames.shape),
        frames_grad.reshape(frames.shape),
        reduced[0],
        reduced[1],
        reduced[2],
        reduced[3],
        small[0],
        small[1],
        small[2],
    )


def solution(mesh):
    in_specs = (
        P(None, "rep", "seg", None),
        P(None, "rep", None),
        P(None, "rep", "seg", None),
        P(None, "rep", "seg"),
        P(None, "rep", "seg"),
        P(None, "rep", "seg"),
        P(None, "rep", "seg"),
        P(),
        P(),
        P(),
    )
    out_specs = (
        P(None, "rep", "seg", None),
        P(None, "rep", "seg", None),
        P(None, "rep", "seg"),
        P(None, "rep", "seg"),
        P(None, "rep", "seg"),
        P(None, "rep", "seg"),
        P(),
        P(),
        P(),
    )
    return jax.shard_map(
        on_device, mesh=mesh, in_specs=in_specs, out_specs=out_specs, check_vma=False
    )
```
